32 devices in a mesh: dp: 4 (over y, x), section: 4 (over z), group: 2 (over core).
Axes of the slice: x: 2, y: 2, z: 4, core: 2. Of those that a mesh axis runs over, the one named last changes fastest.
Arguments:
- tokens_in: bfloat16 [1024, 4096], P(('dp', 'group')), may hold values from -6 to 6
- cotangent: bfloat16 [1024, 4096], P(('dp', 'group')), may hold values from -6 to 6
- gains: float32 [4, 4096], P('section'), may hold values from 0.5 to 1.5
- w_qkv: bfloat16 [4, 4096, 384], P('section'), may hold values from -0.09375 to 0.09375
- w_out: bfloat16 [4, 128, 4096], P('section'), may hold values from -0.5 to 0.5
- segments: int32 [64, 16], P(('dp', 'group')), may hold values from 0 to 3, never falling along the last dimension, each value on 1 to 8 neighbouring positions
- plan: int32 [8, 8], P(('dp', 'group')), may hold values from 0 to 7, each once within a row
Outputs:
- input_grads: bfloat16 [4, 1024, 4096], P('section', ('dp', 'group'))
- gain_grads: float32 [4, 4096], P('section')
The draws below stay inside these ranges and needn't reach their ends.
Inputs may be any that keep to these rules, and one draw needn't show every extreme that they name: Each row of plan names every one of 0 .. 7 once. `segments`: segment numbers never fall along a row and every episode lies within one row.
All inputs are finite; a program needn't handle non-finite values.
Results may differ from the reference program's by a relative error of at most 0.029.
Values may be sent and summed in bfloat16 or wider, within the bound.
No kernel may reach another device: no remote copies, remote signals or barrier semaphores. Data moves between devices by JAX's collectives and lax.ppermute only.
A program may use at most 64 MiB of HBM per device.

```python
import math
import jax
import jax.numpy as jnp
import numpy as np
from jax import lax

D = 4096
HEAD_DIM = 128
ROW = 16
ROWS_DEV = 8
TOKENS = 1024
N_DP = 4
N_SECTION = 4
N_GROUP = 2


def levels(key, extent, pieces, least, largest):
    loudness, own = 1.0, jax.random.fold_in(key, 6)
    for dim, shards_of in pieces:
        heights = jnp.exp(jax.random.uniform(jax.random.fold_in(own, dim), (shards_of,), jnp.float32, least / len(pieces), largest / len(pieces)))
        loudness = loudness * jnp.repeat(heights, extent[dim] // shards_of).reshape([-1 if axis == dim else 1 for axis in range(len(extent))])
    return loudness


def profile(count, total, most, lean):
    weights = [(1 << 20) // math.isqrt(standing ** lean) + 1 for standing in range(2, count + 1)]
    rest, holding = total - most - (count - 1), [1] * (count - 1)
    while rest > 0:
        movable = [i for i in range(count - 1) if holding[i] < most]
        mass, budget = sum([weights[i] for i in movable]), rest
        for i in movable:
            more = min(most - holding[i], max(1, budget * weights[i] // mass), rest)
            holding[i] = holding[i] + more
            rest = rest - more
    return np.array([most] + holding)


def ragged_sizes(own_key, amount, total, reach, slope):
    if amount == 2:
        one = jax.random.randint(own_key, (), max(1, total - reach), min(reach, total - 1) + 1)
        return jnp.stack([one, total - one])
    lengths = jnp.asarray(profile(amount, total, reach, slope), jnp.int32)
    twos = (amount - 1) // 2
    donor, taker = lengths[1:1 + 2 * twos:2], lengths[2:2 + 2 * twos:2]
    slack = jnp.minimum(donor - 1, reach - taker)
    passed = jax.random.randint(jax.random.fold_in(own_key, 1), (twos,), 0, 1 << 20) % (slack + 1)
    lengths = lengths.at[1:1 + 2 * twos:2].set(donor - passed).at[2:2 + 2 * twos:2].set(taker + passed)
    return lengths[jax.random.permutation(jax.random.fold_in(own_key, 2), amount)]


def centred(stream_key, dims, scale, most, cuts=(), kind=jnp.bfloat16):
    drawn = jax.random.normal(stream_key, dims, jnp.float32) * scale
    if len(cuts) > 0:
        drawn = levels(stream_key, dims, cuts, -0.22, 0.18) * drawn
    return jnp.clip(drawn, min=-most, max=most).astype(kind)


def setup_inputs(seed: int = 0) -> dict:
    seeds = jax.random.split(jax.random.key(seed), 8)
    return {
        "tokens_in": centred(seeds[0], (TOKENS, D), 1.0, 6.0, ((0, 8),)),
        "cotangent": centred(seeds[1], (TOKENS, D), 1.0, 6.0, ((0, 8),)),
        "gains": jnp.clip(0.5 + 1.0 * jax.random.uniform(seeds[2], (N_SECTION, D), jnp.float32) ** levels(seeds[2], (N_SECTION, D), ((0, 4),), -0.2, 0.2), 0.5, 1.5),
        "w_qkv": centred(seeds[3], (N_SECTION, D, 3 * HEAD_DIM), D ** -0.5, 0.09375, ((0, 4),)),
        "w_out": centred(seeds[4], (N_SECTION, HEAD_DIM, D), HEAD_DIM ** -0.5, 0.5, ((0, 4),)),
        "segments": jax.vmap(lambda own: jnp.searchsorted(jnp.cumsum(ragged_sizes(own, 4, ROW, 8, 0)), jnp.arange(ROW), side="right"))(jax.random.split(seeds[5], (TOKENS // ROW))).reshape((TOKENS // ROW, ROW)).astype(jnp.int32),
        "plan": jax.vmap(lambda own: jax.random.permutation(own, ROWS_DEV))(jax.random.split(seeds[6], (N_DP * N_GROUP))).reshape((N_DP * N_GROUP, ROWS_DEV)).astype(jnp.int32),
    }


def attend(hidden, segment, gain_row, w_layer, out_layer):
    count = hidden.shape[0]
    length = hidden.shape[1]
    width = hidden.shape[2]
    head = out_layer.shape[0]
    scaled = hidden * lax.rsqrt(lax.optimization_barrier(jnp.mean(hidden * hidden, axis=-1, keepdims=True)) + 1e-05) * gain_row
    normed = scaled.astype(jnp.bfloat16).reshape(count * length, width)
    projected = jnp.dot(normed, w_layer, preferred_element_type=jnp.float32).reshape(count, length, 3 * head)
    query = projected[:, :, :head]
    keyed = projected[:, :, head:2 * head]
    valued = projected[:, :, 2 * head:]
    positions = jnp.arange(length)
    allowed = (positions[:, None] >= positions[None, :])[None] & (segment[:, :, None] == segment[:, None, :])
    scores = jnp.einsum('rid,rjd->rij', query, keyed, precision=lax.Precision.HIGHEST) / math.sqrt(head)
    scores = jnp.where(allowed, scores, -1e+30)
    weights = jax.nn.softmax(scores, axis=-1)
    mixed = jnp.einsum('rij,rjd->rid', weights, valued, precision=lax.Precision.HIGHEST)
    mixed = mixed.astype(jnp.bfloat16).reshape(count * length, head)
    output = jnp.dot(mixed, out_layer, preferred_element_type=jnp.float32).reshape(count, length, width)
    return hidden + output

def reference(tokens_in, cotangent, gains, w_qkv, w_out, segments, plan):
    width = tokens_in.shape[1]
    share = ROWS_DEV // N_GROUP
    blocks = tokens_in.reshape(N_DP, N_GROUP, ROWS_DEV, ROW, width)
    seg_blocks = segments.reshape(N_DP, N_GROUP, ROWS_DEV, ROW)
    order = plan.reshape(N_DP, N_GROUP, ROWS_DEV)
    chosen = jnp.take_along_axis(blocks, order[:, :, :, None, None], axis=2)
    chosen_seg = jnp.take_along_axis(seg_blocks, order[:, :, :, None], axis=2)
    chosen = chosen.reshape(N_DP, N_GROUP, N_GROUP, share, ROW, width).transpose(0, 2, 1, 3, 4, 5)
    chosen_seg = chosen_seg.reshape(N_DP, N_GROUP, N_GROUP, share, ROW).transpose(0, 2, 1, 3, 4)
    current = chosen.reshape(-1, ROW, width)
    seg_rows = chosen_seg.reshape(-1, ROW)
    inputs = []
    for layer in range(N_SECTION):
        inputs.append(current)
        current = attend(current.astype(jnp.float32), seg_rows, gains[layer], w_qkv[layer], w_out[layer]).astype(jnp.bfloat16)
    incoming = cotangent.reshape(-1, ROW, width)
    grads_x = [None] * N_SECTION
    grads_gain = [None] * N_SECTION
    for layer in reversed(range(N_SECTION)):

        def local_layer(hidden, gain_row):
            return attend(hidden, seg_rows, gain_row, w_qkv[layer], w_out[layer])
        _, pullback = jax.vjp(local_layer, inputs[layer].astype(jnp.float32), gains[layer])
        grad_hidden, grad_gain = pullback(incoming.astype(jnp.float32))
        incoming = grad_hidden.astype(jnp.bfloat16)
        grads_x[layer] = incoming.reshape(-1, width)
        grads_gain[layer] = grad_gain
    return (jnp.stack(grads_x), jnp.stack(grads_gain))
```

```python
import functools
import math

import jax
import jax.numpy as jnp
from jax import lax
from jax.experimental import pallas as pl
from jax.experimental.pallas import tpu as pltpu
from jax.sharding import PartitionSpec as P

EPS = 1e-05
VMEM_BYTES = 48 * 1024 * 1024
F32 = jnp.float32
BF16 = jnp.bfloat16


def dot_nn(a, b):
    return lax.dot_general(a, b, (((1,), (0,)), ((), ())), preferred_element_type=F32)


def dot_nt(a, b):
    return lax.dot_general(a, b, (((1,), (1,)), ((), ())), preferred_element_type=F32)


def dot_tn(a, b):
    return lax.dot_general(a, b, (((0,), (0,)), ((), ())), preferred_element_type=F32)


def params():
    return pltpu.CompilerParams(vmem_limit_bytes=VMEM_BYTES)


def pick_rows(tokens, plan, place, groups):
    rows, length, width = tokens.shape
    share = rows // groups

    def kernel(plan_ref, place_ref, tokens_ref, *rest):
        parts, sems = rest[:groups], rest[groups]
        copies = []
        for r in range(groups):
            target = lax.rem(place_ref[0] + r, groups)
            for c in range(share):
                row = plan_ref[0, target * share + c]
                copy = pltpu.make_async_copy(
                    tokens_ref.at[row], parts[r].at[c], sems.at[r * share + c]
                )
                copy.start()
                copies.append(copy)
        for copy in copies:
            copy.wait()

    return pl.pallas_call(
        kernel,
        out_shape=[jax.ShapeDtypeStruct((share, length, width), BF16)] * groups,
        in_specs=[
            pl.BlockSpec(memory_space=pltpu.SMEM),
            pl.BlockSpec(memory_space=pltpu.SMEM),
            pl.BlockSpec(memory_space=pl.ANY),
        ],
        out_specs=[pl.BlockSpec(memory_space=pl.ANY)] * groups,
        scratch_shapes=[pltpu.SemaphoreType.DMA((rows,))],
        compiler_params=params(),
        name="pick_rows",
    )(plan, place, tokens)


def project(parts, cotangent, gain, w_layer, out_layer, place):
    groups = len(parts)
    tokens, width = cotangent.shape
    head = out_layer.shape[0]
    wide = w_layer.shape[1]
    block = tokens // groups
    step = min(width, 1024)

    def kernel(place_ref, *refs):
        part_refs = refs[:groups]
        cot_ref, g_ref, w_ref, o_ref, x_ref, xz_ref, n_ref, acc, square = refs[groups:]
        k = pl.program_id(0)

        @pl.when(k == 0)
        def _():
            acc[...] = jnp.zeros_like(acc)
            square[...] = jnp.zeros_like(square)

        for r in range(groups):
            source = lax.rem(place_ref[0] + groups - r, groups)
            rows = pl.ds(pl.multiple_of(source * block, block), block)
            x_ref[rows, :] = part_refs[r][...]
        x = x_ref[...]
        xf = x.astype(F32)
        acc[:, :wide] += dot_nn((xf * g_ref[...]).astype(BF16), w_ref[...])
        acc[:, wide : wide + head] += dot_nt(x, o_ref[...])
        acc[:, wide + head :] += dot_nt(cot_ref[...], o_ref[...])
        square[...] += jnp.sum(xf * xf, axis=1, keepdims=True)

        @pl.when(k == pl.num_programs(0) - 1)
        def _():
            xz_ref[...] = acc[...].astype(BF16)
            n_ref[...] = square[...]

    spec = lambda shape, index: pl.BlockSpec(shape, index)
    return pl.pallas_call(
        kernel,
        grid=(width // step,),
        out_shape=[
            jax.ShapeDtypeStruct((tokens, width), BF16),
            jax.ShapeDtypeStruct((tokens, wide + 2 * head), BF16),
            jax.ShapeDtypeStruct((tokens, 1), F32),
        ],
        in_specs=[pl.BlockSpec(memory_space=pltpu.SMEM)]
        + [spec((block, step), lambda k: (0, k))] * groups
        + [
            spec((tokens, step), lambda k: (0, k)),
            spec((1, step), lambda k: (0, k)),
            spec((step, wide), lambda k: (k, 0)),
            spec((head, step), lambda k: (0, k)),
        ],
        out_specs=[
            spec((tokens, step), lambda k: (0, k)),
            spec((tokens, wide + 2 * head), lambda k: (0, 0)),
            spec((tokens, 1), lambda k: (0, 0)),
        ],
        scratch_shapes=[
            pltpu.VMEM((tokens, wide + 2 * head), F32),
            pltpu.VMEM((tokens, 1), F32),
        ],
        compiler_params=params(),
        name="project",
    )(place, *parts, cotangent, gain, w_layer, out_layer)


def couple(rows, gain, w_layer, out_layer):
    count, width = rows.shape
    head = out_layer.shape[0]
    wide = w_layer.shape[1]
    step = min(width, 1024)

    def kernel(r_ref, g_ref, w_ref, o_ref, out_ref, acc):
        k = pl.program_id(0)

        @pl.when(k == 0)
        def _():
            acc[...] = jnp.zeros_like(acc)

        r = r_ref[...]
        acc[:, :wide] += dot_nn((r.astype(F32) * g_ref[...]).astype(BF16), w_ref[...])
        acc[:, wide:] += dot_nt(r, o_ref[...])

        @pl.when(k == pl.num_programs(0) - 1)
        def _():
            out_ref[...] = acc[...].astype(BF16)

    return pl.pallas_call(
        kernel,
        grid=(width // step,),
        out_shape=jax.ShapeDtypeStruct((count, wide + head), BF16),
        in_specs=[
            pl.BlockSpec((count, step), lambda k: (0, k)),
            pl.BlockSpec((1, step), lambda k: (0, k)),
            pl.BlockSpec((step, wide), lambda k: (k, 0)),
            pl.BlockSpec((head, step), lambda k: (0, k)),
        ],
        out_specs=pl.BlockSpec((count, wide + head), lambda k: (0, 0)),
        scratch_shapes=[pltpu.VMEM((count, wide + head), F32)],
        compiler_params=params(),
        name="couple",
    )(rows, gain, w_layer, out_layer)


def serial(xz, coupling, norms, mask, section, width, head):
    sections, tokens, _ = xz.shape
    wide = 3 * head
    scale = 1.0 / math.sqrt(head)

    def kernel(s_ref, xz_ref, mg_ref, n_ref, mask_ref, v_ref, t_ref, a_ref, mixes, weights, projs, dmix):
        allowed = mask_ref[...] > 0.5
        norm = n_ref[...]
        rstds, tails = [], []
        for s in range(sections):
            through = xz_ref[s, :, : wide + head].astype(F32)
            if s > 0:
                through = through + dot_nn(mixes[:, : s * head], mg_ref[s, : s * head, :])
            rstd = lax.rsqrt(norm * (1.0 / width) + EPS)
            proj = through[:, :wide] * rstd
            y = through[:, wide:]
            projs[s] = proj.astype(BF16)
            q, k, v = (projs[s, :, i * head : (i + 1) * head] for i in range(3))
            scores = jnp.where(allowed, dot_nt(q, k) * scale, -1e30)
            scores = jnp.exp(scores - jnp.max(scores, axis=1, keepdims=True))
            soft = scores / jnp.sum(scores, axis=1, keepdims=True)
            weights[s] = soft
            mix = dot_nn(soft.astype(BF16), v).astype(BF16)
            mixes[:, s * head : (s + 1) * head] = mix
            tail = y + dot_nn(mix, mg_ref[s, s * head : (s + 1) * head, wide:])
            norm = norm + jnp.sum(mix.astype(F32) * (y + tail), axis=1, keepdims=True)
            norm = jnp.maximum(norm, 0.0)
            rstds.append(rstd)
            tails.append(tail)
            dmix[:, s * head : (s + 1) * head] = xz_ref[s, :, wide + head :].astype(F32)
        mine = s_ref[0]
        total = jnp.zeros((tokens, 1), F32)
        for s in reversed(range(sections)):
            cols = slice(s * head, (s + 1) * head)
            da = (dmix[:, cols] - total * tails[s]).astype(BF16)
            q, k, v = (projs[s, :, i * head : (i + 1) * head] for i in range(3))
            soft = weights[s]
            dv = dot_tn(soft.astype(BF16), da)
            dsoft = dot_nt(da, v)
            dscore = soft * (dsoft - jnp.sum(dsoft * soft, axis=1, keepdims=True))
            dscore = (dscore * scale).astype(BF16)
            dproj = jnp.concatenate([dot_nn(dscore, k), dot_tn(dscore, q), dv], axis=1)
            along = jnp.sum(dproj * projs[s].astype(F32), axis=1, keepdims=True)
            sent = jnp.concatenate(
                [(dproj * rstds[s]), -total * mixes[:, cols].astype(F32)], axis=1
            ).astype(BF16)
            total = total + rstds[s] * rstds[s] * along * (1.0 / width)
            if s > 0:
                dmix[:, : s * head] += dot_nt(sent, mg_ref[s, : s * head, :])

            @pl.when(mine == s)
            def _(sent=sent, total=total):
                v_ref[...] = sent
                t_ref[...] = total

            a_ref[:, cols] = jnp.where(mine > s, mixes[:, cols], jnp.zeros((tokens, head), BF16))

    vmem = pl.BlockSpec(memory_space=pltpu.VMEM)
    return pl.pallas_call(
        kernel,
        out_shape=[
            jax.ShapeDtypeStruct((tokens, wide + head), BF16),
            jax.ShapeDtypeStruct((tokens, 1), F32),
            jax.ShapeDtypeStruct((tokens, sections * head), BF16),
        ],
        in_specs=[pl.BlockSpec(memory_space=pltpu.SMEM)] + [vmem] * 4,
        out_specs=[vmem] * 3,
        scratch_shapes=[
            pltpu.VMEM((tokens, sections * head), BF16),
            pltpu.VMEM((sections, tokens, tokens), F32),
            pltpu.VMEM((sections, tokens, wide), BF16),
            pltpu.VMEM((tokens, sections * head), F32),
        ],
        compiler_params=params(),
        name="serial",
    )(section, xz, coupling, norms, mask)


def widen(sent, total, mixes, lower, x, cotangent, gain, w_layer, out_layer, chunk):
    tokens, width = x.shape
    head = out_layer.shape[0]
    wide = w_layer.shape[1]
    rank = lower.shape[0]

    def kernel(v_ref, t_ref, a_ref, l_ref, x_ref, c_ref, g_ref, w_ref, o_ref, b_ref, f_ref, out_ref, dg_ref):
        back = dot_nt(v_ref[:, :wide], w_ref[...])
        own = back * g_ref[...] + dot_nn(v_ref[:, wide:], o_ref[...])
        here = x_ref[...].astype(F32) + dot_nn(a_ref[...], l_ref[...])
        here = here.astype(BF16).astype(F32)
        full = c_ref[...].astype(F32) + own - t_ref[...] * here
        b_ref[0] = own.astype(BF16)
        f_ref[0] = full
        out_ref[...] = full.astype(BF16)
        dg_ref[...] = jnp.sum(back * here, axis=0, keepdims=True)

    cols = lambda k: (0, k)
    whole = lambda k: (0, 0)
    count = width // chunk
    return pl.pallas_call(
        kernel,
        grid=(count,),
        out_shape=[
            jax.ShapeDtypeStruct((count, tokens, chunk), BF16),
            jax.ShapeDtypeStruct((count, tokens, chunk), F32),
            jax.ShapeDtypeStruct((tokens, width), BF16),
            jax.ShapeDtypeStruct((1, width), F32),
        ],
        in_specs=[
            pl.BlockSpec((tokens, wide + head), whole),
            pl.BlockSpec((tokens, 1), whole),
            pl.BlockSpec((tokens, rank), whole),
            pl.BlockSpec((rank, chunk), cols),
            pl.BlockSpec((tokens, chunk), cols),
            pl.BlockSpec((tokens, chunk), cols),
            pl.BlockSpec((1, chunk), cols),
            pl.BlockSpec((chunk, wide), lambda k: (k, 0)),
            pl.BlockSpec((head, chunk), cols),
        ],
        out_specs=[
            pl.BlockSpec((1, tokens, chunk), lambda k: (k, 0, 0)),
            pl.BlockSpec((1, tokens, chunk), lambda k: (k, 0, 0)),
            pl.BlockSpec((tokens, chunk), cols),
            pl.BlockSpec((1, chunk), cols),
        ],
        compiler_params=params(),
        name="widen",
    )(sent, total, mixes, lower, x, cotangent, gain, w_layer, out_layer)


def join(index, arrived, own, full, out):
    _, tokens, chunk = own.shape

    def kernel(i_ref, r_ref, b_ref, f_ref, _, out_ref, send_ref):
        r = r_ref[...].astype(F32)
        out_ref[...] = (f_ref[0] + r).astype(BF16)
        send_ref[...] = (b_ref[0].astype(F32) + r).astype(BF16)

    return pl.pallas_call(
        kernel,
        grid_spec=pltpu.PrefetchScalarGridSpec(
            num_scalar_prefetch=1,
            grid=(1,),
            in_specs=[
                pl.BlockSpec((tokens, chunk), lambda k, i: (0, 0)),
                pl.BlockSpec((1, tokens, chunk), lambda k, i: (i[0], 0, 0)),
                pl.BlockSpec((1, tokens, chunk), lambda k, i: (i[0], 0, 0)),
                pl.BlockSpec(memory_space=pl.ANY),
            ],
            out_specs=[
                pl.BlockSpec((tokens, chunk), lambda k, i: (0, i[0])),
                pl.BlockSpec((tokens, chunk), lambda k, i: (0, 0)),
            ],
        ),
        out_shape=[
            jax.ShapeDtypeStruct(out.shape, BF16),
            jax.ShapeDtypeStruct((tokens, chunk), BF16),
        ],
        input_output_aliases={4: 0},
        compiler_params=params(),
        name="join",
    )(index, arrived, own, full, out)


STREAMS = 2
CHUNKS = 4


def local(tokens_in, cotangent, gains, w_qkv, w_out, segments, plan):
    sections = lax.axis_size("section")
    groups = lax.axis_size("group")
    plane = lax.axis_size("dp") * groups
    section = lax.axis_index("section")
    member = lax.axis_index("group")
    rows_dev = plan.shape[1]
    length = segments.shape[1]
    tokens, width = tokens_in.shape
    head = w_out.shape[1]
    share = rows_dev // groups
    w_layer, out_layer = w_qkv[0], w_out[0]
    place = member.astype(jnp.int32)[None]

    slice_rows = head // plane
    mine = lax.axis_index("dp") * groups + member
    own_rows = lax.dynamic_slice_in_dim(out_layer, mine * slice_rows, slice_rows, 0)
    slices = lax.all_gather(own_rows, "section")
    slices = slices.reshape(sections * slice_rows, width)

    parts = pick_rows(tokens_in.reshape(rows_dev, length, width), plan, place, groups)
    chosen = jnp.take(segments, plan[0], axis=0, mode="clip").astype(BF16).reshape(groups, share, length)
    moved, moved_seg = [], []
    for r in range(groups):
        if r == 0:
            moved.append(parts[0])
            moved_seg.append(lax.dynamic_index_in_dim(chosen, member, 0, keepdims=False))
            continue
        pairs = [(i, (i + r) % groups) for i in range(groups)]
        outgoing = lax.dynamic_index_in_dim(chosen, (member + r) % groups, 0, keepdims=False)
        moved.append(lax.ppermute(parts[r], "group", pairs))
        moved_seg.append(lax.ppermute(outgoing, "group", pairs))
    moved = [part.reshape(share * length, width) for part in moved]
    order = (member - jnp.arange(groups)) % groups
    seg = jnp.take(jnp.stack(moved_seg), order, axis=0, mode="clip").reshape(tokens)
    at = jnp.arange(tokens)
    mask = (
        (at[:, None] >= at[None, :])
        & (at[:, None] // length == at[None, :] // length)
        & (seg[:, None] == seg[None, :])
    ).astype(F32)

    x, xz, norms = project(moved, cotangent, gains, w_layer, out_layer, place)
    xz_all = lax.all_gather(xz, "section")

    coupling = couple(slices, gains, w_layer, out_layer)
    coupling = lax.all_gather(coupling, ("section", "dp", "group"))
    coupling = coupling.reshape(sections, plane, sections, slice_rows, 4 * head)
    coupling = coupling.transpose(0, 2, 1, 3, 4).reshape(sections, sections * head, 4 * head)
    lower = lax.all_gather(slices, ("dp", "group")).reshape(sections * head, width)

    sent, total, mixes = serial(
        xz_all, coupling, norms, mask, section.astype(jnp.int32)[None], width, head
    )
    mixes = mixes.reshape(tokens, sections, plane, slice_rows).transpose(0, 2, 1, 3)
    mixes = mixes.reshape(tokens, sections * head)

    chunk = width // (STREAMS * CHUNKS)
    own, full, out, gain_part = widen(
        sent, total, mixes, lower, x, cotangent, gains, w_layer, out_layer, chunk
    )
    gain_whole = jnp.sum(lax.all_gather(gain_part, ("dp", "group")), axis=0)

    down = [(i, i - 1) for i in range(1, sections)]
    behind = sections - 1 - section

    def index(tick, stream):
        return jnp.clip(tick - behind, 0, CHUNKS - 1) * STREAMS + stream

    leaving = [
        lax.dynamic_index_in_dim(own, index(0, stream), 0, keepdims=False)
        for stream in range(STREAMS)
    ]
    for tick in range(1, CHUNKS + sections - 1):
        for stream in range(STREAMS):
            arrived = lax.ppermute(leaving[stream], "section", down)
            at_chunk = index(tick, stream).astype(jnp.int32)[None]
            out, leaving[stream] = join(at_chunk, arrived, own, full, out)
    return (out[None], gain_whole)


def attend(hidden, segment, gain_row, w_layer, out_layer):
    count, length, width = hidden.shape
    head = out_layer.shape[0]
    scaled = hidden * lax.rsqrt(jnp.mean(hidden * hidden, axis=-1, keepdims=True) + EPS) * gain_row
    normed = scaled.astype(BF16).reshape(count * length, width)
    projected = jnp.dot(normed, w_layer, preferred_element_type=F32).reshape(count, length, 3 * head)
    query = projected[:, :, :head]
    keyed = projected[:, :, head : 2 * head]
    valued = projected[:, :, 2 * head :]
    positions = jnp.arange(length)
    allowed = (positions[:, None] >= positions[None, :])[None] & (
        segment[:, :, None] == segment[:, None, :]
    )
    scores = jnp.einsum("rid,rjd->rij", query, keyed, precision=lax.Precision.HIGHEST)
    scores = jnp.where(allowed, scores / math.sqrt(head), -1e30)
    weights = jax.nn.softmax(scores, axis=-1)
    mixed = jnp.einsum("rij,rjd->rid", weights, valued, precision=lax.Precision.HIGHEST)
    mixed = mixed.astype(BF16).reshape(count * length, head)
    output = jnp.dot(mixed, out_layer, preferred_element_type=F32).reshape(count, length, width)
    return hidden + output


MB_ROWS = 2


def relay(tokens_in, cotangent, gains, w_qkv, w_out, segments, plan):
    sections = lax.axis_size("section")
    section = lax.axis_index("section")
    rows_dev = plan.shape[1]
    width = tokens_in.shape[1]
    length = segments.shape[1]
    micro = rows_dev // MB_ROWS
    blocks = tokens_in.reshape(rows_dev, length, width)
    chosen = jnp.take(blocks, plan[0], axis=0)
    chosen_seg = jnp.take(segments, plan[0], axis=0).astype(BF16)
    assigned = lax.all_to_all(chosen, "group", split_axis=0, concat_axis=0, tiled=True)
    moved_seg = lax.all_to_all(chosen_seg, "group", split_axis=0, concat_axis=0, tiled=True)
    assigned = assigned.reshape(micro, MB_ROWS, length, width)
    seg_groups = moved_seg.reshape(micro, MB_ROWS, length)
    gain_row, w_layer, out_layer = gains[0], w_qkv[0], w_out[0]
    grad_rows = cotangent.reshape(micro, MB_ROWS, length, width)
    ticks = micro + sections - 1

    def passed_along(array, by):
        pairs = [(i, i + by) for i in range(sections) if 0 <= i + by < sections]
        return lax.ppermute(array, "section", pairs)

    def at(array, i):
        return lax.dynamic_index_in_dim(array, i, 0, keepdims=False)

    def forward_tick(tick, carry):
        saved, arrived = carry
        index = tick - section
        valid = (index >= 0) & (index < micro)
        clipped = jnp.clip(index, 0, micro - 1)
        entering = jnp.where(section == 0, at(assigned, clipped), arrived)
        kept = jnp.where(valid, entering, at(saved, clipped))
        saved = lax.dynamic_update_index_in_dim(saved, kept, clipped, 0)
        segment = at(seg_groups, clipped)

        def run_layer(value):
            return attend(value.astype(F32), segment, gain_row, w_layer, out_layer).astype(BF16)

        leaving = lax.cond(valid, run_layer, jnp.zeros_like, entering)
        return (saved, passed_along(leaving, 1))

    saved_init = jnp.zeros((micro, MB_ROWS, length, width), BF16)
    arrive_init = jnp.zeros((MB_ROWS, length, width), BF16)
    saved, _ = lax.fori_loop(0, ticks, forward_tick, (saved_init, arrive_init))

    def backward_tick(tick, carry):
        grads_x, gain_total, arrived = carry
        index = tick - (sections - 1 - section)
        valid = (index >= 0) & (index < micro)
        clipped = jnp.clip(index, 0, micro - 1)
        entering = jnp.where(section == sections - 1, at(grad_rows, clipped), arrived)
        segment = at(seg_groups, clipped)
        stored = at(saved, clipped).astype(F32)

        def local_layer(hidden, gains_here):
            return attend(hidden, segment, gains_here, w_layer, out_layer)

        def run_back(value):
            _, pullback = jax.vjp(local_layer, stored, gain_row)
            grad_hidden, grad_gain = pullback(value.astype(F32))
            return (grad_hidden.astype(BF16), grad_gain)

        def skip_back(value):
            return (jnp.zeros_like(value), jnp.zeros(gain_row.shape, F32))

        sending, grad_gain = lax.cond(valid, run_back, skip_back, entering)
        kept = jnp.where(valid, sending, at(grads_x, clipped))
        grads_x = lax.dynamic_update_index_in_dim(grads_x, kept, clipped, 0)
        return (grads_x, gain_total + grad_gain, passed_along(sending, -1))

    gain_init = jnp.zeros(gain_row.shape, F32)
    grads_x, gain_total, _ = lax.fori_loop(
        0, ticks, backward_tick, (saved_init, gain_init, arrive_init)
    )
    gain_whole = lax.psum(gain_total, ("dp", "group"))
    return (grads_x.reshape(1, rows_dev * length, width), gain_whole[None])


def solution(mesh):
    placed = (
        P(("dp", "group"), None),
        P(("dp", "group"), None),
        P("section", None),
        P("section", None, None),
        P("section", None, None),
        P(("dp", "group"), None),
        P(("dp", "group"), None),
    )

    def chosen(tokens_in, cotangent, gains, w_qkv, w_out, segments, plan):
        sections, head, width = w_out.shape
        body = local if sections * 4 * head < width else relay
        return jax.shard_map(
            body,
            mesh=mesh,
            in_specs=placed,
            out_specs=(P("section", ("dp", "group"), None), P("section", None)),
            check_vma=False,
        )(tokens_in, cotangent, gains, w_qkv, w_out, segments, plan)

    return chosen
```

```python
import functools
import math

import jax
import jax.numpy as jnp
from jax import lax
from jax.experimental import pallas as pl
from jax.experimental.pallas import tpu as pltpu
from jax.sharding import PartitionSpec as P

EPS = 1e-05
VMEM_BYTES = 48 * 1024 * 1024
F32 = jnp.float32
BF16 = jnp.bfloat16


def dot_nn(a, b):
    return lax.dot_general(a, b, (((1,), (0,)), ((), ())), preferred_element_type=F32)


def dot_nt(a, b):
    return lax.dot_general(a, b, (((1,), (1,)), ((), ())), preferred_element_type=F32)


def dot_tn(a, b):
    return lax.dot_general(a, b, (((0,), (0,)), ((), ())), preferred_element_type=F32)


def params():
    return pltpu.CompilerParams(vmem_limit_bytes=VMEM_BYTES)


def pick_rows(tokens, plan, place, groups):
    rows, length, width = tokens.shape
    share = rows // groups

    def kernel(plan_ref, place_ref, tokens_ref, *rest):
        parts, sems = rest[:groups], rest[groups]
        copies = []
        for r in range(groups):
            target = lax.rem(place_ref[0] + r, groups)
            for c in range(share):
                row = plan_ref[0, target * share + c]
                copy = pltpu.make_async_copy(
                    tokens_ref.at[row], parts[r].at[c], sems.at[r * share + c]
                )
                copy.start()
                copies.append(copy)
        for copy in copies:
            copy.wait()

    return pl.pallas_call(
        kernel,
        out_shape=[jax.ShapeDtypeStruct((share, length, width), BF16)] * groups,
        in_specs=[
            pl.BlockSpec(memory_space=pltpu.SMEM),
            pl.BlockSpec(memory_space=pltpu.SMEM),
            pl.BlockSpec(memory_space=pl.ANY),
        ],
        out_specs=[pl.BlockSpec(memory_space=pl.ANY)] * groups,
        scratch_shapes=[pltpu.SemaphoreType.DMA((rows,))],
        compiler_params=params(),
        name="pick_rows",
    )(plan, place, tokens)


def project(parts, cotangent, gain, w_layer, out_layer, place):
    groups = len(parts)
    tokens, width = cotangent.shape
    head = out_layer.shape[0]
    wide = w_layer.shape[1]
    block = tokens // groups
    step = min(width, 1024)

    def kernel(place_ref, *refs):
        part_refs = refs[:groups]
        cot_ref, g_ref, w_ref, o_ref, x_ref, xz_ref, n_ref, acc, square = refs[groups:]
        k = pl.program_id(0)

        @pl.when(k == 0)
        def _():
            acc[...] = jnp.zeros_like(acc)
            square[...] = jnp.zeros_like(square)

        for r in range(groups):
            source = lax.rem(place_ref[0] + groups - r, groups)
            rows = pl.ds(pl.multiple_of(source * block, block), block)
            x_ref[rows, :] = part_refs[r][...]
        x = x_ref[...]
        xf = x.astype(F32)
        acc[:, :wide] += dot_nn((xf * g_ref[...]).astype(BF16), w_ref[...])
        acc[:, wide : wide + head] += dot_nt(x, o_ref[...])
        acc[:, wide + head :] += dot_nt(cot_ref[...], o_ref[...])
        square[...] += jnp.sum(xf * xf, axis=1, keepdims=True)

        @pl.when(k == pl.num_programs(0) - 1)
        def _():
            xz_ref[...] = acc[...].astype(BF16)
            n_ref[...] = square[...]

    spec = lambda shape, index: pl.BlockSpec(shape, index)
    return pl.pallas_call(
        kernel,
        grid=(width // step,),
        out_shape=[
            jax.ShapeDtypeStruct((tokens, width), BF16),
            jax.ShapeDtypeStruct((tokens, wide + 2 * head), BF16),
            jax.ShapeDtypeStruct((tokens, 1), F32),
        ],
        in_specs=[pl.BlockSpec(memory_space=pltpu.SMEM)]
        + [spec((block, step), lambda k: (0, k))] * groups
        + [
            spec((tokens, step), lambda k: (0, k)),
            spec((1, step), lambda k: (0, k)),
            spec((step, wide), lambda k: (k, 0)),
            spec((head, step), lambda k: (0, k)),
        ],
        out_specs=[
            spec((tokens, step), lambda k: (0, k)),
            spec((tokens, wide + 2 * head), lambda k: (0, 0)),
            spec((tokens, 1), lambda k: (0, 0)),
        ],
        scratch_shapes=[
            pltpu.VMEM((tokens, wide + 2 * head), F32),
            pltpu.VMEM((tokens, 1), F32),
        ],
        compiler_params=params(),
        name="project",
    )(place, *parts, cotangent, gain, w_layer, out_layer)


def couple(slices, gain, w_layer, out_layer, last):
    sections = len(slices)
    count, width = slices[0].shape
    head = out_layer.shape[0]
    wide = w_layer.shape[1]
    step = min(width, 1024)
    below = (sections - 2) * wide
    packed = below + max(wide, (sections - 1) * head)

    def kernel(last_ref, *refs):
        r_refs = refs[:sections]
        g_ref, w_ref, o_ref, out_ref, acc = refs[sections:]
        k = pl.program_id(0)

        @pl.when(k == 0)
        def _():
            acc[...] = jnp.zeros_like(acc)

        r = jnp.concatenate([ref[...] for ref in r_refs], axis=0)
        acc[:, :wide] += dot_nn((r.astype(F32) * g_ref[...]).astype(BF16), w_ref[...])
        acc[:, wide:] += dot_nt(r, o_ref[...])

        @pl.when(k == pl.num_programs(0) - 1)
        def _():
            out_ref[...] = jnp.zeros_like(out_ref)
            rows = [slice(r * count, (r + 1) * count) for r in range(sections)]
            for r in range(1, sections - 1):
                out_ref[:, (r - 1) * wide : r * wide] = acc[rows[r], :wide].astype(BF16)

            @pl.when(last_ref[0] == 1)
            def _():
                out_ref[:, below : below + wide] = acc[rows[-1], :wide].astype(BF16)

            @pl.when(last_ref[0] == 0)
            def _():
                for r in range(sections - 1):
                    cols = slice(below + r * head, below + (r + 1) * head)
                    out_ref[:, cols] = acc[rows[r], wide:].astype(BF16)

    return pl.pallas_call(
        kernel,
        grid=(width // step,),
        out_shape=jax.ShapeDtypeStruct((count, packed), BF16),
        in_specs=[pl.BlockSpec(memory_space=pltpu.SMEM)]
        + [pl.BlockSpec((count, step), lambda k: (0, k))] * sections
        + [
            pl.BlockSpec((1, step), lambda k: (0, k)),
            pl.BlockSpec((step, wide), lambda k: (k, 0)),
            pl.BlockSpec((head, step), lambda k: (0, k)),
        ],
        out_specs=pl.BlockSpec((count, packed), lambda k: (0, 0)),
        scratch_shapes=[pltpu.VMEM((sections * count, wide + head), F32)],
        compiler_params=params(),
        name="couple",
    )(last, *slices, gain, w_layer, out_layer)


def serial(xz, pieces, places, norms, mask, section, width, head):
    sections = len(xz)
    tokens = norms.shape[0]
    wide = 3 * head
    scale = 1.0 / math.sqrt(head)
    below = (sections - 2) * wide
    count, packed = pieces[0].shape[-2:]
    plane = head // count
    n_in = sections + len(pieces)
    copies = sections + sections * plane

    def kernel(s_ref, p_ref, *refs):
        xz_refs, piece_refs = refs[:sections], refs[sections:n_in]
        n_ref, mask_ref, v_ref, t_ref, a_ref = refs[n_in : n_in + 5]
        xz_all, table, mixes, weights, projs, dmix, sems = refs[n_in + 5 :]
        mine = s_ref[0]
        started = []

        def start(source, target):
            copy = pltpu.make_async_copy(source, target, sems.at[len(started)])
            copy.start()
            started.append(copy)

        for r in range(sections):
            start(xz_refs[r], xz_all.at[lax.rem(mine + sections - r, sections)])
        at = 0
        for ref in piece_refs:
            for i in range(ref.shape[0]):
                for r in range(sections):
                    start(ref.at[i, r], table.at[lax.rem(mine + sections - r, sections), p_ref[at]])
                at += 1
        for copy in started:
            copy.wait()

        def through(j, k):
            return table[k, :, :, (k - j - 1) * wide : (k - j) * wide].reshape(head, wide)

        def across(j, k):
            cols = slice(below + (k - j) * head, below + (k - j + 1) * head)
            return table[k, :, :, cols].reshape(head, head)

        allowed = mask_ref[...] > 0.5
        norm = n_ref[...]
        rstds, tails, mixed = [], [], []
        for s in range(sections):
            proj = xz_all[s, :, :wide].astype(F32)
            for j in range(s):
                proj = proj + dot_nn(mixed[j], through(j, s))
            rstd = lax.rsqrt(norm * (1.0 / width) + EPS)
            proj = proj * rstd
            projs[s] = proj.astype(BF16)
            q, k, v = (projs[s, :, i * head : (i + 1) * head] for i in range(3))
            scores = jnp.where(allowed, dot_nt(q, k) * scale, -1e30)
            scores = jnp.exp(scores - jnp.max(scores, axis=1, keepdims=True))
            soft = scores / jnp.sum(scores, axis=1, keepdims=True)
            weights[s] = soft
            mix = dot_nn(soft.astype(BF16), v).astype(BF16)
            mixed.append(mix)
            mixes[:, s * head : (s + 1) * head] = mix
            rstds.append(rstd)
            dmix[:, s * head : (s + 1) * head] = xz_all[s, :, wide + head :].astype(F32)
            if s == sections - 1:
                break
            y = xz_all[s, :, wide : wide + head].astype(F32)
            for j in range(s):
                y = y + dot_nn(mixed[j], across(j, s))
            tail = y + dot_nn(mix, across(s, s))
            norm = norm + jnp.sum(mix.astype(F32) * (y + tail), axis=1, keepdims=True)
            norm = jnp.maximum(norm, 0.0)
            tails.append(tail)
        total = jnp.zeros((tokens, 1), F32)
        for s in reversed(range(sections)):
            cols = slice(s * head, (s + 1) * head)
            da = dmix[:, cols]
            if s < sections - 1:
                da = da - total * tails[s]
            da = da.astype(BF16)
            q, k, v = (projs[s, :, i * head : (i + 1) * head] for i in range(3))
            soft = weights[s]
            dv = dot_tn(soft.astype(BF16), da)
            dsoft = dot_nt(da, v)
            dscore = soft * (dsoft - jnp.sum(dsoft * soft, axis=1, keepdims=True))
            dscore = (dscore * scale).astype(BF16)
            dproj = jnp.concatenate([dot_nn(dscore, k), dot_tn(dscore, q), dv], axis=1)
            along = jnp.sum(dproj * projs[s].astype(F32), axis=1, keepdims=True)
            first = (dproj * rstds[s]).astype(BF16)
            second = (-total * mixes[:, cols].astype(F32)).astype(BF16)
            total = total + rstds[s] * rstds[s] * along * (1.0 / width)
            for j in reversed(range(s)):
                term = dot_nt(first, through(j, s))
                if s < sections - 1:
                    term = term + dot_nt(second, across(j, s))
                dmix[:, j * head : (j + 1) * head] += term

            @pl.when(mine == s)
            def _(first=first, second=second, total=total):
                v_ref[:, :wide] = first
                v_ref[:, wide:] = second
                t_ref[...] = total

            a_ref[:, cols] = jnp.where(mine > s, mixes[:, cols], jnp.zeros((tokens, head), BF16))

    vmem = pl.BlockSpec(memory_space=pltpu.VMEM)
    smem = pl.BlockSpec(memory_space=pltpu.SMEM)
    return pl.pallas_call(
        kernel,
        out_shape=[
            jax.ShapeDtypeStruct((tokens, wide + head), BF16),
            jax.ShapeDtypeStruct((tokens, 1), F32),
            jax.ShapeDtypeStruct((tokens, sections * head), BF16),
        ],
        in_specs=[smem, smem] + [pl.BlockSpec(memory_space=pl.ANY)] * n_in + [vmem, vmem],
        out_specs=[vmem] * 3,
        scratch_shapes=[
            pltpu.VMEM((sections,) + xz[0].shape, BF16),
            pltpu.VMEM((sections, plane, count, packed), BF16),
            pltpu.VMEM((tokens, sections * head), BF16),
            pltpu.VMEM((sections, tokens, tokens), F32),
            pltpu.VMEM((sections, tokens, wide), BF16),
            pltpu.VMEM((tokens, sections * head), F32),
            pltpu.SemaphoreType.DMA((copies,)),
        ],
        compiler_params=params(),
        name="serial",
    )(section, places, *xz, *pieces, norms, mask)


def widen(sent, gain, w_layer, out_layer, chunk):
    tokens = sent.shape[0]
    head, width = out_layer.shape
    wide = w_layer.shape[1]

    def kernel(v_ref, g_ref, w_ref, o_ref, b_ref):
        own = dot_nt(v_ref[:, :wide], w_ref[...]) * g_ref[...]
        b_ref[0] = (own + dot_nn(v_ref[:, wide:], o_ref[...])).astype(BF16)

    return pl.pallas_call(
        kernel,
        grid=(width // chunk,),
        out_shape=jax.ShapeDtypeStruct((width // chunk, tokens, chunk), BF16),
        in_specs=[
            pl.BlockSpec((tokens, wide + head), lambda k: (0, 0)),
            pl.BlockSpec((1, chunk), lambda k: (0, k)),
            pl.BlockSpec((chunk, wide), lambda k: (k, 0)),
            pl.BlockSpec((head, chunk), lambda k: (0, k)),
        ],
        out_specs=pl.BlockSpec((1, tokens, chunk), lambda k: (k, 0, 0)),
        compiler_params=params(),
        name="widen",
    )(sent, gain, w_layer, out_layer)


def settle(sent, total, mixes, lower, x, cotangent, gain, w_layer, out_layer, chunk):
    tokens, width = x.shape
    head = out_layer.shape[0]
    wide = w_layer.shape[1]
    rank = lower.shape[0]

    def kernel(v_ref, t_ref, a_ref, l_ref, x_ref, c_ref, g_ref, w_ref, o_ref, f_ref, out_ref, dg_ref):
        back = dot_nt(v_ref[:, :wide], w_ref[...])
        own = back * g_ref[...] + dot_nn(v_ref[:, wide:], o_ref[...])
        here = x_ref[...].astype(F32) + dot_nn(a_ref[...], l_ref[...])
        full = c_ref[...].astype(F32) + own - t_ref[...] * here
        f_ref[0] = full
        out_ref[...] = full.astype(BF16)
        dg_ref[...] = jnp.sum(back * here, axis=0, keepdims=True)

    cols = lambda k: (0, k)
    whole = lambda k: (0, 0)
    count = width // chunk
    return pl.pallas_call(
        kernel,
        grid=(count,),
        out_shape=[
            jax.ShapeDtypeStruct((count, tokens, chunk), F32),
            jax.ShapeDtypeStruct((tokens, width), BF16),
            jax.ShapeDtypeStruct((1, width), F32),
        ],
        in_specs=[
            pl.BlockSpec((tokens, wide + head), whole),
            pl.BlockSpec((tokens, 1), whole),
            pl.BlockSpec((tokens, rank), whole),
            pl.BlockSpec((rank, chunk), cols),
            pl.BlockSpec((tokens, chunk), cols),
            pl.BlockSpec((tokens, chunk), cols),
            pl.BlockSpec((1, chunk), cols),
            pl.BlockSpec((chunk, wide), lambda k: (k, 0)),
            pl.BlockSpec((head, chunk), cols),
        ],
        out_specs=[
            pl.BlockSpec((1, tokens, chunk), lambda k: (k, 0, 0)),
            pl.BlockSpec((tokens, chunk), cols),
            pl.BlockSpec((1, chunk), cols),
        ],
        compiler_params=params(),
        name="settle",
    )(sent, total, mixes, lower, x, cotangent, gain, w_layer, out_layer)


def send_on(index, arrived, own):
    _, tokens, chunk = own.shape

    def kernel(i_ref, r_ref, b_ref, send_ref):
        send_ref[...] = (b_ref[0].astype(F32) + r_ref[...].astype(F32)).astype(BF16)

    return pl.pallas_call(
        kernel,
        grid_spec=pltpu.PrefetchScalarGridSpec(
            num_scalar_prefetch=1,
            grid=(1,),
            in_specs=[
                pl.BlockSpec((tokens, chunk), lambda k, i: (0, 0)),
                pl.BlockSpec((1, tokens, chunk), lambda k, i: (i[0], 0, 0)),
            ],
            out_specs=pl.BlockSpec((tokens, chunk), lambda k, i: (0, 0)),
        ),
        out_shape=jax.ShapeDtypeStruct((tokens, chunk), BF16),
        compiler_params=params(),
        name="send_on",
    )(index, arrived, own)


def put_out(index, arrived, full, out):
    _, tokens, chunk = full.shape

    def kernel(i_ref, r_ref, f_ref, _, out_ref):
        out_ref[...] = (f_ref[0] + r_ref[...].astype(F32)).astype(BF16)

    return pl.pallas_call(
        kernel,
        grid_spec=pltpu.PrefetchScalarGridSpec(
            num_scalar_prefetch=1,
            grid=(1,),
            in_specs=[
                pl.BlockSpec((tokens, chunk), lambda k, i: (0, 0)),
                pl.BlockSpec((1, tokens, chunk), lambda k, i: (i[0], 0, 0)),
                pl.BlockSpec(memory_space=pl.ANY),
            ],
            out_specs=pl.BlockSpec((tokens, chunk), lambda k, i: (0, i[0])),
        ),
        out_shape=jax.ShapeDtypeStruct(out.shape, BF16),
        input_output_aliases={3: 0},
        compiler_params=params(),
        name="put_out",
    )(index, arrived, full, out)


STREAMS = 2
CHUNKS = 4


def shifted(array, by):
    sections = lax.axis_size("section")
    return lax.ppermute(array, "section", [(i, (i + by) % sections) for i in range(sections)])


def raised(array, by):
    sections = lax.axis_size("section")
    return lax.ppermute(array, "section", [(i, i + by) for i in range(sections - by)])


def swapped(array, step):
    groups = lax.axis_size("group")
    devices = lax.axis_size("dp")
    bits = devices.bit_length() - 1
    pairs = []
    for p in range(devices):
        for g in range(groups):
            pairs.append((p * groups + g, (p ^ (1 << ((step + g) % bits))) * groups + g))
    return lax.ppermute(array, ("dp", "group"), pairs)


def handed(array, by):
    groups = lax.axis_size("group")
    return lax.ppermute(array, "group", [(i, (i + by) % groups) for i in range(groups)])


def spread(array):
    bits = lax.axis_size("dp").bit_length() - 1
    stacks = [array[None]]
    for step in range(bits):
        together = stacks[0] if step == 0 else jnp.concatenate([together, stacks[-1]], axis=0)
        stacks.append(swapped(together, step))
    stacks = stacks[-1:] if bits == 0 else [together, stacks[-1]]
    for r in range(1, lax.axis_size("group")):
        stacks = stacks + [handed(stack, r) for stack in stacks[:2]]
    return stacks


def plane_places():
    groups = lax.axis_size("group")
    bits = lax.axis_size("dp").bit_length() - 1
    masks = []
    for g in range(groups):
        order = [0]
        for step in range(bits):
            order = order + [m ^ (1 << ((step + g) % bits)) for m in order]
        masks.append(order)
    masks = jnp.asarray(masks, jnp.int32)
    dp, member = lax.axis_index("dp"), lax.axis_index("group")
    places = []
    for r in range(groups):
        giver = (member + groups - r) % groups
        places.append((dp ^ masks[giver]) * groups + giver)
    return jnp.concatenate(places).astype(jnp.int32)


def local(tokens_in, cotangent, gains, w_qkv, w_out, segments, plan):
    sections = lax.axis_size("section")
    groups = lax.axis_size("group")
    devices = lax.axis_size("dp")
    plane = devices * groups
    section = lax.axis_index("section")
    member = lax.axis_index("group")
    rows_dev = plan.shape[1]
    length = segments.shape[1]
    tokens, width = tokens_in.shape
    head = w_out.shape[1]
    share = rows_dev // groups
    w_layer, out_layer = w_qkv[0], w_out[0]
    place = member.astype(jnp.int32)[None]
    layer = section.astype(jnp.int32)[None]

    slice_rows = head // plane
    mine = lax.axis_index("dp") * groups + member
    own_rows = lax.dynamic_slice_in_dim(out_layer, mine * slice_rows, slice_rows, 0)
    slices = [own_rows] + [raised(own_rows, r) for r in range(1, sections)]

    parts = pick_rows(tokens_in.reshape(rows_dev, length, width), plan, place, groups)
    chosen = jnp.take(segments, plan[0], axis=0, mode="clip").astype(BF16)
    chosen = chosen.reshape(groups, share, length)
    moved, moved_seg = [], []
    for r in range(groups):
        outgoing = lax.dynamic_index_in_dim(chosen, (member + r) % groups, 0, keepdims=False)
        moved.append(handed(parts[r], r) if r else parts[r])
        moved_seg.append(handed(outgoing, r) if r else outgoing)
    moved = [part.reshape(share * length, width) for part in moved]
    order = (member - jnp.arange(groups)) % groups
    seg = jnp.take(jnp.stack(moved_seg), order, axis=0, mode="clip").reshape(tokens)
    at = jnp.arange(tokens)
    mask = (
        (at[:, None] >= at[None, :])
        & (at[:, None] // length == at[None, :] // length)
        & (seg[:, None] == seg[None, :])
    ).astype(F32)

    x, xz, norms = project(moved, cotangent, gains, w_layer, out_layer, place)

    last = (section == sections - 1).astype(jnp.int32)[None]
    coupling = couple(slices, gains, w_layer, out_layer, last)
    xz, coupling = lax.optimization_barrier((xz, coupling))
    coupling = jnp.stack([coupling] + [shifted(coupling, r) for r in range(1, sections)])
    pieces = spread(coupling)
    xz_all = [xz] + [shifted(xz, r) for r in range(1, sections)]
    places = plane_places()

    sent, total, mixes = serial(xz_all, pieces, places, norms, mask, layer, width, head)

    chunk = width // (STREAMS * CHUNKS)
    own = widen(sent, gains, w_layer, out_layer, chunk)

    down = [(i, i - 1) for i in range(1, sections)]
    behind = sections - 1 - section

    def index(tick, stream):
        return (jnp.clip(tick - behind, 0, CHUNKS - 1) * STREAMS + stream).astype(jnp.int32)

    leaving = [
        lax.dynamic_index_in_dim(own, index(0, stream), 0, keepdims=False)
        for stream in range(STREAMS)
    ]
    arrivals = []
    ticks = CHUNKS + sections - 1
    for tick in range(1, ticks):
        for stream in range(STREAMS):
            arrived = lax.ppermute(leaving[stream], "section", down)
            at_chunk = index(tick, stream)[None]
            arrivals.append((at_chunk, arrived))
            if tick < ticks - 1:
                leaving[stream] = send_on(at_chunk, arrived, own)

    stacks = spread(jnp.concatenate(slices[1:], axis=0))
    lower = jnp.concatenate(stacks, axis=0).reshape(plane * (sections - 1) * slice_rows, width)
    mixes = mixes.reshape(tokens, sections, plane, slice_rows)
    below = (section - 1 - jnp.arange(sections - 1)) % sections
    mixes = jnp.take(jnp.take(mixes, below, axis=1, mode="clip"), places, axis=2, mode="clip")
    mixes = mixes.transpose(0, 2, 1, 3).reshape(tokens, plane * (sections - 1) * slice_rows)
    full, out, gain = settle(
        sent, total, mixes, lower, x, cotangent, gains, w_layer, out_layer, chunk
    )
    for step in range(devices.bit_length() - 1):
        gain = gain + swapped(gain, step)
    gain_whole = sum([handed(gain, r) for r in range(1, groups)], gain)

    for at_chunk, arrived in arrivals:
        out = put_out(at_chunk, arrived, full, out)
    return (out[None], gain_whole)


def attend(hidden, segment, gain_row, w_layer, out_layer):
    count, length, width = hidden.shape
    head = out_layer.shape[0]
    scaled = hidden * lax.rsqrt(jnp.mean(hidden * hidden, axis=-1, keepdims=True) + EPS) * gain_row
    normed = scaled.astype(BF16).reshape(count * length, width)
    projected = jnp.dot(normed, w_layer, preferred_element_type=F32).reshape(count, length, 3 * head)
    query = projected[:, :, :head]
    keyed = projected[:, :, head : 2 * head]
    valued = projected[:, :, 2 * head :]
    positions = jnp.arange(length)
    allowed = (positions[:, None] >= positions[None, :])[None] & (
        segment[:, :, None] == segment[:, None, :]
    )
    scores = jnp.einsum("rid,rjd->rij", query, keyed, precision=lax.Precision.HIGHEST)
    scores = jnp.where(allowed, scores / math.sqrt(head), -1e30)
    weights = jax.nn.softmax(scores, axis=-1)
    mixed = jnp.einsum("rij,rjd->rid", weights, valued, precision=lax.Precision.HIGHEST)
    mixed = mixed.astype(BF16).reshape(count * length, head)
    output = jnp.dot(mixed, out_layer, preferred_element_type=F32).reshape(count, length, width)
    return hidden + output


MB_ROWS = 2


def relay(tokens_in, cotangent, gains, w_qkv, w_out, segments, plan):
    sections = lax.axis_size("section")
    section = lax.axis_index("section")
    rows_dev = plan.shape[1]
    width = tokens_in.shape[1]
    length = segments.shape[1]
    micro = rows_dev // MB_ROWS
    blocks = tokens_in.reshape(rows_dev, length, width)
    chosen = jnp.take(blocks, plan[0], axis=0)
    chosen_seg = jnp.take(segments, plan[0], axis=0).astype(BF16)
    assigned = lax.all_to_all(chosen, "group", split_axis=0, concat_axis=0, tiled=True)
    moved_seg = lax.all_to_all(chosen_seg, "group", split_axis=0, concat_axis=0, tiled=True)
    assigned = assigned.reshape(micro, MB_ROWS, length, width)
    seg_groups = moved_seg.reshape(micro, MB_ROWS, length)
    gain_row, w_layer, out_layer = gains[0], w_qkv[0], w_out[0]
    grad_rows = cotangent.reshape(micro, MB_ROWS, length, width)
    ticks = micro + sections - 1

    def passed_along(array, by):
        pairs = [(i, i + by) for i in range(sections) if 0 <= i + by < sections]
        return lax.ppermute(array, "section", pairs)

    def at(array, i):
        return lax.dynamic_index_in_dim(array, i, 0, keepdims=False)

    def forward_tick(tick, carry):
        saved, arrived = carry
        index = tick - section
        valid = (index >= 0) & (index < micro)
        clipped = jnp.clip(index, 0, micro - 1)
        entering = jnp.where(section == 0, at(assigned, clipped), arrived)
        kept = jnp.where(valid, entering, at(saved, clipped))
        saved = lax.dynamic_update_index_in_dim(saved, kept, clipped, 0)
        segment = at(seg_groups, clipped)

        def run_layer(value):
            return attend(value.astype(F32), segment, gain_row, w_layer, out_layer).astype(BF16)

        leaving = lax.cond(valid, run_layer, jnp.zeros_like, entering)
        return (saved, passed_along(leaving, 1))

    saved_init = jnp.zeros((micro, MB_ROWS, length, width), BF16)
    arrive_init = jnp.zeros((MB_ROWS, length, width), BF16)
    saved, _ = lax.fori_loop(0, ticks, forward_tick, (saved_init, arrive_init))

    def backward_tick(tick, carry):
        grads_x, gain_total, arrived = carry
        index = tick - (sections - 1 - section)
        valid = (index >= 0) & (index < micro)
        clipped = jnp.clip(index, 0, micro - 1)
        entering = jnp.where(section == sections - 1, at(grad_rows, clipped), arrived)
        segment = at(seg_groups, clipped)
        stored = at(saved, clipped).astype(F32)

        def local_layer(hidden, gains_here):
            return attend(hidden, segment, gains_here, w_layer, out_layer)

        def run_back(value):
            _, pullback = jax.vjp(local_layer, stored, gain_row)
            grad_hidden, grad_gain = pullback(value.astype(F32))
            return (grad_hidden.astype(BF16), grad_gain)

        def skip_back(value):
            return (jnp.zeros_like(value), jnp.zeros(gain_row.shape, F32))

        sending, grad_gain = lax.cond(valid, run_back, skip_back, entering)
        kept = jnp.where(valid, sending, at(grads_x, clipped))
        grads_x = lax.dynamic_update_index_in_dim(grads_x, kept, clipped, 0)
        return (grads_x, gain_total + grad_gain, passed_along(sending, -1))

    gain_init = jnp.zeros(gain_row.shape, F32)
    grads_x, gain_total, _ = lax.fori_loop(
        0, ticks, backward_tick, (saved_init, gain_init, arrive_init)
    )
    gain_whole = lax.psum(gain_total, ("dp", "group"))
    return (grads_x.reshape(1, rows_dev * length, width), gain_whole[None])


def solution(mesh):
    placed = (
        P(("dp", "group"), None),
        P(("dp", "group"), None),
        P("section", None),
        P("section", None, None),
        P("section", None, None),
        P(("dp", "group"), None),
        P(("dp", "group"), None),
    )

    def chosen(tokens_in, cotangent, gains, w_qkv, w_out, segments, plan):
        sections, head, width = w_out.shape
        devices = mesh.shape["dp"]
        small = sections * 4 * head < width and devices & (devices - 1) == 0
        body = local if small and sections > 1 else relay
        return jax.shard_map(
            body,
            mesh=mesh,
            in_specs=placed,
            out_specs=(P("section", ("dp", "group"), None), P("section", None)),
            check_vma=False,
        )(tokens_in, cotangent, gains, w_qkv, w_out, segments, plan)

    return chosen
```

```python
import math

import jax
import jax.numpy as jnp
from jax import lax
from jax.experimental import pallas as pl
from jax.experimental.pallas import tpu as pltpu
from jax.sharding import PartitionSpec as P

EPS = 1e-05
VMEM_BYTES = 16 * 1024 * 1024
F32 = jnp.float32
BF16 = jnp.bfloat16


def dot_nn(a, b):
    return lax.dot_general(a, b, (((1,), (0,)), ((), ())), preferred_element_type=F32)


def dot_nt(a, b):
    return lax.dot_general(a, b, (((1,), (1,)), ((), ())), preferred_element_type=F32)


def dot_tn(a, b):
    return lax.dot_general(a, b, (((0,), (0,)), ((), ())), preferred_element_type=F32)


def tied(array, *others):
    return lax.optimization_barrier((array,) + others)[0]


def params():
    return pltpu.CompilerParams(vmem_limit_bytes=VMEM_BYTES)


def pick_rows(tokens, plan, place, groups):
    rows, length, width = tokens.shape
    share = rows // groups

    def kernel(plan_ref, place_ref, tokens_ref, *rest):
        parts, sems = rest[:groups], rest[groups]
        copies = []
        for r in range(groups):
            target = lax.rem(place_ref[0] + r, groups)
            for c in range(share):
                row = plan_ref[0, target * share + c]
                copy = pltpu.make_async_copy(
                    tokens_ref.at[row], parts[r].at[c], sems.at[r * share + c]
                )
                copy.start()
                copies.append(copy)
        for copy in copies:
            copy.wait()

    return pl.pallas_call(
        kernel,
        out_shape=[jax.ShapeDtypeStruct((share, length, width), BF16)] * groups,
        in_specs=[
            pl.BlockSpec(memory_space=pltpu.SMEM),
            pl.BlockSpec(memory_space=pltpu.SMEM),
            pl.BlockSpec(memory_space=pl.ANY),
        ],
        out_specs=[pl.BlockSpec(memory_space=pl.ANY)] * groups,
        scratch_shapes=[pltpu.SemaphoreType.DMA((rows,))],
        compiler_params=params(),
        name="pick_rows",
    )(plan, place, tokens)


def project(parts, cotangent, gain, w_layer, out_layer, place):
    groups = len(parts)
    tokens, width = cotangent.shape
    head = out_layer.shape[0]
    wide = w_layer.shape[1]
    block = tokens // groups
    step = min(width, 1024)

    def kernel(place_ref, *refs):
        part_refs = refs[:groups]
        cot_ref, g_ref, w_ref, o_ref, x_ref, xz_ref, n_ref, acc, square = refs[groups:]
        k = pl.program_id(0)

        @pl.when(k == 0)
        def _():
            acc[...] = jnp.zeros_like(acc)
            square[...] = jnp.zeros_like(square)

        for r in range(groups):
            source = lax.rem(place_ref[0] + groups - r, groups)
            rows = pl.ds(pl.multiple_of(source * block, block), block)
            x_ref[rows, :] = part_refs[r][...]
        x = x_ref[...]
        xf = x.astype(F32)
        acc[:, :wide] += dot_nn((xf * g_ref[...]).astype(BF16), w_ref[...])
        acc[:, wide : wide + head] += dot_nt(x, o_ref[...])
        acc[:, wide + head :] += dot_nt(cot_ref[...], o_ref[...])
        square[...] += jnp.sum(xf * xf, axis=1, keepdims=True)

        @pl.when(k == pl.num_programs(0) - 1)
        def _():
            xz_ref[...] = acc[...].astype(BF16)
            n_ref[...] = square[...]

    spec = lambda shape, index: pl.BlockSpec(shape, index)
    return pl.pallas_call(
        kernel,
        grid=(width // step,),
        out_shape=[
            jax.ShapeDtypeStruct((tokens, width), BF16),
            jax.ShapeDtypeStruct((tokens, wide + 2 * head), BF16),
            jax.ShapeDtypeStruct((tokens, 1), F32),
        ],
        in_specs=[pl.BlockSpec(memory_space=pltpu.SMEM)]
        + [spec((block, step), lambda k: (0, k))] * groups
        + [
            spec((tokens, step), lambda k: (0, k)),
            spec((1, step), lambda k: (0, k)),
            spec((step, wide), lambda k: (k, 0)),
            spec((head, step), lambda k: (0, k)),
        ],
        out_specs=[
            spec((tokens, step), lambda k: (0, k)),
            spec((tokens, wide + 2 * head), lambda k: (0, 0)),
            spec((tokens, 1), lambda k: (0, 0)),
        ],
        scratch_shapes=[
            pltpu.VMEM((tokens, wide + 2 * head), F32),
            pltpu.VMEM((tokens, 1), F32),
        ],
        compiler_params=params(),
        name="project",
    )(place, *parts, cotangent, gain, w_layer, out_layer)


def couple(slices, gain, w_layer, out_layer, last):
    sections = len(slices)
    count, width = slices[0].shape
    head = out_layer.shape[0]
    wide = w_layer.shape[1]
    step = min(width, 1024)
    below = (sections - 2) * wide
    packed = below + max(wide, (sections - 1) * head)

    def kernel(last_ref, *refs):
        r_refs = refs[:sections]
        g_ref, w_ref, o_ref, out_ref, stack_ref, acc = refs[sections:]
        k = pl.program_id(0)

        @pl.when(k == 0)
        def _():
            acc[...] = jnp.zeros_like(acc)

        for i in range(1, sections):
            stack_ref[i - 1] = r_refs[i][...]
        r = jnp.concatenate([ref[...] for ref in r_refs], axis=0)
        acc[:, :wide] += dot_nn((r.astype(F32) * g_ref[...]).astype(BF16), w_ref[...])
        acc[:, wide:] += dot_nt(r, o_ref[...])

        @pl.when(k == pl.num_programs(0) - 1)
        def _():
            out_ref[...] = jnp.zeros_like(out_ref)
            rows = [slice(r * count, (r + 1) * count) for r in range(sections)]
            for r in range(1, sections - 1):
                out_ref[:, (r - 1) * wide : r * wide] = acc[rows[r], :wide].astype(BF16)

            @pl.when(last_ref[0] == 1)
            def _():
                out_ref[:, below : below + wide] = acc[rows[-1], :wide].astype(BF16)

            @pl.when(last_ref[0] == 0)
            def _():
                for r in range(sections - 1):
                    cols = slice(below + r * head, below + (r + 1) * head)
                    out_ref[:, cols] = acc[rows[r], wide:].astype(BF16)

    return pl.pallas_call(
        kernel,
        grid=(width // step,),
        out_shape=[
            jax.ShapeDtypeStruct((count, packed), BF16),
            jax.ShapeDtypeStruct((sections - 1, count, width), BF16),
        ],
        in_specs=[pl.BlockSpec(memory_space=pltpu.SMEM)]
        + [pl.BlockSpec((count, step), lambda k: (0, k))] * sections
        + [
            pl.BlockSpec((1, step), lambda k: (0, k)),
            pl.BlockSpec((step, wide), lambda k: (k, 0)),
            pl.BlockSpec((head, step), lambda k: (0, k)),
        ],
        out_specs=[
            pl.BlockSpec((count, packed), lambda k: (0, 0)),
            pl.BlockSpec((sections - 1, count, step), lambda k: (0, 0, k)),
        ],
        scratch_shapes=[pltpu.VMEM((sections * count, wide + head), F32)],
        compiler_params=params(),
        name="couple",
    )(last, *slices, gain, w_layer, out_layer)


def layout(sections, wide, head):
    through, across, at = {}, {}, 0
    for k in range(sections):
        for j in range(k):
            through[j, k] = slice(at, at + wide)
            at += wide
        for j in range(k + 1 if k < sections - 1 else 0):
            across[j, k] = slice(at, at + head)
            at += head
    return through, across, at


def compact(parts, section, wide, head):
    sections = len(parts)
    count = parts[0].shape[0]
    below = (sections - 2) * wide
    through, across, total = layout(sections, wide, head)

    def kernel(s_ref, *refs):
        part_refs, out_ref = refs[:sections], refs[sections]
        mine = s_ref[0]

        def fill(k, r):
            for j in range(k):
                at = (k - j - 1) * wide
                out_ref[:, through[j, k]] = part_refs[r][:, at : at + wide]
            for j in range(k + 1 if k < sections - 1 else 0):
                at = below + (k - j) * head
                out_ref[:, across[j, k]] = part_refs[r][:, at : at + head]

        for s in range(sections):

            @pl.when(mine == s)
            def _(s=s):
                for r in range(sections):
                    fill((s - r) % sections, r)

    vmem = pl.BlockSpec(memory_space=pltpu.VMEM)
    return pl.pallas_call(
        kernel,
        out_shape=jax.ShapeDtypeStruct((count, total), BF16),
        in_specs=[pl.BlockSpec(memory_space=pltpu.SMEM)] + [vmem] * sections,
        out_specs=vmem,
        compiler_params=params(),
        name="compact",
    )(section, *parts)


def serial(xz, pieces, places, norms, mask, section, width, head):
    sections = len(xz)
    tokens = norms.shape[0]
    wide = 3 * head
    scale = 1.0 / math.sqrt(head)
    through_at, across_at, _ = layout(sections, wide, head)
    count, packed = pieces[0].shape[-2:]
    plane = head // count
    n_in = sections + len(pieces)
    copies = sections + plane

    def kernel(s_ref, p_ref, *refs):
        xz_refs, piece_refs = refs[:sections], refs[sections:n_in]
        n_ref, mask_ref, v_ref, t_ref, a_ref = refs[n_in : n_in + 5]
        xz_all, table, mixes, weights, projs, dmix, sems = refs[n_in + 5 :]
        mine = s_ref[0]
        started = []

        def start(source, target):
            copy = pltpu.make_async_copy(source, target, sems.at[len(started)])
            copy.start()
            started.append(copy)

        for r in range(sections):
            start(xz_refs[r], xz_all.at[lax.rem(mine + sections - r, sections)])
        at = 0
        for ref in piece_refs:
            for i in range(ref.shape[0]):
                start(ref.at[i], table.at[p_ref[at]])
                at += 1
        for copy in started:
            copy.wait()

        def through(j, k):
            return table[:, :, through_at[j, k]].reshape(head, wide)

        def across(j, k):
            return table[:, :, across_at[j, k]].reshape(head, head)

        allowed = mask_ref[...] > 0.5
        norm = n_ref[...]
        rstds, tails, mixed = [], [], []
        for s in range(sections):
            proj = xz_all[s, :, :wide].astype(F32)
            for j in range(s):
                proj = proj + dot_nn(mixed[j], through(j, s))
            rstd = lax.rsqrt(norm * (1.0 / width) + EPS)
            proj = proj * rstd
            projs[s] = proj.astype(BF16)
            q, k, v = (projs[s, :, i * head : (i + 1) * head] for i in range(3))
            scores = jnp.where(allowed, dot_nt(q, k) * scale, -1e30)
            scores = jnp.exp(scores - jnp.max(scores, axis=1, keepdims=True))
            soft = scores / jnp.sum(scores, axis=1, keepdims=True)
            weights[s] = soft
            mix = dot_nn(soft.astype(BF16), v).astype(BF16)
            mixed.append(mix)
            mixes[:, s * head : (s + 1) * head] = mix
            rstds.append(rstd)
            dmix[:, s * head : (s + 1) * head] = xz_all[s, :, wide + head :].astype(F32)
            if s == sections - 1:
                break
            y = xz_all[s, :, wide : wide + head].astype(F32)
            for j in range(s):
                y = y + dot_nn(mixed[j], across(j, s))
            tail = y + dot_nn(mix, across(s, s))
            norm = norm + jnp.sum(mix.astype(F32) * (y + tail), axis=1, keepdims=True)
            norm = jnp.maximum(norm, 0.0)
            tails.append(tail)
        total = jnp.zeros((tokens, 1), F32)
        a_ref[...] = jnp.zeros_like(a_ref)
        for s in reversed(range(sections)):
            cols = slice(s * head, (s + 1) * head)
            da = dmix[:, cols]
            if s < sections - 1:
                da = da - total * tails[s]
            da = da.astype(BF16)
            q, k, v = (projs[s, :, i * head : (i + 1) * head] for i in range(3))
            soft = weights[s]
            dv = dot_tn(soft.astype(BF16), da)
            dsoft = dot_nt(da, v)
            dscore = soft * (dsoft - jnp.sum(dsoft * soft, axis=1, keepdims=True))
            dscore = (dscore * scale).astype(BF16)
            dproj = jnp.concatenate([dot_nn(dscore, k), dot_tn(dscore, q), dv], axis=1)
            along = jnp.sum(dproj * projs[s].astype(F32), axis=1, keepdims=True)
            first = (dproj * rstds[s]).astype(BF16)
            second = (-total * mixes[:, cols].astype(F32)).astype(BF16)
            total = total + rstds[s] * rstds[s] * along * (1.0 / width)
            for j in reversed(range(s)):
                term = dot_nt(first, through(j, s))
                if s < sections - 1:
                    term = term + dot_nt(second, across(j, s))
                dmix[:, j * head : (j + 1) * head] += term

            @pl.when(mine == s)
            def _(first=first, second=second, total=total):
                v_ref[:, :wide] = first
                v_ref[:, wide:] = second
                t_ref[...] = total

            for r in range(1, sections - s):

                @pl.when(mine == s + r)
                def _(r=r, cols=cols):
                    a_ref[:, (r - 1) * head : r * head] = mixes[:, cols]

    vmem = pl.BlockSpec(memory_space=pltpu.VMEM)
    smem = pl.BlockSpec(memory_space=pltpu.SMEM)
    return pl.pallas_call(
        kernel,
        out_shape=[
            jax.ShapeDtypeStruct((tokens, wide + head), BF16),
            jax.ShapeDtypeStruct((tokens, 1), F32),
            jax.ShapeDtypeStruct((tokens, (sections - 1) * head), BF16),
        ],
        in_specs=[smem, smem] + [pl.BlockSpec(memory_space=pl.ANY)] * n_in + [vmem, vmem],
        out_specs=[vmem] * 3,
        scratch_shapes=[
            pltpu.VMEM((sections,) + xz[0].shape, BF16),
            pltpu.VMEM((plane, count, packed), BF16),
            pltpu.VMEM((tokens, sections * head), BF16),
            pltpu.VMEM((sections, tokens, tokens), F32),
            pltpu.VMEM((sections, tokens, wide), BF16),
            pltpu.VMEM((tokens, sections * head), F32),
            pltpu.SemaphoreType.DMA((copies,)),
        ],
        compiler_params=params(),
        name="serial",
    )(section, places, *xz, *pieces, norms, mask)


def widen(sent, gain, w_layer, out_layer, chunk):
    tokens = sent.shape[0]
    head, width = out_layer.shape
    wide = w_layer.shape[1]
    step = min(width, 1024)
    inner = step // chunk

    def kernel(v_ref, g_ref, w_ref, o_ref, back_ref, b_ref):
        back = dot_nt(v_ref[:, :wide], w_ref[...])
        own = back * g_ref[...] + dot_nn(v_ref[:, wide:], o_ref[...])
        back_ref[...] = back.astype(BF16)
        for i in range(inner):
            b_ref[i] = own[:, i * chunk : (i + 1) * chunk].astype(BF16)

    return pl.pallas_call(
        kernel,
        grid=(width // step,),
        out_shape=[
            jax.ShapeDtypeStruct((tokens, width), BF16),
            jax.ShapeDtypeStruct((width // chunk, tokens, chunk), BF16),
        ],
        in_specs=[
            pl.BlockSpec((tokens, wide + head), lambda k: (0, 0)),
            pl.BlockSpec((1, step), lambda k: (0, k)),
            pl.BlockSpec((step, wide), lambda k: (k, 0)),
            pl.BlockSpec((head, step), lambda k: (0, k)),
        ],
        out_specs=[
            pl.BlockSpec((tokens, step), lambda k: (0, k)),
            pl.BlockSpec((inner, tokens, chunk), lambda k: (k, 0, 0)),
        ],
        compiler_params=params(),
        name="widen",
    )(sent, gain, w_layer, out_layer)


def settle(total, mixes, stacks, places, x, cotangent, back, own):
    tokens, width = x.shape
    chunk = own.shape[2]
    layers, count = stacks[0].shape[:2]
    plane = len(stacks)
    head = plane * count
    step = min(width, 1024)
    inner = step // chunk

    def kernel(p_ref, t_ref, a_ref, x_ref, c_ref, back_ref, b_ref, *refs):
        stack_refs = refs[:plane]
        f_ref, out_ref, dg_ref, lower, sems = refs[plane:]

        @pl.when(pl.program_id(0) == 0)
        def _():
            copies = []
            for i in range(plane):
                for r in range(layers):
                    copy = pltpu.make_async_copy(
                        stack_refs[i].at[r], lower.at[r, p_ref[i]], sems.at[i * layers + r]
                    )
                    copy.start()
                    copies.append(copy)
            for copy in copies:
                copy.wait()

        cols = pl.ds(pl.multiple_of(pl.program_id(0) * step, step), step)
        here = x_ref[...].astype(F32)
        here = here + dot_nn(a_ref[...], lower[:, :, :, cols].reshape(layers * head, step))
        rest = c_ref[...].astype(F32) - t_ref[...] * here
        for i in range(inner):
            at = slice(i * chunk, (i + 1) * chunk)
            full = rest[:, at] + b_ref[i].astype(F32)
            f_ref[:, at] = full
            out_ref[:, at] = full.astype(BF16)
        dg_ref[...] = jnp.sum(back_ref[...].astype(F32) * here, axis=0, keepdims=True)

    cols = lambda k: (0, k)
    whole = lambda k: (0, 0)
    return pl.pallas_call(
        kernel,
        grid=(width // step,),
        out_shape=[
            jax.ShapeDtypeStruct((tokens, width), F32),
            jax.ShapeDtypeStruct((tokens, width), BF16),
            jax.ShapeDtypeStruct((1, width), F32),
        ],
        in_specs=[
            pl.BlockSpec(memory_space=pltpu.SMEM),
            pl.BlockSpec((tokens, 1), whole),
            pl.BlockSpec((tokens, layers * head), whole),
            pl.BlockSpec((tokens, step), cols),
            pl.BlockSpec((tokens, step), cols),
            pl.BlockSpec((tokens, step), cols),
            pl.BlockSpec((inner, tokens, chunk), lambda k: (k, 0, 0)),
        ]
        + [pl.BlockSpec(memory_space=pl.ANY)] * plane,
        out_specs=[
            pl.BlockSpec((tokens, step), cols),
            pl.BlockSpec((tokens, step), cols),
            pl.BlockSpec((1, step), cols),
        ],
        scratch_shapes=[
            pltpu.VMEM((layers, plane, count, width), BF16),
            pltpu.SemaphoreType.DMA((plane * layers,)),
        ],
        compiler_params=params(),
        name="settle",
    )(places, total, mixes, x, cotangent, back, own, *stacks)


def send_on(index, arrived, own):
    _, tokens, chunk = own.shape

    def kernel(i_ref, r_ref, b_ref, send_ref):
        send_ref[...] = (b_ref[0].astype(F32) + r_ref[...].astype(F32)).astype(BF16)

    return pl.pallas_call(
        kernel,
        grid_spec=pltpu.PrefetchScalarGridSpec(
            num_scalar_prefetch=1,
            grid=(1,),
            in_specs=[
                pl.BlockSpec((tokens, chunk), lambda k, i: (0, 0)),
                pl.BlockSpec((1, tokens, chunk), lambda k, i: (i[0], 0, 0)),
            ],
            out_specs=pl.BlockSpec((tokens, chunk), lambda k, i: (0, 0)),
        ),
        out_shape=jax.ShapeDtypeStruct((tokens, chunk), BF16),
        compiler_params=params(),
        name="send_on",
    )(index, arrived, own)


def put_out(index, arrived, full, out):
    streams = len(arrived)
    tokens, chunk = arrived[0].shape
    block = streams * chunk

    def kernel(i_ref, *refs):
        r_refs = refs[:streams]
        f_ref, _, out_ref = refs[streams:]
        for i in range(streams):
            at = slice(i * chunk, (i + 1) * chunk)
            out_ref[:, at] = (f_ref[:, at] + r_refs[i][...].astype(F32)).astype(BF16)

    return pl.pallas_call(
        kernel,
        grid_spec=pltpu.PrefetchScalarGridSpec(
            num_scalar_prefetch=1,
            grid=(1,),
            in_specs=[pl.BlockSpec((tokens, chunk), lambda k, i: (0, 0))] * streams
            + [
                pl.BlockSpec((tokens, block), lambda k, i: (0, i[0])),
                pl.BlockSpec(memory_space=pl.ANY),
            ],
            out_specs=pl.BlockSpec((tokens, block), lambda k, i: (0, i[0])),
        ),
        out_shape=jax.ShapeDtypeStruct(out.shape, BF16),
        input_output_aliases={streams + 2: 0},
        compiler_params=params(),
        name="put_out",
    )(index, *arrived, full, out)


STREAMS = 4
CHUNKS = 4


def shifted(array, by):
    sections = lax.axis_size("section")
    return lax.ppermute(array, "section", [(i, (i + by) % sections) for i in range(sections)])


def raised(array, by):
    sections = lax.axis_size("section")
    return lax.ppermute(array, "section", [(i, i + by) for i in range(sections - by)])


def swapped(array, step):
    groups = lax.axis_size("group")
    devices = lax.axis_size("dp")
    bits = devices.bit_length() - 1
    pairs = []
    for p in range(devices):
        for g in range(groups):
            pairs.append((p * groups + g, (p ^ (1 << ((step + g) % bits))) * groups + g))
    return lax.ppermute(array, ("dp", "group"), pairs)


def handed(array, by):
    groups = lax.axis_size("group")
    return lax.ppermute(array, "group", [(i, (i + by) % groups) for i in range(groups)])


def spread(array, before_last):
    bits = lax.axis_size("dp").bit_length() - 1
    stacks = [array[None]]
    for step in range(bits):
        together = stacks[0] if step == 0 else jnp.concatenate([together, stacks[-1]], axis=0)
        if step == bits - 1:
            together = tied(together, *before_last)
        stacks.append(swapped(together, step))
    stacks = stacks[-1:] if bits == 0 else [together, stacks[-1]]
    for r in range(1, lax.axis_size("group")):
        stacks = stacks + [handed(stack, r) for stack in stacks[:2]]
    return stacks


def plane_places():
    groups = lax.axis_size("group")
    bits = lax.axis_size("dp").bit_length() - 1
    masks = []
    for g in range(groups):
        order = [0]
        for step in range(bits):
            order = order + [m ^ (1 << ((step + g) % bits)) for m in order]
        masks.append(order)
    masks = jnp.asarray(masks, jnp.int32)
    dp, member = lax.axis_index("dp"), lax.axis_index("group")
    places = []
    for r in range(groups):
        giver = (member + groups - r) % groups
        places.append((dp ^ masks[giver]) * groups + giver)
    return jnp.concatenate(places).astype(jnp.int32)


def local(tokens_in, cotangent, gains, w_qkv, w_out, segments, plan):
    sections = lax.axis_size("section")
    groups = lax.axis_size("group")
    devices = lax.axis_size("dp")
    plane = devices * groups
    section = lax.axis_index("section")
    member = lax.axis_index("group")
    rows_dev = plan.shape[1]
    length = segments.shape[1]
    tokens, width = tokens_in.shape
    head = w_out.shape[1]
    share = rows_dev // groups
    w_layer, out_layer = w_qkv[0], w_out[0]
    place = member.astype(jnp.int32)[None]
    layer = section.astype(jnp.int32)[None]

    slice_rows = head // plane
    mine = lax.axis_index("dp") * groups + member
    own_rows = lax.dynamic_slice_in_dim(out_layer, mine * slice_rows, slice_rows, 0)
    slices = [own_rows] + [raised(own_rows, r) for r in range(1, sections)]

    parts = pick_rows(tokens_in.reshape(rows_dev, length, width), plan, place, groups)
    chosen = jnp.take(segments, plan[0], axis=0, mode="clip").astype(BF16)
    chosen = chosen.reshape(groups, share, length)
    moved, moved_seg = [], []
    for r in range(groups):
        outgoing = lax.dynamic_index_in_dim(chosen, (member + r) % groups, 0, keepdims=False)
        moved.append(handed(parts[r], r) if r else parts[r])
        moved_seg.append(handed(outgoing, r) if r else outgoing)
    moved = [part.reshape(share * length, width) for part in moved]
    order = (member - jnp.arange(groups)) % groups
    seg = jnp.take(jnp.stack(moved_seg), order, axis=0, mode="clip").reshape(tokens)
    at = jnp.arange(tokens)
    mask = (
        (at[:, None] >= at[None, :])
        & (at[:, None] // length == at[None, :] // length)
        & (seg[:, None] == seg[None, :])
    ).astype(F32)

    x, xz, norms = project(moved, cotangent, gains, w_layer, out_layer, place)

    last = (section == sections - 1).astype(jnp.int32)[None]
    slices[0] = tied(slices[0], xz)
    coupling, stack = couple(slices, gains, w_layer, out_layer, last)
    others = [shifted(coupling, r) for r in range(1, sections)]
    xz_all = [xz] + [shifted(xz, r) for r in range(1, sections)]
    coupling = compact([coupling] + others, layer, 3 * head, head)
    pieces = spread(coupling, xz_all[1:])
    places = plane_places()
    sent, total, mixes = serial(xz_all, pieces, places, norms, mask, layer, width, head)

    stacks = [stack]
    for step in range(devices.bit_length() - 1):
        if step == 1:
            stacks = [tied(array, pieces[-1]) for array in stacks]
        stacks = stacks + [swapped(array, step) for array in stacks]
    stacks = stacks + [handed(array, r) for r in range(1, groups) for array in stacks]

    chunk = width // (STREAMS * CHUNKS)
    back, own = widen(sent, gains, w_layer, out_layer, chunk)
    full, out, gain = settle(total, mixes, stacks, places, x, cotangent, back, own)
    for step in range(devices.bit_length() - 1):
        gain = gain + swapped(gain, step)
    gain_whole = sum([handed(gain, r) for r in range(1, groups)], gain)

    down = [(i, i - 1) for i in range(1, sections)]
    behind = sections - 1 - section

    def index(tick):
        return jnp.clip(tick - behind, 0, CHUNKS - 1).astype(jnp.int32)

    leaving = [
        lax.dynamic_index_in_dim(own, index(0) * STREAMS + stream, 0, keepdims=False)
        for stream in range(STREAMS)
    ]
    ticks = CHUNKS + sections - 1
    for tick in range(1, ticks):
        arrived = []
        for stream in range(STREAMS):
            arrived.append(lax.ppermute(leaving[stream], "section", down))
            if tick < ticks - 1:
                at_chunk = (index(tick) * STREAMS + stream)[None]
                leaving[stream] = send_on(at_chunk, arrived[stream], own)
        out = put_out(index(tick)[None], arrived, full, out)
        if 2 <= tick < ticks - 2:
            leaving[0] = tied(leaving[0], out)
    return (out[None], gain_whole)


def attend(hidden, segment, gain_row, w_layer, out_layer):
    count, length, width = hidden.shape
    head = out_layer.shape[0]
    scaled = hidden * lax.rsqrt(jnp.mean(hidden * hidden, axis=-1, keepdims=True) + EPS) * gain_row
    normed = scaled.astype(BF16).reshape(count * length, width)
    projected = jnp.dot(normed, w_layer, preferred_element_type=F32).reshape(count, length, 3 * head)
    query = projected[:, :, :head]
    keyed = projected[:, :, head : 2 * head]
    valued = projected[:, :, 2 * head :]
    positions = jnp.arange(length)
    allowed = (positions[:, None] >= positions[None, :])[None] & (
        segment[:, :, None] == segment[:, None, :]
    )
    scores = jnp.einsum("rid,rjd->rij", query, keyed, precision=lax.Precision.HIGHEST)
    scores = jnp.where(allowed, scores / math.sqrt(head), -1e30)
    weights = jax.nn.softmax(scores, axis=-1)
    mixed = jnp.einsum("rij,rjd->rid", weights, valued, precision=lax.Precision.HIGHEST)
    mixed = mixed.astype(BF16).reshape(count * length, head)
    output = jnp.dot(mixed, out_layer, preferred_element_type=F32).reshape(count, length, width)
    return hidden + output


MB_ROWS = 2


def relay(tokens_in, cotangent, gains, w_qkv, w_out, segments, plan):
    sections = lax.axis_size("section")
    section = lax.axis_index("section")
    rows_dev = plan.shape[1]
    width = tokens_in.shape[1]
    length = segments.shape[1]
    micro = rows_dev // MB_ROWS
    blocks = tokens_in.reshape(rows_dev, length, width)
    chosen = jnp.take(blocks, plan[0], axis=0)
    chosen_seg = jnp.take(segments, plan[0], axis=0).astype(BF16)
    assigned = lax.all_to_all(chosen, "group", split_axis=0, concat_axis=0, tiled=True)
    moved_seg = lax.all_to_all(chosen_seg, "group", split_axis=0, concat_axis=0, tiled=True)
    assigned = assigned.reshape(micro, MB_ROWS, length, width)
    seg_groups = moved_seg.reshape(micro, MB_ROWS, length)
    gain_row, w_layer, out_layer = gains[0], w_qkv[0], w_out[0]
    grad_rows = cotangent.reshape(micro, MB_ROWS, length, width)
    ticks = micro + sections - 1

    def passed_along(array, by):
        pairs = [(i, i + by) for i in range(sections) if 0 <= i + by < sections]
        return lax.ppermute(array, "section", pairs)

    def at(array, i):
        return lax.dynamic_index_in_dim(array, i, 0, keepdims=False)

    def forward_tick(tick, carry):
        saved, arrived = carry
        index = tick - section
        valid = (index >= 0) & (index < micro)
        clipped = jnp.clip(index, 0, micro - 1)
        entering = jnp.where(section == 0, at(assigned, clipped), arrived)
        kept = jnp.where(valid, entering, at(saved, clipped))
        saved = lax.dynamic_update_index_in_dim(saved, kept, clipped, 0)
        segment = at(seg_groups, clipped)

        def run_layer(value):
            return attend(value.astype(F32), segment, gain_row, w_layer, out_layer).astype(BF16)

        leaving = lax.cond(valid, run_layer, jnp.zeros_like, entering)
        return (saved, passed_along(leaving, 1))

    saved_init = jnp.zeros((micro, MB_ROWS, length, width), BF16)
    arrive_init = jnp.zeros((MB_ROWS, length, width), BF16)
    saved, _ = lax.fori_loop(0, ticks, forward_tick, (saved_init, arrive_init))

    def backward_tick(tick, carry):
        grads_x, gain_total, arrived = carry
        index = tick - (sections - 1 - section)
        valid = (index >= 0) & (index < micro)
        clipped = jnp.clip(index, 0, micro - 1)
        entering = jnp.where(section == sections - 1, at(grad_rows, clipped), arrived)
        segment = at(seg_groups, clipped)
        stored = at(saved, clipped).astype(F32)

        def local_layer(hidden, gains_here):
            return attend(hidden, segment, gains_here, w_layer, out_layer)

        def run_back(value):
            _, pullback = jax.vjp(local_layer, stored, gain_row)
            grad_hidden, grad_gain = pullback(value.astype(F32))
            return (grad_hidden.astype(BF16), grad_gain)

        def skip_back(value):
            return (jnp.zeros_like(value), jnp.zeros(gain_row.shape, F32))

        sending, grad_gain = lax.cond(valid, run_back, skip_back, entering)
        kept = jnp.where(valid, sending, at(grads_x, clipped))
        grads_x = lax.dynamic_update_index_in_dim(grads_x, kept, clipped, 0)
        return (grads_x, gain_total + grad_gain, passed_along(sending, -1))

    gain_init = jnp.zeros(gain_row.shape, F32)
    grads_x, gain_total, _ = lax.fori_loop(
        0, ticks, backward_tick, (saved_init, gain_init, arrive_init)
    )
    gain_whole = lax.psum(gain_total, ("dp", "group"))
    return (grads_x.reshape(1, rows_dev * length, width), gain_whole[None])


def solution(mesh):
    placed = (
        P(("dp", "group"), None),
        P(("dp", "group"), None),
        P("section", None),
        P("section", None, None),
        P("section", None, None),
        P(("dp", "group"), None),
        P(("dp", "group"), None),
    )

    def chosen(tokens_in, cotangent, gains, w_qkv, w_out, segments, plan):
        sections, head, width = w_out.shape
        devices = mesh.shape["dp"]
        small = sections * 4 * head < width and devices & (devices - 1) == 0
        body = local if small and sections > 1 else relay
        return jax.shard_map(
            body,
            mesh=mesh,
            in_specs=placed,
            out_specs=(P("section", ("dp", "group"), None), P("section", None)),
            check_vma=False,
        )(tokens_in, cotangent, gains, w_qkv, w_out, segments, plan)

    return chosen
```

```python
import math

import jax
import jax.numpy as jnp
from jax import lax
from jax.experimental import pallas as pl
from jax.experimental.pallas import tpu as pltpu
from jax.sharding import PartitionSpec as P

EPS = 1e-05
VMEM_BYTES = 60 * 1024 * 1024
SMALL = 16 * 1024 * 1024
F32 = jnp.float32
BF16 = jnp.bfloat16


def dot_nn(a, b):
    return lax.dot_general(a, b, (((1,), (0,)), ((), ())), preferred_element_type=F32)


def dot_nt(a, b):
    return lax.dot_general(a, b, (((1,), (1,)), ((), ())), preferred_element_type=F32)


def dot_tn(a, b):
    return lax.dot_general(a, b, (((0,), (0,)), ((), ())), preferred_element_type=F32)


def tied(array, *others):
    return lax.optimization_barrier((array,) + others)[0]


def params(limit=VMEM_BYTES):
    return pltpu.CompilerParams(vmem_limit_bytes=limit)


def pick(tokens, plan, place, groups, out_layer, mine, slice_rows):
    rows, length, width = tokens.shape
    share = rows // groups

    def kernel(plan_ref, place_ref, mine_ref, tokens_ref, o_ref, *rest):
        slice_ref, parts, sems = rest[0], rest[1 : 1 + groups], rest[1 + groups]
        at = pl.ds(pl.multiple_of(mine_ref[0] * slice_rows, slice_rows), slice_rows)
        copies = [pltpu.make_async_copy(o_ref.at[at], slice_ref, sems.at[rows])]
        copies[0].start()
        for r in range(groups):
            target = lax.rem(place_ref[0] + r, groups)
            for c in range(share):
                row = plan_ref[0, target * share + c]
                copy = pltpu.make_async_copy(
                    tokens_ref.at[row], parts[r].at[c], sems.at[r * share + c]
                )
                copy.start()
                copies.append(copy)
        for copy in copies:
            copy.wait()

    smem = pl.BlockSpec(memory_space=pltpu.SMEM)
    hbm = pl.BlockSpec(memory_space=pl.ANY)
    return pl.pallas_call(
        kernel,
        out_shape=[jax.ShapeDtypeStruct((slice_rows, width), BF16)]
        + [jax.ShapeDtypeStruct((share, length, width), BF16)] * groups,
        in_specs=[smem, smem, smem, hbm, hbm],
        out_specs=[hbm] * (1 + groups),
        scratch_shapes=[pltpu.SemaphoreType.DMA((rows + 1,))],
        compiler_params=params(),
        name="pick",
    )(plan, place, mine, tokens, out_layer)


def project(parts, cotangent, gain, w_layer, out_layer, place):
    groups = len(parts)
    tokens, width = cotangent.shape
    head = out_layer.shape[0]
    wide = w_layer.shape[1]
    block = tokens // groups
    step = min(width, 1024)

    def kernel(place_ref, *refs):
        part_refs = refs[:groups]
        cot_ref, g_ref, w_ref, o_ref, x_ref, xz_ref, n_ref, acc, square = refs[groups:]
        k = pl.program_id(0)

        @pl.when(k == 0)
        def _():
            acc[...] = jnp.zeros_like(acc)
            square[...] = jnp.zeros_like(square)

        for r in range(groups):
            source = lax.rem(place_ref[0] + groups - r, groups)
            rows = pl.ds(pl.multiple_of(source * block, block), block)
            x_ref[rows, :] = part_refs[r][...]
        x = x_ref[...]
        xf = x.astype(F32)
        acc[:, :wide] += dot_nn((xf * g_ref[...]).astype(BF16), w_ref[...])
        acc[:, wide : wide + head] += dot_nt(x, o_ref[...])
        acc[:, wide + head :] += dot_nt(cot_ref[...], o_ref[...])
        square[...] += jnp.sum(xf * xf, axis=1, keepdims=True)

        @pl.when(k == pl.num_programs(0) - 1)
        def _():
            xz_ref[...] = acc[...].astype(BF16)
            n_ref[...] = square[...]

    spec = lambda shape, index: pl.BlockSpec(shape, index)
    return pl.pallas_call(
        kernel,
        grid=(width // step,),
        out_shape=[
            jax.ShapeDtypeStruct((tokens, width), BF16),
            jax.ShapeDtypeStruct((tokens, wide + 2 * head), BF16),
            jax.ShapeDtypeStruct((tokens, 1), F32),
        ],
        in_specs=[pl.BlockSpec(memory_space=pltpu.SMEM)]
        + [spec((block, step), lambda k: (0, k))] * groups
        + [
            spec((tokens, step), lambda k: (0, k)),
            spec((1, step), lambda k: (0, k)),
            spec((step, wide), lambda k: (k, 0)),
            spec((head, step), lambda k: (0, k)),
        ],
        out_specs=[
            spec((tokens, step), lambda k: (0, k)),
            spec((tokens, wide + 2 * head), lambda k: (0, 0)),
            spec((tokens, 1), lambda k: (0, 0)),
        ],
        scratch_shapes=[
            pltpu.VMEM((tokens, wide + 2 * head), F32),
            pltpu.VMEM((tokens, 1), F32),
        ],
        compiler_params=params(),
        name="project",
    )(place, *parts, cotangent, gain, w_layer, out_layer)


def couple(slices, gain, w_layer, out_layer, last):
    sections = len(slices)
    count, width = slices[0].shape
    head = out_layer.shape[0]
    wide = w_layer.shape[1]
    step = min(width, 1024)
    below = (sections - 2) * wide
    packed = below + max(wide, (sections - 1) * head)

    def kernel(last_ref, *refs):
        r_refs = refs[:sections]
        g_ref, w_ref, o_ref, out_ref, stack_ref, acc = refs[sections:]
        k = pl.program_id(0)

        @pl.when(k == 0)
        def _():
            acc[...] = jnp.zeros_like(acc)

        for i in range(1, sections):
            stack_ref[i - 1] = r_refs[i][...]
        r = jnp.concatenate([ref[...] for ref in r_refs], axis=0)
        acc[:, :wide] += dot_nn((r.astype(F32) * g_ref[...]).astype(BF16), w_ref[...])
        acc[:, wide:] += dot_nt(r, o_ref[...])

        @pl.when(k == pl.num_programs(0) - 1)
        def _():
            out_ref[...] = jnp.zeros_like(out_ref)
            rows = [slice(r * count, (r + 1) * count) for r in range(sections)]
            for r in range(1, sections - 1):
                out_ref[:, (r - 1) * wide : r * wide] = acc[rows[r], :wide].astype(BF16)

            @pl.when(last_ref[0] == 1)
            def _():
                out_ref[:, below : below + wide] = acc[rows[-1], :wide].astype(BF16)

            @pl.when(last_ref[0] == 0)
            def _():
                for r in range(sections - 1):
                    cols = slice(below + r * head, below + (r + 1) * head)
                    out_ref[:, cols] = acc[rows[r], wide:].astype(BF16)

    return pl.pallas_call(
        kernel,
        grid=(width // step,),
        out_shape=[
            jax.ShapeDtypeStruct((count, packed), BF16),
            jax.ShapeDtypeStruct((sections - 1, count, width), BF16),
        ],
        in_specs=[pl.BlockSpec(memory_space=pltpu.SMEM)]
        + [pl.BlockSpec((count, step), lambda k: (0, k))] * sections
        + [
            pl.BlockSpec((1, step), lambda k: (0, k)),
            pl.BlockSpec((step, wide), lambda k: (k, 0)),
            pl.BlockSpec((head, step), lambda k: (0, k)),
        ],
        out_specs=[
            pl.BlockSpec((count, packed), lambda k: (0, 0)),
            pl.BlockSpec((sections - 1, count, step), lambda k: (0, 0, k)),
        ],
        scratch_shapes=[pltpu.VMEM((sections * count, wide + head), F32)],
        compiler_params=params(),
        name="couple",
    )(last, *slices, gain, w_layer, out_layer)


def layout(sections, wide, head):
    through, across, at = {}, {}, 0
    for k in range(sections):
        for j in range(k):
            through[j, k] = slice(at, at + wide)
            at += wide
        for j in range(k + 1 if k < sections - 1 else 0):
            across[j, k] = slice(at, at + head)
            at += head
    return through, across, at


def compact(parts, section, wide, head):
    sections = len(parts)
    count = parts[0].shape[0]
    below = (sections - 2) * wide
    through, across, total = layout(sections, wide, head)

    def kernel(s_ref, *refs):
        part_refs, out_ref = refs[:sections], refs[sections]
        mine = s_ref[0]

        def fill(k, r):
            for j in range(k):
                at = (k - j - 1) * wide
                out_ref[:, through[j, k]] = part_refs[r][:, at : at + wide]
            for j in range(k + 1 if k < sections - 1 else 0):
                at = below + (k - j) * head
                out_ref[:, across[j, k]] = part_refs[r][:, at : at + head]

        for s in range(sections):

            @pl.when(mine == s)
            def _(s=s):
                for r in range(sections):
                    fill((s - r) % sections, r)

    vmem = pl.BlockSpec(memory_space=pltpu.VMEM)
    return pl.pallas_call(
        kernel,
        out_shape=jax.ShapeDtypeStruct((count, total), BF16),
        in_specs=[pl.BlockSpec(memory_space=pltpu.SMEM)] + [vmem] * sections,
        out_specs=vmem,
        compiler_params=params(SMALL),
        name="compact",
    )(section, *parts)


def serial(xz, pieces, places, norms, mask, section, width, head):
    sections = len(xz)
    tokens = norms.shape[0]
    wide = 3 * head
    scale = 1.0 / math.sqrt(head)
    through_at, across_at, _ = layout(sections, wide, head)
    count, packed = pieces[0].shape[-2:]
    plane = head // count
    n_in = sections + len(pieces)
    copies = sections + plane

    def kernel(s_ref, p_ref, *refs):
        xz_refs, piece_refs = refs[:sections], refs[sections:n_in]
        n_ref, mask_ref, v_ref, t_ref, a_ref = refs[n_in : n_in + 5]
        xz_all, table, mixes, weights, projs, dmix, sems = refs[n_in + 5 :]
        mine = s_ref[0]
        started = []

        def start(source, target):
            copy = pltpu.make_async_copy(source, target, sems.at[len(started)])
            copy.start()
            started.append(copy)

        for r in range(sections):
            start(xz_refs[r], xz_all.at[lax.rem(mine + sections - r, sections)])
        at = 0
        for ref in piece_refs:
            for i in range(ref.shape[0]):
                start(ref.at[i], table.at[p_ref[at]])
                at += 1
        for copy in started:
            copy.wait()

        def through(j, k):
            return table[:, :, through_at[j, k]].reshape(head, wide)

        def across(j, k):
            return table[:, :, across_at[j, k]].reshape(head, head)

        allowed = mask_ref[...] > 0.5
        norm = n_ref[...]
        rstds, tails, mixed = [], [], []
        for s in range(sections):
            proj = xz_all[s, :, :wide].astype(F32)
            for j in range(s):
                proj = proj + dot_nn(mixed[j], through(j, s))
            rstd = lax.rsqrt(norm * (1.0 / width) + EPS)
            proj = proj * rstd
            projs[s] = proj.astype(BF16)
            q, k, v = (projs[s, :, i * head : (i + 1) * head] for i in range(3))
            scores = jnp.where(allowed, dot_nt(q, k) * scale, -1e30)
            scores = jnp.exp(scores - jnp.max(scores, axis=1, keepdims=True))
            soft = scores / jnp.sum(scores, axis=1, keepdims=True)
            weights[s] = soft
            mix = dot_nn(soft.astype(BF16), v).astype(BF16)
            mixed.append(mix)
            mixes[:, s * head : (s + 1) * head] = mix
            rstds.append(rstd)
            dmix[:, s * head : (s + 1) * head] = xz_all[s, :, wide + head :].astype(F32)
            if s == sections - 1:
                break
            y = xz_all[s, :, wide : wide + head].astype(F32)
            for j in range(s):
                y = y + dot_nn(mixed[j], across(j, s))
            tail = y + dot_nn(mix, across(s, s))
            norm = norm + jnp.sum(mix.astype(F32) * (y + tail), axis=1, keepdims=True)
            norm = jnp.maximum(norm, 0.0)
            tails.append(tail)
        total = jnp.zeros((tokens, 1), F32)
        a_ref[...] = jnp.zeros_like(a_ref)
        for s in reversed(range(sections)):
            cols = slice(s * head, (s + 1) * head)
            da = dmix[:, cols]
            if s < sections - 1:
                da = da - total * tails[s]
            da = da.astype(BF16)
            q, k, v = (projs[s, :, i * head : (i + 1) * head] for i in range(3))
            soft = weights[s]
            dv = dot_tn(soft.astype(BF16), da)
            dsoft = dot_nt(da, v)
            dscore = soft * (dsoft - jnp.sum(dsoft * soft, axis=1, keepdims=True))
            dscore = (dscore * scale).astype(BF16)
            dproj = jnp.concatenate([dot_nn(dscore, k), dot_tn(dscore, q), dv], axis=1)
            along = jnp.sum(dproj * projs[s].astype(F32), axis=1, keepdims=True)
            first = (dproj * rstds[s]).astype(BF16)
            second = (-total * mixes[:, cols].astype(F32)).astype(BF16)
            total = total + rstds[s] * rstds[s] * along * (1.0 / width)
            for j in reversed(range(s)):
                term = dot_nt(first, through(j, s))
                if s < sections - 1:
                    term = term + dot_nt(second, across(j, s))
                dmix[:, j * head : (j + 1) * head] += term

            @pl.when(mine == s)
            def _(first=first, second=second, total=total):
                v_ref[:, :wide] = first
                v_ref[:, wide:] = second
                t_ref[...] = total

            for r in range(1, sections - s):

                @pl.when(mine == s + r)
                def _(r=r, cols=cols):
                    a_ref[:, (r - 1) * head : r * head] = mixes[:, cols]

    vmem = pl.BlockSpec(memory_space=pltpu.VMEM)
    smem = pl.BlockSpec(memory_space=pltpu.SMEM)
    return pl.pallas_call(
        kernel,
        out_shape=[
            jax.ShapeDtypeStruct((tokens, wide + head), BF16),
            jax.ShapeDtypeStruct((tokens, 1), F32),
            jax.ShapeDtypeStruct((tokens, (sections - 1) * head), BF16),
        ],
        in_specs=[smem, smem] + [pl.BlockSpec(memory_space=pl.ANY)] * n_in + [vmem, vmem],
        out_specs=[vmem] * 3,
        scratch_shapes=[
            pltpu.VMEM((sections,) + xz[0].shape, BF16),
            pltpu.VMEM((plane, count, packed), BF16),
            pltpu.VMEM((tokens, sections * head), BF16),
            pltpu.VMEM((sections, tokens, tokens), F32),
            pltpu.VMEM((sections, tokens, wide), BF16),
            pltpu.VMEM((tokens, sections * head), F32),
            pltpu.SemaphoreType.DMA((copies,)),
        ],
        compiler_params=params(),
        name="serial",
    )(section, places, *xz, *pieces, norms, mask)


def widen(sent, gain, w_layer, out_layer, chunk):
    tokens = sent.shape[0]
    head, width = out_layer.shape
    wide = w_layer.shape[1]
    step = min(width, 1024)
    inner = step // chunk

    def kernel(v_ref, g_ref, w_ref, o_ref, back_ref, b_ref):
        back = dot_nt(v_ref[:, :wide], w_ref[...])
        own = back * g_ref[...] + dot_nn(v_ref[:, wide:], o_ref[...])
        back_ref[...] = back.astype(BF16)
        for i in range(inner):
            b_ref[i] = own[:, i * chunk : (i + 1) * chunk].astype(BF16)

    return pl.pallas_call(
        kernel,
        grid=(width // step,),
        out_shape=[
            jax.ShapeDtypeStruct((tokens, width), BF16),
            jax.ShapeDtypeStruct((width // chunk, tokens, chunk), BF16),
        ],
        in_specs=[
            pl.BlockSpec((tokens, wide + head), lambda k: (0, 0)),
            pl.BlockSpec((1, step), lambda k: (0, k)),
            pl.BlockSpec((step, wide), lambda k: (k, 0)),
            pl.BlockSpec((head, step), lambda k: (0, k)),
        ],
        out_specs=[
            pl.BlockSpec((tokens, step), lambda k: (0, k)),
            pl.BlockSpec((inner, tokens, chunk), lambda k: (k, 0, 0)),
        ],
        compiler_params=params(),
        name="widen",
    )(sent, gain, w_layer, out_layer)


def settle(total, mixes, stacks, places, x, cotangent, back, own):
    tokens, width = x.shape
    chunk = own.shape[2]
    layers, count = stacks[0].shape[1:3]
    entries = [(i, e) for i, stack in enumerate(stacks) for e in range(stack.shape[0])]
    plane = len(entries)
    head = plane * count
    step = min(width, 1024)
    inner = step // chunk

    def kernel(p_ref, t_ref, a_ref, x_ref, c_ref, back_ref, b_ref, *refs):
        stack_refs = refs[: len(stacks)]
        f_ref, out_ref, dg_ref, lower, sems = refs[len(stacks) :]

        @pl.when(pl.program_id(0) == 0)
        def _():
            copies = []
            for at, (i, e) in enumerate(entries):
                for r in range(layers):
                    copy = pltpu.make_async_copy(
                        stack_refs[i].at[e, r], lower.at[r, p_ref[at]], sems.at[at * layers + r]
                    )
                    copy.start()
                    copies.append(copy)
            for copy in copies:
                copy.wait()

        cols = pl.ds(pl.multiple_of(pl.program_id(0) * step, step), step)
        here = x_ref[...].astype(F32)
        here = here + dot_nn(a_ref[...], lower[:, :, :, cols].reshape(layers * head, step))
        rest = c_ref[...].astype(F32) - t_ref[...] * here
        for i in range(inner):
            at = slice(i * chunk, (i + 1) * chunk)
            full = rest[:, at] + b_ref[i].astype(F32)
            f_ref[:, at] = full
            out_ref[:, at] = full.astype(BF16)
        dg_ref[...] = jnp.sum(back_ref[...].astype(F32) * here, axis=0, keepdims=True)

    cols = lambda k: (0, k)
    whole = lambda k: (0, 0)
    return pl.pallas_call(
        kernel,
        grid=(width // step,),
        out_shape=[
            jax.ShapeDtypeStruct((tokens, width), F32),
            jax.ShapeDtypeStruct((tokens, width), BF16),
            jax.ShapeDtypeStruct((1, width), F32),
        ],
        in_specs=[
            pl.BlockSpec(memory_space=pltpu.SMEM),
            pl.BlockSpec((tokens, 1), whole),
            pl.BlockSpec((tokens, layers * head), whole),
            pl.BlockSpec((tokens, step), cols),
            pl.BlockSpec((tokens, step), cols),
            pl.BlockSpec((tokens, step), cols),
            pl.BlockSpec((inner, tokens, chunk), lambda k: (k, 0, 0)),
        ]
        + [pl.BlockSpec(memory_space=pl.ANY)] * len(stacks),
        out_specs=[
            pl.BlockSpec((tokens, step), cols),
            pl.BlockSpec((tokens, step), cols),
            pl.BlockSpec((1, step), cols),
        ],
        scratch_shapes=[
            pltpu.VMEM((layers, plane, count, width), BF16),
            pltpu.SemaphoreType.DMA((plane * layers,)),
        ],
        compiler_params=params(),
        name="settle",
    )(places, total, mixes, x, cotangent, back, own, *stacks)


def send_on(index, arrived, own):
    _, tokens, chunk = own.shape

    def kernel(i_ref, r_ref, b_ref, send_ref):
        send_ref[...] = (b_ref[0].astype(F32) + r_ref[...].astype(F32)).astype(BF16)

    return pl.pallas_call(
        kernel,
        grid_spec=pltpu.PrefetchScalarGridSpec(
            num_scalar_prefetch=1,
            grid=(1,),
            in_specs=[
                pl.BlockSpec((tokens, chunk), lambda k, i: (0, 0)),
                pl.BlockSpec((1, tokens, chunk), lambda k, i: (i[0], 0, 0)),
            ],
            out_specs=pl.BlockSpec((tokens, chunk), lambda k, i: (0, 0)),
        ),
        out_shape=jax.ShapeDtypeStruct((tokens, chunk), BF16),
        compiler_params=params(SMALL),
        name="send_on",
    )(index, arrived, own)


def put_out(index, arrived, full, out):
    streams = len(arrived)
    tokens, chunk = arrived[0].shape
    block = streams * chunk

    def kernel(i_ref, *refs):
        r_refs = refs[:streams]
        f_ref, _, out_ref = refs[streams:]
        for i in range(streams):
            at = slice(i * chunk, (i + 1) * chunk)
            out_ref[:, at] = (f_ref[:, at] + r_refs[i][...].astype(F32)).astype(BF16)

    return pl.pallas_call(
        kernel,
        grid_spec=pltpu.PrefetchScalarGridSpec(
            num_scalar_prefetch=1,
            grid=(1,),
            in_specs=[pl.BlockSpec((tokens, chunk), lambda k, i: (0, 0))] * streams
            + [
                pl.BlockSpec((tokens, block), lambda k, i: (0, i[0])),
                pl.BlockSpec(memory_space=pl.ANY),
            ],
            out_specs=pl.BlockSpec((tokens, block), lambda k, i: (0, i[0])),
        ),
        out_shape=jax.ShapeDtypeStruct(out.shape, BF16),
        input_output_aliases={streams + 2: 0},
        compiler_params=params(SMALL),
        name="put_out",
    )(index, *arrived, full, out)


STREAMS = 2
CHUNKS = 4


def shifted(array, by):
    sections = lax.axis_size("section")
    return lax.ppermute(array, "section", [(i, (i + by) % sections) for i in range(sections)])


def raised(array, by):
    sections = lax.axis_size("section")
    return lax.ppermute(array, "section", [(i, i + by) for i in range(sections - by)])


def swapped(array, step):
    groups = lax.axis_size("group")
    devices = lax.axis_size("dp")
    bits = devices.bit_length() - 1
    pairs = []
    for p in range(devices):
        for g in range(groups):
            pairs.append((p * groups + g, (p ^ (1 << ((step + g) % bits))) * groups + g))
    return lax.ppermute(array, ("dp", "group"), pairs)


def handed(array, by):
    groups = lax.axis_size("group")
    return lax.ppermute(array, "group", [(i, (i + by) % groups) for i in range(groups)])


def spread(array, before_last):
    bits = lax.axis_size("dp").bit_length() - 1
    stacks = [array[None]]
    for step in range(bits):
        together = stacks[0] if step == 0 else jnp.concatenate([together, stacks[-1]], axis=0)
        if step == bits - 1:
            together = tied(together, *before_last)
        stacks.append(swapped(together, step))
    stacks = stacks[-1:] if bits == 0 else [together, stacks[-1]]
    for r in range(1, lax.axis_size("group")):
        stacks = stacks + [handed(stack, r) for stack in stacks[:2]]
    return stacks


def plane_places():
    groups = lax.axis_size("group")
    bits = lax.axis_size("dp").bit_length() - 1
    masks = []
    for g in range(groups):
        order = [0]
        for step in range(bits):
            order = order + [m ^ (1 << ((step + g) % bits)) for m in order]
        masks.append(order)
    masks = jnp.asarray(masks, jnp.int32)
    dp, member = lax.axis_index("dp"), lax.axis_index("group")
    places = []
    for r in range(groups):
        giver = (member + groups - r) % groups
        places.append((dp ^ masks[giver]) * groups + giver)
    return jnp.concatenate(places).astype(jnp.int32)


def local(tokens_in, cotangent, gains, w_qkv, w_out, segments, plan):
    sections = lax.axis_size("section")
    groups = lax.axis_size("group")
    devices = lax.axis_size("dp")
    plane = devices * groups
    section = lax.axis_index("section")
    member = lax.axis_index("group")
    rows_dev = plan.shape[1]
    length = segments.shape[1]
    tokens, width = tokens_in.shape
    head = w_out.shape[1]
    share = rows_dev // groups
    w_layer, out_layer = w_qkv[0], w_out[0]
    place = member.astype(jnp.int32)[None]
    layer = section.astype(jnp.int32)[None]

    slice_rows = head // plane
    mine = lax.axis_index("dp") * groups + member
    own_rows, *parts = pick(
        tokens_in.reshape(rows_dev, length, width),
        plan,
        place,
        groups,
        out_layer,
        mine.astype(jnp.int32)[None],
        slice_rows,
    )
    slices = [own_rows] + [raised(own_rows, r) for r in range(1, sections)]
    chosen = jnp.take(segments, plan[0], axis=0, mode="clip").astype(BF16)
    chosen = chosen.reshape(groups, share, length)
    moved, moved_seg = [], []
    for r in range(groups):
        outgoing = lax.dynamic_index_in_dim(chosen, (member + r) % groups, 0, keepdims=False)
        moved.append(handed(parts[r], r) if r else parts[r])
        moved_seg.append(handed(outgoing, r) if r else outgoing)
    moved = [part.reshape(share * length, width) for part in moved]
    order = (member - jnp.arange(groups)) % groups
    seg = jnp.take(jnp.stack(moved_seg), order, axis=0, mode="clip").reshape(tokens)
    at = jnp.arange(tokens)
    mask = (
        (at[:, None] >= at[None, :])
        & (at[:, None] // length == at[None, :] // length)
        & (seg[:, None] == seg[None, :])
    ).astype(F32)

    x, xz, norms = project(moved, cotangent, gains, w_layer, out_layer, place)

    last = (section == sections - 1).astype(jnp.int32)[None]
    places = plane_places()
    xz_all = [xz] + [shifted(xz, r) for r in range(1, sections)]
    slices[0] = tied(slices[0], mask, places, *xz_all[:2])
    coupling, stack = couple(slices, gains, w_layer, out_layer, last)
    others = [shifted(coupling, r) for r in range(1, sections)]
    coupling = compact([tied(coupling, *xz_all[:3])] + others, layer, 3 * head, head)
    pieces = spread(coupling, xz_all)
    sent, total, mixes = serial(xz_all, pieces, places, norms, mask, layer, width, head)

    stacks = spread(stack, pieces)

    chunk = width // (STREAMS * CHUNKS)
    back, own = widen(sent, gains, w_layer, out_layer, chunk)
    full, out, gain = settle(total, mixes, stacks, places, x, cotangent, back, own)
    gains_on = [gain]
    for step in range(devices.bit_length() - 1):
        gains_on.append(gains_on[-1] + swapped(gains_on[-1], step))
    gain_whole = sum([handed(gains_on[-1], r) for r in range(1, groups)], gains_on[-1])
    gains_on = gains_on[1:] + [gain_whole]

    down = [(i, i - 1) for i in range(1, sections)]
    behind = sections - 1 - section

    def index(tick):
        return jnp.clip(tick - behind, 0, CHUNKS - 1).astype(jnp.int32)

    leaving = [
        lax.dynamic_index_in_dim(own, index(0) * STREAMS + stream, 0, keepdims=False)
        for stream in range(STREAMS)
    ]
    ticks = CHUNKS + sections - 1
    own = tied(own, full)
    for tick in range(1, ticks):
        arrived = []
        for stream in range(STREAMS):
            arrived.append(lax.ppermute(leaving[stream], "section", down))
            if tick < ticks - 1:
                at_chunk = (index(tick) * STREAMS + stream)[None]
                leaving[stream] = send_on(at_chunk, arrived[stream], own)
        out = put_out(index(tick)[None], arrived, full, out)
        if tick < ticks - 2:
            leaving[0] = tied(leaving[0], out)
        if tick < ticks - 1:
            leaving[-1] = tied(leaving[-1], *gains_on[tick - 1 : tick])
    return (out[None], gain_whole)


def attend(hidden, segment, gain_row, w_layer, out_layer):
    count, length, width = hidden.shape
    head = out_layer.shape[0]
    scaled = hidden * lax.rsqrt(jnp.mean(hidden * hidden, axis=-1, keepdims=True) + EPS) * gain_row
    normed = scaled.astype(BF16).reshape(count * length, width)
    projected = jnp.dot(normed, w_layer, preferred_element_type=F32).reshape(count, length, 3 * head)
    query = projected[:, :, :head]
    keyed = projected[:, :, head : 2 * head]
    valued = projected[:, :, 2 * head :]
    positions = jnp.arange(length)
    allowed = (positions[:, None] >= positions[None, :])[None] & (
        segment[:, :, None] == segment[:, None, :]
    )
    scores = jnp.einsum("rid,rjd->rij", query, keyed, precision=lax.Precision.HIGHEST)
    scores = jnp.where(allowed, scores / math.sqrt(head), -1e30)
    weights = jax.nn.softmax(scores, axis=-1)
    mixed = jnp.einsum("rij,rjd->rid", weights, valued, precision=lax.Precision.HIGHEST)
    mixed = mixed.astype(BF16).reshape(count * length, head)
    output = jnp.dot(mixed, out_layer, preferred_element_type=F32).reshape(count, length, width)
    return hidden + output


MB_ROWS = 2


def relay(tokens_in, cotangent, gains, w_qkv, w_out, segments, plan):
    sections = lax.axis_size("section")
    section = lax.axis_index("section")
    rows_dev = plan.shape[1]
    width = tokens_in.shape[1]
    length = segments.shape[1]
    micro = rows_dev // MB_ROWS
    blocks = tokens_in.reshape(rows_dev, length, width)
    chosen = jnp.take(blocks, plan[0], axis=0)
    chosen_seg = jnp.take(segments, plan[0], axis=0).astype(BF16)
    assigned = lax.all_to_all(chosen, "group", split_axis=0, concat_axis=0, tiled=True)
    moved_seg = lax.all_to_all(chosen_seg, "group", split_axis=0, concat_axis=0, tiled=True)
    assigned = assigned.reshape(micro, MB_ROWS, length, width)
    seg_groups = moved_seg.reshape(micro, MB_ROWS, length)
    gain_row, w_layer, out_layer = gains[0], w_qkv[0], w_out[0]
    grad_rows = cotangent.reshape(micro, MB_ROWS, length, width)
    ticks = micro + sections - 1

    def passed_along(array, by):
        pairs = [(i, i + by) for i in range(sections) if 0 <= i + by < sections]
        return lax.ppermute(array, "section", pairs)

    def at(array, i):
        return lax.dynamic_index_in_dim(array, i, 0, keepdims=False)

    def forward_tick(tick, carry):
        saved, arrived = carry
        index = tick - section
        valid = (index >= 0) & (index < micro)
        clipped = jnp.clip(index, 0, micro - 1)
        entering = jnp.where(section == 0, at(assigned, clipped), arrived)
        kept = jnp.where(valid, entering, at(saved, clipped))
        saved = lax.dynamic_update_index_in_dim(saved, kept, clipped, 0)
        segment = at(seg_groups, clipped)

        def run_layer(value):
            return attend(value.astype(F32), segment, gain_row, w_layer, out_layer).astype(BF16)

        leaving = lax.cond(valid, run_layer, jnp.zeros_like, entering)
        return (saved, passed_along(leaving, 1))

    saved_init = jnp.zeros((micro, MB_ROWS, length, width), BF16)
    arrive_init = jnp.zeros((MB_ROWS, length, width), BF16)
    saved, _ = lax.fori_loop(0, ticks, forward_tick, (saved_init, arrive_init))

    def backward_tick(tick, carry):
        grads_x, gain_total, arrived = carry
        index = tick - (sections - 1 - section)
        valid = (index >= 0) & (index < micro)
        clipped = jnp.clip(index, 0, micro - 1)
        entering = jnp.where(section == sections - 1, at(grad_rows, clipped), arrived)
        segment = at(seg_groups, clipped)
        stored = at(saved, clipped).astype(F32)

        def local_layer(hidden, gains_here):
            return attend(hidden, segment, gains_here, w_layer, out_layer)

        def run_back(value):
            _, pullback = jax.vjp(local_layer, stored, gain_row)
            grad_hidden, grad_gain = pullback(value.astype(F32))
            return (grad_hidden.astype(BF16), grad_gain)

        def skip_back(value):
            return (jnp.zeros_like(value), jnp.zeros(gain_row.shape, F32))

        sending, grad_gain = lax.cond(valid, run_back, skip_back, entering)
        kept = jnp.where(valid, sending, at(grads_x, clipped))
        grads_x = lax.dynamic_update_index_in_dim(grads_x, kept, clipped, 0)
        return (grads_x, gain_total + grad_gain, passed_along(sending, -1))

    gain_init = jnp.zeros(gain_row.shape, F32)
    grads_x, gain_total, _ = lax.fori_loop(
        0, ticks, backward_tick, (saved_init, gain_init, arrive_init)
    )
    gain_whole = lax.psum(gain_total, ("dp", "group"))
    return (grads_x.reshape(1, rows_dev * length, width), gain_whole[None])


def solution(mesh):
    placed = (
        P(("dp", "group"), None),
        P(("dp", "group"), None),
        P("section", None),
        P("section", None, None),
        P("section", None, None),
        P(("dp", "group"), None),
        P(("dp", "group"), None),
    )

    def chosen(tokens_in, cotangent, gains, w_qkv, w_out, segments, plan):
        sections, head, width = w_out.shape
        devices = mesh.shape["dp"]
        small = sections * 4 * head < width and devices & (devices - 1) == 0
        body = local if small and sections > 1 else relay
        return jax.shard_map(
            body,
            mesh=mesh,
            in_specs=placed,
            out_specs=(P("section", ("dp", "group"), None), P("section", None)),
            check_vma=False,
        )(tokens_in, cotangent, gains, w_qkv, w_out, segments, plan)

    return chosen
```

```python
import math

import jax
import jax.numpy as jnp
from jax import lax
from jax.experimental import pallas as pl
from jax.experimental.pallas import tpu as pltpu
from jax.sharding import PartitionSpec as P

EPS = 1e-05
VMEM_BYTES = 24 * 1024 * 1024
SMALL = 16 * 1024 * 1024
F32 = jnp.float32
BF16 = jnp.bfloat16


def dot_nn(a, b):
    return lax.dot_general(a, b, (((1,), (0,)), ((), ())), preferred_element_type=F32)


def dot_nt(a, b):
    return lax.dot_general(a, b, (((1,), (1,)), ((), ())), preferred_element_type=F32)


def dot_tn(a, b):
    return lax.dot_general(a, b, (((0,), (0,)), ((), ())), preferred_element_type=F32)


def tied(array, *others):
    return lax.optimization_barrier((array,) + others)[0]


def params(limit=VMEM_BYTES):
    return pltpu.CompilerParams(vmem_limit_bytes=limit)


def pick(tokens, plan, place, groups, out_layer, mine, slice_rows):
    rows, length, width = tokens.shape
    share = rows // groups

    def kernel(plan_ref, place_ref, mine_ref, tokens_ref, o_ref, *rest):
        slice_ref, parts, sems = rest[0], rest[1 : 1 + groups], rest[1 + groups]
        at = pl.ds(pl.multiple_of(mine_ref[0] * slice_rows, slice_rows), slice_rows)
        copies = [pltpu.make_async_copy(o_ref.at[at], slice_ref, sems.at[rows])]
        copies[0].start()
        for r in range(groups):
            target = lax.rem(place_ref[0] + r, groups)
            for c in range(share):
                row = plan_ref[0, target * share + c]
                copy = pltpu.make_async_copy(
                    tokens_ref.at[row], parts[r].at[c], sems.at[r * share + c]
                )
                copy.start()
                copies.append(copy)
        for copy in copies:
            copy.wait()

    smem = pl.BlockSpec(memory_space=pltpu.SMEM)
    hbm = pl.BlockSpec(memory_space=pl.ANY)
    return pl.pallas_call(
        kernel,
        out_shape=[jax.ShapeDtypeStruct((slice_rows, width), BF16)]
        + [jax.ShapeDtypeStruct((share, length, width), BF16)] * groups,
        in_specs=[smem, smem, smem, hbm, hbm],
        out_specs=[pl.BlockSpec(memory_space=pltpu.VMEM)] * (1 + groups),
        scratch_shapes=[pltpu.SemaphoreType.DMA((rows + 1,))],
        compiler_params=params(),
        name="pick",
    )(plan, place, mine, tokens, out_layer)


def project(parts, cotangent, gain, w_layer, out_layer, place):
    groups = len(parts)
    tokens, width = cotangent.shape
    head = out_layer.shape[0]
    wide = w_layer.shape[1]
    block = tokens // groups
    step = min(width, 1024)

    def kernel(place_ref, *refs):
        part_refs = refs[:groups]
        cot_ref, g_ref, w_ref, o_ref, x_ref, xz_ref, n_ref, acc, square = refs[groups:]
        k = pl.program_id(0)

        @pl.when(k == 0)
        def _():
            acc[...] = jnp.zeros_like(acc)
            square[...] = jnp.zeros_like(square)

        for r in range(groups):
            source = lax.rem(place_ref[0] + groups - r, groups)
            rows = pl.ds(pl.multiple_of(source * block, block), block)
            x_ref[rows, :] = part_refs[r][...]
        x = x_ref[...]
        xf = x.astype(F32)
        acc[:, :wide] += dot_nn((xf * g_ref[...]).astype(BF16), w_ref[...])
        acc[:, wide : wide + head] += dot_nt(x, o_ref[...])
        acc[:, wide + head :] += dot_nt(cot_ref[...], o_ref[...])
        square[...] += jnp.sum(xf * xf, axis=1, keepdims=True)

        @pl.when(k == pl.num_programs(0) - 1)
        def _():
            xz_ref[...] = acc[...].astype(BF16)
            n_ref[...] = square[...]

    spec = lambda shape, index: pl.BlockSpec(shape, index)
    return pl.pallas_call(
        kernel,
        grid=(width // step,),
        out_shape=[
            jax.ShapeDtypeStruct((tokens, width), BF16),
            jax.ShapeDtypeStruct((tokens, wide + 2 * head), BF16),
            jax.ShapeDtypeStruct((tokens, 1), F32),
        ],
        in_specs=[pl.BlockSpec(memory_space=pltpu.SMEM)]
        + [spec((block, step), lambda k: (0, k))] * groups
        + [
            spec((tokens, step), lambda k: (0, k)),
            spec((1, step), lambda k: (0, k)),
            spec((step, wide), lambda k: (k, 0)),
            spec((head, step), lambda k: (0, k)),
        ],
        out_specs=[
            spec((tokens, step), lambda k: (0, k)),
            spec((tokens, wide + 2 * head), lambda k: (0, 0)),
            spec((tokens, 1), lambda k: (0, 0)),
        ],
        scratch_shapes=[
            pltpu.VMEM((tokens, wide + 2 * head), F32),
            pltpu.VMEM((tokens, 1), F32),
        ],
        compiler_params=params(),
        name="project",
    )(place, *parts, cotangent, gain, w_layer, out_layer)


def couple(slices, gain, w_layer, out_layer, last):
    sections = len(slices)
    count, width = slices[0].shape
    head = out_layer.shape[0]
    wide = w_layer.shape[1]
    step = min(width, 1024)
    below = (sections - 2) * wide
    packed = below + max(wide, (sections - 1) * head)

    def kernel(last_ref, *refs):
        r_refs = refs[:sections]
        g_ref, w_ref, o_ref, out_ref, stack_ref, acc = refs[sections:]
        k = pl.program_id(0)

        @pl.when(k == 0)
        def _():
            acc[...] = jnp.zeros_like(acc)

        for i in range(1, sections):
            stack_ref[i - 1] = r_refs[i][...]
        r = jnp.concatenate([ref[...] for ref in r_refs], axis=0)
        acc[:, :wide] += dot_nn((r.astype(F32) * g_ref[...]).astype(BF16), w_ref[...])
        acc[:, wide:] += dot_nt(r, o_ref[...])

        @pl.when(k == pl.num_programs(0) - 1)
        def _():
            out_ref[...] = jnp.zeros_like(out_ref)
            rows = [slice(r * count, (r + 1) * count) for r in range(sections)]
            for r in range(1, sections - 1):
                out_ref[:, (r - 1) * wide : r * wide] = acc[rows[r], :wide].astype(BF16)

            @pl.when(last_ref[0] == 1)
            def _():
                out_ref[:, below : below + wide] = acc[rows[-1], :wide].astype(BF16)

            @pl.when(last_ref[0] == 0)
            def _():
                for r in range(sections - 1):
                    cols = slice(below + r * head, below + (r + 1) * head)
                    out_ref[:, cols] = acc[rows[r], wide:].astype(BF16)

    return pl.pallas_call(
        kernel,
        grid=(width // step,),
        out_shape=[
            jax.ShapeDtypeStruct((count, packed), BF16),
            jax.ShapeDtypeStruct((sections - 1, count, width), BF16),
        ],
        in_specs=[pl.BlockSpec(memory_space=pltpu.SMEM)]
        + [pl.BlockSpec((count, step), lambda k: (0, k))] * sections
        + [
            pl.BlockSpec((1, step), lambda k: (0, k)),
            pl.BlockSpec((step, wide), lambda k: (k, 0)),
            pl.BlockSpec((head, step), lambda k: (0, k)),
        ],
        out_specs=[
            pl.BlockSpec((count, packed), lambda k: (0, 0)),
            pl.BlockSpec((sections - 1, count, step), lambda k: (0, 0, k)),
        ],
        scratch_shapes=[pltpu.VMEM((sections * count, wide + head), F32)],
        compiler_params=params(),
        name="couple",
    )(last, *slices, gain, w_layer, out_layer)


def layout(sections, wide, head):
    through, across, at = {}, {}, 0
    for k in range(sections):
        for j in range(k):
            through[j, k] = slice(at, at + wide)
            at += wide
        for j in range(k + 1 if k < sections - 1 else 0):
            across[j, k] = slice(at, at + head)
            at += head
    return through, across, at


def compact(parts, section, wide, head):
    sections = len(parts)
    count = parts[0].shape[0]
    below = (sections - 2) * wide
    through, across, total = layout(sections, wide, head)

    def kernel(s_ref, *refs):
        part_refs, out_ref = refs[:sections], refs[sections]
        mine = s_ref[0]

        def fill(k, r):
            for j in range(k):
                at = (k - j - 1) * wide
                out_ref[:, through[j, k]] = part_refs[r][:, at : at + wide]
            for j in range(k + 1 if k < sections - 1 else 0):
                at = below + (k - j) * head
                out_ref[:, across[j, k]] = part_refs[r][:, at : at + head]

        for s in range(sections):

            @pl.when(mine == s)
            def _(s=s):
                for r in range(sections):
                    fill((s - r) % sections, r)

    vmem = pl.BlockSpec(memory_space=pltpu.VMEM)
    return pl.pallas_call(
        kernel,
        out_shape=jax.ShapeDtypeStruct((count, total), BF16),
        in_specs=[pl.BlockSpec(memory_space=pltpu.SMEM)] + [vmem] * sections,
        out_specs=vmem,
        compiler_params=params(SMALL),
        name="compact",
    )(section, *parts)


def serial(xz, pieces, places, norms, mask, section, width, head):
    sections = len(xz)
    tokens = norms.shape[0]
    wide = 3 * head
    scale = 1.0 / math.sqrt(head)
    through_at, across_at, _ = layout(sections, wide, head)
    count, packed = pieces[0].shape[-2:]
    plane = head // count
    n_in = sections + len(pieces)
    copies = sections + plane

    def kernel(s_ref, p_ref, *refs):
        xz_refs, piece_refs = refs[:sections], refs[sections:n_in]
        n_ref, mask_ref, v_ref, t_ref, a_ref = refs[n_in : n_in + 5]
        xz_all, table, mixes, weights, projs, dmix, sems = refs[n_in + 5 :]
        mine = s_ref[0]
        started = []

        def start(source, target):
            copy = pltpu.make_async_copy(source, target, sems.at[len(started)])
            copy.start()
            started.append(copy)

        for r in range(sections):
            start(xz_refs[r], xz_all.at[lax.rem(mine + sections - r, sections)])
        at = 0
        for ref in piece_refs:
            for i in range(ref.shape[0]):
                start(ref.at[i], table.at[p_ref[at]])
                at += 1
        for copy in started:
            copy.wait()

        def through(j, k):
            return table[:, :, through_at[j, k]].reshape(head, wide)

        def across(j, k):
            return table[:, :, across_at[j, k]].reshape(head, head)

        allowed = mask_ref[...] > 0.5
        norm = n_ref[...]
        rstds, tails, mixed = [], [], []
        for s in range(sections):
            proj = xz_all[s, :, :wide].astype(F32)
            for j in range(s):
                proj = proj + dot_nn(mixed[j], through(j, s))
            rstd = lax.rsqrt(norm * (1.0 / width) + EPS)
            proj = proj * rstd
            projs[s] = proj.astype(BF16)
            q, k, v = (projs[s, :, i * head : (i + 1) * head] for i in range(3))
            scores = jnp.where(allowed, dot_nt(q, k) * scale, -1e30)
            scores = jnp.exp(scores - jnp.max(scores, axis=1, keepdims=True))
            soft = scores / jnp.sum(scores, axis=1, keepdims=True)
            weights[s] = soft
            mix = dot_nn(soft.astype(BF16), v).astype(BF16)
            mixed.append(mix)
            mixes[:, s * head : (s + 1) * head] = mix
            rstds.append(rstd)
            dmix[:, s * head : (s + 1) * head] = xz_all[s, :, wide + head :].astype(F32)
            if s == sections - 1:
                break
            y = xz_all[s, :, wide : wide + head].astype(F32)
            for j in range(s):
                y = y + dot_nn(mixed[j], across(j, s))
            tail = y + dot_nn(mix, across(s, s))
            norm = norm + jnp.sum(mix.astype(F32) * (y + tail), axis=1, keepdims=True)
            norm = jnp.maximum(norm, 0.0)
            tails.append(tail)
        total = jnp.zeros((tokens, 1), F32)
        a_ref[...] = jnp.zeros_like(a_ref)
        for s in reversed(range(sections)):
            cols = slice(s * head, (s + 1) * head)
            da = dmix[:, cols]
            if s < sections - 1:
                da = da - total * tails[s]
            da = da.astype(BF16)
            q, k, v = (projs[s, :, i * head : (i + 1) * head] for i in range(3))
            soft = weights[s]
            dv = dot_tn(soft.astype(BF16), da)
            dsoft = dot_nt(da, v)
            dscore = soft * (dsoft - jnp.sum(dsoft * soft, axis=1, keepdims=True))
            dscore = (dscore * scale).astype(BF16)
            dproj = jnp.concatenate([dot_nn(dscore, k), dot_tn(dscore, q), dv], axis=1)
            along = jnp.sum(dproj * projs[s].astype(F32), axis=1, keepdims=True)
            first = (dproj * rstds[s]).astype(BF16)
            second = (-total * mixes[:, cols].astype(F32)).astype(BF16)
            total = total + rstds[s] * rstds[s] * along * (1.0 / width)
            for j in reversed(range(s)):
                term = dot_nt(first, through(j, s))
                if s < sections - 1:
                    term = term + dot_nt(second, across(j, s))
                dmix[:, j * head : (j + 1) * head] += term

            @pl.when(mine == s)
            def _(first=first, second=second, total=total):
                v_ref[:, :wide] = first
                v_ref[:, wide:] = second
                t_ref[...] = total

            for r in range(1, sections - s):

                @pl.when(mine == s + r)
                def _(r=r, cols=cols):
                    a_ref[:, (r - 1) * head : r * head] = mixes[:, cols]

    vmem = pl.BlockSpec(memory_space=pltpu.VMEM)
    smem = pl.BlockSpec(memory_space=pltpu.SMEM)
    return pl.pallas_call(
        kernel,
        out_shape=[
            jax.ShapeDtypeStruct((tokens, wide + head), BF16),
            jax.ShapeDtypeStruct((tokens, 1), F32),
            jax.ShapeDtypeStruct((tokens, (sections - 1) * head), BF16),
        ],
        in_specs=[smem, smem] + [pl.BlockSpec(memory_space=pl.ANY)] * n_in + [vmem, vmem],
        out_specs=[vmem] * 3,
        scratch_shapes=[
            pltpu.VMEM((sections,) + xz[0].shape, BF16),
            pltpu.VMEM((plane, count, packed), BF16),
            pltpu.VMEM((tokens, sections * head), BF16),
            pltpu.VMEM((sections, tokens, tokens), F32),
            pltpu.VMEM((sections, tokens, wide), BF16),
            pltpu.VMEM((tokens, sections * head), F32),
            pltpu.SemaphoreType.DMA((copies,)),
        ],
        compiler_params=params(),
        name="serial",
    )(section, places, *xz, *pieces, norms, mask)


def widen(sent, gain, w_layer, out_layer, chunk):
    tokens = sent.shape[0]
    head, width = out_layer.shape
    wide = w_layer.shape[1]
    step = min(width, 1024)
    inner = step // chunk

    def kernel(v_ref, g_ref, w_ref, o_ref, back_ref, b_ref):
        back = dot_nt(v_ref[:, :wide], w_ref[...])
        own = back * g_ref[...] + dot_nn(v_ref[:, wide:], o_ref[...])
        back_ref[...] = back.astype(BF16)
        for i in range(inner):
            b_ref[i] = own[:, i * chunk : (i + 1) * chunk].astype(BF16)

    return pl.pallas_call(
        kernel,
        grid=(width // step,),
        out_shape=[
            jax.ShapeDtypeStruct((tokens, width), BF16),
            jax.ShapeDtypeStruct((width // chunk, tokens, chunk), BF16),
        ],
        in_specs=[
            pl.BlockSpec((tokens, wide + head), lambda k: (0, 0)),
            pl.BlockSpec((1, step), lambda k: (0, k)),
            pl.BlockSpec((step, wide), lambda k: (k, 0)),
            pl.BlockSpec((head, step), lambda k: (0, k)),
        ],
        out_specs=[
            pl.BlockSpec((tokens, step), lambda k: (0, k)),
            pl.BlockSpec((inner, tokens, chunk), lambda k: (k, 0, 0)),
        ],
        compiler_params=params(),
        name="widen",
    )(sent, gain, w_layer, out_layer)


def settle(total, mixes, stacks, places, x, cotangent, back, own):
    tokens, width = x.shape
    chunk = own.shape[2]
    layers, count = stacks[0].shape[1:3]
    entries = [(i, e) for i, stack in enumerate(stacks) for e in range(stack.shape[0])]
    plane = len(entries)
    head = plane * count
    step = min(width, 1024)
    inner = step // chunk
    lanes = head

    def kernel(p_ref, t_ref, a_ref, x_ref, c_ref, back_ref, b_ref, *refs):
        stack_refs = refs[: len(stacks)]
        f_ref, out_ref, dg_ref, lower, sems = refs[len(stacks) :]

        @pl.when(pl.program_id(0) == 0)
        def _():
            copies = []
            for at, (i, e) in enumerate(entries):
                for r in range(layers):
                    copy = pltpu.make_async_copy(
                        stack_refs[i].at[e, r], lower.at[r, p_ref[at]], sems.at[at * layers + r]
                    )
                    copy.start()
                    copies.append(copy)
            for copy in copies:
                copy.wait()

        cols = pl.ds(pl.multiple_of(pl.program_id(0) * step, step), step)
        here = x_ref[...].astype(F32)
        here = here + dot_nn(a_ref[...], lower[:, :, :, cols].reshape(layers * head, step))
        rest = c_ref[...].astype(F32) - t_ref[...] * here
        for i in range(inner):
            at = slice(i * chunk, (i + 1) * chunk)
            full = rest[:, at] + b_ref[i].astype(F32)
            f_ref[:, at] = full
            out_ref[:, at] = full.astype(BF16)
        gain = jnp.sum(back_ref[...].astype(F32) * here, axis=0, keepdims=True)
        for i in range(step // lanes):
            dg_ref[i : i + 1, :] = gain[:, i * lanes : (i + 1) * lanes]

    cols = lambda k: (0, k)
    whole = lambda k: (0, 0)
    return pl.pallas_call(
        kernel,
        grid=(width // step,),
        out_shape=[
            jax.ShapeDtypeStruct((tokens, width), F32),
            jax.ShapeDtypeStruct((tokens, width), BF16),
            jax.ShapeDtypeStruct((width // lanes, lanes), F32),
        ],
        in_specs=[
            pl.BlockSpec(memory_space=pltpu.SMEM),
            pl.BlockSpec((tokens, 1), whole),
            pl.BlockSpec((tokens, layers * head), whole),
            pl.BlockSpec((tokens, step), cols),
            pl.BlockSpec((tokens, step), cols),
            pl.BlockSpec((tokens, step), cols),
            pl.BlockSpec((inner, tokens, chunk), lambda k: (k, 0, 0)),
        ]
        + [pl.BlockSpec(memory_space=pl.ANY)] * len(stacks),
        out_specs=[
            pl.BlockSpec((tokens, step), cols),
            pl.BlockSpec((tokens, step), cols),
            pl.BlockSpec((step // lanes, lanes), lambda k: (k, 0)),
        ],
        scratch_shapes=[
            pltpu.VMEM((layers, plane, count, width), BF16),
            pltpu.SemaphoreType.DMA((plane * layers,)),
        ],
        compiler_params=params(),
        name="settle",
    )(places, total, mixes, x, cotangent, back, own, *stacks)


def send_on(index, arrived, own):
    _, tokens, chunk = own.shape

    def kernel(i_ref, r_ref, b_ref, send_ref):
        send_ref[...] = (b_ref[0].astype(F32) + r_ref[...].astype(F32)).astype(BF16)

    return pl.pallas_call(
        kernel,
        grid_spec=pltpu.PrefetchScalarGridSpec(
            num_scalar_prefetch=1,
            grid=(1,),
            in_specs=[
                pl.BlockSpec((tokens, chunk), lambda k, i: (0, 0)),
                pl.BlockSpec((1, tokens, chunk), lambda k, i: (i[0], 0, 0)),
            ],
            out_specs=pl.BlockSpec((tokens, chunk), lambda k, i: (0, 0)),
        ),
        out_shape=jax.ShapeDtypeStruct((tokens, chunk), BF16),
        compiler_params=params(SMALL),
        name="send_on",
    )(index, arrived, own)


def put_out(index, arrived, full, out):
    streams = len(arrived)
    tokens, chunk = arrived[0].shape
    block = streams * chunk

    def kernel(i_ref, *refs):
        r_refs = refs[:streams]
        f_ref, _, out_ref = refs[streams:]
        for i in range(streams):
            at = slice(i * chunk, (i + 1) * chunk)
            out_ref[:, at] = (f_ref[:, at] + r_refs[i][...].astype(F32)).astype(BF16)

    return pl.pallas_call(
        kernel,
        grid_spec=pltpu.PrefetchScalarGridSpec(
            num_scalar_prefetch=1,
            grid=(1,),
            in_specs=[pl.BlockSpec((tokens, chunk), lambda k, i: (0, 0))] * streams
            + [
                pl.BlockSpec((tokens, block), lambda k, i: (0, i[0])),
                pl.BlockSpec(memory_space=pl.ANY),
            ],
            out_specs=pl.BlockSpec((tokens, block), lambda k, i: (0, i[0])),
        ),
        out_shape=jax.ShapeDtypeStruct(out.shape, BF16),
        input_output_aliases={streams + 2: 0},
        compiler_params=params(SMALL),
        name="put_out",
    )(index, *arrived, full, out)


STREAMS = 2
CHUNKS = 4


def shifted(array, by):
    sections = lax.axis_size("section")
    return lax.ppermute(array, "section", [(i, (i + by) % sections) for i in range(sections)])


def raised(array, by):
    sections = lax.axis_size("section")
    return lax.ppermute(array, "section", [(i, i + by) for i in range(sections - by)])


def swapped(array, step):
    groups = lax.axis_size("group")
    devices = lax.axis_size("dp")
    bits = devices.bit_length() - 1
    pairs = []
    for p in range(devices):
        for g in range(groups):
            pairs.append((p * groups + g, (p ^ (1 << ((step + g) % bits))) * groups + g))
    return lax.ppermute(array, ("dp", "group"), pairs)


def handed(array, by):
    groups = lax.axis_size("group")
    return lax.ppermute(array, "group", [(i, (i + by) % groups) for i in range(groups)])


def spread(array, before_last=(), before_groups=()):
    bits = lax.axis_size("dp").bit_length() - 1
    stacks = [array[None]]
    for step in range(bits):
        together = stacks[0] if step == 0 else jnp.concatenate([together, stacks[-1]], axis=0)
        if step == bits - 1:
            together = tied(together, *before_last)
        stacks.append(swapped(together, step))
    stacks = stacks[-1:] if bits == 0 else [together, stacks[-1]]
    own = [tied(stack, *before_groups) for stack in stacks]
    for r in range(1, lax.axis_size("group")):
        stacks = stacks + [handed(stack, r) for stack in own]
    return stacks


def plane_places():
    groups = lax.axis_size("group")
    bits = lax.axis_size("dp").bit_length() - 1
    masks = []
    for g in range(groups):
        order = [0]
        for step in range(bits):
            order = order + [m ^ (1 << ((step + g) % bits)) for m in order]
        masks.append(order)
    masks = jnp.asarray(masks, jnp.int32)
    dp, member = lax.axis_index("dp"), lax.axis_index("group")
    places = []
    for r in range(groups):
        giver = (member + groups - r) % groups
        places.append((dp ^ masks[giver]) * groups + giver)
    return jnp.concatenate(places).astype(jnp.int32)


def local(tokens_in, cotangent, gains, w_qkv, w_out, segments, plan):
    sections = lax.axis_size("section")
    groups = lax.axis_size("group")
    devices = lax.axis_size("dp")
    plane = devices * groups
    section = lax.axis_index("section")
    member = lax.axis_index("group")
    rows_dev = plan.shape[1]
    length = segments.shape[1]
    tokens, width = tokens_in.shape
    head = w_out.shape[1]
    share = rows_dev // groups
    w_layer, out_layer = w_qkv[0], w_out[0]
    place = member.astype(jnp.int32)[None]
    layer = section.astype(jnp.int32)[None]

    slice_rows = head // plane
    mine = lax.axis_index("dp") * groups + member
    own_rows, *parts = pick(
        tokens_in.reshape(rows_dev, length, width),
        plan,
        place,
        groups,
        out_layer,
        mine.astype(jnp.int32)[None],
        slice_rows,
    )
    slices = [own_rows] + [raised(own_rows, r) for r in range(1, sections)]
    chosen = jnp.take(segments, plan[0], axis=0, mode="clip").astype(BF16)
    chosen = chosen.reshape(groups, share, length)
    moved, moved_seg = [], []
    for r in range(groups):
        outgoing = lax.dynamic_index_in_dim(chosen, (member + r) % groups, 0, keepdims=False)
        moved.append(handed(parts[r], r) if r else parts[r])
        moved_seg.append(handed(outgoing, r) if r else outgoing)
    moved = [part.reshape(share * length, width) for part in moved]
    order = (member - jnp.arange(groups)) % groups
    seg = jnp.take(jnp.stack(moved_seg), order, axis=0, mode="clip").reshape(tokens)
    at = jnp.arange(tokens)
    mask = (
        (at[:, None] >= at[None, :])
        & (at[:, None] // length == at[None, :] // length)
        & (seg[:, None] == seg[None, :])
    ).astype(F32)

    x, xz, norms = project(moved, cotangent, gains, w_layer, out_layer, place)

    last = (section == sections - 1).astype(jnp.int32)[None]
    places = plane_places()
    xz_all = [xz] + [shifted(xz, r) for r in range(1, sections)]
    slices[0] = tied(slices[0], mask, places, *xz_all[:2])
    coupling, stack = couple(slices, gains, w_layer, out_layer, last)
    others = [shifted(coupling, r) for r in range(1, sections)]
    coupling = compact([tied(coupling, *xz_all)] + others, layer, 3 * head, head)
    pieces = spread(coupling)
    sent, total, mixes = serial(xz_all, pieces, places, norms, mask, layer, width, head)

    stacks = spread(stack, pieces, [sent])

    chunk = width // (STREAMS * CHUNKS)
    back, own = widen(sent, gains, w_layer, out_layer, chunk)
    full, out, gain = settle(total, mixes, stacks, places, x, cotangent, back, own)
    gains_on = [gain]
    for step in range(devices.bit_length() - 1):
        gains_on.append(gains_on[-1] + swapped(gains_on[-1], step))
    gain_whole = sum([handed(gains_on[-1], r) for r in range(1, groups)], gains_on[-1])
    gain_whole = gain_whole.reshape(1, width)
    gains_on = gains_on[1:] + [gain_whole]

    down = [(i, i - 1) for i in range(1, sections)]
    behind = sections - 1 - section

    def index(tick):
        return jnp.clip(tick - behind, 0, CHUNKS - 1).astype(jnp.int32)

    leaving = [
        lax.dynamic_index_in_dim(own, index(0) * STREAMS + stream, 0, keepdims=False)
        for stream in range(STREAMS)
    ]
    ticks = CHUNKS + sections - 1
    own = tied(own, full)
    for tick in range(1, ticks):
        arrived = []
        for stream in range(STREAMS):
            arrived.append(lax.ppermute(leaving[stream], "section", down))
            if tick < ticks - 1:
                at_chunk = (index(tick) * STREAMS + stream)[None]
                leaving[stream] = send_on(at_chunk, arrived[stream], own)
        out = put_out(index(tick)[None], arrived, full, out)
        own = tied(own, out, *gains_on[tick - 1 : tick])
    return (out[None], gain_whole)


def attend(hidden, segment, gain_row, w_layer, out_layer):
    count, length, width = hidden.shape
    head = out_layer.shape[0]
    scaled = hidden * lax.rsqrt(jnp.mean(hidden * hidden, axis=-1, keepdims=True) + EPS) * gain_row
    normed = scaled.astype(BF16).reshape(count * length, width)
    projected = jnp.dot(normed, w_layer, preferred_element_type=F32).reshape(count, length, 3 * head)
    query = projected[:, :, :head]
    keyed = projected[:, :, head : 2 * head]
    valued = projected[:, :, 2 * head :]
    positions = jnp.arange(length)
    allowed = (positions[:, None] >= positions[None, :])[None] & (
        segment[:, :, None] == segment[:, None, :]
    )
    scores = jnp.einsum("rid,rjd->rij", query, keyed, precision=lax.Precision.HIGHEST)
    scores = jnp.where(allowed, scores / math.sqrt(head), -1e30)
    weights = jax.nn.softmax(scores, axis=-1)
    mixed = jnp.einsum("rij,rjd->rid", weights, valued, precision=lax.Precision.HIGHEST)
    mixed = mixed.astype(BF16).reshape(count * length, head)
    output = jnp.dot(mixed, out_layer, preferred_element_type=F32).reshape(count, length, width)
    return hidden + output


MB_ROWS = 2


def relay(tokens_in, cotangent, gains, w_qkv, w_out, segments, plan):
    sections = lax.axis_size("section")
    section = lax.axis_index("section")
    rows_dev = plan.shape[1]
    width = tokens_in.shape[1]
    length = segments.shape[1]
    micro = rows_dev // MB_ROWS
    blocks = tokens_in.reshape(rows_dev, length, width)
    chosen = jnp.take(blocks, plan[0], axis=0)
    chosen_seg = jnp.take(segments, plan[0], axis=0).astype(BF16)
    assigned = lax.all_to_all(chosen, "group", split_axis=0, concat_axis=0, tiled=True)
    moved_seg = lax.all_to_all(chosen_seg, "group", split_axis=0, concat_axis=0, tiled=True)
    assigned = assigned.reshape(micro, MB_ROWS, length, width)
    seg_groups = moved_seg.reshape(micro, MB_ROWS, length)
    gain_row, w_layer, out_layer = gains[0], w_qkv[0], w_out[0]
    grad_rows = cotangent.reshape(micro, MB_ROWS, length, width)
    ticks = micro + sections - 1

    def passed_along(array, by):
        pairs = [(i, i + by) for i in range(sections) if 0 <= i + by < sections]
        return lax.ppermute(array, "section", pairs)

    def at(array, i):
        return lax.dynamic_index_in_dim(array, i, 0, keepdims=False)

    def forward_tick(tick, carry):
        saved, arrived = carry
        index = tick - section
        valid = (index >= 0) & (index < micro)
        clipped = jnp.clip(index, 0, micro - 1)
        entering = jnp.where(section == 0, at(assigned, clipped), arrived)
        kept = jnp.where(valid, entering, at(saved, clipped))
        saved = lax.dynamic_update_index_in_dim(saved, kept, clipped, 0)
        segment = at(seg_groups, clipped)

        def run_layer(value):
            return attend(value.astype(F32), segment, gain_row, w_layer, out_layer).astype(BF16)

        leaving = lax.cond(valid, run_layer, jnp.zeros_like, entering)
        return (saved, passed_along(leaving, 1))

    saved_init = jnp.zeros((micro, MB_ROWS, length, width), BF16)
    arrive_init = jnp.zeros((MB_ROWS, length, width), BF16)
    saved, _ = lax.fori_loop(0, ticks, forward_tick, (saved_init, arrive_init))

    def backward_tick(tick, carry):
        grads_x, gain_total, arrived = carry
        index = tick - (sections - 1 - section)
        valid = (index >= 0) & (index < micro)
        clipped = jnp.clip(index, 0, micro - 1)
        entering = jnp.where(section == sections - 1, at(grad_rows, clipped), arrived)
        segment = at(seg_groups, clipped)
        stored = at(saved, clipped).astype(F32)

        def local_layer(hidden, gains_here):
            return attend(hidden, segment, gains_here, w_layer, out_layer)

        def run_back(value):
            _, pullback = jax.vjp(local_layer, stored, gain_row)
            grad_hidden, grad_gain = pullback(value.astype(F32))
            return (grad_hidden.astype(BF16), grad_gain)

        def skip_back(value):
            return (jnp.zeros_like(value), jnp.zeros(gain_row.shape, F32))

        sending, grad_gain = lax.cond(valid, run_back, skip_back, entering)
        kept = jnp.where(valid, sending, at(grads_x, clipped))
        grads_x = lax.dynamic_update_index_in_dim(grads_x, kept, clipped, 0)
        return (grads_x, gain_total + grad_gain, passed_along(sending, -1))

    gain_init = jnp.zeros(gain_row.shape, F32)
    grads_x, gain_total, _ = lax.fori_loop(
        0, ticks, backward_tick, (saved_init, gain_init, arrive_init)
    )
    gain_whole = lax.psum(gain_total, ("dp", "group"))
    return (grads_x.reshape(1, rows_dev * length, width), gain_whole[None])


def solution(mesh):
    placed = (
        P(("dp", "group"), None),
        P(("dp", "group"), None),
        P("section", None),
        P("section", None, None),
        P("section", None, None),
        P(("dp", "group"), None),
        P(("dp", "group"), None),
    )

    def chosen(tokens_in, cotangent, gains, w_qkv, w_out, segments, plan):
        sections, head, width = w_out.shape
        devices = mesh.shape["dp"]
        small = sections * 4 * head < width and devices & (devices - 1) == 0
        body = local if small and sections > 1 else relay
        return jax.shard_map(
            body,
            mesh=mesh,
            in_specs=placed,
            out_specs=(P("section", ("dp", "group"), None), P("section", None)),
            check_vma=False,
        )(tokens_in, cotangent, gains, w_qkv, w_out, segments, plan)

    return chosen
```

```python
import math

import jax
import jax.numpy as jnp
from jax import lax
from jax.experimental import pallas as pl
from jax.experimental.pallas import tpu as pltpu
from jax.sharding import PartitionSpec as P

EPS = 1e-05
VMEM_BYTES = 24 * 1024 * 1024
SMALL = 16 * 1024 * 1024
F32 = jnp.float32
BF16 = jnp.bfloat16


def dot_nn(a, b):
    return lax.dot_general(a, b, (((1,), (0,)), ((), ())), preferred_element_type=F32)


def dot_nt(a, b):
    return lax.dot_general(a, b, (((1,), (1,)), ((), ())), preferred_element_type=F32)


def dot_tn(a, b):
    return lax.dot_general(a, b, (((0,), (0,)), ((), ())), preferred_element_type=F32)


def tied(array, *others):
    return lax.optimization_barrier((array,) + others)[0]


IN_HBM = pl.BlockSpec(memory_space=pltpu.HBM)
ANYWHERE = pl.BlockSpec(memory_space=pl.ANY)
IN_VMEM = pl.BlockSpec(memory_space=pltpu.VMEM)
IN_SMEM = pl.BlockSpec(memory_space=pltpu.SMEM)


def in_hbm(array):
    return pltpu.with_memory_space_constraint(array, pltpu.HBM)


def in_vmem(array):
    return pltpu.with_memory_space_constraint(array, pltpu.VMEM)


def mover(sems):
    used = []

    def start(source, target):
        copy = pltpu.make_async_copy(source, target, sems.at[len(used)])
        copy.start()
        used.append(copy)
        return copy

    return start


def steps(width):
    step = min(width, 1024)
    return [slice(at, at + step) for at in range(0, width, step)]


def params(limit=VMEM_BYTES):
    return pltpu.CompilerParams(vmem_limit_bytes=limit)


def pick(tokens, plan, place, groups, out_layer, mine, slice_rows):
    rows, length, width = tokens.shape
    share = rows // groups

    def kernel(plan_ref, place_ref, mine_ref, tokens_ref, o_ref, *rest):
        slice_ref, parts = rest[0], rest[1 : 1 + groups]
        slice_in, rows_in, sems = rest[1 + groups :]
        start = mover(sems)
        at = pl.ds(pl.multiple_of(mine_ref[0] * slice_rows, slice_rows), slice_rows)
        loads = [(start(o_ref.at[at], slice_in), slice_in, slice_ref)]
        for r in range(groups):
            target = lax.rem(place_ref[0] + r, groups)
            for c in range(share):
                here = rows_in.at[r * share + c]
                row = plan_ref[0, target * share + c]
                loads.append((start(tokens_ref.at[row], here), here, parts[r].at[c]))
        stores = []
        for load, here, there in loads:
            load.wait()
            stores.append(start(here, there))
        for store in stores:
            store.wait()

    return pl.pallas_call(
        kernel,
        out_shape=[pltpu.HBM((slice_rows, width), BF16)]
        + [pltpu.HBM((share, length, width), BF16)] * groups,
        in_specs=[IN_SMEM, IN_SMEM, IN_SMEM, IN_HBM, IN_HBM],
        out_specs=[IN_HBM] * (1 + groups),
        scratch_shapes=[
            pltpu.VMEM((slice_rows, width), BF16),
            pltpu.VMEM((rows, length, width), BF16),
            pltpu.SemaphoreType.DMA((2 * rows + 2,)),
        ],
        compiler_params=params(),
        name="pick",
    )(plan, place, mine, in_hbm(tokens), in_hbm(out_layer))


def project(parts, cotangent, gain, w_layer, out_layer, place):
    groups = len(parts)
    tokens, width = cotangent.shape
    head = out_layer.shape[0]
    wide = w_layer.shape[1]
    block = tokens // groups
    cuts = steps(width)
    copies = len(cuts) * (groups + 4)

    def kernel(place_ref, *refs):
        part_refs = refs[:groups]
        cot_ref, g_ref, w_ref, o_ref, x_ref, xz_ref, n_ref = refs[groups : groups + 7]
        x_in, c_in, w_in, o_in, sems = refs[groups + 7 :]
        start = mover(sems)
        loads = []
        for cut in cuts:
            mine = [start(w_ref.at[cut], w_in.at[cut])]
            mine.append(start(o_ref.at[:, cut], o_in.at[:, cut]))
            for r in range(groups):
                source = lax.rem(place_ref[0] + groups - r, groups)
                rows = pl.ds(pl.multiple_of(source * block, block), block)
                mine.append(start(part_refs[r].at[:, cut], x_in.at[rows, cut]))
            mine.append(start(cot_ref.at[:, cut], c_in.at[:, cut]))
            loads.append(mine)
        through = jnp.zeros((tokens, wide), F32)
        across = jnp.zeros((tokens, head), F32)
        back = jnp.zeros((tokens, head), F32)
        square = jnp.zeros((tokens, 1), F32)
        stores = []
        for cut, mine in zip(cuts, loads):
            for load in mine:
                load.wait()
            stores.append(start(x_in.at[:, cut], x_ref.at[:, cut]))
            x = x_in[:, cut]
            xf = x.astype(F32)
            through += dot_nn((xf * g_ref[:, cut]).astype(BF16), w_in[cut, :])
            across += dot_nt(x, o_in[:, cut])
            back += dot_nt(c_in[:, cut], o_in[:, cut])
            square += jnp.sum(xf * xf, axis=1, keepdims=True)
        xz_ref[:, :wide] = through.astype(BF16)
        xz_ref[:, wide : wide + head] = across.astype(BF16)
        xz_ref[:, wide + head :] = back.astype(BF16)
        n_ref[...] = square
        for store in stores:
            store.wait()

    return pl.pallas_call(
        kernel,
        out_shape=[
            pltpu.HBM((tokens, width), BF16),
            jax.ShapeDtypeStruct((tokens, wide + 2 * head), BF16),
            jax.ShapeDtypeStruct((tokens, 1), F32),
        ],
        in_specs=[IN_SMEM] + [ANYWHERE] * groups + [IN_HBM, IN_VMEM, IN_HBM, IN_HBM],
        out_specs=[IN_HBM, IN_VMEM, IN_VMEM],
        scratch_shapes=[
            pltpu.VMEM((tokens, width), BF16),
            pltpu.VMEM((tokens, width), BF16),
            pltpu.VMEM((width, wide), BF16),
            pltpu.VMEM((head, width), BF16),
            pltpu.SemaphoreType.DMA((copies,)),
        ],
        compiler_params=params(),
        name="project",
    )(
        place,
        *parts,
        in_hbm(cotangent),
        gain,
        in_hbm(w_layer),
        in_hbm(out_layer),
    )


def couple(slices, gain, w_layer, out_layer, last):
    sections = len(slices)
    count, width = slices[0].shape
    head = out_layer.shape[0]
    wide = w_layer.shape[1]
    below = (sections - 2) * wide
    packed = below + max(wide, (sections - 1) * head)
    cuts = steps(width)
    copies = len(cuts) * (sections + 2) + sections - 1

    def kernel(last_ref, *refs):
        s_refs = refs[:sections]
        g_ref, w_ref, o_ref, out_ref, stack_ref, r_in, w_in, o_in, sems = refs[sections:]
        rows = [slice(r * count, (r + 1) * count) for r in range(sections)]
        start = mover(sems)
        loads = []
        for cut in cuts:
            mine = [start(w_ref.at[cut], w_in.at[cut])]
            mine.append(start(o_ref.at[:, cut], o_in.at[:, cut]))
            for r in range(sections):
                mine.append(start(s_refs[r].at[:, cut], r_in.at[rows[r], cut]))
            loads.append(mine)
        through = jnp.zeros((sections * count, wide), F32)
        across = jnp.zeros((sections * count, head), F32)
        for cut, mine in zip(cuts, loads):
            for load in mine:
                load.wait()
            r = r_in[:, cut]
            through += dot_nn((r.astype(F32) * g_ref[:, cut]).astype(BF16), w_in[cut, :])
            across += dot_nt(r, o_in[:, cut])
        stores = [start(r_in.at[rows[r]], stack_ref.at[r - 1]) for r in range(1, sections)]
        through = through.astype(BF16)
        across = across.astype(BF16)
        out_ref[...] = jnp.zeros_like(out_ref)
        for r in range(1, sections - 1):
            out_ref[:, (r - 1) * wide : r * wide] = through[rows[r]]

        @pl.when(last_ref[0] == 1)
        def _():
            out_ref[:, below : below + wide] = through[rows[-1]]

        @pl.when(last_ref[0] == 0)
        def _():
            for r in range(sections - 1):
                out_ref[:, below + r * head : below + (r + 1) * head] = across[rows[r]]

        for store in stores:
            store.wait()

    return pl.pallas_call(
        kernel,
        out_shape=[
            jax.ShapeDtypeStruct((count, packed), BF16),
            pltpu.HBM((sections - 1, count, width), BF16),
        ],
        in_specs=[IN_SMEM] + [ANYWHERE] * sections + [IN_VMEM, IN_HBM, IN_HBM],
        out_specs=[IN_VMEM, IN_HBM],
        scratch_shapes=[
            pltpu.VMEM((sections * count, width), BF16),
            pltpu.VMEM((width, wide), BF16),
            pltpu.VMEM((head, width), BF16),
            pltpu.SemaphoreType.DMA((copies,)),
        ],
        compiler_params=params(),
        name="couple",
    )(last, *slices, gain, in_hbm(w_layer), in_hbm(out_layer))


def layout(sections, wide, head):
    through, across, at = {}, {}, 0
    for k in range(sections):
        for j in range(k):
            through[j, k] = slice(at, at + wide)
            at += wide
        for j in range(k + 1 if k < sections - 1 else 0):
            across[j, k] = slice(at, at + head)
            at += head
    return through, across, at


def compact(parts, section, wide, head):
    sections = len(parts)
    count = parts[0].shape[0]
    below = (sections - 2) * wide
    through, across, total = layout(sections, wide, head)

    def kernel(s_ref, *refs):
        part_refs, out_ref = refs[:sections], refs[sections]
        mine = s_ref[0]

        def fill(k, r):
            for j in range(k):
                at = (k - j - 1) * wide
                out_ref[:, through[j, k]] = part_refs[r][:, at : at + wide]
            for j in range(k + 1 if k < sections - 1 else 0):
                at = below + (k - j) * head
                out_ref[:, across[j, k]] = part_refs[r][:, at : at + head]

        for s in range(sections):

            @pl.when(mine == s)
            def _(s=s):
                for r in range(sections):
                    fill((s - r) % sections, r)

    vmem = pl.BlockSpec(memory_space=pltpu.VMEM)
    return pl.pallas_call(
        kernel,
        out_shape=jax.ShapeDtypeStruct((count, total), BF16),
        in_specs=[pl.BlockSpec(memory_space=pltpu.SMEM)] + [vmem] * sections,
        out_specs=vmem,
        compiler_params=params(SMALL),
        name="compact",
    )(section, *parts)


def serial(xz, pieces, places, norms, mask, section, width, head):
    sections = len(xz)
    tokens = norms.shape[0]
    wide = 3 * head
    scale = 1.0 / math.sqrt(head)
    through_at, across_at, _ = layout(sections, wide, head)
    count, packed = pieces[0].shape[-2:]
    plane = head // count
    n_in = sections + len(pieces)
    copies = sections + plane

    def kernel(s_ref, p_ref, *refs):
        xz_refs, piece_refs = refs[:sections], refs[sections:n_in]
        n_ref, mask_ref, v_ref, t_ref, a_ref = refs[n_in : n_in + 5]
        xz_all, table, mixes, weights, projs, dmix, sems = refs[n_in + 5 :]
        mine = s_ref[0]
        started = []

        def start(source, target):
            copy = pltpu.make_async_copy(source, target, sems.at[len(started)])
            copy.start()
            started.append(copy)

        for r in range(sections):
            start(xz_refs[r], xz_all.at[lax.rem(mine + sections - r, sections)])
        at = 0
        for ref in piece_refs:
            for i in range(ref.shape[0]):
                start(ref.at[i], table.at[p_ref[at]])
                at += 1
        for copy in started:
            copy.wait()

        def through(j, k):
            return table[:, :, through_at[j, k]].reshape(head, wide)

        def across(j, k):
            return table[:, :, across_at[j, k]].reshape(head, head)

        allowed = mask_ref[...] > 0.5
        norm = n_ref[...]
        rstds, tails, mixed = [], [], []
        for s in range(sections):
            proj = xz_all[s, :, :wide].astype(F32)
            for j in range(s):
                proj = proj + dot_nn(mixed[j], through(j, s))
            rstd = lax.rsqrt(norm * (1.0 / width) + EPS)
            proj = proj * rstd
            projs[s] = proj.astype(BF16)
            q, k, v = (projs[s, :, i * head : (i + 1) * head] for i in range(3))
            scores = jnp.where(allowed, dot_nt(q, k) * scale, -1e30)
            scores = jnp.exp(scores - jnp.max(scores, axis=1, keepdims=True))
            soft = scores / jnp.sum(scores, axis=1, keepdims=True)
            weights[s] = soft
            mix = dot_nn(soft.astype(BF16), v).astype(BF16)
            mixed.append(mix)
            mixes[:, s * head : (s + 1) * head] = mix
            rstds.append(rstd)
            dmix[:, s * head : (s + 1) * head] = xz_all[s, :, wide + head :].astype(F32)
            if s == sections - 1:
                break
            y = xz_all[s, :, wide : wide + head].astype(F32)
            for j in range(s):
                y = y + dot_nn(mixed[j], across(j, s))
            tail = y + dot_nn(mix, across(s, s))
            norm = norm + jnp.sum(mix.astype(F32) * (y + tail), axis=1, keepdims=True)
            norm = jnp.maximum(norm, 0.0)
            tails.append(tail)
        total = jnp.zeros((tokens, 1), F32)
        a_ref[...] = jnp.zeros_like(a_ref)
        for s in reversed(range(sections)):
            cols = slice(s * head, (s + 1) * head)
            da = dmix[:, cols]
            if s < sections - 1:
                da = da - total * tails[s]
            da = da.astype(BF16)
            q, k, v = (projs[s, :, i * head : (i + 1) * head] for i in range(3))
            soft = weights[s]
            dv = dot_tn(soft.astype(BF16), da)
            dsoft = dot_nt(da, v)
            dscore = soft * (dsoft - jnp.sum(dsoft * soft, axis=1, keepdims=True))
            dscore = (dscore * scale).astype(BF16)
            dproj = jnp.concatenate([dot_nn(dscore, k), dot_tn(dscore, q), dv], axis=1)
            along = jnp.sum(dproj * projs[s].astype(F32), axis=1, keepdims=True)
            first = (dproj * rstds[s]).astype(BF16)
            second = (-total * mixes[:, cols].astype(F32)).astype(BF16)
            total = total + rstds[s] * rstds[s] * along * (1.0 / width)
            for j in reversed(range(s)):
                term = dot_nt(first, through(j, s))
                if s < sections - 1:
                    term = term + dot_nt(second, across(j, s))
                dmix[:, j * head : (j + 1) * head] += term

            @pl.when(mine == s)
            def _(first=first, second=second, total=total):
                v_ref[:, :wide] = first
                v_ref[:, wide:] = second
                t_ref[...] = total

            for r in range(1, sections - s):

                @pl.when(mine == s + r)
                def _(r=r, cols=cols):
                    a_ref[:, (r - 1) * head : r * head] = mixes[:, cols]

    vmem = pl.BlockSpec(memory_space=pltpu.VMEM)
    smem = pl.BlockSpec(memory_space=pltpu.SMEM)
    return pl.pallas_call(
        kernel,
        out_shape=[
            jax.ShapeDtypeStruct((tokens, wide + head), BF16),
            jax.ShapeDtypeStruct((tokens, 1), F32),
            jax.ShapeDtypeStruct((tokens, (sections - 1) * head), BF16),
        ],
        in_specs=[smem, smem] + [ANYWHERE] * n_in + [vmem, vmem],
        out_specs=[vmem] * 3,
        scratch_shapes=[
            pltpu.VMEM((sections,) + xz[0].shape, BF16),
            pltpu.VMEM((plane, count, packed), BF16),
            pltpu.VMEM((tokens, sections * head), BF16),
            pltpu.VMEM((sections, tokens, tokens), F32),
            pltpu.VMEM((sections, tokens, wide), BF16),
            pltpu.VMEM((tokens, sections * head), F32),
            pltpu.SemaphoreType.DMA((copies,)),
        ],
        compiler_params=params(),
        name="serial",
    )(section, places, *xz, *pieces, norms, mask)


def widen(sent, gain, w_layer, out_layer, chunk):
    tokens = sent.shape[0]
    head, width = out_layer.shape
    wide = w_layer.shape[1]
    cuts = steps(width)

    def kernel(v_ref, g_ref, w_ref, o_ref, back_ref, b_ref, back_in, w_in, o_in, sems):
        start = mover(sems)
        loads = [
            (start(w_ref.at[cut], w_in.at[cut]), start(o_ref.at[:, cut], o_in.at[:, cut]))
            for cut in cuts
        ]
        stores = []
        for cut, mine in zip(cuts, loads):
            for load in mine:
                load.wait()
            back = dot_nt(v_ref[:, :wide], w_in[cut, :])
            own = back * g_ref[:, cut] + dot_nn(v_ref[:, wide:], o_in[:, cut])
            back_in[:, cut] = back.astype(BF16)
            stores.append(start(back_in.at[:, cut], back_ref.at[:, cut]))
            for at in range(0, own.shape[1], chunk):
                b_ref[(cut.start + at) // chunk] = own[:, at : at + chunk].astype(BF16)
        for store in stores:
            store.wait()

    return pl.pallas_call(
        kernel,
        out_shape=[
            pltpu.HBM((tokens, width), BF16),
            pltpu.VMEM((width // chunk, tokens, chunk), BF16),
        ],
        in_specs=[IN_VMEM, IN_VMEM, IN_HBM, IN_HBM],
        out_specs=[IN_HBM, IN_VMEM],
        scratch_shapes=[
            pltpu.VMEM((tokens, width), BF16),
            pltpu.VMEM((width, wide), BF16),
            pltpu.VMEM((head, width), BF16),
            pltpu.SemaphoreType.DMA((3 * len(cuts),)),
        ],
        compiler_params=params(),
        name="widen",
    )(sent, gain, in_hbm(w_layer), in_hbm(out_layer))


def settle(total, mixes, stacks, places, x, cotangent, back, own):
    tokens, width = x.shape
    chunk = own.shape[2]
    layers, count = stacks[0].shape[1:3]
    entries = [(i, e) for i, stack in enumerate(stacks) for e in range(stack.shape[0])]
    plane = len(entries)
    head = plane * count
    lanes = head
    cuts = steps(width)
    copies = plane * layers + 4 * len(cuts)

    def kernel(p_ref, t_ref, a_ref, b_ref, x_ref, c_ref, back_ref, *refs):
        stack_refs = refs[: len(stacks)]
        f_ref, out_ref, dg_ref = refs[len(stacks) : len(stacks) + 3]
        lower, x_in, c_in, back_in, out_in, sems = refs[len(stacks) + 3 :]
        start = mover(sems)
        first = []
        for at, (i, e) in enumerate(entries):
            for r in range(layers):
                first.append(start(stack_refs[i].at[e, r], lower.at[r, p_ref[at]]))
        loads = []
        for cut in cuts:
            mine = [start(x_ref.at[:, cut], x_in.at[:, cut])]
            mine.append(start(c_ref.at[:, cut], c_in.at[:, cut]))
            mine.append(start(back_ref.at[:, cut], back_in.at[:, cut]))
            loads.append(mine)
        for load in first:
            load.wait()
        stores = []
        for cut, mine in zip(cuts, loads):
            for load in mine:
                load.wait()
            below = lower[:, :, :, cut].reshape(layers * head, cut.stop - cut.start)
            here = x_in[:, cut].astype(F32) + dot_nn(a_ref[...], below)
            rest = c_in[:, cut].astype(F32) - t_ref[...] * here
            gain = jnp.sum(back_in[:, cut].astype(F32) * here, axis=0, keepdims=True)
            for at in range(0, cut.stop - cut.start, chunk):
                full = rest[:, at : at + chunk] + b_ref[(cut.start + at) // chunk].astype(F32)
                cols = slice(cut.start + at, cut.start + at + chunk)
                f_ref[:, cols] = full
                out_in[:, cols] = full.astype(BF16)
            for at in range(0, cut.stop - cut.start, lanes):
                row = (cut.start + at) // lanes
                dg_ref[row : row + 1, :] = gain[:, at : at + lanes]
            stores.append(start(out_in.at[:, cut], out_ref.at[:, cut]))
        for store in stores:
            store.wait()

    return pl.pallas_call(
        kernel,
        out_shape=[
            pltpu.VMEM((tokens, width), F32),
            pltpu.HBM((tokens, width), BF16),
            jax.ShapeDtypeStruct((width // lanes, lanes), F32),
        ],
        in_specs=[IN_SMEM, IN_VMEM, IN_VMEM, IN_VMEM] + [IN_HBM] * 3 + [ANYWHERE] * len(stacks),
        out_specs=[IN_VMEM, IN_HBM, IN_VMEM],
        scratch_shapes=[
            pltpu.VMEM((layers, plane, count, width), BF16),
            pltpu.VMEM((tokens, width), BF16),
            pltpu.VMEM((tokens, width), BF16),
            pltpu.VMEM((tokens, width), BF16),
            pltpu.VMEM((tokens, width), BF16),
            pltpu.SemaphoreType.DMA((copies,)),
        ],
        compiler_params=params(),
        name="settle",
    )(
        places,
        total,
        mixes,
        in_vmem(own),
        *[in_hbm(array) for array in (x, cotangent, back)],
        *stacks,
    )


def send_on(index, arrived, own):
    _, tokens, chunk = own.shape

    def kernel(i_ref, r_ref, b_ref, send_ref):
        send_ref[...] = (b_ref[i_ref[0]].astype(F32) + r_ref[...].astype(F32)).astype(BF16)

    return pl.pallas_call(
        kernel,
        out_shape=pltpu.VMEM((tokens, chunk), BF16),
        in_specs=[IN_SMEM, IN_VMEM, IN_VMEM],
        out_specs=IN_VMEM,
        compiler_params=params(SMALL),
        name="send_on",
    )(index, in_vmem(arrived), in_vmem(own))


def put_out(index, arrived, full, out):
    streams = len(arrived)
    tokens, chunk = arrived[0].shape
    block = streams * chunk

    def kernel(i_ref, *refs):
        r_refs = refs[:streams]
        f_ref, _, out_ref, here, sem = refs[streams:]
        base = pl.multiple_of(i_ref[0] * block, block)
        for i in range(streams):
            cols = pl.ds(pl.multiple_of(base + i * chunk, chunk), chunk)
            full = f_ref[:, cols] + r_refs[i][...].astype(F32)
            here[:, i * chunk : (i + 1) * chunk] = full.astype(BF16)
        copy = pltpu.make_async_copy(here, out_ref.at[:, pl.ds(base, block)], sem)
        copy.start()
        copy.wait()

    return pl.pallas_call(
        kernel,
        out_shape=pltpu.HBM(out.shape, BF16),
        in_specs=[IN_SMEM] + [IN_VMEM] * (streams + 1) + [IN_HBM],
        out_specs=IN_HBM,
        scratch_shapes=[pltpu.VMEM((tokens, block), BF16), pltpu.SemaphoreType.DMA(())],
        input_output_aliases={streams + 2: 0},
        compiler_params=params(SMALL),
        name="put_out",
    )(index, *[in_vmem(array) for array in arrived], in_vmem(full), in_hbm(out))


def added(arrays):
    def kernel(*refs):
        total = refs[0][...]
        for ref in refs[1:-1]:
            total = total + ref[...]
        refs[-1][...] = total

    return pl.pallas_call(
        kernel,
        out_shape=pltpu.VMEM(arrays[0].shape, F32),
        in_specs=[IN_VMEM] * len(arrays),
        out_specs=IN_VMEM,
        compiler_params=params(SMALL),
        name="added",
    )(*[in_vmem(array) for array in arrays])


STREAMS = 2
CHUNKS = 4


def shifted(array, by):
    sections = lax.axis_size("section")
    return lax.ppermute(array, "section", [(i, (i + by) % sections) for i in range(sections)])


def raised(array, by):
    sections = lax.axis_size("section")
    return lax.ppermute(array, "section", [(i, i + by) for i in range(sections - by)])


def swapped(array, step):
    groups = lax.axis_size("group")
    devices = lax.axis_size("dp")
    bits = devices.bit_length() - 1
    pairs = []
    for p in range(devices):
        for g in range(groups):
            pairs.append((p * groups + g, (p ^ (1 << ((step + g) % bits))) * groups + g))
    return lax.ppermute(array, ("dp", "group"), pairs)


def handed(array, by):
    groups = lax.axis_size("group")
    return lax.ppermute(array, "group", [(i, (i + by) % groups) for i in range(groups)])


def spread(array, before_last=(), before_groups=()):
    bits = lax.axis_size("dp").bit_length() - 1
    stacks = [array[None]]
    for step in range(bits):
        together = stacks[0] if step == 0 else jnp.concatenate([together, stacks[-1]], axis=0)
        if step == bits - 1:
            together = tied(together, *before_last)
        stacks.append(swapped(together, step))
    stacks = stacks[-1:] if bits == 0 else [together, stacks[-1]]
    own = [tied(stack, *before_groups) for stack in stacks]
    for r in range(1, lax.axis_size("group")):
        stacks = stacks + [handed(stack, r) for stack in own]
    return stacks


def plane_places():
    groups = lax.axis_size("group")
    bits = lax.axis_size("dp").bit_length() - 1
    masks = []
    for g in range(groups):
        order = [0]
        for step in range(bits):
            order = order + [m ^ (1 << ((step + g) % bits)) for m in order]
        masks.append(order)
    masks = jnp.asarray(masks, jnp.int32)
    dp, member = lax.axis_index("dp"), lax.axis_index("group")
    places = []
    for r in range(groups):
        giver = (member + groups - r) % groups
        places.append((dp ^ masks[giver]) * groups + giver)
    return jnp.concatenate(places).astype(jnp.int32)


def local(tokens_in, cotangent, gains, w_qkv, w_out, segments, plan):
    sections = lax.axis_size("section")
    groups = lax.axis_size("group")
    devices = lax.axis_size("dp")
    plane = devices * groups
    section = lax.axis_index("section")
    member = lax.axis_index("group")
    rows_dev = plan.shape[1]
    length = segments.shape[1]
    tokens, width = tokens_in.shape
    head = w_out.shape[1]
    share = rows_dev // groups
    w_layer, out_layer = w_qkv[0], w_out[0]
    place = member.astype(jnp.int32)[None]
    layer = section.astype(jnp.int32)[None]

    slice_rows = head // plane
    mine = lax.axis_index("dp") * groups + member
    own_rows, *parts = pick(
        tokens_in.reshape(rows_dev, length, width),
        plan,
        place,
        groups,
        out_layer,
        mine.astype(jnp.int32)[None],
        slice_rows,
    )
    slices = [own_rows] + [raised(own_rows, r) for r in range(1, sections)]
    chosen = jnp.take(segments, plan[0], axis=0, mode="clip").astype(BF16)
    chosen = chosen.reshape(groups, share, length)
    moved, moved_seg = [], []
    for r in range(groups):
        outgoing = lax.dynamic_index_in_dim(chosen, (member + r) % groups, 0, keepdims=False)
        moved.append(handed(parts[r], r) if r else parts[r])
        moved_seg.append(handed(outgoing, r) if r else outgoing)
    moved = [part.reshape(share * length, width) for part in moved]
    order = (member - jnp.arange(groups)) % groups
    seg = jnp.take(jnp.stack(moved_seg), order, axis=0, mode="clip").reshape(tokens)
    at = jnp.arange(tokens)
    mask = (
        (at[:, None] >= at[None, :])
        & (at[:, None] // length == at[None, :] // length)
        & (seg[:, None] == seg[None, :])
    ).astype(F32)

    x, xz, norms = project(moved, cotangent, gains, w_layer, out_layer, place)

    last = (section == sections - 1).astype(jnp.int32)[None]
    places = plane_places()
    xz_all = [xz] + [shifted(xz, r) for r in range(1, sections)]
    slices[0] = tied(slices[0], mask, places, *xz_all[:2])
    coupling, stack = couple(slices, gains, w_layer, out_layer, last)
    others = [shifted(coupling, r) for r in range(1, sections)]
    coupling = compact([tied(coupling, *xz_all)] + others, layer, 3 * head, head)
    pieces = spread(coupling)
    sent, total, mixes = serial(xz_all, pieces, places, norms, mask, layer, width, head)

    stacks = spread(stack, pieces, [sent])

    chunk = width // (STREAMS * CHUNKS)
    back, own = widen(sent, gains, w_layer, out_layer, chunk)
    full, out, gain = settle(total, mixes, stacks, places, x, cotangent, back, own)
    def crossed(array, by):
        return lax.ppermute(array, "dp", [(p, p ^ by) for p in range(devices)])

    gain_chip = added([gain] + [crossed(gain, by) for by in range(1, devices)])
    gain_whole = added([gain_chip] + [handed(gain_chip, r) for r in range(1, groups)])
    gain_whole = gain_whole.reshape(1, width)

    down = [(i, i - 1) for i in range(1, sections)]
    behind = sections - 1 - section

    def index(tick):
        return jnp.clip(tick - behind, 0, CHUNKS - 1).astype(jnp.int32)

    leaving = [
        lax.dynamic_index_in_dim(own, index(0) * STREAMS + stream, 0, keepdims=False)
        for stream in range(STREAMS)
    ]
    ticks = CHUNKS + sections - 1
    done = [full]
    for tick in range(1, ticks):
        arrived = []
        chunk_at = tied(index(tick)[None], *done)
        for stream in range(STREAMS):
            arrived.append(lax.ppermute(leaving[stream], "section", down))
            if tick < ticks - 1:
                leaving[stream] = send_on(chunk_at * STREAMS + stream, arrived[stream], own)
        out = put_out(index(tick)[None], arrived, full, out)
        done = [out]
        if tick == ticks - 4:
            done.append(gain_chip)
        if tick == ticks - 3:
            done.append(gain_whole)
    return (out[None], gain_whole)


def attend(hidden, segment, gain_row, w_layer, out_layer):
    count, length, width = hidden.shape
    head = out_layer.shape[0]
    scaled = hidden * lax.rsqrt(jnp.mean(hidden * hidden, axis=-1, keepdims=True) + EPS) * gain_row
    normed = scaled.astype(BF16).reshape(count * length, width)
    projected = jnp.dot(normed, w_layer, preferred_element_type=F32).reshape(count, length, 3 * head)
    query = projected[:, :, :head]
    keyed = projected[:, :, head : 2 * head]
    valued = projected[:, :, 2 * head :]
    positions = jnp.arange(length)
    allowed = (positions[:, None] >= positions[None, :])[None] & (
        segment[:, :, None] == segment[:, None, :]
    )
    scores = jnp.einsum("rid,rjd->rij", query, keyed, precision=lax.Precision.HIGHEST)
    scores = jnp.where(allowed, scores / math.sqrt(head), -1e30)
    weights = jax.nn.softmax(scores, axis=-1)
    mixed = jnp.einsum("rij,rjd->rid", weights, valued, precision=lax.Precision.HIGHEST)
    mixed = mixed.astype(BF16).reshape(count * length, head)
    output = jnp.dot(mixed, out_layer, preferred_element_type=F32).reshape(count, length, width)
    return hidden + output


MB_ROWS = 2


def relay(tokens_in, cotangent, gains, w_qkv, w_out, segments, plan):
    sections = lax.axis_size("section")
    section = lax.axis_index("section")
    rows_dev = plan.shape[1]
    width = tokens_in.shape[1]
    length = segments.shape[1]
    micro = rows_dev // MB_ROWS
    blocks = tokens_in.reshape(rows_dev, length, width)
    chosen = jnp.take(blocks, plan[0], axis=0)
    chosen_seg = jnp.take(segments, plan[0], axis=0).astype(BF16)
    assigned = lax.all_to_all(chosen, "group", split_axis=0, concat_axis=0, tiled=True)
    moved_seg = lax.all_to_all(chosen_seg, "group", split_axis=0, concat_axis=0, tiled=True)
    assigned = assigned.reshape(micro, MB_ROWS, length, width)
    seg_groups = moved_seg.reshape(micro, MB_ROWS, length)
    gain_row, w_layer, out_layer = gains[0], w_qkv[0], w_out[0]
    grad_rows = cotangent.reshape(micro, MB_ROWS, length, width)
    ticks = micro + sections - 1

    def passed_along(array, by):
        pairs = [(i, i + by) for i in range(sections) if 0 <= i + by < sections]
        return lax.ppermute(array, "section", pairs)

    def at(array, i):
        return lax.dynamic_index_in_dim(array, i, 0, keepdims=False)

    def forward_tick(tick, carry):
        saved, arrived = carry
        index = tick - section
        valid = (index >= 0) & (index < micro)
        clipped = jnp.clip(index, 0, micro - 1)
        entering = jnp.where(section == 0, at(assigned, clipped), arrived)
        kept = jnp.where(valid, entering, at(saved, clipped))
        saved = lax.dynamic_update_index_in_dim(saved, kept, clipped, 0)
        segment = at(seg_groups, clipped)

        def run_layer(value):
            return attend(value.astype(F32), segment, gain_row, w_layer, out_layer).astype(BF16)

        leaving = lax.cond(valid, run_layer, jnp.zeros_like, entering)
        return (saved, passed_along(leaving, 1))

    saved_init = jnp.zeros((micro, MB_ROWS, length, width), BF16)
    arrive_init = jnp.zeros((MB_ROWS, length, width), BF16)
    saved, _ = lax.fori_loop(0, ticks, forward_tick, (saved_init, arrive_init))

    def backward_tick(tick, carry):
        grads_x, gain_total, arrived = carry
        index = tick - (sections - 1 - section)
        valid = (index >= 0) & (index < micro)
        clipped = jnp.clip(index, 0, micro - 1)
        entering = jnp.where(section == sections - 1, at(grad_rows, clipped), arrived)
        segment = at(seg_groups, clipped)
        stored = at(saved, clipped).astype(F32)

        def local_layer(hidden, gains_here):
            return attend(hidden, segment, gains_here, w_layer, out_layer)

        def run_back(value):
            _, pullback = jax.vjp(local_layer, stored, gain_row)
            grad_hidden, grad_gain = pullback(value.astype(F32))
            return (grad_hidden.astype(BF16), grad_gain)

        def skip_back(value):
            return (jnp.zeros_like(value), jnp.zeros(gain_row.shape, F32))

        sending, grad_gain = lax.cond(valid, run_back, skip_back, entering)
        kept = jnp.where(valid, sending, at(grads_x, clipped))
        grads_x = lax.dynamic_update_index_in_dim(grads_x, kept, clipped, 0)
        return (grads_x, gain_total + grad_gain, passed_along(sending, -1))

    gain_init = jnp.zeros(gain_row.shape, F32)
    grads_x, gain_total, _ = lax.fori_loop(
        0, ticks, backward_tick, (saved_init, gain_init, arrive_init)
    )
    gain_whole = lax.psum(gain_total, ("dp", "group"))
    return (grads_x.reshape(1, rows_dev * length, width), gain_whole[None])


def solution(mesh):
    placed = (
        P(("dp", "group"), None),
        P(("dp", "group"), None),
        P("section", None),
        P("section", None, None),
        P("section", None, None),
        P(("dp", "group"), None),
        P(("dp", "group"), None),
    )

    def chosen(tokens_in, cotangent, gains, w_qkv, w_out, segments, plan):
        sections, head, width = w_out.shape
        devices = mesh.shape["dp"]
        small = sections * 4 * head < width and devices & (devices - 1) == 0
        body = local if small and sections > 1 else relay
        return jax.shard_map(
            body,
            mesh=mesh,
            in_specs=placed,
            out_specs=(P("section", ("dp", "group"), None), P("section", None)),
            check_vma=False,
        )(tokens_in, cotangent, gains, w_qkv, w_out, segments, plan)

    return chosen
```

```python
import math

import jax
import jax.numpy as jnp
from jax import lax
from jax.experimental import pallas as pl
from jax.experimental.pallas import tpu as pltpu
from jax.sharding import PartitionSpec as P

EPS = 1e-05
VMEM_BYTES = 24 * 1024 * 1024
SMALL = 16 * 1024 * 1024
F32 = jnp.float32
BF16 = jnp.bfloat16


def dot_nn(a, b):
    return lax.dot_general(a, b, (((1,), (0,)), ((), ())), preferred_element_type=F32)


def dot_nt(a, b):
    return lax.dot_general(a, b, (((1,), (1,)), ((), ())), preferred_element_type=F32)


def dot_tn(a, b):
    return lax.dot_general(a, b, (((0,), (0,)), ((), ())), preferred_element_type=F32)


def tied(array, *others):
    return lax.optimization_barrier((array,) + others)[0]


IN_HBM = pl.BlockSpec(memory_space=pltpu.HBM)
ANYWHERE = pl.BlockSpec(memory_space=pl.ANY)
IN_VMEM = pl.BlockSpec(memory_space=pltpu.VMEM)
IN_SMEM = pl.BlockSpec(memory_space=pltpu.SMEM)


def in_hbm(array):
    return pltpu.with_memory_space_constraint(array, pltpu.HBM)


def in_vmem(array):
    return pltpu.with_memory_space_constraint(array, pltpu.VMEM)


MARK = jax.ShapeDtypeStruct((8, 128), F32)


def mover(sems):
    used = []

    def start(source, target):
        copy = pltpu.make_async_copy(source, target, sems.at[len(used)])
        copy.start()
        used.append(copy)
        return copy

    return start


def steps(width):
    step = min(width, 1024)
    return [slice(at, at + step) for at in range(0, width, step)]


def params(limit=VMEM_BYTES):
    return pltpu.CompilerParams(vmem_limit_bytes=limit)


def pick(tokens, plan, place, groups, out_layer, mine, slice_rows):
    rows, length, width = tokens.shape
    share = rows // groups

    def kernel(plan_ref, place_ref, mine_ref, tokens_ref, o_ref, *rest):
        slice_ref, parts = rest[0], rest[1 : 1 + groups]
        slice_in, rows_in, sems = rest[1 + groups :]
        start = mover(sems)
        at = pl.ds(pl.multiple_of(mine_ref[0] * slice_rows, slice_rows), slice_rows)
        loads = [(start(o_ref.at[at], slice_in), slice_in, slice_ref)]
        for r in range(groups):
            target = lax.rem(place_ref[0] + r, groups)
            for c in range(share):
                here = rows_in.at[r * share + c]
                row = plan_ref[0, target * share + c]
                loads.append((start(tokens_ref.at[row], here), here, parts[r].at[c]))
        stores = []
        for load, here, there in loads:
            load.wait()
            stores.append(start(here, there))
        for store in stores:
            store.wait()

    return pl.pallas_call(
        kernel,
        out_shape=[pltpu.HBM((slice_rows, width), BF16)]
        + [pltpu.HBM((share, length, width), BF16)] * groups,
        in_specs=[IN_SMEM, IN_SMEM, IN_SMEM, IN_HBM, IN_HBM],
        out_specs=[IN_HBM] * (1 + groups),
        scratch_shapes=[
            pltpu.VMEM((slice_rows, width), BF16),
            pltpu.VMEM((rows, length, width), BF16),
            pltpu.SemaphoreType.DMA((2 * rows + 2,)),
        ],
        compiler_params=params(),
        name="pick",
    )(plan, place, mine, in_hbm(tokens), in_hbm(out_layer))


def project(parts, cotangent, gain, w_layer, out_layer, place):
    groups = len(parts)
    tokens, width = cotangent.shape
    head = out_layer.shape[0]
    wide = w_layer.shape[1]
    block = tokens // groups
    cuts = steps(width)
    copies = len(cuts) * (groups + 4)

    def kernel(place_ref, *refs):
        part_refs = refs[:groups]
        cot_ref, g_ref, w_ref, o_ref, x_ref, xz_ref, n_ref = refs[groups : groups + 7]
        x_in, c_in, w_in, o_in, sems = refs[groups + 7 :]
        start = mover(sems)
        loads = []
        for cut in cuts:
            mine = [start(w_ref.at[cut], w_in.at[cut])]
            mine.append(start(o_ref.at[:, cut], o_in.at[:, cut]))
            for r in range(groups):
                source = lax.rem(place_ref[0] + groups - r, groups)
                rows = pl.ds(pl.multiple_of(source * block, block), block)
                mine.append(start(part_refs[r].at[:, cut], x_in.at[rows, cut]))
            mine.append(start(cot_ref.at[:, cut], c_in.at[:, cut]))
            loads.append(mine)
        through = jnp.zeros((tokens, wide), F32)
        across = jnp.zeros((tokens, head), F32)
        back = jnp.zeros((tokens, head), F32)
        square = jnp.zeros((tokens, 1), F32)
        stores = []
        for cut, mine in zip(cuts, loads):
            for load in mine:
                load.wait()
            stores.append(start(x_in.at[:, cut], x_ref.at[:, cut]))
            x = x_in[:, cut]
            xf = x.astype(F32)
            through += dot_nn((xf * g_ref[:, cut]).astype(BF16), w_in[cut, :])
            across += dot_nt(x, o_in[:, cut])
            back += dot_nt(c_in[:, cut], o_in[:, cut])
            square += jnp.sum(xf * xf, axis=1, keepdims=True)
        xz_ref[:, :wide] = through.astype(BF16)
        xz_ref[:, wide : wide + head] = across.astype(BF16)
        xz_ref[:, wide + head :] = back.astype(BF16)
        n_ref[...] = square
        for store in stores:
            store.wait()

    return pl.pallas_call(
        kernel,
        out_shape=[
            pltpu.HBM((tokens, width), BF16),
            jax.ShapeDtypeStruct((tokens, wide + 2 * head), BF16),
            jax.ShapeDtypeStruct((tokens, 1), F32),
        ],
        in_specs=[IN_SMEM] + [ANYWHERE] * groups + [IN_HBM, IN_VMEM, IN_HBM, IN_HBM],
        out_specs=[IN_HBM, IN_VMEM, IN_VMEM],
        scratch_shapes=[
            pltpu.VMEM((tokens, width), BF16),
            pltpu.VMEM((tokens, width), BF16),
            pltpu.VMEM((width, wide), BF16),
            pltpu.VMEM((head, width), BF16),
            pltpu.SemaphoreType.DMA((copies,)),
        ],
        compiler_params=params(),
        name="project",
    )(
        place,
        *parts,
        in_hbm(cotangent),
        gain,
        in_hbm(w_layer),
        in_hbm(out_layer),
    )


def couple(slices, gain, w_layer, out_layer, last):
    sections = len(slices)
    count, width = slices[0].shape
    head = out_layer.shape[0]
    wide = w_layer.shape[1]
    below = (sections - 2) * wide
    packed = below + max(wide, (sections - 1) * head)
    cuts = steps(width)
    copies = len(cuts) * (sections + 2) + sections - 1

    def kernel(last_ref, *refs):
        s_refs = refs[:sections]
        g_ref, w_ref, o_ref, out_ref, stack_ref, r_in, w_in, o_in, sems = refs[sections:]
        rows = [slice(r * count, (r + 1) * count) for r in range(sections)]
        start = mover(sems)
        loads = []
        for cut in cuts:
            mine = [start(w_ref.at[cut], w_in.at[cut])]
            mine.append(start(o_ref.at[:, cut], o_in.at[:, cut]))
            for r in range(sections):
                mine.append(start(s_refs[r].at[:, cut], r_in.at[rows[r], cut]))
            loads.append(mine)
        through = jnp.zeros((sections * count, wide), F32)
        across = jnp.zeros((sections * count, head), F32)
        for cut, mine in zip(cuts, loads):
            for load in mine:
                load.wait()
            r = r_in[:, cut]
            through += dot_nn((r.astype(F32) * g_ref[:, cut]).astype(BF16), w_in[cut, :])
            across += dot_nt(r, o_in[:, cut])
        stores = [start(r_in.at[rows[r]], stack_ref.at[r - 1]) for r in range(1, sections)]
        through = through.astype(BF16)
        across = across.astype(BF16)
        out_ref[...] = jnp.zeros_like(out_ref)
        for r in range(1, sections - 1):
            out_ref[:, (r - 1) * wide : r * wide] = through[rows[r]]

        @pl.when(last_ref[0] == 1)
        def _():
            out_ref[:, below : below + wide] = through[rows[-1]]

        @pl.when(last_ref[0] == 0)
        def _():
            for r in range(sections - 1):
                out_ref[:, below + r * head : below + (r + 1) * head] = across[rows[r]]

        for store in stores:
            store.wait()

    return pl.pallas_call(
        kernel,
        out_shape=[
            jax.ShapeDtypeStruct((count, packed), BF16),
            pltpu.HBM((sections - 1, count, width), BF16),
        ],
        in_specs=[IN_SMEM] + [ANYWHERE] * sections + [IN_VMEM, IN_HBM, IN_HBM],
        out_specs=[IN_VMEM, IN_HBM],
        scratch_shapes=[
            pltpu.VMEM((sections * count, width), BF16),
            pltpu.VMEM((width, wide), BF16),
            pltpu.VMEM((head, width), BF16),
            pltpu.SemaphoreType.DMA((copies,)),
        ],
        compiler_params=params(),
        name="couple",
    )(last, *slices, gain, in_hbm(w_layer), in_hbm(out_layer))


def layout(sections, wide, head):
    through, across, at = {}, {}, 0
    for k in range(sections):
        for j in range(k):
            through[j, k] = slice(at, at + wide)
            at += wide
        for j in range(k + 1 if k < sections - 1 else 0):
            across[j, k] = slice(at, at + head)
            at += head
    return through, across, at


def compact(parts, section, wide, head):
    sections = len(parts)
    count = parts[0].shape[0]
    below = (sections - 2) * wide
    through, across, total = layout(sections, wide, head)

    def kernel(s_ref, *refs):
        part_refs, out_ref = refs[:sections], refs[sections]
        mine = s_ref[0]

        def fill(k, r):
            for j in range(k):
                at = (k - j - 1) * wide
                out_ref[:, through[j, k]] = part_refs[r][:, at : at + wide]
            for j in range(k + 1 if k < sections - 1 else 0):
                at = below + (k - j) * head
                out_ref[:, across[j, k]] = part_refs[r][:, at : at + head]

        for s in range(sections):

            @pl.when(mine == s)
            def _(s=s):
                for r in range(sections):
                    fill((s - r) % sections, r)

    vmem = pl.BlockSpec(memory_space=pltpu.VMEM)
    return pl.pallas_call(
        kernel,
        out_shape=jax.ShapeDtypeStruct((count, total), BF16),
        in_specs=[pl.BlockSpec(memory_space=pltpu.SMEM)] + [vmem] * sections,
        out_specs=vmem,
        compiler_params=params(SMALL),
        name="compact",
    )(section, *parts)


def serial(xz, pieces, places, norms, mask, section, width, head):
    sections = len(xz)
    tokens = norms.shape[0]
    wide = 3 * head
    scale = 1.0 / math.sqrt(head)
    through_at, across_at, _ = layout(sections, wide, head)
    count, packed = pieces[0].shape[-2:]
    plane = head // count
    n_in = sections + len(pieces)
    copies = sections + plane

    def kernel(s_ref, p_ref, *refs):
        xz_refs, piece_refs = refs[:sections], refs[sections:n_in]
        n_ref, mask_ref, v_ref, t_ref, a_ref, mark_ref = refs[n_in : n_in + 6]
        xz_all, table, mixes, weights, projs, dmix, sems = refs[n_in + 6 :]
        mark_ref[...] = jnp.zeros_like(mark_ref)
        mine = s_ref[0]
        started = []

        def start(source, target):
            copy = pltpu.make_async_copy(source, target, sems.at[len(started)])
            copy.start()
            started.append(copy)

        for r in range(sections):
            start(xz_refs[r], xz_all.at[lax.rem(mine + sections - r, sections)])
        at = 0
        for ref in piece_refs:
            for i in range(ref.shape[0]):
                start(ref.at[i], table.at[p_ref[at]])
                at += 1
        for copy in started:
            copy.wait()

        def through(j, k):
            return table[:, :, through_at[j, k]].reshape(head, wide)

        def across(j, k):
            return table[:, :, across_at[j, k]].reshape(head, head)

        allowed = mask_ref[...] > 0.5
        norm = n_ref[...]
        rstds, tails, mixed = [], [], []
        for s in range(sections):
            proj = xz_all[s, :, :wide].astype(F32)
            for j in range(s):
                proj = proj + dot_nn(mixed[j], through(j, s))
            rstd = lax.rsqrt(norm * (1.0 / width) + EPS)
            proj = proj * rstd
            projs[s] = proj.astype(BF16)
            q, k, v = (projs[s, :, i * head : (i + 1) * head] for i in range(3))
            scores = jnp.where(allowed, dot_nt(q, k) * scale, -1e30)
            scores = jnp.exp(scores - jnp.max(scores, axis=1, keepdims=True))
            soft = scores / jnp.sum(scores, axis=1, keepdims=True)
            weights[s] = soft
            mix = dot_nn(soft.astype(BF16), v).astype(BF16)
            mixed.append(mix)
            mixes[:, s * head : (s + 1) * head] = mix
            rstds.append(rstd)
            dmix[:, s * head : (s + 1) * head] = xz_all[s, :, wide + head :].astype(F32)
            if s == sections - 1:
                break
            y = xz_all[s, :, wide : wide + head].astype(F32)
            for j in range(s):
                y = y + dot_nn(mixed[j], across(j, s))
            tail = y + dot_nn(mix, across(s, s))
            norm = norm + jnp.sum(mix.astype(F32) * (y + tail), axis=1, keepdims=True)
            norm = jnp.maximum(norm, 0.0)
            tails.append(tail)
        total = jnp.zeros((tokens, 1), F32)
        a_ref[...] = jnp.zeros_like(a_ref)
        for s in reversed(range(sections)):
            cols = slice(s * head, (s + 1) * head)
            da = dmix[:, cols]
            if s < sections - 1:
                da = da - total * tails[s]
            da = da.astype(BF16)
            q, k, v = (projs[s, :, i * head : (i + 1) * head] for i in range(3))
            soft = weights[s]
            dv = dot_tn(soft.astype(BF16), da)
            dsoft = dot_nt(da, v)
            dscore = soft * (dsoft - jnp.sum(dsoft * soft, axis=1, keepdims=True))
            dscore = (dscore * scale).astype(BF16)
            dproj = jnp.concatenate([dot_nn(dscore, k), dot_tn(dscore, q), dv], axis=1)
            along = jnp.sum(dproj * projs[s].astype(F32), axis=1, keepdims=True)
            first = (dproj * rstds[s]).astype(BF16)
            second = (-total * mixes[:, cols].astype(F32)).astype(BF16)
            total = total + rstds[s] * rstds[s] * along * (1.0 / width)
            for j in reversed(range(s)):
                term = dot_nt(first, through(j, s))
                if s < sections - 1:
                    term = term + dot_nt(second, across(j, s))
                dmix[:, j * head : (j + 1) * head] += term

            @pl.when(mine == s)
            def _(first=first, second=second, total=total):
                v_ref[:, :wide] = first
                v_ref[:, wide:] = second
                t_ref[...] = total

            for r in range(1, sections - s):

                @pl.when(mine == s + r)
                def _(r=r, cols=cols):
                    a_ref[:, (r - 1) * head : r * head] = mixes[:, cols]

    vmem = pl.BlockSpec(memory_space=pltpu.VMEM)
    smem = pl.BlockSpec(memory_space=pltpu.SMEM)
    return pl.pallas_call(
        kernel,
        out_shape=[
            pltpu.VMEM((tokens, wide + head), BF16),
            pltpu.VMEM((tokens, 1), F32),
            pltpu.VMEM((tokens, (sections - 1) * head), BF16),
            MARK,
        ],
        in_specs=[smem, smem] + [ANYWHERE] * n_in + [vmem, vmem],
        out_specs=[vmem] * 4,
        scratch_shapes=[
            pltpu.VMEM((sections,) + xz[0].shape, BF16),
            pltpu.VMEM((plane, count, packed), BF16),
            pltpu.VMEM((tokens, sections * head), BF16),
            pltpu.VMEM((sections, tokens, tokens), F32),
            pltpu.VMEM((sections, tokens, wide), BF16),
            pltpu.VMEM((tokens, sections * head), F32),
            pltpu.SemaphoreType.DMA((copies,)),
        ],
        compiler_params=params(),
        name="serial",
    )(section, places, *xz, *pieces, norms, mask)


def widen(sent, gain, w_layer, out_layer, streams):
    tokens = sent.shape[0]
    head, width = out_layer.shape
    wide = w_layer.shape[1]
    chunk = streams[-1].stop
    cuts = [slice(at, at + chunk) for at in range(0, width, chunk)]

    def kernel(v_ref, g_ref, w_ref, o_ref, back_ref, b_ref, *refs):
        first_refs = refs[: len(streams)]
        back_in, w_in, o_in, sems = refs[len(streams) :]
        start = mover(sems)
        loads = [
            (start(w_ref.at[cut], w_in.at[cut]), start(o_ref.at[:, cut], o_in.at[:, cut]))
            for cut in cuts
        ]
        stores = []
        for i, (cut, mine) in enumerate(zip(cuts, loads)):
            for load in mine:
                load.wait()
            back = dot_nt(v_ref[:, :wide], w_in[cut, :])
            own = back * g_ref[:, cut] + dot_nn(v_ref[:, wide:], o_in[:, cut])
            own = own.astype(BF16)
            back_in[:, cut] = back.astype(BF16)
            stores.append(start(back_in.at[:, cut], back_ref.at[:, cut]))
            b_ref[i] = own
            if i == 0:
                for ref, cols in zip(first_refs, streams):
                    ref[...] = own[:, cols]
        for store in stores:
            store.wait()

    return pl.pallas_call(
        kernel,
        out_shape=[
            pltpu.HBM((tokens, width), BF16),
            pltpu.VMEM((len(cuts), tokens, chunk), BF16),
        ]
        + [pltpu.VMEM((tokens, cols.stop - cols.start), BF16) for cols in streams],
        in_specs=[IN_VMEM, IN_VMEM, IN_HBM, IN_HBM],
        out_specs=[IN_HBM, IN_VMEM] + [IN_VMEM] * len(streams),
        scratch_shapes=[
            pltpu.VMEM((tokens, width), BF16),
            pltpu.VMEM((width, wide), BF16),
            pltpu.VMEM((head, width), BF16),
            pltpu.SemaphoreType.DMA((3 * len(cuts),)),
        ],
        compiler_params=params(),
        name="widen",
    )(in_vmem(sent), gain, in_hbm(w_layer), in_hbm(out_layer))


def settle(total, mixes, stacks, places, x, cotangent, back, own):
    tokens, width = x.shape
    count, _, chunk = own.shape
    layers, rows = stacks[0].shape[1:3]
    entries = [(i, e) for i, stack in enumerate(stacks) for e in range(stack.shape[0])]
    plane = len(entries)
    head = plane * rows
    cuts = [slice(at, at + chunk) for at in range(0, width, chunk)]
    copies = plane * layers + 3 * len(cuts)

    def kernel(p_ref, t_ref, a_ref, b_ref, x_ref, c_ref, back_ref, *refs):
        stack_refs = refs[: len(stacks)]
        f_ref, out_ref, dg_ref, mark_ref = refs[len(stacks) : len(stacks) + 4]
        lower, x_in, c_in, back_in, sems = refs[len(stacks) + 4 :]
        start = mover(sems)
        first = []
        for at, (i, e) in enumerate(entries):
            for r in range(layers):
                first.append(start(stack_refs[i].at[e, r], lower.at[r, p_ref[at]]))
        loads = []
        for cut in cuts:
            mine = [start(x_ref.at[:, cut], x_in.at[:, cut])]
            mine.append(start(c_ref.at[:, cut], c_in.at[:, cut]))
            mine.append(start(back_ref.at[:, cut], back_in.at[:, cut]))
            loads.append(mine)
        mark_ref[...] = jnp.zeros_like(mark_ref)
        for load in first:
            load.wait()
        for i, (cut, mine) in enumerate(zip(cuts, loads)):
            for load in mine:
                load.wait()
            below = lower[:, :, :, cut].reshape(layers * head, chunk)
            here = x_in[:, cut].astype(F32) + dot_nn(a_ref[...], below)
            full = c_in[:, cut].astype(F32) - t_ref[...] * here + b_ref[i].astype(F32)
            f_ref[i] = full
            out_ref[i] = full.astype(BF16)
            gain = jnp.sum(back_in[:, cut].astype(F32) * here, axis=0, keepdims=True)
            for at in range(0, chunk, head):
                row = (cut.start + at) // head
                dg_ref[row : row + 1, :] = gain[:, at : at + head]

    return pl.pallas_call(
        kernel,
        out_shape=[
            pltpu.VMEM((count, tokens, chunk), F32),
            pltpu.VMEM((count, tokens, chunk), BF16),
            pltpu.VMEM((width // head, head), F32),
            MARK,
        ],
        in_specs=[IN_SMEM, IN_VMEM, IN_VMEM, IN_VMEM] + [IN_HBM] * (3 + len(stacks)),
        out_specs=[IN_VMEM] * 4,
        scratch_shapes=[
            pltpu.VMEM((layers, plane, rows, width), BF16),
            pltpu.VMEM((tokens, width), BF16),
            pltpu.VMEM((tokens, width), BF16),
            pltpu.VMEM((tokens, width), BF16),
            pltpu.SemaphoreType.DMA((copies,)),
        ],
        compiler_params=params(),
        name="settle",
    )(
        places,
        in_vmem(total),
        in_vmem(mixes),
        in_vmem(own),
        *[in_hbm(array) for array in (x, cotangent, back, *stacks)],
    )


def join(index, arrived, own, full, out, cols):
    tokens, part = arrived.shape

    def kernel(i_ref, r_ref, b_ref, f_ref, _, send_ref, out_ref):
        at = i_ref[0]
        r = r_ref[...].astype(F32)
        send_ref[...] = (b_ref[at, :, cols].astype(F32) + r).astype(BF16)
        out_ref[at, :, cols] = (f_ref[at, :, cols] + r).astype(BF16)

    return pl.pallas_call(
        kernel,
        out_shape=[pltpu.VMEM((tokens, part), BF16), pltpu.VMEM(out.shape, BF16)],
        in_specs=[IN_SMEM] + [IN_VMEM] * 4,
        out_specs=[IN_VMEM] * 2,
        input_output_aliases={4: 1},
        compiler_params=params(SMALL),
        name="join",
    )(index, in_vmem(arrived), in_vmem(own), in_vmem(full), in_vmem(out))


def finish(index, arrived, full, out, streams):
    count, tokens, chunk = out.shape

    def kernel(i_ref, *refs):
        r_refs = refs[: len(streams)]
        f_ref, o_ref, whole_ref, last, sems = refs[len(streams) :]
        at = i_ref[0]
        last[...] = o_ref[at]
        for ref, cols in zip(r_refs, streams):
            last[:, cols] = (f_ref[at, :, cols] + ref[...].astype(F32)).astype(BF16)
        for i in range(count):
            there = whole_ref.at[:, pl.ds(i * chunk, chunk)]

            @pl.when(at == i)
            def _(i=i, there=there):
                pltpu.make_async_copy(last, there, sems.at[i]).start()

            @pl.when(at != i)
            def _(i=i, there=there):
                pltpu.make_async_copy(o_ref.at[i], there, sems.at[i]).start()

        for i in range(count):
            there = whole_ref.at[:, pl.ds(i * chunk, chunk)]
            pltpu.make_async_copy(last, there, sems.at[i]).wait()

    return pl.pallas_call(
        kernel,
        out_shape=pltpu.HBM((tokens, count * chunk), BF16),
        in_specs=[IN_SMEM] + [IN_VMEM] * (len(streams) + 2),
        out_specs=IN_HBM,
        scratch_shapes=[
            pltpu.VMEM((tokens, chunk), BF16),
            pltpu.SemaphoreType.DMA((count,)),
        ],
        compiler_params=params(SMALL),
        name="finish",
    )(index, *[in_vmem(array) for array in arrived], in_vmem(full), in_vmem(out))


def added(arrays):
    def kernel(*refs):
        total = refs[0][...]
        for ref in refs[1:-1]:
            total = total + ref[...]
        refs[-1][...] = total

    return pl.pallas_call(
        kernel,
        out_shape=pltpu.VMEM(arrays[0].shape, F32),
        in_specs=[IN_VMEM] * len(arrays),
        out_specs=IN_VMEM,
        compiler_params=params(SMALL),
        name="added",
    )(*[in_vmem(array) for array in arrays])


STREAMS = 2
CHUNKS = 4


def stream_columns(chunk):
    lanes = 128
    tiles = chunk // lanes
    ends = [-(-tiles * (i + 1) // STREAMS) * lanes for i in range(STREAMS)]
    return [slice(start, end) for start, end in zip([0] + ends, ends)]


def shifted(array, by):
    sections = lax.axis_size("section")
    return lax.ppermute(array, "section", [(i, (i + by) % sections) for i in range(sections)])


def raised(array, by):
    sections = lax.axis_size("section")
    return lax.ppermute(array, "section", [(i, i + by) for i in range(sections - by)])


def swapped(array, step):
    groups = lax.axis_size("group")
    devices = lax.axis_size("dp")
    bits = devices.bit_length() - 1
    pairs = []
    for p in range(devices):
        for g in range(groups):
            pairs.append((p * groups + g, (p ^ (1 << ((step + g) % bits))) * groups + g))
    return lax.ppermute(array, ("dp", "group"), pairs)


def handed(array, by):
    groups = lax.axis_size("group")
    return lax.ppermute(array, "group", [(i, (i + by) % groups) for i in range(groups)])


def spread(array, before_last=(), before_groups=()):
    bits = lax.axis_size("dp").bit_length() - 1
    stacks = [array[None]]
    for step in range(bits):
        together = stacks[0] if step == 0 else jnp.concatenate([together, stacks[-1]], axis=0)
        if step == bits - 1:
            together = tied(together, *before_last)
        stacks.append(swapped(together, step))
    stacks = stacks[-1:] if bits == 0 else [together, stacks[-1]]
    own = [tied(stack, *before_groups) for stack in stacks]
    for r in range(1, lax.axis_size("group")):
        stacks = stacks + [handed(stack, r) for stack in own]
    return stacks


def plane_places():
    groups = lax.axis_size("group")
    bits = lax.axis_size("dp").bit_length() - 1
    masks = []
    for g in range(groups):
        order = [0]
        for step in range(bits):
            order = order + [m ^ (1 << ((step + g) % bits)) for m in order]
        masks.append(order)
    masks = jnp.asarray(masks, jnp.int32)
    dp, member = lax.axis_index("dp"), lax.axis_index("group")
    places = []
    for r in range(groups):
        giver = (member + groups - r) % groups
        places.append((dp ^ masks[giver]) * groups + giver)
    return jnp.concatenate(places).astype(jnp.int32)


def local(tokens_in, cotangent, gains, w_qkv, w_out, segments, plan):
    sections = lax.axis_size("section")
    groups = lax.axis_size("group")
    devices = lax.axis_size("dp")
    plane = devices * groups
    section = lax.axis_index("section")
    member = lax.axis_index("group")
    rows_dev = plan.shape[1]
    length = segments.shape[1]
    tokens, width = tokens_in.shape
    head = w_out.shape[1]
    share = rows_dev // groups
    w_layer, out_layer = w_qkv[0], w_out[0]
    place = member.astype(jnp.int32)[None]
    layer = section.astype(jnp.int32)[None]

    slice_rows = head // plane
    mine = lax.axis_index("dp") * groups + member
    own_rows, *parts = pick(
        tokens_in.reshape(rows_dev, length, width),
        plan,
        place,
        groups,
        out_layer,
        mine.astype(jnp.int32)[None],
        slice_rows,
    )
    slices = [own_rows] + [raised(own_rows, r) for r in range(1, sections)]
    chosen = jnp.take(segments, plan[0], axis=0, mode="clip").astype(BF16)
    chosen = chosen.reshape(groups, share, length)
    moved, moved_seg = [], []
    for r in range(groups):
        outgoing = lax.dynamic_index_in_dim(chosen, (member + r) % groups, 0, keepdims=False)
        moved.append(handed(parts[r], r) if r else parts[r])
        moved_seg.append(handed(outgoing, r) if r else outgoing)
    moved = [part.reshape(share * length, width) for part in moved]
    order = (member - jnp.arange(groups)) % groups
    seg = jnp.take(jnp.stack(moved_seg), order, axis=0, mode="clip").reshape(tokens)
    at = jnp.arange(tokens)
    mask = (
        (at[:, None] >= at[None, :])
        & (at[:, None] // length == at[None, :] // length)
        & (seg[:, None] == seg[None, :])
    ).astype(F32)

    x, xz, norms = project(moved, cotangent, gains, w_layer, out_layer, place)

    last = (section == sections - 1).astype(jnp.int32)[None]
    places = plane_places()
    xz_all = [xz] + [shifted(xz, r) for r in range(1, sections)]
    slices[0] = tied(slices[0], mask, places, *xz_all[:2])
    coupling, stack = couple(slices, gains, w_layer, out_layer, last)
    others = [shifted(coupling, r) for r in range(1, sections)]
    coupling = compact([tied(coupling, *xz_all)] + others, layer, 3 * head, head)
    pieces = spread(coupling)
    sent, total, mixes, served = serial(xz_all, pieces, places, norms, mask, layer, width, head)

    stacks = spread(stack, pieces, [served])

    streams = stream_columns(width // CHUNKS)
    back, own, *leaving = widen(sent, gains, w_layer, out_layer, streams)
    full, out, gain, settled = settle(total, mixes, stacks, places, x, cotangent, back, own)

    def crossed(array, by):
        return lax.ppermute(array, "dp", [(p, p ^ by) for p in range(devices)])

    gain_chip = added([gain] + [crossed(gain, by) for by in range(1, devices)])
    gain_whole = added([gain_chip] + [handed(gain_chip, r) for r in range(1, groups)])
    gain_whole = gain_whole.reshape(1, width)

    down = [(i, i - 1) for i in range(1, sections)]
    behind = sections - 1 - section

    def index(tick):
        return jnp.clip(tick - behind, 0, CHUNKS - 1).astype(jnp.int32)

    ticks = CHUNKS + sections - 1
    done = [settled]
    for tick in range(1, ticks):
        chunk_at = tied(index(tick)[None], *done)
        done = []
        arrived = [lax.ppermute(array, "section", down) for array in leaving]
        if tick < ticks - 1:
            for i, cols in enumerate(streams):
                leaving[i], out = join(chunk_at, arrived[i], own, full, out, cols)
        if tick == ticks - 4:
            done = [gain_chip]
        if tick == ticks - 3:
            done = [gain_whole]
    out = finish(chunk_at, arrived, full, out, streams)
    return (out[None], gain_whole)


def attend(hidden, segment, gain_row, w_layer, out_layer):
    count, length, width = hidden.shape
    head = out_layer.shape[0]
    scaled = hidden * lax.rsqrt(jnp.mean(hidden * hidden, axis=-1, keepdims=True) + EPS) * gain_row
    normed = scaled.astype(BF16).reshape(count * length, width)
    projected = jnp.dot(normed, w_layer, preferred_element_type=F32).reshape(count, length, 3 * head)
    query = projected[:, :, :head]
    keyed = projected[:, :, head : 2 * head]
    valued = projected[:, :, 2 * head :]
    positions = jnp.arange(length)
    allowed = (positions[:, None] >= positions[None, :])[None] & (
        segment[:, :, None] == segment[:, None, :]
    )
    scores = jnp.einsum("rid,rjd->rij", query, keyed, precision=lax.Precision.HIGHEST)
    scores = jnp.where(allowed, scores / math.sqrt(head), -1e30)
    weights = jax.nn.softmax(scores, axis=-1)
    mixed = jnp.einsum("rij,rjd->rid", weights, valued, precision=lax.Precision.HIGHEST)
    mixed = mixed.astype(BF16).reshape(count * length, head)
    output = jnp.dot(mixed, out_layer, preferred_element_type=F32).reshape(count, length, width)
    return hidden + output


MB_ROWS = 2


def relay(tokens_in, cotangent, gains, w_qkv, w_out, segments, plan):
    sections = lax.axis_size("section")
    section = lax.axis_index("section")
    rows_dev = plan.shape[1]
    width = tokens_in.shape[1]
    length = segments.shape[1]
    micro = rows_dev // MB_ROWS
    blocks = tokens_in.reshape(rows_dev, length, width)
    chosen = jnp.take(blocks, plan[0], axis=0)
    chosen_seg = jnp.take(segments, plan[0], axis=0).astype(BF16)
    assigned = lax.all_to_all(chosen, "group", split_axis=0, concat_axis=0, tiled=True)
    moved_seg = lax.all_to_all(chosen_seg, "group", split_axis=0, concat_axis=0, tiled=True)
    assigned = assigned.reshape(micro, MB_ROWS, length, width)
    seg_groups = moved_seg.reshape(micro, MB_ROWS, length)
    gain_row, w_layer, out_layer = gains[0], w_qkv[0], w_out[0]
    grad_rows = cotangent.reshape(micro, MB_ROWS, length, width)
    ticks = micro + sections - 1

    def passed_along(array, by):
        pairs = [(i, i + by) for i in range(sections) if 0 <= i + by < sections]
        return lax.ppermute(array, "section", pairs)

    def at(array, i):
        return lax.dynamic_index_in_dim(array, i, 0, keepdims=False)

    def forward_tick(tick, carry):
        saved, arrived = carry
        index = tick - section
        valid = (index >= 0) & (index < micro)
        clipped = jnp.clip(index, 0, micro - 1)
        entering = jnp.where(section == 0, at(assigned, clipped), arrived)
        kept = jnp.where(valid, entering, at(saved, clipped))
        saved = lax.dynamic_update_index_in_dim(saved, kept, clipped, 0)
        segment = at(seg_groups, clipped)

        def run_layer(value):
            return attend(value.astype(F32), segment, gain_row, w_layer, out_layer).astype(BF16)

        leaving = lax.cond(valid, run_layer, jnp.zeros_like, entering)
        return (saved, passed_along(leaving, 1))

    saved_init = jnp.zeros((micro, MB_ROWS, length, width), BF16)
    arrive_init = jnp.zeros((MB_ROWS, length, width), BF16)
    saved, _ = lax.fori_loop(0, ticks, forward_tick, (saved_init, arrive_init))

    def backward_tick(tick, carry):
        grads_x, gain_total, arrived = carry
        index = tick - (sections - 1 - section)
        valid = (index >= 0) & (index < micro)
        clipped = jnp.clip(index, 0, micro - 1)
        entering = jnp.where(section == sections - 1, at(grad_rows, clipped), arrived)
        segment = at(seg_groups, clipped)
        stored = at(saved, clipped).astype(F32)

        def local_layer(hidden, gains_here):
            return attend(hidden, segment, gains_here, w_layer, out_layer)

        def run_back(value):
            _, pullback = jax.vjp(local_layer, stored, gain_row)
            grad_hidden, grad_gain = pullback(value.astype(F32))
            return (grad_hidden.astype(BF16), grad_gain)

        def skip_back(value):
            return (jnp.zeros_like(value), jnp.zeros(gain_row.shape, F32))

        sending, grad_gain = lax.cond(valid, run_back, skip_back, entering)
        kept = jnp.where(valid, sending, at(grads_x, clipped))
        grads_x = lax.dynamic_update_index_in_dim(grads_x, kept, clipped, 0)
        return (grads_x, gain_total + grad_gain, passed_along(sending, -1))

    gain_init = jnp.zeros(gain_row.shape, F32)
    grads_x, gain_total, _ = lax.fori_loop(
        0, ticks, backward_tick, (saved_init, gain_init, arrive_init)
    )
    gain_whole = lax.psum(gain_total, ("dp", "group"))
    return (grads_x.reshape(1, rows_dev * length, width), gain_whole[None])


def solution(mesh):
    placed = (
        P(("dp", "group"), None),
        P(("dp", "group"), None),
        P("section", None),
        P("section", None, None),
        P("section", None, None),
        P(("dp", "group"), None),
        P(("dp", "group"), None),
    )

    def chosen(tokens_in, cotangent, gains, w_qkv, w_out, segments, plan):
        sections, head, width = w_out.shape
        devices = mesh.shape["dp"]
        small = sections * 4 * head < width and devices & (devices - 1) == 0
        body = local if small and sections > 1 else relay
        return jax.shard_map(
            body,
            mesh=mesh,
            in_specs=placed,
            out_specs=(P("section", ("dp", "group"), None), P("section", None)),
            check_vma=False,
        )(tokens_in, cotangent, gains, w_qkv, w_out, segments, plan)

    return chosen
```

```python
import math

import jax
import jax.numpy as jnp
from jax import lax
from jax.experimental import pallas as pl
from jax.experimental.pallas import tpu as pltpu
from jax.sharding import PartitionSpec as P

EPS = 1e-05
VMEM_BYTES = 48 * 1024 * 1024
F32 = jnp.float32
BF16 = jnp.bfloat16


def dot_nn(a, b):
    return lax.dot_general(a, b, (((1,), (0,)), ((), ())), preferred_element_type=F32)


def dot_nt(a, b):
    return lax.dot_general(a, b, (((1,), (1,)), ((), ())), preferred_element_type=F32)


def dot_tn(a, b):
    return lax.dot_general(a, b, (((0,), (0,)), ((), ())), preferred_element_type=F32)


IN_HBM = pl.BlockSpec(memory_space=pltpu.HBM)
ANYWHERE = pl.BlockSpec(memory_space=pl.ANY)
IN_VMEM = pl.BlockSpec(memory_space=pltpu.VMEM)
IN_SMEM = pl.BlockSpec(memory_space=pltpu.SMEM)


def in_hbm(array):
    return pltpu.with_memory_space_constraint(array, pltpu.HBM)


def in_vmem(array):
    return pltpu.with_memory_space_constraint(array, pltpu.VMEM)


def mover(sems):
    used = []

    def start(source, target):
        copy = pltpu.make_async_copy(source, target, sems.at[len(used)])
        copy.start()
        used.append(copy)
        return copy

    return start


def steps(width):
    step = min(width, 1024)
    return [slice(at, at + step) for at in range(0, width, step)]


def params(limit=VMEM_BYTES):
    return pltpu.CompilerParams(vmem_limit_bytes=limit)


def pick(tokens, plan, place, groups, out_layer, mine, slice_rows):
    rows, length, width = tokens.shape
    share = rows // groups

    def kernel(plan_ref, place_ref, mine_ref, tokens_ref, o_ref, *rest):
        slice_ref, parts = rest[0], rest[1 : 1 + groups]
        slice_in, rows_in, sems = rest[1 + groups :]
        start = mover(sems)
        at = pl.ds(pl.multiple_of(mine_ref[0] * slice_rows, slice_rows), slice_rows)
        loads = [(start(o_ref.at[at], slice_in), slice_in, slice_ref)]
        for r in range(groups):
            target = lax.rem(place_ref[0] + r, groups)
            for c in range(share):
                here = rows_in.at[r * share + c]
                row = plan_ref[0, target * share + c]
                loads.append((start(tokens_ref.at[row], here), here, parts[r].at[c]))
        stores = []
        for load, here, there in loads:
            load.wait()
            stores.append(start(here, there))
        for store in stores:
            store.wait()

    return pl.pallas_call(
        kernel,
        out_shape=[pltpu.HBM((slice_rows, width), BF16)]
        + [pltpu.HBM((share, length, width), BF16)] * groups,
        in_specs=[IN_SMEM, IN_SMEM, IN_SMEM, IN_HBM, IN_HBM],
        out_specs=[IN_HBM] * (1 + groups),
        scratch_shapes=[
            pltpu.VMEM((slice_rows, width), BF16),
            pltpu.VMEM((rows, length, width), BF16),
            pltpu.SemaphoreType.DMA((2 * rows + 2,)),
        ],
        compiler_params=params(),
        name="pick",
    )(plan, place, mine, in_hbm(tokens), in_hbm(out_layer))


def project(parts, cotangent, gain, w_layer, out_layer, place):
    groups = len(parts)
    tokens, width = cotangent.shape
    head = out_layer.shape[0]
    wide = w_layer.shape[1]
    block = tokens // groups
    cuts = steps(width)
    copies = len(cuts) * (groups + 4)

    def kernel(place_ref, *refs):
        part_refs = refs[:groups]
        cot_ref, g_ref, w_ref, o_ref, x_ref, xz_ref, n_ref = refs[groups : groups + 7]
        x_in, c_in, w_in, o_in, sems = refs[groups + 7 :]
        start = mover(sems)
        loads = []
        for cut in cuts:
            mine = [start(w_ref.at[cut], w_in.at[cut])]
            mine.append(start(o_ref.at[:, cut], o_in.at[:, cut]))
            for r in range(groups):
                source = lax.rem(place_ref[0] + groups - r, groups)
                rows = pl.ds(pl.multiple_of(source * block, block), block)
                mine.append(start(part_refs[r].at[:, cut], x_in.at[rows, cut]))
            mine.append(start(cot_ref.at[:, cut], c_in.at[:, cut]))
            loads.append(mine)
        through = jnp.zeros((tokens, wide), F32)
        across = jnp.zeros((tokens, head), F32)
        back = jnp.zeros((tokens, head), F32)
        square = jnp.zeros((tokens, 1), F32)
        stores = []
        for cut, mine in zip(cuts, loads):
            for load in mine:
                load.wait()
            stores.append(start(x_in.at[:, cut], x_ref.at[:, cut]))
            x = x_in[:, cut]
            xf = x.astype(F32)
            through += dot_nn((xf * g_ref[:, cut]).astype(BF16), w_in[cut, :])
            across += dot_nt(x, o_in[:, cut])
            back += dot_nt(c_in[:, cut], o_in[:, cut])
            square += jnp.sum(xf * xf, axis=1, keepdims=True)
        xz_ref[:, :wide] = through.astype(BF16)
        xz_ref[:, wide : wide + head] = across.astype(BF16)
        xz_ref[:, wide + head :] = back.astype(BF16)
        n_ref[...] = square
        for store in stores:
            store.wait()

    return pl.pallas_call(
        kernel,
        out_shape=[
            pltpu.HBM((tokens, width), BF16),
            jax.ShapeDtypeStruct((tokens, wide + 2 * head), BF16),
            jax.ShapeDtypeStruct((tokens, 1), F32),
        ],
        in_specs=[IN_SMEM] + [ANYWHERE] * groups + [IN_HBM, IN_VMEM, IN_HBM, IN_HBM],
        out_specs=[IN_HBM, IN_VMEM, IN_VMEM],
        scratch_shapes=[
            pltpu.VMEM((tokens, width), BF16),
            pltpu.VMEM((tokens, width), BF16),
            pltpu.VMEM((width, wide), BF16),
            pltpu.VMEM((head, width), BF16),
            pltpu.SemaphoreType.DMA((copies,)),
        ],
        compiler_params=params(),
        name="project",
    )(
        place,
        *parts,
        in_hbm(cotangent),
        gain,
        in_hbm(w_layer),
        in_hbm(out_layer),
    )


def couple(slices, gain, w_layer, out_layer, last, passed, after):
    sections = len(slices)
    count, width = slices[0].shape
    head = out_layer.shape[0]
    wide = w_layer.shape[1]
    below = (sections - 2) * wide
    packed = below + max(wide, (sections - 1) * head)
    cuts = steps(width)
    copies = len(cuts) * (sections + 2) + sections - 1

    def kernel(last_ref, *refs):
        s_refs = refs[:sections]
        g_ref, w_ref, o_ref = refs[sections : sections + 3]
        out_ref, stack_ref, _, r_in, w_in, o_in, sems = refs[sections + 4 + len(after) :]
        rows = [slice(r * count, (r + 1) * count) for r in range(sections)]
        start = mover(sems)
        loads = []
        for cut in cuts:
            mine = [start(w_ref.at[cut], w_in.at[cut])]
            mine.append(start(o_ref.at[:, cut], o_in.at[:, cut]))
            for r in range(sections):
                mine.append(start(s_refs[r].at[:, cut], r_in.at[rows[r], cut]))
            loads.append(mine)
        through = jnp.zeros((sections * count, wide), F32)
        across = jnp.zeros((sections * count, head), F32)
        for cut, mine in zip(cuts, loads):
            for load in mine:
                load.wait()
            r = r_in[:, cut]
            through += dot_nn((r.astype(F32) * g_ref[:, cut]).astype(BF16), w_in[cut, :])
            across += dot_nt(r, o_in[:, cut])
        stores = [start(r_in.at[rows[r]], stack_ref.at[r - 1]) for r in range(1, sections)]
        through = through.astype(BF16)
        across = across.astype(BF16)
        out_ref[...] = jnp.zeros_like(out_ref)
        for r in range(1, sections - 1):
            out_ref[:, (r - 1) * wide : r * wide] = through[rows[r]]

        @pl.when(last_ref[0] == 1)
        def _():
            out_ref[:, below : below + wide] = through[rows[-1]]

        @pl.when(last_ref[0] == 0)
        def _():
            for r in range(sections - 1):
                out_ref[:, below + r * head : below + (r + 1) * head] = across[rows[r]]

        for store in stores:
            store.wait()

    return pl.pallas_call(
        kernel,
        out_shape=[
            jax.ShapeDtypeStruct((count, packed), BF16),
            pltpu.HBM((sections - 1, count, width), BF16),
            jax.ShapeDtypeStruct(passed.shape, passed.dtype),
        ],
        in_specs=[IN_SMEM]
        + [ANYWHERE] * sections
        + [IN_VMEM, IN_HBM, IN_HBM]
        + [ANYWHERE] * (1 + len(after)),
        out_specs=[IN_VMEM, IN_HBM, ANYWHERE],
        input_output_aliases={sections + 4: 2},
        scratch_shapes=[
            pltpu.VMEM((sections * count, width), BF16),
            pltpu.VMEM((width, wide), BF16),
            pltpu.VMEM((head, width), BF16),
            pltpu.SemaphoreType.DMA((copies,)),
        ],
        compiler_params=params(),
        name="couple",
    )(last, *slices, gain, in_hbm(w_layer), in_hbm(out_layer), passed, *after)


def layout(sections, wide, head):
    through, across, at = {}, {}, 0
    for k in range(sections):
        for j in range(k):
            through[j, k] = slice(at, at + wide)
            at += wide
        for j in range(k + 1 if k < sections - 1 else 0):
            across[j, k] = slice(at, at + head)
            at += head
    return through, across, at


def compact(parts, section, wide, head, after):
    sections = len(parts)
    count = parts[0].shape[0]
    below = (sections - 2) * wide
    through, across, total = layout(sections, wide, head)

    def kernel(s_ref, *refs):
        part_refs, out_ref = refs[:sections], refs[-1]
        mine = s_ref[0]

        def fill(k, r):
            for j in range(k):
                at = (k - j - 1) * wide
                out_ref[0, :, through[j, k]] = part_refs[r][:, at : at + wide]
            for j in range(k + 1 if k < sections - 1 else 0):
                at = below + (k - j) * head
                out_ref[0, :, across[j, k]] = part_refs[r][:, at : at + head]

        for s in range(sections):

            @pl.when(mine == s)
            def _(s=s):
                for r in range(sections):
                    fill((s - r) % sections, r)

    vmem = pl.BlockSpec(memory_space=pltpu.VMEM)
    return pl.pallas_call(
        kernel,
        out_shape=jax.ShapeDtypeStruct((1, count, total), BF16),
        in_specs=[IN_SMEM] + [vmem] * sections + [ANYWHERE] * len(after),
        out_specs=vmem,
        compiler_params=params(),
        name="compact",
    )(section, *parts, *after)


def merge(first, second, after):
    count = first.shape[0]

    def kernel(first_ref, second_ref, *refs):
        refs[-1][:count] = first_ref[...]
        refs[-1][count:] = second_ref[...]

    return pl.pallas_call(
        kernel,
        out_shape=jax.ShapeDtypeStruct((2 * count,) + first.shape[1:], first.dtype),
        in_specs=[IN_VMEM] * 2 + [ANYWHERE] * len(after),
        out_specs=IN_VMEM,
        compiler_params=params(),
        name="merge",
    )(first, second, *after)


def serial(xz, pieces, places, norms, mask, section, gain, w_layer, out_layer, streams, passed):
    sections = len(xz)
    tokens = norms.shape[0]
    head, width = out_layer.shape
    wide = 3 * head
    scale = 1.0 / math.sqrt(head)
    chunk = streams[-1].stop
    cuts = [slice(at, at + chunk) for at in range(0, width, chunk)]
    through_at, across_at, _ = layout(sections, wide, head)
    count, packed = pieces[0].shape[-2:]
    plane = head // count
    n_in = sections + len(pieces)
    copies = sections + plane + 3 * len(cuts)

    def kernel(s_ref, p_ref, *refs):
        xz_refs, piece_refs = refs[:sections], refs[sections:n_in]
        n_ref, mask_ref, g_ref, w_ref, o_ref = refs[n_in : n_in + 5]
        n_out = n_in + 5 + len(passed)
        back_ref, b_ref, t_ref, a_ref = refs[n_out : n_out + 4]
        first_refs = refs[n_out + 4 : n_out + 4 + len(streams)]
        scratch = refs[n_out + 4 + len(streams) + len(passed) :]
        xz_all, table, mixes, weights, projs, dmix, v_ref, back_in, w_in, o_in, sems = scratch
        mine = s_ref[0]
        started = []

        def start(source, target):
            copy = pltpu.make_async_copy(source, target, sems.at[len(started)])
            copy.start()
            started.append(copy)

        for r in range(sections):
            start(xz_refs[r], xz_all.at[lax.rem(mine + sections - r, sections)])
        at = 0
        for ref in piece_refs:
            for i in range(ref.shape[0]):
                start(ref.at[i], table.at[p_ref[at]])
                at += 1
        small = list(started)
        for cut in cuts:
            start(w_ref.at[cut], w_in.at[cut])
            start(o_ref.at[:, cut], o_in.at[:, cut])
        large = started[len(small) :]
        for copy in small:
            copy.wait()

        def through(j, k):
            return table[:, :, through_at[j, k]].reshape(head, wide)

        def across(j, k):
            return table[:, :, across_at[j, k]].reshape(head, head)

        allowed = mask_ref[...] > 0.5
        norm = n_ref[...]
        rstds, tails, mixed = [], [], []
        for s in range(sections):
            proj = xz_all[s, :, :wide].astype(F32)
            for j in range(s):
                proj = proj + dot_nn(mixed[j], through(j, s))
            rstd = lax.rsqrt(norm * (1.0 / width) + EPS)
            proj = proj * rstd
            projs[s] = proj.astype(BF16)
            q, k, v = (projs[s, :, i * head : (i + 1) * head] for i in range(3))
            scores = jnp.where(allowed, dot_nt(q, k) * scale, -1e30)
            scores = jnp.exp(scores - jnp.max(scores, axis=1, keepdims=True))
            soft = scores / jnp.sum(scores, axis=1, keepdims=True)
            weights[s] = soft
            mix = dot_nn(soft.astype(BF16), v).astype(BF16)
            mixed.append(mix)
            mixes[:, s * head : (s + 1) * head] = mix
            rstds.append(rstd)
            dmix[:, s * head : (s + 1) * head] = xz_all[s, :, wide + head :].astype(F32)
            if s == sections - 1:
                break
            y = xz_all[s, :, wide : wide + head].astype(F32)
            for j in range(s):
                y = y + dot_nn(mixed[j], across(j, s))
            tail = y + dot_nn(mix, across(s, s))
            norm = norm + jnp.sum(mix.astype(F32) * (y + tail), axis=1, keepdims=True)
            norm = jnp.maximum(norm, 0.0)
            tails.append(tail)
        total = jnp.zeros((tokens, 1), F32)
        a_ref[...] = jnp.zeros_like(a_ref)
        for s in reversed(range(sections)):
            cols = slice(s * head, (s + 1) * head)
            da = dmix[:, cols]
            if s < sections - 1:
                da = da - total * tails[s]
            da = da.astype(BF16)
            q, k, v = (projs[s, :, i * head : (i + 1) * head] for i in range(3))
            soft = weights[s]
            dv = dot_tn(soft.astype(BF16), da)
            dsoft = dot_nt(da, v)
            dscore = soft * (dsoft - jnp.sum(dsoft * soft, axis=1, keepdims=True))
            dscore = (dscore * scale).astype(BF16)
            dproj = jnp.concatenate([dot_nn(dscore, k), dot_tn(dscore, q), dv], axis=1)
            along = jnp.sum(dproj * projs[s].astype(F32), axis=1, keepdims=True)
            first = (dproj * rstds[s]).astype(BF16)
            second = (-total * mixes[:, cols].astype(F32)).astype(BF16)
            total = total + rstds[s] * rstds[s] * along * (1.0 / width)
            for j in reversed(range(s)):
                term = dot_nt(first, through(j, s))
                if s < sections - 1:
                    term = term + dot_nt(second, across(j, s))
                dmix[:, j * head : (j + 1) * head] += term

            @pl.when(mine == s)
            def _(first=first, second=second, total=total):
                v_ref[:, :wide] = first
                v_ref[:, wide:] = second
                t_ref[...] = total

            for r in range(1, sections - s):

                @pl.when(mine == s + r)
                def _(r=r, cols=cols):
                    a_ref[:, (r - 1) * head : r * head] = mixes[:, cols]

        for i, cut in enumerate(cuts):
            large[2 * i].wait()
            large[2 * i + 1].wait()
            back = dot_nt(v_ref[:, :wide], w_in[cut, :])
            own = back * g_ref[:, cut] + dot_nn(v_ref[:, wide:], o_in[:, cut])
            own = own.astype(BF16)
            back_in[:, cut] = back.astype(BF16)
            start(back_in.at[:, cut], back_ref.at[:, cut])
            b_ref[i] = own
            if i == 0:
                for ref, part in zip(first_refs, streams):
                    ref[...] = own[:, part]
        for copy in started[len(small) + len(large) :]:
            copy.wait()

    vmem = pl.BlockSpec(memory_space=pltpu.VMEM)
    smem = pl.BlockSpec(memory_space=pltpu.SMEM)
    return pl.pallas_call(
        kernel,
        out_shape=[
            pltpu.HBM((tokens, width), BF16),
            pltpu.VMEM((len(cuts), tokens, chunk), BF16),
            pltpu.VMEM((tokens, 1), F32),
            pltpu.VMEM((tokens, (sections - 1) * head), BF16),
        ]
        + [pltpu.VMEM((tokens, part.stop - part.start), BF16) for part in streams]
        + [jax.ShapeDtypeStruct(array.shape, array.dtype) for array in passed],
        in_specs=[smem, smem]
        + [ANYWHERE] * n_in
        + [vmem, vmem, vmem, IN_HBM, IN_HBM]
        + [ANYWHERE] * len(passed),
        out_specs=[IN_HBM] + [vmem] * (3 + len(streams)) + [ANYWHERE] * len(passed),
        input_output_aliases={
            2 + n_in + 5 + i: 4 + len(streams) + i for i in range(len(passed))
        },
        scratch_shapes=[
            pltpu.VMEM((sections,) + xz[0].shape, BF16),
            pltpu.VMEM((plane, count, packed), BF16),
            pltpu.VMEM((tokens, sections * head), BF16),
            pltpu.VMEM((sections, tokens, tokens), F32),
            pltpu.VMEM((sections, tokens, wide), BF16),
            pltpu.VMEM((tokens, sections * head), F32),
            pltpu.VMEM((tokens, wide + head), BF16),
            pltpu.VMEM((tokens, width), BF16),
            pltpu.VMEM((width, wide), BF16),
            pltpu.VMEM((head, width), BF16),
            pltpu.SemaphoreType.DMA((copies,)),
        ],
        compiler_params=params(),
        name="serial",
    )(
        section,
        places,
        *xz,
        *pieces,
        norms,
        mask,
        gain,
        in_hbm(w_layer),
        in_hbm(out_layer),
        *passed,
    )


def settle(total, mixes, stacks, places, x, cotangent, back, own):
    tokens, width = x.shape
    count, _, chunk = own.shape
    layers, rows = stacks[0].shape[1:3]
    entries = [(i, e) for i, stack in enumerate(stacks) for e in range(stack.shape[0])]
    plane = len(entries)
    head = plane * rows
    cuts = [slice(at, at + chunk) for at in range(0, width, chunk)]
    copies = plane * layers + 3 * len(cuts)

    def kernel(p_ref, t_ref, a_ref, b_ref, x_ref, c_ref, back_ref, *refs):
        stack_refs = refs[: len(stacks)]
        state_ref, dg_ref = refs[len(stacks) : len(stacks) + 2]
        lower, x_in, c_in, back_in, sems = refs[len(stacks) + 2 :]
        start = mover(sems)
        first = []
        for at, (i, e) in enumerate(entries):
            for r in range(layers):
                first.append(start(stack_refs[i].at[e, r], lower.at[r, p_ref[at]]))
        loads = []
        for cut in cuts:
            mine = [start(x_ref.at[:, cut], x_in.at[:, cut])]
            mine.append(start(c_ref.at[:, cut], c_in.at[:, cut]))
            mine.append(start(back_ref.at[:, cut], back_in.at[:, cut]))
            loads.append(mine)
        for load in first:
            load.wait()
        for i, (cut, mine) in enumerate(zip(cuts, loads)):
            for load in mine:
                load.wait()
            below = lower[:, :, :, cut].reshape(layers * head, chunk)
            here = x_in[:, cut].astype(F32) + dot_nn(a_ref[...], below)
            own = b_ref[i].astype(F32)
            full = c_in[:, cut].astype(F32) - t_ref[...] * here + own
            state_ref[0, i] = own
            state_ref[1, i] = full
            state_ref[2, i] = full
            gain = jnp.sum(back_in[:, cut].astype(F32) * here, axis=0, keepdims=True)
            for at in range(0, chunk, head):
                row = (cut.start + at) // head
                dg_ref[row : row + 1, :] = gain[:, at : at + head]

    return pl.pallas_call(
        kernel,
        out_shape=[
            pltpu.VMEM((3, count, tokens, chunk), F32),
            pltpu.VMEM((width // head, head), F32),
        ],
        in_specs=[IN_SMEM, IN_VMEM, IN_VMEM, IN_VMEM] + [IN_HBM] * (3 + len(stacks)),
        out_specs=[IN_VMEM] * 2,
        scratch_shapes=[
            pltpu.VMEM((layers, plane, rows, width), BF16),
            pltpu.VMEM((tokens, width), BF16),
            pltpu.VMEM((tokens, width), BF16),
            pltpu.VMEM((tokens, width), BF16),
            pltpu.SemaphoreType.DMA((copies,)),
        ],
        compiler_params=params(),
        name="settle",
    )(
        places,
        in_vmem(total),
        in_vmem(mixes),
        in_vmem(own),
        *[in_hbm(array) for array in (x, cotangent, back, *stacks)],
    )


def join(index, arrived, state, cols, after):
    tokens, part = arrived.shape

    def kernel(i_ref, r_ref, _, *refs):
        send_ref, state_ref = refs[len(after) :]
        at = i_ref[0]
        r = r_ref[...].astype(F32)
        send_ref[...] = (state_ref[0, at, :, cols] + r).astype(BF16)
        state_ref[2, at, :, cols] = state_ref[1, at, :, cols] + r

    return pl.pallas_call(
        kernel,
        out_shape=[pltpu.VMEM((tokens, part), BF16), pltpu.VMEM(state.shape, F32)],
        in_specs=[IN_SMEM] + [IN_VMEM] * 2 + [ANYWHERE] * len(after),
        out_specs=[IN_VMEM] * 2,
        input_output_aliases={2: 1},
        compiler_params=params(),
        name="join",
    )(index, in_vmem(arrived), in_vmem(state), *after)


def finish(index, arrived, state, streams):
    _, count, tokens, chunk = state.shape

    def kernel(i_ref, *refs):
        r_refs = refs[: len(streams)]
        state_ref, whole_ref, whole, sems = refs[len(streams) :]
        at = i_ref[0]
        copies = []
        for i in range(count):
            whole[i] = state_ref[2, i].astype(BF16)

            @pl.when(at == i)
            def _(i=i):
                for ref, cols in zip(r_refs, streams):
                    full = state_ref[1, i, :, cols] + ref[...].astype(F32)
                    whole[i, :, cols] = full.astype(BF16)

            there = whole_ref.at[:, pl.ds(i * chunk, chunk)]
            copies.append(pltpu.make_async_copy(whole.at[i], there, sems.at[i]))
            copies[-1].start()
        for copy in copies:
            copy.wait()

    return pl.pallas_call(
        kernel,
        out_shape=pltpu.HBM((tokens, count * chunk), BF16),
        in_specs=[IN_SMEM] + [IN_VMEM] * (len(streams) + 1),
        out_specs=IN_HBM,
        scratch_shapes=[
            pltpu.VMEM((count, tokens, chunk), BF16),
            pltpu.SemaphoreType.DMA((count,)),
        ],
        compiler_params=params(),
        name="finish",
    )(index, *[in_vmem(array) for array in arrived], in_vmem(state))


def added(arrays):
    def kernel(*refs):
        total = refs[0][...]
        for ref in refs[1:-1]:
            total = total + ref[...]
        refs[-1][...] = total

    return pl.pallas_call(
        kernel,
        out_shape=pltpu.VMEM(arrays[0].shape, F32),
        in_specs=[IN_VMEM] * len(arrays),
        out_specs=IN_VMEM,
        compiler_params=params(),
        name="added",
    )(*[in_vmem(array) for array in arrays])


STREAMS = 2
CHUNKS = 4


def stream_columns(chunk):
    lanes = 128
    tiles = chunk // lanes
    ends = [-(-tiles * (i + 1) // STREAMS) * lanes for i in range(STREAMS)]
    return [slice(start, end) for start, end in zip([0] + ends, ends)]


def shifted(array, by):
    sections = lax.axis_size("section")
    return lax.ppermute(array, "section", [(i, (i + by) % sections) for i in range(sections)])


def raised(array, by):
    sections = lax.axis_size("section")
    return lax.ppermute(array, "section", [(i, i + by) for i in range(sections - by)])


def swapped(array, step):
    groups = lax.axis_size("group")
    devices = lax.axis_size("dp")
    bits = devices.bit_length() - 1
    pairs = []
    for p in range(devices):
        for g in range(groups):
            pairs.append((p * groups + g, (p ^ (1 << ((step + g) % bits))) * groups + g))
    return lax.ppermute(array, ("dp", "group"), pairs)


def handed(array, by):
    groups = lax.axis_size("group")
    return lax.ppermute(array, "group", [(i, (i + by) % groups) for i in range(groups)])


def plane_places():
    groups = lax.axis_size("group")
    bits = lax.axis_size("dp").bit_length() - 1
    masks = []
    for g in range(groups):
        order = [0]
        for step in range(bits):
            order = order + [m ^ (1 << ((step + g) % bits)) for m in order]
        masks.append(order)
    masks = jnp.asarray(masks, jnp.int32)
    dp, member = lax.axis_index("dp"), lax.axis_index("group")
    places = []
    for r in range(groups):
        giver = (member + groups - r) % groups
        places.append((dp ^ masks[giver]) * groups + giver)
    return jnp.concatenate(places).astype(jnp.int32)


def local(tokens_in, cotangent, gains, w_qkv, w_out, segments, plan):
    sections = lax.axis_size("section")
    groups = lax.axis_size("group")
    devices = lax.axis_size("dp")
    plane = devices * groups
    section = lax.axis_index("section")
    member = lax.axis_index("group")
    rows_dev = plan.shape[1]
    length = segments.shape[1]
    tokens, width = tokens_in.shape
    head = w_out.shape[1]
    share = rows_dev // groups
    w_layer, out_layer = w_qkv[0], w_out[0]
    place = member.astype(jnp.int32)[None]
    layer = section.astype(jnp.int32)[None]

    slice_rows = head // plane
    mine = lax.axis_index("dp") * groups + member
    own_rows, *parts = pick(
        tokens_in.reshape(rows_dev, length, width),
        plan,
        place,
        groups,
        out_layer,
        mine.astype(jnp.int32)[None],
        slice_rows,
    )
    slices = [own_rows] + [raised(own_rows, r) for r in range(1, sections)]
    chosen = jnp.take(segments, plan[0], axis=0, mode="clip").astype(BF16)
    chosen = chosen.reshape(groups, share, length)
    moved, moved_seg = [], []
    for r in range(groups):
        outgoing = lax.dynamic_index_in_dim(chosen, (member + r) % groups, 0, keepdims=False)
        moved.append(handed(parts[r], r) if r else parts[r])
        moved_seg.append(handed(outgoing, r) if r else outgoing)
    moved = [part.reshape(share * length, width) for part in moved]
    order = (member - jnp.arange(groups)) % groups
    seg = jnp.take(jnp.stack(moved_seg), order, axis=0, mode="clip").reshape(tokens)
    at = jnp.arange(tokens)
    mask = (
        (at[:, None] >= at[None, :])
        & (at[:, None] // length == at[None, :] // length)
        & (seg[:, None] == seg[None, :])
    ).astype(F32)

    x, xz, norms = project(moved, cotangent, gains, w_layer, out_layer, place)

    last = (section == sections - 1).astype(jnp.int32)[None]
    places = plane_places()
    streams = stream_columns(width // CHUNKS)
    bits = devices.bit_length() - 1
    xz_all = [xz] + [shifted(xz, r) for r in range(1, min(2, sections))]
    coupling, stack, xz_later = couple(
        slices, gains, w_layer, out_layer, last, xz, [mask, places] + xz_all[1:]
    )
    xz_all = xz_all + [shifted(xz_later, r) for r in range(2, sections)]
    others = [shifted(coupling, r) for r in range(1, sections)]
    pieces = [compact([coupling] + others, layer, 3 * head, head, xz_all[2:3])]

    rows = [stack[None]]
    for step in range(bits):
        if step > 0:
            pieces = [merge(*pieces, xz_all[3:] + rows[1:])]
        pieces = pieces + [swapped(pieces[0], step)]
        rows = rows + [swapped(array, step) for array in rows]
    pieces = pieces + [handed(array, r) for r in range(1, groups) for array in pieces]
    outs = serial(
        xz_all, pieces, places, norms, mask, layer, gains, w_layer, out_layer, streams, rows
    )
    back, own, total, mixes = outs[:4]
    leaving, rows = list(outs[4 : 4 + len(streams)]), list(outs[4 + len(streams) :])
    rows = rows + [handed(array, r) for r in range(1, groups) for array in rows]
    state, gain = settle(total, mixes, rows, places, x, cotangent, back, own)

    def crossed(array, by):
        return lax.ppermute(array, "dp", [(p, p ^ by) for p in range(devices)])

    gain_chip = added([gain] + [crossed(gain, by) for by in range(1, devices)])
    gain_whole = added([gain_chip] + [handed(gain_chip, r) for r in range(1, groups)])
    gain_whole = gain_whole.reshape(1, width)

    down = [(i, i - 1) for i in range(1, sections)]
    behind = sections - 1 - section

    def index(tick):
        return jnp.clip(tick - behind, 0, CHUNKS - 1).astype(jnp.int32)

    ticks = CHUNKS + sections - 1
    for tick in range(1, ticks):
        chunk_at = index(tick)[None]
        arrived = [lax.ppermute(array, "section", down) for array in leaving]
        after = {ticks - 3: [gain_chip], ticks - 2: [gain_whole]}.get(tick, [])
        if tick < ticks - 1:
            for i, cols in enumerate(streams):
                leaving[i], state = join(chunk_at, arrived[i], state, cols, after)
    out = finish(chunk_at, arrived, state, streams)
    return (out[None], gain_whole)


def attend(hidden, segment, gain_row, w_layer, out_layer):
    count, length, width = hidden.shape
    head = out_layer.shape[0]
    scaled = hidden * lax.rsqrt(jnp.mean(hidden * hidden, axis=-1, keepdims=True) + EPS) * gain_row
    normed = scaled.astype(BF16).reshape(count * length, width)
    projected = jnp.dot(normed, w_layer, preferred_element_type=F32).reshape(count, length, 3 * head)
    query = projected[:, :, :head]
    keyed = projected[:, :, head : 2 * head]
    valued = projected[:, :, 2 * head :]
    positions = jnp.arange(length)
    allowed = (positions[:, None] >= positions[None, :])[None] & (
        segment[:, :, None] == segment[:, None, :]
    )
    scores = jnp.einsum("rid,rjd->rij", query, keyed, precision=lax.Precision.HIGHEST)
    scores = jnp.where(allowed, scores / math.sqrt(head), -1e30)
    weights = jax.nn.softmax(scores, axis=-1)
    mixed = jnp.einsum("rij,rjd->rid", weights, valued, precision=lax.Precision.HIGHEST)
    mixed = mixed.astype(BF16).reshape(count * length, head)
    output = jnp.dot(mixed, out_layer, preferred_element_type=F32).reshape(count, length, width)
    return hidden + output


MB_ROWS = 2


def relay(tokens_in, cotangent, gains, w_qkv, w_out, segments, plan):
    sections = lax.axis_size("section")
    section = lax.axis_index("section")
    rows_dev = plan.shape[1]
    width = tokens_in.shape[1]
    length = segments.shape[1]
    micro = rows_dev // MB_ROWS
    blocks = tokens_in.reshape(rows_dev, length, width)
    chosen = jnp.take(blocks, plan[0], axis=0)
    chosen_seg = jnp.take(segments, plan[0], axis=0).astype(BF16)
    assigned = lax.all_to_all(chosen, "group", split_axis=0, concat_axis=0, tiled=True)
    moved_seg = lax.all_to_all(chosen_seg, "group", split_axis=0, concat_axis=0, tiled=True)
    assigned = assigned.reshape(micro, MB_ROWS, length, width)
    seg_groups = moved_seg.reshape(micro, MB_ROWS, length)
    gain_row, w_layer, out_layer = gains[0], w_qkv[0], w_out[0]
    grad_rows = cotangent.reshape(micro, MB_ROWS, length, width)
    ticks = micro + sections - 1

    def passed_along(array, by):
        pairs = [(i, i + by) for i in range(sections) if 0 <= i + by < sections]
        return lax.ppermute(array, "section", pairs)

    def at(array, i):
        return lax.dynamic_index_in_dim(array, i, 0, keepdims=False)

    def forward_tick(tick, carry):
        saved, arrived = carry
        index = tick - section
        valid = (index >= 0) & (index < micro)
        clipped = jnp.clip(index, 0, micro - 1)
        entering = jnp.where(section == 0, at(assigned, clipped), arrived)
        kept = jnp.where(valid, entering, at(saved, clipped))
        saved = lax.dynamic_update_index_in_dim(saved, kept, clipped, 0)
        segment = at(seg_groups, clipped)

        def run_layer(value):
            return attend(value.astype(F32), segment, gain_row, w_layer, out_layer).astype(BF16)

        leaving = lax.cond(valid, run_layer, jnp.zeros_like, entering)
        return (saved, passed_along(leaving, 1))

    saved_init = jnp.zeros((micro, MB_ROWS, length, width), BF16)
    arrive_init = jnp.zeros((MB_ROWS, length, width), BF16)
    saved, _ = lax.fori_loop(0, ticks, forward_tick, (saved_init, arrive_init))

    def backward_tick(tick, carry):
        grads_x, gain_total, arrived = carry
        index = tick - (sections - 1 - section)
        valid = (index >= 0) & (index < micro)
        clipped = jnp.clip(index, 0, micro - 1)
        entering = jnp.where(section == sections - 1, at(grad_rows, clipped), arrived)
        segment = at(seg_groups, clipped)
        stored = at(saved, clipped).astype(F32)

        def local_layer(hidden, gains_here):
            return attend(hidden, segment, gains_here, w_layer, out_layer)

        def run_back(value):
            _, pullback = jax.vjp(local_layer, stored, gain_row)
            grad_hidden, grad_gain = pullback(value.astype(F32))
            return (grad_hidden.astype(BF16), grad_gain)

        def skip_back(value):
            return (jnp.zeros_like(value), jnp.zeros(gain_row.shape, F32))

        sending, grad_gain = lax.cond(valid, run_back, skip_back, entering)
        kept = jnp.where(valid, sending, at(grads_x, clipped))
        grads_x = lax.dynamic_update_index_in_dim(grads_x, kept, clipped, 0)
        return (grads_x, gain_total + grad_gain, passed_along(sending, -1))

    gain_init = jnp.zeros(gain_row.shape, F32)
    grads_x, gain_total, _ = lax.fori_loop(
        0, ticks, backward_tick, (saved_init, gain_init, arrive_init)
    )
    gain_whole = lax.psum(gain_total, ("dp", "group"))
    return (grads_x.reshape(1, rows_dev * length, width), gain_whole[None])


def solution(mesh):
    placed = (
        P(("dp", "group"), None),
        P(("dp", "group"), None),
        P("section", None),
        P("section", None, None),
        P("section", None, None),
        P(("dp", "group"), None),
        P(("dp", "group"), None),
    )

    def chosen(tokens_in, cotangent, gains, w_qkv, w_out, segments, plan):
        sections, head, width = w_out.shape
        devices = mesh.shape["dp"]
        small = sections * 4 * head < width and devices & (devices - 1) == 0
        body = local if small and sections > 1 else relay
        return jax.shard_map(
            body,
            mesh=mesh,
            in_specs=placed,
            out_specs=(P("section", ("dp", "group"), None), P("section", None)),
            check_vma=False,
        )(tokens_in, cotangent, gains, w_qkv, w_out, segments, plan)

    return chosen
```

```python
import math

import jax
import jax.numpy as jnp
from jax import lax
from jax.experimental import pallas as pl
from jax.experimental.pallas import tpu as pltpu
from jax.sharding import PartitionSpec as P

EPS = 1e-05
VMEM_BYTES = 24 * 1024 * 1024
SMALL = 16 * 1024 * 1024
F32 = jnp.float32
BF16 = jnp.bfloat16


def dot_nn(a, b):
    return lax.dot_general(a, b, (((1,), (0,)), ((), ())), preferred_element_type=F32)


def dot_nt(a, b):
    return lax.dot_general(a, b, (((1,), (1,)), ((), ())), preferred_element_type=F32)


def dot_tn(a, b):
    return lax.dot_general(a, b, (((0,), (0,)), ((), ())), preferred_element_type=F32)


IN_HBM = pl.BlockSpec(memory_space=pltpu.HBM)
ANYWHERE = pl.BlockSpec(memory_space=pl.ANY)
IN_VMEM = pl.BlockSpec(memory_space=pltpu.VMEM)
IN_SMEM = pl.BlockSpec(memory_space=pltpu.SMEM)


def in_hbm(array):
    return pltpu.with_memory_space_constraint(array, pltpu.HBM)


def in_vmem(array):
    return pltpu.with_memory_space_constraint(array, pltpu.VMEM)


def mover(sems):
    used = []

    def start(source, target):
        copy = pltpu.make_async_copy(source, target, sems.at[len(used)])
        copy.start()
        used.append(copy)
        return copy

    return start


def steps(width):
    step = min(width, 1024)
    return [slice(at, at + step) for at in range(0, width, step)]


def params(limit=VMEM_BYTES):
    return pltpu.CompilerParams(vmem_limit_bytes=limit)


def pick(tokens, plan, place, groups, out_layer, mine, slice_rows):
    rows, length, width = tokens.shape
    share = rows // groups

    def kernel(plan_ref, place_ref, mine_ref, tokens_ref, o_ref, *rest):
        slice_ref, parts = rest[0], rest[1 : 1 + groups]
        slice_in, rows_in, sems = rest[1 + groups :]
        start = mover(sems)
        at = pl.ds(pl.multiple_of(mine_ref[0] * slice_rows, slice_rows), slice_rows)
        loads = [(start(o_ref.at[at], slice_in), slice_in, slice_ref)]
        for r in range(groups):
            target = lax.rem(place_ref[0] + r, groups)
            for c in range(share):
                here = rows_in.at[r * share + c]
                row = plan_ref[0, target * share + c]
                loads.append((start(tokens_ref.at[row], here), here, parts[r].at[c]))
        stores = []
        for load, here, there in loads:
            load.wait()
            stores.append(start(here, there))
        for store in stores:
            store.wait()

    return pl.pallas_call(
        kernel,
        out_shape=[pltpu.HBM((slice_rows, width), BF16)]
        + [pltpu.HBM((share, length, width), BF16)] * groups,
        in_specs=[IN_SMEM, IN_SMEM, IN_SMEM, IN_HBM, IN_HBM],
        out_specs=[IN_HBM] * (1 + groups),
        scratch_shapes=[
            pltpu.VMEM((slice_rows, width), BF16),
            pltpu.VMEM((rows, length, width), BF16),
            pltpu.SemaphoreType.DMA((2 * rows + 2,)),
        ],
        compiler_params=params(),
        name="pick",
    )(plan, place, mine, in_hbm(tokens), in_hbm(out_layer))


def project(parts, cotangent, gain, w_layer, out_layer, place):
    groups = len(parts)
    tokens, width = cotangent.shape
    head = out_layer.shape[0]
    wide = w_layer.shape[1]
    block = tokens // groups
    cuts = steps(width)
    copies = len(cuts) * (groups + 4)

    def kernel(place_ref, *refs):
        part_refs = refs[:groups]
        cot_ref, g_ref, w_ref, o_ref, x_ref, xz_ref, n_ref = refs[groups : groups + 7]
        x_in, c_in, w_in, o_in, sems = refs[groups + 7 :]
        start = mover(sems)
        loads = []
        for cut in cuts:
            mine = [start(w_ref.at[cut], w_in.at[cut])]
            mine.append(start(o_ref.at[:, cut], o_in.at[:, cut]))
            for r in range(groups):
                source = lax.rem(place_ref[0] + groups - r, groups)
                rows = pl.ds(pl.multiple_of(source * block, block), block)
                mine.append(start(part_refs[r].at[:, cut], x_in.at[rows, cut]))
            mine.append(start(cot_ref.at[:, cut], c_in.at[:, cut]))
            loads.append(mine)
        through = jnp.zeros((tokens, wide), F32)
        across = jnp.zeros((tokens, head), F32)
        back = jnp.zeros((tokens, head), F32)
        square = jnp.zeros((tokens, 1), F32)
        stores = []
        for cut, mine in zip(cuts, loads):
            for load in mine:
                load.wait()
            stores.append(start(x_in.at[:, cut], x_ref.at[:, cut]))
            x = x_in[:, cut]
            xf = x.astype(F32)
            through += dot_nn((xf * g_ref[:, cut]).astype(BF16), w_in[cut, :])
            across += dot_nt(x, o_in[:, cut])
            back += dot_nt(c_in[:, cut], o_in[:, cut])
            square += jnp.sum(xf * xf, axis=1, keepdims=True)
        xz_ref[:, :wide] = through.astype(BF16)
        xz_ref[:, wide : wide + head] = across.astype(BF16)
        xz_ref[:, wide + head :] = back.astype(BF16)
        n_ref[...] = square
        for store in stores:
            store.wait()

    return pl.pallas_call(
        kernel,
        out_shape=[
            pltpu.HBM((tokens, width), BF16),
            jax.ShapeDtypeStruct((tokens, wide + 2 * head), BF16),
            jax.ShapeDtypeStruct((tokens, 1), F32),
        ],
        in_specs=[IN_SMEM] + [ANYWHERE] * groups + [IN_HBM, IN_VMEM, IN_HBM, IN_HBM],
        out_specs=[IN_HBM, IN_VMEM, IN_VMEM],
        scratch_shapes=[
            pltpu.VMEM((tokens, width), BF16),
            pltpu.VMEM((tokens, width), BF16),
            pltpu.VMEM((width, wide), BF16),
            pltpu.VMEM((head, width), BF16),
            pltpu.SemaphoreType.DMA((copies,)),
        ],
        compiler_params=params(),
        name="project",
    )(
        place,
        *parts,
        in_hbm(cotangent),
        gain,
        in_hbm(w_layer),
        in_hbm(out_layer),
    )


def couple(slices, gain, w_layer, out_layer, last, after):
    sections = len(slices)
    count, width = slices[0].shape
    head = out_layer.shape[0]
    wide = w_layer.shape[1]
    below = (sections - 2) * wide
    packed = below + max(wide, (sections - 1) * head)
    cuts = steps(width)
    copies = len(cuts) * (sections + 2) + sections - 1

    def kernel(last_ref, *refs):
        s_refs = refs[:sections]
        g_ref, w_ref, o_ref = refs[sections : sections + 3]
        out_ref, stack_ref, r_in, w_in, o_in, sems = refs[sections + 3 + len(after) :]
        rows = [slice(r * count, (r + 1) * count) for r in range(sections)]
        start = mover(sems)
        loads = []
        for cut in cuts:
            mine = [start(w_ref.at[cut], w_in.at[cut])]
            mine.append(start(o_ref.at[:, cut], o_in.at[:, cut]))
            for r in range(sections):
                mine.append(start(s_refs[r].at[:, cut], r_in.at[rows[r], cut]))
            loads.append(mine)
        through = jnp.zeros((sections * count, wide), F32)
        across = jnp.zeros((sections * count, head), F32)
        for cut, mine in zip(cuts, loads):
            for load in mine:
                load.wait()
            r = r_in[:, cut]
            through += dot_nn((r.astype(F32) * g_ref[:, cut]).astype(BF16), w_in[cut, :])
            across += dot_nt(r, o_in[:, cut])
        stores = [start(r_in.at[rows[r]], stack_ref.at[r - 1]) for r in range(1, sections)]
        through = through.astype(BF16)
        across = across.astype(BF16)
        out_ref[...] = jnp.zeros_like(out_ref)
        for r in range(1, sections - 1):
            out_ref[:, (r - 1) * wide : r * wide] = through[rows[r]]

        @pl.when(last_ref[0] == 1)
        def _():
            out_ref[:, below : below + wide] = through[rows[-1]]

        @pl.when(last_ref[0] == 0)
        def _():
            for r in range(sections - 1):
                out_ref[:, below + r * head : below + (r + 1) * head] = across[rows[r]]

        for store in stores:
            store.wait()

    return pl.pallas_call(
        kernel,
        out_shape=[
            jax.ShapeDtypeStruct((count, packed), BF16),
            pltpu.HBM((sections - 1, count, width), BF16),
        ],
        in_specs=[IN_SMEM]
        + [ANYWHERE] * sections
        + [IN_VMEM, IN_HBM, IN_HBM]
        + [ANYWHERE] * len(after),
        out_specs=[IN_VMEM, IN_HBM],
        scratch_shapes=[
            pltpu.VMEM((sections * count, width), BF16),
            pltpu.VMEM((width, wide), BF16),
            pltpu.VMEM((head, width), BF16),
            pltpu.SemaphoreType.DMA((copies,)),
        ],
        compiler_params=params(),
        name="couple",
    )(last, *slices, gain, in_hbm(w_layer), in_hbm(out_layer), *after)


def layout(sections, wide, head):
    through, across, at = {}, {}, 0
    for k in range(sections):
        for j in range(k):
            through[j, k] = slice(at, at + wide)
            at += wide
        for j in range(k + 1 if k < sections - 1 else 0):
            across[j, k] = slice(at, at + head)
            at += head
    return through, across, at


def compact(parts, section, wide, head, after):
    sections = len(parts)
    count = parts[0].shape[0]
    below = (sections - 2) * wide
    through, across, total = layout(sections, wide, head)

    def kernel(s_ref, *refs):
        part_refs, out_ref = refs[:sections], refs[-1]
        mine = s_ref[0]

        def fill(k, r):
            for j in range(k):
                at = (k - j - 1) * wide
                out_ref[0, :, through[j, k]] = part_refs[r][:, at : at + wide]
            for j in range(k + 1 if k < sections - 1 else 0):
                at = below + (k - j) * head
                out_ref[0, :, across[j, k]] = part_refs[r][:, at : at + head]

        for s in range(sections):

            @pl.when(mine == s)
            def _(s=s):
                for r in range(sections):
                    fill((s - r) % sections, r)

    vmem = pl.BlockSpec(memory_space=pltpu.VMEM)
    return pl.pallas_call(
        kernel,
        out_shape=jax.ShapeDtypeStruct((1, count, total), BF16),
        in_specs=[IN_SMEM] + [vmem] * sections + [ANYWHERE] * len(after),
        out_specs=vmem,
        compiler_params=params(SMALL),
        name="compact",
    )(section, *parts, *after)


def merge(first, second, after):
    count = first.shape[0]

    def kernel(first_ref, second_ref, *refs):
        refs[-1][:count] = first_ref[...]
        refs[-1][count:] = second_ref[...]

    return pl.pallas_call(
        kernel,
        out_shape=jax.ShapeDtypeStruct((2 * count,) + first.shape[1:], first.dtype),
        in_specs=[IN_VMEM] * 2 + [ANYWHERE] * len(after),
        out_specs=IN_VMEM,
        compiler_params=params(SMALL),
        name="merge",
    )(first, second, *after)


def serial(xz, pieces, places, norms, mask, section, gain, w_layer, out_layer, streams):
    sections = len(xz)
    tokens = norms.shape[0]
    head, width = out_layer.shape
    wide = 3 * head
    scale = 1.0 / math.sqrt(head)
    chunk = streams[-1].stop
    cuts = [slice(at, at + chunk) for at in range(0, width, chunk)]
    through_at, across_at, _ = layout(sections, wide, head)
    count, packed = pieces[0].shape[-2:]
    plane = head // count
    n_in = sections + len(pieces)
    copies = sections + plane + 3 * len(cuts)

    def kernel(s_ref, p_ref, *refs):
        xz_refs, piece_refs = refs[:sections], refs[sections:n_in]
        n_ref, mask_ref, g_ref, w_ref, o_ref = refs[n_in : n_in + 5]
        n_out = n_in + 5
        back_ref, b_ref, t_ref, a_ref = refs[n_out : n_out + 4]
        first_refs = refs[n_out + 4 : n_out + 4 + len(streams)]
        scratch = refs[n_out + 4 + len(streams) :]
        xz_all, table, mixes, weights, projs, dmix, v_ref, back_in, w_in, o_in, sems = scratch
        mine = s_ref[0]
        started = []

        def start(source, target):
            copy = pltpu.make_async_copy(source, target, sems.at[len(started)])
            copy.start()
            started.append(copy)

        for r in range(sections):
            start(xz_refs[r], xz_all.at[mine ^ r])
        at = 0
        for ref in piece_refs:
            for i in range(ref.shape[0]):
                start(ref.at[i], table.at[p_ref[at]])
                at += 1
        small = list(started)
        for cut in cuts:
            start(w_ref.at[cut], w_in.at[cut])
            start(o_ref.at[:, cut], o_in.at[:, cut])
        large = started[len(small) :]
        for copy in small:
            copy.wait()

        def through(j, k):
            return table[:, :, through_at[j, k]].reshape(head, wide)

        def across(j, k):
            return table[:, :, across_at[j, k]].reshape(head, head)

        allowed = mask_ref[...] > 0.5
        norm = n_ref[...]
        rstds, tails, mixed = [], [], []
        for s in range(sections):
            proj = xz_all[s, :, :wide].astype(F32)
            for j in range(s):
                proj = proj + dot_nn(mixed[j], through(j, s))
            rstd = lax.rsqrt(norm * (1.0 / width) + EPS)
            proj = proj * rstd
            projs[s] = proj.astype(BF16)
            q, k, v = (projs[s, :, i * head : (i + 1) * head] for i in range(3))
            scores = jnp.where(allowed, dot_nt(q, k) * scale, -1e30)
            scores = jnp.exp(scores - jnp.max(scores, axis=1, keepdims=True))
            soft = scores / jnp.sum(scores, axis=1, keepdims=True)
            weights[s] = soft
            mix = dot_nn(soft.astype(BF16), v).astype(BF16)
            mixed.append(mix)
            mixes[:, s * head : (s + 1) * head] = mix
            rstds.append(rstd)
            dmix[:, s * head : (s + 1) * head] = xz_all[s, :, wide + head :].astype(F32)
            if s == sections - 1:
                break
            y = xz_all[s, :, wide : wide + head].astype(F32)
            for j in range(s):
                y = y + dot_nn(mixed[j], across(j, s))
            tail = y + dot_nn(mix, across(s, s))
            norm = norm + jnp.sum(mix.astype(F32) * (y + tail), axis=1, keepdims=True)
            norm = jnp.maximum(norm, 0.0)
            tails.append(tail)
        total = jnp.zeros((tokens, 1), F32)
        a_ref[...] = jnp.zeros_like(a_ref)
        for s in reversed(range(sections)):
            cols = slice(s * head, (s + 1) * head)
            da = dmix[:, cols]
            if s < sections - 1:
                da = da - total * tails[s]
            da = da.astype(BF16)
            q, k, v = (projs[s, :, i * head : (i + 1) * head] for i in range(3))
            soft = weights[s]
            dv = dot_tn(soft.astype(BF16), da)
            dsoft = dot_nt(da, v)
            dscore = soft * (dsoft - jnp.sum(dsoft * soft, axis=1, keepdims=True))
            dscore = (dscore * scale).astype(BF16)
            dproj = jnp.concatenate([dot_nn(dscore, k), dot_tn(dscore, q), dv], axis=1)
            along = jnp.sum(dproj * projs[s].astype(F32), axis=1, keepdims=True)
            first = (dproj * rstds[s]).astype(BF16)
            second = (-total * mixes[:, cols].astype(F32)).astype(BF16)
            total = total + rstds[s] * rstds[s] * along * (1.0 / width)
            for j in reversed(range(s)):
                term = dot_nt(first, through(j, s))
                if s < sections - 1:
                    term = term + dot_nt(second, across(j, s))
                dmix[:, j * head : (j + 1) * head] += term

            @pl.when(mine == s)
            def _(first=first, second=second, total=total):
                v_ref[:, :wide] = first
                v_ref[:, wide:] = second
                t_ref[...] = total

            for r in range(1, sections - s):

                @pl.when(mine == s + r)
                def _(r=r, cols=cols):
                    a_ref[:, (r - 1) * head : r * head] = mixes[:, cols]

        for i, cut in enumerate(cuts):
            large[2 * i].wait()
            large[2 * i + 1].wait()
            back = dot_nt(v_ref[:, :wide], w_in[cut, :])
            own = back * g_ref[:, cut] + dot_nn(v_ref[:, wide:], o_in[:, cut])
            own = own.astype(BF16)
            back_in[:, cut] = back.astype(BF16)
            start(back_in.at[:, cut], back_ref.at[:, cut])
            b_ref[i] = own
            if i == 0:
                for ref, part in zip(first_refs, streams):
                    ref[...] = own[:, part]
        for copy in started[len(small) + len(large) :]:
            copy.wait()

    vmem = pl.BlockSpec(memory_space=pltpu.VMEM)
    smem = pl.BlockSpec(memory_space=pltpu.SMEM)
    return pl.pallas_call(
        kernel,
        out_shape=[
            pltpu.HBM((tokens, width), BF16),
            pltpu.VMEM((len(cuts), tokens, chunk), BF16),
            pltpu.VMEM((tokens, 1), F32),
            pltpu.VMEM((tokens, (sections - 1) * head), BF16),
        ]
        + [pltpu.VMEM((tokens, part.stop - part.start), BF16) for part in streams],
        in_specs=[smem, smem] + [ANYWHERE] * n_in + [vmem, vmem, vmem, IN_HBM, IN_HBM],
        out_specs=[IN_HBM] + [vmem] * (3 + len(streams)),
        scratch_shapes=[
            pltpu.VMEM((sections,) + xz[0].shape, BF16),
            pltpu.VMEM((plane, count, packed), BF16),
            pltpu.VMEM((tokens, sections * head), BF16),
            pltpu.VMEM((sections, tokens, tokens), F32),
            pltpu.VMEM((sections, tokens, wide), BF16),
            pltpu.VMEM((tokens, sections * head), F32),
            pltpu.VMEM((tokens, wide + head), BF16),
            pltpu.VMEM((tokens, width), BF16),
            pltpu.VMEM((width, wide), BF16),
            pltpu.VMEM((head, width), BF16),
            pltpu.SemaphoreType.DMA((copies,)),
        ],
        compiler_params=params(),
        name="serial",
    )(
        section,
        places,
        *xz,
        *pieces,
        norms,
        mask,
        gain,
        in_hbm(w_layer),
        in_hbm(out_layer),
    )


def hold(arrays, after):
    def kernel(*refs):
        pass

    return pl.pallas_call(
        kernel,
        out_shape=[pltpu.HBM(array.shape, array.dtype) for array in arrays],
        in_specs=[IN_HBM] * len(arrays) + [ANYWHERE] * len(after),
        out_specs=[IN_HBM] * len(arrays),
        input_output_aliases={i: i for i in range(len(arrays))},
        compiler_params=params(SMALL),
        name="hold",
    )(*[in_hbm(array) for array in arrays], *after)


def settle(total, mixes, stacks, places, x, cotangent, back, own, index, arrived, streams):
    tokens, width = x.shape
    count, _, chunk = own.shape
    layers, rows = stacks[0].shape[1:3]
    entries = [(i, e) for i, stack in enumerate(stacks) for e in range(stack.shape[0])]
    plane = len(entries)
    head = plane * rows
    cuts = [slice(at, at + chunk) for at in range(0, width, chunk)]
    copies = plane * layers + 3 * len(cuts)

    def kernel(p_ref, i_ref, t_ref, a_ref, b_ref, *refs):
        r_refs, refs = refs[: len(streams)], refs[len(streams) :]
        x_ref, c_ref, back_ref = refs[:3]
        stack_refs, refs = refs[3 : 3 + len(stacks)], refs[3:]
        both_ref, out_ref, dg_ref = refs[len(stacks) : len(stacks) + 3]
        lower, x_in, c_in, back_in, sems = refs[len(stacks) + 3 :]
        start = mover(sems)
        first = []
        for at, (i, e) in enumerate(entries):
            for r in range(layers):
                first.append(start(stack_refs[i].at[e, r], lower.at[r, p_ref[at]]))
        loads = []
        for cut in cuts:
            mine = [start(x_ref.at[:, cut], x_in.at[:, cut])]
            mine.append(start(c_ref.at[:, cut], c_in.at[:, cut]))
            mine.append(start(back_ref.at[:, cut], back_in.at[:, cut]))
            loads.append(mine)
        for load in first:
            load.wait()
        for i, (cut, mine) in enumerate(zip(cuts, loads)):
            for load in mine:
                load.wait()
            below = lower[:, :, :, cut].reshape(layers * head, chunk)
            here = x_in[:, cut].astype(F32) + dot_nn(a_ref[...], below)
            own = b_ref[i].astype(F32)
            full = c_in[:, cut].astype(F32) - t_ref[...] * here + own
            both_ref[0, i] = own
            both_ref[1, i] = full
            out_ref[i] = full.astype(BF16)
            gain = jnp.sum(back_in[:, cut].astype(F32) * here, axis=0, keepdims=True)
            for at in range(0, chunk, head):
                row = (cut.start + at) // head
                dg_ref[row : row + 1, :] = gain[:, at : at + head]
        at = i_ref[0]
        for ref, part in zip(r_refs, streams):
            full = both_ref[1, at, :, part] + ref[...].astype(F32)
            out_ref[at, :, part] = full.astype(BF16)

    return pl.pallas_call(
        kernel,
        out_shape=[
            pltpu.VMEM((2, count, tokens, chunk), F32),
            pltpu.VMEM((count, tokens, chunk), BF16),
            pltpu.VMEM((width // head, head), F32),
        ],
        in_specs=[IN_SMEM] * 2 + [IN_VMEM] * (3 + len(streams)) + [IN_HBM] * (3 + len(stacks)),
        out_specs=[IN_VMEM] * 3,
        scratch_shapes=[
            pltpu.VMEM((layers, plane, rows, width), BF16),
            pltpu.VMEM((tokens, width), BF16),
            pltpu.VMEM((tokens, width), BF16),
            pltpu.VMEM((tokens, width), BF16),
            pltpu.SemaphoreType.DMA((copies,)),
        ],
        compiler_params=params(),
        name="settle",
    )(
        places,
        index,
        in_vmem(total),
        in_vmem(mixes),
        in_vmem(own),
        *[in_vmem(array) for array in arrived],
        *[in_hbm(array) for array in (x, cotangent, back, *stacks)],
    )


def forward(index, arrived, own, cols):
    def kernel(i_ref, r_ref, b_ref, send_ref):
        own = b_ref[i_ref[0], :, cols].astype(F32)
        send_ref[...] = (own + r_ref[...].astype(F32)).astype(BF16)

    return pl.pallas_call(
        kernel,
        out_shape=pltpu.VMEM(arrived.shape, BF16),
        in_specs=[IN_SMEM, IN_VMEM, IN_VMEM],
        out_specs=IN_VMEM,
        compiler_params=params(SMALL),
        name="forward",
    )(index, in_vmem(arrived), in_vmem(own))


def join(index, arrived, both, out, cols, after):
    tokens, part = arrived.shape

    def kernel(i_ref, r_ref, both_ref, _, *refs):
        send_ref, out_ref = refs[len(after) :]
        at = i_ref[0]
        r = r_ref[...].astype(F32)
        send_ref[...] = (both_ref[0, at, :, cols] + r).astype(BF16)
        out_ref[at, :, cols] = (both_ref[1, at, :, cols] + r).astype(BF16)

    return pl.pallas_call(
        kernel,
        out_shape=[pltpu.VMEM((tokens, part), BF16), pltpu.VMEM(out.shape, BF16)],
        in_specs=[IN_SMEM] + [IN_VMEM] * 3 + [ANYWHERE] * len(after),
        out_specs=[IN_VMEM] * 2,
        input_output_aliases={3: 1},
        compiler_params=params(SMALL),
        name="join",
    )(index, in_vmem(arrived), in_vmem(both), in_vmem(out), *after)


def finish(index, arrived, both, out, streams):
    count, tokens, chunk = out.shape

    def kernel(i_ref, *refs):
        r_refs = refs[: len(streams)]
        both_ref, out_ref, whole_ref, last, sems = refs[len(streams) :]
        at = i_ref[0]
        last[...] = out_ref[...]
        for ref, cols in zip(r_refs, streams):
            full = both_ref[1, at, :, cols] + ref[...].astype(F32)
            last[at, :, cols] = full.astype(BF16)
        copies = []
        for i in range(count):
            there = whole_ref.at[:, pl.ds(i * chunk, chunk)]
            copies.append(pltpu.make_async_copy(last.at[i], there, sems.at[i]))
            copies[-1].start()
        for copy in copies:
            copy.wait()

    return pl.pallas_call(
        kernel,
        out_shape=pltpu.HBM((tokens, count * chunk), BF16),
        in_specs=[IN_SMEM] + [IN_VMEM] * (len(streams) + 2),
        out_specs=IN_HBM,
        scratch_shapes=[
            pltpu.VMEM((count, tokens, chunk), BF16),
            pltpu.SemaphoreType.DMA((count,)),
        ],
        compiler_params=params(SMALL),
        name="finish",
    )(index, *[in_vmem(array) for array in arrived], in_vmem(both), in_vmem(out))


def added(arrays):
    def kernel(*refs):
        total = refs[0][...]
        for ref in refs[1:-1]:
            total = total + ref[...]
        refs[-1][...] = total

    return pl.pallas_call(
        kernel,
        out_shape=pltpu.VMEM(arrays[0].shape, F32),
        in_specs=[IN_VMEM] * len(arrays),
        out_specs=IN_VMEM,
        compiler_params=params(SMALL),
        name="added",
    )(*[in_vmem(array) for array in arrays])


STREAMS = 2
CHUNKS = 4


def stream_columns(chunk):
    lanes = 128
    tiles = chunk // lanes
    ends = [-(-tiles * (i + 1) // STREAMS) * lanes for i in range(STREAMS)]
    return [slice(start, end) for start, end in zip([0] + ends, ends)]


def shifted(array, by):
    sections = lax.axis_size("section")
    return lax.ppermute(array, "section", [(i, (i + by) % sections) for i in range(sections)])


def raised(array, by):
    sections = lax.axis_size("section")
    return lax.ppermute(array, "section", [(i, i + by) for i in range(sections - by)])


def swapped(array, step):
    groups = lax.axis_size("group")
    devices = lax.axis_size("dp")
    bits = devices.bit_length() - 1
    pairs = []
    for p in range(devices):
        for g in range(groups):
            pairs.append((p * groups + g, (p ^ (1 << ((step + g) % bits))) * groups + g))
    return lax.ppermute(array, ("dp", "group"), pairs)


def handed(array, by):
    groups = lax.axis_size("group")
    return lax.ppermute(array, "group", [(i, (i + by) % groups) for i in range(groups)])


def plane_places():
    groups = lax.axis_size("group")
    bits = lax.axis_size("dp").bit_length() - 1
    masks = []
    for g in range(groups):
        order = [0]
        for step in range(bits):
            order = order + [m ^ (1 << ((step + g) % bits)) for m in order]
        masks.append(order)
    masks = jnp.asarray(masks, jnp.int32)
    dp, member = lax.axis_index("dp"), lax.axis_index("group")
    places = []
    for r in range(groups):
        giver = (member + groups - r) % groups
        places.append((dp ^ masks[giver]) * groups + giver)
    return jnp.concatenate(places).astype(jnp.int32)


def local(tokens_in, cotangent, gains, w_qkv, w_out, segments, plan):
    sections = lax.axis_size("section")
    groups = lax.axis_size("group")
    devices = lax.axis_size("dp")
    plane = devices * groups
    section = lax.axis_index("section")
    member = lax.axis_index("group")
    rows_dev = plan.shape[1]
    length = segments.shape[1]
    tokens, width = tokens_in.shape
    head = w_out.shape[1]
    share = rows_dev // groups
    w_layer, out_layer = w_qkv[0], w_out[0]
    place = member.astype(jnp.int32)[None]
    layer = section.astype(jnp.int32)[None]

    slice_rows = head // plane
    mine = lax.axis_index("dp") * groups + member
    own_rows, *parts = pick(
        tokens_in.reshape(rows_dev, length, width),
        plan,
        place,
        groups,
        out_layer,
        mine.astype(jnp.int32)[None],
        slice_rows,
    )
    slices = [own_rows] + [raised(own_rows, r) for r in range(1, sections)]
    chosen = jnp.take(segments, plan[0], axis=0, mode="clip").astype(BF16)
    chosen = chosen.reshape(groups, share, length)
    moved, moved_seg = [], []
    for r in range(groups):
        outgoing = lax.dynamic_index_in_dim(chosen, (member + r) % groups, 0, keepdims=False)
        moved.append(handed(parts[r], r) if r else parts[r])
        moved_seg.append(handed(outgoing, r) if r else outgoing)
    moved = [part.reshape(share * length, width) for part in moved]
    order = (member - jnp.arange(groups)) % groups
    seg = jnp.take(jnp.stack(moved_seg), order, axis=0, mode="clip").reshape(tokens)
    at = jnp.arange(tokens)
    mask = (
        (at[:, None] >= at[None, :])
        & (at[:, None] // length == at[None, :] // length)
        & (seg[:, None] == seg[None, :])
    ).astype(F32)

    x, xz, norms = project(moved, cotangent, gains, w_layer, out_layer, place)

    last = (section == sections - 1).astype(jnp.int32)[None]
    places = plane_places()
    streams = stream_columns(width // CHUNKS)
    bits = devices.bit_length() - 1
    def facing(array, by):
        return lax.ppermute(array, "section", [(i, i ^ by) for i in range(sections)])

    arrays, masks, by = [xz], [0], sections // 2
    while by > 0:
        arrays = arrays + [facing(array, by) for array in arrays]
        masks = masks + [mask_of ^ by for mask_of in masks]
        by = by // 2
    xz_all = [arrays[masks.index(r)] for r in range(sections)]
    early = [xz_all[sections // 2]]
    late = [xz_all[r] for r in range(1, sections) if r != sections // 2]
    coupling, stack = couple(slices, gains, w_layer, out_layer, last, [mask, places] + early)
    others = [shifted(coupling, r) for r in range(1, sections)]
    pieces = [compact([coupling] + others, layer, 3 * head, head, late)]

    rows = [stack[None]]
    for step in range(bits):
        if step > 0:
            pieces = [merge(*pieces, rows[1:])]
        pieces = pieces + [swapped(pieces[0], step)]
        rows = rows + [swapped(array, step) for array in rows]
    pieces = pieces + [handed(array, r) for r in range(1, groups) for array in pieces]
    back, own, total, mixes, *leaving = serial(
        xz_all, pieces, places, norms, mask, layer, gains, w_layer, out_layer, streams
    )
    down = [(i, i - 1) for i in range(1, sections)]
    behind = sections - 1 - section

    def index(tick):
        return jnp.clip(tick - behind, 0, CHUNKS - 1).astype(jnp.int32)[None]

    def lowered(arrays):
        return [lax.ppermute(array, "section", down) for array in arrays]

    arrived = lowered(leaving)
    leaving = [forward(index(1), array, own, cols) for array, cols in zip(arrived, streams)]

    rows = list(hold(rows, leaving))
    rows = rows + [handed(array, r) for r in range(1, groups) for array in rows]
    both, out, gain = settle(
        total, mixes, rows, places, x, cotangent, back, own, index(1), arrived, streams
    )

    def crossed(array, by):
        return lax.ppermute(array, "dp", [(p, p ^ by) for p in range(devices)])

    gain_chip = added([gain] + [crossed(gain, by) for by in range(1, devices)])
    gain_whole = added([gain_chip] + [handed(gain_chip, r) for r in range(1, groups)])
    gain_whole = gain_whole.reshape(1, width)

    ticks = CHUNKS + sections - 1
    for tick in range(2, ticks):
        arrived = lowered(leaving)
        after = {ticks - 3: [gain_chip], ticks - 2: [gain_whole]}.get(tick, [])
        if tick < ticks - 1:
            for i, cols in enumerate(streams):
                leaving[i], out = join(index(tick), arrived[i], both, out, cols, after)
    out = finish(index(ticks - 1), arrived, both, out, streams)
    return (out[None], gain_whole)


def attend(hidden, segment, gain_row, w_layer, out_layer):
    count, length, width = hidden.shape
    head = out_layer.shape[0]
    scaled = hidden * lax.rsqrt(jnp.mean(hidden * hidden, axis=-1, keepdims=True) + EPS) * gain_row
    normed = scaled.astype(BF16).reshape(count * length, width)
    projected = jnp.dot(normed, w_layer, preferred_element_type=F32).reshape(count, length, 3 * head)
    query = projected[:, :, :head]
    keyed = projected[:, :, head : 2 * head]
    valued = projected[:, :, 2 * head :]
    positions = jnp.arange(length)
    allowed = (positions[:, None] >= positions[None, :])[None] & (
        segment[:, :, None] == segment[:, None, :]
    )
    scores = jnp.einsum("rid,rjd->rij", query, keyed, precision=lax.Precision.HIGHEST)
    scores = jnp.where(allowed, scores / math.sqrt(head), -1e30)
    weights = jax.nn.softmax(scores, axis=-1)
    mixed = jnp.einsum("rij,rjd->rid", weights, valued, precision=lax.Precision.HIGHEST)
    mixed = mixed.astype(BF16).reshape(count * length, head)
    output = jnp.dot(mixed, out_layer, preferred_element_type=F32).reshape(count, length, width)
    return hidden + output


MB_ROWS = 2


def relay(tokens_in, cotangent, gains, w_qkv, w_out, segments, plan):
    sections = lax.axis_size("section")
    section = lax.axis_index("section")
    rows_dev = plan.shape[1]
    width = tokens_in.shape[1]
    length = segments.shape[1]
    micro = rows_dev // MB_ROWS
    blocks = tokens_in.reshape(rows_dev, length, width)
    chosen = jnp.take(blocks, plan[0], axis=0)
    chosen_seg = jnp.take(segments, plan[0], axis=0).astype(BF16)
    assigned = lax.all_to_all(chosen, "group", split_axis=0, concat_axis=0, tiled=True)
    moved_seg = lax.all_to_all(chosen_seg, "group", split_axis=0, concat_axis=0, tiled=True)
    assigned = assigned.reshape(micro, MB_ROWS, length, width)
    seg_groups = moved_seg.reshape(micro, MB_ROWS, length)
    gain_row, w_layer, out_layer = gains[0], w_qkv[0], w_out[0]
    grad_rows = cotangent.reshape(micro, MB_ROWS, length, width)
    ticks = micro + sections - 1

    def passed_along(array, by):
        pairs = [(i, i + by) for i in range(sections) if 0 <= i + by < sections]
        return lax.ppermute(array, "section", pairs)

    def at(array, i):
        return lax.dynamic_index_in_dim(array, i, 0, keepdims=False)

    def forward_tick(tick, carry):
        saved, arrived = carry
        index = tick - section
        valid = (index >= 0) & (index < micro)
        clipped = jnp.clip(index, 0, micro - 1)
        entering = jnp.where(section == 0, at(assigned, clipped), arrived)
        kept = jnp.where(valid, entering, at(saved, clipped))
        saved = lax.dynamic_update_index_in_dim(saved, kept, clipped, 0)
        segment = at(seg_groups, clipped)

        def run_layer(value):
            return attend(value.astype(F32), segment, gain_row, w_layer, out_layer).astype(BF16)

        leaving = lax.cond(valid, run_layer, jnp.zeros_like, entering)
        return (saved, passed_along(leaving, 1))

    saved_init = jnp.zeros((micro, MB_ROWS, length, width), BF16)
    arrive_init = jnp.zeros((MB_ROWS, length, width), BF16)
    saved, _ = lax.fori_loop(0, ticks, forward_tick, (saved_init, arrive_init))

    def backward_tick(tick, carry):
        grads_x, gain_total, arrived = carry
        index = tick - (sections - 1 - section)
        valid = (index >= 0) & (index < micro)
        clipped = jnp.clip(index, 0, micro - 1)
        entering = jnp.where(section == sections - 1, at(grad_rows, clipped), arrived)
        segment = at(seg_groups, clipped)
        stored = at(saved, clipped).astype(F32)

        def local_layer(hidden, gains_here):
            return attend(hidden, segment, gains_here, w_layer, out_layer)

        def run_back(value):
            _, pullback = jax.vjp(local_layer, stored, gain_row)
            grad_hidden, grad_gain = pullback(value.astype(F32))
            return (grad_hidden.astype(BF16), grad_gain)

        def skip_back(value):
            return (jnp.zeros_like(value), jnp.zeros(gain_row.shape, F32))

        sending, grad_gain = lax.cond(valid, run_back, skip_back, entering)
        kept = jnp.where(valid, sending, at(grads_x, clipped))
        grads_x = lax.dynamic_update_index_in_dim(grads_x, kept, clipped, 0)
        return (grads_x, gain_total + grad_gain, passed_along(sending, -1))

    gain_init = jnp.zeros(gain_row.shape, F32)
    grads_x, gain_total, _ = lax.fori_loop(
        0, ticks, backward_tick, (saved_init, gain_init, arrive_init)
    )
    gain_whole = lax.psum(gain_total, ("dp", "group"))
    return (grads_x.reshape(1, rows_dev * length, width), gain_whole[None])


def solution(mesh):
    placed = (
        P(("dp", "group"), None),
        P(("dp", "group"), None),
        P("section", None),
        P("section", None, None),
        P("section", None, None),
        P(("dp", "group"), None),
        P(("dp", "group"), None),
    )

    def chosen(tokens_in, cotangent, gains, w_qkv, w_out, segments, plan):
        sections, head, width = w_out.shape
        devices = mesh.shape["dp"]
        small = sections * 4 * head < width and sections > 1
        halves = devices & (devices - 1) == 0 and sections & (sections - 1) == 0
        body = local if small and halves else relay
        return jax.shard_map(
            body,
            mesh=mesh,
            in_specs=placed,
            out_specs=(P("section", ("dp", "group"), None), P("section", None)),
            check_vma=False,
        )(tokens_in, cotangent, gains, w_qkv, w_out, segments, plan)

    return chosen
```

```python
import math

import jax
import jax.numpy as jnp
from jax import lax
from jax.experimental import pallas as pl
from jax.experimental.pallas import tpu as pltpu
from jax.sharding import PartitionSpec as P

EPS = 1e-05
VMEM_BYTES = 24 * 1024 * 1024
SMALL = 16 * 1024 * 1024
F32 = jnp.float32
BF16 = jnp.bfloat16


def dot_nn(a, b):
    return lax.dot_general(a, b, (((1,), (0,)), ((), ())), preferred_element_type=F32)


def dot_nt(a, b):
    return lax.dot_general(a, b, (((1,), (1,)), ((), ())), preferred_element_type=F32)


def dot_tn(a, b):
    return lax.dot_general(a, b, (((0,), (0,)), ((), ())), preferred_element_type=F32)


IN_HBM = pl.BlockSpec(memory_space=pltpu.HBM)
ANYWHERE = pl.BlockSpec(memory_space=pl.ANY)
IN_VMEM = pl.BlockSpec(memory_space=pltpu.VMEM)
IN_SMEM = pl.BlockSpec(memory_space=pltpu.SMEM)


def in_hbm(array):
    return pltpu.with_memory_space_constraint(array, pltpu.HBM)


def in_vmem(array):
    return pltpu.with_memory_space_constraint(array, pltpu.VMEM)


def mover(sems):
    used = []

    def start(source, target):
        copy = pltpu.make_async_copy(source, target, sems.at[len(used)])
        copy.start()
        used.append(copy)
        return copy

    return start


def steps(width):
    step = min(width, 1024)
    return [slice(at, at + step) for at in range(0, width, step)]


def params(limit=VMEM_BYTES):
    return pltpu.CompilerParams(vmem_limit_bytes=limit)


def pick(tokens, plan, place, groups, out_layer, mine, slice_rows):
    rows, length, width = tokens.shape
    share = rows // groups

    def kernel(plan_ref, place_ref, mine_ref, tokens_ref, o_ref, *rest):
        slice_ref, parts = rest[0], rest[1 : 1 + groups]
        slice_in, rows_in, sems = rest[1 + groups :]
        start = mover(sems)
        at = pl.ds(pl.multiple_of(mine_ref[0] * slice_rows, slice_rows), slice_rows)
        loads = [(start(o_ref.at[at], slice_in), slice_in, slice_ref)]
        for r in range(groups):
            target = lax.rem(place_ref[0] + r, groups)
            for c in range(share):
                here = rows_in.at[r * share + c]
                row = plan_ref[0, target * share + c]
                loads.append((start(tokens_ref.at[row], here), here, parts[r].at[c]))
        stores = []
        for load, here, there in loads:
            load.wait()
            stores.append(start(here, there))
        for store in stores:
            store.wait()

    return pl.pallas_call(
        kernel,
        out_shape=[pltpu.HBM((slice_rows, width), BF16)]
        + [pltpu.HBM((share, length, width), BF16)] * groups,
        in_specs=[IN_SMEM, IN_SMEM, IN_SMEM, IN_HBM, IN_HBM],
        out_specs=[IN_HBM] * (1 + groups),
        scratch_shapes=[
            pltpu.VMEM((slice_rows, width), BF16),
            pltpu.VMEM((rows, length, width), BF16),
            pltpu.SemaphoreType.DMA((2 * rows + 2,)),
        ],
        compiler_params=params(),
        name="pick",
    )(plan, place, mine, in_hbm(tokens), in_hbm(out_layer))


def project(parts, cotangent, gain, w_layer, out_layer, place):
    groups = len(parts)
    tokens, width = cotangent.shape
    head = out_layer.shape[0]
    wide = w_layer.shape[1]
    block = tokens // groups
    cuts = steps(width)
    copies = len(cuts) * (groups + 4)

    def kernel(place_ref, *refs):
        part_refs = refs[:groups]
        cot_ref, g_ref, w_ref, o_ref, x_ref, xz_ref, n_ref = refs[groups : groups + 7]
        x_in, c_in, w_in, o_in, sems = refs[groups + 7 :]
        start = mover(sems)
        loads = []
        for cut in cuts:
            mine = [start(w_ref.at[cut], w_in.at[cut])]
            mine.append(start(o_ref.at[:, cut], o_in.at[:, cut]))
            for r in range(groups):
                source = lax.rem(place_ref[0] + groups - r, groups)
                rows = pl.ds(pl.multiple_of(source * block, block), block)
                mine.append(start(part_refs[r].at[:, cut], x_in.at[rows, cut]))
            mine.append(start(cot_ref.at[:, cut], c_in.at[:, cut]))
            loads.append(mine)
        through = jnp.zeros((tokens, wide), F32)
        across = jnp.zeros((tokens, head), F32)
        back = jnp.zeros((tokens, head), F32)
        square = jnp.zeros((tokens, 1), F32)
        stores = []
        for cut, mine in zip(cuts, loads):
            for load in mine:
                load.wait()
            stores.append(start(x_in.at[:, cut], x_ref.at[:, cut]))
            x = x_in[:, cut]
            xf = x.astype(F32)
            through += dot_nn((xf * g_ref[:, cut]).astype(BF16), w_in[cut, :])
            across += dot_nt(x, o_in[:, cut])
            back += dot_nt(c_in[:, cut], o_in[:, cut])
            square += jnp.sum(xf * xf, axis=1, keepdims=True)
        xz_ref[:, :wide] = through.astype(BF16)
        xz_ref[:, wide : wide + head] = across.astype(BF16)
        xz_ref[:, wide + head :] = back.astype(BF16)
        n_ref[...] = square
        for store in stores:
            store.wait()

    return pl.pallas_call(
        kernel,
        out_shape=[
            pltpu.HBM((tokens, width), BF16),
            jax.ShapeDtypeStruct((tokens, wide + 2 * head), BF16),
            jax.ShapeDtypeStruct((tokens, 1), F32),
        ],
        in_specs=[IN_SMEM] + [ANYWHERE] * groups + [IN_HBM, IN_VMEM, IN_HBM, IN_HBM],
        out_specs=[IN_HBM, IN_VMEM, IN_VMEM],
        scratch_shapes=[
            pltpu.VMEM((tokens, width), BF16),
            pltpu.VMEM((tokens, width), BF16),
            pltpu.VMEM((width, wide), BF16),
            pltpu.VMEM((head, width), BF16),
            pltpu.SemaphoreType.DMA((copies,)),
        ],
        compiler_params=params(),
        name="project",
    )(
        place,
        *parts,
        in_hbm(cotangent),
        gain,
        in_hbm(w_layer),
        in_hbm(out_layer),
    )


def couple(slices, gain, w_layer, out_layer, last, after):
    sections = len(slices)
    count, width = slices[0].shape
    head = out_layer.shape[0]
    wide = w_layer.shape[1]
    below = (sections - 2) * wide
    packed = below + max(wide, (sections - 1) * head)
    cuts = steps(width)
    copies = len(cuts) * (sections + 2) + sections - 1

    def kernel(last_ref, *refs):
        s_refs = refs[:sections][::-1]
        g_ref, w_ref, o_ref = refs[sections : sections + 3]
        out_ref, stack_ref, r_in, w_in, o_in, sems = refs[sections + 3 + len(after) :]
        rows = [slice(r * count, (r + 1) * count) for r in range(sections)]
        start = mover(sems)
        loads = []
        for cut in cuts:
            mine = [start(w_ref.at[cut], w_in.at[cut])]
            mine.append(start(o_ref.at[:, cut], o_in.at[:, cut]))
            for r in range(sections):
                mine.append(start(s_refs[r].at[:, cut], r_in.at[rows[r], cut]))
            loads.append(mine)
        through = jnp.zeros((sections * count, wide), F32)
        across = jnp.zeros((sections * count, head), F32)
        for cut, mine in zip(cuts, loads):
            for load in mine:
                load.wait()
            r = r_in[:, cut]
            through += dot_nn((r.astype(F32) * g_ref[:, cut]).astype(BF16), w_in[cut, :])
            across += dot_nt(r, o_in[:, cut])
        stores = [start(r_in.at[rows[r]], stack_ref.at[r - 1]) for r in range(1, sections)]
        through = through.astype(BF16)
        across = across.astype(BF16)
        out_ref[...] = jnp.zeros_like(out_ref)
        for r in range(1, sections - 1):
            out_ref[:, (r - 1) * wide : r * wide] = through[rows[r]]

        @pl.when(last_ref[0] == 1)
        def _():
            out_ref[:, below : below + wide] = through[rows[-1]]

        @pl.when(last_ref[0] == 0)
        def _():
            for r in range(sections - 1):
                out_ref[:, below + r * head : below + (r + 1) * head] = across[rows[r]]

        for store in stores:
            store.wait()

    return pl.pallas_call(
        kernel,
        out_shape=[
            jax.ShapeDtypeStruct((count, packed), BF16),
            pltpu.HBM((sections - 1, count, width), BF16),
        ],
        in_specs=[IN_SMEM]
        + [ANYWHERE] * sections
        + [IN_VMEM, IN_HBM, IN_HBM]
        + [ANYWHERE] * len(after),
        out_specs=[IN_VMEM, IN_HBM],
        scratch_shapes=[
            pltpu.VMEM((sections * count, width), BF16),
            pltpu.VMEM((width, wide), BF16),
            pltpu.VMEM((head, width), BF16),
            pltpu.SemaphoreType.DMA((copies,)),
        ],
        compiler_params=params(),
        name="couple",
    )(last, *slices[::-1], gain, in_hbm(w_layer), in_hbm(out_layer), *after)


def layout(sections, wide, head):
    through, across, at = {}, {}, 0
    for k in range(sections):
        for j in range(k):
            through[j, k] = slice(at, at + wide)
            at += wide
        for j in range(k + 1 if k < sections - 1 else 0):
            across[j, k] = slice(at, at + head)
            at += head
    return through, across, at


def compact(parts, section, wide, head, after):
    sections = len(parts)
    count = parts[0].shape[0]
    below = (sections - 2) * wide
    through, across, total = layout(sections, wide, head)

    def kernel(s_ref, *refs):
        part_refs, out_ref = refs[:sections], refs[-1]
        mine = s_ref[0]

        def fill(k, r):
            for j in range(k):
                at = (k - j - 1) * wide
                out_ref[0, :, through[j, k]] = part_refs[r][:, at : at + wide]
            for j in range(k + 1 if k < sections - 1 else 0):
                at = below + (k - j) * head
                out_ref[0, :, across[j, k]] = part_refs[r][:, at : at + head]

        for s in range(sections):

            @pl.when(mine == s)
            def _(s=s):
                for r in range(sections):
                    fill((s - r) % sections, r)

    vmem = pl.BlockSpec(memory_space=pltpu.VMEM)
    return pl.pallas_call(
        kernel,
        out_shape=jax.ShapeDtypeStruct((1, count, total), BF16),
        in_specs=[IN_SMEM] + [vmem] * sections + [ANYWHERE] * len(after),
        out_specs=vmem,
        compiler_params=params(SMALL),
        name="compact",
    )(section, *parts, *after)


def merge(first, second, after):
    count = first.shape[0]

    def kernel(first_ref, second_ref, *refs):
        refs[-1][:count] = first_ref[...]
        refs[-1][count:] = second_ref[...]

    return pl.pallas_call(
        kernel,
        out_shape=jax.ShapeDtypeStruct((2 * count,) + first.shape[1:], first.dtype),
        in_specs=[IN_VMEM] * 2 + [ANYWHERE] * len(after),
        out_specs=IN_VMEM,
        compiler_params=params(SMALL),
        name="merge",
    )(first, second, *after)


def serial(xz, pieces, places, norms, mask, section, gain, w_layer, out_layer, streams):
    sections = len(xz)
    tokens = norms.shape[0]
    head, width = out_layer.shape
    wide = 3 * head
    scale = 1.0 / math.sqrt(head)
    chunk = streams[-1].stop
    cuts = [slice(at, at + chunk) for at in range(0, width, chunk)]
    through_at, across_at, _ = layout(sections, wide, head)
    count, packed = pieces[0].shape[-2:]
    plane = head // count
    n_in = sections + len(pieces)
    copies = sections + plane + 3 * len(cuts)

    def kernel(s_ref, p_ref, *refs):
        xz_refs, piece_refs = refs[:sections], refs[sections:n_in]
        n_ref, mask_ref, g_ref, w_ref, o_ref = refs[n_in : n_in + 5]
        n_out = n_in + 5
        back_ref, b_ref, t_ref, a_ref = refs[n_out : n_out + 4]
        first_refs = refs[n_out + 4 : n_out + 4 + len(streams)]
        scratch = refs[n_out + 4 + len(streams) :]
        xz_all, table, mixes, weights, projs, dmix, v_ref, back_in, w_in, o_in, sems = scratch
        mine = s_ref[0]
        started = []

        def start(source, target):
            copy = pltpu.make_async_copy(source, target, sems.at[len(started)])
            copy.start()
            started.append(copy)

        for r in range(sections):
            start(xz_refs[r], xz_all.at[mine ^ r])
        at = 0
        for ref in piece_refs:
            for i in range(ref.shape[0]):
                start(ref.at[i], table.at[p_ref[at]])
                at += 1
        small = list(started)
        for cut in cuts:
            start(w_ref.at[cut], w_in.at[cut])
            start(o_ref.at[:, cut], o_in.at[:, cut])
        large = started[len(small) :]
        for copy in small:
            copy.wait()

        def through(j, k):
            return table[:, :, through_at[j, k]].reshape(head, wide)

        def across(j, k):
            return table[:, :, across_at[j, k]].reshape(head, head)

        allowed = mask_ref[...] > 0.5
        norm = n_ref[...]
        rstds, tails, mixed = [], [], []
        for s in range(sections):
            proj = xz_all[s, :, :wide].astype(F32)
            for j in range(s):
                proj = proj + dot_nn(mixed[j], through(j, s))
            rstd = lax.rsqrt(norm * (1.0 / width) + EPS)
            proj = proj * rstd
            projs[s] = proj.astype(BF16)
            q, k, v = (projs[s, :, i * head : (i + 1) * head] for i in range(3))
            scores = jnp.where(allowed, dot_nt(q, k) * scale, -1e30)
            scores = jnp.exp(scores - jnp.max(scores, axis=1, keepdims=True))
            soft = scores / jnp.sum(scores, axis=1, keepdims=True)
            weights[s] = soft
            mix = dot_nn(soft.astype(BF16), v).astype(BF16)
            mixed.append(mix)
            mixes[:, s * head : (s + 1) * head] = mix
            rstds.append(rstd)
            dmix[:, s * head : (s + 1) * head] = xz_all[s, :, wide + head :].astype(F32)
            if s == sections - 1:
                break
            y = xz_all[s, :, wide : wide + head].astype(F32)
            for j in range(s):
                y = y + dot_nn(mixed[j], across(j, s))
            tail = y + dot_nn(mix, across(s, s))
            norm = norm + jnp.sum(mix.astype(F32) * (y + tail), axis=1, keepdims=True)
            norm = jnp.maximum(norm, 0.0)
            tails.append(tail)
        total = jnp.zeros((tokens, 1), F32)
        a_ref[...] = jnp.zeros_like(a_ref)
        for s in reversed(range(sections)):
            cols = slice(s * head, (s + 1) * head)
            da = dmix[:, cols]
            if s < sections - 1:
                da = da - total * tails[s]
            da = da.astype(BF16)
            q, k, v = (projs[s, :, i * head : (i + 1) * head] for i in range(3))
            soft = weights[s]
            dv = dot_tn(soft.astype(BF16), da)
            dsoft = dot_nt(da, v)
            dscore = soft * (dsoft - jnp.sum(dsoft * soft, axis=1, keepdims=True))
            dscore = (dscore * scale).astype(BF16)
            dproj = jnp.concatenate([dot_nn(dscore, k), dot_tn(dscore, q), dv], axis=1)
            along = jnp.sum(dproj * projs[s].astype(F32), axis=1, keepdims=True)
            first = (dproj * rstds[s]).astype(BF16)
            second = (-total * mixes[:, cols].astype(F32)).astype(BF16)
            total = total + rstds[s] * rstds[s] * along * (1.0 / width)
            for j in reversed(range(s)):
                term = dot_nt(first, through(j, s))
                if s < sections - 1:
                    term = term + dot_nt(second, across(j, s))
                dmix[:, j * head : (j + 1) * head] += term

            @pl.when(mine == s)
            def _(first=first, second=second, total=total):
                v_ref[:, :wide] = first
                v_ref[:, wide:] = second
                t_ref[...] = total

            for r in range(1, sections - s):

                @pl.when(mine == s + r)
                def _(r=r, cols=cols):
                    a_ref[:, (r - 1) * head : r * head] = mixes[:, cols]

        for i, cut in enumerate(cuts):
            large[2 * i].wait()
            large[2 * i + 1].wait()
            back = dot_nt(v_ref[:, :wide], w_in[cut, :])
            own = back * g_ref[:, cut] + dot_nn(v_ref[:, wide:], o_in[:, cut])
            own = own.astype(BF16)
            back_in[:, cut] = back.astype(BF16)
            start(back_in.at[:, cut], back_ref.at[:, cut])
            b_ref[0, i] = own
            b_ref[1, i] = jnp.zeros_like(own)
            if i == 0:
                for ref, part in zip(first_refs, streams):
                    ref[...] = own[:, part]
        for copy in started[len(small) + len(large) :]:
            copy.wait()

    vmem = pl.BlockSpec(memory_space=pltpu.VMEM)
    smem = pl.BlockSpec(memory_space=pltpu.SMEM)
    return pl.pallas_call(
        kernel,
        out_shape=[
            pltpu.HBM((tokens, width), BF16),
            pltpu.VMEM((2, len(cuts), tokens, chunk), BF16),
            pltpu.VMEM((tokens, 1), F32),
            pltpu.VMEM((tokens, (sections - 1) * head), BF16),
        ]
        + [pltpu.VMEM((tokens, part.stop - part.start), BF16) for part in streams],
        in_specs=[smem, smem] + [ANYWHERE] * n_in + [vmem, vmem, vmem, IN_HBM, IN_HBM],
        out_specs=[IN_HBM] + [vmem] * (3 + len(streams)),
        scratch_shapes=[
            pltpu.VMEM((sections,) + xz[0].shape, BF16),
            pltpu.VMEM((plane, count, packed), BF16),
            pltpu.VMEM((tokens, sections * head), BF16),
            pltpu.VMEM((sections, tokens, tokens), F32),
            pltpu.VMEM((sections, tokens, wide), BF16),
            pltpu.VMEM((tokens, sections * head), F32),
            pltpu.VMEM((tokens, wide + head), BF16),
            pltpu.VMEM((tokens, width), BF16),
            pltpu.VMEM((width, wide), BF16),
            pltpu.VMEM((head, width), BF16),
            pltpu.SemaphoreType.DMA((copies,)),
        ],
        compiler_params=params(),
        name="serial",
    )(
        section,
        places,
        *xz,
        *pieces,
        norms,
        mask,
        gain,
        in_hbm(w_layer),
        in_hbm(out_layer),
    )


def hold(arrays, after):
    def kernel(*refs):
        pass

    return pl.pallas_call(
        kernel,
        out_shape=[pltpu.HBM(array.shape, array.dtype) for array in arrays],
        in_specs=[IN_HBM] * len(arrays) + [ANYWHERE] * len(after),
        out_specs=[IN_HBM] * len(arrays),
        input_output_aliases={i: i for i in range(len(arrays))},
        compiler_params=params(SMALL),
        name="hold",
    )(*[in_hbm(array) for array in arrays], *after)


def settle(total, mixes, stacks, places, x, cotangent, back, chunk):
    tokens, width = x.shape
    layers, rows = stacks[0].shape[1:3]
    entries = [(i, e) for i, stack in enumerate(stacks) for e in range(stack.shape[0])]
    plane = len(entries)
    head = plane * rows
    cuts = [slice(at, at + chunk) for at in range(0, width, chunk)]
    copies = plane * layers + 3 * len(cuts)

    def kernel(p_ref, t_ref, a_ref, x_ref, c_ref, back_ref, *refs):
        stack_refs = refs[: len(stacks)]
        rest_ref, dg_ref = refs[len(stacks) : len(stacks) + 2]
        lower, x_in, c_in, back_in, sems = refs[len(stacks) + 2 :]
        start = mover(sems)
        first = []
        for at, (i, e) in enumerate(entries):
            for r in range(layers):
                first.append(start(stack_refs[i].at[e, r], lower.at[r, p_ref[at]]))
        loads = []
        for cut in cuts:
            mine = [start(x_ref.at[:, cut], x_in.at[:, cut])]
            mine.append(start(c_ref.at[:, cut], c_in.at[:, cut]))
            mine.append(start(back_ref.at[:, cut], back_in.at[:, cut]))
            loads.append(mine)
        for load in first:
            load.wait()
        for i, (cut, mine) in enumerate(zip(cuts, loads)):
            for load in mine:
                load.wait()
            below = lower[:, :, :, cut].reshape(layers * head, chunk)
            here = x_in[:, cut].astype(F32) + dot_nn(a_ref[...], below)
            rest_ref[i] = c_in[:, cut].astype(F32) - t_ref[...] * here
            gain = jnp.sum(back_in[:, cut].astype(F32) * here, axis=0, keepdims=True)
            for at in range(0, chunk, head):
                row = (cut.start + at) // head
                dg_ref[row : row + 1, :] = gain[:, at : at + head]

    return pl.pallas_call(
        kernel,
        out_shape=[
            pltpu.VMEM((len(cuts), tokens, chunk), F32),
            pltpu.VMEM((width // head, head), F32),
        ],
        in_specs=[IN_SMEM] + [IN_VMEM] * 2 + [IN_HBM] * (3 + len(stacks)),
        out_specs=[IN_VMEM] * 2,
        scratch_shapes=[
            pltpu.VMEM((layers, plane, rows, width), BF16),
            pltpu.VMEM((tokens, width), BF16),
            pltpu.VMEM((tokens, width), BF16),
            pltpu.VMEM((tokens, width), BF16),
            pltpu.SemaphoreType.DMA((copies,)),
        ],
        compiler_params=params(),
        name="settle",
    )(
        places,
        in_vmem(total),
        in_vmem(mixes),
        *[in_hbm(array) for array in (x, cotangent, back, *stacks)],
    )


def join(index, arrived, pair, cols, after):
    tokens, part = arrived.shape

    def kernel(i_ref, r_ref, _, *refs):
        send_ref, pair_ref = refs[len(after) :]
        at = i_ref[0]
        r = r_ref[...]
        send_ref[...] = (pair_ref[0, at, :, cols].astype(F32) + r.astype(F32)).astype(BF16)
        pair_ref[1, at, :, cols] = r

    return pl.pallas_call(
        kernel,
        out_shape=[pltpu.VMEM((tokens, part), BF16), pltpu.VMEM(pair.shape, BF16)],
        in_specs=[IN_SMEM] + [IN_VMEM] * 2 + [ANYWHERE] * len(after),
        out_specs=[IN_VMEM] * 2,
        input_output_aliases={2: 1},
        compiler_params=params(SMALL),
        name="join",
    )(index, in_vmem(arrived), in_vmem(pair), *after)


def finish(index, arrived, pair, rest, streams):
    _, count, tokens, chunk = pair.shape

    def kernel(i_ref, *refs):
        r_refs = refs[: len(streams)]
        pair_ref, rest_ref, whole_ref, whole, sems = refs[len(streams) :]
        at = i_ref[0]
        copies = []
        for i in range(count):
            full = rest_ref[i] + pair_ref[0, i].astype(F32)
            whole[i] = (full + pair_ref[1, i].astype(F32)).astype(BF16)

            @pl.when(at == i)
            def _(i=i, full=full):
                for ref, cols in zip(r_refs, streams):
                    whole[i, :, cols] = (full[:, cols] + ref[...].astype(F32)).astype(BF16)

            there = whole_ref.at[:, pl.ds(i * chunk, chunk)]
            copies.append(pltpu.make_async_copy(whole.at[i], there, sems.at[i]))
            copies[-1].start()
        for copy in copies:
            copy.wait()

    return pl.pallas_call(
        kernel,
        out_shape=pltpu.HBM((tokens, count * chunk), BF16),
        in_specs=[IN_SMEM] + [IN_VMEM] * (len(streams) + 2),
        out_specs=IN_HBM,
        scratch_shapes=[
            pltpu.VMEM((count, tokens, chunk), BF16),
            pltpu.SemaphoreType.DMA((count,)),
        ],
        compiler_params=params(SMALL),
        name="finish",
    )(index, *[in_vmem(array) for array in arrived], in_vmem(pair), in_vmem(rest))


def added(arrays):
    def kernel(*refs):
        total = refs[0][...]
        for ref in refs[1:-1]:
            total = total + ref[...]
        refs[-1][...] = total

    return pl.pallas_call(
        kernel,
        out_shape=pltpu.VMEM(arrays[0].shape, F32),
        in_specs=[IN_VMEM] * len(arrays),
        out_specs=IN_VMEM,
        compiler_params=params(SMALL),
        name="added",
    )(*[in_vmem(array) for array in arrays])


STREAMS = 2
CHUNKS = 4


def stream_columns(chunk):
    lanes = 128
    tiles = chunk // lanes
    ends = [-(-tiles * (i + 1) // STREAMS) * lanes for i in range(STREAMS)]
    return [slice(start, end) for start, end in zip([0] + ends, ends)]


def shifted(array, by):
    sections = lax.axis_size("section")
    return lax.ppermute(array, "section", [(i, (i + by) % sections) for i in range(sections)])


def raised(array, by):
    sections = lax.axis_size("section")
    return lax.ppermute(array, "section", [(i, i + by) for i in range(sections - by)])


def swapped(array, step):
    groups = lax.axis_size("group")
    devices = lax.axis_size("dp")
    bits = devices.bit_length() - 1
    pairs = []
    for p in range(devices):
        for g in range(groups):
            pairs.append((p * groups + g, (p ^ (1 << ((step + g) % bits))) * groups + g))
    return lax.ppermute(array, ("dp", "group"), pairs)


def handed(array, by):
    groups = lax.axis_size("group")
    return lax.ppermute(array, "group", [(i, (i + by) % groups) for i in range(groups)])


def plane_places():
    groups = lax.axis_size("group")
    bits = lax.axis_size("dp").bit_length() - 1
    masks = []
    for g in range(groups):
        order = [0]
        for step in range(bits):
            order = order + [m ^ (1 << ((step + g) % bits)) for m in order]
        masks.append(order)
    masks = jnp.asarray(masks, jnp.int32)
    dp, member = lax.axis_index("dp"), lax.axis_index("group")
    places = []
    for r in range(groups):
        giver = (member + groups - r) % groups
        places.append((dp ^ masks[giver]) * groups + giver)
    return jnp.concatenate(places).astype(jnp.int32)


def local(tokens_in, cotangent, gains, w_qkv, w_out, segments, plan):
    sections = lax.axis_size("section")
    groups = lax.axis_size("group")
    devices = lax.axis_size("dp")
    plane = devices * groups
    section = lax.axis_index("section")
    member = lax.axis_index("group")
    rows_dev = plan.shape[1]
    length = segments.shape[1]
    tokens, width = tokens_in.shape
    head = w_out.shape[1]
    share = rows_dev // groups
    w_layer, out_layer = w_qkv[0], w_out[0]
    place = member.astype(jnp.int32)[None]
    layer = section.astype(jnp.int32)[None]

    slice_rows = head // plane
    mine = lax.axis_index("dp") * groups + member
    own_rows, *parts = pick(
        tokens_in.reshape(rows_dev, length, width),
        plan,
        place,
        groups,
        out_layer,
        mine.astype(jnp.int32)[None],
        slice_rows,
    )
    slices = [raised(own_rows, r) for r in range(sections - 1, 0, -1)]
    slices = [own_rows] + slices[::-1]
    chosen = jnp.take(segments, plan[0], axis=0, mode="clip").astype(BF16)
    chosen = chosen.reshape(groups, share, length)
    moved, moved_seg = [], []
    for r in range(groups):
        outgoing = lax.dynamic_index_in_dim(chosen, (member + r) % groups, 0, keepdims=False)
        moved.append(handed(parts[r], r) if r else parts[r])
        moved_seg.append(handed(outgoing, r) if r else outgoing)
    moved = [part.reshape(share * length, width) for part in moved]
    order = (member - jnp.arange(groups)) % groups
    seg = jnp.take(jnp.stack(moved_seg), order, axis=0, mode="clip").reshape(tokens)
    at = jnp.arange(tokens)
    mask = (
        (at[:, None] >= at[None, :])
        & (at[:, None] // length == at[None, :] // length)
        & (seg[:, None] == seg[None, :])
    ).astype(F32)

    x, xz, norms = project(moved, cotangent, gains, w_layer, out_layer, place)

    last = (section == sections - 1).astype(jnp.int32)[None]
    places = plane_places()
    streams = stream_columns(width // CHUNKS)
    bits = devices.bit_length() - 1
    def facing(array, by):
        return lax.ppermute(array, "section", [(i, i ^ by) for i in range(sections)])

    arrays, masks, by = [xz], [0], sections // 2
    while by > 0:
        arrays = arrays + [facing(array, by) for array in arrays]
        masks = masks + [mask_of ^ by for mask_of in masks]
        by = by // 2
    xz_all = [arrays[masks.index(r)] for r in range(sections)]
    early = [xz_all[r] for r in range(1, sections) if r & (r - 1) == 0]
    late = [xz_all[r] for r in range(1, sections) if r & (r - 1) != 0]
    coupling, stack = couple(slices, gains, w_layer, out_layer, last, [mask, places] + early)
    others = [shifted(coupling, r) for r in range(1, sections)]
    pieces = [compact([coupling] + others, layer, 3 * head, head, late)]

    rows = [stack[None]]
    for step in range(bits):
        if step > 0:
            pieces = [merge(*pieces, rows[1:])]
        pieces = pieces + [swapped(pieces[0], step)]
        rows = rows + [swapped(array, step) for array in rows]
    pieces = pieces + [handed(array, r) for r in range(1, groups) for array in pieces]
    back, pair, total, mixes, *leaving = serial(
        xz_all, pieces, places, norms, mask, layer, gains, w_layer, out_layer, streams
    )
    down = [(i, i - 1) for i in range(1, sections)]
    behind = sections - 1 - section

    def index(tick):
        return jnp.clip(tick - behind, 0, CHUNKS - 1).astype(jnp.int32)[None]

    def lowered(arrays):
        return [lax.ppermute(array, "section", down) for array in arrays]

    rows = list(hold(rows, [total]))
    rows = rows + [handed(array, r) for r in range(1, groups) for array in rows]
    rest, gain = settle(total, mixes, rows, places, x, cotangent, back, width // CHUNKS)

    def crossed(array, by):
        return lax.ppermute(array, "dp", [(p, p ^ by) for p in range(devices)])

    gain_chip = added([gain] + [crossed(gain, by) for by in range(1, devices)])
    gain_whole = added([gain_chip] + [handed(gain_chip, r) for r in range(1, groups)])
    gain_whole = gain_whole.reshape(1, width)

    ticks = CHUNKS + sections - 1
    for tick in range(1, ticks):
        arrived = lowered(leaving)
        after = {ticks - 3: [gain_chip], ticks - 2: [gain_whole]}.get(tick, [])
        if tick < ticks - 1:
            for i, cols in enumerate(streams):
                leaving[i], pair = join(index(tick), arrived[i], pair, cols, after)
    out = finish(index(ticks - 1), arrived, pair, rest, streams)
    return (out[None], gain_whole)


def attend(hidden, segment, gain_row, w_layer, out_layer):
    count, length, width = hidden.shape
    head = out_layer.shape[0]
    scaled = hidden * lax.rsqrt(jnp.mean(hidden * hidden, axis=-1, keepdims=True) + EPS) * gain_row
    normed = scaled.astype(BF16).reshape(count * length, width)
    projected = jnp.dot(normed, w_layer, preferred_element_type=F32).reshape(count, length, 3 * head)
    query = projected[:, :, :head]
    keyed = projected[:, :, head : 2 * head]
    valued = projected[:, :, 2 * head :]
    positions = jnp.arange(length)
    allowed = (positions[:, None] >= positions[None, :])[None] & (
        segment[:, :, None] == segment[:, None, :]
    )
    scores = jnp.einsum("rid,rjd->rij", query, keyed, precision=lax.Precision.HIGHEST)
    scores = jnp.where(allowed, scores / math.sqrt(head), -1e30)
    weights = jax.nn.softmax(scores, axis=-1)
    mixed = jnp.einsum("rij,rjd->rid", weights, valued, precision=lax.Precision.HIGHEST)
    mixed = mixed.astype(BF16).reshape(count * length, head)
    output = jnp.dot(mixed, out_layer, preferred_element_type=F32).reshape(count, length, width)
    return hidden + output


MB_ROWS = 2


def relay(tokens_in, cotangent, gains, w_qkv, w_out, segments, plan):
    sections = lax.axis_size("section")
    section = lax.axis_index("section")
    rows_dev = plan.shape[1]
    width = tokens_in.shape[1]
    length = segments.shape[1]
    micro = rows_dev // MB_ROWS
    blocks = tokens_in.reshape(rows_dev, length, width)
    chosen = jnp.take(blocks, plan[0], axis=0)
    chosen_seg = jnp.take(segments, plan[0], axis=0).astype(BF16)
    assigned = lax.all_to_all(chosen, "group", split_axis=0, concat_axis=0, tiled=True)
    moved_seg = lax.all_to_all(chosen_seg, "group", split_axis=0, concat_axis=0, tiled=True)
    assigned = assigned.reshape(micro, MB_ROWS, length, width)
    seg_groups = moved_seg.reshape(micro, MB_ROWS, length)
    gain_row, w_layer, out_layer = gains[0], w_qkv[0], w_out[0]
    grad_rows = cotangent.reshape(micro, MB_ROWS, length, width)
    ticks = micro + sections - 1

    def passed_along(array, by):
        pairs = [(i, i + by) for i in range(sections) if 0 <= i + by < sections]
        return lax.ppermute(array, "section", pairs)

    def at(array, i):
        return lax.dynamic_index_in_dim(array, i, 0, keepdims=False)

    def forward_tick(tick, carry):
        saved, arrived = carry
        index = tick - section
        valid = (index >= 0) & (index < micro)
        clipped = jnp.clip(index, 0, micro - 1)
        entering = jnp.where(section == 0, at(assigned, clipped), arrived)
        kept = jnp.where(valid, entering, at(saved, clipped))
        saved = lax.dynamic_update_index_in_dim(saved, kept, clipped, 0)
        segment = at(seg_groups, clipped)

        def run_layer(value):
            return attend(value.astype(F32), segment, gain_row, w_layer, out_layer).astype(BF16)

        leaving = lax.cond(valid, run_layer, jnp.zeros_like, entering)
        return (saved, passed_along(leaving, 1))

    saved_init = jnp.zeros((micro, MB_ROWS, length, width), BF16)
    arrive_init = jnp.zeros((MB_ROWS, length, width), BF16)
    saved, _ = lax.fori_loop(0, ticks, forward_tick, (saved_init, arrive_init))

    def backward_tick(tick, carry):
        grads_x, gain_total, arrived = carry
        index = tick - (sections - 1 - section)
        valid = (index >= 0) & (index < micro)
        clipped = jnp.clip(index, 0, micro - 1)
        entering = jnp.where(section == sections - 1, at(grad_rows, clipped), arrived)
        segment = at(seg_groups, clipped)
        stored = at(saved, clipped).astype(F32)

        def local_layer(hidden, gains_here):
            return attend(hidden, segment, gains_here, w_layer, out_layer)

        def run_back(value):
            _, pullback = jax.vjp(local_layer, stored, gain_row)
            grad_hidden, grad_gain = pullback(value.astype(F32))
            return (grad_hidden.astype(BF16), grad_gain)

        def skip_back(value):
            return (jnp.zeros_like(value), jnp.zeros(gain_row.shape, F32))

        sending, grad_gain = lax.cond(valid, run_back, skip_back, entering)
        kept = jnp.where(valid, sending, at(grads_x, clipped))
        grads_x = lax.dynamic_update_index_in_dim(grads_x, kept, clipped, 0)
        return (grads_x, gain_total + grad_gain, passed_along(sending, -1))

    gain_init = jnp.zeros(gain_row.shape, F32)
    grads_x, gain_total, _ = lax.fori_loop(
        0, ticks, backward_tick, (saved_init, gain_init, arrive_init)
    )
    gain_whole = lax.psum(gain_total, ("dp", "group"))
    return (grads_x.reshape(1, rows_dev * length, width), gain_whole[None])


def solution(mesh):
    placed = (
        P(("dp", "group"), None),
        P(("dp", "group"), None),
        P("section", None),
        P("section", None, None),
        P("section", None, None),
        P(("dp", "group"), None),
        P(("dp", "group"), None),
    )

    def chosen(tokens_in, cotangent, gains, w_qkv, w_out, segments, plan):
        sections, head, width = w_out.shape
        devices = mesh.shape["dp"]
        small = sections * 4 * head < width and sections > 1
        halves = devices & (devices - 1) == 0 and sections & (sections - 1) == 0
        body = local if small and halves else relay
        return jax.shard_map(
            body,
            mesh=mesh,
            in_specs=placed,
            out_specs=(P("section", ("dp", "group"), None), P("section", None)),
            check_vma=False,
        )(tokens_in, cotangent, gains, w_qkv, w_out, segments, plan)

    return chosen
```

```python
import math

import jax
import jax.numpy as jnp
from jax import lax
from jax.experimental import pallas as pl
from jax.experimental.pallas import tpu as pltpu
from jax.sharding import PartitionSpec as P

EPS = 1e-05
VMEM_BYTES = 24 * 1024 * 1024
SMALL = 16 * 1024 * 1024
F32 = jnp.float32
BF16 = jnp.bfloat16


def dot_nn(a, b):
    return lax.dot_general(a, b, (((1,), (0,)), ((), ())), preferred_element_type=F32)


def dot_nt(a, b):
    return lax.dot_general(a, b, (((1,), (1,)), ((), ())), preferred_element_type=F32)


def dot_tn(a, b):
    return lax.dot_general(a, b, (((0,), (0,)), ((), ())), preferred_element_type=F32)


IN_HBM = pl.BlockSpec(memory_space=pltpu.HBM)
ANYWHERE = pl.BlockSpec(memory_space=pl.ANY)
IN_VMEM = pl.BlockSpec(memory_space=pltpu.VMEM)
IN_SMEM = pl.BlockSpec(memory_space=pltpu.SMEM)


def in_hbm(array):
    return pltpu.with_memory_space_constraint(array, pltpu.HBM)


def in_vmem(array):
    return pltpu.with_memory_space_constraint(array, pltpu.VMEM)


def mover(sems):
    used = []

    def start(source, target):
        copy = pltpu.make_async_copy(source, target, sems.at[len(used)])
        copy.start()
        used.append(copy)
        return copy

    return start


def steps(width):
    step = min(width, 1024)
    return [slice(at, at + step) for at in range(0, width, step)]


def params(limit=VMEM_BYTES):
    return pltpu.CompilerParams(vmem_limit_bytes=limit)


def pick(tokens, plan, place, groups, out_layer, mine, slice_rows):
    rows, length, width = tokens.shape
    share = rows // groups

    def kernel(plan_ref, place_ref, mine_ref, tokens_ref, o_ref, *rest):
        slice_ref, parts = rest[0], rest[1 : 1 + groups]
        slice_in, rows_in, sems = rest[1 + groups :]
        start = mover(sems)
        at = pl.ds(pl.multiple_of(mine_ref[0] * slice_rows, slice_rows), slice_rows)
        loads = [(start(o_ref.at[at], slice_in), slice_in, slice_ref)]
        for r in range(groups):
            target = lax.rem(place_ref[0] + r, groups)
            for c in range(share):
                here = rows_in.at[r * share + c]
                row = plan_ref[0, target * share + c]
                loads.append((start(tokens_ref.at[row], here), here, parts[r].at[c]))
        stores = []
        for load, here, there in loads:
            load.wait()
            stores.append(start(here, there))
        for store in stores:
            store.wait()

    return pl.pallas_call(
        kernel,
        out_shape=[pltpu.HBM((slice_rows, width), BF16)]
        + [pltpu.HBM((share, length, width), BF16)] * groups,
        in_specs=[IN_SMEM, IN_SMEM, IN_SMEM, IN_HBM, IN_HBM],
        out_specs=[IN_HBM] * (1 + groups),
        scratch_shapes=[
            pltpu.VMEM((slice_rows, width), BF16),
            pltpu.VMEM((rows, length, width), BF16),
            pltpu.SemaphoreType.DMA((2 * rows + 2,)),
        ],
        compiler_params=params(),
        name="pick",
    )(plan, place, mine, in_hbm(tokens), in_hbm(out_layer))


def project(parts, cotangent, gain, w_layer, out_layer, place):
    groups = len(parts)
    tokens, width = cotangent.shape
    head = out_layer.shape[0]
    wide = w_layer.shape[1]
    block = tokens // groups
    cuts = steps(width)
    copies = len(cuts) * (groups + 4)

    def kernel(place_ref, *refs):
        part_refs = refs[:groups]
        cot_ref, g_ref, w_ref, o_ref, x_ref, xz_ref, n_ref = refs[groups : groups + 7]
        x_in, c_in, w_in, o_in, sems = refs[groups + 7 :]
        start = mover(sems)
        loads = []
        for cut in cuts:
            mine = [start(w_ref.at[cut], w_in.at[cut])]
            mine.append(start(o_ref.at[:, cut], o_in.at[:, cut]))
            for r in range(groups):
                source = lax.rem(place_ref[0] + groups - r, groups)
                rows = pl.ds(pl.multiple_of(source * block, block), block)
                mine.append(start(part_refs[r].at[:, cut], x_in.at[rows, cut]))
            mine.append(start(cot_ref.at[:, cut], c_in.at[:, cut]))
            loads.append(mine)
        through = jnp.zeros((tokens, wide), F32)
        across = jnp.zeros((tokens, head), F32)
        back = jnp.zeros((tokens, head), F32)
        square = jnp.zeros((tokens, 1), F32)
        stores = []
        for cut, mine in zip(cuts, loads):
            for load in mine:
                load.wait()
            stores.append(start(x_in.at[:, cut], x_ref.at[:, cut]))
            x = x_in[:, cut]
            xf = x.astype(F32)
            through += dot_nn((xf * g_ref[:, cut]).astype(BF16), w_in[cut, :])
            across += dot_nt(x, o_in[:, cut])
            back += dot_nt(c_in[:, cut], o_in[:, cut])
            square += jnp.sum(xf * xf, axis=1, keepdims=True)
        xz_ref[:, :wide] = through.astype(BF16)
        xz_ref[:, wide : wide + head] = across.astype(BF16)
        xz_ref[:, wide + head :] = back.astype(BF16)
        n_ref[...] = square
        for store in stores:
            store.wait()

    return pl.pallas_call(
        kernel,
        out_shape=[
            pltpu.HBM((tokens, width), BF16),
            jax.ShapeDtypeStruct((tokens, wide + 2 * head), BF16),
            jax.ShapeDtypeStruct((tokens, 1), F32),
        ],
        in_specs=[IN_SMEM] + [ANYWHERE] * groups + [IN_HBM, IN_VMEM, IN_HBM, IN_HBM],
        out_specs=[IN_HBM, IN_VMEM, IN_VMEM],
        scratch_shapes=[
            pltpu.VMEM((tokens, width), BF16),
            pltpu.VMEM((tokens, width), BF16),
            pltpu.VMEM((width, wide), BF16),
            pltpu.VMEM((head, width), BF16),
            pltpu.SemaphoreType.DMA((copies,)),
        ],
        compiler_params=params(),
        name="project",
    )(
        place,
        *parts,
        in_hbm(cotangent),
        gain,
        in_hbm(w_layer),
        in_hbm(out_layer),
    )


def couple(slices, gain, w_layer, out_layer, last, after):
    sections = len(slices)
    count, width = slices[0].shape
    head = out_layer.shape[0]
    wide = w_layer.shape[1]
    below = (sections - 2) * wide
    packed = below + max(wide, (sections - 1) * head)
    cuts = steps(width)
    copies = len(cuts) * (sections + 2) + sections - 1

    def kernel(last_ref, *refs):
        s_refs = refs[:sections][::-1]
        g_ref, w_ref, o_ref = refs[sections : sections + 3]
        out_ref, stack_ref, r_in, w_in, o_in, sems = refs[sections + 3 + len(after) :]
        rows = [slice(r * count, (r + 1) * count) for r in range(sections)]
        start = mover(sems)
        loads = []
        for cut in cuts:
            mine = [start(w_ref.at[cut], w_in.at[cut])]
            mine.append(start(o_ref.at[:, cut], o_in.at[:, cut]))
            for r in range(sections):
                mine.append(start(s_refs[r].at[:, cut], r_in.at[rows[r], cut]))
            loads.append(mine)
        through = jnp.zeros((sections * count, wide), F32)
        across = jnp.zeros((sections * count, head), F32)
        for cut, mine in zip(cuts, loads):
            for load in mine:
                load.wait()
            r = r_in[:, cut]
            through += dot_nn((r.astype(F32) * g_ref[:, cut]).astype(BF16), w_in[cut, :])
            across += dot_nt(r, o_in[:, cut])
        stores = [start(r_in.at[rows[r]], stack_ref.at[r - 1]) for r in range(1, sections)]
        through = through.astype(BF16)
        across = across.astype(BF16)
        out_ref[...] = jnp.zeros_like(out_ref)
        for r in range(1, sections - 1):
            out_ref[:, (r - 1) * wide : r * wide] = through[rows[r]]

        @pl.when(last_ref[0] == 1)
        def _():
            out_ref[:, below : below + wide] = through[rows[-1]]

        @pl.when(last_ref[0] == 0)
        def _():
            for r in range(sections - 1):
                out_ref[:, below + r * head : below + (r + 1) * head] = across[rows[r]]

        for store in stores:
            store.wait()

    return pl.pallas_call(
        kernel,
        out_shape=[
            jax.ShapeDtypeStruct((count, packed), BF16),
            pltpu.HBM((sections - 1, count, width), BF16),
        ],
        in_specs=[IN_SMEM]
        + [ANYWHERE] * sections
        + [IN_VMEM, IN_HBM, IN_HBM]
        + [ANYWHERE] * len(after),
        out_specs=[IN_VMEM, IN_HBM],
        scratch_shapes=[
            pltpu.VMEM((sections * count, width), BF16),
            pltpu.VMEM((width, wide), BF16),
            pltpu.VMEM((head, width), BF16),
            pltpu.SemaphoreType.DMA((copies,)),
        ],
        compiler_params=params(),
        name="couple",
    )(last, *slices[::-1], gain, in_hbm(w_layer), in_hbm(out_layer), *after)


def layout(sections, wide, head):
    through, across, at = {}, {}, 0
    for k in range(sections):
        for j in range(k):
            through[j, k] = slice(at, at + wide)
            at += wide
        for j in range(k + 1 if k < sections - 1 else 0):
            across[j, k] = slice(at, at + head)
            at += head
    return through, across, at


def compact(parts, section, wide, head, after):
    sections = len(parts)
    count = parts[0].shape[0]
    below = (sections - 2) * wide
    through, across, total = layout(sections, wide, head)

    def kernel(s_ref, *refs):
        part_refs, out_ref = refs[:sections], refs[-1]
        mine = s_ref[0]

        def fill(k, r):
            for j in range(k):
                at = (k - j - 1) * wide
                out_ref[0, :, through[j, k]] = part_refs[r][:, at : at + wide]
            for j in range(k + 1 if k < sections - 1 else 0):
                at = below + (k - j) * head
                out_ref[0, :, across[j, k]] = part_refs[r][:, at : at + head]

        for s in range(sections):

            @pl.when(mine == s)
            def _(s=s):
                for r in range(sections):
                    fill((s - r) % sections, r)

    vmem = pl.BlockSpec(memory_space=pltpu.VMEM)
    return pl.pallas_call(
        kernel,
        out_shape=jax.ShapeDtypeStruct((1, count, total), BF16),
        in_specs=[IN_SMEM] + [vmem] * sections + [ANYWHERE] * len(after),
        out_specs=vmem,
        compiler_params=params(SMALL),
        name="compact",
    )(section, *parts, *after)


def merge(first, second, after):
    count = first.shape[0]

    def kernel(first_ref, second_ref, *refs):
        refs[-1][:count] = first_ref[...]
        refs[-1][count:] = second_ref[...]

    return pl.pallas_call(
        kernel,
        out_shape=jax.ShapeDtypeStruct((2 * count,) + first.shape[1:], first.dtype),
        in_specs=[IN_VMEM] * 2 + [ANYWHERE] * len(after),
        out_specs=IN_VMEM,
        compiler_params=params(SMALL),
        name="merge",
    )(first, second, *after)


def serial(xz, pieces, places, norms, mask, section, gain, w_layer, out_layer, streams):
    sections = len(xz)
    tokens = norms.shape[0]
    head, width = out_layer.shape
    wide = 3 * head
    scale = 1.0 / math.sqrt(head)
    chunk = streams[-1].stop
    cuts = [slice(at, at + chunk) for at in range(0, width, chunk)]
    through_at, across_at, _ = layout(sections, wide, head)
    count, packed = pieces[0].shape[-2:]
    plane = head // count
    n_in = sections + len(pieces)
    copies = sections + plane + 3 * len(cuts)

    def kernel(s_ref, p_ref, *refs):
        xz_refs, piece_refs = refs[:sections], refs[sections:n_in]
        n_ref, mask_ref, g_ref, w_ref, o_ref = refs[n_in : n_in + 5]
        n_out = n_in + 5
        back_ref, b_ref, t_ref, a_ref = refs[n_out : n_out + 4]
        first_refs = refs[n_out + 4 : n_out + 4 + len(streams)]
        scratch = refs[n_out + 4 + len(streams) :]
        xz_all, table, mixes, weights, projs, dmix, v_ref, back_in, w_in, o_in, sems = scratch
        mine = s_ref[0]
        started = []

        def start(source, target):
            copy = pltpu.make_async_copy(source, target, sems.at[len(started)])
            copy.start()
            started.append(copy)

        for r in range(sections):
            start(xz_refs[r], xz_all.at[mine ^ r])
        at = 0
        for ref in piece_refs:
            for i in range(ref.shape[0]):
                start(ref.at[i], table.at[p_ref[at]])
                at += 1
        small = list(started)
        for cut in cuts:
            start(w_ref.at[cut], w_in.at[cut])
            start(o_ref.at[:, cut], o_in.at[:, cut])
        large = started[len(small) :]
        for copy in small:
            copy.wait()

        def through(j, k):
            return table[:, :, through_at[j, k]].reshape(head, wide)

        def across(j, k):
            return table[:, :, across_at[j, k]].reshape(head, head)

        allowed = mask_ref[...] > 0.5
        norm = n_ref[...]
        rstds, tails, mixed = [], [], []
        for s in range(sections):
            proj = xz_all[s, :, :wide].astype(F32)
            for j in range(s):
                proj = proj + dot_nn(mixed[j], through(j, s))
            rstd = lax.rsqrt(norm * (1.0 / width) + EPS)
            proj = proj * rstd
            projs[s] = proj.astype(BF16)
            q, k, v = (projs[s, :, i * head : (i + 1) * head] for i in range(3))
            scores = jnp.where(allowed, dot_nt(q, k) * scale, -1e30)
            scores = jnp.exp(scores - jnp.max(scores, axis=1, keepdims=True))
            soft = scores / jnp.sum(scores, axis=1, keepdims=True)
            weights[s] = soft
            mix = dot_nn(soft.astype(BF16), v).astype(BF16)
            mixed.append(mix)
            mixes[:, s * head : (s + 1) * head] = mix
            rstds.append(rstd)
            dmix[:, s * head : (s + 1) * head] = xz_all[s, :, wide + head :].astype(F32)
            if s == sections - 1:
                break
            y = xz_all[s, :, wide : wide + head].astype(F32)
            for j in range(s):
                y = y + dot_nn(mixed[j], across(j, s))
            tail = y + dot_nn(mix, across(s, s))
            norm = norm + jnp.sum(mix.astype(F32) * (y + tail), axis=1, keepdims=True)
            norm = jnp.maximum(norm, 0.0)
            tails.append(tail)
        total = jnp.zeros((tokens, 1), F32)
        a_ref[...] = jnp.zeros_like(a_ref)
        for s in reversed(range(sections)):
            cols = slice(s * head, (s + 1) * head)
            da = dmix[:, cols]
            if s < sections - 1:
                da = da - total * tails[s]
            da = da.astype(BF16)
            q, k, v = (projs[s, :, i * head : (i + 1) * head] for i in range(3))
            soft = weights[s]
            dv = dot_tn(soft.astype(BF16), da)
            dsoft = dot_nt(da, v)
            dscore = soft * (dsoft - jnp.sum(dsoft * soft, axis=1, keepdims=True))
            dscore = (dscore * scale).astype(BF16)
            dproj = jnp.concatenate([dot_nn(dscore, k), dot_tn(dscore, q), dv], axis=1)
            along = jnp.sum(dproj * projs[s].astype(F32), axis=1, keepdims=True)
            first = (dproj * rstds[s]).astype(BF16)
            second = (-total * mixes[:, cols].astype(F32)).astype(BF16)
            total = total + rstds[s] * rstds[s] * along * (1.0 / width)
            for j in reversed(range(s)):
                term = dot_nt(first, through(j, s))
                if s < sections - 1:
                    term = term + dot_nt(second, across(j, s))
                dmix[:, j * head : (j + 1) * head] += term

            @pl.when(mine == s)
            def _(first=first, second=second, total=total):
                v_ref[:, :wide] = first
                v_ref[:, wide:] = second
                t_ref[...] = total

            for r in range(1, sections - s):

                @pl.when(mine == s + r)
                def _(r=r, cols=cols):
                    a_ref[:, (r - 1) * head : r * head] = mixes[:, cols]

        for i, cut in enumerate(cuts):
            large[2 * i].wait()
            large[2 * i + 1].wait()
            back = dot_nt(v_ref[:, :wide], w_in[cut, :])
            own = back * g_ref[:, cut] + dot_nn(v_ref[:, wide:], o_in[:, cut])
            own = own.astype(BF16)
            back_in[:, cut] = back.astype(BF16)
            start(back_in.at[:, cut], back_ref.at[:, cut])
            b_ref[0, i] = own
            b_ref[1, i] = jnp.zeros_like(own)
            if i == 0:
                for ref, part in zip(first_refs, streams):
                    ref[...] = own[:, part]
        for copy in started[len(small) + len(large) :]:
            copy.wait()

    vmem = pl.BlockSpec(memory_space=pltpu.VMEM)
    smem = pl.BlockSpec(memory_space=pltpu.SMEM)
    return pl.pallas_call(
        kernel,
        out_shape=[
            pltpu.HBM((tokens, width), BF16),
            pltpu.VMEM((2, len(cuts), tokens, chunk), BF16),
            pltpu.VMEM((tokens, 1), F32),
            pltpu.VMEM((tokens, (sections - 1) * head), BF16),
        ]
        + [pltpu.VMEM((tokens, part.stop - part.start), BF16) for part in streams],
        in_specs=[smem, smem] + [ANYWHERE] * n_in + [vmem, vmem, vmem, IN_HBM, IN_HBM],
        out_specs=[IN_HBM] + [vmem] * (3 + len(streams)),
        scratch_shapes=[
            pltpu.VMEM((sections,) + xz[0].shape, BF16),
            pltpu.VMEM((plane, count, packed), BF16),
            pltpu.VMEM((tokens, sections * head), BF16),
            pltpu.VMEM((sections, tokens, tokens), F32),
            pltpu.VMEM((sections, tokens, wide), BF16),
            pltpu.VMEM((tokens, sections * head), F32),
            pltpu.VMEM((tokens, wide + head), BF16),
            pltpu.VMEM((tokens, width), BF16),
            pltpu.VMEM((width, wide), BF16),
            pltpu.VMEM((head, width), BF16),
            pltpu.SemaphoreType.DMA((copies,)),
        ],
        compiler_params=params(),
        name="serial",
    )(
        section,
        places,
        *xz,
        *pieces,
        norms,
        mask,
        gain,
        in_hbm(w_layer),
        in_hbm(out_layer),
    )


def gather_two(first, second, after):
    count = first.shape[0]

    def kernel(first_ref, second_ref, *refs):
        out_ref, sems = refs[len(after) :]
        start = mover(sems)
        copies = [start(first_ref, out_ref.at[:count]), start(second_ref, out_ref.at[count:])]
        for copy in copies:
            copy.wait()

    return pl.pallas_call(
        kernel,
        out_shape=jax.ShapeDtypeStruct((2 * count,) + first.shape[1:], first.dtype),
        in_specs=[ANYWHERE] * (2 + len(after)),
        out_specs=IN_VMEM,
        scratch_shapes=[pltpu.SemaphoreType.DMA((2,))],
        compiler_params=params(SMALL),
        name="gather_two",
    )(first, second, *after)


def settle(total, mixes, stacks, places, x, cotangent, back, chunk):
    tokens, width = x.shape
    layers, rows = stacks[0].shape[1:3]
    entries = [(i, e) for i, stack in enumerate(stacks) for e in range(stack.shape[0])]
    plane = len(entries)
    head = plane * rows
    cuts = [slice(at, at + chunk) for at in range(0, width, chunk)]
    copies = plane * layers + 3 * len(cuts)

    def kernel(p_ref, t_ref, a_ref, x_ref, c_ref, back_ref, *refs):
        stack_refs = refs[: len(stacks)]
        rest_ref, dg_ref = refs[len(stacks) : len(stacks) + 2]
        lower, x_in, c_in, back_in, sems = refs[len(stacks) + 2 :]
        start = mover(sems)
        first = []
        for at, (i, e) in enumerate(entries):
            for r in range(layers):
                first.append(start(stack_refs[i].at[e, r], lower.at[r, p_ref[at]]))
        loads = []
        for cut in cuts:
            mine = [start(x_ref.at[:, cut], x_in.at[:, cut])]
            mine.append(start(c_ref.at[:, cut], c_in.at[:, cut]))
            mine.append(start(back_ref.at[:, cut], back_in.at[:, cut]))
            loads.append(mine)
        for load in first:
            load.wait()
        for i, (cut, mine) in enumerate(zip(cuts, loads)):
            for load in mine:
                load.wait()
            below = lower[:, :, :, cut].reshape(layers * head, chunk)
            here = x_in[:, cut].astype(F32) + dot_nn(a_ref[...], below)
            rest_ref[i] = (c_in[:, cut].astype(F32) - t_ref[...] * here).astype(BF16)
            gain = jnp.sum(back_in[:, cut].astype(F32) * here, axis=0, keepdims=True)
            for at in range(0, chunk, head):
                row = (cut.start + at) // head
                dg_ref[row : row + 1, :] = gain[:, at : at + head]

    return pl.pallas_call(
        kernel,
        out_shape=[
            pltpu.VMEM((len(cuts), tokens, chunk), BF16),
            pltpu.VMEM((width // head, head), F32),
        ],
        in_specs=[IN_SMEM] + [IN_VMEM] * 2 + [IN_HBM] * (3 + len(stacks)),
        out_specs=[IN_VMEM] * 2,
        scratch_shapes=[
            pltpu.VMEM((layers, plane, rows, width), BF16),
            pltpu.VMEM((tokens, width), BF16),
            pltpu.VMEM((tokens, width), BF16),
            pltpu.VMEM((tokens, width), BF16),
            pltpu.SemaphoreType.DMA((copies,)),
        ],
        compiler_params=params(),
        name="settle",
    )(
        places,
        in_vmem(total),
        in_vmem(mixes),
        *[in_hbm(array) for array in (x, cotangent, back, *stacks)],
    )


def join(index, arrived, pair, cols, after):
    tokens, part = arrived.shape

    def kernel(i_ref, r_ref, _, *refs):
        send_ref, pair_ref = refs[len(after) :]
        at = i_ref[0]
        r = r_ref[...]
        send_ref[...] = (pair_ref[0, at, :, cols].astype(F32) + r.astype(F32)).astype(BF16)
        pair_ref[1, at, :, cols] = r

    return pl.pallas_call(
        kernel,
        out_shape=[pltpu.VMEM((tokens, part), BF16), pltpu.VMEM(pair.shape, BF16)],
        in_specs=[IN_SMEM] + [IN_VMEM] * 2 + [ANYWHERE] * len(after),
        out_specs=[IN_VMEM] * 2,
        input_output_aliases={2: 1},
        compiler_params=params(SMALL),
        name="join",
    )(index, in_vmem(arrived), in_vmem(pair), *after)


def finish(index, arrived, pair, rest, streams):
    _, count, tokens, chunk = pair.shape

    def kernel(i_ref, *refs):
        r_refs = refs[: len(streams)]
        pair_ref, rest_ref, whole_ref, whole, sems = refs[len(streams) :]
        at = i_ref[0]
        copies = []
        for i in range(count):
            full = rest_ref[i].astype(F32) + pair_ref[0, i].astype(F32)
            whole[i] = (full + pair_ref[1, i].astype(F32)).astype(BF16)

            @pl.when(at == i)
            def _(i=i, full=full):
                for ref, cols in zip(r_refs, streams):
                    whole[i, :, cols] = (full[:, cols] + ref[...].astype(F32)).astype(BF16)

            there = whole_ref.at[:, pl.ds(i * chunk, chunk)]
            copies.append(pltpu.make_async_copy(whole.at[i], there, sems.at[i]))
            copies[-1].start()
        for copy in copies:
            copy.wait()

    return pl.pallas_call(
        kernel,
        out_shape=pltpu.HBM((tokens, count * chunk), BF16),
        in_specs=[IN_SMEM] + [IN_VMEM] * (len(streams) + 2),
        out_specs=IN_HBM,
        scratch_shapes=[
            pltpu.VMEM((count, tokens, chunk), BF16),
            pltpu.SemaphoreType.DMA((count,)),
        ],
        compiler_params=params(SMALL),
        name="finish",
    )(index, *[in_vmem(array) for array in arrived], in_vmem(pair), in_vmem(rest))


def added(arrays):
    def kernel(*refs):
        total = refs[0][...]
        for ref in refs[1:-1]:
            total = total + ref[...]
        refs[-1][...] = total

    return pl.pallas_call(
        kernel,
        out_shape=pltpu.VMEM(arrays[0].shape, F32),
        in_specs=[IN_VMEM] * len(arrays),
        out_specs=IN_VMEM,
        compiler_params=params(SMALL),
        name="added",
    )(*[in_vmem(array) for array in arrays])


STREAMS = 2
CHUNKS = 4


def stream_columns(chunk):
    lanes = 128
    tiles = chunk // lanes
    ends = [-(-tiles * (i + 1) // STREAMS) * lanes for i in range(STREAMS)]
    return [slice(start, end) for start, end in zip([0] + ends, ends)]


def shifted(array, by):
    sections = lax.axis_size("section")
    return lax.ppermute(array, "section", [(i, (i + by) % sections) for i in range(sections)])


def raised(array, by):
    sections = lax.axis_size("section")
    return lax.ppermute(array, "section", [(i, i + by) for i in range(sections - by)])


def swapped(array, step):
    groups = lax.axis_size("group")
    devices = lax.axis_size("dp")
    bits = devices.bit_length() - 1
    pairs = []
    for p in range(devices):
        for g in range(groups):
            pairs.append((p * groups + g, (p ^ (1 << ((step + g) % bits))) * groups + g))
    return lax.ppermute(array, ("dp", "group"), pairs)


def handed(array, by):
    groups = lax.axis_size("group")
    return lax.ppermute(array, "group", [(i, (i + by) % groups) for i in range(groups)])


def plane_places():
    groups = lax.axis_size("group")
    bits = lax.axis_size("dp").bit_length() - 1
    masks = []
    for g in range(groups):
        order = [0]
        for step in range(bits):
            order = order + [m ^ (1 << ((step + g) % bits)) for m in order]
        masks.append(order)
    masks = jnp.asarray(masks, jnp.int32)
    dp, member = lax.axis_index("dp"), lax.axis_index("group")
    places = []
    for r in range(groups):
        giver = (member + groups - r) % groups
        places.append((dp ^ masks[giver]) * groups + giver)
    return jnp.concatenate(places).astype(jnp.int32)


def local(tokens_in, cotangent, gains, w_qkv, w_out, segments, plan):
    sections = lax.axis_size("section")
    groups = lax.axis_size("group")
    devices = lax.axis_size("dp")
    plane = devices * groups
    section = lax.axis_index("section")
    member = lax.axis_index("group")
    rows_dev = plan.shape[1]
    length = segments.shape[1]
    tokens, width = tokens_in.shape
    head = w_out.shape[1]
    share = rows_dev // groups
    w_layer, out_layer = w_qkv[0], w_out[0]
    place = member.astype(jnp.int32)[None]
    layer = section.astype(jnp.int32)[None]

    slice_rows = head // plane
    mine = lax.axis_index("dp") * groups + member
    own_rows, *parts = pick(
        tokens_in.reshape(rows_dev, length, width),
        plan,
        place,
        groups,
        out_layer,
        mine.astype(jnp.int32)[None],
        slice_rows,
    )
    slices = [raised(own_rows, r) for r in range(sections - 1, 0, -1)]
    slices = [own_rows] + slices[::-1]
    chosen = jnp.take(segments, plan[0], axis=0, mode="clip").astype(BF16)
    chosen = chosen.reshape(groups, share, length)
    moved, moved_seg = [], []
    for r in range(groups):
        outgoing = lax.dynamic_index_in_dim(chosen, (member + r) % groups, 0, keepdims=False)
        moved.append(handed(parts[r], r) if r else parts[r])
        moved_seg.append(handed(outgoing, r) if r else outgoing)
    moved = [part.reshape(share * length, width) for part in moved]
    order = (member - jnp.arange(groups)) % groups
    seg = jnp.take(jnp.stack(moved_seg), order, axis=0, mode="clip").reshape(tokens)
    at = jnp.arange(tokens)
    mask = (
        (at[:, None] >= at[None, :])
        & (at[:, None] // length == at[None, :] // length)
        & (seg[:, None] == seg[None, :])
    ).astype(F32)

    x, xz, norms = project(moved, cotangent, gains, w_layer, out_layer, place)

    last = (section == sections - 1).astype(jnp.int32)[None]
    places = plane_places()
    streams = stream_columns(width // CHUNKS)
    bits = devices.bit_length() - 1
    def facing(array, by):
        return lax.ppermute(array, "section", [(i, i ^ by) for i in range(sections)])

    arrays, masks, by = [xz], [0], sections // 2
    while by > 0:
        arrays = arrays + [facing(array, by) for array in arrays]
        masks = masks + [mask_of ^ by for mask_of in masks]
        by = by // 2
    xz_all = [arrays[masks.index(r)] for r in range(sections)]
    early = [xz_all[r] for r in range(1, sections) if r & (r - 1) == 0]
    late = [xz_all[r] for r in range(1, sections) if r & (r - 1) != 0]
    coupling, stack = couple(slices, gains, w_layer, out_layer, last, [mask, places] + early)
    others = [shifted(coupling, r) for r in range(1, sections)]
    pieces = [compact([coupling] + others, layer, 3 * head, head, late)]

    rows = [stack[None]]
    for step in range(bits):
        if step > 0:
            pieces = [merge(*pieces, rows[1:])]
        pieces = pieces + [swapped(pieces[0], step)]
        rows = rows + [swapped(array, step) for array in rows]
    pieces = pieces + [handed(array, r) for r in range(1, groups) for array in pieces]
    back, pair, total, mixes, *leaving = serial(
        xz_all, pieces, places, norms, mask, layer, gains, w_layer, out_layer, streams
    )
    down = [(i, i - 1) for i in range(1, sections)]
    behind = sections - 1 - section

    def index(tick):
        return jnp.clip(tick - behind, 0, CHUNKS - 1).astype(jnp.int32)[None]

    def lowered(arrays):
        return [lax.ppermute(array, "section", down) for array in arrays]

    def crossed(array, by):
        return lax.ppermute(array, "dp", [(p, p ^ by) for p in range(devices)])

    ticks = CHUNKS + sections - 1
    after = {}
    for tick in range(1, ticks):
        arrived = lowered(leaving)
        if tick < ticks - 1:
            for i, cols in enumerate(streams):
                leaving[i], pair = join(
                    index(tick), arrived[i], pair, cols, after.get(tick, [])
                )
        if tick == 1:
            while len(rows) > 2:
                rows = [gather_two(*rows[i : i + 2], leaving) for i in range(0, len(rows), 2)]
            rows = rows + [handed(array, r) for r in range(1, groups) for array in rows]
            rest, gain = settle(
                total, mixes, rows, places, x, cotangent, back, width // CHUNKS
            )
            gain_chip = added([gain] + [crossed(gain, by) for by in range(1, devices)])
            gain_whole = added([gain_chip] + [handed(gain_chip, r) for r in range(1, groups)])
            gain_whole = gain_whole.reshape(1, width)
            after = {ticks - 4: [gain], ticks - 3: [gain_chip], ticks - 2: [gain_whole]}
    out = finish(index(ticks - 1), arrived, pair, rest, streams)
    return (out[None], gain_whole)


def attend(hidden, segment, gain_row, w_layer, out_layer):
    count, length, width = hidden.shape
    head = out_layer.shape[0]
    scaled = hidden * lax.rsqrt(jnp.mean(hidden * hidden, axis=-1, keepdims=True) + EPS) * gain_row
    normed = scaled.astype(BF16).reshape(count * length, width)
    projected = jnp.dot(normed, w_layer, preferred_element_type=F32).reshape(count, length, 3 * head)
    query = projected[:, :, :head]
    keyed = projected[:, :, head : 2 * head]
    valued = projected[:, :, 2 * head :]
    positions = jnp.arange(length)
    allowed = (positions[:, None] >= positions[None, :])[None] & (
        segment[:, :, None] == segment[:, None, :]
    )
    scores = jnp.einsum("rid,rjd->rij", query, keyed, precision=lax.Precision.HIGHEST)
    scores = jnp.where(allowed, scores / math.sqrt(head), -1e30)
    weights = jax.nn.softmax(scores, axis=-1)
    mixed = jnp.einsum("rij,rjd->rid", weights, valued, precision=lax.Precision.HIGHEST)
    mixed = mixed.astype(BF16).reshape(count * length, head)
    output = jnp.dot(mixed, out_layer, preferred_element_type=F32).reshape(count, length, width)
    return hidden + output


MB_ROWS = 2


def relay(tokens_in, cotangent, gains, w_qkv, w_out, segments, plan):
    sections = lax.axis_size("section")
    section = lax.axis_index("section")
    rows_dev = plan.shape[1]
    width = tokens_in.shape[1]
    length = segments.shape[1]
    micro = rows_dev // MB_ROWS
    blocks = tokens_in.reshape(rows_dev, length, width)
    chosen = jnp.take(blocks, plan[0], axis=0)
    chosen_seg = jnp.take(segments, plan[0], axis=0).astype(BF16)
    assigned = lax.all_to_all(chosen, "group", split_axis=0, concat_axis=0, tiled=True)
    moved_seg = lax.all_to_all(chosen_seg, "group", split_axis=0, concat_axis=0, tiled=True)
    assigned = assigned.reshape(micro, MB_ROWS, length, width)
    seg_groups = moved_seg.reshape(micro, MB_ROWS, length)
    gain_row, w_layer, out_layer = gains[0], w_qkv[0], w_out[0]
    grad_rows = cotangent.reshape(micro, MB_ROWS, length, width)
    ticks = micro + sections - 1

    def passed_along(array, by):
        pairs = [(i, i + by) for i in range(sections) if 0 <= i + by < sections]
        return lax.ppermute(array, "section", pairs)

    def at(array, i):
        return lax.dynamic_index_in_dim(array, i, 0, keepdims=False)

    def forward_tick(tick, carry):
        saved, arrived = carry
        index = tick - section
        valid = (index >= 0) & (index < micro)
        clipped = jnp.clip(index, 0, micro - 1)
        entering = jnp.where(section == 0, at(assigned, clipped), arrived)
        kept = jnp.where(valid, entering, at(saved, clipped))
        saved = lax.dynamic_update_index_in_dim(saved, kept, clipped, 0)
        segment = at(seg_groups, clipped)

        def run_layer(value):
            return attend(value.astype(F32), segment, gain_row, w_layer, out_layer).astype(BF16)

        leaving = lax.cond(valid, run_layer, jnp.zeros_like, entering)
        return (saved, passed_along(leaving, 1))

    saved_init = jnp.zeros((micro, MB_ROWS, length, width), BF16)
    arrive_init = jnp.zeros((MB_ROWS, length, width), BF16)
    saved, _ = lax.fori_loop(0, ticks, forward_tick, (saved_init, arrive_init))

    def backward_tick(tick, carry):
        grads_x, gain_total, arrived = carry
        index = tick - (sections - 1 - section)
        valid = (index >= 0) & (index < micro)
        clipped = jnp.clip(index, 0, micro - 1)
        entering = jnp.where(section == sections - 1, at(grad_rows, clipped), arrived)
        segment = at(seg_groups, clipped)
        stored = at(saved, clipped).astype(F32)

        def local_layer(hidden, gains_here):
            return attend(hidden, segment, gains_here, w_layer, out_layer)

        def run_back(value):
            _, pullback = jax.vjp(local_layer, stored, gain_row)
            grad_hidden, grad_gain = pullback(value.astype(F32))
            return (grad_hidden.astype(BF16), grad_gain)

        def skip_back(value):
            return (jnp.zeros_like(value), jnp.zeros(gain_row.shape, F32))

        sending, grad_gain = lax.cond(valid, run_back, skip_back, entering)
        kept = jnp.where(valid, sending, at(grads_x, clipped))
        grads_x = lax.dynamic_update_index_in_dim(grads_x, kept, clipped, 0)
        return (grads_x, gain_total + grad_gain, passed_along(sending, -1))

    gain_init = jnp.zeros(gain_row.shape, F32)
    grads_x, gain_total, _ = lax.fori_loop(
        0, ticks, backward_tick, (saved_init, gain_init, arrive_init)
    )
    gain_whole = lax.psum(gain_total, ("dp", "group"))
    return (grads_x.reshape(1, rows_dev * length, width), gain_whole[None])


def solution(mesh):
    placed = (
        P(("dp", "group"), None),
        P(("dp", "group"), None),
        P("section", None),
        P("section", None, None),
        P("section", None, None),
        P(("dp", "group"), None),
        P(("dp", "group"), None),
    )

    def chosen(tokens_in, cotangent, gains, w_qkv, w_out, segments, plan):
        sections, head, width = w_out.shape
        devices = mesh.shape["dp"]
        small = sections * 4 * head < width and sections > 1
        halves = devices & (devices - 1) == 0 and sections & (sections - 1) == 0
        body = local if small and halves else relay
        return jax.shard_map(
            body,
            mesh=mesh,
            in_specs=placed,
            out_specs=(P("section", ("dp", "group"), None), P("section", None)),
            check_vma=False,
        )(tokens_in, cotangent, gains, w_qkv, w_out, segments, plan)

    return chosen
```

```python
import math

import jax
import jax.numpy as jnp
from jax import lax
from jax.experimental import pallas as pl
from jax.experimental.pallas import tpu as pltpu
from jax.sharding import PartitionSpec as P

EPS = 1e-05
VMEM_BYTES = 24 * 1024 * 1024
SMALL = 16 * 1024 * 1024
HOPS = 4
F32 = jnp.float32
BF16 = jnp.bfloat16


def dot_nn(a, b):
    return lax.dot_general(a, b, (((1,), (0,)), ((), ())), preferred_element_type=F32)


def dot_nt(a, b):
    return lax.dot_general(a, b, (((1,), (1,)), ((), ())), preferred_element_type=F32)


def dot_tn(a, b):
    return lax.dot_general(a, b, (((0,), (0,)), ((), ())), preferred_element_type=F32)


IN_HBM = pl.BlockSpec(memory_space=pltpu.HBM)
ANYWHERE = pl.BlockSpec(memory_space=pl.ANY)
IN_VMEM = pl.BlockSpec(memory_space=pltpu.VMEM)
IN_SMEM = pl.BlockSpec(memory_space=pltpu.SMEM)


def in_hbm(array):
    return pltpu.with_memory_space_constraint(array, pltpu.HBM)


def in_vmem(array):
    return pltpu.with_memory_space_constraint(array, pltpu.VMEM)


def mover(sems):
    used = []

    def start(source, target):
        copy = pltpu.make_async_copy(source, target, sems.at[len(used)])
        copy.start()
        used.append(copy)
        return copy

    return start


def steps(width):
    step = min(width, 1024)
    return [slice(at, at + step) for at in range(0, width, step)]


def params(limit=VMEM_BYTES):
    return pltpu.CompilerParams(vmem_limit_bytes=limit)


def pick(tokens, plan, place, groups, out_layer, mine, slice_rows):
    rows, length, width = tokens.shape
    share = rows // groups

    def kernel(plan_ref, place_ref, mine_ref, tokens_ref, o_ref, *rest):
        slice_ref, parts = rest[0], rest[1 : 1 + groups]
        slice_in, rows_in, sems = rest[1 + groups :]
        start = mover(sems)
        at = pl.ds(pl.multiple_of(mine_ref[0] * slice_rows, slice_rows), slice_rows)
        loads = [(start(o_ref.at[at], slice_in), slice_in, slice_ref)]
        for r in range(groups):
            target = lax.rem(place_ref[0] + r, groups)
            for c in range(share):
                here = rows_in.at[r * share + c]
                row = plan_ref[0, target * share + c]
                loads.append((start(tokens_ref.at[row], here), here, parts[r].at[c]))
        stores = []
        for load, here, there in loads:
            load.wait()
            stores.append(start(here, there))
        for store in stores:
            store.wait()

    return pl.pallas_call(
        kernel,
        out_shape=[pltpu.HBM((slice_rows, width), BF16)]
        + [pltpu.HBM((share, length, width), BF16)] * groups,
        in_specs=[IN_SMEM, IN_SMEM, IN_SMEM, IN_HBM, IN_HBM],
        out_specs=[IN_HBM] * (1 + groups),
        scratch_shapes=[
            pltpu.VMEM((slice_rows, width), BF16),
            pltpu.VMEM((rows, length, width), BF16),
            pltpu.SemaphoreType.DMA((2 * rows + 2,)),
        ],
        compiler_params=params(),
        name="pick",
    )(plan, place, mine, in_hbm(tokens), in_hbm(out_layer))


def project(parts, cotangent, gain, w_layer, out_layer, place, after):
    groups = len(parts)
    tokens, width = cotangent.shape
    head = out_layer.shape[0]
    wide = w_layer.shape[1]
    block = tokens // groups
    cuts = steps(width)
    copies = len(cuts) * (groups + 4)

    def kernel(place_ref, *refs):
        part_refs = refs[:groups]
        cot_ref, g_ref, w_ref, o_ref = refs[groups : groups + 4]
        x_ref, xz_ref, n_ref = refs[groups + 4 + len(after) : groups + 7 + len(after)]
        x_in, c_in, w_in, o_in, sems = refs[groups + 7 + len(after) :]
        start = mover(sems)
        loads = []
        for cut in cuts:
            mine = [start(w_ref.at[cut], w_in.at[cut])]
            mine.append(start(o_ref.at[:, cut], o_in.at[:, cut]))
            for r in range(groups):
                source = lax.rem(place_ref[0] + groups - r, groups)
                rows = pl.ds(pl.multiple_of(source * block, block), block)
                mine.append(start(part_refs[r].at[:, cut], x_in.at[rows, cut]))
            mine.append(start(cot_ref.at[:, cut], c_in.at[:, cut]))
            loads.append(mine)
        through = jnp.zeros((tokens, wide), F32)
        across = jnp.zeros((tokens, head), F32)
        back = jnp.zeros((tokens, head), F32)
        square = jnp.zeros((tokens, 1), F32)
        stores = []
        for cut, mine in zip(cuts, loads):
            for load in mine:
                load.wait()
            stores.append(start(x_in.at[:, cut], x_ref.at[:, cut]))
            x = x_in[:, cut]
            xf = x.astype(F32)
            through += dot_nn((xf * g_ref[:, cut]).astype(BF16), w_in[cut, :])
            across += dot_nt(x, o_in[:, cut])
            back += dot_nt(c_in[:, cut], o_in[:, cut])
            square += jnp.sum(xf * xf, axis=1, keepdims=True)
        xz_ref[:, :wide] = through.astype(BF16)
        xz_ref[:, wide : wide + head] = across.astype(BF16)
        xz_ref[:, wide + head :] = back.astype(BF16)
        n_ref[...] = square
        for store in stores:
            store.wait()

    return pl.pallas_call(
        kernel,
        out_shape=[
            pltpu.HBM((tokens, width), BF16),
            jax.ShapeDtypeStruct((tokens, wide + 2 * head), BF16),
            jax.ShapeDtypeStruct((tokens, 1), F32),
        ],
        in_specs=[IN_SMEM]
        + [ANYWHERE] * groups
        + [IN_HBM, IN_VMEM, IN_HBM, IN_HBM]
        + [ANYWHERE] * len(after),
        out_specs=[IN_HBM, IN_VMEM, IN_VMEM],
        scratch_shapes=[
            pltpu.VMEM((tokens, width), BF16),
            pltpu.VMEM((tokens, width), BF16),
            pltpu.VMEM((width, wide), BF16),
            pltpu.VMEM((head, width), BF16),
            pltpu.SemaphoreType.DMA((copies,)),
        ],
        compiler_params=params(),
        name="project",
    )(
        place,
        *parts,
        in_hbm(cotangent),
        gain,
        in_hbm(w_layer),
        in_hbm(out_layer),
        *after,
    )


def slab(gain, w_layer, out_layer, mine, rows, after):
    head, width = out_layer.shape
    wide = w_layer.shape[1]

    def kernel(mine_ref, g_ref, w_ref, o_ref, *refs):
        out_ref, w_in, o_in, sems = refs[len(after) :]
        start = mover(sems)
        here = pl.ds(pl.multiple_of(mine_ref[0] * rows, rows), rows)
        loads = [start(w_ref.at[here], w_in), start(o_ref.at[:, here], o_in)]
        for load in loads:
            load.wait()
        scale = jnp.transpose(jnp.broadcast_to(g_ref[:, here], (8, rows)))[:, :1]
        out_ref[0, :, :wide] = (w_in[...].astype(F32) * scale).astype(BF16)
        out_ref[0, :, wide:] = jnp.transpose(o_in[...].astype(F32)).astype(BF16)

    return pl.pallas_call(
        kernel,
        out_shape=jax.ShapeDtypeStruct((1, rows, wide + head), BF16),
        in_specs=[IN_SMEM, IN_VMEM, IN_HBM, IN_HBM] + [ANYWHERE] * len(after),
        out_specs=IN_VMEM,
        scratch_shapes=[
            pltpu.VMEM((rows, wide), BF16),
            pltpu.VMEM((head, rows), BF16),
            pltpu.SemaphoreType.DMA((2,)),
        ],
        compiler_params=params(),
        name="slab",
    )(mine, gain, in_hbm(w_layer), in_hbm(out_layer), *after)


def couple(slices, gain, w_layer, out_layer, last, after):
    sections = len(slices)
    count, width = slices[0].shape
    head = out_layer.shape[0]
    wide = w_layer.shape[1]
    below = (sections - 2) * wide
    packed = below + max(wide, (sections - 1) * head)
    cuts = steps(width)
    copies = len(cuts) * (sections + 2) + sections - 1

    def kernel(last_ref, *refs):
        s_refs = refs[:sections][::-1]
        g_ref, w_ref, o_ref = refs[sections : sections + 3]
        out_ref, stack_ref, r_in, w_in, o_in, sems = refs[sections + 3 + len(after) :]
        rows = [slice(r * count, (r + 1) * count) for r in range(sections)]
        start = mover(sems)
        loads = []
        for cut in cuts:
            mine = [start(w_ref.at[cut], w_in.at[cut])]
            mine.append(start(o_ref.at[:, cut], o_in.at[:, cut]))
            for r in range(sections):
                mine.append(start(s_refs[r].at[:, cut], r_in.at[rows[r], cut]))
            loads.append(mine)
        through = jnp.zeros((sections * count, wide), F32)
        across = jnp.zeros((sections * count, head), F32)
        for cut, mine in zip(cuts, loads):
            for load in mine:
                load.wait()
            r = r_in[:, cut]
            through += dot_nn((r.astype(F32) * g_ref[:, cut]).astype(BF16), w_in[cut, :])
            across += dot_nt(r, o_in[:, cut])
        stores = [start(r_in.at[rows[r]], stack_ref.at[r - 1]) for r in range(1, sections)]
        through = through.astype(BF16)
        across = across.astype(BF16)
        out_ref[...] = jnp.zeros_like(out_ref)
        for r in range(1, sections - 1):
            out_ref[:, (r - 1) * wide : r * wide] = through[rows[r]]

        @pl.when(last_ref[0] == 1)
        def _():
            out_ref[:, below : below + wide] = through[rows[-1]]

        @pl.when(last_ref[0] == 0)
        def _():
            for r in range(sections - 1):
                out_ref[:, below + r * head : below + (r + 1) * head] = across[rows[r]]

        for store in stores:
            store.wait()

    return pl.pallas_call(
        kernel,
        out_shape=[
            jax.ShapeDtypeStruct((count, packed), BF16),
            pltpu.HBM((sections - 1, count, width), BF16),
        ],
        in_specs=[IN_SMEM]
        + [ANYWHERE] * sections
        + [IN_VMEM, IN_HBM, IN_HBM]
        + [ANYWHERE] * len(after),
        out_specs=[IN_VMEM, IN_HBM],
        scratch_shapes=[
            pltpu.VMEM((sections * count, width), BF16),
            pltpu.VMEM((width, wide), BF16),
            pltpu.VMEM((head, width), BF16),
            pltpu.SemaphoreType.DMA((copies,)),
        ],
        compiler_params=params(),
        name="couple",
    )(last, *slices[::-1], gain, in_hbm(w_layer), in_hbm(out_layer), *after)


def layout(sections, wide, head):
    through, across, at = {}, {}, 0
    for k in range(sections):
        for j in range(k):
            through[j, k] = slice(at, at + wide)
            at += wide
        for j in range(k + 1 if k < sections - 1 else 0):
            across[j, k] = slice(at, at + head)
            at += head
    return through, across, at


def compact(parts, section, wide, head, after):
    sections = len(parts)
    count = parts[0].shape[0]
    below = (sections - 2) * wide
    through, across, total = layout(sections, wide, head)

    def kernel(s_ref, *refs):
        part_refs, out_ref = refs[:sections], refs[-1]
        mine = s_ref[0]

        def fill(k, r):
            for j in range(k):
                at = (k - j - 1) * wide
                out_ref[0, :, through[j, k]] = part_refs[r][:, at : at + wide]
            for j in range(k + 1 if k < sections - 1 else 0):
                at = below + (k - j) * head
                out_ref[0, :, across[j, k]] = part_refs[r][:, at : at + head]

        for s in range(sections):

            @pl.when(mine == s)
            def _(s=s):
                for r in range(sections):
                    fill((s - r) % sections, r)

    vmem = pl.BlockSpec(memory_space=pltpu.VMEM)
    return pl.pallas_call(
        kernel,
        out_shape=jax.ShapeDtypeStruct((1, count, total), BF16),
        in_specs=[IN_SMEM] + [vmem] * sections + [ANYWHERE] * len(after),
        out_specs=vmem,
        compiler_params=params(SMALL),
        name="compact",
    )(section, *parts, *after)


def merge(first, second, after):
    count = first.shape[0]

    def kernel(first_ref, second_ref, *refs):
        refs[-1][:count] = first_ref[...]
        refs[-1][count:] = second_ref[...]

    return pl.pallas_call(
        kernel,
        out_shape=jax.ShapeDtypeStruct((2 * count,) + first.shape[1:], first.dtype),
        in_specs=[IN_VMEM] * 2 + [ANYWHERE] * len(after),
        out_specs=IN_VMEM,
        compiler_params=params(SMALL),
        name="merge",
    )(first, second, *after)


def serial(xz, pieces, places, norms, mask, section, gain, w_layer, out_layer, chunk):
    sections = len(xz)
    tokens = norms.shape[0]
    head, width = out_layer.shape
    wide = 3 * head
    scale = 1.0 / math.sqrt(head)
    cuts = [slice(at, at + chunk) for at in range(0, width, chunk)]
    beyond = range(2, sections)
    group = len(cuts) // HOPS
    through_at, across_at, _ = layout(sections, wide, head)
    count, packed = pieces[0].shape[-2:]
    plane = head // count
    n_in = sections + len(pieces)
    copies = sections + plane + 3 * len(cuts)

    def kernel(s_ref, p_ref, *refs):
        xz_refs, piece_refs = refs[:sections], refs[sections:n_in]
        n_ref, mask_ref, g_ref, w_ref, o_ref = refs[n_in : n_in + 5]
        n_out = n_in + 5
        back_ref, t_ref, a_ref = refs[n_out : n_out + 3]
        b_refs, refs = refs[n_out + 3 : n_out + 3 + HOPS], refs[HOPS:]
        far_refs = refs[n_out + 3 : n_out + 3 + len(beyond)]
        scratch = refs[n_out + 3 + len(beyond) :]
        xz_all, table, mixes, weights, projs, dmix, v_ref, back_in, w_in, o_in, sems = scratch
        mine = s_ref[0]
        started = []

        def start(source, target):
            copy = pltpu.make_async_copy(source, target, sems.at[len(started)])
            copy.start()
            started.append(copy)

        for r in range(sections):
            start(xz_refs[r], xz_all.at[mine ^ r])
        at = 0
        for ref in piece_refs:
            for i in range(ref.shape[0]):
                start(ref.at[i], table.at[p_ref[at]])
                at += 1
        small = list(started)
        for cut in cuts:
            start(w_ref.at[cut], w_in.at[cut])
            start(o_ref.at[:, cut], o_in.at[:, cut])
        large = started[len(small) :]
        for copy in small:
            copy.wait()

        def through(j, k):
            return table[:, :, through_at[j, k]].reshape(head, wide)

        def across(j, k):
            return table[:, :, across_at[j, k]].reshape(head, head)

        allowed = mask_ref[...] > 0.5
        norm = n_ref[...]
        rstds, tails, mixed = [], [], []
        for s in range(sections):
            proj = xz_all[s, :, :wide].astype(F32)
            for j in range(s):
                proj = proj + dot_nn(mixed[j], through(j, s))
            rstd = lax.rsqrt(norm * (1.0 / width) + EPS)
            proj = proj * rstd
            projs[s] = proj.astype(BF16)
            q, k, v = (projs[s, :, i * head : (i + 1) * head] for i in range(3))
            scores = jnp.where(allowed, dot_nt(q, k) * scale, -1e30)
            scores = jnp.exp(scores - jnp.max(scores, axis=1, keepdims=True))
            soft = scores / jnp.sum(scores, axis=1, keepdims=True)
            weights[s] = soft
            mix = dot_nn(soft.astype(BF16), v).astype(BF16)
            mixed.append(mix)
            mixes[:, s * head : (s + 1) * head] = mix
            rstds.append(rstd)
            dmix[:, s * head : (s + 1) * head] = xz_all[s, :, wide + head :].astype(F32)
            if s == sections - 1:
                break
            y = xz_all[s, :, wide : wide + head].astype(F32)
            for j in range(s):
                y = y + dot_nn(mixed[j], across(j, s))
            tail = y + dot_nn(mix, across(s, s))
            norm = norm + jnp.sum(mix.astype(F32) * (y + tail), axis=1, keepdims=True)
            norm = jnp.maximum(norm, 0.0)
            tails.append(tail)
        total = jnp.zeros((tokens, 1), F32)
        a_ref[...] = jnp.zeros_like(a_ref)
        for ref in far_refs:
            ref[...] = jnp.zeros_like(ref)
        for s in reversed(range(sections)):
            cols = slice(s * head, (s + 1) * head)
            da = dmix[:, cols]
            if s < sections - 1:
                da = da - total * tails[s]
            da = da.astype(BF16)
            q, k, v = (projs[s, :, i * head : (i + 1) * head] for i in range(3))
            soft = weights[s]
            dv = dot_tn(soft.astype(BF16), da)
            dsoft = dot_nt(da, v)
            dscore = soft * (dsoft - jnp.sum(dsoft * soft, axis=1, keepdims=True))
            dscore = (dscore * scale).astype(BF16)
            dproj = jnp.concatenate([dot_nn(dscore, k), dot_tn(dscore, q), dv], axis=1)
            along = jnp.sum(dproj * projs[s].astype(F32), axis=1, keepdims=True)
            first = (dproj * rstds[s]).astype(BF16)
            second = (-total * mixes[:, cols].astype(F32)).astype(BF16)
            total = total + rstds[s] * rstds[s] * along * (1.0 / width)
            for j in reversed(range(s)):
                term = dot_nt(first, through(j, s))
                if s < sections - 1:
                    term = term + dot_nt(second, across(j, s))
                dmix[:, j * head : (j + 1) * head] += term

            @pl.when(mine == s)
            def _(first=first, second=second, total=total):
                v_ref[:, :wide] = first
                v_ref[:, wide:] = second
                t_ref[...] = total

            for ref, d in zip(far_refs, beyond):

                @pl.when(mine + d == s)
                def _(ref=ref, first=first, second=second):
                    ref[:, :wide] = first
                    ref[:, wide:] = second

            for r in range(1, sections - s):

                @pl.when(mine == s + r)
                def _(r=r, cols=cols):
                    a_ref[:, (r - 1) * head : r * head] = mixes[:, cols]

        for i, cut in enumerate(cuts):
            large[2 * i].wait()
            large[2 * i + 1].wait()
            back = dot_nt(v_ref[:, :wide], w_in[cut, :])
            own = back * g_ref[:, cut] + dot_nn(v_ref[:, wide:], o_in[:, cut])
            own = own.astype(BF16)
            back_in[:, cut] = back.astype(BF16)
            start(back_in.at[:, cut], back_ref.at[:, cut])
            b_refs[i // group][i % group] = own
        for copy in started[len(small) + len(large) :]:
            copy.wait()

    vmem = pl.BlockSpec(memory_space=pltpu.VMEM)
    smem = pl.BlockSpec(memory_space=pltpu.SMEM)
    return pl.pallas_call(
        kernel,
        out_shape=[
            pltpu.HBM((tokens, width), BF16),
            pltpu.VMEM((tokens, 1), F32),
            pltpu.VMEM((tokens, (sections - 1) * head), BF16),
        ]
        + [pltpu.VMEM((group, tokens, chunk), BF16)] * HOPS
        + [pltpu.VMEM((tokens, wide + head), BF16) for _ in beyond],
        in_specs=[smem, smem] + [ANYWHERE] * n_in + [vmem, vmem, vmem, IN_HBM, IN_HBM],
        out_specs=[IN_HBM] + [vmem] * (2 + HOPS + len(beyond)),
        scratch_shapes=[
            pltpu.VMEM((sections,) + xz[0].shape, BF16),
            pltpu.VMEM((plane, count, packed), BF16),
            pltpu.VMEM((tokens, sections * head), BF16),
            pltpu.VMEM((sections, tokens, tokens), F32),
            pltpu.VMEM((sections, tokens, wide), BF16),
            pltpu.VMEM((tokens, sections * head), F32),
            pltpu.VMEM((tokens, wide + head), BF16),
            pltpu.VMEM((tokens, width), BF16),
            pltpu.VMEM((width, wide), BF16),
            pltpu.VMEM((head, width), BF16),
            pltpu.SemaphoreType.DMA((copies,)),
        ],
        compiler_params=params(),
        name="serial",
    )(
        section,
        places,
        *xz,
        *pieces,
        norms,
        mask,
        gain,
        in_hbm(w_layer),
        in_hbm(out_layer),
    )


def hold(array, after):
    def kernel(*refs):
        pass

    return pl.pallas_call(
        kernel,
        out_shape=jax.ShapeDtypeStruct(array.shape, array.dtype),
        in_specs=[ANYWHERE] * (1 + len(after)),
        out_specs=ANYWHERE,
        input_output_aliases={0: 0},
        compiler_params=params(SMALL),
        name="hold",
    )(array, *after)


def gather_two(first, second, after):
    count = first.shape[0]

    def kernel(first_ref, second_ref, *refs):
        out_ref, sems = refs[len(after) :]
        start = mover(sems)
        copies = [start(first_ref, out_ref.at[:count]), start(second_ref, out_ref.at[count:])]
        for copy in copies:
            copy.wait()

    return pl.pallas_call(
        kernel,
        out_shape=jax.ShapeDtypeStruct((2 * count,) + first.shape[1:], first.dtype),
        in_specs=[ANYWHERE] * (2 + len(after)),
        out_specs=IN_VMEM,
        scratch_shapes=[pltpu.SemaphoreType.DMA((2,))],
        compiler_params=params(SMALL),
        name="gather_two",
    )(first, second, *after)


def settle(total, mixes, stacks, places, x, cotangent, back, chunk):
    tokens, width = x.shape
    layers, rows = stacks[0].shape[1:3]
    entries = [(i, e) for i, stack in enumerate(stacks) for e in range(stack.shape[0])]
    plane = len(entries)
    head = plane * rows
    cuts = [slice(at, at + chunk) for at in range(0, width, chunk)]
    copies = plane * layers + 3 * len(cuts)

    def kernel(p_ref, t_ref, a_ref, x_ref, c_ref, back_ref, *refs):
        stack_refs = refs[: len(stacks)]
        rest_ref, dg_ref = refs[len(stacks) : len(stacks) + 2]
        lower, x_in, c_in, back_in, sems = refs[len(stacks) + 2 :]
        start = mover(sems)
        first = []
        for at, (i, e) in enumerate(entries):
            for r in range(layers):
                first.append(start(stack_refs[i].at[e, r], lower.at[r, p_ref[at]]))
        loads = []
        for cut in cuts:
            mine = [start(x_ref.at[:, cut], x_in.at[:, cut])]
            mine.append(start(c_ref.at[:, cut], c_in.at[:, cut]))
            mine.append(start(back_ref.at[:, cut], back_in.at[:, cut]))
            loads.append(mine)
        for load in first:
            load.wait()
        for i, (cut, mine) in enumerate(zip(cuts, loads)):
            for load in mine:
                load.wait()
            below = lower[:, :, :, cut].reshape(layers * head, chunk)
            here = x_in[:, cut].astype(F32) + dot_nn(a_ref[...], below)
            rest_ref[i] = (c_in[:, cut].astype(F32) - t_ref[...] * here).astype(BF16)
            gain = jnp.sum(back_in[:, cut].astype(F32) * here, axis=0, keepdims=True)
            for at in range(0, chunk, head):
                row = (cut.start + at) // head
                dg_ref[row : row + 1, :] = gain[:, at : at + head]

    return pl.pallas_call(
        kernel,
        out_shape=[
            pltpu.VMEM((len(cuts), tokens, chunk), BF16),
            pltpu.VMEM((width // head, head), F32),
        ],
        in_specs=[IN_SMEM] + [IN_VMEM] * 2 + [IN_HBM] * (3 + len(stacks)),
        out_specs=[IN_VMEM] * 2,
        scratch_shapes=[
            pltpu.VMEM((layers, plane, rows, width), BF16),
            pltpu.VMEM((tokens, width), BF16),
            pltpu.VMEM((tokens, width), BF16),
            pltpu.VMEM((tokens, width), BF16),
            pltpu.SemaphoreType.DMA((copies,)),
        ],
        compiler_params=params(),
        name="settle",
    )(
        places,
        in_vmem(total),
        in_vmem(mixes),
        *[in_hbm(array) for array in (x, cotangent, back, *stacks)],
    )


def far(sent, stacks, places):
    tokens, rank = sent.shape
    entries = [(i, e) for i, stack in enumerate(stacks) for e in range(stack.shape[0])]
    plane = len(entries)
    rows = stacks[0].shape[1]

    def kernel(p_ref, v_ref, *refs):
        stack_refs, out_ref = refs[: len(stacks)], refs[len(stacks)]
        slabs, sems = refs[len(stacks) + 1 :]
        start = mover(sems)
        loads = [start(stack_refs[i].at[e], slabs.at[at]) for at, (i, e) in enumerate(entries)]
        for at, load in enumerate(loads):
            load.wait()
            out_ref[p_ref[at]] = dot_nt(v_ref[...], slabs[at]).astype(BF16)

    return pl.pallas_call(
        kernel,
        out_shape=jax.ShapeDtypeStruct((plane, tokens, rows), BF16),
        in_specs=[IN_SMEM, IN_VMEM] + [ANYWHERE] * len(stacks),
        out_specs=IN_VMEM,
        scratch_shapes=[
            pltpu.VMEM((plane, rows, rank), BF16),
            pltpu.SemaphoreType.DMA((plane,)),
        ],
        compiler_params=params(),
        name="far",
    )(places, sent, *stacks)


def finish(terms):
    arrays = [array for term in terms for array in term]
    count = sum(array.shape[0] for array in terms[0])
    _, tokens, chunk = arrays[0].shape

    def kernel(*refs):
        whole_ref, terms_in, whole, sems = refs[len(arrays) :]
        start = mover(sems)
        loads = [[] for _ in range(count)]
        at = 0
        for n, term in enumerate(terms):
            i = 0
            for array in term:
                for e in range(array.shape[0]):
                    loads[i].append((refs[at].at[e], terms_in.at[n, i]))
                    i += 1
                at += 1
        loads = [[start(*pair) for pair in mine] for mine in loads]
        stores = []
        for i, mine in enumerate(loads):
            for load in mine:
                load.wait()
            total = terms_in[0, i].astype(F32)
            for n in range(1, len(terms)):
                total = total + terms_in[n, i].astype(F32)
            whole[i] = total.astype(BF16)
            stores.append(start(whole.at[i], whole_ref.at[:, pl.ds(i * chunk, chunk)]))
        for store in stores:
            store.wait()

    return pl.pallas_call(
        kernel,
        out_shape=pltpu.HBM((tokens, count * chunk), BF16),
        in_specs=[ANYWHERE] * len(arrays),
        out_specs=IN_HBM,
        scratch_shapes=[
            pltpu.VMEM((len(terms), count, tokens, chunk), BF16),
            pltpu.VMEM((count, tokens, chunk), BF16),
            pltpu.SemaphoreType.DMA((count * (len(terms) + 1),)),
        ],
        compiler_params=params(SMALL),
        name="finish",
    )(*arrays)


def added(arrays):
    def kernel(*refs):
        total = refs[0][...]
        for ref in refs[1:-1]:
            total = total + ref[...]
        refs[-1][...] = total

    return pl.pallas_call(
        kernel,
        out_shape=pltpu.VMEM(arrays[0].shape, F32),
        in_specs=[IN_VMEM] * len(arrays),
        out_specs=IN_VMEM,
        compiler_params=params(SMALL),
        name="added",
    )(*[in_vmem(array) for array in arrays])


def shifted(array, by):
    sections = lax.axis_size("section")
    return lax.ppermute(array, "section", [(i, (i + by) % sections) for i in range(sections)])


def raised(array, by):
    sections = lax.axis_size("section")
    return lax.ppermute(array, "section", [(i, i + by) for i in range(sections - by)])


def lowered(array, by):
    sections = lax.axis_size("section")
    return lax.ppermute(array, "section", [(i, i - by) for i in range(by, sections)])


def swapped(array, step):
    groups = lax.axis_size("group")
    devices = lax.axis_size("dp")
    bits = devices.bit_length() - 1
    pairs = []
    for p in range(devices):
        for g in range(groups):
            pairs.append((p * groups + g, (p ^ (1 << ((step + g) % bits))) * groups + g))
    return lax.ppermute(array, ("dp", "group"), pairs)


def handed(array, by):
    groups = lax.axis_size("group")
    return lax.ppermute(array, "group", [(i, (i + by) % groups) for i in range(groups)])


def plane_places():
    groups = lax.axis_size("group")
    bits = lax.axis_size("dp").bit_length() - 1
    masks = []
    for g in range(groups):
        order = [0]
        for step in range(bits):
            order = order + [m ^ (1 << ((step + g) % bits)) for m in order]
        masks.append(order)
    masks = jnp.asarray(masks, jnp.int32)
    dp, member = lax.axis_index("dp"), lax.axis_index("group")
    places = []
    for r in range(groups):
        giver = (member + groups - r) % groups
        places.append((dp ^ masks[giver]) * groups + giver)
    return jnp.concatenate(places).astype(jnp.int32)


def local(tokens_in, cotangent, gains, w_qkv, w_out, segments, plan):
    sections = lax.axis_size("section")
    groups = lax.axis_size("group")
    devices = lax.axis_size("dp")
    plane = devices * groups
    section = lax.axis_index("section")
    member = lax.axis_index("group")
    rows_dev = plan.shape[1]
    length = segments.shape[1]
    tokens, width = tokens_in.shape
    head = w_out.shape[1]
    share = rows_dev // groups
    w_layer, out_layer = w_qkv[0], w_out[0]
    place = member.astype(jnp.int32)[None]
    layer = section.astype(jnp.int32)[None]

    slice_rows = head // plane
    mine = lax.axis_index("dp") * groups + member
    own_rows, *parts = pick(
        tokens_in.reshape(rows_dev, length, width),
        plan,
        place,
        groups,
        out_layer,
        mine.astype(jnp.int32)[None],
        slice_rows,
    )
    slices = [raised(own_rows, r) for r in range(sections - 1, 0, -1)]
    slices = [own_rows] + slices[::-1]
    chosen = jnp.take(segments, plan[0], axis=0, mode="clip").astype(BF16)
    chosen = chosen.reshape(groups, share, length)
    moved, moved_seg = [], []
    for r in range(groups):
        outgoing = lax.dynamic_index_in_dim(chosen, (member + r) % groups, 0, keepdims=False)
        moved.append(handed(parts[r], r) if r else parts[r])
        moved_seg.append(handed(outgoing, r) if r else outgoing)
    moved = [part.reshape(share * length, width) for part in moved]
    order = (member - jnp.arange(groups)) % groups
    seg = jnp.take(jnp.stack(moved_seg), order, axis=0, mode="clip").reshape(tokens)
    at = jnp.arange(tokens)
    mask = (
        (at[:, None] >= at[None, :])
        & (at[:, None] // length == at[None, :] // length)
        & (seg[:, None] == seg[None, :])
    ).astype(F32)

    piece = slab(
        gains, w_layer, out_layer, mine.astype(jnp.int32)[None], width // plane, [mask]
    )
    slabs = [lowered(piece, 2)] if sections > 2 else []

    last = (section == sections - 1).astype(jnp.int32)[None]
    bits = devices.bit_length() - 1
    places = plane_places()
    coupling, stack = couple(slices, gains, w_layer, out_layer, last, [mask, places])
    others = [shifted(coupling, r) for r in range(1, sections)]

    x, xz, norms = project(
        moved, cotangent, gains, w_layer, out_layer, place, slices[1:]
    )
    chunk = width // plane

    def facing(array, by):
        return lax.ppermute(array, "section", [(i, i ^ by) for i in range(sections)])

    arrays, masks, by = [xz], [0], sections // 2
    while by > 0:
        arrays = arrays + [facing(array, by) for array in arrays]
        masks = masks + [mask_of ^ by for mask_of in masks]
        by = by // 2
    xz_all = [arrays[masks.index(r)] for r in range(sections)]
    early = [xz_all[r] for r in range(1, sections) if r & (r - 1) == 0]
    pieces = [compact([coupling] + others, layer, 3 * head, head, [xz])]

    rows = [stack[None]]
    for step in range(bits):
        if step > 0:
            pieces = [merge(*pieces, early + rows[1:])]
        pieces = pieces + [swapped(pieces[0], step)]
        rows = rows + [swapped(array, step) for array in rows]
    pieces = pieces + [handed(array, r) for r in range(1, groups) for array in pieces]
    for by in range(3, sections):
        slabs.append(lowered(hold(piece, pieces[:1]), by))
    back, total, mixes, *sent = serial(
        xz_all, pieces, places, norms, mask, layer, gains, w_layer, out_layer, chunk
    )

    def everywhere(stacks, after):
        for step in range(bits):
            if step > 0:
                stacks = [gather_two(*stacks, after)]
            stacks = stacks + [swapped(stacks[0], step)]
        return stacks + [handed(array, r) for r in range(1, groups) for array in stacks]

    own, sent, arrived = sent[:HOPS], sent[HOPS:], []
    for at in range(HOPS):
        own[at] = hold(own[at], arrived[-1:])
        arrived.append(lowered(own[at], 1))
    terms = [own, arrived]
    for at, (slab_of, sent_of) in enumerate(zip(slabs, sent)):
        after = pieces[1:2] if at == 0 else arrived[:1]
        slab_of = slab_of if at == 0 else hold(slab_of, [total])
        terms.append([far(sent_of, everywhere([slab_of], after), places)])

    while len(rows) > 2:
        rows = [gather_two(*rows[i : i + 2], arrived[:1]) for i in range(0, len(rows), 2)]
    rows = rows + [handed(array, r) for r in range(1, groups) for array in rows]
    rest, gain = settle(total, mixes, rows, places, x, cotangent, back, chunk)

    def crossed(array, by):
        return lax.ppermute(array, "dp", [(p, p ^ by) for p in range(devices)])

    gain_chip = added([gain] + [crossed(gain, by) for by in range(1, devices)])
    gain_whole = added([gain_chip] + [handed(gain_chip, r) for r in range(1, groups)])
    gain_whole = gain_whole.reshape(1, width)
    out = finish([[rest]] + terms)
    return (out[None], gain_whole)


def attend(hidden, segment, gain_row, w_layer, out_layer):
    count, length, width = hidden.shape
    head = out_layer.shape[0]
    scaled = hidden * lax.rsqrt(jnp.mean(hidden * hidden, axis=-1, keepdims=True) + EPS) * gain_row
    normed = scaled.astype(BF16).reshape(count * length, width)
    projected = jnp.dot(normed, w_layer, preferred_element_type=F32).reshape(count, length, 3 * head)
    query = projected[:, :, :head]
    keyed = projected[:, :, head : 2 * head]
    valued = projected[:, :, 2 * head :]
    positions = jnp.arange(length)
    allowed = (positions[:, None] >= positions[None, :])[None] & (
        segment[:, :, None] == segment[:, None, :]
    )
    scores = jnp.einsum("rid,rjd->rij", query, keyed, precision=lax.Precision.HIGHEST)
    scores = jnp.where(allowed, scores / math.sqrt(head), -1e30)
    weights = jax.nn.softmax(scores, axis=-1)
    mixed = jnp.einsum("rij,rjd->rid", weights, valued, precision=lax.Precision.HIGHEST)
    mixed = mixed.astype(BF16).reshape(count * length, head)
    output = jnp.dot(mixed, out_layer, preferred_element_type=F32).reshape(count, length, width)
    return hidden + output


MB_ROWS = 2


def relay(tokens_in, cotangent, gains, w_qkv, w_out, segments, plan):
    sections = lax.axis_size("section")
    section = lax.axis_index("section")
    rows_dev = plan.shape[1]
    width = tokens_in.shape[1]
    length = segments.shape[1]
    micro = rows_dev // MB_ROWS
    blocks = tokens_in.reshape(rows_dev, length, width)
    chosen = jnp.take(blocks, plan[0], axis=0)
    chosen_seg = jnp.take(segments, plan[0], axis=0).astype(BF16)
    assigned = lax.all_to_all(chosen, "group", split_axis=0, concat_axis=0, tiled=True)
    moved_seg = lax.all_to_all(chosen_seg, "group", split_axis=0, concat_axis=0, tiled=True)
    assigned = assigned.reshape(micro, MB_ROWS, length, width)
    seg_groups = moved_seg.reshape(micro, MB_ROWS, length)
    gain_row, w_layer, out_layer = gains[0], w_qkv[0], w_out[0]
    grad_rows = cotangent.reshape(micro, MB_ROWS, length, width)
    ticks = micro + sections - 1

    def passed_along(array, by):
        pairs = [(i, i + by) for i in range(sections) if 0 <= i + by < sections]
        return lax.ppermute(array, "section", pairs)

    def at(array, i):
        return lax.dynamic_index_in_dim(array, i, 0, keepdims=False)

    def forward_tick(tick, carry):
        saved, arrived = carry
        index = tick - section
        valid = (index >= 0) & (index < micro)
        clipped = jnp.clip(index, 0, micro - 1)
        entering = jnp.where(section == 0, at(assigned, clipped), arrived)
        kept = jnp.where(valid, entering, at(saved, clipped))
        saved = lax.dynamic_update_index_in_dim(saved, kept, clipped, 0)
        segment = at(seg_groups, clipped)

        def run_layer(value):
            return attend(value.astype(F32), segment, gain_row, w_layer, out_layer).astype(BF16)

        leaving = lax.cond(valid, run_layer, jnp.zeros_like, entering)
        return (saved, passed_along(leaving, 1))

    saved_init = jnp.zeros((micro, MB_ROWS, length, width), BF16)
    arrive_init = jnp.zeros((MB_ROWS, length, width), BF16)
    saved, _ = lax.fori_loop(0, ticks, forward_tick, (saved_init, arrive_init))

    def backward_tick(tick, carry):
        grads_x, gain_total, arrived = carry
        index = tick - (sections - 1 - section)
        valid = (index >= 0) & (index < micro)
        clipped = jnp.clip(index, 0, micro - 1)
        entering = jnp.where(section == sections - 1, at(grad_rows, clipped), arrived)
        segment = at(seg_groups, clipped)
        stored = at(saved, clipped).astype(F32)

        def local_layer(hidden, gains_here):
            return attend(hidden, segment, gains_here, w_layer, out_layer)

        def run_back(value):
            _, pullback = jax.vjp(local_layer, stored, gain_row)
            grad_hidden, grad_gain = pullback(value.astype(F32))
            return (grad_hidden.astype(BF16), grad_gain)

        def skip_back(value):
            return (jnp.zeros_like(value), jnp.zeros(gain_row.shape, F32))

        sending, grad_gain = lax.cond(valid, run_back, skip_back, entering)
        kept = jnp.where(valid, sending, at(grads_x, clipped))
        grads_x = lax.dynamic_update_index_in_dim(grads_x, kept, clipped, 0)
        return (grads_x, gain_total + grad_gain, passed_along(sending, -1))

    gain_init = jnp.zeros(gain_row.shape, F32)
    grads_x, gain_total, _ = lax.fori_loop(
        0, ticks, backward_tick, (saved_init, gain_init, arrive_init)
    )
    gain_whole = lax.psum(gain_total, ("dp", "group"))
    return (grads_x.reshape(1, rows_dev * length, width), gain_whole[None])


def solution(mesh):
    placed = (
        P(("dp", "group"), None),
        P(("dp", "group"), None),
        P("section", None),
        P("section", None, None),
        P("section", None, None),
        P(("dp", "group"), None),
        P(("dp", "group"), None),
    )

    def chosen(tokens_in, cotangent, gains, w_qkv, w_out, segments, plan):
        sections, head, width = w_out.shape
        devices = mesh.shape["dp"]
        small = sections * 4 * head < width and sections > 1
        halves = devices & (devices - 1) == 0 and sections & (sections - 1) == 0
        body = local if small and halves else relay
        return jax.shard_map(
            body,
            mesh=mesh,
            in_specs=placed,
            out_specs=(P("section", ("dp", "group"), None), P("section", None)),
            check_vma=False,
        )(tokens_in, cotangent, gains, w_qkv, w_out, segments, plan)

    return chosen
```

```python
import math

import jax
import jax.numpy as jnp
from jax import lax
from jax.experimental import pallas as pl
from jax.experimental.pallas import tpu as pltpu
from jax.sharding import PartitionSpec as P

EPS = 1e-05
VMEM_BYTES = 24 * 1024 * 1024
SMALL = 16 * 1024 * 1024
F32 = jnp.float32
BF16 = jnp.bfloat16


def dot_nn(a, b):
    return lax.dot_general(a, b, (((1,), (0,)), ((), ())), preferred_element_type=F32)


def dot_nt(a, b):
    return lax.dot_general(a, b, (((1,), (1,)), ((), ())), preferred_element_type=F32)


def dot_tn(a, b):
    return lax.dot_general(a, b, (((0,), (0,)), ((), ())), preferred_element_type=F32)


IN_HBM = pl.BlockSpec(memory_space=pltpu.HBM)
ANYWHERE = pl.BlockSpec(memory_space=pl.ANY)
IN_VMEM = pl.BlockSpec(memory_space=pltpu.VMEM)
IN_SMEM = pl.BlockSpec(memory_space=pltpu.SMEM)


def in_hbm(array):
    return pltpu.with_memory_space_constraint(array, pltpu.HBM)


def in_vmem(array):
    return pltpu.with_memory_space_constraint(array, pltpu.VMEM)


def mover(sems):
    used = []

    def start(source, target):
        copy = pltpu.make_async_copy(source, target, sems.at[len(used)])
        copy.start()
        used.append(copy)
        return copy

    return start


def steps(width):
    step = min(width, 1024)
    return [slice(at, at + step) for at in range(0, width, step)]


def params(limit=VMEM_BYTES):
    return pltpu.CompilerParams(vmem_limit_bytes=limit)


def pick(tokens, plan, place, groups, out_layer, mine, slice_rows):
    rows, length, width = tokens.shape
    share = rows // groups

    def kernel(plan_ref, place_ref, mine_ref, tokens_ref, o_ref, *rest):
        slice_ref, parts = rest[0], rest[1 : 1 + groups]
        slice_in, rows_in, sems = rest[1 + groups :]
        start = mover(sems)
        at = pl.ds(pl.multiple_of(mine_ref[0] * slice_rows, slice_rows), slice_rows)
        loads = [(start(o_ref.at[at], slice_in), slice_in, slice_ref)]
        for r in range(groups):
            target = lax.rem(place_ref[0] + r, groups)
            for c in range(share):
                here = rows_in.at[r * share + c]
                row = plan_ref[0, target * share + c]
                loads.append((start(tokens_ref.at[row], here), here, parts[r].at[c]))
        stores = []
        for load, here, there in loads:
            load.wait()
            stores.append(start(here, there))
        for store in stores:
            store.wait()

    return pl.pallas_call(
        kernel,
        out_shape=[pltpu.HBM((slice_rows, width), BF16)]
        + [pltpu.HBM((share, length, width), BF16)] * groups,
        in_specs=[IN_SMEM, IN_SMEM, IN_SMEM, IN_HBM, IN_HBM],
        out_specs=[IN_HBM] * (1 + groups),
        scratch_shapes=[
            pltpu.VMEM((slice_rows, width), BF16),
            pltpu.VMEM((rows, length, width), BF16),
            pltpu.SemaphoreType.DMA((2 * rows + 2,)),
        ],
        compiler_params=params(),
        name="pick",
    )(plan, place, mine, in_hbm(tokens), in_hbm(out_layer))


def project(parts, cotangent, gain, w_layer, out_layer, place, after):
    groups = len(parts)
    tokens, width = cotangent.shape
    head = out_layer.shape[0]
    wide = w_layer.shape[1]
    block = tokens // groups
    cuts = steps(width)
    copies = len(cuts) * (groups + 4)

    def kernel(place_ref, *refs):
        part_refs = refs[:groups]
        cot_ref, g_ref, w_ref, o_ref = refs[groups : groups + 4]
        x_ref, xz_ref, n_ref = refs[groups + 4 + len(after) : groups + 7 + len(after)]
        x_in, c_in, w_in, o_in, sems = refs[groups + 7 + len(after) :]
        start = mover(sems)
        loads = []
        for cut in cuts:
            mine = [start(w_ref.at[cut], w_in.at[cut])]
            mine.append(start(o_ref.at[:, cut], o_in.at[:, cut]))
            for r in range(groups):
                source = lax.rem(place_ref[0] + groups - r, groups)
                rows = pl.ds(pl.multiple_of(source * block, block), block)
                mine.append(start(part_refs[r].at[:, cut], x_in.at[rows, cut]))
            mine.append(start(cot_ref.at[:, cut], c_in.at[:, cut]))
            loads.append(mine)
        through = jnp.zeros((tokens, wide), F32)
        across = jnp.zeros((tokens, head), F32)
        back = jnp.zeros((tokens, head), F32)
        square = jnp.zeros((tokens, 1), F32)
        stores = []
        for cut, mine in zip(cuts, loads):
            for load in mine:
                load.wait()
            stores.append(start(x_in.at[:, cut], x_ref.at[:, cut]))
            x = x_in[:, cut]
            xf = x.astype(F32)
            through += dot_nn((xf * g_ref[:, cut]).astype(BF16), w_in[cut, :])
            across += dot_nt(x, o_in[:, cut])
            back += dot_nt(c_in[:, cut], o_in[:, cut])
            square += jnp.sum(xf * xf, axis=1, keepdims=True)
        xz_ref[:, :wide] = through.astype(BF16)
        xz_ref[:, wide : wide + head] = across.astype(BF16)
        xz_ref[:, wide + head :] = back.astype(BF16)
        n_ref[...] = square
        for store in stores:
            store.wait()

    return pl.pallas_call(
        kernel,
        out_shape=[
            pltpu.HBM((tokens, width), BF16),
            jax.ShapeDtypeStruct((tokens, wide + 2 * head), BF16),
            jax.ShapeDtypeStruct((tokens, 1), F32),
        ],
        in_specs=[IN_SMEM]
        + [ANYWHERE] * groups
        + [IN_HBM, IN_VMEM, IN_HBM, IN_HBM]
        + [ANYWHERE] * len(after),
        out_specs=[IN_HBM, IN_VMEM, IN_VMEM],
        scratch_shapes=[
            pltpu.VMEM((tokens, width), BF16),
            pltpu.VMEM((tokens, width), BF16),
            pltpu.VMEM((width, wide), BF16),
            pltpu.VMEM((head, width), BF16),
            pltpu.SemaphoreType.DMA((copies,)),
        ],
        compiler_params=params(),
        name="project",
    )(
        place,
        *parts,
        in_hbm(cotangent),
        gain,
        in_hbm(w_layer),
        in_hbm(out_layer),
        *after,
    )


def couple(slices, gain, w_layer, out_layer, last, after):
    sections = len(slices)
    count, width = slices[0].shape
    head = out_layer.shape[0]
    wide = w_layer.shape[1]
    below = (sections - 2) * wide
    packed = below + max(wide, (sections - 1) * head)
    cuts = steps(width)
    copies = len(cuts) * (sections + 2) + sections - 1

    def kernel(last_ref, *refs):
        s_refs = refs[:sections][::-1]
        g_ref, w_ref, o_ref = refs[sections : sections + 3]
        out_ref, stack_ref, r_in, w_in, o_in, sems = refs[sections + 3 + len(after) :]
        rows = [slice(r * count, (r + 1) * count) for r in range(sections)]
        start = mover(sems)
        loads = []
        for cut in cuts:
            mine = [start(w_ref.at[cut], w_in.at[cut])]
            mine.append(start(o_ref.at[:, cut], o_in.at[:, cut]))
            for r in range(sections):
                mine.append(start(s_refs[r].at[:, cut], r_in.at[rows[r], cut]))
            loads.append(mine)
        through = jnp.zeros((sections * count, wide), F32)
        across = jnp.zeros((sections * count, head), F32)
        for cut, mine in zip(cuts, loads):
            for load in mine:
                load.wait()
            r = r_in[:, cut]
            through += dot_nn((r.astype(F32) * g_ref[:, cut]).astype(BF16), w_in[cut, :])
            across += dot_nt(r, o_in[:, cut])
        stores = [start(r_in.at[rows[r]], stack_ref.at[r - 1]) for r in range(1, sections)]
        through = through.astype(BF16)
        across = across.astype(BF16)
        out_ref[...] = jnp.zeros_like(out_ref)
        for r in range(1, sections - 1):
            out_ref[:, (r - 1) * wide : r * wide] = through[rows[r]]

        @pl.when(last_ref[0] == 1)
        def _():
            out_ref[:, below : below + wide] = through[rows[-1]]

        @pl.when(last_ref[0] == 0)
        def _():
            for r in range(sections - 1):
                out_ref[:, below + r * head : below + (r + 1) * head] = across[rows[r]]

        for store in stores:
            store.wait()

    return pl.pallas_call(
        kernel,
        out_shape=[
            jax.ShapeDtypeStruct((count, packed), BF16),
            pltpu.HBM((sections - 1, count, width), BF16),
        ],
        in_specs=[IN_SMEM]
        + [ANYWHERE] * sections
        + [IN_VMEM, IN_HBM, IN_HBM]
        + [ANYWHERE] * len(after),
        out_specs=[IN_VMEM, IN_HBM],
        scratch_shapes=[
            pltpu.VMEM((sections * count, width), BF16),
            pltpu.VMEM((width, wide), BF16),
            pltpu.VMEM((head, width), BF16),
            pltpu.SemaphoreType.DMA((copies,)),
        ],
        compiler_params=params(),
        name="couple",
    )(last, *slices[::-1], gain, in_hbm(w_layer), in_hbm(out_layer), *after)


def layout(sections, wide, head):
    through, across, at = {}, {}, 0
    for k in range(sections):
        for j in range(k):
            through[j, k] = slice(at, at + wide)
            at += wide
        for j in range(k + 1 if k < sections - 1 else 0):
            across[j, k] = slice(at, at + head)
            at += head
    return through, across, at


def compact(parts, section, wide, head, after):
    sections = len(parts)
    count = parts[0].shape[0]
    below = (sections - 2) * wide
    through, across, total = layout(sections, wide, head)

    def kernel(s_ref, *refs):
        part_refs, out_ref = refs[:sections], refs[-1]
        mine = s_ref[0]

        def fill(k, r):
            for j in range(k):
                at = (k - j - 1) * wide
                out_ref[0, :, through[j, k]] = part_refs[r][:, at : at + wide]
            for j in range(k + 1 if k < sections - 1 else 0):
                at = below + (k - j) * head
                out_ref[0, :, across[j, k]] = part_refs[r][:, at : at + head]

        for s in range(sections):

            @pl.when(mine == s)
            def _(s=s):
                for r in range(sections):
                    fill((s - r) % sections, r)

    vmem = pl.BlockSpec(memory_space=pltpu.VMEM)
    return pl.pallas_call(
        kernel,
        out_shape=jax.ShapeDtypeStruct((1, count, total), BF16),
        in_specs=[IN_SMEM] + [vmem] * sections + [ANYWHERE] * len(after),
        out_specs=vmem,
        compiler_params=params(SMALL),
        name="compact",
    )(section, *parts, *after)


def merge(first, second, after):
    count = first.shape[0]

    def kernel(first_ref, second_ref, *refs):
        refs[-1][:count] = first_ref[...]
        refs[-1][count:] = second_ref[...]

    return pl.pallas_call(
        kernel,
        out_shape=jax.ShapeDtypeStruct((2 * count,) + first.shape[1:], first.dtype),
        in_specs=[IN_VMEM] * 2 + [ANYWHERE] * len(after),
        out_specs=IN_VMEM,
        compiler_params=params(SMALL),
        name="merge",
    )(first, second, *after)


def serial(xz, pieces, places, norms, mask, section, gain, w_layer, out_layer, streams):
    sections = len(xz)
    tokens = norms.shape[0]
    head, width = out_layer.shape
    wide = 3 * head
    scale = 1.0 / math.sqrt(head)
    chunk = streams[-1].stop
    cuts = [slice(at, at + chunk) for at in range(0, width, chunk)]
    through_at, across_at, _ = layout(sections, wide, head)
    count, packed = pieces[0].shape[-2:]
    plane = head // count
    n_in = sections + len(pieces)
    copies = sections + plane + 3 * len(cuts)

    def kernel(s_ref, p_ref, *refs):
        xz_refs, piece_refs = refs[:sections], refs[sections:n_in]
        n_ref, mask_ref, g_ref, w_ref, o_ref = refs[n_in : n_in + 5]
        n_out = n_in + 5
        back_ref, b_ref, t_ref, a_ref = refs[n_out : n_out + 4]
        first_refs = refs[n_out + 4 : n_out + 4 + len(streams)]
        scratch = refs[n_out + 4 + len(streams) :]
        xz_all, table, mixes, weights, projs, dmix, v_ref, back_in, w_in, o_in, sems = scratch
        mine = s_ref[0]
        started = []

        def start(source, target):
            copy = pltpu.make_async_copy(source, target, sems.at[len(started)])
            copy.start()
            started.append(copy)

        for r in range(sections):
            start(xz_refs[r], xz_all.at[mine ^ r])
        at = 0
        for ref in piece_refs:
            for i in range(ref.shape[0]):
                start(ref.at[i], table.at[p_ref[at]])
                at += 1
        small = list(started)
        for cut in cuts:
            start(w_ref.at[cut], w_in.at[cut])
            start(o_ref.at[:, cut], o_in.at[:, cut])
        large = started[len(small) :]
        for copy in small:
            copy.wait()

        def through(j, k):
            return table[:, :, through_at[j, k]].reshape(head, wide)

        def across(j, k):
            return table[:, :, across_at[j, k]].reshape(head, head)

        allowed = mask_ref[...] > 0.5
        norm = n_ref[...]
        rstds, tails, mixed = [], [], []
        for s in range(sections):
            proj = xz_all[s, :, :wide].astype(F32)
            for j in range(s):
                proj = proj + dot_nn(mixed[j], through(j, s))
            rstd = lax.rsqrt(norm * (1.0 / width) + EPS)
            proj = proj * rstd
            projs[s] = proj.astype(BF16)
            q, k, v = (projs[s, :, i * head : (i + 1) * head] for i in range(3))
            scores = jnp.where(allowed, dot_nt(q, k) * scale, -1e30)
            scores = jnp.exp(scores - jnp.max(scores, axis=1, keepdims=True))
            soft = scores / jnp.sum(scores, axis=1, keepdims=True)
            weights[s] = soft
            mix = dot_nn(soft.astype(BF16), v).astype(BF16)
            mixed.append(mix)
            mixes[:, s * head : (s + 1) * head] = mix
            rstds.append(rstd)
            dmix[:, s * head : (s + 1) * head] = xz_all[s, :, wide + head :].astype(F32)
            if s == sections - 1:
                break
            y = xz_all[s, :, wide : wide + head].astype(F32)
            for j in range(s):
                y = y + dot_nn(mixed[j], across(j, s))
            tail = y + dot_nn(mix, across(s, s))
            norm = norm + jnp.sum(mix.astype(F32) * (y + tail), axis=1, keepdims=True)
            norm = jnp.maximum(norm, 0.0)
            tails.append(tail)
        total = jnp.zeros((tokens, 1), F32)
        a_ref[...] = jnp.zeros_like(a_ref)
        for s in reversed(range(sections)):
            cols = slice(s * head, (s + 1) * head)
            da = dmix[:, cols]
            if s < sections - 1:
                da = da - total * tails[s]
            da = da.astype(BF16)
            q, k, v = (projs[s, :, i * head : (i + 1) * head] for i in range(3))
            soft = weights[s]
            dv = dot_tn(soft.astype(BF16), da)
            dsoft = dot_nt(da, v)
            dscore = soft * (dsoft - jnp.sum(dsoft * soft, axis=1, keepdims=True))
            dscore = (dscore * scale).astype(BF16)
            dproj = jnp.concatenate([dot_nn(dscore, k), dot_tn(dscore, q), dv], axis=1)
            along = jnp.sum(dproj * projs[s].astype(F32), axis=1, keepdims=True)
            first = (dproj * rstds[s]).astype(BF16)
            second = (-total * mixes[:, cols].astype(F32)).astype(BF16)
            total = total + rstds[s] * rstds[s] * along * (1.0 / width)
            for j in reversed(range(s)):
                term = dot_nt(first, through(j, s))
                if s < sections - 1:
                    term = term + dot_nt(second, across(j, s))
                dmix[:, j * head : (j + 1) * head] += term

            @pl.when(mine == s)
            def _(first=first, second=second, total=total):
                v_ref[:, :wide] = first
                v_ref[:, wide:] = second
                t_ref[...] = total

            for r in range(1, sections - s):

                @pl.when(mine == s + r)
                def _(r=r, cols=cols):
                    a_ref[:, (r - 1) * head : r * head] = mixes[:, cols]

        for i, cut in enumerate(cuts):
            large[2 * i].wait()
            large[2 * i + 1].wait()
            back = dot_nt(v_ref[:, :wide], w_in[cut, :])
            own = back * g_ref[:, cut] + dot_nn(v_ref[:, wide:], o_in[:, cut])
            own = own.astype(BF16)
            back_in[:, cut] = back.astype(BF16)
            start(back_in.at[:, cut], back_ref.at[:, cut])
            b_ref[0, i] = own
            b_ref[1, i] = jnp.zeros_like(own)
            if i == 0:
                for ref, part in zip(first_refs, streams):
                    ref[...] = own[:, part]
        for copy in started[len(small) + len(large) :]:
            copy.wait()

    vmem = pl.BlockSpec(memory_space=pltpu.VMEM)
    smem = pl.BlockSpec(memory_space=pltpu.SMEM)
    return pl.pallas_call(
        kernel,
        out_shape=[
            pltpu.HBM((tokens, width), BF16),
            pltpu.VMEM((2, len(cuts), tokens, chunk), BF16),
            pltpu.VMEM((tokens, 1), F32),
            pltpu.VMEM((tokens, (sections - 1) * head), BF16),
        ]
        + [pltpu.VMEM((tokens, part.stop - part.start), BF16) for part in streams],
        in_specs=[smem, smem] + [ANYWHERE] * n_in + [vmem, vmem, vmem, IN_HBM, IN_HBM],
        out_specs=[IN_HBM] + [vmem] * (3 + len(streams)),
        scratch_shapes=[
            pltpu.VMEM((sections,) + xz[0].shape, BF16),
            pltpu.VMEM((plane, count, packed), BF16),
            pltpu.VMEM((tokens, sections * head), BF16),
            pltpu.VMEM((sections, tokens, tokens), F32),
            pltpu.VMEM((sections, tokens, wide), BF16),
            pltpu.VMEM((tokens, sections * head), F32),
            pltpu.VMEM((tokens, wide + head), BF16),
            pltpu.VMEM((tokens, width), BF16),
            pltpu.VMEM((width, wide), BF16),
            pltpu.VMEM((head, width), BF16),
            pltpu.SemaphoreType.DMA((copies,)),
        ],
        compiler_params=params(),
        name="serial",
    )(
        section,
        places,
        *xz,
        *pieces,
        norms,
        mask,
        gain,
        in_hbm(w_layer),
        in_hbm(out_layer),
    )


def hold(array, after):
    def kernel(*refs):
        pass

    return pl.pallas_call(
        kernel,
        out_shape=jax.ShapeDtypeStruct(array.shape, array.dtype),
        in_specs=[ANYWHERE] * (1 + len(after)),
        out_specs=ANYWHERE,
        input_output_aliases={0: 0},
        compiler_params=params(SMALL),
        name="hold",
    )(array, *after)


def gather_two(first, second, after):
    count = first.shape[0]

    def kernel(first_ref, second_ref, *refs):
        out_ref, sems = refs[len(after) :]
        start = mover(sems)
        copies = [start(first_ref, out_ref.at[:count]), start(second_ref, out_ref.at[count:])]
        for copy in copies:
            copy.wait()

    return pl.pallas_call(
        kernel,
        out_shape=jax.ShapeDtypeStruct((2 * count,) + first.shape[1:], first.dtype),
        in_specs=[ANYWHERE] * (2 + len(after)),
        out_specs=IN_VMEM,
        scratch_shapes=[pltpu.SemaphoreType.DMA((2,))],
        compiler_params=params(SMALL),
        name="gather_two",
    )(first, second, *after)


def settle(total, mixes, stacks, places, x, cotangent, back, chunk):
    tokens, width = x.shape
    layers, rows = stacks[0].shape[1:3]
    entries = [(i, e) for i, stack in enumerate(stacks) for e in range(stack.shape[0])]
    plane = len(entries)
    head = plane * rows
    cuts = [slice(at, at + chunk) for at in range(0, width, chunk)]
    copies = plane * layers + 3 * len(cuts)

    def kernel(p_ref, t_ref, a_ref, x_ref, c_ref, back_ref, *refs):
        stack_refs = refs[: len(stacks)]
        rest_ref, dg_ref = refs[len(stacks) : len(stacks) + 2]
        lower, x_in, c_in, back_in, sems = refs[len(stacks) + 2 :]
        start = mover(sems)
        first = []
        for at, (i, e) in enumerate(entries):
            for r in range(layers):
                first.append(start(stack_refs[i].at[e, r], lower.at[r, p_ref[at]]))
        loads = []
        for cut in cuts:
            mine = [start(x_ref.at[:, cut], x_in.at[:, cut])]
            mine.append(start(c_ref.at[:, cut], c_in.at[:, cut]))
            mine.append(start(back_ref.at[:, cut], back_in.at[:, cut]))
            loads.append(mine)
        for load in first:
            load.wait()
        for i, (cut, mine) in enumerate(zip(cuts, loads)):
            for load in mine:
                load.wait()
            below = lower[:, :, :, cut].reshape(layers * head, chunk)
            here = x_in[:, cut].astype(F32) + dot_nn(a_ref[...], below)
            rest_ref[i] = (c_in[:, cut].astype(F32) - t_ref[...] * here).astype(BF16)
            gain = jnp.sum(back_in[:, cut].astype(F32) * here, axis=0, keepdims=True)
            for at in range(0, chunk, head):
                row = (cut.start + at) // head
                dg_ref[row : row + 1, :] = gain[:, at : at + head]

    return pl.pallas_call(
        kernel,
        out_shape=[
            pltpu.VMEM((len(cuts), tokens, chunk), BF16),
            pltpu.VMEM((width // head, head), F32),
        ],
        in_specs=[IN_SMEM] + [IN_VMEM] * 2 + [IN_HBM] * (3 + len(stacks)),
        out_specs=[IN_VMEM] * 2,
        scratch_shapes=[
            pltpu.VMEM((layers, plane, rows, width), BF16),
            pltpu.VMEM((tokens, width), BF16),
            pltpu.VMEM((tokens, width), BF16),
            pltpu.VMEM((tokens, width), BF16),
            pltpu.SemaphoreType.DMA((copies,)),
        ],
        compiler_params=params(),
        name="settle",
    )(
        places,
        in_vmem(total),
        in_vmem(mixes),
        *[in_hbm(array) for array in (x, cotangent, back, *stacks)],
    )


def join(index, arrived, pair, cols, after):
    tokens, part = arrived.shape

    def kernel(i_ref, r_ref, _, *refs):
        send_ref, pair_ref = refs[len(after) :]
        at = i_ref[0]
        r = r_ref[...]
        send_ref[...] = (pair_ref[0, at, :, cols].astype(F32) + r.astype(F32)).astype(BF16)
        pair_ref[1, at, :, cols] = r

    return pl.pallas_call(
        kernel,
        out_shape=[pltpu.VMEM((tokens, part), BF16), pltpu.VMEM(pair.shape, BF16)],
        in_specs=[IN_SMEM] + [IN_VMEM] * 2 + [ANYWHERE] * len(after),
        out_specs=[IN_VMEM] * 2,
        input_output_aliases={2: 1},
        compiler_params=params(SMALL),
        name="join",
    )(index, in_vmem(arrived), in_vmem(pair), *after)


def finish(index, arrived, pair, rest, streams):
    _, count, tokens, chunk = pair.shape

    def kernel(i_ref, *refs):
        r_refs = refs[: len(streams)]
        pair_ref, rest_ref, whole_ref, whole, sems = refs[len(streams) :]
        at = i_ref[0]
        copies = []
        for i in range(count):
            full = rest_ref[i].astype(F32) + pair_ref[0, i].astype(F32)
            whole[i] = (full + pair_ref[1, i].astype(F32)).astype(BF16)

            @pl.when(at == i)
            def _(i=i, full=full):
                for ref, cols in zip(r_refs, streams):
                    whole[i, :, cols] = (full[:, cols] + ref[...].astype(F32)).astype(BF16)

            there = whole_ref.at[:, pl.ds(i * chunk, chunk)]
            copies.append(pltpu.make_async_copy(whole.at[i], there, sems.at[i]))
            copies[-1].start()
        for copy in copies:
            copy.wait()

    return pl.pallas_call(
        kernel,
        out_shape=pltpu.HBM((tokens, count * chunk), BF16),
        in_specs=[IN_SMEM] + [IN_VMEM] * (len(streams) + 2),
        out_specs=IN_HBM,
        scratch_shapes=[
            pltpu.VMEM((count, tokens, chunk), BF16),
            pltpu.SemaphoreType.DMA((count,)),
        ],
        compiler_params=params(SMALL),
        name="finish",
    )(index, *[in_vmem(array) for array in arrived], in_vmem(pair), in_vmem(rest))


def added(arrays):
    def kernel(*refs):
        total = refs[0][...]
        for ref in refs[1:-1]:
            total = total + ref[...]
        refs[-1][...] = total

    return pl.pallas_call(
        kernel,
        out_shape=pltpu.VMEM(arrays[0].shape, F32),
        in_specs=[IN_VMEM] * len(arrays),
        out_specs=IN_VMEM,
        compiler_params=params(SMALL),
        name="added",
    )(*[in_vmem(array) for array in arrays])


STREAMS = 2
CHUNKS = 4


def stream_columns(chunk):
    lanes = 128
    tiles = chunk // lanes
    ends = [-(-tiles * (i + 1) // STREAMS) * lanes for i in range(STREAMS)]
    return [slice(start, end) for start, end in zip([0] + ends, ends)]


def shifted(array, by):
    sections = lax.axis_size("section")
    return lax.ppermute(array, "section", [(i, (i + by) % sections) for i in range(sections)])


def raised(array, by):
    sections = lax.axis_size("section")
    return lax.ppermute(array, "section", [(i, i + by) for i in range(sections - by)])


def swapped(array, step):
    groups = lax.axis_size("group")
    devices = lax.axis_size("dp")
    bits = devices.bit_length() - 1
    pairs = []
    for p in range(devices):
        for g in range(groups):
            pairs.append((p * groups + g, (p ^ (1 << ((step + g) % bits))) * groups + g))
    return lax.ppermute(array, ("dp", "group"), pairs)


def handed(array, by):
    groups = lax.axis_size("group")
    return lax.ppermute(array, "group", [(i, (i + by) % groups) for i in range(groups)])


def plane_places():
    groups = lax.axis_size("group")
    bits = lax.axis_size("dp").bit_length() - 1
    masks = []
    for g in range(groups):
        order = [0]
        for step in range(bits):
            order = order + [m ^ (1 << ((step + g) % bits)) for m in order]
        masks.append(order)
    masks = jnp.asarray(masks, jnp.int32)
    dp, member = lax.axis_index("dp"), lax.axis_index("group")
    places = []
    for r in range(groups):
        giver = (member + groups - r) % groups
        places.append((dp ^ masks[giver]) * groups + giver)
    return jnp.concatenate(places).astype(jnp.int32)


def local(tokens_in, cotangent, gains, w_qkv, w_out, segments, plan):
    sections = lax.axis_size("section")
    groups = lax.axis_size("group")
    devices = lax.axis_size("dp")
    plane = devices * groups
    section = lax.axis_index("section")
    member = lax.axis_index("group")
    rows_dev = plan.shape[1]
    length = segments.shape[1]
    tokens, width = tokens_in.shape
    head = w_out.shape[1]
    share = rows_dev // groups
    w_layer, out_layer = w_qkv[0], w_out[0]
    place = member.astype(jnp.int32)[None]
    layer = section.astype(jnp.int32)[None]

    slice_rows = head // plane
    mine = lax.axis_index("dp") * groups + member
    own_rows, *parts = pick(
        tokens_in.reshape(rows_dev, length, width),
        plan,
        place,
        groups,
        out_layer,
        mine.astype(jnp.int32)[None],
        slice_rows,
    )
    slices = [raised(own_rows, r) for r in range(sections - 1, 0, -1)]
    slices = [own_rows] + slices[::-1]
    chosen = jnp.take(segments, plan[0], axis=0, mode="clip").astype(BF16)
    chosen = chosen.reshape(groups, share, length)
    moved, moved_seg = [], []
    for r in range(groups):
        outgoing = lax.dynamic_index_in_dim(chosen, (member + r) % groups, 0, keepdims=False)
        moved.append(handed(parts[r], r) if r else parts[r])
        moved_seg.append(handed(outgoing, r) if r else outgoing)
    moved = [part.reshape(share * length, width) for part in moved]
    order = (member - jnp.arange(groups)) % groups
    seg = jnp.take(jnp.stack(moved_seg), order, axis=0, mode="clip").reshape(tokens)
    at = jnp.arange(tokens)
    mask = (
        (at[:, None] >= at[None, :])
        & (at[:, None] // length == at[None, :] // length)
        & (seg[:, None] == seg[None, :])
    ).astype(F32)

    last = (section == sections - 1).astype(jnp.int32)[None]
    bits = devices.bit_length() - 1
    places = plane_places()
    coupling, stack = couple(slices, gains, w_layer, out_layer, last, [mask, places])
    others = [shifted(coupling, r) for r in range(1, sections)]

    x, xz, norms = project(
        moved, cotangent, gains, w_layer, out_layer, place, slices[:0:-1]
    )
    streams = stream_columns(width // CHUNKS)

    def facing(array, by):
        return lax.ppermute(array, "section", [(i, i ^ by) for i in range(sections)])

    arrays, masks, by = [hold(xz, others)], [0], sections // 2
    while by > 0:
        arrays = arrays + [facing(array, by) for array in arrays]
        masks = masks + [mask_of ^ by for mask_of in masks]
        by = by // 2
    xz_all = [arrays[masks.index(r)] for r in range(sections)]
    early = [xz_all[r] for r in range(1, sections) if r & (r - 1) == 0]
    late = [xz_all[r] for r in range(1, sections) if r & (r - 1) != 0]
    pieces = [compact([coupling] + others, layer, 3 * head, head, [xz])]

    rows = [stack[None]]
    for step in range(bits):
        if step > 0:
            pieces = [merge(*pieces, early)]
            rows = [gather_two(*rows, pieces)]
        pieces = pieces + [swapped(pieces[0], step)]
        rows = rows + [swapped(rows[0], step)]
    pieces = pieces[:-1] + [hold(pieces[-1], late)]
    pieces = pieces + [handed(array, r) for r in range(1, groups) for array in pieces]
    back, pair, total, mixes, *leaving = serial(
        xz_all, pieces, places, norms, mask, layer, gains, w_layer, out_layer, streams
    )
    down = [(i, i - 1) for i in range(1, sections)]
    behind = sections - 1 - section

    def index(tick):
        return jnp.clip(tick - behind, 0, CHUNKS - 1).astype(jnp.int32)[None]

    def lowered(arrays):
        return [lax.ppermute(array, "section", down) for array in arrays]

    def crossed(array, by):
        return lax.ppermute(array, "dp", [(p, p ^ by) for p in range(devices)])

    ticks = CHUNKS + sections - 1
    after = {}
    for tick in range(1, ticks):
        arrived = lowered(leaving)
        if tick < ticks - 1:
            for i, cols in enumerate(streams):
                leaving[i], pair = join(
                    index(tick), arrived[i], pair, cols, after.get(tick, [])
                )
        if tick == 1:
            rows = [hold(array, leaving) for array in rows]
            rows = rows + [handed(array, r) for r in range(1, groups) for array in rows]
            rest, gain = settle(
                total, mixes, rows, places, x, cotangent, back, width // CHUNKS
            )
            crossing = [crossed(gain, by) for by in range(1, devices)]
            gain_chip = added([gain] + crossing)
            gain_whole = added([gain_chip] + [handed(gain_chip, r) for r in range(1, groups)])
            gain_whole = gain_whole.reshape(1, width)
            after = {2: [gain], 3: crossing[: devices // 2], 4: [gain_chip], 5: [gain_whole]}
    out = finish(index(ticks - 1), arrived, pair, rest, streams)
    return (out[None], gain_whole)


def attend(hidden, segment, gain_row, w_layer, out_layer):
    count, length, width = hidden.shape
    head = out_layer.shape[0]
    scaled = hidden * lax.rsqrt(jnp.mean(hidden * hidden, axis=-1, keepdims=True) + EPS) * gain_row
    normed = scaled.astype(BF16).reshape(count * length, width)
    projected = jnp.dot(normed, w_layer, preferred_element_type=F32).reshape(count, length, 3 * head)
    query = projected[:, :, :head]
    keyed = projected[:, :, head : 2 * head]
    valued = projected[:, :, 2 * head :]
    positions = jnp.arange(length)
    allowed = (positions[:, None] >= positions[None, :])[None] & (
        segment[:, :, None] == segment[:, None, :]
    )
    scores = jnp.einsum("rid,rjd->rij", query, keyed, precision=lax.Precision.HIGHEST)
    scores = jnp.where(allowed, scores / math.sqrt(head), -1e30)
    weights = jax.nn.softmax(scores, axis=-1)
    mixed = jnp.einsum("rij,rjd->rid", weights, valued, precision=lax.Precision.HIGHEST)
    mixed = mixed.astype(BF16).reshape(count * length, head)
    output = jnp.dot(mixed, out_layer, preferred_element_type=F32).reshape(count, length, width)
    return hidden + output


MB_ROWS = 2


def relay(tokens_in, cotangent, gains, w_qkv, w_out, segments, plan):
    sections = lax.axis_size("section")
    section = lax.axis_index("section")
    rows_dev = plan.shape[1]
    width = tokens_in.shape[1]
    length = segments.shape[1]
    micro = rows_dev // MB_ROWS
    blocks = tokens_in.reshape(rows_dev, length, width)
    chosen = jnp.take(blocks, plan[0], axis=0)
    chosen_seg = jnp.take(segments, plan[0], axis=0).astype(BF16)
    assigned = lax.all_to_all(chosen, "group", split_axis=0, concat_axis=0, tiled=True)
    moved_seg = lax.all_to_all(chosen_seg, "group", split_axis=0, concat_axis=0, tiled=True)
    assigned = assigned.reshape(micro, MB_ROWS, length, width)
    seg_groups = moved_seg.reshape(micro, MB_ROWS, length)
    gain_row, w_layer, out_layer = gains[0], w_qkv[0], w_out[0]
    grad_rows = cotangent.reshape(micro, MB_ROWS, length, width)
    ticks = micro + sections - 1

    def passed_along(array, by):
        pairs = [(i, i + by) for i in range(sections) if 0 <= i + by < sections]
        return lax.ppermute(array, "section", pairs)

    def at(array, i):
        return lax.dynamic_index_in_dim(array, i, 0, keepdims=False)

    def forward_tick(tick, carry):
        saved, arrived = carry
        index = tick - section
        valid = (index >= 0) & (index < micro)
        clipped = jnp.clip(index, 0, micro - 1)
        entering = jnp.where(section == 0, at(assigned, clipped), arrived)
        kept = jnp.where(valid, entering, at(saved, clipped))
        saved = lax.dynamic_update_index_in_dim(saved, kept, clipped, 0)
        segment = at(seg_groups, clipped)

        def run_layer(value):
            return attend(value.astype(F32), segment, gain_row, w_layer, out_layer).astype(BF16)

        leaving = lax.cond(valid, run_layer, jnp.zeros_like, entering)
        return (saved, passed_along(leaving, 1))

    saved_init = jnp.zeros((micro, MB_ROWS, length, width), BF16)
    arrive_init = jnp.zeros((MB_ROWS, length, width), BF16)
    saved, _ = lax.fori_loop(0, ticks, forward_tick, (saved_init, arrive_init))

    def backward_tick(tick, carry):
        grads_x, gain_total, arrived = carry
        index = tick - (sections - 1 - section)
        valid = (index >= 0) & (index < micro)
        clipped = jnp.clip(index, 0, micro - 1)
        entering = jnp.where(section == sections - 1, at(grad_rows, clipped), arrived)
        segment = at(seg_groups, clipped)
        stored = at(saved, clipped).astype(F32)

        def local_layer(hidden, gains_here):
            return attend(hidden, segment, gains_here, w_layer, out_layer)

        def run_back(value):
            _, pullback = jax.vjp(local_layer, stored, gain_row)
            grad_hidden, grad_gain = pullback(value.astype(F32))
            return (grad_hidden.astype(BF16), grad_gain)

        def skip_back(value):
            return (jnp.zeros_like(value), jnp.zeros(gain_row.shape, F32))

        sending, grad_gain = lax.cond(valid, run_back, skip_back, entering)
        kept = jnp.where(valid, sending, at(grads_x, clipped))
        grads_x = lax.dynamic_update_index_in_dim(grads_x, kept, clipped, 0)
        return (grads_x, gain_total + grad_gain, passed_along(sending, -1))

    gain_init = jnp.zeros(gain_row.shape, F32)
    grads_x, gain_total, _ = lax.fori_loop(
        0, ticks, backward_tick, (saved_init, gain_init, arrive_init)
    )
    gain_whole = lax.psum(gain_total, ("dp", "group"))
    return (grads_x.reshape(1, rows_dev * length, width), gain_whole[None])


def solution(mesh):
    placed = (
        P(("dp", "group"), None),
        P(("dp", "group"), None),
        P("section", None),
        P("section", None, None),
        P("section", None, None),
        P(("dp", "group"), None),
        P(("dp", "group"), None),
    )

    def chosen(tokens_in, cotangent, gains, w_qkv, w_out, segments, plan):
        sections, head, width = w_out.shape
        devices = mesh.shape["dp"]
        small = sections * 4 * head < width and sections > 1
        halves = devices & (devices - 1) == 0 and sections & (sections - 1) == 0
        body = local if small and halves else relay
        return jax.shard_map(
            body,
            mesh=mesh,
            in_specs=placed,
            out_specs=(P("section", ("dp", "group"), None), P("section", None)),
            check_vma=False,
        )(tokens_in, cotangent, gains, w_qkv, w_out, segments, plan)

    return chosen
```

```python
import math

import jax
import jax.numpy as jnp
from jax import lax
from jax.experimental import pallas as pl
from jax.experimental.pallas import tpu as pltpu
from jax.sharding import PartitionSpec as P

EPS = 1e-05
VMEM_BYTES = 24 * 1024 * 1024
SMALL = 16 * 1024 * 1024
F32 = jnp.float32
BF16 = jnp.bfloat16


def dot_nn(a, b):
    return lax.dot_general(a, b, (((1,), (0,)), ((), ())), preferred_element_type=F32)


def dot_nt(a, b):
    return lax.dot_general(a, b, (((1,), (1,)), ((), ())), preferred_element_type=F32)


def dot_tn(a, b):
    return lax.dot_general(a, b, (((0,), (0,)), ((), ())), preferred_element_type=F32)


IN_HBM = pl.BlockSpec(memory_space=pltpu.HBM)
ANYWHERE = pl.BlockSpec(memory_space=pl.ANY)
IN_VMEM = pl.BlockSpec(memory_space=pltpu.VMEM)
IN_SMEM = pl.BlockSpec(memory_space=pltpu.SMEM)


def in_hbm(array):
    return pltpu.with_memory_space_constraint(array, pltpu.HBM)


def in_vmem(array):
    return pltpu.with_memory_space_constraint(array, pltpu.VMEM)


def mover(sems):
    used = []

    def start(source, target):
        copy = pltpu.make_async_copy(source, target, sems.at[len(used)])
        copy.start()
        used.append(copy)
        return copy

    return start


def steps(width):
    step = min(width, 1024)
    return [slice(at, at + step) for at in range(0, width, step)]


def params(limit=VMEM_BYTES):
    return pltpu.CompilerParams(vmem_limit_bytes=limit)


def pick(tokens, plan, place, groups, out_layer, mine, slice_rows):
    rows, length, width = tokens.shape
    share = rows // groups

    def kernel(plan_ref, place_ref, mine_ref, tokens_ref, o_ref, *rest):
        slice_ref, parts = rest[0], rest[1 : 1 + groups]
        slice_in, rows_in, sems = rest[1 + groups :]
        start = mover(sems)
        at = pl.ds(pl.multiple_of(mine_ref[0] * slice_rows, slice_rows), slice_rows)
        loads = [(start(o_ref.at[at], slice_in), slice_in, slice_ref)]
        for r in range(groups):
            target = lax.rem(place_ref[0] + r, groups)
            for c in range(share):
                here = rows_in.at[r * share + c]
                row = plan_ref[0, target * share + c]
                loads.append((start(tokens_ref.at[row], here), here, parts[r].at[c]))
        stores = []
        for load, here, there in loads:
            load.wait()
            stores.append(start(here, there))
        for store in stores:
            store.wait()

    return pl.pallas_call(
        kernel,
        out_shape=[pltpu.HBM((slice_rows, width), BF16)]
        + [pltpu.HBM((share, length, width), BF16)] * groups,
        in_specs=[IN_SMEM, IN_SMEM, IN_SMEM, IN_HBM, IN_HBM],
        out_specs=[IN_HBM] * (1 + groups),
        scratch_shapes=[
            pltpu.VMEM((slice_rows, width), BF16),
            pltpu.VMEM((rows, length, width), BF16),
            pltpu.SemaphoreType.DMA((2 * rows + 2,)),
        ],
        compiler_params=params(),
        name="pick",
    )(plan, place, mine, in_hbm(tokens), in_hbm(out_layer))


def project(parts, cotangent, gain, w_layer, out_layer, place, after):
    groups = len(parts)
    tokens, width = cotangent.shape
    head = out_layer.shape[0]
    wide = w_layer.shape[1]
    block = tokens // groups
    cuts = steps(width)
    copies = len(cuts) * (groups + 4)

    def kernel(place_ref, *refs):
        part_refs = refs[:groups]
        cot_ref, g_ref, w_ref, o_ref = refs[groups : groups + 4]
        x_ref, xz_ref, n_ref = refs[groups + 4 + len(after) : groups + 7 + len(after)]
        x_in, c_in, w_in, o_in, sems = refs[groups + 7 + len(after) :]
        start = mover(sems)
        loads = []
        for cut in cuts:
            mine = [start(w_ref.at[cut], w_in.at[cut])]
            mine.append(start(o_ref.at[:, cut], o_in.at[:, cut]))
            for r in range(groups):
                source = lax.rem(place_ref[0] + groups - r, groups)
                rows = pl.ds(pl.multiple_of(source * block, block), block)
                mine.append(start(part_refs[r].at[:, cut], x_in.at[rows, cut]))
            mine.append(start(cot_ref.at[:, cut], c_in.at[:, cut]))
            loads.append(mine)
        through = jnp.zeros((tokens, wide), F32)
        across = jnp.zeros((tokens, head), F32)
        back = jnp.zeros((tokens, head), F32)
        square = jnp.zeros((tokens, 1), F32)
        stores = []
        for cut, mine in zip(cuts, loads):
            for load in mine:
                load.wait()
            stores.append(start(x_in.at[:, cut], x_ref.at[:, cut]))
            x = x_in[:, cut]
            xf = x.astype(F32)
            through += dot_nn((xf * g_ref[:, cut]).astype(BF16), w_in[cut, :])
            across += dot_nt(x, o_in[:, cut])
            back += dot_nt(c_in[:, cut], o_in[:, cut])
            square += jnp.sum(xf * xf, axis=1, keepdims=True)
        xz_ref[:, :wide] = through.astype(BF16)
        xz_ref[:, wide : wide + head] = across.astype(BF16)
        xz_ref[:, wide + head :] = back.astype(BF16)
        n_ref[...] = square
        for store in stores:
            store.wait()

    return pl.pallas_call(
        kernel,
        out_shape=[
            pltpu.HBM((tokens, width), BF16),
            jax.ShapeDtypeStruct((tokens, wide + 2 * head), BF16),
            jax.ShapeDtypeStruct((tokens, 1), F32),
        ],
        in_specs=[IN_SMEM]
        + [ANYWHERE] * groups
        + [IN_HBM, IN_VMEM, IN_HBM, IN_HBM]
        + [ANYWHERE] * len(after),
        out_specs=[IN_HBM, IN_VMEM, IN_VMEM],
        scratch_shapes=[
            pltpu.VMEM((tokens, width), BF16),
            pltpu.VMEM((tokens, width), BF16),
            pltpu.VMEM((width, wide), BF16),
            pltpu.VMEM((head, width), BF16),
            pltpu.SemaphoreType.DMA((copies,)),
        ],
        compiler_params=params(),
        name="project",
    )(
        place,
        *parts,
        in_hbm(cotangent),
        gain,
        in_hbm(w_layer),
        in_hbm(out_layer),
        *after,
    )


def couple(slices, gain, w_layer, out_layer, last, after):
    sections = len(slices)
    count, width = slices[0].shape
    head = out_layer.shape[0]
    wide = w_layer.shape[1]
    below = (sections - 2) * wide
    packed = below + max(wide, (sections - 1) * head)
    cuts = steps(width)
    copies = len(cuts) * (sections + 2) + sections - 1

    def kernel(last_ref, *refs):
        s_refs = refs[:sections][::-1]
        g_ref, w_ref, o_ref = refs[sections : sections + 3]
        out_ref, stack_ref, r_in, w_in, o_in, sems = refs[sections + 3 + len(after) :]
        rows = [slice(r * count, (r + 1) * count) for r in range(sections)]
        start = mover(sems)
        loads = []
        for cut in cuts:
            mine = [start(w_ref.at[cut], w_in.at[cut])]
            mine.append(start(o_ref.at[:, cut], o_in.at[:, cut]))
            for r in range(sections):
                mine.append(start(s_refs[r].at[:, cut], r_in.at[rows[r], cut]))
            loads.append(mine)
        through = jnp.zeros((sections * count, wide), F32)
        across = jnp.zeros((sections * count, head), F32)
        for cut, mine in zip(cuts, loads):
            for load in mine:
                load.wait()
            r = r_in[:, cut]
            through += dot_nn((r.astype(F32) * g_ref[:, cut]).astype(BF16), w_in[cut, :])
            across += dot_nt(r, o_in[:, cut])
        stores = [start(r_in.at[rows[r]], stack_ref.at[r - 1]) for r in range(1, sections)]
        through = through.astype(BF16)
        across = across.astype(BF16)
        out_ref[...] = jnp.zeros_like(out_ref)
        for r in range(1, sections - 1):
            out_ref[:, (r - 1) * wide : r * wide] = through[rows[r]]

        @pl.when(last_ref[0] == 1)
        def _():
            out_ref[:, below : below + wide] = through[rows[-1]]

        @pl.when(last_ref[0] == 0)
        def _():
            for r in range(sections - 1):
                out_ref[:, below + r * head : below + (r + 1) * head] = across[rows[r]]

        for store in stores:
            store.wait()

    return pl.pallas_call(
        kernel,
        out_shape=[
            jax.ShapeDtypeStruct((count, packed), BF16),
            pltpu.HBM((sections - 1, count, width), BF16),
        ],
        in_specs=[IN_SMEM]
        + [ANYWHERE] * sections
        + [IN_VMEM, IN_HBM, IN_HBM]
        + [ANYWHERE] * len(after),
        out_specs=[IN_VMEM, IN_HBM],
        scratch_shapes=[
            pltpu.VMEM((sections * count, width), BF16),
            pltpu.VMEM((width, wide), BF16),
            pltpu.VMEM((head, width), BF16),
            pltpu.SemaphoreType.DMA((copies,)),
        ],
        compiler_params=params(),
        name="couple",
    )(last, *slices[::-1], gain, in_hbm(w_layer), in_hbm(out_layer), *after)


def layout(sections, wide, head):
    through, across, at = {}, {}, 0
    for k in range(sections):
        for j in range(k):
            through[j, k] = slice(at, at + wide)
            at += wide
        for j in range(k + 1 if k < sections - 1 else 0):
            across[j, k] = slice(at, at + head)
            at += head
    return through, across, at


def compact(parts, section, wide, head, after):
    sections = len(parts)
    count = parts[0].shape[0]
    below = (sections - 2) * wide
    through, across, total = layout(sections, wide, head)

    def kernel(s_ref, *refs):
        part_refs, out_ref = refs[:sections], refs[-1]
        mine = s_ref[0]

        def fill(k, r):
            for j in range(k):
                at = (k - j - 1) * wide
                out_ref[0, :, through[j, k]] = part_refs[r][:, at : at + wide]
            for j in range(k + 1 if k < sections - 1 else 0):
                at = below + (k - j) * head
                out_ref[0, :, across[j, k]] = part_refs[r][:, at : at + head]

        for s in range(sections):

            @pl.when(mine == s)
            def _(s=s):
                for r in range(sections):
                    fill((s - r) % sections, r)

    vmem = pl.BlockSpec(memory_space=pltpu.VMEM)
    return pl.pallas_call(
        kernel,
        out_shape=jax.ShapeDtypeStruct((1, count, total), BF16),
        in_specs=[IN_SMEM] + [vmem] * sections + [ANYWHERE] * len(after),
        out_specs=vmem,
        compiler_params=params(SMALL),
        name="compact",
    )(section, *parts, *after)


def merge(first, second, after):
    count = first.shape[0]

    def kernel(first_ref, second_ref, *refs):
        refs[-1][:count] = first_ref[...]
        refs[-1][count:] = second_ref[...]

    return pl.pallas_call(
        kernel,
        out_shape=jax.ShapeDtypeStruct((2 * count,) + first.shape[1:], first.dtype),
        in_specs=[IN_VMEM] * 2 + [ANYWHERE] * len(after),
        out_specs=IN_VMEM,
        compiler_params=params(SMALL),
        name="merge",
    )(first, second, *after)


def serial(xz, pieces, places, norms, mask, section, gain, w_layer, out_layer, streams):
    sections = len(xz)
    tokens = norms.shape[0]
    head, width = out_layer.shape
    wide = 3 * head
    scale = 1.0 / math.sqrt(head)
    lead = slice(0, streams[-1].stop)
    through_at, across_at, _ = layout(sections, wide, head)
    count, packed = pieces[0].shape[-2:]
    plane = head // count
    n_in = sections + len(pieces)
    copies = sections + plane + 2

    def kernel(s_ref, p_ref, *refs):
        xz_refs, piece_refs = refs[:sections], refs[sections:n_in]
        n_ref, mask_ref, g_ref, w_ref, o_ref = refs[n_in : n_in + 5]
        n_out = n_in + 5
        v_ref, t_ref, a_ref = refs[n_out : n_out + 3]
        first_refs = refs[n_out + 3 : n_out + 3 + len(streams)]
        scratch = refs[n_out + 3 + len(streams) :]
        xz_all, table, mixes, weights, projs, dmix, w_in, o_in, sems = scratch
        mine = s_ref[0]
        started = []

        def start(source, target):
            copy = pltpu.make_async_copy(source, target, sems.at[len(started)])
            copy.start()
            started.append(copy)

        for r in range(sections):
            start(xz_refs[r], xz_all.at[mine ^ r])
        at = 0
        for ref in piece_refs:
            for i in range(ref.shape[0]):
                start(ref.at[i], table.at[p_ref[at]])
                at += 1
        small = list(started)
        start(w_ref.at[lead], w_in)
        start(o_ref.at[:, lead], o_in)
        for copy in small:
            copy.wait()

        def through(j, k):
            return table[:, :, through_at[j, k]].reshape(head, wide)

        def across(j, k):
            return table[:, :, across_at[j, k]].reshape(head, head)

        allowed = mask_ref[...] > 0.5
        norm = n_ref[...]
        rstds, tails, mixed = [], [], []
        for s in range(sections):
            proj = xz_all[s, :, :wide].astype(F32)
            for j in range(s):
                proj = proj + dot_nn(mixed[j], through(j, s))
            rstd = lax.rsqrt(norm * (1.0 / width) + EPS)
            proj = proj * rstd
            projs[s] = proj.astype(BF16)
            q, k, v = (projs[s, :, i * head : (i + 1) * head] for i in range(3))
            scores = jnp.where(allowed, dot_nt(q, k) * scale, -1e30)
            scores = jnp.exp(scores - jnp.max(scores, axis=1, keepdims=True))
            soft = scores / jnp.sum(scores, axis=1, keepdims=True)
            weights[s] = soft
            mix = dot_nn(soft.astype(BF16), v).astype(BF16)
            mixed.append(mix)
            mixes[:, s * head : (s + 1) * head] = mix
            rstds.append(rstd)
            dmix[:, s * head : (s + 1) * head] = xz_all[s, :, wide + head :].astype(F32)
            if s == sections - 1:
                break
            y = xz_all[s, :, wide : wide + head].astype(F32)
            for j in range(s):
                y = y + dot_nn(mixed[j], across(j, s))
            tail = y + dot_nn(mix, across(s, s))
            norm = norm + jnp.sum(mix.astype(F32) * (y + tail), axis=1, keepdims=True)
            norm = jnp.maximum(norm, 0.0)
            tails.append(tail)
        total = jnp.zeros((tokens, 1), F32)
        a_ref[...] = jnp.zeros_like(a_ref)
        for s in reversed(range(sections)):
            cols = slice(s * head, (s + 1) * head)
            da = dmix[:, cols]
            if s < sections - 1:
                da = da - total * tails[s]
            da = da.astype(BF16)
            q, k, v = (projs[s, :, i * head : (i + 1) * head] for i in range(3))
            soft = weights[s]
            dv = dot_tn(soft.astype(BF16), da)
            dsoft = dot_nt(da, v)
            dscore = soft * (dsoft - jnp.sum(dsoft * soft, axis=1, keepdims=True))
            dscore = (dscore * scale).astype(BF16)
            dproj = jnp.concatenate([dot_nn(dscore, k), dot_tn(dscore, q), dv], axis=1)
            along = jnp.sum(dproj * projs[s].astype(F32), axis=1, keepdims=True)
            first = (dproj * rstds[s]).astype(BF16)
            second = (-total * mixes[:, cols].astype(F32)).astype(BF16)
            total = total + rstds[s] * rstds[s] * along * (1.0 / width)
            for j in reversed(range(s)):
                term = dot_nt(first, through(j, s))
                if s < sections - 1:
                    term = term + dot_nt(second, across(j, s))
                dmix[:, j * head : (j + 1) * head] += term

            @pl.when(mine == s)
            def _(first=first, second=second, total=total):
                v_ref[:, :wide] = first
                v_ref[:, wide:] = second
                t_ref[...] = total

            for r in range(1, sections - s):

                @pl.when(mine == s + r)
                def _(r=r, cols=cols):
                    a_ref[:, (r - 1) * head : r * head] = mixes[:, cols]

        for copy in started[len(small) :]:
            copy.wait()
        own = dot_nt(v_ref[:, :wide], w_in[...]) * g_ref[:, lead]
        own = (own + dot_nn(v_ref[:, wide:], o_in[...])).astype(BF16)
        for ref, part in zip(first_refs, streams):
            ref[...] = own[:, part]

    vmem = pl.BlockSpec(memory_space=pltpu.VMEM)
    smem = pl.BlockSpec(memory_space=pltpu.SMEM)
    return pl.pallas_call(
        kernel,
        out_shape=[
            pltpu.VMEM((tokens, wide + head), BF16),
            pltpu.VMEM((tokens, 1), F32),
            pltpu.VMEM((tokens, (sections - 1) * head), BF16),
        ]
        + [pltpu.VMEM((tokens, part.stop - part.start), BF16) for part in streams],
        in_specs=[smem, smem] + [ANYWHERE] * n_in + [vmem, vmem, vmem, IN_HBM, IN_HBM],
        out_specs=[vmem] * (3 + len(streams)),
        scratch_shapes=[
            pltpu.VMEM((sections,) + xz[0].shape, BF16),
            pltpu.VMEM((plane, count, packed), BF16),
            pltpu.VMEM((tokens, sections * head), BF16),
            pltpu.VMEM((sections, tokens, tokens), F32),
            pltpu.VMEM((sections, tokens, wide), BF16),
            pltpu.VMEM((tokens, sections * head), F32),
            pltpu.VMEM((lead.stop, wide), BF16),
            pltpu.VMEM((head, lead.stop), BF16),
            pltpu.SemaphoreType.DMA((copies,)),
        ],
        compiler_params=params(),
        name="serial",
    )(
        section,
        places,
        *xz,
        *pieces,
        norms,
        mask,
        gain,
        in_hbm(w_layer),
        in_hbm(out_layer),
    )


def hold(array, after):
    def kernel(*refs):
        pass

    return pl.pallas_call(
        kernel,
        out_shape=jax.ShapeDtypeStruct(array.shape, array.dtype),
        in_specs=[ANYWHERE] * (1 + len(after)),
        out_specs=ANYWHERE,
        input_output_aliases={0: 0},
        compiler_params=params(SMALL),
        name="hold",
    )(array, *after)


def gather_two(first, second, after):
    count = first.shape[0]

    def kernel(first_ref, second_ref, *refs):
        out_ref, sems = refs[len(after) :]
        start = mover(sems)
        copies = [start(first_ref, out_ref.at[:count]), start(second_ref, out_ref.at[count:])]
        for copy in copies:
            copy.wait()

    return pl.pallas_call(
        kernel,
        out_shape=jax.ShapeDtypeStruct((2 * count,) + first.shape[1:], first.dtype),
        in_specs=[ANYWHERE] * (2 + len(after)),
        out_specs=IN_VMEM,
        scratch_shapes=[pltpu.SemaphoreType.DMA((2,))],
        compiler_params=params(SMALL),
        name="gather_two",
    )(first, second, *after)


def widen(sent, gain, w_layer, out_layer, chunk):
    tokens = sent.shape[0]
    head, width = out_layer.shape
    wide = w_layer.shape[1]
    cuts = [slice(at, at + chunk) for at in range(0, width, chunk)]

    def kernel(v_ref, g_ref, w_ref, o_ref, back_ref, pair_ref, back_in, w_in, o_in, sems):
        start = mover(sems)
        loads = [
            (start(w_ref.at[cut], w_in.at[cut]), start(o_ref.at[:, cut], o_in.at[:, cut]))
            for cut in cuts
        ]
        stores = []
        for i, (cut, mine) in enumerate(zip(cuts, loads)):
            for load in mine:
                load.wait()
            back = dot_nt(v_ref[:, :wide], w_in[cut, :])
            own = back * g_ref[:, cut] + dot_nn(v_ref[:, wide:], o_in[:, cut])
            back_in[:, cut] = back.astype(BF16)
            stores.append(start(back_in.at[:, cut], back_ref.at[:, cut]))
            pair_ref[0, i] = own.astype(BF16)
            pair_ref[1, i] = jnp.zeros_like(pair_ref[1, i])
        for store in stores:
            store.wait()

    return pl.pallas_call(
        kernel,
        out_shape=[
            pltpu.HBM((tokens, width), BF16),
            pltpu.VMEM((2, len(cuts), tokens, chunk), BF16),
        ],
        in_specs=[IN_VMEM, IN_VMEM, IN_HBM, IN_HBM],
        out_specs=[IN_HBM, IN_VMEM],
        scratch_shapes=[
            pltpu.VMEM((tokens, width), BF16),
            pltpu.VMEM((width, wide), BF16),
            pltpu.VMEM((head, width), BF16),
            pltpu.SemaphoreType.DMA((3 * len(cuts),)),
        ],
        compiler_params=params(),
        name="widen",
    )(in_vmem(sent), gain, in_hbm(w_layer), in_hbm(out_layer))


def settle(total, mixes, stacks, places, x, cotangent, back, chunk):
    tokens, width = x.shape
    layers, rows = stacks[0].shape[1:3]
    entries = [(i, e) for i, stack in enumerate(stacks) for e in range(stack.shape[0])]
    plane = len(entries)
    head = plane * rows
    cuts = [slice(at, at + chunk) for at in range(0, width, chunk)]
    copies = plane * layers + 3 * len(cuts)

    def kernel(p_ref, t_ref, a_ref, x_ref, c_ref, back_ref, *refs):
        stack_refs = refs[: len(stacks)]
        rest_ref, dg_ref = refs[len(stacks) : len(stacks) + 2]
        lower, x_in, c_in, back_in, sems = refs[len(stacks) + 2 :]
        start = mover(sems)
        first = []
        for at, (i, e) in enumerate(entries):
            for r in range(layers):
                first.append(start(stack_refs[i].at[e, r], lower.at[r, p_ref[at]]))
        loads = []
        for cut in cuts:
            mine = [start(x_ref.at[:, cut], x_in.at[:, cut])]
            mine.append(start(c_ref.at[:, cut], c_in.at[:, cut]))
            mine.append(start(back_ref.at[:, cut], back_in.at[:, cut]))
            loads.append(mine)
        for load in first:
            load.wait()
        for i, (cut, mine) in enumerate(zip(cuts, loads)):
            for load in mine:
                load.wait()
            below = lower[:, :, :, cut].reshape(layers * head, chunk)
            here = x_in[:, cut].astype(F32) + dot_nn(a_ref[...], below)
            rest_ref[i] = (c_in[:, cut].astype(F32) - t_ref[...] * here).astype(BF16)
            gain = jnp.sum(back_in[:, cut].astype(F32) * here, axis=0, keepdims=True)
            for at in range(0, chunk, head):
                row = (cut.start + at) // head
                dg_ref[row : row + 1, :] = gain[:, at : at + head]

    return pl.pallas_call(
        kernel,
        out_shape=[
            pltpu.VMEM((len(cuts), tokens, chunk), BF16),
            pltpu.VMEM((width // head, head), F32),
        ],
        in_specs=[IN_SMEM] + [IN_VMEM] * 2 + [IN_HBM] * (3 + len(stacks)),
        out_specs=[IN_VMEM] * 2,
        scratch_shapes=[
            pltpu.VMEM((layers, plane, rows, width), BF16),
            pltpu.VMEM((tokens, width), BF16),
            pltpu.VMEM((tokens, width), BF16),
            pltpu.VMEM((tokens, width), BF16),
            pltpu.SemaphoreType.DMA((copies,)),
        ],
        compiler_params=params(),
        name="settle",
    )(
        places,
        in_vmem(total),
        in_vmem(mixes),
        *[in_hbm(array) for array in (x, cotangent, back, *stacks)],
    )


def join(index, arrived, pair, cols, after):
    tokens, part = arrived.shape

    def kernel(i_ref, r_ref, _, *refs):
        send_ref, pair_ref = refs[len(after) :]
        at = i_ref[0]
        r = r_ref[...]
        send_ref[...] = (pair_ref[0, at, :, cols].astype(F32) + r.astype(F32)).astype(BF16)
        pair_ref[1, at, :, cols] = r

    return pl.pallas_call(
        kernel,
        out_shape=[pltpu.VMEM((tokens, part), BF16), pltpu.VMEM(pair.shape, BF16)],
        in_specs=[IN_SMEM] + [IN_VMEM] * 2 + [ANYWHERE] * len(after),
        out_specs=[IN_VMEM] * 2,
        input_output_aliases={2: 1},
        compiler_params=params(SMALL),
        name="join",
    )(index, in_vmem(arrived), in_vmem(pair), *after)


def finish(index, arrived, pair, rest, streams):
    _, count, tokens, chunk = pair.shape

    def kernel(i_ref, *refs):
        r_refs = refs[: len(streams)]
        pair_ref, rest_ref, whole_ref, whole, sems = refs[len(streams) :]
        at = i_ref[0]
        copies = []
        for i in range(count):
            full = rest_ref[i].astype(F32) + pair_ref[0, i].astype(F32)
            whole[i] = (full + pair_ref[1, i].astype(F32)).astype(BF16)

            @pl.when(at == i)
            def _(i=i, full=full):
                for ref, cols in zip(r_refs, streams):
                    whole[i, :, cols] = (full[:, cols] + ref[...].astype(F32)).astype(BF16)

            there = whole_ref.at[:, pl.ds(i * chunk, chunk)]
            copies.append(pltpu.make_async_copy(whole.at[i], there, sems.at[i]))
            copies[-1].start()
        for copy in copies:
            copy.wait()

    return pl.pallas_call(
        kernel,
        out_shape=pltpu.HBM((tokens, count * chunk), BF16),
        in_specs=[IN_SMEM] + [IN_VMEM] * (len(streams) + 2),
        out_specs=IN_HBM,
        scratch_shapes=[
            pltpu.VMEM((count, tokens, chunk), BF16),
            pltpu.SemaphoreType.DMA((count,)),
        ],
        compiler_params=params(SMALL),
        name="finish",
    )(index, *[in_vmem(array) for array in arrived], in_vmem(pair), in_vmem(rest))


def added(arrays):
    def kernel(*refs):
        total = refs[0][...]
        for ref in refs[1:-1]:
            total = total + ref[...]
        refs[-1][...] = total

    return pl.pallas_call(
        kernel,
        out_shape=pltpu.VMEM(arrays[0].shape, F32),
        in_specs=[IN_VMEM] * len(arrays),
        out_specs=IN_VMEM,
        compiler_params=params(SMALL),
        name="added",
    )(*[in_vmem(array) for array in arrays])


STREAMS = 2
CHUNKS = 4


def stream_columns(chunk):
    lanes = 128
    tiles = chunk // lanes
    ends = [-(-tiles * (i + 1) // STREAMS) * lanes for i in range(STREAMS)]
    return [slice(start, end) for start, end in zip([0] + ends, ends)]


def shifted(array, by):
    sections = lax.axis_size("section")
    return lax.ppermute(array, "section", [(i, (i + by) % sections) for i in range(sections)])


def raised(array, by):
    sections = lax.axis_size("section")
    return lax.ppermute(array, "section", [(i, i + by) for i in range(sections - by)])


def swapped(array, step):
    groups = lax.axis_size("group")
    devices = lax.axis_size("dp")
    bits = devices.bit_length() - 1
    pairs = []
    for p in range(devices):
        for g in range(groups):
            pairs.append((p * groups + g, (p ^ (1 << ((step + g) % bits))) * groups + g))
    return lax.ppermute(array, ("dp", "group"), pairs)


def handed(array, by):
    groups = lax.axis_size("group")
    return lax.ppermute(array, "group", [(i, (i + by) % groups) for i in range(groups)])


def plane_places():
    groups = lax.axis_size("group")
    bits = lax.axis_size("dp").bit_length() - 1
    masks = []
    for g in range(groups):
        order = [0]
        for step in range(bits):
            order = order + [m ^ (1 << ((step + g) % bits)) for m in order]
        masks.append(order)
    masks = jnp.asarray(masks, jnp.int32)
    dp, member = lax.axis_index("dp"), lax.axis_index("group")
    places = []
    for r in range(groups):
        giver = (member + groups - r) % groups
        places.append((dp ^ masks[giver]) * groups + giver)
    return jnp.concatenate(places).astype(jnp.int32)


def local(tokens_in, cotangent, gains, w_qkv, w_out, segments, plan):
    sections = lax.axis_size("section")
    groups = lax.axis_size("group")
    devices = lax.axis_size("dp")
    plane = devices * groups
    section = lax.axis_index("section")
    member = lax.axis_index("group")
    rows_dev = plan.shape[1]
    length = segments.shape[1]
    tokens, width = tokens_in.shape
    head = w_out.shape[1]
    share = rows_dev // groups
    w_layer, out_layer = w_qkv[0], w_out[0]
    place = member.astype(jnp.int32)[None]
    layer = section.astype(jnp.int32)[None]

    slice_rows = head // plane
    mine = lax.axis_index("dp") * groups + member
    own_rows, *parts = pick(
        tokens_in.reshape(rows_dev, length, width),
        plan,
        place,
        groups,
        out_layer,
        mine.astype(jnp.int32)[None],
        slice_rows,
    )
    slices = [raised(own_rows, r) for r in range(sections - 1, 0, -1)]
    slices = [own_rows] + slices[::-1]
    chosen = jnp.take(segments, plan[0], axis=0, mode="clip").astype(BF16)
    chosen = chosen.reshape(groups, share, length)
    moved, moved_seg = [], []
    for r in range(groups):
        outgoing = lax.dynamic_index_in_dim(chosen, (member + r) % groups, 0, keepdims=False)
        moved.append(handed(parts[r], r) if r else parts[r])
        moved_seg.append(handed(outgoing, r) if r else outgoing)
    moved = [part.reshape(share * length, width) for part in moved]
    order = (member - jnp.arange(groups)) % groups
    seg = jnp.take(jnp.stack(moved_seg), order, axis=0, mode="clip").reshape(tokens)
    at = jnp.arange(tokens)
    mask = (
        (at[:, None] >= at[None, :])
        & (at[:, None] // length == at[None, :] // length)
        & (seg[:, None] == seg[None, :])
    ).astype(F32)

    last = (section == sections - 1).astype(jnp.int32)[None]
    bits = devices.bit_length() - 1
    places = plane_places()
    x, xz, norms = project(
        moved, cotangent, gains, w_layer, out_layer, place, []
    )
    coupling, stack = couple(slices, gains, w_layer, out_layer, last, [mask, places, xz])
    others = [shifted(coupling, r) for r in range(1, sections)]

    streams = stream_columns(width // CHUNKS)

    def facing(array, by):
        return lax.ppermute(array, "section", [(i, i ^ by) for i in range(sections)])

    arrays, masks, by = [hold(xz, others)], [0], sections // 2
    while by > 0:
        arrays = arrays + [facing(array, by) for array in arrays]
        masks = masks + [mask_of ^ by for mask_of in masks]
        by = by // 2
    xz_all = [arrays[masks.index(r)] for r in range(sections)]
    early = [xz_all[r] for r in range(1, sections) if r & (r - 1) == 0]
    late = [xz_all[r] for r in range(1, sections) if r & (r - 1) != 0]
    pieces = [compact([coupling] + others, layer, 3 * head, head, [xz])]

    rows = [stack[None]]
    for step in range(bits):
        if step > 0:
            pieces = [merge(*pieces, early)]
        pieces = pieces + [swapped(pieces[0], step)]
        if step == bits - 1:
            pieces[-1] = hold(pieces[-1], late)
        if step > 0:
            rows = [gather_two(*rows, pieces[-1:])]
        rows = rows + [swapped(rows[0], step)]
    pieces = pieces + [handed(array, r) for r in range(1, groups) for array in pieces]
    sent, total, mixes, *leaving = serial(
        xz_all, pieces, places, norms, mask, layer, gains, w_layer, out_layer, streams
    )
    back, pair = widen(sent, gains, w_layer, out_layer, width // CHUNKS)

    down = [(i, i - 1) for i in range(1, sections)]
    behind = sections - 1 - section

    def index(tick):
        return jnp.clip(tick - behind, 0, CHUNKS - 1).astype(jnp.int32)[None]

    def lowered(arrays):
        return [lax.ppermute(array, "section", down) for array in arrays]

    def crossed(array, by):
        return lax.ppermute(array, "dp", [(p, p ^ by) for p in range(devices)])

    ticks = CHUNKS + sections - 1
    after = {}
    for tick in range(1, ticks):
        arrived = lowered(leaving)
        if tick < ticks - 1:
            for i, cols in enumerate(streams):
                leaving[i], pair = join(
                    index(tick), arrived[i], pair, cols, after.get(tick, [])
                )
        if tick == 1:
            rows = [hold(array, leaving) for array in rows]
            rows = rows + [handed(array, r) for r in range(1, groups) for array in rows]
            rest, gain = settle(
                total, mixes, rows, places, x, cotangent, back, width // CHUNKS
            )
            crossing = [crossed(gain, by) for by in range(1, devices)]
            gain_chip = added([gain] + crossing)
            gain_whole = added([gain_chip] + [handed(gain_chip, r) for r in range(1, groups)])
            gain_whole = gain_whole.reshape(1, width)
            after = {2: [gain], 3: crossing[: devices // 2], 4: [gain_chip], 5: [gain_whole]}
    out = finish(index(ticks - 1), arrived, pair, rest, streams)
    return (out[None], gain_whole)


def attend(hidden, segment, gain_row, w_layer, out_layer):
    count, length, width = hidden.shape
    head = out_layer.shape[0]
    scaled = hidden * lax.rsqrt(jnp.mean(hidden * hidden, axis=-1, keepdims=True) + EPS) * gain_row
    normed = scaled.astype(BF16).reshape(count * length, width)
    projected = jnp.dot(normed, w_layer, preferred_element_type=F32).reshape(count, length, 3 * head)
    query = projected[:, :, :head]
    keyed = projected[:, :, head : 2 * head]
    valued = projected[:, :, 2 * head :]
    positions = jnp.arange(length)
    allowed = (positions[:, None] >= positions[None, :])[None] & (
        segment[:, :, None] == segment[:, None, :]
    )
    scores = jnp.einsum("rid,rjd->rij", query, keyed, precision=lax.Precision.HIGHEST)
    scores = jnp.where(allowed, scores / math.sqrt(head), -1e30)
    weights = jax.nn.softmax(scores, axis=-1)
    mixed = jnp.einsum("rij,rjd->rid", weights, valued, precision=lax.Precision.HIGHEST)
    mixed = mixed.astype(BF16).reshape(count * length, head)
    output = jnp.dot(mixed, out_layer, preferred_element_type=F32).reshape(count, length, width)
    return hidden + output


MB_ROWS = 2


def relay(tokens_in, cotangent, gains, w_qkv, w_out, segments, plan):
    sections = lax.axis_size("section")
    section = lax.axis_index("section")
    rows_dev = plan.shape[1]
    width = tokens_in.shape[1]
    length = segments.shape[1]
    micro = rows_dev // MB_ROWS
    blocks = tokens_in.reshape(rows_dev, length, width)
    chosen = jnp.take(blocks, plan[0], axis=0)
    chosen_seg = jnp.take(segments, plan[0], axis=0).astype(BF16)
    assigned = lax.all_to_all(chosen, "group", split_axis=0, concat_axis=0, tiled=True)
    moved_seg = lax.all_to_all(chosen_seg, "group", split_axis=0, concat_axis=0, tiled=True)
    assigned = assigned.reshape(micro, MB_ROWS, length, width)
    seg_groups = moved_seg.reshape(micro, MB_ROWS, length)
    gain_row, w_layer, out_layer = gains[0], w_qkv[0], w_out[0]
    grad_rows = cotangent.reshape(micro, MB_ROWS, length, width)
    ticks = micro + sections - 1

    def passed_along(array, by):
        pairs = [(i, i + by) for i in range(sections) if 0 <= i + by < sections]
        return lax.ppermute(array, "section", pairs)

    def at(array, i):
        return lax.dynamic_index_in_dim(array, i, 0, keepdims=False)

    def forward_tick(tick, carry):
        saved, arrived = carry
        index = tick - section
        valid = (index >= 0) & (index < micro)
        clipped = jnp.clip(index, 0, micro - 1)
        entering = jnp.where(section == 0, at(assigned, clipped), arrived)
        kept = jnp.where(valid, entering, at(saved, clipped))
        saved = lax.dynamic_update_index_in_dim(saved, kept, clipped, 0)
        segment = at(seg_groups, clipped)

        def run_layer(value):
            return attend(value.astype(F32), segment, gain_row, w_layer, out_layer).astype(BF16)

        leaving = lax.cond(valid, run_layer, jnp.zeros_like, entering)
        return (saved, passed_along(leaving, 1))

    saved_init = jnp.zeros((micro, MB_ROWS, length, width), BF16)
    arrive_init = jnp.zeros((MB_ROWS, length, width), BF16)
    saved, _ = lax.fori_loop(0, ticks, forward_tick, (saved_init, arrive_init))

    def backward_tick(tick, carry):
        grads_x, gain_total, arrived = carry
        index = tick - (sections - 1 - section)
        valid = (index >= 0) & (index < micro)
        clipped = jnp.clip(index, 0, micro - 1)
        entering = jnp.where(section == sections - 1, at(grad_rows, clipped), arrived)
        segment = at(seg_groups, clipped)
        stored = at(saved, clipped).astype(F32)

        def local_layer(hidden, gains_here):
            return attend(hidden, segment, gains_here, w_layer, out_layer)

        def run_back(value):
            _, pullback = jax.vjp(local_layer, stored, gain_row)
            grad_hidden, grad_gain = pullback(value.astype(F32))
            return (grad_hidden.astype(BF16), grad_gain)

        def skip_back(value):
            return (jnp.zeros_like(value), jnp.zeros(gain_row.shape, F32))

        sending, grad_gain = lax.cond(valid, run_back, skip_back, entering)
        kept = jnp.where(valid, sending, at(grads_x, clipped))
        grads_x = lax.dynamic_update_index_in_dim(grads_x, kept, clipped, 0)
        return (grads_x, gain_total + grad_gain, passed_along(sending, -1))

    gain_init = jnp.zeros(gain_row.shape, F32)
    grads_x, gain_total, _ = lax.fori_loop(
        0, ticks, backward_tick, (saved_init, gain_init, arrive_init)
    )
    gain_whole = lax.psum(gain_total, ("dp", "group"))
    return (grads_x.reshape(1, rows_dev * length, width), gain_whole[None])


def solution(mesh):
    placed = (
        P(("dp", "group"), None),
        P(("dp", "group"), None),
        P("section", None),
        P("section", None, None),
        P("section", None, None),
        P(("dp", "group"), None),
        P(("dp", "group"), None),
    )

    def chosen(tokens_in, cotangent, gains, w_qkv, w_out, segments, plan):
        sections, head, width = w_out.shape
        devices = mesh.shape["dp"]
        small = sections * 4 * head < width and sections > 1
        halves = devices & (devices - 1) == 0 and sections & (sections - 1) == 0
        body = local if small and halves else relay
        return jax.shard_map(
            body,
            mesh=mesh,
            in_specs=placed,
            out_specs=(P("section", ("dp", "group"), None), P("section", None)),
            check_vma=False,
        )(tokens_in, cotangent, gains, w_qkv, w_out, segments, plan)

    return chosen
```

```python
import math

import jax
import jax.numpy as jnp
from jax import lax
from jax.experimental import pallas as pl
from jax.experimental.pallas import tpu as pltpu
from jax.sharding import PartitionSpec as P

EPS = 1e-05
VMEM_BYTES = 24 * 1024 * 1024
SMALL = 16 * 1024 * 1024
F32 = jnp.float32
BF16 = jnp.bfloat16


def dot_nn(a, b):
    return lax.dot_general(a, b, (((1,), (0,)), ((), ())), preferred_element_type=F32)


def dot_nt(a, b):
    return lax.dot_general(a, b, (((1,), (1,)), ((), ())), preferred_element_type=F32)


def dot_tn(a, b):
    return lax.dot_general(a, b, (((0,), (0,)), ((), ())), preferred_element_type=F32)


IN_HBM = pl.BlockSpec(memory_space=pltpu.HBM)
ANYWHERE = pl.BlockSpec(memory_space=pl.ANY)
IN_VMEM = pl.BlockSpec(memory_space=pltpu.VMEM)
IN_SMEM = pl.BlockSpec(memory_space=pltpu.SMEM)


def in_hbm(array):
    return pltpu.with_memory_space_constraint(array, pltpu.HBM)


def in_vmem(array):
    return pltpu.with_memory_space_constraint(array, pltpu.VMEM)


def mover(sems):
    used = []

    def start(source, target):
        copy = pltpu.make_async_copy(source, target, sems.at[len(used)])
        copy.start()
        used.append(copy)
        return copy

    return start


def steps(width):
    step = min(width, 1024)
    return [slice(at, at + step) for at in range(0, width, step)]


def params(limit=VMEM_BYTES):
    return pltpu.CompilerParams(vmem_limit_bytes=limit)


def pick(tokens, plan, place, groups, out_layer, mine, slice_rows):
    rows, length, width = tokens.shape
    share = rows // groups

    def kernel(plan_ref, place_ref, mine_ref, tokens_ref, o_ref, *rest):
        slice_ref, parts = rest[0], rest[1 : 1 + groups]
        slice_in, rows_in, sems = rest[1 + groups :]
        start = mover(sems)
        at = pl.ds(pl.multiple_of(mine_ref[0] * slice_rows, slice_rows), slice_rows)
        loads = [(start(o_ref.at[at], slice_in), slice_in, slice_ref)]
        for r in range(groups):
            target = lax.rem(place_ref[0] + r, groups)
            for c in range(share):
                here = rows_in.at[r * share + c]
                row = plan_ref[0, target * share + c]
                loads.append((start(tokens_ref.at[row], here), here, parts[r].at[c]))
        stores = []
        for load, here, there in loads:
            load.wait()
            stores.append(start(here, there))
        for store in stores:
            store.wait()

    return pl.pallas_call(
        kernel,
        out_shape=[pltpu.HBM((slice_rows, width), BF16)]
        + [pltpu.HBM((share, length, width), BF16)] * groups,
        in_specs=[IN_SMEM, IN_SMEM, IN_SMEM, IN_HBM, IN_HBM],
        out_specs=[IN_HBM] * (1 + groups),
        scratch_shapes=[
            pltpu.VMEM((slice_rows, width), BF16),
            pltpu.VMEM((rows, length, width), BF16),
            pltpu.SemaphoreType.DMA((2 * rows + 2,)),
        ],
        compiler_params=params(),
        name="pick",
    )(plan, place, mine, in_hbm(tokens), in_hbm(out_layer))


def project(parts, cotangent, gain, w_layer, out_layer, place, after):
    groups = len(parts)
    tokens, width = cotangent.shape
    head = out_layer.shape[0]
    wide = w_layer.shape[1]
    block = tokens // groups
    cuts = steps(width)
    copies = len(cuts) * (groups + 4)

    def kernel(place_ref, *refs):
        part_refs = refs[:groups]
        cot_ref, g_ref, w_ref, o_ref = refs[groups : groups + 4]
        x_ref, xz_ref, n_ref = refs[groups + 4 + len(after) : groups + 7 + len(after)]
        x_in, c_in, w_in, o_in, sems = refs[groups + 7 + len(after) :]
        start = mover(sems)
        loads = []
        for cut in cuts:
            mine = [start(w_ref.at[cut], w_in.at[cut])]
            mine.append(start(o_ref.at[:, cut], o_in.at[:, cut]))
            for r in range(groups):
                source = lax.rem(place_ref[0] + groups - r, groups)
                rows = pl.ds(pl.multiple_of(source * block, block), block)
                mine.append(start(part_refs[r].at[:, cut], x_in.at[rows, cut]))
            mine.append(start(cot_ref.at[:, cut], c_in.at[:, cut]))
            loads.append(mine)
        through = jnp.zeros((tokens, wide), F32)
        across = jnp.zeros((tokens, head), F32)
        back = jnp.zeros((tokens, head), F32)
        square = jnp.zeros((tokens, 1), F32)
        stores = []
        for cut, mine in zip(cuts, loads):
            for load in mine:
                load.wait()
            stores.append(start(x_in.at[:, cut], x_ref.at[:, cut]))
            x = x_in[:, cut]
            xf = x.astype(F32)
            through += dot_nn((xf * g_ref[:, cut]).astype(BF16), w_in[cut, :])
            across += dot_nt(x, o_in[:, cut])
            back += dot_nt(c_in[:, cut], o_in[:, cut])
            square += jnp.sum(xf * xf, axis=1, keepdims=True)
        xz_ref[:, :wide] = through.astype(BF16)
        xz_ref[:, wide : wide + head] = across.astype(BF16)
        xz_ref[:, wide + head :] = back.astype(BF16)
        n_ref[...] = square
        for store in stores:
            store.wait()

    return pl.pallas_call(
        kernel,
        out_shape=[
            pltpu.HBM((tokens, width), BF16),
            jax.ShapeDtypeStruct((tokens, wide + 2 * head), BF16),
            jax.ShapeDtypeStruct((tokens, 1), F32),
        ],
        in_specs=[IN_SMEM]
        + [ANYWHERE] * groups
        + [IN_HBM, IN_VMEM, IN_HBM, IN_HBM]
        + [ANYWHERE] * len(after),
        out_specs=[IN_HBM, IN_VMEM, IN_VMEM],
        scratch_shapes=[
            pltpu.VMEM((tokens, width), BF16),
            pltpu.VMEM((tokens, width), BF16),
            pltpu.VMEM((width, wide), BF16),
            pltpu.VMEM((head, width), BF16),
            pltpu.SemaphoreType.DMA((copies,)),
        ],
        compiler_params=params(),
        name="project",
    )(
        place,
        *parts,
        in_hbm(cotangent),
        gain,
        in_hbm(w_layer),
        in_hbm(out_layer),
        *after,
    )


def couple(slices, gain, w_layer, out_layer, last, after):
    sections = len(slices)
    count, width = slices[0].shape
    head = out_layer.shape[0]
    wide = w_layer.shape[1]
    below = (sections - 2) * wide
    packed = below + max(wide, (sections - 1) * head)
    cuts = steps(width)
    copies = len(cuts) * (sections + 2) + sections - 1

    def kernel(last_ref, *refs):
        s_refs = refs[:sections][::-1]
        g_ref, w_ref, o_ref = refs[sections : sections + 3]
        out_ref, stack_ref, r_in, w_in, o_in, sems = refs[sections + 3 + len(after) :]
        rows = [slice(r * count, (r + 1) * count) for r in range(sections)]
        start = mover(sems)
        loads = []
        for cut in cuts:
            mine = [start(w_ref.at[cut], w_in.at[cut])]
            mine.append(start(o_ref.at[:, cut], o_in.at[:, cut]))
            for r in range(sections):
                mine.append(start(s_refs[r].at[:, cut], r_in.at[rows[r], cut]))
            loads.append(mine)
        through = jnp.zeros((sections * count, wide), F32)
        across = jnp.zeros((sections * count, head), F32)
        for cut, mine in zip(cuts, loads):
            for load in mine:
                load.wait()
            r = r_in[:, cut]
            through += dot_nn((r.astype(F32) * g_ref[:, cut]).astype(BF16), w_in[cut, :])
            across += dot_nt(r, o_in[:, cut])
        stores = [start(r_in.at[rows[r]], stack_ref.at[r - 1]) for r in range(1, sections)]
        through = through.astype(BF16)
        across = across.astype(BF16)
        out_ref[...] = jnp.zeros_like(out_ref)
        for r in range(1, sections - 1):
            out_ref[:, (r - 1) * wide : r * wide] = through[rows[r]]

        @pl.when(last_ref[0] == 1)
        def _():
            out_ref[:, below : below + wide] = through[rows[-1]]

        @pl.when(last_ref[0] == 0)
        def _():
            for r in range(sections - 1):
                out_ref[:, below + r * head : below + (r + 1) * head] = across[rows[r]]

        for store in stores:
            store.wait()

    return pl.pallas_call(
        kernel,
        out_shape=[
            jax.ShapeDtypeStruct((count, packed), BF16),
            pltpu.HBM((sections - 1, count, width), BF16),
        ],
        in_specs=[IN_SMEM]
        + [ANYWHERE] * sections
        + [IN_VMEM, IN_HBM, IN_HBM]
        + [ANYWHERE] * len(after),
        out_specs=[IN_VMEM, IN_HBM],
        scratch_shapes=[
            pltpu.VMEM((sections * count, width), BF16),
            pltpu.VMEM((width, wide), BF16),
            pltpu.VMEM((head, width), BF16),
            pltpu.SemaphoreType.DMA((copies,)),
        ],
        compiler_params=params(),
        name="couple",
    )(last, *slices[::-1], gain, in_hbm(w_layer), in_hbm(out_layer), *after)


def layout(sections, wide, head):
    through, across, at = {}, {}, 0
    for k in range(sections):
        for j in range(k):
            through[j, k] = slice(at, at + wide)
            at += wide
        for j in range(k + 1 if k < sections - 1 else 0):
            across[j, k] = slice(at, at + head)
            at += head
    return through, across, at


def compact(parts, section, wide, head, after):
    sections = len(parts)
    count = parts[0].shape[0]
    below = (sections - 2) * wide
    through, across, total = layout(sections, wide, head)

    def kernel(s_ref, *refs):
        part_refs, out_ref = refs[:sections], refs[-1]
        mine = s_ref[0]

        def fill(k, r):
            for j in range(k):
                at = (k - j - 1) * wide
                out_ref[0, :, through[j, k]] = part_refs[r][:, at : at + wide]
            for j in range(k + 1 if k < sections - 1 else 0):
                at = below + (k - j) * head
                out_ref[0, :, across[j, k]] = part_refs[r][:, at : at + head]

        for s in range(sections):

            @pl.when(mine == s)
            def _(s=s):
                for r in range(sections):
                    fill((s - r) % sections, r)

    vmem = pl.BlockSpec(memory_space=pltpu.VMEM)
    return pl.pallas_call(
        kernel,
        out_shape=jax.ShapeDtypeStruct((1, count, total), BF16),
        in_specs=[IN_SMEM] + [vmem] * sections + [ANYWHERE] * len(after),
        out_specs=vmem,
        compiler_params=params(SMALL),
        name="compact",
    )(section, *parts, *after)


def merge(first, second, after):
    count = first.shape[0]

    def kernel(first_ref, second_ref, *refs):
        refs[-1][:count] = first_ref[...]
        refs[-1][count:] = second_ref[...]

    return pl.pallas_call(
        kernel,
        out_shape=jax.ShapeDtypeStruct((2 * count,) + first.shape[1:], first.dtype),
        in_specs=[IN_VMEM] * 2 + [ANYWHERE] * len(after),
        out_specs=IN_VMEM,
        compiler_params=params(SMALL),
        name="merge",
    )(first, second, *after)


def serial(xz, pieces, places, norms, mask, section, gain, w_layer, out_layer, streams):
    sections = len(xz)
    tokens = norms.shape[0]
    head, width = out_layer.shape
    wide = 3 * head
    scale = 1.0 / math.sqrt(head)
    lead = slice(0, streams[-1].stop)
    through_at, across_at, _ = layout(sections, wide, head)
    count, packed = pieces[0].shape[-2:]
    plane = head // count
    n_in = sections + len(pieces)
    copies = sections + plane + 2

    def kernel(s_ref, p_ref, *refs):
        xz_refs, piece_refs = refs[:sections], refs[sections:n_in]
        n_ref, mask_ref, g_ref, w_ref, o_ref = refs[n_in : n_in + 5]
        n_out = n_in + 5
        v_ref, t_ref, a_ref = refs[n_out : n_out + 3]
        first_refs = refs[n_out + 3 : n_out + 3 + len(streams)]
        scratch = refs[n_out + 3 + len(streams) :]
        xz_all, table, mixes, weights, projs, dmix, w_in, o_in, sems = scratch
        mine = s_ref[0]
        started = []

        def start(source, target):
            copy = pltpu.make_async_copy(source, target, sems.at[len(started)])
            copy.start()
            started.append(copy)

        for r in range(sections):
            start(xz_refs[r], xz_all.at[mine ^ r])
        at = 0
        for ref in piece_refs:
            for i in range(ref.shape[0]):
                start(ref.at[i], table.at[p_ref[at]])
                at += 1
        small = list(started)
        start(w_ref.at[lead], w_in)
        start(o_ref.at[:, lead], o_in)
        for copy in small:
            copy.wait()

        def through(j, k):
            return table[:, :, through_at[j, k]].reshape(head, wide)

        def across(j, k):
            return table[:, :, across_at[j, k]].reshape(head, head)

        allowed = mask_ref[...] > 0.5
        norm = n_ref[...]
        rstds, tails, mixed = [], [], []
        for s in range(sections):
            proj = xz_all[s, :, :wide].astype(F32)
            for j in range(s):
                proj = proj + dot_nn(mixed[j], through(j, s))
            rstd = lax.rsqrt(norm * (1.0 / width) + EPS)
            proj = proj * rstd
            projs[s] = proj.astype(BF16)
            q, k, v = (projs[s, :, i * head : (i + 1) * head] for i in range(3))
            scores = jnp.where(allowed, dot_nt(q, k) * scale, -1e30)
            scores = jnp.exp(scores - jnp.max(scores, axis=1, keepdims=True))
            soft = scores / jnp.sum(scores, axis=1, keepdims=True)
            weights[s] = soft
            mix = dot_nn(soft.astype(BF16), v).astype(BF16)
            mixed.append(mix)
            mixes[:, s * head : (s + 1) * head] = mix
            rstds.append(rstd)
            dmix[:, s * head : (s + 1) * head] = xz_all[s, :, wide + head :].astype(F32)
            if s == sections - 1:
                break
            y = xz_all[s, :, wide : wide + head].astype(F32)
            for j in range(s):
                y = y + dot_nn(mixed[j], across(j, s))
            tail = y + dot_nn(mix, across(s, s))
            norm = norm + jnp.sum(mix.astype(F32) * (y + tail), axis=1, keepdims=True)
            norm = jnp.maximum(norm, 0.0)
            tails.append(tail)
        total = jnp.zeros((tokens, 1), F32)
        a_ref[...] = jnp.zeros_like(a_ref)
        for s in reversed(range(sections)):
            cols = slice(s * head, (s + 1) * head)
            da = dmix[:, cols]
            if s < sections - 1:
                da = da - total * tails[s]
            da = da.astype(BF16)
            q, k, v = (projs[s, :, i * head : (i + 1) * head] for i in range(3))
            soft = weights[s]
            dv = dot_tn(soft.astype(BF16), da)
            dsoft = dot_nt(da, v)
            dscore = soft * (dsoft - jnp.sum(dsoft * soft, axis=1, keepdims=True))
            dscore = (dscore * scale).astype(BF16)
            dproj = jnp.concatenate([dot_nn(dscore, k), dot_tn(dscore, q), dv], axis=1)
            along = jnp.sum(dproj * projs[s].astype(F32), axis=1, keepdims=True)
            first = (dproj * rstds[s]).astype(BF16)
            second = (-total * mixes[:, cols].astype(F32)).astype(BF16)
            total = total + rstds[s] * rstds[s] * along * (1.0 / width)
            for j in reversed(range(s)):
                term = dot_nt(first, through(j, s))
                if s < sections - 1:
                    term = term + dot_nt(second, across(j, s))
                dmix[:, j * head : (j + 1) * head] += term

            @pl.when(mine == s)
            def _(first=first, second=second, total=total):
                v_ref[:, :wide] = first
                v_ref[:, wide:] = second
                t_ref[...] = total

            for r in range(1, sections - s):

                @pl.when(mine == s + r)
                def _(r=r, cols=cols):
                    a_ref[:, (r - 1) * head : r * head] = mixes[:, cols]

        for copy in started[len(small) :]:
            copy.wait()
        own = dot_nt(v_ref[:, :wide], w_in[...]) * g_ref[:, lead]
        own = (own + dot_nn(v_ref[:, wide:], o_in[...])).astype(BF16)
        for ref, part in zip(first_refs, streams):
            ref[...] = own[:, part]

    vmem = pl.BlockSpec(memory_space=pltpu.VMEM)
    smem = pl.BlockSpec(memory_space=pltpu.SMEM)
    return pl.pallas_call(
        kernel,
        out_shape=[
            pltpu.VMEM((tokens, wide + head), BF16),
            pltpu.VMEM((tokens, 1), F32),
            pltpu.VMEM((tokens, (sections - 1) * head), BF16),
        ]
        + [pltpu.VMEM((tokens, part.stop - part.start), BF16) for part in streams],
        in_specs=[smem, smem] + [ANYWHERE] * n_in + [vmem, vmem, vmem, IN_HBM, IN_HBM],
        out_specs=[vmem] * (3 + len(streams)),
        scratch_shapes=[
            pltpu.VMEM((sections,) + xz[0].shape, BF16),
            pltpu.VMEM((plane, count, packed), BF16),
            pltpu.VMEM((tokens, sections * head), BF16),
            pltpu.VMEM((sections, tokens, tokens), F32),
            pltpu.VMEM((sections, tokens, wide), BF16),
            pltpu.VMEM((tokens, sections * head), F32),
            pltpu.VMEM((lead.stop, wide), BF16),
            pltpu.VMEM((head, lead.stop), BF16),
            pltpu.SemaphoreType.DMA((copies,)),
        ],
        compiler_params=params(),
        name="serial",
    )(
        section,
        places,
        *xz,
        *pieces,
        norms,
        mask,
        gain,
        in_hbm(w_layer),
        in_hbm(out_layer),
    )


def hold(array, after):
    def kernel(*refs):
        pass

    return pl.pallas_call(
        kernel,
        out_shape=jax.ShapeDtypeStruct(array.shape, array.dtype),
        in_specs=[ANYWHERE] * (1 + len(after)),
        out_specs=ANYWHERE,
        input_output_aliases={0: 0},
        compiler_params=params(SMALL),
        name="hold",
    )(array, *after)


def gather_two(first, second, after):
    count = first.shape[0]

    def kernel(first_ref, second_ref, *refs):
        out_ref, sems = refs[len(after) :]
        start = mover(sems)
        copies = [start(first_ref, out_ref.at[:count]), start(second_ref, out_ref.at[count:])]
        for copy in copies:
            copy.wait()

    return pl.pallas_call(
        kernel,
        out_shape=jax.ShapeDtypeStruct((2 * count,) + first.shape[1:], first.dtype),
        in_specs=[ANYWHERE] * (2 + len(after)),
        out_specs=IN_VMEM,
        scratch_shapes=[pltpu.SemaphoreType.DMA((2,))],
        compiler_params=params(SMALL),
        name="gather_two",
    )(first, second, *after)


def widen(sent, gain, w_layer, out_layer, chunk):
    tokens = sent.shape[0]
    head, width = out_layer.shape
    wide = w_layer.shape[1]
    cuts = [slice(at, at + chunk) for at in range(0, width, chunk)]

    def kernel(v_ref, g_ref, w_ref, o_ref, back_ref, pair_ref, back_in, w_in, o_in, sems):
        start = mover(sems)
        loads = [
            (start(w_ref.at[cut], w_in.at[cut]), start(o_ref.at[:, cut], o_in.at[:, cut]))
            for cut in cuts
        ]
        stores = []
        for i, (cut, mine) in enumerate(zip(cuts, loads)):
            for load in mine:
                load.wait()
            back = dot_nt(v_ref[:, :wide], w_in[cut, :])
            own = back * g_ref[:, cut] + dot_nn(v_ref[:, wide:], o_in[:, cut])
            back_in[:, cut] = back.astype(BF16)
            stores.append(start(back_in.at[:, cut], back_ref.at[:, cut]))
            pair_ref[0, i] = own.astype(BF16)
            pair_ref[1, i] = jnp.zeros_like(pair_ref[1, i])
        for store in stores:
            store.wait()

    return pl.pallas_call(
        kernel,
        out_shape=[
            pltpu.HBM((tokens, width), BF16),
            pltpu.VMEM((2, len(cuts), tokens, chunk), BF16),
        ],
        in_specs=[IN_VMEM, IN_VMEM, IN_HBM, IN_HBM],
        out_specs=[IN_HBM, IN_VMEM],
        scratch_shapes=[
            pltpu.VMEM((tokens, width), BF16),
            pltpu.VMEM((width, wide), BF16),
            pltpu.VMEM((head, width), BF16),
            pltpu.SemaphoreType.DMA((3 * len(cuts),)),
        ],
        compiler_params=params(),
        name="widen",
    )(in_vmem(sent), gain, in_hbm(w_layer), in_hbm(out_layer))


def settle(total, mixes, stacks, places, x, cotangent, back, chunk, part, parts):
    tokens, width = x.shape
    layers, rows = stacks[0].shape[1:3]
    entries = [(i, e) for i, stack in enumerate(stacks) for e in range(stack.shape[0])]
    plane = len(entries)
    head = plane * rows
    span = width // parts
    base = part * span
    cuts = [slice(at, at + chunk) for at in range(0, span, chunk)]
    copies = plane * layers + 3 * len(cuts)

    def kernel(p_ref, t_ref, a_ref, x_ref, c_ref, back_ref, *refs):
        stack_refs = refs[: len(stacks)]
        rest_ref, dg_ref = refs[len(stacks) : len(stacks) + 2]
        lower, x_in, c_in, back_in, sems = refs[len(stacks) + 2 :]
        start = mover(sems)
        first = []
        for at, (i, e) in enumerate(entries):
            for r in range(layers):
                here = pl.ds(base, span)
                first.append(start(stack_refs[i].at[e, r, :, here], lower.at[r, p_ref[at]]))
        loads = []
        for cut in cuts:
            there = pl.ds(base + cut.start, chunk)
            mine = [start(x_ref.at[:, there], x_in.at[:, cut])]
            mine.append(start(c_ref.at[:, there], c_in.at[:, cut]))
            mine.append(start(back_ref.at[:, there], back_in.at[:, cut]))
            loads.append(mine)
        for load in first:
            load.wait()
        for i, (cut, mine) in enumerate(zip(cuts, loads)):
            for load in mine:
                load.wait()
            below = lower[:, :, :, cut].reshape(layers * head, chunk)
            here = x_in[:, cut].astype(F32) + dot_nn(a_ref[...], below)
            rest_ref[i] = (c_in[:, cut].astype(F32) - t_ref[...] * here).astype(BF16)
            gain = jnp.sum(back_in[:, cut].astype(F32) * here, axis=0, keepdims=True)
            for at in range(0, chunk, head):
                row = (cut.start + at) // head
                dg_ref[row : row + 1, :] = gain[:, at : at + head]

    return pl.pallas_call(
        kernel,
        out_shape=[
            pltpu.VMEM((len(cuts), tokens, chunk), BF16),
            pltpu.VMEM((span // head, head), F32),
        ],
        in_specs=[IN_SMEM] + [IN_VMEM] * 2 + [IN_HBM] * (3 + len(stacks)),
        out_specs=[IN_VMEM] * 2,
        scratch_shapes=[
            pltpu.VMEM((layers, plane, rows, span), BF16),
            pltpu.VMEM((tokens, span), BF16),
            pltpu.VMEM((tokens, span), BF16),
            pltpu.VMEM((tokens, span), BF16),
            pltpu.SemaphoreType.DMA((copies,)),
        ],
        compiler_params=params(),
        name="settle",
    )(
        places,
        in_vmem(total),
        in_vmem(mixes),
        *[in_hbm(array) for array in (x, cotangent, back, *stacks)],
    )


def join(index, arrived, pair, cols, after):
    tokens, part = arrived.shape

    def kernel(i_ref, r_ref, _, *refs):
        send_ref, pair_ref = refs[len(after) :]
        at = i_ref[0]
        r = r_ref[...]
        send_ref[...] = (pair_ref[0, at, :, cols].astype(F32) + r.astype(F32)).astype(BF16)
        pair_ref[1, at, :, cols] = r

    return pl.pallas_call(
        kernel,
        out_shape=[pltpu.VMEM((tokens, part), BF16), pltpu.VMEM(pair.shape, BF16)],
        in_specs=[IN_SMEM] + [IN_VMEM] * 2 + [ANYWHERE] * len(after),
        out_specs=[IN_VMEM] * 2,
        input_output_aliases={2: 1},
        compiler_params=params(SMALL),
        name="join",
    )(index, in_vmem(arrived), in_vmem(pair), *after)


def finish(index, arrived, pair, rests, streams):
    _, count, tokens, chunk = pair.shape

    def kernel(i_ref, *refs):
        r_refs = refs[: len(streams)]
        pair_ref, rest_refs = refs[len(streams)], refs[len(streams) + 1 :][: len(rests)]
        whole_ref, whole, sems = refs[len(streams) + 1 + len(rests) :]
        each = count // len(rests)
        at = i_ref[0]
        copies = []
        for i in range(count):
            full = rest_refs[i // each][i % each].astype(F32) + pair_ref[0, i].astype(F32)
            whole[i] = (full + pair_ref[1, i].astype(F32)).astype(BF16)

            @pl.when(at == i)
            def _(i=i, full=full):
                for ref, cols in zip(r_refs, streams):
                    whole[i, :, cols] = (full[:, cols] + ref[...].astype(F32)).astype(BF16)

            there = whole_ref.at[:, pl.ds(i * chunk, chunk)]
            copies.append(pltpu.make_async_copy(whole.at[i], there, sems.at[i]))
            copies[-1].start()
        for copy in copies:
            copy.wait()

    return pl.pallas_call(
        kernel,
        out_shape=pltpu.HBM((tokens, count * chunk), BF16),
        in_specs=[IN_SMEM] + [IN_VMEM] * (len(streams) + 1 + len(rests)),
        out_specs=IN_HBM,
        scratch_shapes=[
            pltpu.VMEM((count, tokens, chunk), BF16),
            pltpu.SemaphoreType.DMA((count,)),
        ],
        compiler_params=params(SMALL),
        name="finish",
    )(index, *[in_vmem(array) for array in (*arrived, pair, *rests)])


def stacked(arrays):
    rows = arrays[0].shape[0]

    def kernel(*refs):
        for i, ref in enumerate(refs[:-1]):
            refs[-1][i * rows : (i + 1) * rows, :] = ref[...]

    return pl.pallas_call(
        kernel,
        out_shape=pltpu.VMEM((len(arrays) * rows, arrays[0].shape[1]), F32),
        in_specs=[IN_VMEM] * len(arrays),
        out_specs=IN_VMEM,
        compiler_params=params(SMALL),
        name="stacked",
    )(*[in_vmem(array) for array in arrays])


def added(arrays):
    def kernel(*refs):
        total = refs[0][...]
        for ref in refs[1:-1]:
            total = total + ref[...]
        refs[-1][...] = total

    return pl.pallas_call(
        kernel,
        out_shape=pltpu.VMEM(arrays[0].shape, F32),
        in_specs=[IN_VMEM] * len(arrays),
        out_specs=IN_VMEM,
        compiler_params=params(SMALL),
        name="added",
    )(*[in_vmem(array) for array in arrays])


STREAMS = 2
CHUNKS = 4
PARTS = 2


def stream_columns(chunk):
    lanes = 128
    tiles = chunk // lanes
    ends = [-(-tiles * (i + 1) // STREAMS) * lanes for i in range(STREAMS)]
    return [slice(start, end) for start, end in zip([0] + ends, ends)]


def shifted(array, by):
    sections = lax.axis_size("section")
    return lax.ppermute(array, "section", [(i, (i + by) % sections) for i in range(sections)])


def raised(array, by):
    sections = lax.axis_size("section")
    return lax.ppermute(array, "section", [(i, i + by) for i in range(sections - by)])


def swapped(array, step):
    groups = lax.axis_size("group")
    devices = lax.axis_size("dp")
    bits = devices.bit_length() - 1
    pairs = []
    for p in range(devices):
        for g in range(groups):
            pairs.append((p * groups + g, (p ^ (1 << ((step + g) % bits))) * groups + g))
    return lax.ppermute(array, ("dp", "group"), pairs)


def handed(array, by):
    groups = lax.axis_size("group")
    return lax.ppermute(array, "group", [(i, (i + by) % groups) for i in range(groups)])


def plane_places():
    groups = lax.axis_size("group")
    bits = lax.axis_size("dp").bit_length() - 1
    masks = []
    for g in range(groups):
        order = [0]
        for step in range(bits):
            order = order + [m ^ (1 << ((step + g) % bits)) for m in order]
        masks.append(order)
    masks = jnp.asarray(masks, jnp.int32)
    dp, member = lax.axis_index("dp"), lax.axis_index("group")
    places = []
    for r in range(groups):
        giver = (member + groups - r) % groups
        places.append((dp ^ masks[giver]) * groups + giver)
    return jnp.concatenate(places).astype(jnp.int32)


def local(tokens_in, cotangent, gains, w_qkv, w_out, segments, plan):
    sections = lax.axis_size("section")
    groups = lax.axis_size("group")
    devices = lax.axis_size("dp")
    plane = devices * groups
    section = lax.axis_index("section")
    member = lax.axis_index("group")
    rows_dev = plan.shape[1]
    length = segments.shape[1]
    tokens, width = tokens_in.shape
    head = w_out.shape[1]
    share = rows_dev // groups
    w_layer, out_layer = w_qkv[0], w_out[0]
    place = member.astype(jnp.int32)[None]
    layer = section.astype(jnp.int32)[None]

    slice_rows = head // plane
    mine = lax.axis_index("dp") * groups + member
    own_rows, *parts = pick(
        tokens_in.reshape(rows_dev, length, width),
        plan,
        place,
        groups,
        out_layer,
        mine.astype(jnp.int32)[None],
        slice_rows,
    )
    slices = [raised(own_rows, r) for r in range(sections - 1, 0, -1)]
    slices = [own_rows] + slices[::-1]
    chosen = jnp.take(segments, plan[0], axis=0, mode="clip").astype(BF16)
    chosen = chosen.reshape(groups, share, length)
    moved, moved_seg = [], []
    for r in range(groups):
        outgoing = lax.dynamic_index_in_dim(chosen, (member + r) % groups, 0, keepdims=False)
        moved.append(handed(parts[r], r) if r else parts[r])
        moved_seg.append(handed(outgoing, r) if r else outgoing)
    moved = [part.reshape(share * length, width) for part in moved]
    order = (member - jnp.arange(groups)) % groups
    seg = jnp.take(jnp.stack(moved_seg), order, axis=0, mode="clip").reshape(tokens)
    at = jnp.arange(tokens)
    mask = (
        (at[:, None] >= at[None, :])
        & (at[:, None] // length == at[None, :] // length)
        & (seg[:, None] == seg[None, :])
    ).astype(F32)

    last = (section == sections - 1).astype(jnp.int32)[None]
    bits = devices.bit_length() - 1
    places = plane_places()
    x, xz, norms = project(
        moved, cotangent, gains, w_layer, out_layer, place, []
    )
    coupling, stack = couple(slices, gains, w_layer, out_layer, last, [mask, places, xz])
    others = [shifted(coupling, r) for r in range(1, sections)]

    streams = stream_columns(width // CHUNKS)

    def facing(array, by):
        return lax.ppermute(array, "section", [(i, i ^ by) for i in range(sections)])

    arrays, masks, by = [hold(xz, others)], [0], sections // 2
    while by > 0:
        arrays = arrays + [facing(array, by) for array in arrays]
        masks = masks + [mask_of ^ by for mask_of in masks]
        by = by // 2
    xz_all = [arrays[masks.index(r)] for r in range(sections)]
    early = [xz_all[r] for r in range(1, sections) if r & (r - 1) == 0]
    late = [xz_all[r] for r in range(1, sections) if r & (r - 1) != 0]
    pieces = [compact([coupling] + others, layer, 3 * head, head, [xz])]

    rows = [stack[None]]
    for step in range(bits):
        if step > 0:
            pieces = [merge(*pieces, early)]
        pieces = pieces + [swapped(pieces[0], step)]
        if step == bits - 1:
            pieces[-1] = hold(pieces[-1], late)
        if step > 0:
            rows = [gather_two(*rows, pieces[-1:])]
        rows = rows + [swapped(rows[0], step)]
    pieces = pieces + [handed(array, r) for r in range(1, groups) for array in pieces]
    sent, total, mixes, *leaving = serial(
        xz_all, pieces, places, norms, mask, layer, gains, w_layer, out_layer, streams
    )
    back, pair = widen(sent, gains, w_layer, out_layer, width // CHUNKS)

    down = [(i, i - 1) for i in range(1, sections)]
    behind = sections - 1 - section

    def index(tick):
        return jnp.clip(tick - behind, 0, CHUNKS - 1).astype(jnp.int32)[None]

    def lowered(arrays):
        return [lax.ppermute(array, "section", down) for array in arrays]

    def crossed(array, by):
        return lax.ppermute(array, "dp", [(p, p ^ by) for p in range(devices)])

    ticks = CHUNKS + sections - 1
    after = {}
    for tick in range(1, ticks):
        arrived = lowered(leaving)
        if tick < ticks - 1:
            for i, cols in enumerate(streams):
                leaving[i], pair = join(
                    index(tick), arrived[i], pair, cols, after.get(tick, [])
                )
        if tick == 1:
            rows = [hold(array, leaving) for array in rows]
            rows = rows + [handed(array, r) for r in range(1, groups) for array in rows]
            rests, halves = [], []
            for part in range(PARTS):
                rest, half = settle(
                    total, mixes, rows, places, x, cotangent, back, width // CHUNKS, part, PARTS
                )
                rests.append(rest)
                halves.append(half)
            gain = stacked(halves)
            crossing = [crossed(gain, by) for by in range(1, devices)]
            gain_chip = added([gain] + crossing)
            gain_whole = added([gain_chip] + [handed(gain_chip, r) for r in range(1, groups)])
            gain_whole = gain_whole.reshape(1, width)
            after = {2: halves[:1], 3: halves[1:], 4: crossing[: devices // 2], 5: [gain_chip]}
    out = finish(index(ticks - 1), arrived, pair, rests, streams)
    return (out[None], gain_whole)


def attend(hidden, segment, gain_row, w_layer, out_layer):
    count, length, width = hidden.shape
    head = out_layer.shape[0]
    scaled = hidden * lax.rsqrt(jnp.mean(hidden * hidden, axis=-1, keepdims=True) + EPS) * gain_row
    normed = scaled.astype(BF16).reshape(count * length, width)
    projected = jnp.dot(normed, w_layer, preferred_element_type=F32).reshape(count, length, 3 * head)
    query = projected[:, :, :head]
    keyed = projected[:, :, head : 2 * head]
    valued = projected[:, :, 2 * head :]
    positions = jnp.arange(length)
    allowed = (positions[:, None] >= positions[None, :])[None] & (
        segment[:, :, None] == segment[:, None, :]
    )
    scores = jnp.einsum("rid,rjd->rij", query, keyed, precision=lax.Precision.HIGHEST)
    scores = jnp.where(allowed, scores / math.sqrt(head), -1e30)
    weights = jax.nn.softmax(scores, axis=-1)
    mixed = jnp.einsum("rij,rjd->rid", weights, valued, precision=lax.Precision.HIGHEST)
    mixed = mixed.astype(BF16).reshape(count * length, head)
    output = jnp.dot(mixed, out_layer, preferred_element_type=F32).reshape(count, length, width)
    return hidden + output


MB_ROWS = 2


def relay(tokens_in, cotangent, gains, w_qkv, w_out, segments, plan):
    sections = lax.axis_size("section")
    section = lax.axis_index("section")
    rows_dev = plan.shape[1]
    width = tokens_in.shape[1]
    length = segments.shape[1]
    micro = rows_dev // MB_ROWS
    blocks = tokens_in.reshape(rows_dev, length, width)
    chosen = jnp.take(blocks, plan[0], axis=0)
    chosen_seg = jnp.take(segments, plan[0], axis=0).astype(BF16)
    assigned = lax.all_to_all(chosen, "group", split_axis=0, concat_axis=0, tiled=True)
    moved_seg = lax.all_to_all(chosen_seg, "group", split_axis=0, concat_axis=0, tiled=True)
    assigned = assigned.reshape(micro, MB_ROWS, length, width)
    seg_groups = moved_seg.reshape(micro, MB_ROWS, length)
    gain_row, w_layer, out_layer = gains[0], w_qkv[0], w_out[0]
    grad_rows = cotangent.reshape(micro, MB_ROWS, length, width)
    ticks = micro + sections - 1

    def passed_along(array, by):
        pairs = [(i, i + by) for i in range(sections) if 0 <= i + by < sections]
        return lax.ppermute(array, "section", pairs)

    def at(array, i):
        return lax.dynamic_index_in_dim(array, i, 0, keepdims=False)

    def forward_tick(tick, carry):
        saved, arrived = carry
        index = tick - section
        valid = (index >= 0) & (index < micro)
        clipped = jnp.clip(index, 0, micro - 1)
        entering = jnp.where(section == 0, at(assigned, clipped), arrived)
        kept = jnp.where(valid, entering, at(saved, clipped))
        saved = lax.dynamic_update_index_in_dim(saved, kept, clipped, 0)
        segment = at(seg_groups, clipped)

        def run_layer(value):
            return attend(value.astype(F32), segment, gain_row, w_layer, out_layer).astype(BF16)

        leaving = lax.cond(valid, run_layer, jnp.zeros_like, entering)
        return (saved, passed_along(leaving, 1))

    saved_init = jnp.zeros((micro, MB_ROWS, length, width), BF16)
    arrive_init = jnp.zeros((MB_ROWS, length, width), BF16)
    saved, _ = lax.fori_loop(0, ticks, forward_tick, (saved_init, arrive_init))

    def backward_tick(tick, carry):
        grads_x, gain_total, arrived = carry
        index = tick - (sections - 1 - section)
        valid = (index >= 0) & (index < micro)
        clipped = jnp.clip(index, 0, micro - 1)
        entering = jnp.where(section == sections - 1, at(grad_rows, clipped), arrived)
        segment = at(seg_groups, clipped)
        stored = at(saved, clipped).astype(F32)

        def local_layer(hidden, gains_here):
            return attend(hidden, segment, gains_here, w_layer, out_layer)

        def run_back(value):
            _, pullback = jax.vjp(local_layer, stored, gain_row)
            grad_hidden, grad_gain = pullback(value.astype(F32))
            return (grad_hidden.astype(BF16), grad_gain)

        def skip_back(value):
            return (jnp.zeros_like(value), jnp.zeros(gain_row.shape, F32))

        sending, grad_gain = lax.cond(valid, run_back, skip_back, entering)
        kept = jnp.where(valid, sending, at(grads_x, clipped))
        grads_x = lax.dynamic_update_index_in_dim(grads_x, kept, clipped, 0)
        return (grads_x, gain_total + grad_gain, passed_along(sending, -1))

    gain_init = jnp.zeros(gain_row.shape, F32)
    grads_x, gain_total, _ = lax.fori_loop(
        0, ticks, backward_tick, (saved_init, gain_init, arrive_init)
    )
    gain_whole = lax.psum(gain_total, ("dp", "group"))
    return (grads_x.reshape(1, rows_dev * length, width), gain_whole[None])


def solution(mesh):
    placed = (
        P(("dp", "group"), None),
        P(("dp", "group"), None),
        P("section", None),
        P("section", None, None),
        P("section", None, None),
        P(("dp", "group"), None),
        P(("dp", "group"), None),
    )

    def chosen(tokens_in, cotangent, gains, w_qkv, w_out, segments, plan):
        sections, head, width = w_out.shape
        devices = mesh.shape["dp"]
        small = sections * 4 * head < width and sections > 1
        halves = devices & (devices - 1) == 0 and sections & (sections - 1) == 0
        body = local if small and halves else relay
        return jax.shard_map(
            body,
            mesh=mesh,
            in_specs=placed,
            out_specs=(P("section", ("dp", "group"), None), P("section", None)),
            check_vma=False,
        )(tokens_in, cotangent, gains, w_qkv, w_out, segments, plan)

    return chosen
```

```python
import math

import jax
import jax.numpy as jnp
from jax import lax
from jax.experimental import pallas as pl
from jax.experimental.pallas import tpu as pltpu
from jax.sharding import PartitionSpec as P

EPS = 1e-05
VMEM_BYTES = 24 * 1024 * 1024
SMALL = 16 * 1024 * 1024
F32 = jnp.float32
BF16 = jnp.bfloat16


def dot_nn(a, b):
    return lax.dot_general(a, b, (((1,), (0,)), ((), ())), preferred_element_type=F32)


def dot_nt(a, b):
    return lax.dot_general(a, b, (((1,), (1,)), ((), ())), preferred_element_type=F32)


def dot_tn(a, b):
    return lax.dot_general(a, b, (((0,), (0,)), ((), ())), preferred_element_type=F32)


IN_HBM = pl.BlockSpec(memory_space=pltpu.HBM)
ANYWHERE = pl.BlockSpec(memory_space=pl.ANY)
IN_VMEM = pl.BlockSpec(memory_space=pltpu.VMEM)
IN_SMEM = pl.BlockSpec(memory_space=pltpu.SMEM)


def in_hbm(array):
    return pltpu.with_memory_space_constraint(array, pltpu.HBM)


def in_vmem(array):
    return pltpu.with_memory_space_constraint(array, pltpu.VMEM)


def mover(sems):
    used = []

    def start(source, target):
        copy = pltpu.make_async_copy(source, target, sems.at[len(used)])
        copy.start()
        used.append(copy)
        return copy

    return start


def steps(width):
    step = min(width, 1024)
    return [slice(at, at + step) for at in range(0, width, step)]


def params(limit=VMEM_BYTES):
    return pltpu.CompilerParams(vmem_limit_bytes=limit)


def pick(tokens, plan, place, groups, out_layer, mine, slice_rows):
    rows, length, width = tokens.shape
    share = rows // groups

    def kernel(plan_ref, place_ref, mine_ref, tokens_ref, o_ref, *rest):
        slice_ref, parts = rest[0], rest[1 : 1 + groups]
        slice_in, rows_in, sems = rest[1 + groups :]
        start = mover(sems)
        at = pl.ds(pl.multiple_of(mine_ref[0] * slice_rows, slice_rows), slice_rows)
        loads = [(start(o_ref.at[at], slice_in), slice_in, slice_ref)]
        for r in range(groups):
            target = lax.rem(place_ref[0] + r, groups)
            for c in range(share):
                here = rows_in.at[r * share + c]
                row = plan_ref[0, target * share + c]
                loads.append((start(tokens_ref.at[row], here), here, parts[r].at[c]))
        stores = []
        for load, here, there in loads:
            load.wait()
            stores.append(start(here, there))
        for store in stores:
            store.wait()

    return pl.pallas_call(
        kernel,
        out_shape=[pltpu.HBM((slice_rows, width), BF16)]
        + [pltpu.HBM((share, length, width), BF16)] * groups,
        in_specs=[IN_SMEM, IN_SMEM, IN_SMEM, IN_HBM, IN_HBM],
        out_specs=[IN_HBM] * (1 + groups),
        scratch_shapes=[
            pltpu.VMEM((slice_rows, width), BF16),
            pltpu.VMEM((rows, length, width), BF16),
            pltpu.SemaphoreType.DMA((2 * rows + 2,)),
        ],
        compiler_params=params(),
        name="pick",
    )(plan, place, mine, in_hbm(tokens), in_hbm(out_layer))


def project(parts, cotangent, gain, w_layer, out_layer, place, after):
    groups = len(parts)
    tokens, width = cotangent.shape
    head = out_layer.shape[0]
    wide = w_layer.shape[1]
    block = tokens // groups
    cuts = steps(width)
    copies = len(cuts) * (groups + 4)

    def kernel(place_ref, *refs):
        part_refs = refs[:groups]
        cot_ref, g_ref, w_ref, o_ref = refs[groups : groups + 4]
        x_ref, xz_ref, n_ref = refs[groups + 4 + len(after) : groups + 7 + len(after)]
        x_in, c_in, w_in, o_in, sems = refs[groups + 7 + len(after) :]
        start = mover(sems)
        loads = []
        for cut in cuts:
            mine = [start(w_ref.at[cut], w_in.at[cut])]
            mine.append(start(o_ref.at[:, cut], o_in.at[:, cut]))
            for r in range(groups):
                source = lax.rem(place_ref[0] + groups - r, groups)
                rows = pl.ds(pl.multiple_of(source * block, block), block)
                mine.append(start(part_refs[r].at[:, cut], x_in.at[rows, cut]))
            mine.append(start(cot_ref.at[:, cut], c_in.at[:, cut]))
            loads.append(mine)
        through = jnp.zeros((tokens, wide), F32)
        across = jnp.zeros((tokens, head), F32)
        back = jnp.zeros((tokens, head), F32)
        square = jnp.zeros((tokens, 1), F32)
        stores = []
        for cut, mine in zip(cuts, loads):
            for load in mine:
                load.wait()
            stores.append(start(x_in.at[:, cut], x_ref.at[:, cut]))
            x = x_in[:, cut]
            xf = x.astype(F32)
            through += dot_nn((xf * g_ref[:, cut]).astype(BF16), w_in[cut, :])
            across += dot_nt(x, o_in[:, cut])
            back += dot_nt(c_in[:, cut], o_in[:, cut])
            square += jnp.sum(xf * xf, axis=1, keepdims=True)
        xz_ref[:, :wide] = through.astype(BF16)
        xz_ref[:, wide : wide + head] = across.astype(BF16)
        xz_ref[:, wide + head :] = back.astype(BF16)
        n_ref[...] = square
        for store in stores:
            store.wait()

    return pl.pallas_call(
        kernel,
        out_shape=[
            pltpu.HBM((tokens, width), BF16),
            jax.ShapeDtypeStruct((tokens, wide + 2 * head), BF16),
            jax.ShapeDtypeStruct((tokens, 1), F32),
        ],
        in_specs=[IN_SMEM]
        + [ANYWHERE] * groups
        + [IN_HBM, IN_VMEM, IN_HBM, IN_HBM]
        + [ANYWHERE] * len(after),
        out_specs=[IN_HBM, IN_VMEM, IN_VMEM],
        scratch_shapes=[
            pltpu.VMEM((tokens, width), BF16),
            pltpu.VMEM((tokens, width), BF16),
            pltpu.VMEM((width, wide), BF16),
            pltpu.VMEM((head, width), BF16),
            pltpu.SemaphoreType.DMA((copies,)),
        ],
        compiler_params=params(),
        name="project",
    )(
        place,
        *parts,
        in_hbm(cotangent),
        gain,
        in_hbm(w_layer),
        in_hbm(out_layer),
        *after,
    )


def couple(slices, gain, w_layer, out_layer, last, after):
    sections = len(slices)
    count, width = slices[0].shape
    head = out_layer.shape[0]
    wide = w_layer.shape[1]
    below = (sections - 2) * wide
    packed = below + max(wide, (sections - 1) * head)
    cuts = steps(width)
    copies = len(cuts) * (sections + 2) + sections - 1

    def kernel(last_ref, *refs):
        s_refs = refs[:sections][::-1]
        g_ref, w_ref, o_ref = refs[sections : sections + 3]
        out_ref, stack_ref, r_in, w_in, o_in, sems = refs[sections + 3 + len(after) :]
        rows = [slice(r * count, (r + 1) * count) for r in range(sections)]
        start = mover(sems)
        loads = []
        for cut in cuts:
            mine = [start(w_ref.at[cut], w_in.at[cut])]
            mine.append(start(o_ref.at[:, cut], o_in.at[:, cut]))
            for r in range(sections):
                mine.append(start(s_refs[r].at[:, cut], r_in.at[rows[r], cut]))
            loads.append(mine)
        through = jnp.zeros((sections * count, wide), F32)
        across = jnp.zeros((sections * count, head), F32)
        for cut, mine in zip(cuts, loads):
            for load in mine:
                load.wait()
            r = r_in[:, cut]
            through += dot_nn((r.astype(F32) * g_ref[:, cut]).astype(BF16), w_in[cut, :])
            across += dot_nt(r, o_in[:, cut])
        stores = [start(r_in.at[rows[r]], stack_ref.at[r - 1]) for r in range(1, sections)]
        through = through.astype(BF16)
        across = across.astype(BF16)
        out_ref[...] = jnp.zeros_like(out_ref)
        for r in range(1, sections - 1):
            out_ref[:, (r - 1) * wide : r * wide] = through[rows[r]]

        @pl.when(last_ref[0] == 1)
        def _():
            out_ref[:, below : below + wide] = through[rows[-1]]

        @pl.when(last_ref[0] == 0)
        def _():
            for r in range(sections - 1):
                out_ref[:, below + r * head : below + (r + 1) * head] = across[rows[r]]

        for store in stores:
            store.wait()

    return pl.pallas_call(
        kernel,
        out_shape=[
            jax.ShapeDtypeStruct((count, packed), BF16),
            pltpu.HBM((sections - 1, count, width), BF16),
        ],
        in_specs=[IN_SMEM]
        + [ANYWHERE] * sections
        + [IN_VMEM, IN_HBM, IN_HBM]
        + [ANYWHERE] * len(after),
        out_specs=[IN_VMEM, IN_HBM],
        scratch_shapes=[
            pltpu.VMEM((sections * count, width), BF16),
            pltpu.VMEM((width, wide), BF16),
            pltpu.VMEM((head, width), BF16),
            pltpu.SemaphoreType.DMA((copies,)),
        ],
        compiler_params=params(),
        name="couple",
    )(last, *slices[::-1], gain, in_hbm(w_layer), in_hbm(out_layer), *after)


def layout(sections, wide, head):
    through, across, at = {}, {}, 0
    for k in range(sections):
        for j in range(k):
            through[j, k] = slice(at, at + wide)
            at += wide
        for j in range(k + 1 if k < sections - 1 else 0):
            across[j, k] = slice(at, at + head)
            at += head
    return through, across, at


def compact(parts, section, wide, head, after):
    sections = len(parts)
    count = parts[0].shape[0]
    below = (sections - 2) * wide
    through, across, total = layout(sections, wide, head)

    def kernel(s_ref, *refs):
        part_refs, out_ref = refs[:sections], refs[-1]
        mine = s_ref[0]

        def fill(k, r):
            for j in range(k):
                at = (k - j - 1) * wide
                out_ref[0, :, through[j, k]] = part_refs[r][:, at : at + wide]
            for j in range(k + 1 if k < sections - 1 else 0):
                at = below + (k - j) * head
                out_ref[0, :, across[j, k]] = part_refs[r][:, at : at + head]

        for s in range(sections):

            @pl.when(mine == s)
            def _(s=s):
                for r in range(sections):
                    fill((s - r) % sections, r)

    vmem = pl.BlockSpec(memory_space=pltpu.VMEM)
    return pl.pallas_call(
        kernel,
        out_shape=jax.ShapeDtypeStruct((1, count, total), BF16),
        in_specs=[IN_SMEM] + [vmem] * sections + [ANYWHERE] * len(after),
        out_specs=vmem,
        compiler_params=params(SMALL),
        name="compact",
    )(section, *parts, *after)


def merge(first, second, after):
    count = first.shape[0]

    def kernel(first_ref, second_ref, *refs):
        refs[-1][:count] = first_ref[...]
        refs[-1][count:] = second_ref[...]

    return pl.pallas_call(
        kernel,
        out_shape=jax.ShapeDtypeStruct((2 * count,) + first.shape[1:], first.dtype),
        in_specs=[IN_VMEM] * 2 + [ANYWHERE] * len(after),
        out_specs=IN_VMEM,
        compiler_params=params(SMALL),
        name="merge",
    )(first, second, *after)


def serial(xz, pieces, places, norms, mask, section, gain, w_layer, out_layer, streams):
    sections = len(xz)
    tokens = norms.shape[0]
    head, width = out_layer.shape
    wide = 3 * head
    scale = 1.0 / math.sqrt(head)
    lead = slice(0, streams[-1].stop)
    through_at, across_at, _ = layout(sections, wide, head)
    count, packed = pieces[0].shape[-2:]
    plane = head // count
    n_in = sections + len(pieces)
    copies = sections + plane + 2

    def kernel(s_ref, p_ref, *refs):
        xz_refs, piece_refs = refs[:sections], refs[sections:n_in]
        n_ref, mask_ref, g_ref, w_ref, o_ref = refs[n_in : n_in + 5]
        n_out = n_in + 5
        v_ref, t_ref, a_ref = refs[n_out : n_out + 3]
        first_refs = refs[n_out + 3 : n_out + 3 + len(streams)]
        scratch = refs[n_out + 3 + len(streams) :]
        xz_all, table, mixes, weights, projs, dmix, w_in, o_in, sems = scratch
        mine = s_ref[0]
        started = []

        def start(source, target):
            copy = pltpu.make_async_copy(source, target, sems.at[len(started)])
            copy.start()
            started.append(copy)

        for r in range(sections):
            start(xz_refs[r], xz_all.at[mine ^ r])
        at = 0
        for ref in piece_refs:
            for i in range(ref.shape[0]):
                start(ref.at[i], table.at[p_ref[at]])
                at += 1
        small = list(started)
        start(w_ref.at[lead], w_in)
        start(o_ref.at[:, lead], o_in)
        for copy in small:
            copy.wait()

        def through(j, k):
            return table[:, :, through_at[j, k]].reshape(head, wide)

        def across(j, k):
            return table[:, :, across_at[j, k]].reshape(head, head)

        allowed = mask_ref[...] > 0.5
        norm = n_ref[...]
        rstds, tails, mixed = [], [], []
        for s in range(sections):
            proj = xz_all[s, :, :wide].astype(F32)
            for j in range(s):
                proj = proj + dot_nn(mixed[j], through(j, s))
            rstd = lax.rsqrt(norm * (1.0 / width) + EPS)
            proj = proj * rstd
            projs[s] = proj.astype(BF16)
            q, k, v = (projs[s, :, i * head : (i + 1) * head] for i in range(3))
            scores = jnp.where(allowed, dot_nt(q, k) * scale, -1e30)
            scores = jnp.exp(scores - jnp.max(scores, axis=1, keepdims=True))
            soft = scores / jnp.sum(scores, axis=1, keepdims=True)
            weights[s] = soft
            mix = dot_nn(soft.astype(BF16), v).astype(BF16)
            mixed.append(mix)
            mixes[:, s * head : (s + 1) * head] = mix
            rstds.append(rstd)
            dmix[:, s * head : (s + 1) * head] = xz_all[s, :, wide + head :].astype(F32)
            if s == sections - 1:
                break
            y = xz_all[s, :, wide : wide + head].astype(F32)
            for j in range(s):
                y = y + dot_nn(mixed[j], across(j, s))
            tail = y + dot_nn(mix, across(s, s))
            norm = norm + jnp.sum(mix.astype(F32) * (y + tail), axis=1, keepdims=True)
            norm = jnp.maximum(norm, 0.0)
            tails.append(tail)
        total = jnp.zeros((tokens, 1), F32)
        a_ref[...] = jnp.zeros_like(a_ref)
        for s in reversed(range(sections)):
            cols = slice(s * head, (s + 1) * head)
            da = dmix[:, cols]
            if s < sections - 1:
                da = da - total * tails[s]
            da = da.astype(BF16)
            q, k, v = (projs[s, :, i * head : (i + 1) * head] for i in range(3))
            soft = weights[s]
            dv = dot_tn(soft.astype(BF16), da)
            dsoft = dot_nt(da, v)
            dscore = soft * (dsoft - jnp.sum(dsoft * soft, axis=1, keepdims=True))
            dscore = (dscore * scale).astype(BF16)
            dproj = jnp.concatenate([dot_nn(dscore, k), dot_tn(dscore, q), dv], axis=1)
            along = jnp.sum(dproj * projs[s].astype(F32), axis=1, keepdims=True)
            first = (dproj * rstds[s]).astype(BF16)
            second = (-total * mixes[:, cols].astype(F32)).astype(BF16)
            total = total + rstds[s] * rstds[s] * along * (1.0 / width)
            for j in reversed(range(s)):
                term = dot_nt(first, through(j, s))
                if s < sections - 1:
                    term = term + dot_nt(second, across(j, s))
                dmix[:, j * head : (j + 1) * head] += term

            @pl.when(mine == s)
            def _(first=first, second=second, total=total):
                v_ref[:, :wide] = first
                v_ref[:, wide:] = second
                t_ref[...] = total

            for r in range(1, sections - s):

                @pl.when(mine == s + r)
                def _(r=r, cols=cols):
                    a_ref[:, (r - 1) * head : r * head] = mixes[:, cols]

        for copy in started[len(small) :]:
            copy.wait()
        own = dot_nt(v_ref[:, :wide], w_in[...]) * g_ref[:, lead]
        own = (own + dot_nn(v_ref[:, wide:], o_in[...])).astype(BF16)
        for ref, part in zip(first_refs, streams):
            ref[...] = own[:, part]

    vmem = pl.BlockSpec(memory_space=pltpu.VMEM)
    smem = pl.BlockSpec(memory_space=pltpu.SMEM)
    return pl.pallas_call(
        kernel,
        out_shape=[
            pltpu.VMEM((tokens, wide + head), BF16),
            pltpu.VMEM((tokens, 1), F32),
            pltpu.VMEM((tokens, (sections - 1) * head), BF16),
        ]
        + [pltpu.VMEM((tokens, part.stop - part.start), BF16) for part in streams],
        in_specs=[smem, smem] + [ANYWHERE] * n_in + [vmem, vmem, vmem, IN_HBM, IN_HBM],
        out_specs=[vmem] * (3 + len(streams)),
        scratch_shapes=[
            pltpu.VMEM((sections,) + xz[0].shape, BF16),
            pltpu.VMEM((plane, count, packed), BF16),
            pltpu.VMEM((tokens, sections * head), BF16),
            pltpu.VMEM((sections, tokens, tokens), F32),
            pltpu.VMEM((sections, tokens, wide), BF16),
            pltpu.VMEM((tokens, sections * head), F32),
            pltpu.VMEM((lead.stop, wide), BF16),
            pltpu.VMEM((head, lead.stop), BF16),
            pltpu.SemaphoreType.DMA((copies,)),
        ],
        compiler_params=params(),
        name="serial",
    )(
        section,
        places,
        *xz,
        *pieces,
        norms,
        mask,
        gain,
        in_hbm(w_layer),
        in_hbm(out_layer),
    )


def hold(array, after):
    def kernel(*refs):
        pass

    return pl.pallas_call(
        kernel,
        out_shape=jax.ShapeDtypeStruct(array.shape, array.dtype),
        in_specs=[ANYWHERE] * (1 + len(after)),
        out_specs=ANYWHERE,
        input_output_aliases={0: 0},
        compiler_params=params(SMALL),
        name="hold",
    )(array, *after)


def gather_two(first, second, after):
    count = first.shape[0]

    def kernel(first_ref, second_ref, *refs):
        out_ref, sems = refs[len(after) :]
        start = mover(sems)
        copies = [start(first_ref, out_ref.at[:count]), start(second_ref, out_ref.at[count:])]
        for copy in copies:
            copy.wait()

    return pl.pallas_call(
        kernel,
        out_shape=jax.ShapeDtypeStruct((2 * count,) + first.shape[1:], first.dtype),
        in_specs=[ANYWHERE] * (2 + len(after)),
        out_specs=IN_VMEM,
        scratch_shapes=[pltpu.SemaphoreType.DMA((2,))],
        compiler_params=params(SMALL),
        name="gather_two",
    )(first, second, *after)


def widen(sent, gain, w_layer, out_layer, chunk):
    tokens = sent.shape[0]
    head, width = out_layer.shape
    wide = w_layer.shape[1]
    cuts = [slice(at, at + chunk) for at in range(0, width, chunk)]

    def kernel(v_ref, g_ref, w_ref, o_ref, back_ref, pair_ref, back_in, w_in, o_in, sems):
        start = mover(sems)
        loads = [
            (start(w_ref.at[cut], w_in.at[cut]), start(o_ref.at[:, cut], o_in.at[:, cut]))
            for cut in cuts
        ]
        stores = []
        for i, (cut, mine) in enumerate(zip(cuts, loads)):
            for load in mine:
                load.wait()
            back = dot_nt(v_ref[:, :wide], w_in[cut, :])
            own = back * g_ref[:, cut] + dot_nn(v_ref[:, wide:], o_in[:, cut])
            back_in[:, cut] = back.astype(BF16)
            stores.append(start(back_in.at[:, cut], back_ref.at[:, cut]))
            pair_ref[0, i] = own.astype(BF16)
            pair_ref[1, i] = jnp.zeros_like(pair_ref[1, i])
        for store in stores:
            store.wait()

    return pl.pallas_call(
        kernel,
        out_shape=[
            pltpu.HBM((tokens, width), BF16),
            pltpu.VMEM((2, len(cuts), tokens, chunk), BF16),
        ],
        in_specs=[IN_VMEM, IN_VMEM, IN_HBM, IN_HBM],
        out_specs=[IN_HBM, IN_VMEM],
        scratch_shapes=[
            pltpu.VMEM((tokens, width), BF16),
            pltpu.VMEM((width, wide), BF16),
            pltpu.VMEM((head, width), BF16),
            pltpu.SemaphoreType.DMA((3 * len(cuts),)),
        ],
        compiler_params=params(),
        name="widen",
    )(in_vmem(sent), gain, in_hbm(w_layer), in_hbm(out_layer))


def settle(total, mixes, stacks, places, x, cotangent, back, chunk, part, parts):
    tokens, width = x.shape
    layers, rows = stacks[0].shape[1:3]
    entries = [(i, e) for i, stack in enumerate(stacks) for e in range(stack.shape[0])]
    plane = len(entries)
    head = plane * rows
    span = width // parts
    base = part * span
    cuts = [slice(at, at + chunk) for at in range(0, span, chunk)]
    copies = plane * layers + 3 * len(cuts)

    def kernel(p_ref, t_ref, a_ref, x_ref, c_ref, back_ref, *refs):
        stack_refs = refs[: len(stacks)]
        rest_ref, dg_ref = refs[len(stacks) : len(stacks) + 2]
        lower, x_in, c_in, back_in, sems = refs[len(stacks) + 2 :]
        start = mover(sems)
        first = []
        for at, (i, e) in enumerate(entries):
            for r in range(layers):
                here = pl.ds(base, span)
                first.append(start(stack_refs[i].at[e, r, :, here], lower.at[r, p_ref[at]]))
        loads = []
        for cut in cuts:
            there = pl.ds(base + cut.start, chunk)
            mine = [start(x_ref.at[:, there], x_in.at[:, cut])]
            mine.append(start(c_ref.at[:, there], c_in.at[:, cut]))
            mine.append(start(back_ref.at[:, there], back_in.at[:, cut]))
            loads.append(mine)
        for load in first:
            load.wait()
        for i, (cut, mine) in enumerate(zip(cuts, loads)):
            for load in mine:
                load.wait()
            below = lower[:, :, :, cut].reshape(layers * head, chunk)
            here = x_in[:, cut].astype(F32) + dot_nn(a_ref[...], below)
            rest_ref[i] = (c_in[:, cut].astype(F32) - t_ref[...] * here).astype(BF16)
            gain = jnp.sum(back_in[:, cut].astype(F32) * here, axis=0, keepdims=True)
            for at in range(0, chunk, head):
                row = (cut.start + at) // head
                dg_ref[row : row + 1, :] = gain[:, at : at + head]

    return pl.pallas_call(
        kernel,
        out_shape=[
            pltpu.VMEM((len(cuts), tokens, chunk), BF16),
            pltpu.VMEM((span // head, head), F32),
        ],
        in_specs=[IN_SMEM] + [IN_VMEM] * 2 + [IN_HBM] * (3 + len(stacks)),
        out_specs=[IN_VMEM] * 2,
        scratch_shapes=[
            pltpu.VMEM((layers, plane, rows, span), BF16),
            pltpu.VMEM((tokens, span), BF16),
            pltpu.VMEM((tokens, span), BF16),
            pltpu.VMEM((tokens, span), BF16),
            pltpu.SemaphoreType.DMA((copies,)),
        ],
        compiler_params=params(),
        name="settle",
    )(
        places,
        in_vmem(total),
        in_vmem(mixes),
        *[in_hbm(array) for array in (x, cotangent, back, *stacks)],
    )


def join(index, arrived, pair, cols, after):
    tokens, part = arrived.shape

    def kernel(i_ref, r_ref, _, *refs):
        send_ref, pair_ref = refs[len(after) :]
        at = i_ref[0]
        r = r_ref[...]
        send_ref[...] = (pair_ref[0, at, :, cols].astype(F32) + r.astype(F32)).astype(BF16)
        pair_ref[1, at, :, cols] = r

    return pl.pallas_call(
        kernel,
        out_shape=[pltpu.VMEM((tokens, part), BF16), pltpu.VMEM(pair.shape, BF16)],
        in_specs=[IN_SMEM] + [IN_VMEM] * 2 + [ANYWHERE] * len(after),
        out_specs=[IN_VMEM] * 2,
        input_output_aliases={2: 1},
        compiler_params=params(SMALL),
        name="join",
    )(index, in_vmem(arrived), in_vmem(pair), *after)


def finish(index, arrived, pair, rests, streams):
    _, count, tokens, chunk = pair.shape

    def kernel(i_ref, *refs):
        r_refs = refs[: len(streams)]
        pair_ref, rest_refs = refs[len(streams)], refs[len(streams) + 1 :][: len(rests)]
        whole_ref, whole, sems = refs[len(streams) + 1 + len(rests) :]
        each = count // len(rests)
        at = i_ref[0]
        copies = []
        for i in range(count):
            full = rest_refs[i // each][i % each].astype(F32) + pair_ref[0, i].astype(F32)
            whole[i] = (full + pair_ref[1, i].astype(F32)).astype(BF16)

            @pl.when(at == i)
            def _(i=i, full=full):
                for ref, cols in zip(r_refs, streams):
                    whole[i, :, cols] = (full[:, cols] + ref[...].astype(F32)).astype(BF16)

            there = whole_ref.at[:, pl.ds(i * chunk, chunk)]
            copies.append(pltpu.make_async_copy(whole.at[i], there, sems.at[i]))
            copies[-1].start()
        for copy in copies:
            copy.wait()

    return pl.pallas_call(
        kernel,
        out_shape=pltpu.HBM((tokens, count * chunk), BF16),
        in_specs=[IN_SMEM] + [IN_VMEM] * (len(streams) + 1 + len(rests)),
        out_specs=IN_HBM,
        scratch_shapes=[
            pltpu.VMEM((count, tokens, chunk), BF16),
            pltpu.SemaphoreType.DMA((count,)),
        ],
        compiler_params=params(SMALL),
        name="finish",
    )(index, *[in_vmem(array) for array in (*arrived, pair, *rests)])


def stacked(arrays):
    rows = arrays[0].shape[0]

    def kernel(*refs):
        for i, ref in enumerate(refs[:-1]):
            refs[-1][i * rows : (i + 1) * rows, :] = ref[...]

    return pl.pallas_call(
        kernel,
        out_shape=pltpu.VMEM((len(arrays) * rows, arrays[0].shape[1]), F32),
        in_specs=[IN_VMEM] * len(arrays),
        out_specs=IN_VMEM,
        compiler_params=params(SMALL),
        name="stacked",
    )(*[in_vmem(array) for array in arrays])


def added(arrays):
    def kernel(*refs):
        total = refs[0][...]
        for ref in refs[1:-1]:
            total = total + ref[...]
        refs[-1][...] = total

    return pl.pallas_call(
        kernel,
        out_shape=pltpu.VMEM(arrays[0].shape, F32),
        in_specs=[IN_VMEM] * len(arrays),
        out_specs=IN_VMEM,
        compiler_params=params(SMALL),
        name="added",
    )(*[in_vmem(array) for array in arrays])


STREAMS = 1
CHUNKS = 4
PARTS = 1


def stream_columns(chunk):
    lanes = 128
    tiles = chunk // lanes
    ends = [-(-tiles * (i + 1) // STREAMS) * lanes for i in range(STREAMS)]
    return [slice(start, end) for start, end in zip([0] + ends, ends)]


def shifted(array, by):
    sections = lax.axis_size("section")
    return lax.ppermute(array, "section", [(i, (i + by) % sections) for i in range(sections)])


def raised(array, by):
    sections = lax.axis_size("section")
    return lax.ppermute(array, "section", [(i, i + by) for i in range(sections - by)])


def swapped(array, step):
    groups = lax.axis_size("group")
    devices = lax.axis_size("dp")
    bits = devices.bit_length() - 1
    pairs = []
    for p in range(devices):
        for g in range(groups):
            pairs.append((p * groups + g, (p ^ (1 << ((step + g) % bits))) * groups + g))
    return lax.ppermute(array, ("dp", "group"), pairs)


def handed(array, by):
    groups = lax.axis_size("group")
    return lax.ppermute(array, "group", [(i, (i + by) % groups) for i in range(groups)])


def plane_places():
    groups = lax.axis_size("group")
    bits = lax.axis_size("dp").bit_length() - 1
    masks = []
    for g in range(groups):
        order = [0]
        for step in range(bits):
            order = order + [m ^ (1 << ((step + g) % bits)) for m in order]
        masks.append(order)
    masks = jnp.asarray(masks, jnp.int32)
    dp, member = lax.axis_index("dp"), lax.axis_index("group")
    places = []
    for r in range(groups):
        giver = (member + groups - r) % groups
        places.append((dp ^ masks[giver]) * groups + giver)
    return jnp.concatenate(places).astype(jnp.int32)


def local(tokens_in, cotangent, gains, w_qkv, w_out, segments, plan):
    sections = lax.axis_size("section")
    groups = lax.axis_size("group")
    devices = lax.axis_size("dp")
    plane = devices * groups
    section = lax.axis_index("section")
    member = lax.axis_index("group")
    rows_dev = plan.shape[1]
    length = segments.shape[1]
    tokens, width = tokens_in.shape
    head = w_out.shape[1]
    share = rows_dev // groups
    w_layer, out_layer = w_qkv[0], w_out[0]
    place = member.astype(jnp.int32)[None]
    layer = section.astype(jnp.int32)[None]

    slice_rows = head // plane
    mine = lax.axis_index("dp") * groups + member
    own_rows, *parts = pick(
        tokens_in.reshape(rows_dev, length, width),
        plan,
        place,
        groups,
        out_layer,
        mine.astype(jnp.int32)[None],
        slice_rows,
    )
    slices = [raised(own_rows, r) for r in range(sections - 1, 0, -1)]
    slices = [own_rows] + slices[::-1]
    chosen = jnp.take(segments, plan[0], axis=0, mode="clip").astype(BF16)
    chosen = chosen.reshape(groups, share, length)
    moved, moved_seg = [], []
    for r in range(groups):
        outgoing = lax.dynamic_index_in_dim(chosen, (member + r) % groups, 0, keepdims=False)
        moved.append(handed(parts[r], r) if r else parts[r])
        moved_seg.append(handed(outgoing, r) if r else outgoing)
    moved = [part.reshape(share * length, width) for part in moved]
    order = (member - jnp.arange(groups)) % groups
    seg = jnp.take(jnp.stack(moved_seg), order, axis=0, mode="clip").reshape(tokens)
    at = jnp.arange(tokens)
    mask = (
        (at[:, None] >= at[None, :])
        & (at[:, None] // length == at[None, :] // length)
        & (seg[:, None] == seg[None, :])
    ).astype(F32)

    last = (section == sections - 1).astype(jnp.int32)[None]
    bits = devices.bit_length() - 1
    places = plane_places()
    x, xz, norms = project(
        moved, cotangent, gains, w_layer, out_layer, place, []
    )
    coupling, stack = couple(slices, gains, w_layer, out_layer, last, [mask, places, xz])
    others = [shifted(coupling, r) for r in range(1, sections)]

    streams = stream_columns(width // CHUNKS)

    def facing(array, by):
        return lax.ppermute(array, "section", [(i, i ^ by) for i in range(sections)])

    arrays, masks, by = [hold(xz, others)], [0], sections // 2
    while by > 0:
        arrays = arrays + [facing(array, by) for array in arrays]
        masks = masks + [mask_of ^ by for mask_of in masks]
        by = by // 2
    xz_all = [arrays[masks.index(r)] for r in range(sections)]
    early = [xz_all[r] for r in range(1, sections) if r & (r - 1) == 0]
    late = [xz_all[r] for r in range(1, sections) if r & (r - 1) != 0]
    pieces = [compact([coupling] + others, layer, 3 * head, head, [xz])]

    rows = [stack[None]]
    for step in range(bits):
        if step > 0:
            pieces = [merge(*pieces, early)]
        pieces = pieces + [swapped(pieces[0], step)]
        if step == bits - 1:
            pieces[-1] = hold(pieces[-1], late)
        if step > 0:
            rows = [gather_two(*rows, pieces[-1:])]
        rows = rows + [swapped(rows[0], step)]
    pieces = pieces + [handed(array, r) for r in range(1, groups) for array in pieces]
    sent, total, mixes, *leaving = serial(
        xz_all, pieces, places, norms, mask, layer, gains, w_layer, out_layer, streams
    )
    back, pair = widen(sent, gains, w_layer, out_layer, width // CHUNKS)

    down = [(i, i - 1) for i in range(1, sections)]
    behind = sections - 1 - section

    def index(tick):
        return jnp.clip(tick - behind, 0, CHUNKS - 1).astype(jnp.int32)[None]

    def lowered(arrays):
        return [lax.ppermute(array, "section", down) for array in arrays]

    ticks = CHUNKS + sections - 1
    after = {}
    for tick in range(1, ticks):
        arrived = lowered(leaving)
        if tick < ticks - 1:
            for i, cols in enumerate(streams):
                leaving[i], pair = join(
                    index(tick), arrived[i], pair, cols, after.get(tick, [])
                )
        if tick == 1:
            rows = [hold(array, leaving) for array in rows]
            rows = rows + [handed(array, r) for r in range(1, groups) for array in rows]
            rests, halves = [], []
            for part in range(PARTS):
                rest, half = settle(
                    total, mixes, rows, places, x, cotangent, back, width // CHUNKS, part, PARTS
                )
                rests.append(rest)
                halves.append(half)
            sums = [stacked(halves)]
            for step in range(bits):
                sums.append(added([sums[-1], swapped(sums[-1], step)]))
            sums.append(added(sums[-1:] + [handed(sums[-1], r) for r in range(1, groups)]))
            gain_whole = sums[-1].reshape(1, width)
            after = {2 + i: [array] for i, array in enumerate(sums)}
    out = finish(index(ticks - 1), arrived, pair, rests, streams)
    return (out[None], gain_whole)


def attend(hidden, segment, gain_row, w_layer, out_layer):
    count, length, width = hidden.shape
    head = out_layer.shape[0]
    scaled = hidden * lax.rsqrt(jnp.mean(hidden * hidden, axis=-1, keepdims=True) + EPS) * gain_row
    normed = scaled.astype(BF16).reshape(count * length, width)
    projected = jnp.dot(normed, w_layer, preferred_element_type=F32).reshape(count, length, 3 * head)
    query = projected[:, :, :head]
    keyed = projected[:, :, head : 2 * head]
    valued = projected[:, :, 2 * head :]
    positions = jnp.arange(length)
    allowed = (positions[:, None] >= positions[None, :])[None] & (
        segment[:, :, None] == segment[:, None, :]
    )
    scores = jnp.einsum("rid,rjd->rij", query, keyed, precision=lax.Precision.HIGHEST)
    scores = jnp.where(allowed, scores / math.sqrt(head), -1e30)
    weights = jax.nn.softmax(scores, axis=-1)
    mixed = jnp.einsum("rij,rjd->rid", weights, valued, precision=lax.Precision.HIGHEST)
    mixed = mixed.astype(BF16).reshape(count * length, head)
    output = jnp.dot(mixed, out_layer, preferred_element_type=F32).reshape(count, length, width)
    return hidden + output


MB_ROWS = 2


def relay(tokens_in, cotangent, gains, w_qkv, w_out, segments, plan):
    sections = lax.axis_size("section")
    section = lax.axis_index("section")
    rows_dev = plan.shape[1]
    width = tokens_in.shape[1]
    length = segments.shape[1]
    micro = rows_dev // MB_ROWS
    blocks = tokens_in.reshape(rows_dev, length, width)
    chosen = jnp.take(blocks, plan[0], axis=0)
    chosen_seg = jnp.take(segments, plan[0], axis=0).astype(BF16)
    assigned = lax.all_to_all(chosen, "group", split_axis=0, concat_axis=0, tiled=True)
    moved_seg = lax.all_to_all(chosen_seg, "group", split_axis=0, concat_axis=0, tiled=True)
    assigned = assigned.reshape(micro, MB_ROWS, length, width)
    seg_groups = moved_seg.reshape(micro, MB_ROWS, length)
    gain_row, w_layer, out_layer = gains[0], w_qkv[0], w_out[0]
    grad_rows = cotangent.reshape(micro, MB_ROWS, length, width)
    ticks = micro + sections - 1

    def passed_along(array, by):
        pairs = [(i, i + by) for i in range(sections) if 0 <= i + by < sections]
        return lax.ppermute(array, "section", pairs)

    def at(array, i):
        return lax.dynamic_index_in_dim(array, i, 0, keepdims=False)

    def forward_tick(tick, carry):
        saved, arrived = carry
        index = tick - section
        valid = (index >= 0) & (index < micro)
        clipped = jnp.clip(index, 0, micro - 1)
        entering = jnp.where(section == 0, at(assigned, clipped), arrived)
        kept = jnp.where(valid, entering, at(saved, clipped))
        saved = lax.dynamic_update_index_in_dim(saved, kept, clipped, 0)
        segment = at(seg_groups, clipped)

        def run_layer(value):
            return attend(value.astype(F32), segment, gain_row, w_layer, out_layer).astype(BF16)

        leaving = lax.cond(valid, run_layer, jnp.zeros_like, entering)
        return (saved, passed_along(leaving, 1))

    saved_init = jnp.zeros((micro, MB_ROWS, length, width), BF16)
    arrive_init = jnp.zeros((MB_ROWS, length, width), BF16)
    saved, _ = lax.fori_loop(0, ticks, forward_tick, (saved_init, arrive_init))

    def backward_tick(tick, carry):
        grads_x, gain_total, arrived = carry
        index = tick - (sections - 1 - section)
        valid = (index >= 0) & (index < micro)
        clipped = jnp.clip(index, 0, micro - 1)
        entering = jnp.where(section == sections - 1, at(grad_rows, clipped), arrived)
        segment = at(seg_groups, clipped)
        stored = at(saved, clipped).astype(F32)

        def local_layer(hidden, gains_here):
            return attend(hidden, segment, gains_here, w_layer, out_layer)

        def run_back(value):
            _, pullback = jax.vjp(local_layer, stored, gain_row)
            grad_hidden, grad_gain = pullback(value.astype(F32))
            return (grad_hidden.astype(BF16), grad_gain)

        def skip_back(value):
            return (jnp.zeros_like(value), jnp.zeros(gain_row.shape, F32))

        sending, grad_gain = lax.cond(valid, run_back, skip_back, entering)
        kept = jnp.where(valid, sending, at(grads_x, clipped))
        grads_x = lax.dynamic_update_index_in_dim(grads_x, kept, clipped, 0)
        return (grads_x, gain_total + grad_gain, passed_along(sending, -1))

    gain_init = jnp.zeros(gain_row.shape, F32)
    grads_x, gain_total, _ = lax.fori_loop(
        0, ticks, backward_tick, (saved_init, gain_init, arrive_init)
    )
    gain_whole = lax.psum(gain_total, ("dp", "group"))
    return (grads_x.reshape(1, rows_dev * length, width), gain_whole[None])


def solution(mesh):
    placed = (
        P(("dp", "group"), None),
        P(("dp", "group"), None),
        P("section", None),
        P("section", None, None),
        P("section", None, None),
        P(("dp", "group"), None),
        P(("dp", "group"), None),
    )

    def chosen(tokens_in, cotangent, gains, w_qkv, w_out, segments, plan):
        sections, head, width = w_out.shape
        devices = mesh.shape["dp"]
        small = sections * 4 * head < width and sections > 1
        halves = devices & (devices - 1) == 0 and sections & (sections - 1) == 0
        body = local if small and halves else relay
        return jax.shard_map(
            body,
            mesh=mesh,
            in_specs=placed,
            out_specs=(P("section", ("dp", "group"), None), P("section", None)),
            check_vma=False,
        )(tokens_in, cotangent, gains, w_qkv, w_out, segments, plan)

    return chosen
```

```python
import math

import jax
import jax.numpy as jnp
from jax import lax
from jax.experimental import pallas as pl
from jax.experimental.pallas import tpu as pltpu
from jax.sharding import PartitionSpec as P

EPS = 1e-05
VMEM_BYTES = 24 * 1024 * 1024
SMALL = 16 * 1024 * 1024
F32 = jnp.float32
BF16 = jnp.bfloat16


def dot_nn(a, b):
    return lax.dot_general(a, b, (((1,), (0,)), ((), ())), preferred_element_type=F32)


def dot_nt(a, b):
    return lax.dot_general(a, b, (((1,), (1,)), ((), ())), preferred_element_type=F32)


def dot_tn(a, b):
    return lax.dot_general(a, b, (((0,), (0,)), ((), ())), preferred_element_type=F32)


IN_HBM = pl.BlockSpec(memory_space=pltpu.HBM)
ANYWHERE = pl.BlockSpec(memory_space=pl.ANY)
IN_VMEM = pl.BlockSpec(memory_space=pltpu.VMEM)
IN_SMEM = pl.BlockSpec(memory_space=pltpu.SMEM)


def in_hbm(array):
    return pltpu.with_memory_space_constraint(array, pltpu.HBM)


def in_vmem(array):
    return pltpu.with_memory_space_constraint(array, pltpu.VMEM)


def mover(sems):
    used = []

    def start(source, target):
        copy = pltpu.make_async_copy(source, target, sems.at[len(used)])
        copy.start()
        used.append(copy)
        return copy

    return start


def steps(width):
    step = min(width, 1024)
    return [slice(at, at + step) for at in range(0, width, step)]


def params(limit=VMEM_BYTES):
    return pltpu.CompilerParams(vmem_limit_bytes=limit)


def pick(tokens, plan, place, groups, out_layer, mine, slice_rows):
    rows, length, width = tokens.shape
    share = rows // groups

    def kernel(plan_ref, place_ref, mine_ref, tokens_ref, o_ref, *rest):
        slice_ref, parts = rest[0], rest[1 : 1 + groups]
        slice_in, rows_in, sems = rest[1 + groups :]
        start = mover(sems)
        at = pl.ds(pl.multiple_of(mine_ref[0] * slice_rows, slice_rows), slice_rows)
        loads = [(start(o_ref.at[at], slice_in), slice_in, slice_ref)]
        for r in range(groups):
            target = lax.rem(place_ref[0] + r, groups)
            for c in range(share):
                here = rows_in.at[r * share + c]
                row = plan_ref[0, target * share + c]
                loads.append((start(tokens_ref.at[row], here), here, parts[r].at[c]))
        stores = []
        for load, here, there in loads:
            load.wait()
            stores.append(start(here, there))
        for store in stores:
            store.wait()

    return pl.pallas_call(
        kernel,
        out_shape=[pltpu.HBM((slice_rows, width), BF16)]
        + [pltpu.HBM((share, length, width), BF16)] * groups,
        in_specs=[IN_SMEM, IN_SMEM, IN_SMEM, IN_HBM, IN_HBM],
        out_specs=[IN_HBM] * (1 + groups),
        scratch_shapes=[
            pltpu.VMEM((slice_rows, width), BF16),
            pltpu.VMEM((rows, length, width), BF16),
            pltpu.SemaphoreType.DMA((2 * rows + 2,)),
        ],
        compiler_params=params(),
        name="pick",
    )(plan, place, mine, in_hbm(tokens), in_hbm(out_layer))


def project(parts, cotangent, gain, w_layer, out_layer, place, after):
    groups = len(parts)
    tokens, width = cotangent.shape
    head = out_layer.shape[0]
    wide = w_layer.shape[1]
    block = tokens // groups
    cuts = steps(width)
    copies = len(cuts) * (groups + 4)

    def kernel(place_ref, *refs):
        part_refs = refs[:groups]
        cot_ref, g_ref, w_ref, o_ref = refs[groups : groups + 4]
        x_ref, xz_ref, n_ref = refs[groups + 4 + len(after) : groups + 7 + len(after)]
        x_in, c_in, w_in, o_in, sems = refs[groups + 7 + len(after) :]
        start = mover(sems)
        loads = []
        for cut in cuts:
            mine = [start(w_ref.at[cut], w_in.at[cut])]
            mine.append(start(o_ref.at[:, cut], o_in.at[:, cut]))
            for r in range(groups):
                source = lax.rem(place_ref[0] + groups - r, groups)
                rows = pl.ds(pl.multiple_of(source * block, block), block)
                mine.append(start(part_refs[r].at[:, cut], x_in.at[rows, cut]))
            mine.append(start(cot_ref.at[:, cut], c_in.at[:, cut]))
            loads.append(mine)
        through = jnp.zeros((tokens, wide), F32)
        across = jnp.zeros((tokens, head), F32)
        back = jnp.zeros((tokens, head), F32)
        square = jnp.zeros((tokens, 1), F32)
        stores = []
        for cut, mine in zip(cuts, loads):
            for load in mine:
                load.wait()
            stores.append(start(x_in.at[:, cut], x_ref.at[:, cut]))
            x = x_in[:, cut]
            xf = x.astype(F32)
            through += dot_nn((xf * g_ref[:, cut]).astype(BF16), w_in[cut, :])
            across += dot_nt(x, o_in[:, cut])
            back += dot_nt(c_in[:, cut], o_in[:, cut])
            square += jnp.sum(xf * xf, axis=1, keepdims=True)
        xz_ref[:, :wide] = through.astype(BF16)
        xz_ref[:, wide : wide + head] = across.astype(BF16)
        xz_ref[:, wide + head :] = back.astype(BF16)
        n_ref[...] = square
        for store in stores:
            store.wait()

    return pl.pallas_call(
        kernel,
        out_shape=[
            pltpu.HBM((tokens, width), BF16),
            jax.ShapeDtypeStruct((tokens, wide + 2 * head), BF16),
            jax.ShapeDtypeStruct((tokens, 1), F32),
        ],
        in_specs=[IN_SMEM]
        + [ANYWHERE] * groups
        + [IN_HBM, IN_VMEM, IN_HBM, IN_HBM]
        + [ANYWHERE] * len(after),
        out_specs=[IN_HBM, IN_VMEM, IN_VMEM],
        scratch_shapes=[
            pltpu.VMEM((tokens, width), BF16),
            pltpu.VMEM((tokens, width), BF16),
            pltpu.VMEM((width, wide), BF16),
            pltpu.VMEM((head, width), BF16),
            pltpu.SemaphoreType.DMA((copies,)),
        ],
        compiler_params=params(),
        name="project",
    )(
        place,
        *parts,
        in_hbm(cotangent),
        gain,
        in_hbm(w_layer),
        in_hbm(out_layer),
        *after,
    )


def couple(slices, gain, w_layer, out_layer, last, after):
    sections = len(slices)
    count, width = slices[0].shape
    head = out_layer.shape[0]
    wide = w_layer.shape[1]
    below = (sections - 2) * wide
    packed = below + max(wide, (sections - 1) * head)
    cuts = steps(width)
    copies = len(cuts) * (sections + 2) + sections - 1

    def kernel(last_ref, *refs):
        s_refs = refs[:sections][::-1]
        g_ref, w_ref, o_ref = refs[sections : sections + 3]
        out_ref, stack_ref, r_in, w_in, o_in, sems = refs[sections + 3 + len(after) :]
        rows = [slice(r * count, (r + 1) * count) for r in range(sections)]
        start = mover(sems)
        loads = []
        for cut in cuts:
            mine = [start(w_ref.at[cut], w_in.at[cut])]
            mine.append(start(o_ref.at[:, cut], o_in.at[:, cut]))
            for r in range(sections):
                mine.append(start(s_refs[r].at[:, cut], r_in.at[rows[r], cut]))
            loads.append(mine)
        through = jnp.zeros((sections * count, wide), F32)
        across = jnp.zeros((sections * count, head), F32)
        for cut, mine in zip(cuts, loads):
            for load in mine:
                load.wait()
            r = r_in[:, cut]
            through += dot_nn((r.astype(F32) * g_ref[:, cut]).astype(BF16), w_in[cut, :])
            across += dot_nt(r, o_in[:, cut])
        stores = [start(r_in.at[rows[r]], stack_ref.at[r - 1]) for r in range(1, sections)]
        through = through.astype(BF16)
        across = across.astype(BF16)
        out_ref[...] = jnp.zeros_like(out_ref)
        for r in range(1, sections - 1):
            out_ref[:, (r - 1) * wide : r * wide] = through[rows[r]]

        @pl.when(last_ref[0] == 1)
        def _():
            out_ref[:, below : below + wide] = through[rows[-1]]

        @pl.when(last_ref[0] == 0)
        def _():
            for r in range(sections - 1):
                out_ref[:, below + r * head : below + (r + 1) * head] = across[rows[r]]

        for store in stores:
            store.wait()

    return pl.pallas_call(
        kernel,
        out_shape=[
            jax.ShapeDtypeStruct((count, packed), BF16),
            pltpu.HBM((sections - 1, count, width), BF16),
        ],
        in_specs=[IN_SMEM]
        + [ANYWHERE] * sections
        + [IN_VMEM, IN_HBM, IN_HBM]
        + [ANYWHERE] * len(after),
        out_specs=[IN_VMEM, IN_HBM],
        scratch_shapes=[
            pltpu.VMEM((sections * count, width), BF16),
            pltpu.VMEM((width, wide), BF16),
            pltpu.VMEM((head, width), BF16),
            pltpu.SemaphoreType.DMA((copies,)),
        ],
        compiler_params=params(),
        name="couple",
    )(last, *slices[::-1], gain, in_hbm(w_layer), in_hbm(out_layer), *after)


def layout(sections, wide, head):
    through, across, at = {}, {}, 0
    for k in range(sections):
        for j in range(k):
            through[j, k] = slice(at, at + wide)
            at += wide
        for j in range(k + 1 if k < sections - 1 else 0):
            across[j, k] = slice(at, at + head)
            at += head
    return through, across, at


def compact(parts, section, wide, head, after):
    sections = len(parts)
    count = parts[0].shape[0]
    below = (sections - 2) * wide
    through, across, total = layout(sections, wide, head)

    def kernel(s_ref, *refs):
        part_refs, out_ref = refs[:sections], refs[-1]
        mine = s_ref[0]

        def fill(k, r):
            for j in range(k):
                at = (k - j - 1) * wide
                out_ref[0, :, through[j, k]] = part_refs[r][:, at : at + wide]
            for j in range(k + 1 if k < sections - 1 else 0):
                at = below + (k - j) * head
                out_ref[0, :, across[j, k]] = part_refs[r][:, at : at + head]

        for s in range(sections):

            @pl.when(mine == s)
            def _(s=s):
                for r in range(sections):
                    fill((s - r) % sections, r)

    vmem = pl.BlockSpec(memory_space=pltpu.VMEM)
    return pl.pallas_call(
        kernel,
        out_shape=jax.ShapeDtypeStruct((1, count, total), BF16),
        in_specs=[IN_SMEM] + [vmem] * sections + [ANYWHERE] * len(after),
        out_specs=vmem,
        compiler_params=params(SMALL),
        name="compact",
    )(section, *parts, *after)


def merge(first, second, after):
    count = first.shape[0]

    def kernel(first_ref, second_ref, *refs):
        refs[-1][:count] = first_ref[...]
        refs[-1][count:] = second_ref[...]

    return pl.pallas_call(
        kernel,
        out_shape=jax.ShapeDtypeStruct((2 * count,) + first.shape[1:], first.dtype),
        in_specs=[IN_VMEM] * 2 + [ANYWHERE] * len(after),
        out_specs=IN_VMEM,
        compiler_params=params(SMALL),
        name="merge",
    )(first, second, *after)


def serial(xz, pieces, places, norms, mask, section, gain, w_layer, out_layer, streams):
    sections = len(xz)
    tokens = norms.shape[0]
    head, width = out_layer.shape
    wide = 3 * head
    scale = 1.0 / math.sqrt(head)
    lead = slice(0, streams[-1].stop)
    through_at, across_at, _ = layout(sections, wide, head)
    count, packed = pieces[0].shape[-2:]
    plane = head // count
    n_in = sections + len(pieces)
    copies = sections + plane + 2

    def kernel(s_ref, p_ref, *refs):
        xz_refs, piece_refs = refs[:sections], refs[sections:n_in]
        n_ref, mask_ref, g_ref, w_ref, o_ref = refs[n_in : n_in + 5]
        n_out = n_in + 5
        v_ref, t_ref, a_ref = refs[n_out : n_out + 3]
        first_refs = refs[n_out + 3 : n_out + 3 + len(streams)]
        scratch = refs[n_out + 3 + len(streams) :]
        xz_all, table, mixes, weights, projs, dmix, w_in, o_in, sems = scratch
        mine = s_ref[0]
        started = []

        def start(source, target):
            copy = pltpu.make_async_copy(source, target, sems.at[len(started)])
            copy.start()
            started.append(copy)

        for r in range(sections):
            start(xz_refs[r], xz_all.at[mine ^ r])
        at = 0
        for ref in piece_refs:
            for i in range(ref.shape[0]):
                start(ref.at[i], table.at[p_ref[at]])
                at += 1
        small = list(started)
        start(w_ref.at[lead], w_in)
        start(o_ref.at[:, lead], o_in)
        for copy in small:
            copy.wait()

        def through(j, k):
            return table[:, :, through_at[j, k]].reshape(head, wide)

        def across(j, k):
            return table[:, :, across_at[j, k]].reshape(head, head)

        allowed = mask_ref[...] > 0.5
        norm = n_ref[...]
        rstds, tails, mixed = [], [], []
        for s in range(sections):
            proj = xz_all[s, :, :wide].astype(F32)
            for j in range(s):
                proj = proj + dot_nn(mixed[j], through(j, s))
            rstd = lax.rsqrt(norm * (1.0 / width) + EPS)
            proj = proj * rstd
            projs[s] = proj.astype(BF16)
            q, k, v = (projs[s, :, i * head : (i + 1) * head] for i in range(3))
            scores = jnp.where(allowed, dot_nt(q, k) * scale, -1e30)
            scores = jnp.exp(scores - jnp.max(scores, axis=1, keepdims=True))
            soft = scores / jnp.sum(scores, axis=1, keepdims=True)
            weights[s] = soft
            mix = dot_nn(soft.astype(BF16), v).astype(BF16)
            mixed.append(mix)
            mixes[:, s * head : (s + 1) * head] = mix
            rstds.append(rstd)
            dmix[:, s * head : (s + 1) * head] = xz_all[s, :, wide + head :].astype(F32)
            if s == sections - 1:
                break
            y = xz_all[s, :, wide : wide + head].astype(F32)
            for j in range(s):
                y = y + dot_nn(mixed[j], across(j, s))
            tail = y + dot_nn(mix, across(s, s))
            norm = norm + jnp.sum(mix.astype(F32) * (y + tail), axis=1, keepdims=True)
            norm = jnp.maximum(norm, 0.0)
            tails.append(tail)
        total = jnp.zeros((tokens, 1), F32)
        a_ref[...] = jnp.zeros_like(a_ref)
        for s in reversed(range(sections)):
            cols = slice(s * head, (s + 1) * head)
            da = dmix[:, cols]
            if s < sections - 1:
                da = da - total * tails[s]
            da = da.astype(BF16)
            q, k, v = (projs[s, :, i * head : (i + 1) * head] for i in range(3))
            soft = weights[s]
            dv = dot_tn(soft.astype(BF16), da)
            dsoft = dot_nt(da, v)
            dscore = soft * (dsoft - jnp.sum(dsoft * soft, axis=1, keepdims=True))
            dscore = (dscore * scale).astype(BF16)
            dproj = jnp.concatenate([dot_nn(dscore, k), dot_tn(dscore, q), dv], axis=1)
            along = jnp.sum(dproj * projs[s].astype(F32), axis=1, keepdims=True)
            first = (dproj * rstds[s]).astype(BF16)
            second = (-total * mixes[:, cols].astype(F32)).astype(BF16)
            total = total + rstds[s] * rstds[s] * along * (1.0 / width)
            for j in reversed(range(s)):
                term = dot_nt(first, through(j, s))
                if s < sections - 1:
                    term = term + dot_nt(second, across(j, s))
                dmix[:, j * head : (j + 1) * head] += term

            @pl.when(mine == s)
            def _(first=first, second=second, total=total):
                v_ref[:, :wide] = first
                v_ref[:, wide:] = second
                t_ref[...] = total

            for r in range(1, sections - s):

                @pl.when(mine == s + r)
                def _(r=r, cols=cols):
                    a_ref[:, (r - 1) * head : r * head] = mixes[:, cols]

        for copy in started[len(small) :]:
            copy.wait()
        own = dot_nt(v_ref[:, :wide], w_in[...]) * g_ref[:, lead]
        own = (own + dot_nn(v_ref[:, wide:], o_in[...])).astype(BF16)
        for ref, part in zip(first_refs, streams):
            ref[...] = own[:, part]

    vmem = pl.BlockSpec(memory_space=pltpu.VMEM)
    smem = pl.BlockSpec(memory_space=pltpu.SMEM)
    return pl.pallas_call(
        kernel,
        out_shape=[
            pltpu.VMEM((tokens, wide + head), BF16),
            pltpu.VMEM((tokens, 1), F32),
            pltpu.VMEM((tokens, (sections - 1) * head), BF16),
        ]
        + [pltpu.VMEM((tokens, part.stop - part.start), BF16) for part in streams],
        in_specs=[smem, smem] + [ANYWHERE] * n_in + [vmem, vmem, vmem, IN_HBM, IN_HBM],
        out_specs=[vmem] * (3 + len(streams)),
        scratch_shapes=[
            pltpu.VMEM((sections,) + xz[0].shape, BF16),
            pltpu.VMEM((plane, count, packed), BF16),
            pltpu.VMEM((tokens, sections * head), BF16),
            pltpu.VMEM((sections, tokens, tokens), F32),
            pltpu.VMEM((sections, tokens, wide), BF16),
            pltpu.VMEM((tokens, sections * head), F32),
            pltpu.VMEM((lead.stop, wide), BF16),
            pltpu.VMEM((head, lead.stop), BF16),
            pltpu.SemaphoreType.DMA((copies,)),
        ],
        compiler_params=params(),
        name="serial",
    )(
        section,
        places,
        *xz,
        *pieces,
        norms,
        mask,
        gain,
        in_hbm(w_layer),
        in_hbm(out_layer),
    )


def hold(array, after):
    def kernel(*refs):
        pass

    return pl.pallas_call(
        kernel,
        out_shape=jax.ShapeDtypeStruct(array.shape, array.dtype),
        in_specs=[ANYWHERE] * (1 + len(after)),
        out_specs=ANYWHERE,
        input_output_aliases={0: 0},
        compiler_params=params(SMALL),
        name="hold",
    )(array, *after)


def gather_two(first, second, after):
    count = first.shape[0]

    def kernel(first_ref, second_ref, *refs):
        out_ref, sems = refs[len(after) :]
        start = mover(sems)
        copies = [start(first_ref, out_ref.at[:count]), start(second_ref, out_ref.at[count:])]
        for copy in copies:
            copy.wait()

    return pl.pallas_call(
        kernel,
        out_shape=jax.ShapeDtypeStruct((2 * count,) + first.shape[1:], first.dtype),
        in_specs=[ANYWHERE] * (2 + len(after)),
        out_specs=IN_VMEM,
        scratch_shapes=[pltpu.SemaphoreType.DMA((2,))],
        compiler_params=params(SMALL),
        name="gather_two",
    )(first, second, *after)


def widen(sent, gain, w_layer, out_layer, chunk):
    tokens = sent.shape[0]
    head, width = out_layer.shape
    wide = w_layer.shape[1]
    cuts = [slice(at, at + chunk) for at in range(0, width, chunk)]

    def kernel(v_ref, g_ref, w_ref, o_ref, back_ref, pair_ref, back_in, w_in, o_in, sems):
        start = mover(sems)
        loads = [
            (start(w_ref.at[cut], w_in.at[cut]), start(o_ref.at[:, cut], o_in.at[:, cut]))
            for cut in cuts
        ]
        stores = []
        for i, (cut, mine) in enumerate(zip(cuts, loads)):
            for load in mine:
                load.wait()
            back = dot_nt(v_ref[:, :wide], w_in[cut, :])
            own = back * g_ref[:, cut] + dot_nn(v_ref[:, wide:], o_in[:, cut])
            back_in[:, cut] = back.astype(BF16)
            stores.append(start(back_in.at[:, cut], back_ref.at[:, cut]))
            pair_ref[0, i] = own.astype(BF16)
            pair_ref[1, i] = jnp.zeros_like(pair_ref[1, i])
        for store in stores:
            store.wait()

    return pl.pallas_call(
        kernel,
        out_shape=[
            pltpu.HBM((tokens, width), BF16),
            pltpu.VMEM((2, len(cuts), tokens, chunk), BF16),
        ],
        in_specs=[IN_VMEM, IN_VMEM, IN_HBM, IN_HBM],
        out_specs=[IN_HBM, IN_VMEM],
        scratch_shapes=[
            pltpu.VMEM((tokens, width), BF16),
            pltpu.VMEM((width, wide), BF16),
            pltpu.VMEM((head, width), BF16),
            pltpu.SemaphoreType.DMA((3 * len(cuts),)),
        ],
        compiler_params=params(),
        name="widen",
    )(in_vmem(sent), gain, in_hbm(w_layer), in_hbm(out_layer))


def settle(total, mixes, stacks, places, x, cotangent, back, chunk, part, parts):
    tokens, width = x.shape
    layers, rows = stacks[0].shape[1:3]
    entries = [(i, e) for i, stack in enumerate(stacks) for e in range(stack.shape[0])]
    plane = len(entries)
    head = plane * rows
    span = width // parts
    base = part * span
    cuts = [slice(at, at + chunk) for at in range(0, span, chunk)]
    copies = plane * layers + 3 * len(cuts)

    def kernel(p_ref, t_ref, a_ref, x_ref, c_ref, back_ref, *refs):
        stack_refs = refs[: len(stacks)]
        rest_ref, dg_ref = refs[len(stacks) : len(stacks) + 2]
        lower, x_in, c_in, back_in, sems = refs[len(stacks) + 2 :]
        start = mover(sems)
        first = []
        for at, (i, e) in enumerate(entries):
            for r in range(layers):
                here = pl.ds(base, span)
                first.append(start(stack_refs[i].at[e, r, :, here], lower.at[r, p_ref[at]]))
        loads = []
        for cut in cuts:
            there = pl.ds(base + cut.start, chunk)
            mine = [start(x_ref.at[:, there], x_in.at[:, cut])]
            mine.append(start(c_ref.at[:, there], c_in.at[:, cut]))
            mine.append(start(back_ref.at[:, there], back_in.at[:, cut]))
            loads.append(mine)
        for load in first:
            load.wait()
        for i, (cut, mine) in enumerate(zip(cuts, loads)):
            for load in mine:
                load.wait()
            below = lower[:, :, :, cut].reshape(layers * head, chunk)
            here = x_in[:, cut].astype(F32) + dot_nn(a_ref[...], below)
            rest_ref[i] = (c_in[:, cut].astype(F32) - t_ref[...] * here).astype(BF16)
            gain = jnp.sum(back_in[:, cut].astype(F32) * here, axis=0, keepdims=True)
            for at in range(0, chunk, head):
                row = (cut.start + at) // head
                dg_ref[row : row + 1, :] = gain[:, at : at + head]

    return pl.pallas_call(
        kernel,
        out_shape=[
            pltpu.VMEM((len(cuts), tokens, chunk), BF16),
            pltpu.VMEM((span // head, head), F32),
        ],
        in_specs=[IN_SMEM] + [IN_VMEM] * 2 + [IN_HBM] * (3 + len(stacks)),
        out_specs=[IN_VMEM] * 2,
        scratch_shapes=[
            pltpu.VMEM((layers, plane, rows, span), BF16),
            pltpu.VMEM((tokens, span), BF16),
            pltpu.VMEM((tokens, span), BF16),
            pltpu.VMEM((tokens, span), BF16),
            pltpu.SemaphoreType.DMA((copies,)),
        ],
        compiler_params=params(),
        name="settle",
    )(
        places,
        in_vmem(total),
        in_vmem(mixes),
        *[in_hbm(array) for array in (x, cotangent, back, *stacks)],
    )


def join(index, arrived, pair, cols, after):
    tokens, part = arrived.shape

    def kernel(i_ref, r_ref, _, *refs):
        send_ref, pair_ref = refs[len(after) :]
        at = i_ref[0]
        r = r_ref[...]
        send_ref[...] = (pair_ref[0, at, :, cols].astype(F32) + r.astype(F32)).astype(BF16)
        pair_ref[1, at, :, cols] = r

    return pl.pallas_call(
        kernel,
        out_shape=[pltpu.VMEM((tokens, part), BF16), pltpu.VMEM(pair.shape, BF16)],
        in_specs=[IN_SMEM] + [IN_VMEM] * 2 + [ANYWHERE] * len(after),
        out_specs=[IN_VMEM] * 2,
        input_output_aliases={2: 1},
        compiler_params=params(SMALL),
        name="join",
    )(index, in_vmem(arrived), in_vmem(pair), *after)


def finish(index, arrived, pair, rests, streams):
    _, count, tokens, chunk = pair.shape

    def kernel(i_ref, *refs):
        r_refs = refs[: len(streams)]
        pair_ref, rest_refs = refs[len(streams)], refs[len(streams) + 1 :][: len(rests)]
        whole_ref, whole, sems = refs[len(streams) + 1 + len(rests) :]
        each = count // len(rests)
        at = i_ref[0]
        copies = []
        for i in range(count):
            full = rest_refs[i // each][i % each].astype(F32) + pair_ref[0, i].astype(F32)
            whole[i] = (full + pair_ref[1, i].astype(F32)).astype(BF16)

            @pl.when(at == i)
            def _(i=i, full=full):
                for ref, cols in zip(r_refs, streams):
                    whole[i, :, cols] = (full[:, cols] + ref[...].astype(F32)).astype(BF16)

            there = whole_ref.at[:, pl.ds(i * chunk, chunk)]
            copies.append(pltpu.make_async_copy(whole.at[i], there, sems.at[i]))
            copies[-1].start()
        for copy in copies:
            copy.wait()

    return pl.pallas_call(
        kernel,
        out_shape=pltpu.HBM((tokens, count * chunk), BF16),
        in_specs=[IN_SMEM] + [IN_VMEM] * (len(streams) + 1 + len(rests)),
        out_specs=IN_HBM,
        scratch_shapes=[
            pltpu.VMEM((count, tokens, chunk), BF16),
            pltpu.SemaphoreType.DMA((count,)),
        ],
        compiler_params=params(SMALL),
        name="finish",
    )(index, *[in_vmem(array) for array in (*arrived, pair, *rests)])


def stacked(arrays):
    rows = arrays[0].shape[0]

    def kernel(*refs):
        for i, ref in enumerate(refs[:-1]):
            refs[-1][i * rows : (i + 1) * rows, :] = ref[...]

    return pl.pallas_call(
        kernel,
        out_shape=pltpu.VMEM((len(arrays) * rows, arrays[0].shape[1]), F32),
        in_specs=[IN_VMEM] * len(arrays),
        out_specs=IN_VMEM,
        compiler_params=params(SMALL),
        name="stacked",
    )(*[in_vmem(array) for array in arrays])


def added(arrays):
    def kernel(*refs):
        total = refs[0][...]
        for ref in refs[1:-1]:
            total = total + ref[...]
        refs[-1][...] = total

    return pl.pallas_call(
        kernel,
        out_shape=pltpu.VMEM(arrays[0].shape, F32),
        in_specs=[IN_VMEM] * len(arrays),
        out_specs=IN_VMEM,
        compiler_params=params(SMALL),
        name="added",
    )(*[in_vmem(array) for array in arrays])


STREAMS = 2
CHUNKS = 4
PARTS = 1


def stream_columns(chunk):
    lanes = 128
    tiles = chunk // lanes
    ends = [-(-tiles * (i + 1) // STREAMS) * lanes for i in range(STREAMS)]
    return [slice(start, end) for start, end in zip([0] + ends, ends)]


def shifted(array, by):
    sections = lax.axis_size("section")
    return lax.ppermute(array, "section", [(i, (i + by) % sections) for i in range(sections)])


def raised(array, by):
    sections = lax.axis_size("section")
    return lax.ppermute(array, "section", [(i, i + by) for i in range(sections - by)])


def swapped(array, step):
    groups = lax.axis_size("group")
    devices = lax.axis_size("dp")
    bits = devices.bit_length() - 1
    pairs = []
    for p in range(devices):
        for g in range(groups):
            pairs.append((p * groups + g, (p ^ (1 << ((step + g) % bits))) * groups + g))
    return lax.ppermute(array, ("dp", "group"), pairs)


def handed(array, by):
    groups = lax.axis_size("group")
    return lax.ppermute(array, "group", [(i, (i + by) % groups) for i in range(groups)])


def plane_places():
    groups = lax.axis_size("group")
    bits = lax.axis_size("dp").bit_length() - 1
    masks = []
    for g in range(groups):
        order = [0]
        for step in range(bits):
            order = order + [m ^ (1 << ((step + g) % bits)) for m in order]
        masks.append(order)
    masks = jnp.asarray(masks, jnp.int32)
    dp, member = lax.axis_index("dp"), lax.axis_index("group")
    places = []
    for r in range(groups):
        giver = (member + groups - r) % groups
        places.append((dp ^ masks[giver]) * groups + giver)
    return jnp.concatenate(places).astype(jnp.int32)


def local(tokens_in, cotangent, gains, w_qkv, w_out, segments, plan):
    sections = lax.axis_size("section")
    groups = lax.axis_size("group")
    devices = lax.axis_size("dp")
    plane = devices * groups
    section = lax.axis_index("section")
    member = lax.axis_index("group")
    rows_dev = plan.shape[1]
    length = segments.shape[1]
    tokens, width = tokens_in.shape
    head = w_out.shape[1]
    share = rows_dev // groups
    w_layer, out_layer = w_qkv[0], w_out[0]
    place = member.astype(jnp.int32)[None]
    layer = section.astype(jnp.int32)[None]

    slice_rows = head // plane
    mine = lax.axis_index("dp") * groups + member
    own_rows, *parts = pick(
        tokens_in.reshape(rows_dev, length, width),
        plan,
        place,
        groups,
        out_layer,
        mine.astype(jnp.int32)[None],
        slice_rows,
    )
    slices = [raised(own_rows, r) for r in range(sections - 1, 0, -1)]
    slices = [own_rows] + slices[::-1]
    chosen = jnp.take(segments, plan[0], axis=0, mode="clip").astype(BF16)
    chosen = chosen.reshape(groups, share, length)
    moved, moved_seg = [], []
    for r in range(groups):
        outgoing = lax.dynamic_index_in_dim(chosen, (member + r) % groups, 0, keepdims=False)
        moved.append(handed(parts[r], r) if r else parts[r])
        moved_seg.append(handed(outgoing, r) if r else outgoing)
    moved = [part.reshape(share * length, width) for part in moved]
    order = (member - jnp.arange(groups)) % groups
    seg = jnp.take(jnp.stack(moved_seg), order, axis=0, mode="clip").reshape(tokens)
    at = jnp.arange(tokens)
    mask = (
        (at[:, None] >= at[None, :])
        & (at[:, None] // length == at[None, :] // length)
        & (seg[:, None] == seg[None, :])
    ).astype(F32)

    last = (section == sections - 1).astype(jnp.int32)[None]
    bits = devices.bit_length() - 1
    places = plane_places()
    x, xz, norms = project(
        moved, cotangent, gains, w_layer, out_layer, place, []
    )
    coupling, stack = couple(slices, gains, w_layer, out_layer, last, [mask, places, xz])
    others = [shifted(coupling, r) for r in range(1, sections)]

    streams = stream_columns(width // CHUNKS)

    def facing(array, by):
        return lax.ppermute(array, "section", [(i, i ^ by) for i in range(sections)])

    arrays, masks, by = [hold(xz, others)], [0], sections // 2
    while by > 0:
        arrays = arrays + [facing(array, by) for array in arrays]
        masks = masks + [mask_of ^ by for mask_of in masks]
        by = by // 2
    xz_all = [arrays[masks.index(r)] for r in range(sections)]
    early = [xz_all[r] for r in range(1, sections) if r & (r - 1) == 0]
    late = [xz_all[r] for r in range(1, sections) if r & (r - 1) != 0]
    pieces = [compact([coupling] + others, layer, 3 * head, head, [xz])]

    rows = [stack[None]]
    for step in range(bits):
        if step > 0:
            pieces = [merge(*pieces, early)]
        pieces = pieces + [swapped(pieces[0], step)]
        if step == bits - 1:
            pieces[-1] = hold(pieces[-1], late)
        if step > 0:
            rows = [gather_two(*rows, pieces[-1:])]
        rows = rows + [swapped(rows[0], step)]
    pieces = pieces + [handed(array, r) for r in range(1, groups) for array in pieces]
    sent, total, mixes, *leaving = serial(
        xz_all, pieces, places, norms, mask, layer, gains, w_layer, out_layer, streams
    )
    back, pair = widen(sent, gains, w_layer, out_layer, width // CHUNKS)

    down = [(i, i - 1) for i in range(1, sections)]
    behind = sections - 1 - section

    def index(tick):
        return jnp.clip(tick - behind, 0, CHUNKS - 1).astype(jnp.int32)[None]

    def lowered(arrays):
        return [lax.ppermute(array, "section", down) for array in arrays]

    ticks = CHUNKS + sections - 1
    after = {}
    for tick in range(1, ticks):
        arrived = lowered(leaving)
        if tick < ticks - 1:
            for i, cols in enumerate(streams):
                leaving[i], pair = join(
                    index(tick), arrived[i], pair, cols, after.get(tick, [])
                )
        if tick == 1:
            rows = [hold(array, leaving) for array in rows]
            rows = rows + [handed(array, r) for r in range(1, groups) for array in rows]
            rests, halves = [], []
            for part in range(PARTS):
                rest, half = settle(
                    total, mixes, rows, places, x, cotangent, back, width // CHUNKS, part, PARTS
                )
                rests.append(rest)
                halves.append(half)
            sums = [stacked(halves)]
            for step in range(bits):
                sums.append(added([sums[-1], swapped(sums[-1], step)]))
            sums.append(added(sums[-1:] + [handed(sums[-1], r) for r in range(1, groups)]))
            gain_whole = sums[-1].reshape(1, width)
            after = {2 + i: [array] for i, array in enumerate(sums)}
    out = finish(index(ticks - 1), arrived, pair, rests, streams)
    return (out[None], gain_whole)


def attend(hidden, segment, gain_row, w_layer, out_layer):
    count, length, width = hidden.shape
    head = out_layer.shape[0]
    scaled = hidden * lax.rsqrt(jnp.mean(hidden * hidden, axis=-1, keepdims=True) + EPS) * gain_row
    normed = scaled.astype(BF16).reshape(count * length, width)
    projected = jnp.dot(normed, w_layer, preferred_element_type=F32).reshape(count, length, 3 * head)
    query = projected[:, :, :head]
    keyed = projected[:, :, head : 2 * head]
    valued = projected[:, :, 2 * head :]
    positions = jnp.arange(length)
    allowed = (positions[:, None] >= positions[None, :])[None] & (
        segment[:, :, None] == segment[:, None, :]
    )
    scores = jnp.einsum("rid,rjd->rij", query, keyed, precision=lax.Precision.HIGHEST)
    scores = jnp.where(allowed, scores / math.sqrt(head), -1e30)
    weights = jax.nn.softmax(scores, axis=-1)
    mixed = jnp.einsum("rij,rjd->rid", weights, valued, precision=lax.Precision.HIGHEST)
    mixed = mixed.astype(BF16).reshape(count * length, head)
    output = jnp.dot(mixed, out_layer, preferred_element_type=F32).reshape(count, length, width)
    return hidden + output


MB_ROWS = 2


def relay(tokens_in, cotangent, gains, w_qkv, w_out, segments, plan):
    sections = lax.axis_size("section")
    section = lax.axis_index("section")
    rows_dev = plan.shape[1]
    width = tokens_in.shape[1]
    length = segments.shape[1]
    micro = rows_dev // MB_ROWS
    blocks = tokens_in.reshape(rows_dev, length, width)
    chosen = jnp.take(blocks, plan[0], axis=0)
    chosen_seg = jnp.take(segments, plan[0], axis=0).astype(BF16)
    assigned = lax.all_to_all(chosen, "group", split_axis=0, concat_axis=0, tiled=True)
    moved_seg = lax.all_to_all(chosen_seg, "group", split_axis=0, concat_axis=0, tiled=True)
    assigned = assigned.reshape(micro, MB_ROWS, length, width)
    seg_groups = moved_seg.reshape(micro, MB_ROWS, length)
    gain_row, w_layer, out_layer = gains[0], w_qkv[0], w_out[0]
    grad_rows = cotangent.reshape(micro, MB_ROWS, length, width)
    ticks = micro + sections - 1

    def passed_along(array, by):
        pairs = [(i, i + by) for i in range(sections) if 0 <= i + by < sections]
        return lax.ppermute(array, "section", pairs)

    def at(array, i):
        return lax.dynamic_index_in_dim(array, i, 0, keepdims=False)

    def forward_tick(tick, carry):
        saved, arrived = carry
        index = tick - section
        valid = (index >= 0) & (index < micro)
        clipped = jnp.clip(index, 0, micro - 1)
        entering = jnp.where(section == 0, at(assigned, clipped), arrived)
        kept = jnp.where(valid, entering, at(saved, clipped))
        saved = lax.dynamic_update_index_in_dim(saved, kept, clipped, 0)
        segment = at(seg_groups, clipped)

        def run_layer(value):
            return attend(value.astype(F32), segment, gain_row, w_layer, out_layer).astype(BF16)

        leaving = lax.cond(valid, run_layer, jnp.zeros_like, entering)
        return (saved, passed_along(leaving, 1))

    saved_init = jnp.zeros((micro, MB_ROWS, length, width), BF16)
    arrive_init = jnp.zeros((MB_ROWS, length, width), BF16)
    saved, _ = lax.fori_loop(0, ticks, forward_tick, (saved_init, arrive_init))

    def backward_tick(tick, carry):
        grads_x, gain_total, arrived = carry
        index = tick - (sections - 1 - section)
        valid = (index >= 0) & (index < micro)
        clipped = jnp.clip(index, 0, micro - 1)
        entering = jnp.where(section == sections - 1, at(grad_rows, clipped), arrived)
        segment = at(seg_groups, clipped)
        stored = at(saved, clipped).astype(F32)

        def local_layer(hidden, gains_here):
            return attend(hidden, segment, gains_here, w_layer, out_layer)

        def run_back(value):
            _, pullback = jax.vjp(local_layer, stored, gain_row)
            grad_hidden, grad_gain = pullback(value.astype(F32))
            return (grad_hidden.astype(BF16), grad_gain)

        def skip_back(value):
            return (jnp.zeros_like(value), jnp.zeros(gain_row.shape, F32))

        sending, grad_gain = lax.cond(valid, run_back, skip_back, entering)
        kept = jnp.where(valid, sending, at(grads_x, clipped))
        grads_x = lax.dynamic_update_index_in_dim(grads_x, kept, clipped, 0)
        return (grads_x, gain_total + grad_gain, passed_along(sending, -1))

    gain_init = jnp.zeros(gain_row.shape, F32)
    grads_x, gain_total, _ = lax.fori_loop(
        0, ticks, backward_tick, (saved_init, gain_init, arrive_init)
    )
    gain_whole = lax.psum(gain_total, ("dp", "group"))
    return (grads_x.reshape(1, rows_dev * length, width), gain_whole[None])


def solution(mesh):
    placed = (
        P(("dp", "group"), None),
        P(("dp", "group"), None),
        P("section", None),
        P("section", None, None),
        P("section", None, None),
        P(("dp", "group"), None),
        P(("dp", "group"), None),
    )

    def chosen(tokens_in, cotangent, gains, w_qkv, w_out, segments, plan):
        sections, head, width = w_out.shape
        devices = mesh.shape["dp"]
        small = sections * 4 * head < width and sections > 1
        halves = devices & (devices - 1) == 0 and sections & (sections - 1) == 0
        body = local if small and halves else relay
        return jax.shard_map(
            body,
            mesh=mesh,
            in_specs=placed,
            out_specs=(P("section", ("dp", "group"), None), P("section", None)),
            check_vma=False,
        )(tokens_in, cotangent, gains, w_qkv, w_out, segments, plan)

    return chosen
```

```python
import math

import jax
import jax.numpy as jnp
from jax import lax
from jax.experimental import pallas as pl
from jax.experimental.pallas import tpu as pltpu
from jax.sharding import PartitionSpec as P

EPS = 1e-05
VMEM_BYTES = 24 * 1024 * 1024
SMALL = 16 * 1024 * 1024
F32 = jnp.float32
BF16 = jnp.bfloat16


def dot_nn(a, b):
    return lax.dot_general(a, b, (((1,), (0,)), ((), ())), preferred_element_type=F32)


def dot_nt(a, b):
    return lax.dot_general(a, b, (((1,), (1,)), ((), ())), preferred_element_type=F32)


def dot_tn(a, b):
    return lax.dot_general(a, b, (((0,), (0,)), ((), ())), preferred_element_type=F32)


IN_HBM = pl.BlockSpec(memory_space=pltpu.HBM)
ANYWHERE = pl.BlockSpec(memory_space=pl.ANY)
IN_VMEM = pl.BlockSpec(memory_space=pltpu.VMEM)
IN_SMEM = pl.BlockSpec(memory_space=pltpu.SMEM)


def in_hbm(array):
    return pltpu.with_memory_space_constraint(array, pltpu.HBM)


def in_vmem(array):
    return pltpu.with_memory_space_constraint(array, pltpu.VMEM)


def mover(sems):
    used = []

    def start(source, target):
        copy = pltpu.make_async_copy(source, target, sems.at[len(used)])
        copy.start()
        used.append(copy)
        return copy

    return start


def steps(width):
    step = min(width, 1024)
    return [slice(at, at + step) for at in range(0, width, step)]


def params(limit=VMEM_BYTES):
    return pltpu.CompilerParams(vmem_limit_bytes=limit)


def cut(out_layer, mine, rows):
    width = out_layer.shape[1]

    def kernel(mine_ref, o_ref, slice_ref, sem):
        at = pl.ds(pl.multiple_of(mine_ref[0] * rows, rows), rows)
        copy = pltpu.make_async_copy(o_ref.at[at], slice_ref, sem)
        copy.start()
        copy.wait()

    return pl.pallas_call(
        kernel,
        out_shape=jax.ShapeDtypeStruct((rows, width), BF16),
        in_specs=[IN_SMEM, IN_HBM],
        out_specs=IN_VMEM,
        scratch_shapes=[pltpu.SemaphoreType.DMA(())],
        compiler_params=params(SMALL),
        name="cut",
    )(mine, in_hbm(out_layer))


def pick(tokens, plan, place, groups, after):
    rows, length, width = tokens.shape
    share = rows // groups

    def kernel(plan_ref, place_ref, tokens_ref, *rest):
        parts = rest[len(after) : len(after) + groups]
        rows_in, sems = rest[len(after) + groups :]
        start = mover(sems)
        loads = []
        for r in range(groups):
            target = lax.rem(place_ref[0] + r, groups)
            for c in range(share):
                here = rows_in.at[r * share + c]
                row = plan_ref[0, target * share + c]
                loads.append((start(tokens_ref.at[row], here), here, parts[r].at[c]))
        stores = []
        for load, here, there in loads:
            load.wait()
            stores.append(start(here, there))
        for store in stores:
            store.wait()

    return pl.pallas_call(
        kernel,
        out_shape=[pltpu.HBM((share, length, width), BF16)] * groups,
        in_specs=[IN_SMEM, IN_SMEM, IN_HBM] + [ANYWHERE] * len(after),
        out_specs=[IN_HBM] * groups,
        scratch_shapes=[
            pltpu.VMEM((rows, length, width), BF16),
            pltpu.SemaphoreType.DMA((2 * rows,)),
        ],
        compiler_params=params(),
        name="pick",
    )(plan, place, in_hbm(tokens), *after)


def project(parts, cotangent, gain, w_layer, out_layer, place, after):
    groups = len(parts)
    tokens, width = cotangent.shape
    head = out_layer.shape[0]
    wide = w_layer.shape[1]
    block = tokens // groups
    cuts = steps(width)
    copies = len(cuts) * (groups + 4)

    def kernel(place_ref, *refs):
        part_refs = refs[:groups]
        cot_ref, g_ref, w_ref, o_ref = refs[groups : groups + 4]
        x_ref, xz_ref, n_ref = refs[groups + 4 + len(after) : groups + 7 + len(after)]
        x_in, c_in, w_in, o_in, sems = refs[groups + 7 + len(after) :]
        start = mover(sems)
        loads = []
        for cut in cuts:
            mine = [start(w_ref.at[cut], w_in.at[cut])]
            mine.append(start(o_ref.at[:, cut], o_in.at[:, cut]))
            for r in range(groups):
                source = lax.rem(place_ref[0] + groups - r, groups)
                rows = pl.ds(pl.multiple_of(source * block, block), block)
                mine.append(start(part_refs[r].at[:, cut], x_in.at[rows, cut]))
            mine.append(start(cot_ref.at[:, cut], c_in.at[:, cut]))
            loads.append(mine)
        through = jnp.zeros((tokens, wide), F32)
        across = jnp.zeros((tokens, head), F32)
        back = jnp.zeros((tokens, head), F32)
        square = jnp.zeros((tokens, 1), F32)
        stores = []
        for cut, mine in zip(cuts, loads):
            for load in mine:
                load.wait()
            stores.append(start(x_in.at[:, cut], x_ref.at[:, cut]))
            x = x_in[:, cut]
            xf = x.astype(F32)
            through += dot_nn((xf * g_ref[:, cut]).astype(BF16), w_in[cut, :])
            across += dot_nt(x, o_in[:, cut])
            back += dot_nt(c_in[:, cut], o_in[:, cut])
            square += jnp.sum(xf * xf, axis=1, keepdims=True)
        xz_ref[:, :wide] = through.astype(BF16)
        xz_ref[:, wide : wide + head] = across.astype(BF16)
        xz_ref[:, wide + head :] = back.astype(BF16)
        n_ref[...] = square
        for store in stores:
            store.wait()

    return pl.pallas_call(
        kernel,
        out_shape=[
            pltpu.HBM((tokens, width), BF16),
            jax.ShapeDtypeStruct((tokens, wide + 2 * head), BF16),
            jax.ShapeDtypeStruct((tokens, 1), F32),
        ],
        in_specs=[IN_SMEM]
        + [ANYWHERE] * groups
        + [IN_HBM, IN_VMEM, IN_HBM, IN_HBM]
        + [ANYWHERE] * len(after),
        out_specs=[IN_HBM, IN_VMEM, IN_VMEM],
        scratch_shapes=[
            pltpu.VMEM((tokens, width), BF16),
            pltpu.VMEM((tokens, width), BF16),
            pltpu.VMEM((width, wide), BF16),
            pltpu.VMEM((head, width), BF16),
            pltpu.SemaphoreType.DMA((copies,)),
        ],
        compiler_params=params(),
        name="project",
    )(
        place,
        *parts,
        in_hbm(cotangent),
        gain,
        in_hbm(w_layer),
        in_hbm(out_layer),
        *after,
    )


def couple(slices, gain, w_layer, out_layer, last, after):
    sections = len(slices)
    count, width = slices[0].shape
    head = out_layer.shape[0]
    wide = w_layer.shape[1]
    below = (sections - 2) * wide
    packed = below + max(wide, (sections - 1) * head)
    cuts = steps(width)
    copies = len(cuts) * (sections + 2) + sections - 1

    def kernel(last_ref, *refs):
        s_refs = refs[:sections][::-1]
        g_ref, w_ref, o_ref = refs[sections : sections + 3]
        out_ref, stack_ref, r_in, w_in, o_in, sems = refs[sections + 3 + len(after) :]
        rows = [slice(r * count, (r + 1) * count) for r in range(sections)]
        start = mover(sems)
        loads = []
        for cut in cuts:
            mine = [start(w_ref.at[cut], w_in.at[cut])]
            mine.append(start(o_ref.at[:, cut], o_in.at[:, cut]))
            for r in range(sections):
                mine.append(start(s_refs[r].at[:, cut], r_in.at[rows[r], cut]))
            loads.append(mine)
        through = jnp.zeros((sections * count, wide), F32)
        across = jnp.zeros((sections * count, head), F32)
        for cut, mine in zip(cuts, loads):
            for load in mine:
                load.wait()
            r = r_in[:, cut]
            through += dot_nn((r.astype(F32) * g_ref[:, cut]).astype(BF16), w_in[cut, :])
            across += dot_nt(r, o_in[:, cut])
        stores = [start(r_in.at[rows[r]], stack_ref.at[r - 1]) for r in range(1, sections)]
        through = through.astype(BF16)
        across = across.astype(BF16)
        out_ref[...] = jnp.zeros_like(out_ref)
        for r in range(1, sections - 1):
            out_ref[:, (r - 1) * wide : r * wide] = through[rows[r]]

        @pl.when(last_ref[0] == 1)
        def _():
            out_ref[:, below : below + wide] = through[rows[-1]]

        @pl.when(last_ref[0] == 0)
        def _():
            for r in range(sections - 1):
                out_ref[:, below + r * head : below + (r + 1) * head] = across[rows[r]]

        for store in stores:
            store.wait()

    return pl.pallas_call(
        kernel,
        out_shape=[
            jax.ShapeDtypeStruct((count, packed), BF16),
            pltpu.HBM((sections - 1, count, width), BF16),
        ],
        in_specs=[IN_SMEM]
        + [ANYWHERE] * sections
        + [IN_VMEM, IN_HBM, IN_HBM]
        + [ANYWHERE] * len(after),
        out_specs=[IN_VMEM, IN_HBM],
        scratch_shapes=[
            pltpu.VMEM((sections * count, width), BF16),
            pltpu.VMEM((width, wide), BF16),
            pltpu.VMEM((head, width), BF16),
            pltpu.SemaphoreType.DMA((copies,)),
        ],
        compiler_params=params(),
        name="couple",
    )(last, *slices[::-1], gain, in_hbm(w_layer), in_hbm(out_layer), *after)


def layout(sections, wide, head):
    through, across, at = {}, {}, 0
    for k in range(sections):
        for j in range(k):
            through[j, k] = slice(at, at + wide)
            at += wide
        for j in range(k + 1 if k < sections - 1 else 0):
            across[j, k] = slice(at, at + head)
            at += head
    return through, across, at


def compact(parts, section, wide, head, after):
    sections = len(parts)
    count = parts[0].shape[0]
    below = (sections - 2) * wide
    through, across, total = layout(sections, wide, head)

    def kernel(s_ref, *refs):
        part_refs, out_ref = refs[:sections], refs[-1]
        mine = s_ref[0]

        def fill(k, r):
            for j in range(k):
                at = (k - j - 1) * wide
                out_ref[0, :, through[j, k]] = part_refs[r][:, at : at + wide]
            for j in range(k + 1 if k < sections - 1 else 0):
                at = below + (k - j) * head
                out_ref[0, :, across[j, k]] = part_refs[r][:, at : at + head]

        for s in range(sections):

            @pl.when(mine == s)
            def _(s=s):
                for r in range(sections):
                    fill((s - r) % sections, r)

    vmem = pl.BlockSpec(memory_space=pltpu.VMEM)
    return pl.pallas_call(
        kernel,
        out_shape=jax.ShapeDtypeStruct((1, count, total), BF16),
        in_specs=[IN_SMEM] + [vmem] * sections + [ANYWHERE] * len(after),
        out_specs=vmem,
        compiler_params=params(SMALL),
        name="compact",
    )(section, *parts, *after)


def merge(first, second, after):
    count = first.shape[0]

    def kernel(first_ref, second_ref, *refs):
        refs[-1][:count] = first_ref[...]
        refs[-1][count:] = second_ref[...]

    return pl.pallas_call(
        kernel,
        out_shape=jax.ShapeDtypeStruct((2 * count,) + first.shape[1:], first.dtype),
        in_specs=[IN_VMEM] * 2 + [ANYWHERE] * len(after),
        out_specs=IN_VMEM,
        compiler_params=params(SMALL),
        name="merge",
    )(first, second, *after)


def serial(xz, pieces, places, norms, mask, section, gain, w_layer, out_layer, streams):
    sections = len(xz)
    tokens = norms.shape[0]
    head, width = out_layer.shape
    wide = 3 * head
    scale = 1.0 / math.sqrt(head)
    lead = slice(0, streams[-1].stop)
    through_at, across_at, _ = layout(sections, wide, head)
    count, packed = pieces[0].shape[-2:]
    plane = head // count
    n_in = sections + len(pieces)
    copies = sections + plane + 2

    def kernel(s_ref, p_ref, *refs):
        xz_refs, piece_refs = refs[:sections], refs[sections:n_in]
        n_ref, mask_ref, g_ref, w_ref, o_ref = refs[n_in : n_in + 5]
        n_out = n_in + 5
        v_ref, t_ref, a_ref = refs[n_out : n_out + 3]
        first_refs = refs[n_out + 3 : n_out + 3 + len(streams)]
        scratch = refs[n_out + 3 + len(streams) :]
        xz_all, table, mixes, weights, projs, dmix, w_in, o_in, sems = scratch
        mine = s_ref[0]
        started = []

        def start(source, target):
            copy = pltpu.make_async_copy(source, target, sems.at[len(started)])
            copy.start()
            started.append(copy)

        for r in range(sections):
            start(xz_refs[r], xz_all.at[mine ^ r])
        at = 0
        for ref in piece_refs:
            for i in range(ref.shape[0]):
                start(ref.at[i], table.at[p_ref[at]])
                at += 1
        small = list(started)
        start(w_ref.at[lead], w_in)
        start(o_ref.at[:, lead], o_in)
        for copy in small:
            copy.wait()

        def through(j, k):
            return table[:, :, through_at[j, k]].reshape(head, wide)

        def across(j, k):
            return table[:, :, across_at[j, k]].reshape(head, head)

        allowed = mask_ref[...] > 0.5
        norm = n_ref[...]
        rstds, tails, mixed = [], [], []
        for s in range(sections):
            proj = xz_all[s, :, :wide].astype(F32)
            for j in range(s):
                proj = proj + dot_nn(mixed[j], through(j, s))
            rstd = lax.rsqrt(norm * (1.0 / width) + EPS)
            proj = proj * rstd
            projs[s] = proj.astype(BF16)
            q, k, v = (projs[s, :, i * head : (i + 1) * head] for i in range(3))
            scores = jnp.where(allowed, dot_nt(q, k) * scale, -1e30)
            scores = jnp.exp(scores - jnp.max(scores, axis=1, keepdims=True))
            soft = scores / jnp.sum(scores, axis=1, keepdims=True)
            weights[s] = soft
            mix = dot_nn(soft.astype(BF16), v).astype(BF16)
            mixed.append(mix)
            mixes[:, s * head : (s + 1) * head] = mix
            rstds.append(rstd)
            dmix[:, s * head : (s + 1) * head] = xz_all[s, :, wide + head :].astype(F32)
            if s == sections - 1:
                break
            y = xz_all[s, :, wide : wide + head].astype(F32)
            for j in range(s):
                y = y + dot_nn(mixed[j], across(j, s))
            tail = y + dot_nn(mix, across(s, s))
            norm = norm + jnp.sum(mix.astype(F32) * (y + tail), axis=1, keepdims=True)
            norm = jnp.maximum(norm, 0.0)
            tails.append(tail)
        total = jnp.zeros((tokens, 1), F32)
        a_ref[...] = jnp.zeros_like(a_ref)
        for s in reversed(range(sections)):
            cols = slice(s * head, (s + 1) * head)
            da = dmix[:, cols]
            if s < sections - 1:
                da = da - total * tails[s]
            da = da.astype(BF16)
            q, k, v = (projs[s, :, i * head : (i + 1) * head] for i in range(3))
            soft = weights[s]
            dv = dot_tn(soft.astype(BF16), da)
            dsoft = dot_nt(da, v)
            dscore = soft * (dsoft - jnp.sum(dsoft * soft, axis=1, keepdims=True))
            dscore = (dscore * scale).astype(BF16)
            dproj = jnp.concatenate([dot_nn(dscore, k), dot_tn(dscore, q), dv], axis=1)
            along = jnp.sum(dproj * projs[s].astype(F32), axis=1, keepdims=True)
            first = (dproj * rstds[s]).astype(BF16)
            second = (-total * mixes[:, cols].astype(F32)).astype(BF16)
            total = total + rstds[s] * rstds[s] * along * (1.0 / width)
            for j in reversed(range(s)):
                term = dot_nt(first, through(j, s))
                if s < sections - 1:
                    term = term + dot_nt(second, across(j, s))
                dmix[:, j * head : (j + 1) * head] += term

            @pl.when(mine == s)
            def _(first=first, second=second, total=total):
                v_ref[:, :wide] = first
                v_ref[:, wide:] = second
                t_ref[...] = total

            for r in range(1, sections - s):

                @pl.when(mine == s + r)
                def _(r=r, cols=cols):
                    a_ref[:, (r - 1) * head : r * head] = mixes[:, cols]

        for copy in started[len(small) :]:
            copy.wait()
        own = dot_nt(v_ref[:, :wide], w_in[...]) * g_ref[:, lead]
        own = (own + dot_nn(v_ref[:, wide:], o_in[...])).astype(BF16)
        for ref, part in zip(first_refs, streams):
            ref[...] = own[:, part]

    vmem = pl.BlockSpec(memory_space=pltpu.VMEM)
    smem = pl.BlockSpec(memory_space=pltpu.SMEM)
    return pl.pallas_call(
        kernel,
        out_shape=[
            pltpu.VMEM((tokens, wide + head), BF16),
            pltpu.VMEM((tokens, 1), F32),
            pltpu.VMEM((tokens, (sections - 1) * head), BF16),
        ]
        + [pltpu.VMEM((tokens, part.stop - part.start), BF16) for part in streams],
        in_specs=[smem, smem] + [ANYWHERE] * n_in + [vmem, vmem, vmem, IN_HBM, IN_HBM],
        out_specs=[vmem] * (3 + len(streams)),
        scratch_shapes=[
            pltpu.VMEM((sections,) + xz[0].shape, BF16),
            pltpu.VMEM((plane, count, packed), BF16),
            pltpu.VMEM((tokens, sections * head), BF16),
            pltpu.VMEM((sections, tokens, tokens), F32),
            pltpu.VMEM((sections, tokens, wide), BF16),
            pltpu.VMEM((tokens, sections * head), F32),
            pltpu.VMEM((lead.stop, wide), BF16),
            pltpu.VMEM((head, lead.stop), BF16),
            pltpu.SemaphoreType.DMA((copies,)),
        ],
        compiler_params=params(),
        name="serial",
    )(
        section,
        places,
        *xz,
        *pieces,
        norms,
        mask,
        gain,
        in_hbm(w_layer),
        in_hbm(out_layer),
    )


def hold(array, after):
    def kernel(*refs):
        pass

    return pl.pallas_call(
        kernel,
        out_shape=jax.ShapeDtypeStruct(array.shape, array.dtype),
        in_specs=[ANYWHERE] * (1 + len(after)),
        out_specs=ANYWHERE,
        input_output_aliases={0: 0},
        compiler_params=params(SMALL),
        name="hold",
    )(array, *after)


def gather_two(first, second, after):
    count = first.shape[0]

    def kernel(first_ref, second_ref, *refs):
        out_ref, sems = refs[len(after) :]
        start = mover(sems)
        copies = [start(first_ref, out_ref.at[:count]), start(second_ref, out_ref.at[count:])]
        for copy in copies:
            copy.wait()

    return pl.pallas_call(
        kernel,
        out_shape=jax.ShapeDtypeStruct((2 * count,) + first.shape[1:], first.dtype),
        in_specs=[ANYWHERE] * (2 + len(after)),
        out_specs=IN_VMEM,
        scratch_shapes=[pltpu.SemaphoreType.DMA((2,))],
        compiler_params=params(SMALL),
        name="gather_two",
    )(first, second, *after)


def widen(sent, gain, w_layer, out_layer, chunk):
    tokens = sent.shape[0]
    head, width = out_layer.shape
    wide = w_layer.shape[1]
    cuts = [slice(at, at + chunk) for at in range(0, width, chunk)]

    def kernel(v_ref, g_ref, w_ref, o_ref, back_ref, pair_ref, back_in, w_in, o_in, sems):
        start = mover(sems)
        loads = [
            (start(w_ref.at[cut], w_in.at[cut]), start(o_ref.at[:, cut], o_in.at[:, cut]))
            for cut in cuts
        ]
        stores = []
        for i, (cut, mine) in enumerate(zip(cuts, loads)):
            for load in mine:
                load.wait()
            back = dot_nt(v_ref[:, :wide], w_in[cut, :])
            own = back * g_ref[:, cut] + dot_nn(v_ref[:, wide:], o_in[:, cut])
            back_in[:, cut] = back.astype(BF16)
            stores.append(start(back_in.at[:, cut], back_ref.at[:, cut]))
            pair_ref[0, i] = own.astype(BF16)
            pair_ref[1, i] = jnp.zeros_like(pair_ref[1, i])
        for store in stores:
            store.wait()

    return pl.pallas_call(
        kernel,
        out_shape=[
            pltpu.HBM((tokens, width), BF16),
            pltpu.VMEM((2, len(cuts), tokens, chunk), BF16),
        ],
        in_specs=[IN_VMEM, IN_VMEM, IN_HBM, IN_HBM],
        out_specs=[IN_HBM, IN_VMEM],
        scratch_shapes=[
            pltpu.VMEM((tokens, width), BF16),
            pltpu.VMEM((width, wide), BF16),
            pltpu.VMEM((head, width), BF16),
            pltpu.SemaphoreType.DMA((3 * len(cuts),)),
        ],
        compiler_params=params(),
        name="widen",
    )(in_vmem(sent), gain, in_hbm(w_layer), in_hbm(out_layer))


def settle(total, mixes, stacks, places, x, cotangent, back, chunk, part, parts):
    tokens, width = x.shape
    layers, rows = stacks[0].shape[1:3]
    entries = [(i, e) for i, stack in enumerate(stacks) for e in range(stack.shape[0])]
    plane = len(entries)
    head = plane * rows
    span = width // parts
    base = part * span
    cuts = [slice(at, at + chunk) for at in range(0, span, chunk)]
    copies = plane * layers + 3 * len(cuts)

    def kernel(p_ref, t_ref, a_ref, x_ref, c_ref, back_ref, *refs):
        stack_refs = refs[: len(stacks)]
        rest_ref, dg_ref = refs[len(stacks) : len(stacks) + 2]
        lower, x_in, c_in, back_in, sems = refs[len(stacks) + 2 :]
        start = mover(sems)
        first = []
        for at, (i, e) in enumerate(entries):
            for r in range(layers):
                here = pl.ds(base, span)
                first.append(start(stack_refs[i].at[e, r, :, here], lower.at[r, p_ref[at]]))
        loads = []
        for cut in cuts:
            there = pl.ds(base + cut.start, chunk)
            mine = [start(x_ref.at[:, there], x_in.at[:, cut])]
            mine.append(start(c_ref.at[:, there], c_in.at[:, cut]))
            mine.append(start(back_ref.at[:, there], back_in.at[:, cut]))
            loads.append(mine)
        for load in first:
            load.wait()
        for i, (cut, mine) in enumerate(zip(cuts, loads)):
            for load in mine:
                load.wait()
            below = lower[:, :, :, cut].reshape(layers * head, chunk)
            here = x_in[:, cut].astype(F32) + dot_nn(a_ref[...], below)
            rest_ref[i] = (c_in[:, cut].astype(F32) - t_ref[...] * here).astype(BF16)
            gain = jnp.sum(back_in[:, cut].astype(F32) * here, axis=0, keepdims=True)
            for at in range(0, chunk, head):
                row = (cut.start + at) // head
                dg_ref[row : row + 1, :] = gain[:, at : at + head]

    return pl.pallas_call(
        kernel,
        out_shape=[
            pltpu.VMEM((len(cuts), tokens, chunk), BF16),
            pltpu.VMEM((span // head, head), F32),
        ],
        in_specs=[IN_SMEM] + [IN_VMEM] * 2 + [IN_HBM] * (3 + len(stacks)),
        out_specs=[IN_VMEM] * 2,
        scratch_shapes=[
            pltpu.VMEM((layers, plane, rows, span), BF16),
            pltpu.VMEM((tokens, span), BF16),
            pltpu.VMEM((tokens, span), BF16),
            pltpu.VMEM((tokens, span), BF16),
            pltpu.SemaphoreType.DMA((copies,)),
        ],
        compiler_params=params(),
        name="settle",
    )(
        places,
        in_vmem(total),
        in_vmem(mixes),
        *[in_hbm(array) for array in (x, cotangent, back, *stacks)],
    )


def join(index, arrived, pair, cols, after):
    tokens, part = arrived.shape

    def kernel(i_ref, r_ref, _, *refs):
        send_ref, pair_ref = refs[len(after) :]
        at = i_ref[0]
        r = r_ref[...]
        send_ref[...] = (pair_ref[0, at, :, cols].astype(F32) + r.astype(F32)).astype(BF16)
        pair_ref[1, at, :, cols] = r

    return pl.pallas_call(
        kernel,
        out_shape=[pltpu.VMEM((tokens, part), BF16), pltpu.VMEM(pair.shape, BF16)],
        in_specs=[IN_SMEM] + [IN_VMEM] * 2 + [ANYWHERE] * len(after),
        out_specs=[IN_VMEM] * 2,
        input_output_aliases={2: 1},
        compiler_params=params(SMALL),
        name="join",
    )(index, in_vmem(arrived), in_vmem(pair), *after)


def finish(index, arrived, pair, rests, streams):
    _, count, tokens, chunk = pair.shape

    def kernel(i_ref, *refs):
        r_refs = refs[: len(streams)]
        pair_ref, rest_refs = refs[len(streams)], refs[len(streams) + 1 :][: len(rests)]
        whole_ref, whole, sems = refs[len(streams) + 1 + len(rests) :]
        each = count // len(rests)
        at = i_ref[0]
        copies = []
        for i in range(count):
            full = rest_refs[i // each][i % each].astype(F32) + pair_ref[0, i].astype(F32)
            whole[i] = (full + pair_ref[1, i].astype(F32)).astype(BF16)

            @pl.when(at == i)
            def _(i=i, full=full):
                for ref, cols in zip(r_refs, streams):
                    whole[i, :, cols] = (full[:, cols] + ref[...].astype(F32)).astype(BF16)

            there = whole_ref.at[:, pl.ds(i * chunk, chunk)]
            copies.append(pltpu.make_async_copy(whole.at[i], there, sems.at[i]))
            copies[-1].start()
        for copy in copies:
            copy.wait()

    return pl.pallas_call(
        kernel,
        out_shape=pltpu.HBM((tokens, count * chunk), BF16),
        in_specs=[IN_SMEM] + [IN_VMEM] * (len(streams) + 1 + len(rests)),
        out_specs=IN_HBM,
        scratch_shapes=[
            pltpu.VMEM((count, tokens, chunk), BF16),
            pltpu.SemaphoreType.DMA((count,)),
        ],
        compiler_params=params(SMALL),
        name="finish",
    )(index, *[in_vmem(array) for array in (*arrived, pair, *rests)])


def stacked(arrays):
    rows = arrays[0].shape[0]

    def kernel(*refs):
        for i, ref in enumerate(refs[:-1]):
            refs[-1][i * rows : (i + 1) * rows, :] = ref[...]

    return pl.pallas_call(
        kernel,
        out_shape=pltpu.VMEM((len(arrays) * rows, arrays[0].shape[1]), F32),
        in_specs=[IN_VMEM] * len(arrays),
        out_specs=IN_VMEM,
        compiler_params=params(SMALL),
        name="stacked",
    )(*[in_vmem(array) for array in arrays])


def added(arrays):
    def kernel(*refs):
        total = refs[0][...]
        for ref in refs[1:-1]:
            total = total + ref[...]
        refs[-1][...] = total

    return pl.pallas_call(
        kernel,
        out_shape=pltpu.VMEM(arrays[0].shape, F32),
        in_specs=[IN_VMEM] * len(arrays),
        out_specs=IN_VMEM,
        compiler_params=params(SMALL),
        name="added",
    )(*[in_vmem(array) for array in arrays])


STREAMS = 2
CHUNKS = 4
PARTS = 1


def stream_columns(chunk):
    lanes = 128
    tiles = chunk // lanes
    ends = [-(-tiles * (i + 1) // STREAMS) * lanes for i in range(STREAMS)]
    return [slice(start, end) for start, end in zip([0] + ends, ends)]


def shifted(array, by):
    sections = lax.axis_size("section")
    return lax.ppermute(array, "section", [(i, (i + by) % sections) for i in range(sections)])


def raised(array, by):
    sections = lax.axis_size("section")
    return lax.ppermute(array, "section", [(i, i + by) for i in range(sections - by)])


def swapped(array, step):
    groups = lax.axis_size("group")
    devices = lax.axis_size("dp")
    bits = devices.bit_length() - 1
    pairs = []
    for p in range(devices):
        for g in range(groups):
            pairs.append((p * groups + g, (p ^ (1 << ((step + g) % bits))) * groups + g))
    return lax.ppermute(array, ("dp", "group"), pairs)


def handed(array, by):
    groups = lax.axis_size("group")
    return lax.ppermute(array, "group", [(i, (i + by) % groups) for i in range(groups)])


def plane_places():
    groups = lax.axis_size("group")
    bits = lax.axis_size("dp").bit_length() - 1
    masks = []
    for g in range(groups):
        order = [0]
        for step in range(bits):
            order = order + [m ^ (1 << ((step + g) % bits)) for m in order]
        masks.append(order)
    masks = jnp.asarray(masks, jnp.int32)
    dp, member = lax.axis_index("dp"), lax.axis_index("group")
    places = []
    for r in range(groups):
        giver = (member + groups - r) % groups
        places.append((dp ^ masks[giver]) * groups + giver)
    return jnp.concatenate(places).astype(jnp.int32)


def local(tokens_in, cotangent, gains, w_qkv, w_out, segments, plan):
    sections = lax.axis_size("section")
    groups = lax.axis_size("group")
    devices = lax.axis_size("dp")
    plane = devices * groups
    section = lax.axis_index("section")
    member = lax.axis_index("group")
    rows_dev = plan.shape[1]
    length = segments.shape[1]
    tokens, width = tokens_in.shape
    head = w_out.shape[1]
    share = rows_dev // groups
    w_layer, out_layer = w_qkv[0], w_out[0]
    place = member.astype(jnp.int32)[None]
    layer = section.astype(jnp.int32)[None]

    slice_rows = head // plane
    mine = lax.axis_index("dp") * groups + member
    own_rows = cut(out_layer, mine.astype(jnp.int32)[None], slice_rows)
    parts = pick(tokens_in.reshape(rows_dev, length, width), plan, place, groups, [own_rows])
    slices = [raised(own_rows, r) for r in range(sections - 1, 0, -1)]
    slices = [own_rows] + slices[::-1]
    chosen = jnp.take(segments, plan[0], axis=0, mode="clip").astype(BF16)
    chosen = chosen.reshape(groups, share, length)
    moved, moved_seg = [], []
    for r in range(groups):
        outgoing = lax.dynamic_index_in_dim(chosen, (member + r) % groups, 0, keepdims=False)
        moved.append(handed(parts[r], r) if r else parts[r])
        moved_seg.append(handed(outgoing, r) if r else outgoing)
    moved = [part.reshape(share * length, width) for part in moved]
    order = (member - jnp.arange(groups)) % groups
    seg = jnp.take(jnp.stack(moved_seg), order, axis=0, mode="clip").reshape(tokens)
    at = jnp.arange(tokens)
    mask = (
        (at[:, None] >= at[None, :])
        & (at[:, None] // length == at[None, :] // length)
        & (seg[:, None] == seg[None, :])
    ).astype(F32)

    last = (section == sections - 1).astype(jnp.int32)[None]
    bits = devices.bit_length() - 1
    places = plane_places()
    x, xz, norms = project(
        moved, cotangent, gains, w_layer, out_layer, place, []
    )
    coupling, stack = couple(slices, gains, w_layer, out_layer, last, [mask, places, xz])
    others = [shifted(coupling, r) for r in range(1, sections)]

    streams = stream_columns(width // CHUNKS)

    def facing(array, by):
        return lax.ppermute(array, "section", [(i, i ^ by) for i in range(sections)])

    arrays, masks, by = [hold(xz, others[:1])], [0], sections // 2
    while by > 0:
        arrays = arrays + [facing(array, by) for array in arrays]
        masks = masks + [mask_of ^ by for mask_of in masks]
        by = by // 2
    xz_all = [arrays[masks.index(r)] for r in range(sections)]
    early = [xz_all[r] for r in range(1, sections) if r & (r - 1) == 0]
    late = [xz_all[r] for r in range(1, sections) if r & (r - 1) != 0]
    pieces = [compact([coupling] + others, layer, 3 * head, head, [xz])]

    rows = [stack[None]]
    for step in range(bits):
        if step > 0:
            pieces = [merge(*pieces, early)]
        pieces = pieces + [swapped(pieces[0], step)]
        if step == bits - 1:
            pieces[-1] = hold(pieces[-1], late)
        if step > 0:
            rows = [gather_two(*rows, pieces[-1:])]
        rows = rows + [swapped(rows[0], step)]
    pieces = pieces + [handed(array, r) for r in range(1, groups) for array in pieces]
    sent, total, mixes, *leaving = serial(
        xz_all, pieces, places, norms, mask, layer, gains, w_layer, out_layer, streams
    )
    back, pair = widen(sent, gains, w_layer, out_layer, width // CHUNKS)

    down = [(i, i - 1) for i in range(1, sections)]
    behind = sections - 1 - section

    def index(tick):
        return jnp.clip(tick - behind, 0, CHUNKS - 1).astype(jnp.int32)[None]

    def lowered(arrays):
        return [lax.ppermute(array, "section", down) for array in arrays]

    ticks = CHUNKS + sections - 1
    after = {}
    for tick in range(1, ticks):
        arrived = lowered(leaving)
        if tick < ticks - 1:
            for i, cols in enumerate(streams):
                leaving[i], pair = join(
                    index(tick), arrived[i], pair, cols, after.get(tick, [])
                )
        if tick == 1:
            rows = [hold(array, leaving) for array in rows]
            rows = rows + [handed(array, r) for r in range(1, groups) for array in rows]
            rests, halves = [], []
            for part in range(PARTS):
                rest, half = settle(
                    total, mixes, rows, places, x, cotangent, back, width // CHUNKS, part, PARTS
                )
                rests.append(rest)
                halves.append(half)
            sums = [stacked(halves)]
            for step in range(bits):
                sums.append(added([sums[-1], swapped(sums[-1], step)]))
            sums.append(added(sums[-1:] + [handed(sums[-1], r) for r in range(1, groups)]))
            gain_whole = sums[-1].reshape(1, width)
            after = {2 + i: [array] for i, array in enumerate(sums)}
    out = finish(index(ticks - 1), arrived, pair, rests, streams)
    return (out[None], gain_whole)


def attend(hidden, segment, gain_row, w_layer, out_layer):
    count, length, width = hidden.shape
    head = out_layer.shape[0]
    scaled = hidden * lax.rsqrt(jnp.mean(hidden * hidden, axis=-1, keepdims=True) + EPS) * gain_row
    normed = scaled.astype(BF16).reshape(count * length, width)
    projected = jnp.dot(normed, w_layer, preferred_element_type=F32).reshape(count, length, 3 * head)
    query = projected[:, :, :head]
    keyed = projected[:, :, head : 2 * head]
    valued = projected[:, :, 2 * head :]
    positions = jnp.arange(length)
    allowed = (positions[:, None] >= positions[None, :])[None] & (
        segment[:, :, None] == segment[:, None, :]
    )
    scores = jnp.einsum("rid,rjd->rij", query, keyed, precision=lax.Precision.HIGHEST)
    scores = jnp.where(allowed, scores / math.sqrt(head), -1e30)
    weights = jax.nn.softmax(scores, axis=-1)
    mixed = jnp.einsum("rij,rjd->rid", weights, valued, precision=lax.Precision.HIGHEST)
    mixed = mixed.astype(BF16).reshape(count * length, head)
    output = jnp.dot(mixed, out_layer, preferred_element_type=F32).reshape(count, length, width)
    return hidden + output


MB_ROWS = 2


def relay(tokens_in, cotangent, gains, w_qkv, w_out, segments, plan):
    sections = lax.axis_size("section")
    section = lax.axis_index("section")
    rows_dev = plan.shape[1]
    width = tokens_in.shape[1]
    length = segments.shape[1]
    micro = rows_dev // MB_ROWS
    blocks = tokens_in.reshape(rows_dev, length, width)
    chosen = jnp.take(blocks, plan[0], axis=0)
    chosen_seg = jnp.take(segments, plan[0], axis=0).astype(BF16)
    assigned = lax.all_to_all(chosen, "group", split_axis=0, concat_axis=0, tiled=True)
    moved_seg = lax.all_to_all(chosen_seg, "group", split_axis=0, concat_axis=0, tiled=True)
    assigned = assigned.reshape(micro, MB_ROWS, length, width)
    seg_groups = moved_seg.reshape(micro, MB_ROWS, length)
    gain_row, w_layer, out_layer = gains[0], w_qkv[0], w_out[0]
    grad_rows = cotangent.reshape(micro, MB_ROWS, length, width)
    ticks = micro + sections - 1

    def passed_along(array, by):
        pairs = [(i, i + by) for i in range(sections) if 0 <= i + by < sections]
        return lax.ppermute(array, "section", pairs)

    def at(array, i):
        return lax.dynamic_index_in_dim(array, i, 0, keepdims=False)

    def forward_tick(tick, carry):
        saved, arrived = carry
        index = tick - section
        valid = (index >= 0) & (index < micro)
        clipped = jnp.clip(index, 0, micro - 1)
        entering = jnp.where(section == 0, at(assigned, clipped), arrived)
        kept = jnp.where(valid, entering, at(saved, clipped))
        saved = lax.dynamic_update_index_in_dim(saved, kept, clipped, 0)
        segment = at(seg_groups, clipped)

        def run_layer(value):
            return attend(value.astype(F32), segment, gain_row, w_layer, out_layer).astype(BF16)

        leaving = lax.cond(valid, run_layer, jnp.zeros_like, entering)
        return (saved, passed_along(leaving, 1))

    saved_init = jnp.zeros((micro, MB_ROWS, length, width), BF16)
    arrive_init = jnp.zeros((MB_ROWS, length, width), BF16)
    saved, _ = lax.fori_loop(0, ticks, forward_tick, (saved_init, arrive_init))

    def backward_tick(tick, carry):
        grads_x, gain_total, arrived = carry
        index = tick - (sections - 1 - section)
        valid = (index >= 0) & (index < micro)
        clipped = jnp.clip(index, 0, micro - 1)
        entering = jnp.where(section == sections - 1, at(grad_rows, clipped), arrived)
        segment = at(seg_groups, clipped)
        stored = at(saved, clipped).astype(F32)

        def local_layer(hidden, gains_here):
            return attend(hidden, segment, gains_here, w_layer, out_layer)

        def run_back(value):
            _, pullback = jax.vjp(local_layer, stored, gain_row)
            grad_hidden, grad_gain = pullback(value.astype(F32))
            return (grad_hidden.astype(BF16), grad_gain)

        def skip_back(value):
            return (jnp.zeros_like(value), jnp.zeros(gain_row.shape, F32))

        sending, grad_gain = lax.cond(valid, run_back, skip_back, entering)
        kept = jnp.where(valid, sending, at(grads_x, clipped))
        grads_x = lax.dynamic_update_index_in_dim(grads_x, kept, clipped, 0)
        return (grads_x, gain_total + grad_gain, passed_along(sending, -1))

    gain_init = jnp.zeros(gain_row.shape, F32)
    grads_x, gain_total, _ = lax.fori_loop(
        0, ticks, backward_tick, (saved_init, gain_init, arrive_init)
    )
    gain_whole = lax.psum(gain_total, ("dp", "group"))
    return (grads_x.reshape(1, rows_dev * length, width), gain_whole[None])


def solution(mesh):
    placed = (
        P(("dp", "group"), None),
        P(("dp", "group"), None),
        P("section", None),
        P("section", None, None),
        P("section", None, None),
        P(("dp", "group"), None),
        P(("dp", "group"), None),
    )

    def chosen(tokens_in, cotangent, gains, w_qkv, w_out, segments, plan):
        sections, head, width = w_out.shape
        devices = mesh.shape["dp"]
        small = sections * 4 * head < width and sections > 1
        halves = devices & (devices - 1) == 0 and sections & (sections - 1) == 0
        body = local if small and halves else relay
        return jax.shard_map(
            body,
            mesh=mesh,
            in_specs=placed,
            out_specs=(P("section", ("dp", "group"), None), P("section", None)),
            check_vma=False,
        )(tokens_in, cotangent, gains, w_qkv, w_out, segments, plan)

    return chosen
```

```python
import math

import jax
import jax.numpy as jnp
from jax import lax
from jax.experimental import pallas as pl
from jax.experimental.pallas import tpu as pltpu
from jax.sharding import PartitionSpec as P

EPS = 1e-05
VMEM_BYTES = 24 * 1024 * 1024
SMALL = 16 * 1024 * 1024
F32 = jnp.float32
BF16 = jnp.bfloat16


def dot_nn(a, b):
    return lax.dot_general(a, b, (((1,), (0,)), ((), ())), preferred_element_type=F32)


def dot_nt(a, b):
    return lax.dot_general(a, b, (((1,), (1,)), ((), ())), preferred_element_type=F32)


def dot_tn(a, b):
    return lax.dot_general(a, b, (((0,), (0,)), ((), ())), preferred_element_type=F32)


IN_HBM = pl.BlockSpec(memory_space=pltpu.HBM)
ANYWHERE = pl.BlockSpec(memory_space=pl.ANY)
IN_VMEM = pl.BlockSpec(memory_space=pltpu.VMEM)
IN_SMEM = pl.BlockSpec(memory_space=pltpu.SMEM)


def in_hbm(array):
    return pltpu.with_memory_space_constraint(array, pltpu.HBM)


def in_vmem(array):
    return pltpu.with_memory_space_constraint(array, pltpu.VMEM)


def mover(sems):
    used = []

    def start(source, target):
        copy = pltpu.make_async_copy(source, target, sems.at[len(used)])
        copy.start()
        used.append(copy)
        return copy

    return start


def steps(width):
    step = min(width, 1024)
    return [slice(at, at + step) for at in range(0, width, step)]


def params(limit=VMEM_BYTES):
    return pltpu.CompilerParams(vmem_limit_bytes=limit)


def pick(tokens, plan, place, groups, out_layer, mine, slice_rows):
    rows, length, width = tokens.shape
    share = rows // groups

    def kernel(plan_ref, place_ref, mine_ref, tokens_ref, o_ref, *rest):
        slice_ref, parts = rest[0], rest[1 : 1 + groups]
        slice_in, rows_in, sems = rest[1 + groups :]
        start = mover(sems)
        at = pl.ds(pl.multiple_of(mine_ref[0] * slice_rows, slice_rows), slice_rows)
        loads = [(start(o_ref.at[at], slice_in), slice_in, slice_ref)]
        for r in range(groups):
            target = lax.rem(place_ref[0] + r, groups)
            for c in range(share):
                here = rows_in.at[r * share + c]
                row = plan_ref[0, target * share + c]
                loads.append((start(tokens_ref.at[row], here), here, parts[r].at[c]))
        stores = []
        for load, here, there in loads:
            load.wait()
            stores.append(start(here, there))
        for store in stores:
            store.wait()

    return pl.pallas_call(
        kernel,
        out_shape=[pltpu.HBM((slice_rows, width), BF16)]
        + [pltpu.HBM((share, length, width), BF16)] * groups,
        in_specs=[IN_SMEM, IN_SMEM, IN_SMEM, IN_HBM, IN_HBM],
        out_specs=[IN_HBM] * (1 + groups),
        scratch_shapes=[
            pltpu.VMEM((slice_rows, width), BF16),
            pltpu.VMEM((rows, length, width), BF16),
            pltpu.SemaphoreType.DMA((2 * rows + 2,)),
        ],
        compiler_params=params(),
        name="pick",
    )(plan, place, mine, in_hbm(tokens), in_hbm(out_layer))


def project(parts, cotangent, gain, w_layer, out_layer, place, after):
    groups = len(parts)
    tokens, width = cotangent.shape
    head = out_layer.shape[0]
    wide = w_layer.shape[1]
    block = tokens // groups
    cuts = steps(width)
    copies = len(cuts) * (groups + 4)

    def kernel(place_ref, *refs):
        part_refs = refs[:groups]
        cot_ref, g_ref, w_ref, o_ref = refs[groups : groups + 4]
        x_ref, xz_ref, n_ref = refs[groups + 4 + len(after) : groups + 7 + len(after)]
        x_in, c_in, w_in, o_in, sems = refs[groups + 7 + len(after) :]
        start = mover(sems)
        loads = []
        for cut in cuts:
            mine = [start(w_ref.at[cut], w_in.at[cut])]
            mine.append(start(o_ref.at[:, cut], o_in.at[:, cut]))
            for r in range(groups):
                source = lax.rem(place_ref[0] + groups - r, groups)
                rows = pl.ds(pl.multiple_of(source * block, block), block)
                mine.append(start(part_refs[r].at[:, cut], x_in.at[rows, cut]))
            mine.append(start(cot_ref.at[:, cut], c_in.at[:, cut]))
            loads.append(mine)
        through = jnp.zeros((tokens, wide), F32)
        across = jnp.zeros((tokens, head), F32)
        back = jnp.zeros((tokens, head), F32)
        square = jnp.zeros((tokens, 1), F32)
        stores = []
        for cut, mine in zip(cuts, loads):
            for load in mine:
                load.wait()
            stores.append(start(x_in.at[:, cut], x_ref.at[:, cut]))
            x = x_in[:, cut]
            xf = x.astype(F32)
            through += dot_nn((xf * g_ref[:, cut]).astype(BF16), w_in[cut, :])
            across += dot_nt(x, o_in[:, cut])
            back += dot_nt(c_in[:, cut], o_in[:, cut])
            square += jnp.sum(xf * xf, axis=1, keepdims=True)
        xz_ref[:, :wide] = through.astype(BF16)
        xz_ref[:, wide : wide + head] = across.astype(BF16)
        xz_ref[:, wide + head :] = back.astype(BF16)
        n_ref[...] = square
        for store in stores:
            store.wait()

    return pl.pallas_call(
        kernel,
        out_shape=[
            pltpu.HBM((tokens, width), BF16),
            jax.ShapeDtypeStruct((tokens, wide + 2 * head), BF16),
            jax.ShapeDtypeStruct((tokens, 1), F32),
        ],
        in_specs=[IN_SMEM]
        + [ANYWHERE] * groups
        + [IN_HBM, IN_VMEM, IN_HBM, IN_HBM]
        + [ANYWHERE] * len(after),
        out_specs=[IN_HBM, IN_VMEM, IN_VMEM],
        scratch_shapes=[
            pltpu.VMEM((tokens, width), BF16),
            pltpu.VMEM((tokens, width), BF16),
            pltpu.VMEM((width, wide), BF16),
            pltpu.VMEM((head, width), BF16),
            pltpu.SemaphoreType.DMA((copies,)),
        ],
        compiler_params=params(),
        name="project",
    )(
        place,
        in_hbm(parts[0]),
        *[in_vmem(part) for part in parts[1:]],
        in_hbm(cotangent),
        gain,
        in_hbm(w_layer),
        in_hbm(out_layer),
        *after,
    )


def couple(slices, gain, w_layer, out_layer, last, after):
    sections = len(slices)
    count, width = slices[0].shape
    head = out_layer.shape[0]
    wide = w_layer.shape[1]
    below = (sections - 2) * wide
    packed = below + max(wide, (sections - 1) * head)
    cuts = steps(width)
    copies = len(cuts) * (sections + 2) + sections - 1

    def kernel(last_ref, *refs):
        s_refs = refs[:sections][::-1]
        g_ref, w_ref, o_ref = refs[sections : sections + 3]
        out_ref, stack_ref, r_in, w_in, o_in, sems = refs[sections + 3 + len(after) :]
        rows = [slice(r * count, (r + 1) * count) for r in range(sections)]
        start = mover(sems)
        loads = []
        for cut in cuts:
            mine = [start(w_ref.at[cut], w_in.at[cut])]
            mine.append(start(o_ref.at[:, cut], o_in.at[:, cut]))
            for r in range(sections):
                mine.append(start(s_refs[r].at[:, cut], r_in.at[rows[r], cut]))
            loads.append(mine)
        through = jnp.zeros((sections * count, wide), F32)
        across = jnp.zeros((sections * count, head), F32)
        for cut, mine in zip(cuts, loads):
            for load in mine:
                load.wait()
            r = r_in[:, cut]
            through += dot_nn((r.astype(F32) * g_ref[:, cut]).astype(BF16), w_in[cut, :])
            across += dot_nt(r, o_in[:, cut])
        stores = [start(r_in.at[rows[r]], stack_ref.at[r - 1]) for r in range(1, sections)]
        through = through.astype(BF16)
        across = across.astype(BF16)
        out_ref[...] = jnp.zeros_like(out_ref)
        for r in range(1, sections - 1):
            out_ref[:, (r - 1) * wide : r * wide] = through[rows[r]]

        @pl.when(last_ref[0] == 1)
        def _():
            out_ref[:, below : below + wide] = through[rows[-1]]

        @pl.when(last_ref[0] == 0)
        def _():
            for r in range(sections - 1):
                out_ref[:, below + r * head : below + (r + 1) * head] = across[rows[r]]

        for store in stores:
            store.wait()

    return pl.pallas_call(
        kernel,
        out_shape=[
            jax.ShapeDtypeStruct((count, packed), BF16),
            pltpu.HBM((sections - 1, count, width), BF16),
        ],
        in_specs=[IN_SMEM]
        + [ANYWHERE] * sections
        + [IN_VMEM, IN_HBM, IN_HBM]
        + [ANYWHERE] * len(after),
        out_specs=[IN_VMEM, IN_HBM],
        scratch_shapes=[
            pltpu.VMEM((sections * count, width), BF16),
            pltpu.VMEM((width, wide), BF16),
            pltpu.VMEM((head, width), BF16),
            pltpu.SemaphoreType.DMA((copies,)),
        ],
        compiler_params=params(),
        name="couple",
    )(last, *slices[::-1], gain, in_hbm(w_layer), in_hbm(out_layer), *after)


def layout(sections, wide, head):
    through, across, at = {}, {}, 0
    for k in range(sections):
        for j in range(k):
            through[j, k] = slice(at, at + wide)
            at += wide
        for j in range(k + 1 if k < sections - 1 else 0):
            across[j, k] = slice(at, at + head)
            at += head
    return through, across, at


def compact(parts, section, wide, head, after):
    sections = len(parts)
    count = parts[0].shape[0]
    below = (sections - 2) * wide
    through, across, total = layout(sections, wide, head)

    def kernel(s_ref, *refs):
        part_refs, out_ref = refs[:sections], refs[-1]
        mine = s_ref[0]

        def fill(k, r):
            for j in range(k):
                at = (k - j - 1) * wide
                out_ref[0, :, through[j, k]] = part_refs[r][:, at : at + wide]
            for j in range(k + 1 if k < sections - 1 else 0):
                at = below + (k - j) * head
                out_ref[0, :, across[j, k]] = part_refs[r][:, at : at + head]

        for s in range(sections):

            @pl.when(mine == s)
            def _(s=s):
                for r in range(sections):
                    fill((s - r) % sections, r)

    vmem = pl.BlockSpec(memory_space=pltpu.VMEM)
    return pl.pallas_call(
        kernel,
        out_shape=jax.ShapeDtypeStruct((1, count, total), BF16),
        in_specs=[IN_SMEM] + [vmem] * sections + [ANYWHERE] * len(after),
        out_specs=vmem,
        compiler_params=params(SMALL),
        name="compact",
    )(section, *parts, *after)


def merge(first, second, after):
    count = first.shape[0]

    def kernel(first_ref, second_ref, *refs):
        refs[-1][:count] = first_ref[...]
        refs[-1][count:] = second_ref[...]

    return pl.pallas_call(
        kernel,
        out_shape=jax.ShapeDtypeStruct((2 * count,) + first.shape[1:], first.dtype),
        in_specs=[IN_VMEM] * 2 + [ANYWHERE] * len(after),
        out_specs=IN_VMEM,
        compiler_params=params(SMALL),
        name="merge",
    )(first, second, *after)


def serial(xz, pieces, places, norms, mask, section, gain, w_layer, out_layer, streams):
    sections = len(xz)
    tokens = norms.shape[0]
    head, width = out_layer.shape
    wide = 3 * head
    scale = 1.0 / math.sqrt(head)
    lead = slice(0, streams[-1].stop)
    through_at, across_at, _ = layout(sections, wide, head)
    count, packed = pieces[0].shape[-2:]
    plane = head // count
    n_in = sections + len(pieces)
    copies = sections + plane + 2

    def kernel(s_ref, p_ref, *refs):
        xz_refs, piece_refs = refs[:sections], refs[sections:n_in]
        n_ref, mask_ref, g_ref, w_ref, o_ref = refs[n_in : n_in + 5]
        n_out = n_in + 5
        v_ref, t_ref, a_ref = refs[n_out : n_out + 3]
        first_refs = refs[n_out + 3 : n_out + 3 + len(streams)]
        scratch = refs[n_out + 3 + len(streams) :]
        xz_all, table, mixes, weights, projs, dmix, w_in, o_in, sems = scratch
        mine = s_ref[0]
        started = []

        def start(source, target):
            copy = pltpu.make_async_copy(source, target, sems.at[len(started)])
            copy.start()
            started.append(copy)

        for r in range(sections):
            start(xz_refs[r], xz_all.at[mine ^ r])
        at = 0
        for ref in piece_refs:
            for i in range(ref.shape[0]):
                start(ref.at[i], table.at[p_ref[at]])
                at += 1
        small = list(started)
        start(w_ref.at[lead], w_in)
        start(o_ref.at[:, lead], o_in)
        for copy in small:
            copy.wait()

        def through(j, k):
            return table[:, :, through_at[j, k]].reshape(head, wide)

        def across(j, k):
            return table[:, :, across_at[j, k]].reshape(head, head)

        allowed = mask_ref[...] > 0.5
        norm = n_ref[...]
        rstds, tails, mixed = [], [], []
        for s in range(sections):
            proj = xz_all[s, :, :wide].astype(F32)
            for j in range(s):
                proj = proj + dot_nn(mixed[j], through(j, s))
            rstd = lax.rsqrt(norm * (1.0 / width) + EPS)
            proj = proj * rstd
            projs[s] = proj.astype(BF16)
            q, k, v = (projs[s, :, i * head : (i + 1) * head] for i in range(3))
            scores = jnp.where(allowed, dot_nt(q, k) * scale, -1e30)
            scores = jnp.exp(scores - jnp.max(scores, axis=1, keepdims=True))
            soft = scores / jnp.sum(scores, axis=1, keepdims=True)
            weights[s] = soft
            mix = dot_nn(soft.astype(BF16), v).astype(BF16)
            mixed.append(mix)
            mixes[:, s * head : (s + 1) * head] = mix
            rstds.append(rstd)
            dmix[:, s * head : (s + 1) * head] = xz_all[s, :, wide + head :].astype(F32)
            if s == sections - 1:
                break
            y = xz_all[s, :, wide : wide + head].astype(F32)
            for j in range(s):
                y = y + dot_nn(mixed[j], across(j, s))
            tail = y + dot_nn(mix, across(s, s))
            norm = norm + jnp.sum(mix.astype(F32) * (y + tail), axis=1, keepdims=True)
            norm = jnp.maximum(norm, 0.0)
            tails.append(tail)
        total = jnp.zeros((tokens, 1), F32)
        a_ref[...] = jnp.zeros_like(a_ref)
        for s in reversed(range(sections)):
            cols = slice(s * head, (s + 1) * head)
            da = dmix[:, cols]
            if s < sections - 1:
                da = da - total * tails[s]
            da = da.astype(BF16)
            q, k, v = (projs[s, :, i * head : (i + 1) * head] for i in range(3))
            soft = weights[s]
            dv = dot_tn(soft.astype(BF16), da)
            dsoft = dot_nt(da, v)
            dscore = soft * (dsoft - jnp.sum(dsoft * soft, axis=1, keepdims=True))
            dscore = (dscore * scale).astype(BF16)
            dproj = jnp.concatenate([dot_nn(dscore, k), dot_tn(dscore, q), dv], axis=1)
            along = jnp.sum(dproj * projs[s].astype(F32), axis=1, keepdims=True)
            first = (dproj * rstds[s]).astype(BF16)
            second = (-total * mixes[:, cols].astype(F32)).astype(BF16)
            total = total + rstds[s] * rstds[s] * along * (1.0 / width)
            for j in reversed(range(s)):
                term = dot_nt(first, through(j, s))
                if s < sections - 1:
                    term = term + dot_nt(second, across(j, s))
                dmix[:, j * head : (j + 1) * head] += term

            @pl.when(mine == s)
            def _(first=first, second=second, total=total):
                v_ref[:, :wide] = first
                v_ref[:, wide:] = second
                t_ref[...] = total

            for r in range(1, sections - s):

                @pl.when(mine == s + r)
                def _(r=r, cols=cols):
                    a_ref[:, (r - 1) * head : r * head] = mixes[:, cols]

        for copy in started[len(small) :]:
            copy.wait()
        own = dot_nt(v_ref[:, :wide], w_in[...]) * g_ref[:, lead]
        own = (own + dot_nn(v_ref[:, wide:], o_in[...])).astype(BF16)
        for ref, part in zip(first_refs, streams):
            ref[...] = own[:, part]

    vmem = pl.BlockSpec(memory_space=pltpu.VMEM)
    smem = pl.BlockSpec(memory_space=pltpu.SMEM)
    return pl.pallas_call(
        kernel,
        out_shape=[
            pltpu.VMEM((tokens, wide + head), BF16),
            pltpu.VMEM((tokens, 1), F32),
            pltpu.VMEM((tokens, (sections - 1) * head), BF16),
        ]
        + [pltpu.VMEM((tokens, part.stop - part.start), BF16) for part in streams],
        in_specs=[smem, smem] + [ANYWHERE] * n_in + [vmem, vmem, vmem, IN_HBM, IN_HBM],
        out_specs=[vmem] * (3 + len(streams)),
        scratch_shapes=[
            pltpu.VMEM((sections,) + xz[0].shape, BF16),
            pltpu.VMEM((plane, count, packed), BF16),
            pltpu.VMEM((tokens, sections * head), BF16),
            pltpu.VMEM((sections, tokens, tokens), F32),
            pltpu.VMEM((sections, tokens, wide), BF16),
            pltpu.VMEM((tokens, sections * head), F32),
            pltpu.VMEM((lead.stop, wide), BF16),
            pltpu.VMEM((head, lead.stop), BF16),
            pltpu.SemaphoreType.DMA((copies,)),
        ],
        compiler_params=params(),
        name="serial",
    )(
        section,
        places,
        *xz,
        *pieces,
        norms,
        mask,
        gain,
        in_hbm(w_layer),
        in_hbm(out_layer),
    )


def hold(array, after):
    def kernel(*refs):
        pass

    return pl.pallas_call(
        kernel,
        out_shape=jax.ShapeDtypeStruct(array.shape, array.dtype),
        in_specs=[ANYWHERE] * (1 + len(after)),
        out_specs=ANYWHERE,
        input_output_aliases={0: 0},
        compiler_params=params(SMALL),
        name="hold",
    )(array, *after)


def gather_two(first, second, after):
    count = first.shape[0]

    def kernel(first_ref, second_ref, *refs):
        out_ref, sems = refs[len(after) :]
        start = mover(sems)
        copies = [start(first_ref, out_ref.at[:count]), start(second_ref, out_ref.at[count:])]
        for copy in copies:
            copy.wait()

    return pl.pallas_call(
        kernel,
        out_shape=jax.ShapeDtypeStruct((2 * count,) + first.shape[1:], first.dtype),
        in_specs=[ANYWHERE] * (2 + len(after)),
        out_specs=IN_VMEM,
        scratch_shapes=[pltpu.SemaphoreType.DMA((2,))],
        compiler_params=params(SMALL),
        name="gather_two",
    )(first, second, *after)


def widen(sent, gain, w_layer, out_layer, chunk):
    tokens = sent.shape[0]
    head, width = out_layer.shape
    wide = w_layer.shape[1]
    cuts = [slice(at, at + chunk) for at in range(0, width, chunk)]

    def kernel(v_ref, g_ref, w_ref, o_ref, back_ref, pair_ref, back_in, w_in, o_in, sems):
        start = mover(sems)
        loads = [
            (start(w_ref.at[cut], w_in.at[cut]), start(o_ref.at[:, cut], o_in.at[:, cut]))
            for cut in cuts
        ]
        stores = []
        for i, (cut, mine) in enumerate(zip(cuts, loads)):
            for load in mine:
                load.wait()
            back = dot_nt(v_ref[:, :wide], w_in[cut, :])
            own = back * g_ref[:, cut] + dot_nn(v_ref[:, wide:], o_in[:, cut])
            back_in[:, cut] = back.astype(BF16)
            stores.append(start(back_in.at[:, cut], back_ref.at[:, cut]))
            pair_ref[0, i] = own.astype(BF16)
            pair_ref[1, i] = jnp.zeros_like(pair_ref[1, i])
        for store in stores:
            store.wait()

    return pl.pallas_call(
        kernel,
        out_shape=[
            pltpu.HBM((tokens, width), BF16),
            pltpu.VMEM((2, len(cuts), tokens, chunk), BF16),
        ],
        in_specs=[IN_VMEM, IN_VMEM, IN_HBM, IN_HBM],
        out_specs=[IN_HBM, IN_VMEM],
        scratch_shapes=[
            pltpu.VMEM((tokens, width), BF16),
            pltpu.VMEM((width, wide), BF16),
            pltpu.VMEM((head, width), BF16),
            pltpu.SemaphoreType.DMA((3 * len(cuts),)),
        ],
        compiler_params=params(),
        name="widen",
    )(in_vmem(sent), gain, in_hbm(w_layer), in_hbm(out_layer))


def settle(total, mixes, stacks, places, x, cotangent, back, chunk, part, parts):
    tokens, width = x.shape
    layers, rows = stacks[0].shape[1:3]
    entries = [(i, e) for i, stack in enumerate(stacks) for e in range(stack.shape[0])]
    plane = len(entries)
    head = plane * rows
    span = width // parts
    base = part * span
    cuts = [slice(at, at + chunk) for at in range(0, span, chunk)]
    copies = plane * layers + 3 * len(cuts)

    def kernel(p_ref, t_ref, a_ref, x_ref, c_ref, back_ref, *refs):
        stack_refs = refs[: len(stacks)]
        rest_ref, dg_ref = refs[len(stacks) : len(stacks) + 2]
        lower, x_in, c_in, back_in, sems = refs[len(stacks) + 2 :]
        start = mover(sems)
        first = []
        for at, (i, e) in enumerate(entries):
            for r in range(layers):
                here = pl.ds(base, span)
                first.append(start(stack_refs[i].at[e, r, :, here], lower.at[r, p_ref[at]]))
        loads = []
        for cut in cuts:
            there = pl.ds(base + cut.start, chunk)
            mine = [start(x_ref.at[:, there], x_in.at[:, cut])]
            mine.append(start(c_ref.at[:, there], c_in.at[:, cut]))
            mine.append(start(back_ref.at[:, there], back_in.at[:, cut]))
            loads.append(mine)
        for load in first:
            load.wait()
        for i, (cut, mine) in enumerate(zip(cuts, loads)):
            for load in mine:
                load.wait()
            below = lower[:, :, :, cut].reshape(layers * head, chunk)
            here = x_in[:, cut].astype(F32) + dot_nn(a_ref[...], below)
            rest_ref[i] = (c_in[:, cut].astype(F32) - t_ref[...] * here).astype(BF16)
            gain = jnp.sum(back_in[:, cut].astype(F32) * here, axis=0, keepdims=True)
            for at in range(0, chunk, head):
                row = (cut.start + at) // head
                dg_ref[row : row + 1, :] = gain[:, at : at + head]

    return pl.pallas_call(
        kernel,
        out_shape=[
            pltpu.VMEM((len(cuts), tokens, chunk), BF16),
            pltpu.VMEM((span // head, head), F32),
        ],
        in_specs=[IN_SMEM] + [IN_VMEM] * 2 + [IN_HBM] * (3 + len(stacks)),
        out_specs=[IN_VMEM] * 2,
        scratch_shapes=[
            pltpu.VMEM((layers, plane, rows, span), BF16),
            pltpu.VMEM((tokens, span), BF16),
            pltpu.VMEM((tokens, span), BF16),
            pltpu.VMEM((tokens, span), BF16),
            pltpu.SemaphoreType.DMA((copies,)),
        ],
        compiler_params=params(),
        name="settle",
    )(
        places,
        in_vmem(total),
        in_vmem(mixes),
        *[in_hbm(array) for array in (x, cotangent, back, *stacks)],
    )


def join(index, arrived, pair, cols, after):
    tokens, part = arrived.shape

    def kernel(i_ref, r_ref, _, *refs):
        send_ref, pair_ref = refs[len(after) :]
        at = i_ref[0]
        r = r_ref[...]
        send_ref[...] = (pair_ref[0, at, :, cols].astype(F32) + r.astype(F32)).astype(BF16)
        pair_ref[1, at, :, cols] = r

    return pl.pallas_call(
        kernel,
        out_shape=[pltpu.VMEM((tokens, part), BF16), pltpu.VMEM(pair.shape, BF16)],
        in_specs=[IN_SMEM] + [IN_VMEM] * 2 + [ANYWHERE] * len(after),
        out_specs=[IN_VMEM] * 2,
        input_output_aliases={2: 1},
        compiler_params=params(SMALL),
        name="join",
    )(index, in_vmem(arrived), in_vmem(pair), *after)


def finish(index, arrived, pair, rests, streams):
    _, count, tokens, chunk = pair.shape

    def kernel(i_ref, *refs):
        r_refs = refs[: len(streams)]
        pair_ref, rest_refs = refs[len(streams)], refs[len(streams) + 1 :][: len(rests)]
        whole_ref, whole, sems = refs[len(streams) + 1 + len(rests) :]
        each = count // len(rests)
        at = i_ref[0]
        copies = []
        for i in range(count):
            full = rest_refs[i // each][i % each].astype(F32) + pair_ref[0, i].astype(F32)
            whole[i] = (full + pair_ref[1, i].astype(F32)).astype(BF16)

            @pl.when(at == i)
            def _(i=i, full=full):
                for ref, cols in zip(r_refs, streams):
                    whole[i, :, cols] = (full[:, cols] + ref[...].astype(F32)).astype(BF16)

            there = whole_ref.at[:, pl.ds(i * chunk, chunk)]
            copies.append(pltpu.make_async_copy(whole.at[i], there, sems.at[i]))
            copies[-1].start()
        for copy in copies:
            copy.wait()

    return pl.pallas_call(
        kernel,
        out_shape=pltpu.HBM((tokens, count * chunk), BF16),
        in_specs=[IN_SMEM] + [IN_VMEM] * (len(streams) + 1 + len(rests)),
        out_specs=IN_HBM,
        scratch_shapes=[
            pltpu.VMEM((count, tokens, chunk), BF16),
            pltpu.SemaphoreType.DMA((count,)),
        ],
        compiler_params=params(SMALL),
        name="finish",
    )(index, *[in_vmem(array) for array in (*arrived, pair, *rests)])


def stacked(arrays):
    rows = arrays[0].shape[0]

    def kernel(*refs):
        for i, ref in enumerate(refs[:-1]):
            refs[-1][i * rows : (i + 1) * rows, :] = ref[...]

    return pl.pallas_call(
        kernel,
        out_shape=pltpu.VMEM((len(arrays) * rows, arrays[0].shape[1]), F32),
        in_specs=[IN_VMEM] * len(arrays),
        out_specs=IN_VMEM,
        compiler_params=params(SMALL),
        name="stacked",
    )(*[in_vmem(array) for array in arrays])


def added(arrays):
    def kernel(*refs):
        total = refs[0][...]
        for ref in refs[1:-1]:
            total = total + ref[...]
        refs[-1][...] = total

    return pl.pallas_call(
        kernel,
        out_shape=pltpu.VMEM(arrays[0].shape, F32),
        in_specs=[IN_VMEM] * len(arrays),
        out_specs=IN_VMEM,
        compiler_params=params(SMALL),
        name="added",
    )(*[in_vmem(array) for array in arrays])


STREAMS = 2
CHUNKS = 4
PARTS = 1


def stream_columns(chunk):
    lanes = 128
    tiles = chunk // lanes
    ends = [-(-tiles * (i + 1) // STREAMS) * lanes for i in range(STREAMS)]
    return [slice(start, end) for start, end in zip([0] + ends, ends)]


def shifted(array, by):
    sections = lax.axis_size("section")
    return lax.ppermute(array, "section", [(i, (i + by) % sections) for i in range(sections)])


def raised(array, by):
    sections = lax.axis_size("section")
    return lax.ppermute(array, "section", [(i, i + by) for i in range(sections - by)])


def swapped(array, step):
    groups = lax.axis_size("group")
    devices = lax.axis_size("dp")
    bits = devices.bit_length() - 1
    pairs = []
    for p in range(devices):
        for g in range(groups):
            pairs.append((p * groups + g, (p ^ (1 << ((step + g) % bits))) * groups + g))
    return lax.ppermute(array, ("dp", "group"), pairs)


def handed(array, by):
    groups = lax.axis_size("group")
    return lax.ppermute(array, "group", [(i, (i + by) % groups) for i in range(groups)])


def plane_places():
    groups = lax.axis_size("group")
    bits = lax.axis_size("dp").bit_length() - 1
    masks = []
    for g in range(groups):
        order = [0]
        for step in range(bits):
            order = order + [m ^ (1 << ((step + g) % bits)) for m in order]
        masks.append(order)
    masks = jnp.asarray(masks, jnp.int32)
    dp, member = lax.axis_index("dp"), lax.axis_index("group")
    places = []
    for r in range(groups):
        giver = (member + groups - r) % groups
        places.append((dp ^ masks[giver]) * groups + giver)
    return jnp.concatenate(places).astype(jnp.int32)


def local(tokens_in, cotangent, gains, w_qkv, w_out, segments, plan):
    sections = lax.axis_size("section")
    groups = lax.axis_size("group")
    devices = lax.axis_size("dp")
    plane = devices * groups
    section = lax.axis_index("section")
    member = lax.axis_index("group")
    rows_dev = plan.shape[1]
    length = segments.shape[1]
    tokens, width = tokens_in.shape
    head = w_out.shape[1]
    share = rows_dev // groups
    w_layer, out_layer = w_qkv[0], w_out[0]
    place = member.astype(jnp.int32)[None]
    layer = section.astype(jnp.int32)[None]

    slice_rows = head // plane
    mine = lax.axis_index("dp") * groups + member
    own_rows, *parts = pick(
        tokens_in.reshape(rows_dev, length, width),
        plan,
        place,
        groups,
        out_layer,
        mine.astype(jnp.int32)[None],
        slice_rows,
    )
    slices = [raised(own_rows, r) for r in range(sections - 1, 0, -1)]
    slices = [own_rows] + slices[::-1]
    chosen = jnp.take(segments, plan[0], axis=0, mode="clip").astype(BF16)
    chosen = chosen.reshape(groups, share, length)
    moved, moved_seg = [], []
    for r in range(groups):
        outgoing = lax.dynamic_index_in_dim(chosen, (member + r) % groups, 0, keepdims=False)
        moved.append(handed(parts[r], r) if r else parts[r])
        moved_seg.append(handed(outgoing, r) if r else outgoing)
    moved = [part.reshape(share * length, width) for part in moved]
    order = (member - jnp.arange(groups)) % groups
    seg = jnp.take(jnp.stack(moved_seg), order, axis=0, mode="clip").reshape(tokens)
    at = jnp.arange(tokens)
    mask = (
        (at[:, None] >= at[None, :])
        & (at[:, None] // length == at[None, :] // length)
        & (seg[:, None] == seg[None, :])
    ).astype(F32)

    last = (section == sections - 1).astype(jnp.int32)[None]
    bits = devices.bit_length() - 1
    places = plane_places()
    x, xz, norms = project(
        moved, cotangent, gains, w_layer, out_layer, place, []
    )
    coupling, stack = couple(slices, gains, w_layer, out_layer, last, [mask, places, xz])
    others = [shifted(coupling, r) for r in range(1, sections)]

    streams = stream_columns(width // CHUNKS)

    def facing(array, by):
        return lax.ppermute(array, "section", [(i, i ^ by) for i in range(sections)])

    arrays, masks, by = [hold(xz, others)], [0], sections // 2
    while by > 0:
        arrays = arrays + [facing(array, by) for array in arrays]
        masks = masks + [mask_of ^ by for mask_of in masks]
        by = by // 2
    xz_all = [arrays[masks.index(r)] for r in range(sections)]
    early = [xz_all[r] for r in range(1, sections) if r & (r - 1) == 0]
    late = [xz_all[r] for r in range(1, sections) if r & (r - 1) != 0]
    pieces = [compact([coupling] + others, layer, 3 * head, head, [xz])]

    rows = [stack[None]]
    for step in range(bits):
        if step > 0:
            pieces = [merge(*pieces, early)]
        pieces = pieces + [swapped(pieces[0], step)]
        if step == bits - 1:
            pieces[-1] = hold(pieces[-1], late)
        if step > 0:
            rows = [gather_two(*rows, pieces[-1:])]
        rows = rows + [swapped(rows[0], step)]
    pieces = pieces + [handed(array, r) for r in range(1, groups) for array in pieces]
    sent, total, mixes, *leaving = serial(
        xz_all, pieces, places, norms, mask, layer, gains, w_layer, out_layer, streams
    )
    back, pair = widen(sent, gains, w_layer, out_layer, width // CHUNKS)

    down = [(i, i - 1) for i in range(1, sections)]
    behind = sections - 1 - section

    def index(tick):
        return jnp.clip(tick - behind, 0, CHUNKS - 1).astype(jnp.int32)[None]

    def lowered(arrays):
        return [lax.ppermute(array, "section", down) for array in arrays]

    ticks = CHUNKS + sections - 1
    after = {}
    for tick in range(1, ticks):
        arrived = lowered(leaving)
        if tick < ticks - 1:
            for i, cols in enumerate(streams):
                waits = after.get(tick, []) if tick < ticks - 2 or i == STREAMS - 1 else []
                leaving[i], pair = join(index(tick), arrived[i], pair, cols, waits)
        if tick == 1:
            rows = [hold(array, leaving) for array in rows]
            rows = rows + [handed(array, r) for r in range(1, groups) for array in rows]
            rests, halves = [], []
            for part in range(PARTS):
                rest, half = settle(
                    total, mixes, rows, places, x, cotangent, back, width // CHUNKS, part, PARTS
                )
                rests.append(rest)
                halves.append(half)
            sums = [stacked(halves)]
            for step in range(bits):
                sums.append(added([sums[-1], swapped(sums[-1], step)]))
            sums.append(added(sums[-1:] + [handed(sums[-1], r) for r in range(1, groups)]))
            gain_whole = sums[-1].reshape(1, width)
            after = {2 + i: [array] for i, array in enumerate(sums)}
    out = finish(index(ticks - 1), arrived, pair, rests, streams)
    return (out[None], gain_whole)


def attend(hidden, segment, gain_row, w_layer, out_layer):
    count, length, width = hidden.shape
    head = out_layer.shape[0]
    scaled = hidden * lax.rsqrt(jnp.mean(hidden * hidden, axis=-1, keepdims=True) + EPS) * gain_row
    normed = scaled.astype(BF16).reshape(count * length, width)
    projected = jnp.dot(normed, w_layer, preferred_element_type=F32).reshape(count, length, 3 * head)
    query = projected[:, :, :head]
    keyed = projected[:, :, head : 2 * head]
    valued = projected[:, :, 2 * head :]
    positions = jnp.arange(length)
    allowed = (positions[:, None] >= positions[None, :])[None] & (
        segment[:, :, None] == segment[:, None, :]
    )
    scores = jnp.einsum("rid,rjd->rij", query, keyed, precision=lax.Precision.HIGHEST)
    scores = jnp.where(allowed, scores / math.sqrt(head), -1e30)
    weights = jax.nn.softmax(scores, axis=-1)
    mixed = jnp.einsum("rij,rjd->rid", weights, valued, precision=lax.Precision.HIGHEST)
    mixed = mixed.astype(BF16).reshape(count * length, head)
    output = jnp.dot(mixed, out_layer, preferred_element_type=F32).reshape(count, length, width)
    return hidden + output


MB_ROWS = 2


def relay(tokens_in, cotangent, gains, w_qkv, w_out, segments, plan):
    sections = lax.axis_size("section")
    section = lax.axis_index("section")
    rows_dev = plan.shape[1]
    width = tokens_in.shape[1]
    length = segments.shape[1]
    micro = rows_dev // MB_ROWS
    blocks = tokens_in.reshape(rows_dev, length, width)
    chosen = jnp.take(blocks, plan[0], axis=0)
    chosen_seg = jnp.take(segments, plan[0], axis=0).astype(BF16)
    assigned = lax.all_to_all(chosen, "group", split_axis=0, concat_axis=0, tiled=True)
    moved_seg = lax.all_to_all(chosen_seg, "group", split_axis=0, concat_axis=0, tiled=True)
    assigned = assigned.reshape(micro, MB_ROWS, length, width)
    seg_groups = moved_seg.reshape(micro, MB_ROWS, length)
    gain_row, w_layer, out_layer = gains[0], w_qkv[0], w_out[0]
    grad_rows = cotangent.reshape(micro, MB_ROWS, length, width)
    ticks = micro + sections - 1

    def passed_along(array, by):
        pairs = [(i, i + by) for i in range(sections) if 0 <= i + by < sections]
        return lax.ppermute(array, "section", pairs)

    def at(array, i):
        return lax.dynamic_index_in_dim(array, i, 0, keepdims=False)

    def forward_tick(tick, carry):
        saved, arrived = carry
        index = tick - section
        valid = (index >= 0) & (index < micro)
        clipped = jnp.clip(index, 0, micro - 1)
        entering = jnp.where(section == 0, at(assigned, clipped), arrived)
        kept = jnp.where(valid, entering, at(saved, clipped))
        saved = lax.dynamic_update_index_in_dim(saved, kept, clipped, 0)
        segment = at(seg_groups, clipped)

        def run_layer(value):
            return attend(value.astype(F32), segment, gain_row, w_layer, out_layer).astype(BF16)

        leaving = lax.cond(valid, run_layer, jnp.zeros_like, entering)
        return (saved, passed_along(leaving, 1))

    saved_init = jnp.zeros((micro, MB_ROWS, length, width), BF16)
    arrive_init = jnp.zeros((MB_ROWS, length, width), BF16)
    saved, _ = lax.fori_loop(0, ticks, forward_tick, (saved_init, arrive_init))

    def backward_tick(tick, carry):
        grads_x, gain_total, arrived = carry
        index = tick - (sections - 1 - section)
        valid = (index >= 0) & (index < micro)
        clipped = jnp.clip(index, 0, micro - 1)
        entering = jnp.where(section == sections - 1, at(grad_rows, clipped), arrived)
        segment = at(seg_groups, clipped)
        stored = at(saved, clipped).astype(F32)

        def local_layer(hidden, gains_here):
            return attend(hidden, segment, gains_here, w_layer, out_layer)

        def run_back(value):
            _, pullback = jax.vjp(local_layer, stored, gain_row)
            grad_hidden, grad_gain = pullback(value.astype(F32))
            return (grad_hidden.astype(BF16), grad_gain)

        def skip_back(value):
            return (jnp.zeros_like(value), jnp.zeros(gain_row.shape, F32))

        sending, grad_gain = lax.cond(valid, run_back, skip_back, entering)
        kept = jnp.where(valid, sending, at(grads_x, clipped))
        grads_x = lax.dynamic_update_index_in_dim(grads_x, kept, clipped, 0)
        return (grads_x, gain_total + grad_gain, passed_along(sending, -1))

    gain_init = jnp.zeros(gain_row.shape, F32)
    grads_x, gain_total, _ = lax.fori_loop(
        0, ticks, backward_tick, (saved_init, gain_init, arrive_init)
    )
    gain_whole = lax.psum(gain_total, ("dp", "group"))
    return (grads_x.reshape(1, rows_dev * length, width), gain_whole[None])


def solution(mesh):
    placed = (
        P(("dp", "group"), None),
        P(("dp", "group"), None),
        P("section", None),
        P("section", None, None),
        P("section", None, None),
        P(("dp", "group"), None),
        P(("dp", "group"), None),
    )

    def chosen(tokens_in, cotangent, gains, w_qkv, w_out, segments, plan):
        sections, head, width = w_out.shape
        devices = mesh.shape["dp"]
        small = sections * 4 * head < width and sections > 1
        halves = devices & (devices - 1) == 0 and sections & (sections - 1) == 0
        body = local if small and halves else relay
        return jax.shard_map(
            body,
            mesh=mesh,
            in_specs=placed,
            out_specs=(P("section", ("dp", "group"), None), P("section", None)),
            check_vma=False,
        )(tokens_in, cotangent, gains, w_qkv, w_out, segments, plan)

    return chosen
```

```python
import math

import jax
import jax.numpy as jnp
from jax import lax
from jax.experimental import pallas as pl
from jax.experimental.pallas import tpu as pltpu
from jax.sharding import PartitionSpec as P

EPS = 1e-05
VMEM_BYTES = 24 * 1024 * 1024
SMALL = 16 * 1024 * 1024
F32 = jnp.float32
BF16 = jnp.bfloat16


def dot_nn(a, b):
    return lax.dot_general(a, b, (((1,), (0,)), ((), ())), preferred_element_type=F32)


def dot_nt(a, b):
    return lax.dot_general(a, b, (((1,), (1,)), ((), ())), preferred_element_type=F32)


def dot_tn(a, b):
    return lax.dot_general(a, b, (((0,), (0,)), ((), ())), preferred_element_type=F32)


IN_HBM = pl.BlockSpec(memory_space=pltpu.HBM)
ANYWHERE = pl.BlockSpec(memory_space=pl.ANY)
IN_VMEM = pl.BlockSpec(memory_space=pltpu.VMEM)
IN_SMEM = pl.BlockSpec(memory_space=pltpu.SMEM)


def in_hbm(array):
    return pltpu.with_memory_space_constraint(array, pltpu.HBM)


def in_vmem(array):
    return pltpu.with_memory_space_constraint(array, pltpu.VMEM)


def mover(sems):
    used = []

    def start(source, target):
        copy = pltpu.make_async_copy(source, target, sems.at[len(used)])
        copy.start()
        used.append(copy)
        return copy

    return start


def steps(width):
    step = min(width, 1024)
    return [slice(at, at + step) for at in range(0, width, step)]


def params(limit=VMEM_BYTES):
    return pltpu.CompilerParams(vmem_limit_bytes=limit)


def pick(tokens, plan, place, groups, out_layer, mine, slice_rows):
    rows, length, width = tokens.shape
    share = rows // groups

    def kernel(plan_ref, place_ref, mine_ref, tokens_ref, o_ref, *rest):
        slice_ref, parts = rest[0], rest[1 : 1 + groups]
        slice_in, rows_in, sems = rest[1 + groups :]
        start = mover(sems)
        at = pl.ds(pl.multiple_of(mine_ref[0] * slice_rows, slice_rows), slice_rows)
        loads = [(start(o_ref.at[at], slice_in), slice_in, slice_ref)]
        for r in range(groups):
            target = lax.rem(place_ref[0] + r, groups)
            for c in range(share):
                here = rows_in.at[r * share + c]
                row = plan_ref[0, target * share + c]
                loads.append((start(tokens_ref.at[row], here), here, parts[r].at[c]))
        stores = []
        for load, here, there in loads:
            load.wait()
            stores.append(start(here, there))
        for store in stores:
            store.wait()

    return pl.pallas_call(
        kernel,
        out_shape=[pltpu.HBM((slice_rows, width), BF16)]
        + [pltpu.HBM((share, length, width), BF16)] * groups,
        in_specs=[IN_SMEM, IN_SMEM, IN_SMEM, IN_HBM, IN_HBM],
        out_specs=[IN_HBM] * (1 + groups),
        scratch_shapes=[
            pltpu.VMEM((slice_rows, width), BF16),
            pltpu.VMEM((rows, length, width), BF16),
            pltpu.SemaphoreType.DMA((2 * rows + 2,)),
        ],
        compiler_params=params(),
        name="pick",
    )(plan, place, mine, in_hbm(tokens), in_hbm(out_layer))


def project(parts, cotangent, gain, w_layer, out_layer, place, after):
    groups = len(parts)
    tokens, width = cotangent.shape
    head = out_layer.shape[0]
    wide = w_layer.shape[1]
    block = tokens // groups
    cuts = steps(width)
    copies = len(cuts) * (groups + 4)

    def kernel(place_ref, *refs):
        part_refs = refs[:groups]
        cot_ref, g_ref, w_ref, o_ref = refs[groups : groups + 4]
        x_ref, xz_ref, n_ref = refs[groups + 4 + len(after) : groups + 7 + len(after)]
        x_in, c_in, w_in, o_in, sems = refs[groups + 7 + len(after) :]
        start = mover(sems)
        loads = []
        for cut in cuts:
            mine = [start(w_ref.at[cut], w_in.at[cut])]
            mine.append(start(o_ref.at[:, cut], o_in.at[:, cut]))
            for r in range(groups):
                source = lax.rem(place_ref[0] + groups - r, groups)
                rows = pl.ds(pl.multiple_of(source * block, block), block)
                mine.append(start(part_refs[r].at[:, cut], x_in.at[rows, cut]))
            mine.append(start(cot_ref.at[:, cut], c_in.at[:, cut]))
            loads.append(mine)
        through = jnp.zeros((tokens, wide), F32)
        across = jnp.zeros((tokens, head), F32)
        back = jnp.zeros((tokens, head), F32)
        square = jnp.zeros((tokens, 1), F32)
        stores = []
        for cut, mine in zip(cuts, loads):
            for load in mine:
                load.wait()
            stores.append(start(x_in.at[:, cut], x_ref.at[:, cut]))
            x = x_in[:, cut]
            xf = x.astype(F32)
            through += dot_nn((xf * g_ref[:, cut]).astype(BF16), w_in[cut, :])
            across += dot_nt(x, o_in[:, cut])
            back += dot_nt(c_in[:, cut], o_in[:, cut])
            square += jnp.sum(xf * xf, axis=1, keepdims=True)
        xz_ref[:, :wide] = through.astype(BF16)
        xz_ref[:, wide : wide + head] = across.astype(BF16)
        xz_ref[:, wide + head :] = back.astype(BF16)
        n_ref[...] = square
        for store in stores:
            store.wait()

    return pl.pallas_call(
        kernel,
        out_shape=[
            pltpu.HBM((tokens, width), BF16),
            jax.ShapeDtypeStruct((tokens, wide + 2 * head), BF16),
            jax.ShapeDtypeStruct((tokens, 1), F32),
        ],
        in_specs=[IN_SMEM]
        + [ANYWHERE] * groups
        + [IN_HBM, IN_VMEM, IN_HBM, IN_HBM]
        + [ANYWHERE] * len(after),
        out_specs=[IN_HBM, IN_VMEM, IN_VMEM],
        scratch_shapes=[
            pltpu.VMEM((tokens, width), BF16),
            pltpu.VMEM((tokens, width), BF16),
            pltpu.VMEM((width, wide), BF16),
            pltpu.VMEM((head, width), BF16),
            pltpu.SemaphoreType.DMA((copies,)),
        ],
        compiler_params=params(),
        name="project",
    )(
        place,
        in_hbm(parts[0]),
        *[in_vmem(part) for part in parts[1:]],
        in_hbm(cotangent),
        gain,
        in_hbm(w_layer),
        in_hbm(out_layer),
        *after,
    )


def couple(slices, gain, w_layer, out_layer, last, after):
    sections = len(slices)
    count, width = slices[0].shape
    head = out_layer.shape[0]
    wide = w_layer.shape[1]
    below = (sections - 2) * wide
    packed = below + max(wide, (sections - 1) * head)
    cuts = steps(width)
    copies = len(cuts) * (sections + 2) + sections - 1

    def kernel(last_ref, *refs):
        s_refs = refs[:sections][::-1]
        g_ref, w_ref, o_ref = refs[sections : sections + 3]
        out_ref, stack_ref, r_in, w_in, o_in, sems = refs[sections + 3 + len(after) :]
        rows = [slice(r * count, (r + 1) * count) for r in range(sections)]
        start = mover(sems)
        loads = []
        for cut in cuts:
            mine = [start(w_ref.at[cut], w_in.at[cut])]
            mine.append(start(o_ref.at[:, cut], o_in.at[:, cut]))
            for r in range(sections):
                mine.append(start(s_refs[r].at[:, cut], r_in.at[rows[r], cut]))
            loads.append(mine)
        through = jnp.zeros((sections * count, wide), F32)
        across = jnp.zeros((sections * count, head), F32)
        for cut, mine in zip(cuts, loads):
            for load in mine:
                load.wait()
            r = r_in[:, cut]
            through += dot_nn((r.astype(F32) * g_ref[:, cut]).astype(BF16), w_in[cut, :])
            across += dot_nt(r, o_in[:, cut])
        stores = [start(r_in.at[rows[r]], stack_ref.at[r - 1]) for r in range(1, sections)]
        through = through.astype(BF16)
        across = across.astype(BF16)
        out_ref[...] = jnp.zeros_like(out_ref)
        for r in range(1, sections - 1):
            out_ref[:, (r - 1) * wide : r * wide] = through[rows[r]]

        @pl.when(last_ref[0] == 1)
        def _():
            out_ref[:, below : below + wide] = through[rows[-1]]

        @pl.when(last_ref[0] == 0)
        def _():
            for r in range(sections - 1):
                out_ref[:, below + r * head : below + (r + 1) * head] = across[rows[r]]

        for store in stores:
            store.wait()

    return pl.pallas_call(
        kernel,
        out_shape=[
            jax.ShapeDtypeStruct((count, packed), BF16),
            pltpu.HBM((sections - 1, count, width), BF16),
        ],
        in_specs=[IN_SMEM]
        + [ANYWHERE] * sections
        + [IN_VMEM, IN_HBM, IN_HBM]
        + [ANYWHERE] * len(after),
        out_specs=[IN_VMEM, IN_HBM],
        scratch_shapes=[
            pltpu.VMEM((sections * count, width), BF16),
            pltpu.VMEM((width, wide), BF16),
            pltpu.VMEM((head, width), BF16),
            pltpu.SemaphoreType.DMA((copies,)),
        ],
        compiler_params=params(),
        name="couple",
    )(last, *slices[::-1], gain, in_hbm(w_layer), in_hbm(out_layer), *after)


def layout(sections, wide, head):
    through, across, spans, at = {}, {}, {}, 0
    for j in range(sections - 1):
        begin = at
        across[j, j] = slice(at, at + head)
        at += head
        for k in range(j + 1, sections):
            through[j, k] = slice(at, at + wide)
            at += wide
            if k < sections - 1:
                across[j, k] = slice(at, at + head)
                at += head
        spans[j] = slice(begin, at)
    return through, across, spans, at


def compact(parts, section, wide, head, after):
    sections = len(parts)
    count = parts[0].shape[0]
    below = (sections - 2) * wide
    through, across, _, total = layout(sections, wide, head)

    def kernel(s_ref, *refs):
        part_refs, out_ref = refs[:sections], refs[-1]
        mine = s_ref[0]

        def fill(k, r):
            for j in range(k):
                at = (k - j - 1) * wide
                out_ref[0, :, through[j, k]] = part_refs[r][:, at : at + wide]
            for j in range(k + 1 if k < sections - 1 else 0):
                at = below + (k - j) * head
                out_ref[0, :, across[j, k]] = part_refs[r][:, at : at + head]

        for s in range(sections):

            @pl.when(mine == s)
            def _(s=s):
                for r in range(sections):
                    fill((s - r) % sections, r)

    vmem = pl.BlockSpec(memory_space=pltpu.VMEM)
    return pl.pallas_call(
        kernel,
        out_shape=jax.ShapeDtypeStruct((1, count, total), BF16),
        in_specs=[IN_SMEM] + [vmem] * sections + [ANYWHERE] * len(after),
        out_specs=vmem,
        compiler_params=params(SMALL),
        name="compact",
    )(section, *parts, *after)


def merge(first, second, after):
    count = first.shape[0]

    def kernel(first_ref, second_ref, *refs):
        refs[-1][:count] = first_ref[...]
        refs[-1][count:] = second_ref[...]

    return pl.pallas_call(
        kernel,
        out_shape=jax.ShapeDtypeStruct((2 * count,) + first.shape[1:], first.dtype),
        in_specs=[IN_VMEM] * 2 + [ANYWHERE] * len(after),
        out_specs=IN_VMEM,
        compiler_params=params(SMALL),
        name="merge",
    )(first, second, *after)


def serial(xz, pieces, places, norms, mask, section, gain, w_layer, out_layer, streams):
    sections = len(xz)
    tokens = norms.shape[0]
    head, width = out_layer.shape
    wide = 3 * head
    scale = 1.0 / math.sqrt(head)
    lead = slice(0, streams[-1].stop)
    through_at, across_at, spans, _ = layout(sections, wide, head)
    count, packed = pieces[0].shape[-2:]
    plane = head // count
    n_in = sections + len(pieces)
    copies = sections + plane + 2

    def kernel(s_ref, p_ref, *refs):
        xz_refs, piece_refs = refs[:sections], refs[sections:n_in]
        n_ref, mask_ref, g_ref, w_ref, o_ref = refs[n_in : n_in + 5]
        n_out = n_in + 5
        v_ref, t_ref, a_ref = refs[n_out : n_out + 3]
        first_refs = refs[n_out + 3 : n_out + 3 + len(streams)]
        scratch = refs[n_out + 3 + len(streams) :]
        xz_all, table, mixes, weights, projs, dmix, w_in, o_in, sems = scratch
        mine = s_ref[0]
        started = []

        def start(source, target):
            copy = pltpu.make_async_copy(source, target, sems.at[len(started)])
            copy.start()
            started.append(copy)

        for r in range(sections):
            start(xz_refs[r], xz_all.at[mine ^ r])
        at = 0
        for ref in piece_refs:
            for i in range(ref.shape[0]):
                start(ref.at[i], table.at[p_ref[at]])
                at += 1
        small = list(started)
        start(w_ref.at[lead], w_in)
        start(o_ref.at[:, lead], o_in)
        for copy in small:
            copy.wait()

        def couplings(cols):
            return table[:, :, cols].reshape(head, cols.stop - cols.start)

        allowed = mask_ref[...] > 0.5
        norm = n_ref[...]
        rstds, tails = [], []
        projected = [xz_all[s, :, :wide].astype(F32) for s in range(sections)]
        crossed = [xz_all[s, :, wide : wide + head].astype(F32) for s in range(sections - 1)]
        for s in range(sections):
            proj = projected[s]
            rstd = lax.rsqrt(norm * (1.0 / width) + EPS)
            proj = proj * rstd
            projs[s] = proj.astype(BF16)
            q, k, v = (projs[s, :, i * head : (i + 1) * head] for i in range(3))
            scores = jnp.where(allowed, dot_nt(q, k) * scale, -1e30)
            scores = jnp.exp(scores - jnp.max(scores, axis=1, keepdims=True))
            soft = scores / jnp.sum(scores, axis=1, keepdims=True)
            weights[s] = soft
            mix = dot_nn(soft.astype(BF16), v).astype(BF16)
            mixes[:, s * head : (s + 1) * head] = mix
            rstds.append(rstd)
            dmix[:, s * head : (s + 1) * head] = xz_all[s, :, wide + head :].astype(F32)
            if s == sections - 1:
                break
            added_on = dot_nn(mix, couplings(spans[s]))

            def part(cols, added_on=added_on, begin=spans[s].start):
                return added_on[:, cols.start - begin : cols.stop - begin]

            for k in range(s + 1, sections):
                projected[k] = projected[k] + part(through_at[s, k])
                if k < sections - 1:
                    crossed[k] = crossed[k] + part(across_at[s, k])
            y = crossed[s]
            tail = y + part(across_at[s, s])
            norm = norm + jnp.sum(mix.astype(F32) * (y + tail), axis=1, keepdims=True)
            norm = jnp.maximum(norm, 0.0)
            tails.append(tail)
        total = jnp.zeros((tokens, 1), F32)
        a_ref[...] = jnp.zeros_like(a_ref)
        for s in reversed(range(sections)):
            cols = slice(s * head, (s + 1) * head)
            da = dmix[:, cols]
            if s < sections - 1:
                da = da - total * tails[s]
            da = da.astype(BF16)
            q, k, v = (projs[s, :, i * head : (i + 1) * head] for i in range(3))
            soft = weights[s]
            dv = dot_tn(soft.astype(BF16), da)
            dsoft = dot_nt(da, v)
            dscore = soft * (dsoft - jnp.sum(dsoft * soft, axis=1, keepdims=True))
            dscore = (dscore * scale).astype(BF16)
            dproj = jnp.concatenate([dot_nn(dscore, k), dot_tn(dscore, q), dv], axis=1)
            along = jnp.sum(dproj * projs[s].astype(F32), axis=1, keepdims=True)
            first = (dproj * rstds[s]).astype(BF16)
            second = (-total * mixes[:, cols].astype(F32)).astype(BF16)
            total = total + rstds[s] * rstds[s] * along * (1.0 / width)
            for j in reversed(range(s)):
                cols = through_at[j, s]
                if s < sections - 1:
                    both = jnp.concatenate([first, second], axis=1)
                    term = dot_nt(both, couplings(slice(cols.start, across_at[j, s].stop)))
                else:
                    term = dot_nt(first, couplings(cols))
                dmix[:, j * head : (j + 1) * head] += term

            @pl.when(mine == s)
            def _(first=first, second=second, total=total):
                v_ref[:, :wide] = first
                v_ref[:, wide:] = second
                t_ref[...] = total

            for r in range(1, sections - s):

                @pl.when(mine == s + r)
                def _(r=r, s=s):
                    a_ref[:, (r - 1) * head : r * head] = mixes[:, s * head : (s + 1) * head]

        for copy in started[len(small) :]:
            copy.wait()
        own = dot_nt(v_ref[:, :wide], w_in[...]) * g_ref[:, lead]
        own = (own + dot_nn(v_ref[:, wide:], o_in[...])).astype(BF16)
        for ref, part in zip(first_refs, streams):
            ref[...] = own[:, part]

    vmem = pl.BlockSpec(memory_space=pltpu.VMEM)
    smem = pl.BlockSpec(memory_space=pltpu.SMEM)
    return pl.pallas_call(
        kernel,
        out_shape=[
            pltpu.VMEM((tokens, wide + head), BF16),
            pltpu.VMEM((tokens, 1), F32),
            pltpu.VMEM((tokens, (sections - 1) * head), BF16),
        ]
        + [pltpu.VMEM((tokens, part.stop - part.start), BF16) for part in streams],
        in_specs=[smem, smem] + [ANYWHERE] * n_in + [vmem, vmem, vmem, IN_HBM, IN_HBM],
        out_specs=[vmem] * (3 + len(streams)),
        scratch_shapes=[
            pltpu.VMEM((sections,) + xz[0].shape, BF16),
            pltpu.VMEM((plane, count, packed), BF16),
            pltpu.VMEM((tokens, sections * head), BF16),
            pltpu.VMEM((sections, tokens, tokens), F32),
            pltpu.VMEM((sections, tokens, wide), BF16),
            pltpu.VMEM((tokens, sections * head), F32),
            pltpu.VMEM((lead.stop, wide), BF16),
            pltpu.VMEM((head, lead.stop), BF16),
            pltpu.SemaphoreType.DMA((copies,)),
        ],
        compiler_params=params(),
        name="serial",
    )(
        section,
        places,
        *xz,
        *pieces,
        norms,
        mask,
        gain,
        in_hbm(w_layer),
        in_hbm(out_layer),
    )


def hold(array, after):
    def kernel(*refs):
        pass

    return pl.pallas_call(
        kernel,
        out_shape=jax.ShapeDtypeStruct(array.shape, array.dtype),
        in_specs=[ANYWHERE] * (1 + len(after)),
        out_specs=ANYWHERE,
        input_output_aliases={0: 0},
        compiler_params=params(SMALL),
        name="hold",
    )(array, *after)


def gather_two(first, second, after):
    count = first.shape[0]

    def kernel(first_ref, second_ref, *refs):
        out_ref, sems = refs[len(after) :]
        start = mover(sems)
        copies = [start(first_ref, out_ref.at[:count]), start(second_ref, out_ref.at[count:])]
        for copy in copies:
            copy.wait()

    return pl.pallas_call(
        kernel,
        out_shape=jax.ShapeDtypeStruct((2 * count,) + first.shape[1:], first.dtype),
        in_specs=[ANYWHERE] * (2 + len(after)),
        out_specs=IN_VMEM,
        scratch_shapes=[pltpu.SemaphoreType.DMA((2,))],
        compiler_params=params(SMALL),
        name="gather_two",
    )(first, second, *after)


def widen(sent, gain, w_layer, out_layer, chunk):
    tokens = sent.shape[0]
    head, width = out_layer.shape
    wide = w_layer.shape[1]
    cuts = [slice(at, at + chunk) for at in range(0, width, chunk)]

    def kernel(v_ref, g_ref, w_ref, o_ref, back_ref, pair_ref, back_in, w_in, o_in, sems):
        start = mover(sems)
        loads = [
            (start(w_ref.at[cut], w_in.at[cut]), start(o_ref.at[:, cut], o_in.at[:, cut]))
            for cut in cuts
        ]
        stores = []
        for i, (cut, mine) in enumerate(zip(cuts, loads)):
            for load in mine:
                load.wait()
            back = dot_nt(v_ref[:, :wide], w_in[cut, :])
            own = back * g_ref[:, cut] + dot_nn(v_ref[:, wide:], o_in[:, cut])
            back_in[:, cut] = back.astype(BF16)
            stores.append(start(back_in.at[:, cut], back_ref.at[:, cut]))
            pair_ref[0, i] = own.astype(BF16)
            pair_ref[1, i] = jnp.zeros_like(pair_ref[1, i])
        for store in stores:
            store.wait()

    return pl.pallas_call(
        kernel,
        out_shape=[
            pltpu.HBM((tokens, width), BF16),
            pltpu.VMEM((2, len(cuts), tokens, chunk), BF16),
        ],
        in_specs=[IN_VMEM, IN_VMEM, IN_HBM, IN_HBM],
        out_specs=[IN_HBM, IN_VMEM],
        scratch_shapes=[
            pltpu.VMEM((tokens, width), BF16),
            pltpu.VMEM((width, wide), BF16),
            pltpu.VMEM((head, width), BF16),
            pltpu.SemaphoreType.DMA((3 * len(cuts),)),
        ],
        compiler_params=params(),
        name="widen",
    )(in_vmem(sent), gain, in_hbm(w_layer), in_hbm(out_layer))


def settle(total, mixes, stacks, places, x, cotangent, back, chunk, part, parts):
    tokens, width = x.shape
    layers, rows = stacks[0].shape[1:3]
    entries = [(i, e) for i, stack in enumerate(stacks) for e in range(stack.shape[0])]
    plane = len(entries)
    head = plane * rows
    span = width // parts
    base = part * span
    cuts = [slice(at, at + chunk) for at in range(0, span, chunk)]
    copies = plane * layers + 3 * len(cuts)

    def kernel(p_ref, t_ref, a_ref, x_ref, c_ref, back_ref, *refs):
        stack_refs = refs[: len(stacks)]
        rest_ref, dg_ref = refs[len(stacks) : len(stacks) + 2]
        lower, x_in, c_in, back_in, sems = refs[len(stacks) + 2 :]
        start = mover(sems)
        first = []
        for at, (i, e) in enumerate(entries):
            for r in range(layers):
                here = pl.ds(base, span)
                first.append(start(stack_refs[i].at[e, r, :, here], lower.at[r, p_ref[at]]))
        loads = []
        for cut in cuts:
            there = pl.ds(base + cut.start, chunk)
            mine = [start(x_ref.at[:, there], x_in.at[:, cut])]
            mine.append(start(c_ref.at[:, there], c_in.at[:, cut]))
            mine.append(start(back_ref.at[:, there], back_in.at[:, cut]))
            loads.append(mine)
        for load in first:
            load.wait()
        for i, (cut, mine) in enumerate(zip(cuts, loads)):
            for load in mine:
                load.wait()
            below = lower[:, :, :, cut].reshape(layers * head, chunk)
            here = x_in[:, cut].astype(F32) + dot_nn(a_ref[...], below)
            rest_ref[i] = (c_in[:, cut].astype(F32) - t_ref[...] * here).astype(BF16)
            gain = jnp.sum(back_in[:, cut].astype(F32) * here, axis=0, keepdims=True)
            for at in range(0, chunk, head):
                row = (cut.start + at) // head
                dg_ref[row : row + 1, :] = gain[:, at : at + head]

    return pl.pallas_call(
        kernel,
        out_shape=[
            pltpu.VMEM((len(cuts), tokens, chunk), BF16),
            pltpu.VMEM((span // head, head), F32),
        ],
        in_specs=[IN_SMEM] + [IN_VMEM] * 2 + [IN_HBM] * (3 + len(stacks)),
        out_specs=[IN_VMEM] * 2,
        scratch_shapes=[
            pltpu.VMEM((layers, plane, rows, span), BF16),
            pltpu.VMEM((tokens, span), BF16),
            pltpu.VMEM((tokens, span), BF16),
            pltpu.VMEM((tokens, span), BF16),
            pltpu.SemaphoreType.DMA((copies,)),
        ],
        compiler_params=params(),
        name="settle",
    )(
        places,
        in_vmem(total),
        in_vmem(mixes),
        *[in_hbm(array) for array in (x, cotangent, back, *stacks)],
    )


def join(index, arrived, pair, cols, after):
    tokens, part = arrived.shape

    def kernel(i_ref, r_ref, _, *refs):
        send_ref, pair_ref = refs[len(after) :]
        at = i_ref[0]
        r = r_ref[...]
        send_ref[...] = (pair_ref[0, at, :, cols].astype(F32) + r.astype(F32)).astype(BF16)
        pair_ref[1, at, :, cols] = r

    return pl.pallas_call(
        kernel,
        out_shape=[pltpu.VMEM((tokens, part), BF16), pltpu.VMEM(pair.shape, BF16)],
        in_specs=[IN_SMEM] + [IN_VMEM] * 2 + [ANYWHERE] * len(after),
        out_specs=[IN_VMEM] * 2,
        input_output_aliases={2: 1},
        compiler_params=params(SMALL),
        name="join",
    )(index, in_vmem(arrived), in_vmem(pair), *after)


def finish(index, arrived, pair, rests, streams):
    _, count, tokens, chunk = pair.shape

    def kernel(i_ref, *refs):
        r_refs = refs[: len(streams)]
        pair_ref, rest_refs = refs[len(streams)], refs[len(streams) + 1 :][: len(rests)]
        whole_ref, whole, sems = refs[len(streams) + 1 + len(rests) :]
        each = count // len(rests)
        at = i_ref[0]
        copies = []
        for i in range(count):
            full = rest_refs[i // each][i % each].astype(F32) + pair_ref[0, i].astype(F32)
            whole[i] = (full + pair_ref[1, i].astype(F32)).astype(BF16)

            @pl.when(at == i)
            def _(i=i, full=full):
                for ref, cols in zip(r_refs, streams):
                    whole[i, :, cols] = (full[:, cols] + ref[...].astype(F32)).astype(BF16)

            there = whole_ref.at[:, pl.ds(i * chunk, chunk)]
            copies.append(pltpu.make_async_copy(whole.at[i], there, sems.at[i]))
            copies[-1].start()
        for copy in copies:
            copy.wait()

    return pl.pallas_call(
        kernel,
        out_shape=pltpu.HBM((tokens, count * chunk), BF16),
        in_specs=[IN_SMEM] + [IN_VMEM] * (len(streams) + 1 + len(rests)),
        out_specs=IN_HBM,
        scratch_shapes=[
            pltpu.VMEM((count, tokens, chunk), BF16),
            pltpu.SemaphoreType.DMA((count,)),
        ],
        compiler_params=params(SMALL),
        name="finish",
    )(index, *[in_vmem(array) for array in (*arrived, pair, *rests)])


def stacked(arrays):
    rows = arrays[0].shape[0]

    def kernel(*refs):
        for i, ref in enumerate(refs[:-1]):
            refs[-1][i * rows : (i + 1) * rows, :] = ref[...]

    return pl.pallas_call(
        kernel,
        out_shape=pltpu.VMEM((len(arrays) * rows, arrays[0].shape[1]), F32),
        in_specs=[IN_VMEM] * len(arrays),
        out_specs=IN_VMEM,
        compiler_params=params(SMALL),
        name="stacked",
    )(*[in_vmem(array) for array in arrays])


def added(arrays):
    def kernel(*refs):
        total = refs[0][...]
        for ref in refs[1:-1]:
            total = total + ref[...]
        refs[-1][...] = total

    return pl.pallas_call(
        kernel,
        out_shape=pltpu.VMEM(arrays[0].shape, F32),
        in_specs=[IN_VMEM] * len(arrays),
        out_specs=IN_VMEM,
        compiler_params=params(SMALL),
        name="added",
    )(*[in_vmem(array) for array in arrays])


STREAMS = 2
CHUNKS = 4
PARTS = 1


def stream_columns(chunk):
    lanes = 128
    tiles = chunk // lanes
    ends = [-(-tiles * (i + 1) // STREAMS) * lanes for i in range(STREAMS)]
    return [slice(start, end) for start, end in zip([0] + ends, ends)]


def shifted(array, by):
    sections = lax.axis_size("section")
    return lax.ppermute(array, "section", [(i, (i + by) % sections) for i in range(sections)])


def raised(array, by):
    sections = lax.axis_size("section")
    return lax.ppermute(array, "section", [(i, i + by) for i in range(sections - by)])


def swapped(array, step):
    groups = lax.axis_size("group")
    devices = lax.axis_size("dp")
    bits = devices.bit_length() - 1
    pairs = []
    for p in range(devices):
        for g in range(groups):
            pairs.append((p * groups + g, (p ^ (1 << ((step + g) % bits))) * groups + g))
    return lax.ppermute(array, ("dp", "group"), pairs)


def handed(array, by):
    groups = lax.axis_size("group")
    return lax.ppermute(array, "group", [(i, (i + by) % groups) for i in range(groups)])


def plane_places():
    groups = lax.axis_size("group")
    bits = lax.axis_size("dp").bit_length() - 1
    masks = []
    for g in range(groups):
        order = [0]
        for step in range(bits):
            order = order + [m ^ (1 << ((step + g) % bits)) for m in order]
        masks.append(order)
    masks = jnp.asarray(masks, jnp.int32)
    dp, member = lax.axis_index("dp"), lax.axis_index("group")
    places = []
    for r in range(groups):
        giver = (member + groups - r) % groups
        places.append((dp ^ masks[giver]) * groups + giver)
    return jnp.concatenate(places).astype(jnp.int32)


def local(tokens_in, cotangent, gains, w_qkv, w_out, segments, plan):
    sections = lax.axis_size("section")
    groups = lax.axis_size("group")
    devices = lax.axis_size("dp")
    plane = devices * groups
    section = lax.axis_index("section")
    member = lax.axis_index("group")
    rows_dev = plan.shape[1]
    length = segments.shape[1]
    tokens, width = tokens_in.shape
    head = w_out.shape[1]
    share = rows_dev // groups
    w_layer, out_layer = w_qkv[0], w_out[0]
    place = member.astype(jnp.int32)[None]
    layer = section.astype(jnp.int32)[None]

    slice_rows = head // plane
    mine = lax.axis_index("dp") * groups + member
    own_rows, *parts = pick(
        tokens_in.reshape(rows_dev, length, width),
        plan,
        place,
        groups,
        out_layer,
        mine.astype(jnp.int32)[None],
        slice_rows,
    )
    slices = [raised(own_rows, r) for r in range(sections - 1, 0, -1)]
    slices = [own_rows] + slices[::-1]
    chosen = jnp.take(segments, plan[0], axis=0, mode="clip").astype(BF16)
    chosen = chosen.reshape(groups, share, length)
    moved, moved_seg = [], []
    for r in range(groups):
        outgoing = lax.dynamic_index_in_dim(chosen, (member + r) % groups, 0, keepdims=False)
        moved.append(handed(parts[r], r) if r else parts[r])
        moved_seg.append(handed(outgoing, r) if r else outgoing)
    moved = [part.reshape(share * length, width) for part in moved]
    order = (member - jnp.arange(groups)) % groups
    seg = jnp.take(jnp.stack(moved_seg), order, axis=0, mode="clip").reshape(tokens)
    at = jnp.arange(tokens)
    mask = (
        (at[:, None] >= at[None, :])
        & (at[:, None] // length == at[None, :] // length)
        & (seg[:, None] == seg[None, :])
    ).astype(F32)

    last = (section == sections - 1).astype(jnp.int32)[None]
    bits = devices.bit_length() - 1
    places = plane_places()
    x, xz, norms = project(
        moved, cotangent, gains, w_layer, out_layer, place, []
    )
    coupling, stack = couple(slices, gains, w_layer, out_layer, last, [mask, places, xz])
    others = [shifted(coupling, r) for r in range(1, sections)]

    streams = stream_columns(width // CHUNKS)

    def facing(array, by):
        return lax.ppermute(array, "section", [(i, i ^ by) for i in range(sections)])

    arrays, masks, by = [hold(xz, others)], [0], sections // 2
    while by > 0:
        arrays = arrays + [facing(array, by) for array in arrays]
        masks = masks + [mask_of ^ by for mask_of in masks]
        by = by // 2
    xz_all = [arrays[masks.index(r)] for r in range(sections)]
    early = [xz_all[r] for r in range(1, sections) if r & (r - 1) == 0]
    late = [xz_all[r] for r in range(1, sections) if r & (r - 1) != 0]
    pieces = [compact([coupling] + others, layer, 3 * head, head, [xz])]

    rows = [stack[None]]
    for step in range(bits):
        if step > 0:
            pieces = [merge(*pieces, early)]
        pieces = pieces + [swapped(pieces[0], step)]
        if step == bits - 1:
            pieces[-1] = hold(pieces[-1], late)
        if step > 0:
            rows = [gather_two(*rows, pieces[-1:])]
        rows = rows + [swapped(rows[0], step)]
    pieces = pieces + [handed(array, r) for r in range(1, groups) for array in pieces]
    sent, total, mixes, *leaving = serial(
        xz_all, pieces, places, norms, mask, layer, gains, w_layer, out_layer, streams
    )
    back, pair = widen(sent, gains, w_layer, out_layer, width // CHUNKS)

    down = [(i, i - 1) for i in range(1, sections)]
    behind = sections - 1 - section

    def index(tick):
        return jnp.clip(tick - behind, 0, CHUNKS - 1).astype(jnp.int32)[None]

    def lowered(arrays):
        return [lax.ppermute(array, "section", down) for array in arrays]

    ticks = CHUNKS + sections - 1
    after = {}
    for tick in range(1, ticks):
        arrived = lowered(leaving)
        if tick < ticks - 1:
            for i, cols in enumerate(streams):
                waits = after.get(tick, []) if tick < ticks - 2 or i == STREAMS - 1 else []
                leaving[i], pair = join(index(tick), arrived[i], pair, cols, waits)
        if tick == 1:
            rows = [hold(array, leaving) for array in rows]
            rows = rows + [handed(array, r) for r in range(1, groups) for array in rows]
            rests, halves = [], []
            for part in range(PARTS):
                rest, half = settle(
                    total, mixes, rows, places, x, cotangent, back, width // CHUNKS, part, PARTS
                )
                rests.append(rest)
                halves.append(half)
            sums = [stacked(halves)]
            for step in range(bits):
                sums.append(added([sums[-1], swapped(sums[-1], step)]))
            sums.append(added(sums[-1:] + [handed(sums[-1], r) for r in range(1, groups)]))
            gain_whole = sums[-1].reshape(1, width)
            after = {2 + i: [array] for i, array in enumerate(sums)}
    out = finish(index(ticks - 1), arrived, pair, rests, streams)
    return (out[None], gain_whole)


def attend(hidden, segment, gain_row, w_layer, out_layer):
    count, length, width = hidden.shape
    head = out_layer.shape[0]
    scaled = hidden * lax.rsqrt(jnp.mean(hidden * hidden, axis=-1, keepdims=True) + EPS) * gain_row
    normed = scaled.astype(BF16).reshape(count * length, width)
    projected = jnp.dot(normed, w_layer, preferred_element_type=F32).reshape(count, length, 3 * head)
    query = projected[:, :, :head]
    keyed = projected[:, :, head : 2 * head]
    valued = projected[:, :, 2 * head :]
    positions = jnp.arange(length)
    allowed = (positions[:, None] >= positions[None, :])[None] & (
        segment[:, :, None] == segment[:, None, :]
    )
    scores = jnp.einsum("rid,rjd->rij", query, keyed, precision=lax.Precision.HIGHEST)
    scores = jnp.where(allowed, scores / math.sqrt(head), -1e30)
    weights = jax.nn.softmax(scores, axis=-1)
    mixed = jnp.einsum("rij,rjd->rid", weights, valued, precision=lax.Precision.HIGHEST)
    mixed = mixed.astype(BF16).reshape(count * length, head)
    output = jnp.dot(mixed, out_layer, preferred_element_type=F32).reshape(count, length, width)
    return hidden + output


MB_ROWS = 2


def relay(tokens_in, cotangent, gains, w_qkv, w_out, segments, plan):
    sections = lax.axis_size("section")
    section = lax.axis_index("section")
    rows_dev = plan.shape[1]
    width = tokens_in.shape[1]
    length = segments.shape[1]
    micro = rows_dev // MB_ROWS
    blocks = tokens_in.reshape(rows_dev, length, width)
    chosen = jnp.take(blocks, plan[0], axis=0)
    chosen_seg = jnp.take(segments, plan[0], axis=0).astype(BF16)
    assigned = lax.all_to_all(chosen, "group", split_axis=0, concat_axis=0, tiled=True)
    moved_seg = lax.all_to_all(chosen_seg, "group", split_axis=0, concat_axis=0, tiled=True)
    assigned = assigned.reshape(micro, MB_ROWS, length, width)
    seg_groups = moved_seg.reshape(micro, MB_ROWS, length)
    gain_row, w_layer, out_layer = gains[0], w_qkv[0], w_out[0]
    grad_rows = cotangent.reshape(micro, MB_ROWS, length, width)
    ticks = micro + sections - 1

    def passed_along(array, by):
        pairs = [(i, i + by) for i in range(sections) if 0 <= i + by < sections]
        return lax.ppermute(array, "section", pairs)

    def at(array, i):
        return lax.dynamic_index_in_dim(array, i, 0, keepdims=False)

    def forward_tick(tick, carry):
        saved, arrived = carry
        index = tick - section
        valid = (index >= 0) & (index < micro)
        clipped = jnp.clip(index, 0, micro - 1)
        entering = jnp.where(section == 0, at(assigned, clipped), arrived)
        kept = jnp.where(valid, entering, at(saved, clipped))
        saved = lax.dynamic_update_index_in_dim(saved, kept, clipped, 0)
        segment = at(seg_groups, clipped)

        def run_layer(value):
            return attend(value.astype(F32), segment, gain_row, w_layer, out_layer).astype(BF16)

        leaving = lax.cond(valid, run_layer, jnp.zeros_like, entering)
        return (saved, passed_along(leaving, 1))

    saved_init = jnp.zeros((micro, MB_ROWS, length, width), BF16)
    arrive_init = jnp.zeros((MB_ROWS, length, width), BF16)
    saved, _ = lax.fori_loop(0, ticks, forward_tick, (saved_init, arrive_init))

    def backward_tick(tick, carry):
        grads_x, gain_total, arrived = carry
        index = tick - (sections - 1 - section)
        valid = (index >= 0) & (index < micro)
        clipped = jnp.clip(index, 0, micro - 1)
        entering = jnp.where(section == sections - 1, at(grad_rows, clipped), arrived)
        segment = at(seg_groups, clipped)
        stored = at(saved, clipped).astype(F32)

        def local_layer(hidden, gains_here):
            return attend(hidden, segment, gains_here, w_layer, out_layer)

        def run_back(value):
            _, pullback = jax.vjp(local_layer, stored, gain_row)
            grad_hidden, grad_gain = pullback(value.astype(F32))
            return (grad_hidden.astype(BF16), grad_gain)

        def skip_back(value):
            return (jnp.zeros_like(value), jnp.zeros(gain_row.shape, F32))

        sending, grad_gain = lax.cond(valid, run_back, skip_back, entering)
        kept = jnp.where(valid, sending, at(grads_x, clipped))
        grads_x = lax.dynamic_update_index_in_dim(grads_x, kept, clipped, 0)
        return (grads_x, gain_total + grad_gain, passed_along(sending, -1))

    gain_init = jnp.zeros(gain_row.shape, F32)
    grads_x, gain_total, _ = lax.fori_loop(
        0, ticks, backward_tick, (saved_init, gain_init, arrive_init)
    )
    gain_whole = lax.psum(gain_total, ("dp", "group"))
    return (grads_x.reshape(1, rows_dev * length, width), gain_whole[None])


def solution(mesh):
    placed = (
        P(("dp", "group"), None),
        P(("dp", "group"), None),
        P("section", None),
        P("section", None, None),
        P("section", None, None),
        P(("dp", "group"), None),
        P(("dp", "group"), None),
    )

    def chosen(tokens_in, cotangent, gains, w_qkv, w_out, segments, plan):
        sections, head, width = w_out.shape
        devices = mesh.shape["dp"]
        small = sections * 4 * head < width and sections > 1
        halves = devices & (devices - 1) == 0 and sections & (sections - 1) == 0
        body = local if small and halves else relay
        return jax.shard_map(
            body,
            mesh=mesh,
            in_specs=placed,
            out_specs=(P("section", ("dp", "group"), None), P("section", None)),
            check_vma=False,
        )(tokens_in, cotangent, gains, w_qkv, w_out, segments, plan)

    return chosen
```

```python
import math

import jax
import jax.numpy as jnp
from jax import lax
from jax.experimental import pallas as pl
from jax.experimental.pallas import tpu as pltpu
from jax.sharding import PartitionSpec as P

EPS = 1e-05
VMEM_BYTES = 24 * 1024 * 1024
SMALL = 16 * 1024 * 1024
F32 = jnp.float32
BF16 = jnp.bfloat16


def dot_nn(a, b):
    return lax.dot_general(a, b, (((1,), (0,)), ((), ())), preferred_element_type=F32)


def dot_nt(a, b):
    return lax.dot_general(a, b, (((1,), (1,)), ((), ())), preferred_element_type=F32)


def dot_tn(a, b):
    return lax.dot_general(a, b, (((0,), (0,)), ((), ())), preferred_element_type=F32)


IN_HBM = pl.BlockSpec(memory_space=pltpu.HBM)
ANYWHERE = pl.BlockSpec(memory_space=pl.ANY)
IN_VMEM = pl.BlockSpec(memory_space=pltpu.VMEM)
IN_SMEM = pl.BlockSpec(memory_space=pltpu.SMEM)


def in_hbm(array):
    return pltpu.with_memory_space_constraint(array, pltpu.HBM)


def in_vmem(array):
    return pltpu.with_memory_space_constraint(array, pltpu.VMEM)


def mover(sems):
    used = []

    def start(source, target):
        copy = pltpu.make_async_copy(source, target, sems.at[len(used)])
        copy.start()
        used.append(copy)
        return copy

    return start


def steps(width):
    step = min(width, 1024)
    return [slice(at, at + step) for at in range(0, width, step)]


def params(limit=VMEM_BYTES):
    return pltpu.CompilerParams(vmem_limit_bytes=limit)


def pick(tokens, plan, place, groups, out_layer, mine, slice_rows):
    rows, length, width = tokens.shape
    share = rows // groups

    def kernel(plan_ref, place_ref, mine_ref, tokens_ref, o_ref, *rest):
        slice_ref, parts = rest[0], rest[1 : 1 + groups]
        slice_in, rows_in, sems = rest[1 + groups :]
        start = mover(sems)
        at = pl.ds(pl.multiple_of(mine_ref[0] * slice_rows, slice_rows), slice_rows)
        loads = [(start(o_ref.at[at], slice_in), slice_in, slice_ref)]
        for r in range(groups):
            target = lax.rem(place_ref[0] + r, groups)
            for c in range(share):
                here = rows_in.at[r * share + c]
                row = plan_ref[0, target * share + c]
                loads.append((start(tokens_ref.at[row], here), here, parts[r].at[c]))
        stores = []
        for load, here, there in loads:
            load.wait()
            stores.append(start(here, there))
        for store in stores:
            store.wait()

    return pl.pallas_call(
        kernel,
        out_shape=[pltpu.HBM((slice_rows, width), BF16)]
        + [pltpu.HBM((share, length, width), BF16)] * groups,
        in_specs=[IN_SMEM, IN_SMEM, IN_SMEM, IN_HBM, IN_HBM],
        out_specs=[IN_HBM] * (1 + groups),
        scratch_shapes=[
            pltpu.VMEM((slice_rows, width), BF16),
            pltpu.VMEM((rows, length, width), BF16),
            pltpu.SemaphoreType.DMA((2 * rows + 2,)),
        ],
        compiler_params=params(),
        name="pick",
    )(plan, place, mine, in_hbm(tokens), in_hbm(out_layer))


def project(parts, cotangent, gain, w_layer, out_layer, place, after):
    groups = len(parts)
    tokens, width = cotangent.shape
    head = out_layer.shape[0]
    wide = w_layer.shape[1]
    block = tokens // groups
    cuts = steps(width)
    copies = len(cuts) * (groups + 4)

    def kernel(place_ref, *refs):
        part_refs = refs[:groups]
        cot_ref, g_ref, w_ref, o_ref = refs[groups : groups + 4]
        x_ref, xz_ref, n_ref = refs[groups + 4 + len(after) : groups + 7 + len(after)]
        x_in, c_in, w_in, o_in, sems = refs[groups + 7 + len(after) :]
        start = mover(sems)
        loads = []
        for cut in cuts:
            mine = [start(w_ref.at[cut], w_in.at[cut])]
            mine.append(start(o_ref.at[:, cut], o_in.at[:, cut]))
            for r in range(groups):
                source = lax.rem(place_ref[0] + groups - r, groups)
                rows = pl.ds(pl.multiple_of(source * block, block), block)
                mine.append(start(part_refs[r].at[:, cut], x_in.at[rows, cut]))
            mine.append(start(cot_ref.at[:, cut], c_in.at[:, cut]))
            loads.append(mine)
        through = jnp.zeros((tokens, wide), F32)
        across = jnp.zeros((tokens, head), F32)
        back = jnp.zeros((tokens, head), F32)
        square = jnp.zeros((tokens, 1), F32)
        stores = []
        for cut, mine in zip(cuts, loads):
            for load in mine:
                load.wait()
            stores.append(start(x_in.at[:, cut], x_ref.at[:, cut]))
            x = x_in[:, cut]
            xf = x.astype(F32)
            through += dot_nn((xf * g_ref[:, cut]).astype(BF16), w_in[cut, :])
            across += dot_nt(x, o_in[:, cut])
            back += dot_nt(c_in[:, cut], o_in[:, cut])
            square += jnp.sum(xf * xf, axis=1, keepdims=True)
        xz_ref[:, :wide] = through.astype(BF16)
        xz_ref[:, wide : wide + head] = across.astype(BF16)
        xz_ref[:, wide + head :] = back.astype(BF16)
        n_ref[...] = square
        for store in stores:
            store.wait()

    return pl.pallas_call(
        kernel,
        out_shape=[
            pltpu.HBM((tokens, width), BF16),
            jax.ShapeDtypeStruct((tokens, wide + 2 * head), BF16),
            jax.ShapeDtypeStruct((tokens, 1), F32),
        ],
        in_specs=[IN_SMEM]
        + [ANYWHERE] * groups
        + [IN_HBM, IN_VMEM, IN_HBM, IN_HBM]
        + [ANYWHERE] * len(after),
        out_specs=[IN_HBM, IN_VMEM, IN_VMEM],
        scratch_shapes=[
            pltpu.VMEM((tokens, width), BF16),
            pltpu.VMEM((tokens, width), BF16),
            pltpu.VMEM((width, wide), BF16),
            pltpu.VMEM((head, width), BF16),
            pltpu.SemaphoreType.DMA((copies,)),
        ],
        compiler_params=params(),
        name="project",
    )(
        place,
        in_hbm(parts[0]),
        *[in_vmem(part) for part in parts[1:]],
        in_hbm(cotangent),
        gain,
        in_hbm(w_layer),
        in_hbm(out_layer),
        *after,
    )


def couple(slices, gain, w_layer, out_layer, last, after):
    sections = len(slices)
    count, width = slices[0].shape
    head = out_layer.shape[0]
    wide = w_layer.shape[1]
    below = (sections - 2) * wide
    packed = below + max(wide, (sections - 1) * head)
    cuts = steps(width)
    copies = len(cuts) * (sections + 2) + sections - 1

    def kernel(last_ref, *refs):
        s_refs = refs[:sections][::-1]
        g_ref, w_ref, o_ref = refs[sections : sections + 3]
        out_ref, stack_ref, r_in, w_in, o_in, sems = refs[sections + 3 + len(after) :]
        rows = [slice(r * count, (r + 1) * count) for r in range(sections)]
        start = mover(sems)
        loads = []
        for cut in cuts:
            mine = [start(w_ref.at[cut], w_in.at[cut])]
            mine.append(start(o_ref.at[:, cut], o_in.at[:, cut]))
            for r in range(sections):
                mine.append(start(s_refs[r].at[:, cut], r_in.at[rows[r], cut]))
            loads.append(mine)
        through = jnp.zeros((sections * count, wide), F32)
        across = jnp.zeros((sections * count, head), F32)
        for cut, mine in zip(cuts, loads):
            for load in mine:
                load.wait()
            r = r_in[:, cut]
            through += dot_nn((r.astype(F32) * g_ref[:, cut]).astype(BF16), w_in[cut, :])
            across += dot_nt(r, o_in[:, cut])
        stores = [start(r_in.at[rows[r]], stack_ref.at[r - 1]) for r in range(1, sections)]
        through = through.astype(BF16)
        across = across.astype(BF16)
        out_ref[...] = jnp.zeros_like(out_ref)
        for r in range(1, sections - 1):
            out_ref[:, (r - 1) * wide : r * wide] = through[rows[r]]

        @pl.when(last_ref[0] == 1)
        def _():
            out_ref[:, below : below + wide] = through[rows[-1]]

        @pl.when(last_ref[0] == 0)
        def _():
            for r in range(sections - 1):
                out_ref[:, below + r * head : below + (r + 1) * head] = across[rows[r]]

        for store in stores:
            store.wait()

    return pl.pallas_call(
        kernel,
        out_shape=[
            jax.ShapeDtypeStruct((count, packed), BF16),
            pltpu.HBM((sections - 1, count, width), BF16),
        ],
        in_specs=[IN_SMEM]
        + [ANYWHERE] * sections
        + [IN_VMEM, IN_HBM, IN_HBM]
        + [ANYWHERE] * len(after),
        out_specs=[IN_VMEM, IN_HBM],
        scratch_shapes=[
            pltpu.VMEM((sections * count, width), BF16),
            pltpu.VMEM((width, wide), BF16),
            pltpu.VMEM((head, width), BF16),
            pltpu.SemaphoreType.DMA((copies,)),
        ],
        compiler_params=params(),
        name="couple",
    )(last, *slices[::-1], gain, in_hbm(w_layer), in_hbm(out_layer), *after)


def layout(sections, wide, head):
    through, across, spans, at = {}, {}, {}, 0
    for j in range(sections - 1):
        begin = at
        across[j, j] = slice(at, at + head)
        at += head
        for k in range(j + 1, sections):
            through[j, k] = slice(at, at + wide)
            at += wide
            if k < sections - 1:
                across[j, k] = slice(at, at + head)
                at += head
        spans[j] = slice(begin, at)
    return through, across, spans, at


def compact(parts, section, wide, head, after):
    sections = len(parts)
    count = parts[0].shape[0]
    below = (sections - 2) * wide
    through, across, _, total = layout(sections, wide, head)

    def kernel(s_ref, *refs):
        part_refs, out_ref = refs[:sections], refs[-1]
        mine = s_ref[0]

        def fill(k, r):
            for j in range(k):
                at = (k - j - 1) * wide
                out_ref[0, :, through[j, k]] = part_refs[r][:, at : at + wide]
            for j in range(k + 1 if k < sections - 1 else 0):
                at = below + (k - j) * head
                out_ref[0, :, across[j, k]] = part_refs[r][:, at : at + head]

        for s in range(sections):

            @pl.when(mine == s)
            def _(s=s):
                for r in range(sections):
                    fill((s - r) % sections, r)

    vmem = pl.BlockSpec(memory_space=pltpu.VMEM)
    return pl.pallas_call(
        kernel,
        out_shape=jax.ShapeDtypeStruct((1, count, total), BF16),
        in_specs=[IN_SMEM] + [vmem] * sections + [ANYWHERE] * len(after),
        out_specs=vmem,
        compiler_params=params(SMALL),
        name="compact",
    )(section, *parts, *after)


def merge(first, second, after):
    count = first.shape[0]

    def kernel(first_ref, second_ref, *refs):
        refs[-1][:count] = first_ref[...]
        refs[-1][count:] = second_ref[...]

    return pl.pallas_call(
        kernel,
        out_shape=jax.ShapeDtypeStruct((2 * count,) + first.shape[1:], first.dtype),
        in_specs=[IN_VMEM] * 2 + [ANYWHERE] * len(after),
        out_specs=IN_VMEM,
        compiler_params=params(SMALL),
        name="merge",
    )(first, second, *after)


def layer_back(s, sections, total, da, rstd, width, head, couplings, projs, weights, mixes, dmix):
    wide = 3 * head
    scale = 1.0 / math.sqrt(head)
    through_at, across_at, _, _ = layout(sections, wide, head)
    da = da.astype(BF16)
    q, k, v = (projs[s, :, i * head : (i + 1) * head] for i in range(3))
    soft = weights[s]
    dv = dot_tn(soft.astype(BF16), da)
    dsoft = dot_nt(da, v)
    dscore = soft * (dsoft - jnp.sum(dsoft * soft, axis=1, keepdims=True))
    dscore = (dscore * scale).astype(BF16)
    dproj = jnp.concatenate([dot_nn(dscore, k), dot_tn(dscore, q), dv], axis=1)
    along = jnp.sum(dproj * projs[s].astype(F32), axis=1, keepdims=True)
    first = (dproj * rstd).astype(BF16)
    second = (-total * mixes[:, s * head : (s + 1) * head].astype(F32)).astype(BF16)
    total = total + rstd * rstd * along * (1.0 / width)
    for j in reversed(range(s)):
        cols = through_at[j, s]
        if s < sections - 1:
            both = jnp.concatenate([first, second], axis=1)
            term = dot_nt(both, couplings(slice(cols.start, across_at[j, s].stop)))
        else:
            term = dot_nt(first, couplings(cols))
        dmix[:, j * head : (j + 1) * head] += term
    return first, second, total


def serial(xz, pieces, places, norms, mask, section, gain, w_layer, out_layer, streams):
    sections = len(xz)
    tokens = norms.shape[0]
    head, width = out_layer.shape
    wide = 3 * head
    scale = 1.0 / math.sqrt(head)
    lead = slice(0, streams[-1].stop)
    through_at, across_at, spans, _ = layout(sections, wide, head)
    count, packed = pieces[0].shape[-2:]
    plane = head // count
    n_in = sections + len(pieces)
    copies = sections + plane + 2

    def kernel(s_ref, p_ref, *refs):
        xz_refs, piece_refs = refs[:sections], refs[sections:n_in]
        n_ref, mask_ref, g_ref, w_ref, o_ref = refs[n_in : n_in + 5]
        n_out = n_in + 5
        kept = refs[n_out : n_out + 9]
        projs, weights, mixes, dmix, tails_ref, rstds_ref, t_ref, v_ref, table = kept
        first_refs = refs[n_out + 9 : n_out + 9 + len(streams)]
        scratch = refs[n_out + 9 + len(streams) :]
        xz_all, w_in, o_in, sems = scratch
        mine = s_ref[0]
        started = []

        def start(source, target):
            copy = pltpu.make_async_copy(source, target, sems.at[len(started)])
            copy.start()
            started.append(copy)

        for r in range(sections):
            start(xz_refs[r], xz_all.at[mine ^ r])
        at = 0
        for ref in piece_refs:
            for i in range(ref.shape[0]):
                start(ref.at[i], table.at[p_ref[at]])
                at += 1
        small = list(started)
        start(w_ref.at[lead], w_in)
        start(o_ref.at[:, lead], o_in)
        for copy in small:
            copy.wait()

        def couplings(cols):
            return table[:, :, cols].reshape(head, cols.stop - cols.start)

        allowed = mask_ref[...] > 0.5
        norm = n_ref[...]
        rstds = []
        projected = [xz_all[s, :, :wide].astype(F32) for s in range(sections)]
        crossed = [xz_all[s, :, wide : wide + head].astype(F32) for s in range(sections - 1)]
        for s in range(sections):
            proj = projected[s]
            rstd = lax.rsqrt(norm * (1.0 / width) + EPS)
            proj = proj * rstd
            projs[s] = proj.astype(BF16)
            q, k, v = (projs[s, :, i * head : (i + 1) * head] for i in range(3))
            scores = jnp.where(allowed, dot_nt(q, k) * scale, -1e30)
            scores = jnp.exp(scores - jnp.max(scores, axis=1, keepdims=True))
            soft = scores / jnp.sum(scores, axis=1, keepdims=True)
            weights[s] = soft
            mix = dot_nn(soft.astype(BF16), v).astype(BF16)
            mixes[:, s * head : (s + 1) * head] = mix
            rstds.append(rstd)
            rstds_ref[s] = rstd
            dmix[:, s * head : (s + 1) * head] = xz_all[s, :, wide + head :].astype(F32)
            if s == sections - 1:
                break
            added_on = dot_nn(mix, couplings(spans[s]))

            def part(cols, added_on=added_on, begin=spans[s].start):
                return added_on[:, cols.start - begin : cols.stop - begin]

            for k in range(s + 1, sections):
                projected[k] = projected[k] + part(through_at[s, k])
                if k < sections - 1:
                    crossed[k] = crossed[k] + part(across_at[s, k])
            y = crossed[s]
            tail = y + part(across_at[s, s])
            norm = norm + jnp.sum(mix.astype(F32) * (y + tail), axis=1, keepdims=True)
            norm = jnp.maximum(norm, 0.0)
            tails_ref[s] = tail
        end = sections - 1
        total = jnp.zeros((tokens, 1), F32)
        da = dmix[:, end * head :]
        first, second, total = layer_back(
            end, sections, total, da, rstds[end], width, head, couplings, projs, weights, mixes, dmix
        )
        v_ref[:, :wide] = first
        v_ref[:, wide:] = second
        t_ref[...] = total

        for copy in started[len(small) :]:
            copy.wait()
        own = dot_nt(v_ref[:, :wide], w_in[...]) * g_ref[:, lead]
        own = (own + dot_nn(v_ref[:, wide:], o_in[...])).astype(BF16)
        for ref, part in zip(first_refs, streams):
            ref[...] = own[:, part]

    vmem = pl.BlockSpec(memory_space=pltpu.VMEM)
    smem = pl.BlockSpec(memory_space=pltpu.SMEM)
    return pl.pallas_call(
        kernel,
        out_shape=[
            pltpu.VMEM((sections, tokens, wide), BF16),
            pltpu.VMEM((sections, tokens, tokens), F32),
            pltpu.VMEM((tokens, sections * head), BF16),
            pltpu.VMEM((tokens, sections * head), F32),
            pltpu.VMEM((sections - 1, tokens, head), F32),
            pltpu.VMEM((sections, tokens, 1), F32),
            pltpu.VMEM((tokens, 1), F32),
            pltpu.VMEM((tokens, wide + head), BF16),
            pltpu.VMEM((plane, count, packed), BF16),
        ]
        + [pltpu.VMEM((tokens, part.stop - part.start), BF16) for part in streams],
        in_specs=[smem, smem] + [ANYWHERE] * n_in + [vmem, vmem, vmem, IN_HBM, IN_HBM],
        out_specs=[vmem] * (9 + len(streams)),
        scratch_shapes=[
            pltpu.VMEM((sections,) + xz[0].shape, BF16),
            pltpu.VMEM((lead.stop, wide), BF16),
            pltpu.VMEM((head, lead.stop), BF16),
            pltpu.SemaphoreType.DMA((copies,)),
        ],
        compiler_params=params(),
        name="serial",
    )(
        section,
        places,
        *xz,
        *pieces,
        norms,
        mask,
        gain,
        in_hbm(w_layer),
        in_hbm(out_layer),
    )


def serial_back(section, kept, width, head):
    sections, tokens, wide = kept[0].shape

    def kernel(s_ref, *refs):
        projs, weights, mixes, given, tails, rstds, t_in, v_in, table = refs[:9]
        v_ref, t_ref, a_ref, dmix = refs[9:]
        mine = s_ref[0]

        def couplings(cols):
            return table[:, :, cols].reshape(head, cols.stop - cols.start)

        dmix[...] = given[...]
        total = t_in[...]
        v_ref[...] = v_in[...]
        t_ref[...] = total
        a_ref[...] = jnp.zeros_like(a_ref)
        for s in reversed(range(sections - 1)):
            cols = slice(s * head, (s + 1) * head)
            da = dmix[:, cols] - total * tails[s]
            first, second, total = layer_back(
                s, sections, total, da, rstds[s], width, head, couplings, projs, weights, mixes, dmix
            )

            @pl.when(mine == s)
            def _(first=first, second=second, total=total):
                v_ref[:, :wide] = first
                v_ref[:, wide:] = second
                t_ref[...] = total

            for r in range(1, sections - s):

                @pl.when(mine == s + r)
                def _(r=r, cols=cols):
                    a_ref[:, (r - 1) * head : r * head] = mixes[:, cols]

    return pl.pallas_call(
        kernel,
        out_shape=[
            pltpu.VMEM((tokens, wide + head), BF16),
            pltpu.VMEM((tokens, 1), F32),
            pltpu.VMEM((tokens, (sections - 1) * head), BF16),
        ],
        in_specs=[IN_SMEM] + [IN_VMEM] * 9,
        out_specs=[IN_VMEM] * 3,
        scratch_shapes=[pltpu.VMEM((tokens, sections * head), F32)],
        compiler_params=params(SMALL),
        name="serial_back",
    )(section, *[in_vmem(array) for array in kept])


def hold(array, after):
    def kernel(*refs):
        pass

    return pl.pallas_call(
        kernel,
        out_shape=jax.ShapeDtypeStruct(array.shape, array.dtype),
        in_specs=[ANYWHERE] * (1 + len(after)),
        out_specs=ANYWHERE,
        input_output_aliases={0: 0},
        compiler_params=params(SMALL),
        name="hold",
    )(array, *after)


def gather_two(first, second, after):
    count = first.shape[0]

    def kernel(first_ref, second_ref, *refs):
        out_ref, sems = refs[len(after) :]
        start = mover(sems)
        copies = [start(first_ref, out_ref.at[:count]), start(second_ref, out_ref.at[count:])]
        for copy in copies:
            copy.wait()

    return pl.pallas_call(
        kernel,
        out_shape=jax.ShapeDtypeStruct((2 * count,) + first.shape[1:], first.dtype),
        in_specs=[ANYWHERE] * (2 + len(after)),
        out_specs=IN_VMEM,
        scratch_shapes=[pltpu.SemaphoreType.DMA((2,))],
        compiler_params=params(SMALL),
        name="gather_two",
    )(first, second, *after)


def widen(sent, gain, w_layer, out_layer, chunk):
    tokens = sent.shape[0]
    head, width = out_layer.shape
    wide = w_layer.shape[1]
    cuts = [slice(at, at + chunk) for at in range(0, width, chunk)]

    def kernel(v_ref, g_ref, w_ref, o_ref, back_ref, pair_ref, back_in, w_in, o_in, sems):
        start = mover(sems)
        loads = [
            (start(w_ref.at[cut], w_in.at[cut]), start(o_ref.at[:, cut], o_in.at[:, cut]))
            for cut in cuts
        ]
        stores = []
        for i, (cut, mine) in enumerate(zip(cuts, loads)):
            for load in mine:
                load.wait()
            back = dot_nt(v_ref[:, :wide], w_in[cut, :])
            own = back * g_ref[:, cut] + dot_nn(v_ref[:, wide:], o_in[:, cut])
            back_in[:, cut] = back.astype(BF16)
            stores.append(start(back_in.at[:, cut], back_ref.at[:, cut]))
            pair_ref[0, i] = own.astype(BF16)
            pair_ref[1, i] = jnp.zeros_like(pair_ref[1, i])
        for store in stores:
            store.wait()

    return pl.pallas_call(
        kernel,
        out_shape=[
            pltpu.HBM((tokens, width), BF16),
            pltpu.VMEM((2, len(cuts), tokens, chunk), BF16),
        ],
        in_specs=[IN_VMEM, IN_VMEM, IN_HBM, IN_HBM],
        out_specs=[IN_HBM, IN_VMEM],
        scratch_shapes=[
            pltpu.VMEM((tokens, width), BF16),
            pltpu.VMEM((width, wide), BF16),
            pltpu.VMEM((head, width), BF16),
            pltpu.SemaphoreType.DMA((3 * len(cuts),)),
        ],
        compiler_params=params(),
        name="widen",
    )(in_vmem(sent), gain, in_hbm(w_layer), in_hbm(out_layer))


def settle(total, mixes, stacks, places, x, cotangent, back, chunk, part, parts):
    tokens, width = x.shape
    layers, rows = stacks[0].shape[1:3]
    entries = [(i, e) for i, stack in enumerate(stacks) for e in range(stack.shape[0])]
    plane = len(entries)
    head = plane * rows
    span = width // parts
    base = part * span
    cuts = [slice(at, at + chunk) for at in range(0, span, chunk)]
    copies = plane * layers + 3 * len(cuts)

    def kernel(p_ref, t_ref, a_ref, x_ref, c_ref, back_ref, *refs):
        stack_refs = refs[: len(stacks)]
        rest_ref, dg_ref = refs[len(stacks) : len(stacks) + 2]
        lower, x_in, c_in, back_in, sems = refs[len(stacks) + 2 :]
        start = mover(sems)
        first = []
        for at, (i, e) in enumerate(entries):
            for r in range(layers):
                here = pl.ds(base, span)
                first.append(start(stack_refs[i].at[e, r, :, here], lower.at[r, p_ref[at]]))
        loads = []
        for cut in cuts:
            there = pl.ds(base + cut.start, chunk)
            mine = [start(x_ref.at[:, there], x_in.at[:, cut])]
            mine.append(start(c_ref.at[:, there], c_in.at[:, cut]))
            mine.append(start(back_ref.at[:, there], back_in.at[:, cut]))
            loads.append(mine)
        for load in first:
            load.wait()
        for i, (cut, mine) in enumerate(zip(cuts, loads)):
            for load in mine:
                load.wait()
            below = lower[:, :, :, cut].reshape(layers * head, chunk)
            here = x_in[:, cut].astype(F32) + dot_nn(a_ref[...], below)
            rest_ref[i] = (c_in[:, cut].astype(F32) - t_ref[...] * here).astype(BF16)
            gain = jnp.sum(back_in[:, cut].astype(F32) * here, axis=0, keepdims=True)
            for at in range(0, chunk, head):
                row = (cut.start + at) // head
                dg_ref[row : row + 1, :] = gain[:, at : at + head]

    return pl.pallas_call(
        kernel,
        out_shape=[
            pltpu.VMEM((len(cuts), tokens, chunk), BF16),
            pltpu.VMEM((span // head, head), F32),
        ],
        in_specs=[IN_SMEM] + [IN_VMEM] * 2 + [IN_HBM] * (3 + len(stacks)),
        out_specs=[IN_VMEM] * 2,
        scratch_shapes=[
            pltpu.VMEM((layers, plane, rows, span), BF16),
            pltpu.VMEM((tokens, span), BF16),
            pltpu.VMEM((tokens, span), BF16),
            pltpu.VMEM((tokens, span), BF16),
            pltpu.SemaphoreType.DMA((copies,)),
        ],
        compiler_params=params(),
        name="settle",
    )(
        places,
        in_vmem(total),
        in_vmem(mixes),
        *[in_hbm(array) for array in (x, cotangent, back, *stacks)],
    )


def join(index, arrived, pair, cols, after):
    tokens, part = arrived.shape

    def kernel(i_ref, r_ref, _, *refs):
        send_ref, pair_ref = refs[len(after) :]
        at = i_ref[0]
        r = r_ref[...]
        send_ref[...] = (pair_ref[0, at, :, cols].astype(F32) + r.astype(F32)).astype(BF16)
        pair_ref[1, at, :, cols] = r

    return pl.pallas_call(
        kernel,
        out_shape=[pltpu.VMEM((tokens, part), BF16), pltpu.VMEM(pair.shape, BF16)],
        in_specs=[IN_SMEM] + [IN_VMEM] * 2 + [ANYWHERE] * len(after),
        out_specs=[IN_VMEM] * 2,
        input_output_aliases={2: 1},
        compiler_params=params(SMALL),
        name="join",
    )(index, in_vmem(arrived), in_vmem(pair), *after)


def finish(index, arrived, pair, rests, streams):
    _, count, tokens, chunk = pair.shape

    def kernel(i_ref, *refs):
        r_refs = refs[: len(streams)]
        pair_ref, rest_refs = refs[len(streams)], refs[len(streams) + 1 :][: len(rests)]
        whole_ref, whole, sems = refs[len(streams) + 1 + len(rests) :]
        each = count // len(rests)
        at = i_ref[0]
        copies = []
        for i in range(count):
            full = rest_refs[i // each][i % each].astype(F32) + pair_ref[0, i].astype(F32)
            whole[i] = (full + pair_ref[1, i].astype(F32)).astype(BF16)

            @pl.when(at == i)
            def _(i=i, full=full):
                for ref, cols in zip(r_refs, streams):
                    whole[i, :, cols] = (full[:, cols] + ref[...].astype(F32)).astype(BF16)

            there = whole_ref.at[:, pl.ds(i * chunk, chunk)]
            copies.append(pltpu.make_async_copy(whole.at[i], there, sems.at[i]))
            copies[-1].start()
        for copy in copies:
            copy.wait()

    return pl.pallas_call(
        kernel,
        out_shape=pltpu.HBM((tokens, count * chunk), BF16),
        in_specs=[IN_SMEM] + [IN_VMEM] * (len(streams) + 1 + len(rests)),
        out_specs=IN_HBM,
        scratch_shapes=[
            pltpu.VMEM((count, tokens, chunk), BF16),
            pltpu.SemaphoreType.DMA((count,)),
        ],
        compiler_params=params(SMALL),
        name="finish",
    )(index, *[in_vmem(array) for array in (*arrived, pair, *rests)])


def stacked(arrays):
    rows = arrays[0].shape[0]

    def kernel(*refs):
        for i, ref in enumerate(refs[:-1]):
            refs[-1][i * rows : (i + 1) * rows, :] = ref[...]

    return pl.pallas_call(
        kernel,
        out_shape=pltpu.VMEM((len(arrays) * rows, arrays[0].shape[1]), F32),
        in_specs=[IN_VMEM] * len(arrays),
        out_specs=IN_VMEM,
        compiler_params=params(SMALL),
        name="stacked",
    )(*[in_vmem(array) for array in arrays])


def added(arrays):
    def kernel(*refs):
        total = refs[0][...]
        for ref in refs[1:-1]:
            total = total + ref[...]
        refs[-1][...] = total

    return pl.pallas_call(
        kernel,
        out_shape=pltpu.VMEM(arrays[0].shape, F32),
        in_specs=[IN_VMEM] * len(arrays),
        out_specs=IN_VMEM,
        compiler_params=params(SMALL),
        name="added",
    )(*[in_vmem(array) for array in arrays])


STREAMS = 2
CHUNKS = 4
PARTS = 1


def stream_columns(chunk):
    lanes = 128
    tiles = chunk // lanes
    ends = [-(-tiles * (i + 1) // STREAMS) * lanes for i in range(STREAMS)]
    return [slice(start, end) for start, end in zip([0] + ends, ends)]


def shifted(array, by):
    sections = lax.axis_size("section")
    return lax.ppermute(array, "section", [(i, (i + by) % sections) for i in range(sections)])


def raised(array, by):
    sections = lax.axis_size("section")
    return lax.ppermute(array, "section", [(i, i + by) for i in range(sections - by)])


def swapped(array, step):
    groups = lax.axis_size("group")
    devices = lax.axis_size("dp")
    bits = devices.bit_length() - 1
    pairs = []
    for p in range(devices):
        for g in range(groups):
            pairs.append((p * groups + g, (p ^ (1 << ((step + g) % bits))) * groups + g))
    return lax.ppermute(array, ("dp", "group"), pairs)


def handed(array, by):
    groups = lax.axis_size("group")
    return lax.ppermute(array, "group", [(i, (i + by) % groups) for i in range(groups)])


def plane_places():
    groups = lax.axis_size("group")
    bits = lax.axis_size("dp").bit_length() - 1
    masks = []
    for g in range(groups):
        order = [0]
        for step in range(bits):
            order = order + [m ^ (1 << ((step + g) % bits)) for m in order]
        masks.append(order)
    masks = jnp.asarray(masks, jnp.int32)
    dp, member = lax.axis_index("dp"), lax.axis_index("group")
    places = []
    for r in range(groups):
        giver = (member + groups - r) % groups
        places.append((dp ^ masks[giver]) * groups + giver)
    return jnp.concatenate(places).astype(jnp.int32)


def local(tokens_in, cotangent, gains, w_qkv, w_out, segments, plan):
    sections = lax.axis_size("section")
    groups = lax.axis_size("group")
    devices = lax.axis_size("dp")
    plane = devices * groups
    section = lax.axis_index("section")
    member = lax.axis_index("group")
    rows_dev = plan.shape[1]
    length = segments.shape[1]
    tokens, width = tokens_in.shape
    head = w_out.shape[1]
    share = rows_dev // groups
    w_layer, out_layer = w_qkv[0], w_out[0]
    place = member.astype(jnp.int32)[None]
    layer = section.astype(jnp.int32)[None]

    slice_rows = head // plane
    mine = lax.axis_index("dp") * groups + member
    own_rows, *parts = pick(
        tokens_in.reshape(rows_dev, length, width),
        plan,
        place,
        groups,
        out_layer,
        mine.astype(jnp.int32)[None],
        slice_rows,
    )
    slices = [raised(own_rows, r) for r in range(sections - 1, 0, -1)]
    slices = [own_rows] + slices[::-1]
    chosen = jnp.take(segments, plan[0], axis=0, mode="clip").astype(BF16)
    chosen = chosen.reshape(groups, share, length)
    moved, moved_seg = [], []
    for r in range(groups):
        outgoing = lax.dynamic_index_in_dim(chosen, (member + r) % groups, 0, keepdims=False)
        moved.append(handed(parts[r], r) if r else parts[r])
        moved_seg.append(handed(outgoing, r) if r else outgoing)
    moved = [part.reshape(share * length, width) for part in moved]
    order = (member - jnp.arange(groups)) % groups
    seg = jnp.take(jnp.stack(moved_seg), order, axis=0, mode="clip").reshape(tokens)
    at = jnp.arange(tokens)
    mask = (
        (at[:, None] >= at[None, :])
        & (at[:, None] // length == at[None, :] // length)
        & (seg[:, None] == seg[None, :])
    ).astype(F32)

    last = (section == sections - 1).astype(jnp.int32)[None]
    bits = devices.bit_length() - 1
    places = plane_places()
    x, xz, norms = project(
        moved, cotangent, gains, w_layer, out_layer, place, []
    )
    coupling, stack = couple(slices, gains, w_layer, out_layer, last, [mask, places, xz])
    others = [shifted(coupling, r) for r in range(1, sections)]

    streams = stream_columns(width // CHUNKS)

    def facing(array, by):
        return lax.ppermute(array, "section", [(i, i ^ by) for i in range(sections)])

    arrays, masks, by = [hold(xz, others)], [0], sections // 2
    while by > 0:
        arrays = arrays + [facing(array, by) for array in arrays]
        masks = masks + [mask_of ^ by for mask_of in masks]
        by = by // 2
    xz_all = [arrays[masks.index(r)] for r in range(sections)]
    early = [xz_all[r] for r in range(1, sections) if r & (r - 1) == 0]
    late = [xz_all[r] for r in range(1, sections) if r & (r - 1) != 0]
    pieces = [compact([coupling] + others, layer, 3 * head, head, [xz])]

    rows = [stack[None]]
    for step in range(bits):
        if step > 0:
            pieces = [merge(*pieces, early)]
        pieces = pieces + [swapped(pieces[0], step)]
        if step == bits - 1:
            pieces[-1] = hold(pieces[-1], late)
        if step > 0:
            rows = [gather_two(*rows, pieces[-1:])]
        rows = rows + [swapped(rows[0], step)]
    pieces = pieces + [handed(array, r) for r in range(1, groups) for array in pieces]
    kept = serial(
        xz_all, pieces, places, norms, mask, layer, gains, w_layer, out_layer, streams
    )
    kept, leaving = kept[:9], list(kept[9:])
    sent, total, mixes = serial_back(layer, kept, width, head)
    back, pair = widen(sent, gains, w_layer, out_layer, width // CHUNKS)

    down = [(i, i - 1) for i in range(1, sections)]
    behind = sections - 1 - section

    def index(tick):
        return jnp.clip(tick - behind, 0, CHUNKS - 1).astype(jnp.int32)[None]

    def lowered(arrays):
        return [lax.ppermute(array, "section", down) for array in arrays]

    ticks = CHUNKS + sections - 1
    after = {}
    for tick in range(1, ticks):
        arrived = lowered(leaving)
        if tick < ticks - 1:
            for i, cols in enumerate(streams):
                waits = after.get(tick, []) if tick < ticks - 2 or i == STREAMS - 1 else []
                leaving[i], pair = join(index(tick), arrived[i], pair, cols, waits)
        if tick == 1:
            rows = [hold(array, leaving) for array in rows]
            rows = rows + [handed(array, r) for r in range(1, groups) for array in rows]
            rests, halves = [], []
            for part in range(PARTS):
                rest, half = settle(
                    total, mixes, rows, places, x, cotangent, back, width // CHUNKS, part, PARTS
                )
                rests.append(rest)
                halves.append(half)
            sums = [stacked(halves)]
            for step in range(bits):
                sums.append(added([sums[-1], swapped(sums[-1], step)]))
            sums.append(added(sums[-1:] + [handed(sums[-1], r) for r in range(1, groups)]))
            gain_whole = sums[-1].reshape(1, width)
            after = {2 + i: [array] for i, array in enumerate(sums)}
    out = finish(index(ticks - 1), arrived, pair, rests, streams)
    return (out[None], gain_whole)


def attend(hidden, segment, gain_row, w_layer, out_layer):
    count, length, width = hidden.shape
    head = out_layer.shape[0]
    scaled = hidden * lax.rsqrt(jnp.mean(hidden * hidden, axis=-1, keepdims=True) + EPS) * gain_row
    normed = scaled.astype(BF16).reshape(count * length, width)
    projected = jnp.dot(normed, w_layer, preferred_element_type=F32).reshape(count, length, 3 * head)
    query = projected[:, :, :head]
    keyed = projected[:, :, head : 2 * head]
    valued = projected[:, :, 2 * head :]
    positions = jnp.arange(length)
    allowed = (positions[:, None] >= positions[None, :])[None] & (
        segment[:, :, None] == segment[:, None, :]
    )
    scores = jnp.einsum("rid,rjd->rij", query, keyed, precision=lax.Precision.HIGHEST)
    scores = jnp.where(allowed, scores / math.sqrt(head), -1e30)
    weights = jax.nn.softmax(scores, axis=-1)
    mixed = jnp.einsum("rij,rjd->rid", weights, valued, precision=lax.Precision.HIGHEST)
    mixed = mixed.astype(BF16).reshape(count * length, head)
    output = jnp.dot(mixed, out_layer, preferred_element_type=F32).reshape(count, length, width)
    return hidden + output


MB_ROWS = 2


def relay(tokens_in, cotangent, gains, w_qkv, w_out, segments, plan):
    sections = lax.axis_size("section")
    section = lax.axis_index("section")
    rows_dev = plan.shape[1]
    width = tokens_in.shape[1]
    length = segments.shape[1]
    micro = rows_dev // MB_ROWS
    blocks = tokens_in.reshape(rows_dev, length, width)
    chosen = jnp.take(blocks, plan[0], axis=0)
    chosen_seg = jnp.take(segments, plan[0], axis=0).astype(BF16)
    assigned = lax.all_to_all(chosen, "group", split_axis=0, concat_axis=0, tiled=True)
    moved_seg = lax.all_to_all(chosen_seg, "group", split_axis=0, concat_axis=0, tiled=True)
    assigned = assigned.reshape(micro, MB_ROWS, length, width)
    seg_groups = moved_seg.reshape(micro, MB_ROWS, length)
    gain_row, w_layer, out_layer = gains[0], w_qkv[0], w_out[0]
    grad_rows = cotangent.reshape(micro, MB_ROWS, length, width)
    ticks = micro + sections - 1

    def passed_along(array, by):
        pairs = [(i, i + by) for i in range(sections) if 0 <= i + by < sections]
        return lax.ppermute(array, "section", pairs)

    def at(array, i):
        return lax.dynamic_index_in_dim(array, i, 0, keepdims=False)

    def forward_tick(tick, carry):
        saved, arrived = carry
        index = tick - section
        valid = (index >= 0) & (index < micro)
        clipped = jnp.clip(index, 0, micro - 1)
        entering = jnp.where(section == 0, at(assigned, clipped), arrived)
        kept = jnp.where(valid, entering, at(saved, clipped))
        saved = lax.dynamic_update_index_in_dim(saved, kept, clipped, 0)
        segment = at(seg_groups, clipped)

        def run_layer(value):
            return attend(value.astype(F32), segment, gain_row, w_layer, out_layer).astype(BF16)

        leaving = lax.cond(valid, run_layer, jnp.zeros_like, entering)
        return (saved, passed_along(leaving, 1))

    saved_init = jnp.zeros((micro, MB_ROWS, length, width), BF16)
    arrive_init = jnp.zeros((MB_ROWS, length, width), BF16)
    saved, _ = lax.fori_loop(0, ticks, forward_tick, (saved_init, arrive_init))

    def backward_tick(tick, carry):
        grads_x, gain_total, arrived = carry
        index = tick - (sections - 1 - section)
        valid = (index >= 0) & (index < micro)
        clipped = jnp.clip(index, 0, micro - 1)
        entering = jnp.where(section == sections - 1, at(grad_rows, clipped), arrived)
        segment = at(seg_groups, clipped)
        stored = at(saved, clipped).astype(F32)

        def local_layer(hidden, gains_here):
            return attend(hidden, segment, gains_here, w_layer, out_layer)

        def run_back(value):
            _, pullback = jax.vjp(local_layer, stored, gain_row)
            grad_hidden, grad_gain = pullback(value.astype(F32))
            return (grad_hidden.astype(BF16), grad_gain)

        def skip_back(value):
            return (jnp.zeros_like(value), jnp.zeros(gain_row.shape, F32))

        sending, grad_gain = lax.cond(valid, run_back, skip_back, entering)
        kept = jnp.where(valid, sending, at(grads_x, clipped))
        grads_x = lax.dynamic_update_index_in_dim(grads_x, kept, clipped, 0)
        return (grads_x, gain_total + grad_gain, passed_along(sending, -1))

    gain_init = jnp.zeros(gain_row.shape, F32)
    grads_x, gain_total, _ = lax.fori_loop(
        0, ticks, backward_tick, (saved_init, gain_init, arrive_init)
    )
    gain_whole = lax.psum(gain_total, ("dp", "group"))
    return (grads_x.reshape(1, rows_dev * length, width), gain_whole[None])


def solution(mesh):
    placed = (
        P(("dp", "group"), None),
        P(("dp", "group"), None),
        P("section", None),
        P("section", None, None),
        P("section", None, None),
        P(("dp", "group"), None),
        P(("dp", "group"), None),
    )

    def chosen(tokens_in, cotangent, gains, w_qkv, w_out, segments, plan):
        sections, head, width = w_out.shape
        devices = mesh.shape["dp"]
        small = sections * 4 * head < width and sections > 1
        halves = devices & (devices - 1) == 0 and sections & (sections - 1) == 0
        body = local if small and halves else relay
        return jax.shard_map(
            body,
            mesh=mesh,
            in_specs=placed,
            out_specs=(P("section", ("dp", "group"), None), P("section", None)),
            check_vma=False,
        )(tokens_in, cotangent, gains, w_qkv, w_out, segments, plan)

    return chosen
```

```python
import math

import jax
import jax.numpy as jnp
from jax import lax
from jax.experimental import pallas as pl
from jax.experimental.pallas import tpu as pltpu
from jax.sharding import PartitionSpec as P

EPS = 1e-05
VMEM_BYTES = 24 * 1024 * 1024
SMALL = 16 * 1024 * 1024
F32 = jnp.float32
BF16 = jnp.bfloat16


def dot_nn(a, b):
    return lax.dot_general(a, b, (((1,), (0,)), ((), ())), preferred_element_type=F32)


def dot_nt(a, b):
    return lax.dot_general(a, b, (((1,), (1,)), ((), ())), preferred_element_type=F32)


def dot_tn(a, b):
    return lax.dot_general(a, b, (((0,), (0,)), ((), ())), preferred_element_type=F32)


IN_HBM = pl.BlockSpec(memory_space=pltpu.HBM)
ANYWHERE = pl.BlockSpec(memory_space=pl.ANY)
IN_VMEM = pl.BlockSpec(memory_space=pltpu.VMEM)
IN_SMEM = pl.BlockSpec(memory_space=pltpu.SMEM)


def in_hbm(array):
    return pltpu.with_memory_space_constraint(array, pltpu.HBM)


def in_vmem(array):
    return pltpu.with_memory_space_constraint(array, pltpu.VMEM)


def mover(sems):
    used = []

    def start(source, target):
        copy = pltpu.make_async_copy(source, target, sems.at[len(used)])
        copy.start()
        used.append(copy)
        return copy

    return start


def steps(width):
    step = min(width, 1024)
    return [slice(at, at + step) for at in range(0, width, step)]


def params(limit=VMEM_BYTES):
    return pltpu.CompilerParams(vmem_limit_bytes=limit)


def pick(tokens, plan, place, groups, out_layer, mine, slice_rows):
    rows, length, width = tokens.shape
    share = rows // groups

    def kernel(plan_ref, place_ref, mine_ref, tokens_ref, o_ref, *rest):
        slice_ref, parts = rest[0], rest[1 : 1 + groups]
        slice_in, rows_in, sems = rest[1 + groups :]
        start = mover(sems)
        at = pl.ds(pl.multiple_of(mine_ref[0] * slice_rows, slice_rows), slice_rows)
        loads = [(start(o_ref.at[at], slice_in), slice_in, slice_ref)]
        for r in range(groups):
            target = lax.rem(place_ref[0] + r, groups)
            for c in range(share):
                here = rows_in.at[r * share + c]
                row = plan_ref[0, target * share + c]
                loads.append((start(tokens_ref.at[row], here), here, parts[r].at[c]))
        stores = []
        for load, here, there in loads:
            load.wait()
            stores.append(start(here, there))
        for store in stores:
            store.wait()

    return pl.pallas_call(
        kernel,
        out_shape=[pltpu.HBM((slice_rows, width), BF16)]
        + [pltpu.HBM((share, length, width), BF16)] * groups,
        in_specs=[IN_SMEM, IN_SMEM, IN_SMEM, IN_HBM, IN_HBM],
        out_specs=[IN_HBM] * (1 + groups),
        scratch_shapes=[
            pltpu.VMEM((slice_rows, width), BF16),
            pltpu.VMEM((rows, length, width), BF16),
            pltpu.SemaphoreType.DMA((2 * rows + 2,)),
        ],
        compiler_params=params(),
        name="pick",
    )(plan, place, mine, in_hbm(tokens), in_hbm(out_layer))


def project(parts, cotangent, gain, w_layer, out_layer, place, after):
    groups = len(parts)
    tokens, width = cotangent.shape
    head = out_layer.shape[0]
    wide = w_layer.shape[1]
    block = tokens // groups
    cuts = steps(width)
    copies = len(cuts) * (groups + 4)

    def kernel(place_ref, *refs):
        part_refs = refs[:groups]
        cot_ref, g_ref, w_ref, o_ref = refs[groups : groups + 4]
        x_ref, xz_ref, n_ref = refs[groups + 4 + len(after) : groups + 7 + len(after)]
        x_in, c_in, w_in, o_in, sems = refs[groups + 7 + len(after) :]
        start = mover(sems)
        loads = []
        for cut in cuts:
            mine = [start(w_ref.at[cut], w_in.at[cut])]
            mine.append(start(o_ref.at[:, cut], o_in.at[:, cut]))
            for r in range(groups):
                source = lax.rem(place_ref[0] + groups - r, groups)
                rows = pl.ds(pl.multiple_of(source * block, block), block)
                mine.append(start(part_refs[r].at[:, cut], x_in.at[rows, cut]))
            mine.append(start(cot_ref.at[:, cut], c_in.at[:, cut]))
            loads.append(mine)
        through = jnp.zeros((tokens, wide), F32)
        across = jnp.zeros((tokens, head), F32)
        back = jnp.zeros((tokens, head), F32)
        square = jnp.zeros((tokens, 1), F32)
        stores = []
        for cut, mine in zip(cuts, loads):
            for load in mine:
                load.wait()
            stores.append(start(x_in.at[:, cut], x_ref.at[:, cut]))
            x = x_in[:, cut]
            xf = x.astype(F32)
            through += dot_nn((xf * g_ref[:, cut]).astype(BF16), w_in[cut, :])
            across += dot_nt(x, o_in[:, cut])
            back += dot_nt(c_in[:, cut], o_in[:, cut])
            square += jnp.sum(xf * xf, axis=1, keepdims=True)
        xz_ref[:, :wide] = through.astype(BF16)
        xz_ref[:, wide : wide + head] = across.astype(BF16)
        xz_ref[:, wide + head :] = back.astype(BF16)
        n_ref[...] = square
        for store in stores:
            store.wait()

    return pl.pallas_call(
        kernel,
        out_shape=[
            pltpu.HBM((tokens, width), BF16),
            jax.ShapeDtypeStruct((tokens, wide + 2 * head), BF16),
            jax.ShapeDtypeStruct((tokens, 1), F32),
        ],
        in_specs=[IN_SMEM]
        + [ANYWHERE] * groups
        + [IN_HBM, IN_VMEM, IN_HBM, IN_HBM]
        + [ANYWHERE] * len(after),
        out_specs=[IN_HBM, IN_VMEM, IN_VMEM],
        scratch_shapes=[
            pltpu.VMEM((tokens, width), BF16),
            pltpu.VMEM((tokens, width), BF16),
            pltpu.VMEM((width, wide), BF16),
            pltpu.VMEM((head, width), BF16),
            pltpu.SemaphoreType.DMA((copies,)),
        ],
        compiler_params=params(),
        name="project",
    )(
        place,
        in_hbm(parts[0]),
        *[in_vmem(part) for part in parts[1:]],
        in_hbm(cotangent),
        gain,
        in_hbm(w_layer),
        in_hbm(out_layer),
        *after,
    )


def couple(slices, gain, w_layer, out_layer, last, after):
    sections = len(slices)
    count, width = slices[0].shape
    head = out_layer.shape[0]
    wide = w_layer.shape[1]
    below = (sections - 2) * wide
    packed = below + max(wide, (sections - 1) * head)
    cuts = steps(width)
    copies = len(cuts) * (sections + 2) + sections - 1

    def kernel(last_ref, *refs):
        s_refs = refs[:sections][::-1]
        g_ref, w_ref, o_ref = refs[sections : sections + 3]
        out_ref, stack_ref, r_in, w_in, o_in, sems = refs[sections + 3 + len(after) :]
        rows = [slice(r * count, (r + 1) * count) for r in range(sections)]
        start = mover(sems)
        loads = []
        for cut in cuts:
            mine = [start(w_ref.at[cut], w_in.at[cut])]
            mine.append(start(o_ref.at[:, cut], o_in.at[:, cut]))
            for r in range(sections):
                mine.append(start(s_refs[r].at[:, cut], r_in.at[rows[r], cut]))
            loads.append(mine)
        through = jnp.zeros((sections * count, wide), F32)
        across = jnp.zeros((sections * count, head), F32)
        for cut, mine in zip(cuts, loads):
            for load in mine:
                load.wait()
            r = r_in[:, cut]
            through += dot_nn((r.astype(F32) * g_ref[:, cut]).astype(BF16), w_in[cut, :])
            across += dot_nt(r, o_in[:, cut])
        stores = [start(r_in.at[rows[r]], stack_ref.at[r - 1]) for r in range(1, sections)]
        through = through.astype(BF16)
        across = across.astype(BF16)
        out_ref[...] = jnp.zeros_like(out_ref)
        for r in range(1, sections - 1):
            out_ref[:, (r - 1) * wide : r * wide] = through[rows[r]]

        @pl.when(last_ref[0] == 1)
        def _():
            out_ref[:, below : below + wide] = through[rows[-1]]

        @pl.when(last_ref[0] == 0)
        def _():
            for r in range(sections - 1):
                out_ref[:, below + r * head : below + (r + 1) * head] = across[rows[r]]

        for store in stores:
            store.wait()

    return pl.pallas_call(
        kernel,
        out_shape=[
            jax.ShapeDtypeStruct((count, packed), BF16),
            pltpu.HBM((sections - 1, count, width), BF16),
        ],
        in_specs=[IN_SMEM]
        + [ANYWHERE] * sections
        + [IN_VMEM, IN_HBM, IN_HBM]
        + [ANYWHERE] * len(after),
        out_specs=[IN_VMEM, IN_HBM],
        scratch_shapes=[
            pltpu.VMEM((sections * count, width), BF16),
            pltpu.VMEM((width, wide), BF16),
            pltpu.VMEM((head, width), BF16),
            pltpu.SemaphoreType.DMA((copies,)),
        ],
        compiler_params=params(),
        name="couple",
    )(last, *slices[::-1], gain, in_hbm(w_layer), in_hbm(out_layer), *after)


def layout(sections, wide, head):
    through, across, at = {}, {}, 0
    for k in range(sections):
        for j in range(k):
            through[j, k] = slice(at, at + wide)
            at += wide
        for j in range(k + 1 if k < sections - 1 else 0):
            across[j, k] = slice(at, at + head)
            at += head
    return through, across, at


def compact(parts, section, wide, head, after):
    sections = len(parts)
    count = parts[0].shape[0]
    below = (sections - 2) * wide
    through, across, total = layout(sections, wide, head)

    def kernel(s_ref, *refs):
        part_refs, out_ref = refs[:sections], refs[-1]
        mine = s_ref[0]

        def fill(k, r):
            for j in range(k):
                at = (k - j - 1) * wide
                out_ref[0, :, through[j, k]] = part_refs[r][:, at : at + wide]
            for j in range(k + 1 if k < sections - 1 else 0):
                at = below + (k - j) * head
                out_ref[0, :, across[j, k]] = part_refs[r][:, at : at + head]

        for s in range(sections):

            @pl.when(mine == s)
            def _(s=s):
                for r in range(sections):
                    fill((s - r) % sections, r)

    vmem = pl.BlockSpec(memory_space=pltpu.VMEM)
    return pl.pallas_call(
        kernel,
        out_shape=jax.ShapeDtypeStruct((1, count, total), BF16),
        in_specs=[IN_SMEM] + [vmem] * sections + [ANYWHERE] * len(after),
        out_specs=vmem,
        compiler_params=params(SMALL),
        name="compact",
    )(section, *parts, *after)


def merge(first, second, after):
    count = first.shape[0]

    def kernel(first_ref, second_ref, *refs):
        refs[-1][:count] = first_ref[...]
        refs[-1][count:] = second_ref[...]

    return pl.pallas_call(
        kernel,
        out_shape=jax.ShapeDtypeStruct((2 * count,) + first.shape[1:], first.dtype),
        in_specs=[IN_VMEM] * 2 + [ANYWHERE] * len(after),
        out_specs=IN_VMEM,
        compiler_params=params(SMALL),
        name="merge",
    )(first, second, *after)


def serial(xz, pieces, places, norms, mask, section, gain, w_layer, out_layer, streams):
    sections = len(xz)
    tokens = norms.shape[0]
    head, width = out_layer.shape
    wide = 3 * head
    scale = 1.0 / math.sqrt(head)
    lead = slice(0, streams[-1].stop)
    through_at, across_at, _ = layout(sections, wide, head)
    count, packed = pieces[0].shape[-2:]
    plane = head // count
    n_in = sections + len(pieces)
    copies = sections + plane + 4

    def kernel(s_ref, p_ref, *refs):
        xz_refs, piece_refs = refs[:sections], refs[sections:n_in]
        n_ref, mask_ref, g_ref, w_ref, o_ref = refs[n_in : n_in + 5]
        n_out = n_in + 5
        v_ref, t_out, a_out = refs[n_out : n_out + 3]
        first_refs = refs[n_out + 3 : n_out + 3 + len(streams)]
        scratch = refs[n_out + 3 + len(streams) :]
        xz_all, table, mixes, weights, projs, dmix, w_in, o_in, t_ref, a_ref, sems = scratch
        mine = s_ref[0]
        started = []

        def start(source, target):
            copy = pltpu.make_async_copy(source, target, sems.at[len(started)])
            copy.start()
            started.append(copy)

        for r in range(sections):
            start(xz_refs[r], xz_all.at[mine ^ r])
        at = 0
        for ref in piece_refs:
            for i in range(ref.shape[0]):
                start(ref.at[i], table.at[p_ref[at]])
                at += 1
        small = list(started)
        start(w_ref.at[lead], w_in)
        start(o_ref.at[:, lead], o_in)
        for copy in small:
            copy.wait()

        def through(j, k):
            return table[:, :, through_at[j, k]].reshape(head, wide)

        def across(j, k):
            return table[:, :, across_at[j, k]].reshape(head, head)

        allowed = mask_ref[...] > 0.5
        norm = n_ref[...]
        rstds, tails, mixed = [], [], []
        for s in range(sections):
            proj = xz_all[s, :, :wide].astype(F32)
            for j in range(s):
                proj = proj + dot_nn(mixed[j], through(j, s))
            rstd = lax.rsqrt(norm * (1.0 / width) + EPS)
            proj = proj * rstd
            projs[s] = proj.astype(BF16)
            q, k, v = (projs[s, :, i * head : (i + 1) * head] for i in range(3))
            scores = jnp.where(allowed, dot_nt(q, k) * scale, -1e30)
            scores = jnp.exp(scores - jnp.max(scores, axis=1, keepdims=True))
            soft = scores / jnp.sum(scores, axis=1, keepdims=True)
            weights[s] = soft
            mix = dot_nn(soft.astype(BF16), v).astype(BF16)
            mixed.append(mix)
            mixes[:, s * head : (s + 1) * head] = mix
            rstds.append(rstd)
            dmix[:, s * head : (s + 1) * head] = xz_all[s, :, wide + head :].astype(F32)
            if s == sections - 1:
                break
            y = xz_all[s, :, wide : wide + head].astype(F32)
            for j in range(s):
                y = y + dot_nn(mixed[j], across(j, s))
            tail = y + dot_nn(mix, across(s, s))
            norm = norm + jnp.sum(mix.astype(F32) * (y + tail), axis=1, keepdims=True)
            norm = jnp.maximum(norm, 0.0)
            tails.append(tail)
        total = jnp.zeros((tokens, 1), F32)
        a_ref[...] = jnp.zeros_like(a_ref)
        for s in reversed(range(sections)):
            cols = slice(s * head, (s + 1) * head)
            da = dmix[:, cols]
            if s < sections - 1:
                da = da - total * tails[s]
            da = da.astype(BF16)
            q, k, v = (projs[s, :, i * head : (i + 1) * head] for i in range(3))
            soft = weights[s]
            dv = dot_tn(soft.astype(BF16), da)
            dsoft = dot_nt(da, v)
            dscore = soft * (dsoft - jnp.sum(dsoft * soft, axis=1, keepdims=True))
            dscore = (dscore * scale).astype(BF16)
            dproj = jnp.concatenate([dot_nn(dscore, k), dot_tn(dscore, q), dv], axis=1)
            along = jnp.sum(dproj * projs[s].astype(F32), axis=1, keepdims=True)
            first = (dproj * rstds[s]).astype(BF16)
            second = (-total * mixes[:, cols].astype(F32)).astype(BF16)
            total = total + rstds[s] * rstds[s] * along * (1.0 / width)
            for j in reversed(range(s)):
                term = dot_nt(first, through(j, s))
                if s < sections - 1:
                    term = term + dot_nt(second, across(j, s))
                dmix[:, j * head : (j + 1) * head] += term

            @pl.when(mine == s)
            def _(first=first, second=second, total=total):
                v_ref[:, :wide] = first
                v_ref[:, wide:] = second
                t_ref[...] = total

            for r in range(1, sections - s):

                @pl.when(mine == s + r)
                def _(r=r, cols=cols):
                    a_ref[:, (r - 1) * head : r * head] = mixes[:, cols]

        weights_in = started[len(small) :]
        start(t_ref, t_out)
        start(a_ref, a_out)
        for copy in weights_in:
            copy.wait()
        own = dot_nt(v_ref[:, :wide], w_in[...]) * g_ref[:, lead]
        own = (own + dot_nn(v_ref[:, wide:], o_in[...])).astype(BF16)
        for ref, part in zip(first_refs, streams):
            ref[...] = own[:, part]
        for copy in started[-2:]:
            copy.wait()

    vmem = pl.BlockSpec(memory_space=pltpu.VMEM)
    smem = pl.BlockSpec(memory_space=pltpu.SMEM)
    return pl.pallas_call(
        kernel,
        out_shape=[
            pltpu.VMEM((tokens, wide + head), BF16),
            pltpu.HBM((tokens, 1), F32),
            pltpu.HBM((tokens, (sections - 1) * head), BF16),
        ]
        + [pltpu.VMEM((tokens, part.stop - part.start), BF16) for part in streams],
        in_specs=[smem, smem] + [ANYWHERE] * n_in + [vmem, vmem, vmem, IN_HBM, IN_HBM],
        out_specs=[vmem, IN_HBM, IN_HBM] + [vmem] * len(streams),
        scratch_shapes=[
            pltpu.VMEM((sections,) + xz[0].shape, BF16),
            pltpu.VMEM((plane, count, packed), BF16),
            pltpu.VMEM((tokens, sections * head), BF16),
            pltpu.VMEM((sections, tokens, tokens), F32),
            pltpu.VMEM((sections, tokens, wide), BF16),
            pltpu.VMEM((tokens, sections * head), F32),
            pltpu.VMEM((lead.stop, wide), BF16),
            pltpu.VMEM((head, lead.stop), BF16),
            pltpu.VMEM((tokens, 1), F32),
            pltpu.VMEM((tokens, (sections - 1) * head), BF16),
            pltpu.SemaphoreType.DMA((copies,)),
        ],
        compiler_params=params(),
        name="serial",
    )(
        section,
        places,
        *xz,
        *pieces,
        norms,
        mask,
        gain,
        in_hbm(w_layer),
        in_hbm(out_layer),
    )


def hold(array, after):
    def kernel(*refs):
        pass

    return pl.pallas_call(
        kernel,
        out_shape=jax.ShapeDtypeStruct(array.shape, array.dtype),
        in_specs=[ANYWHERE] * (1 + len(after)),
        out_specs=ANYWHERE,
        input_output_aliases={0: 0},
        compiler_params=params(SMALL),
        name="hold",
    )(array, *after)


def gather_two(first, second, after):
    count = first.shape[0]

    def kernel(first_ref, second_ref, *refs):
        out_ref, sems = refs[len(after) :]
        start = mover(sems)
        copies = [start(first_ref, out_ref.at[:count]), start(second_ref, out_ref.at[count:])]
        for copy in copies:
            copy.wait()

    return pl.pallas_call(
        kernel,
        out_shape=jax.ShapeDtypeStruct((2 * count,) + first.shape[1:], first.dtype),
        in_specs=[ANYWHERE] * (2 + len(after)),
        out_specs=IN_VMEM,
        scratch_shapes=[pltpu.SemaphoreType.DMA((2,))],
        compiler_params=params(SMALL),
        name="gather_two",
    )(first, second, *after)


def widen(sent, gain, w_layer, out_layer, chunk):
    tokens = sent.shape[0]
    head, width = out_layer.shape
    wide = w_layer.shape[1]
    cuts = [slice(at, at + chunk) for at in range(0, width, chunk)]

    def kernel(v_ref, g_ref, w_ref, o_ref, back_ref, pair_ref, back_in, w_in, o_in, sems):
        start = mover(sems)
        loads = [
            (start(w_ref.at[cut], w_in.at[cut]), start(o_ref.at[:, cut], o_in.at[:, cut]))
            for cut in cuts
        ]
        stores = []
        for i, (cut, mine) in enumerate(zip(cuts, loads)):
            for load in mine:
                load.wait()
            back = dot_nt(v_ref[:, :wide], w_in[cut, :])
            own = back * g_ref[:, cut] + dot_nn(v_ref[:, wide:], o_in[:, cut])
            back_in[:, cut] = back.astype(BF16)
            stores.append(start(back_in.at[:, cut], back_ref.at[:, cut]))
            pair_ref[0, i] = own.astype(BF16)
            pair_ref[1, i] = jnp.zeros_like(pair_ref[1, i])
        for store in stores:
            store.wait()

    return pl.pallas_call(
        kernel,
        out_shape=[
            pltpu.HBM((tokens, width), BF16),
            pltpu.VMEM((2, len(cuts), tokens, chunk), BF16),
        ],
        in_specs=[IN_VMEM, IN_VMEM, IN_HBM, IN_HBM],
        out_specs=[IN_HBM, IN_VMEM],
        scratch_shapes=[
            pltpu.VMEM((tokens, width), BF16),
            pltpu.VMEM((width, wide), BF16),
            pltpu.VMEM((head, width), BF16),
            pltpu.SemaphoreType.DMA((3 * len(cuts),)),
        ],
        compiler_params=params(),
        name="widen",
    )(in_vmem(sent), gain, in_hbm(w_layer), in_hbm(out_layer))


def settle(total, mixes, stacks, places, x, cotangent, back, chunk, part, parts):
    tokens, width = x.shape
    layers, rows = stacks[0].shape[1:3]
    entries = [(i, e) for i, stack in enumerate(stacks) for e in range(stack.shape[0])]
    plane = len(entries)
    head = plane * rows
    span = width // parts
    base = part * span
    cuts = [slice(at, at + chunk) for at in range(0, span, chunk)]
    copies = plane * layers + 3 * len(cuts) + 2

    def kernel(p_ref, t_far, a_far, x_ref, c_ref, back_ref, *refs):
        stack_refs = refs[: len(stacks)]
        rest_ref, dg_ref = refs[len(stacks) : len(stacks) + 2]
        lower, x_in, c_in, back_in, t_ref, a_ref, sems = refs[len(stacks) + 2 :]
        start = mover(sems)
        first = [start(t_far, t_ref), start(a_far, a_ref)]
        for at, (i, e) in enumerate(entries):
            for r in range(layers):
                here = pl.ds(base, span)
                first.append(start(stack_refs[i].at[e, r, :, here], lower.at[r, p_ref[at]]))
        loads = []
        for cut in cuts:
            there = pl.ds(base + cut.start, chunk)
            mine = [start(x_ref.at[:, there], x_in.at[:, cut])]
            mine.append(start(c_ref.at[:, there], c_in.at[:, cut]))
            mine.append(start(back_ref.at[:, there], back_in.at[:, cut]))
            loads.append(mine)
        for load in first:
            load.wait()
        for i, (cut, mine) in enumerate(zip(cuts, loads)):
            for load in mine:
                load.wait()
            below = lower[:, :, :, cut].reshape(layers * head, chunk)
            here = x_in[:, cut].astype(F32) + dot_nn(a_ref[...], below)
            rest_ref[i] = (c_in[:, cut].astype(F32) - t_ref[...] * here).astype(BF16)
            gain = jnp.sum(back_in[:, cut].astype(F32) * here, axis=0, keepdims=True)
            for at in range(0, chunk, head):
                row = (cut.start + at) // head
                dg_ref[row : row + 1, :] = gain[:, at : at + head]

    return pl.pallas_call(
        kernel,
        out_shape=[
            pltpu.VMEM((len(cuts), tokens, chunk), BF16),
            pltpu.VMEM((span // head, head), F32),
        ],
        in_specs=[IN_SMEM] + [IN_HBM] * (5 + len(stacks)),
        out_specs=[IN_VMEM] * 2,
        scratch_shapes=[
            pltpu.VMEM((layers, plane, rows, span), BF16),
            pltpu.VMEM((tokens, span), BF16),
            pltpu.VMEM((tokens, span), BF16),
            pltpu.VMEM((tokens, span), BF16),
            pltpu.VMEM((tokens, 1), F32),
            pltpu.VMEM((tokens, layers * head), BF16),
            pltpu.SemaphoreType.DMA((copies,)),
        ],
        compiler_params=params(),
        name="settle",
    )(
        places,
        *[in_hbm(array) for array in (total, mixes, x, cotangent, back, *stacks)],
    )


def join(index, arrived, pair, cols, after):
    tokens, part = arrived.shape

    def kernel(i_ref, r_ref, _, *refs):
        send_ref, pair_ref = refs[len(after) :]
        at = i_ref[0]
        r = r_ref[...]
        send_ref[...] = (pair_ref[0, at, :, cols].astype(F32) + r.astype(F32)).astype(BF16)
        pair_ref[1, at, :, cols] = r

    return pl.pallas_call(
        kernel,
        out_shape=[pltpu.VMEM((tokens, part), BF16), pltpu.VMEM(pair.shape, BF16)],
        in_specs=[IN_SMEM] + [IN_VMEM] * 2 + [ANYWHERE] * len(after),
        out_specs=[IN_VMEM] * 2,
        input_output_aliases={2: 1},
        compiler_params=params(SMALL),
        name="join",
    )(index, in_vmem(arrived), in_vmem(pair), *after)


def join_last(index, arrived, pair, streams, after):
    _, _, tokens, chunk = pair.shape

    def kernel(i_ref, *refs):
        r_refs = refs[: len(streams)]
        send_ref, pair_ref = refs[len(streams) + 1 + len(after) :]
        at = i_ref[0]
        for ref, cols in zip(r_refs, streams):
            r = ref[...]
            send = pair_ref[0, at, :, cols].astype(F32) + r.astype(F32)
            send_ref[:, cols] = send.astype(BF16)
            pair_ref[1, at, :, cols] = r

    return pl.pallas_call(
        kernel,
        out_shape=[pltpu.VMEM((tokens, chunk), BF16), pltpu.VMEM(pair.shape, BF16)],
        in_specs=[IN_SMEM] + [IN_VMEM] * (len(streams) + 1) + [ANYWHERE] * len(after),
        out_specs=[IN_VMEM] * 2,
        input_output_aliases={len(streams) + 1: 1},
        compiler_params=params(SMALL),
        name="join_last",
    )(index, *[in_vmem(array) for array in (*arrived, pair)], *after)


def finish(index, arrived, pair, rests, streams):
    _, count, tokens, chunk = pair.shape

    def kernel(i_ref, *refs):
        r_refs = refs[: len(streams)]
        pair_ref, rest_refs = refs[len(streams)], refs[len(streams) + 1 :][: len(rests)]
        whole_ref, whole, sems = refs[len(streams) + 1 + len(rests) :]
        each = count // len(rests)
        at = i_ref[0]
        copies = []
        for i in range(count):
            full = rest_refs[i // each][i % each].astype(F32) + pair_ref[0, i].astype(F32)
            whole[i] = (full + pair_ref[1, i].astype(F32)).astype(BF16)

            @pl.when(at == i)
            def _(i=i, full=full):
                for ref, cols in zip(r_refs, streams):
                    whole[i, :, cols] = (full[:, cols] + ref[...].astype(F32)).astype(BF16)

            there = whole_ref.at[:, pl.ds(i * chunk, chunk)]
            copies.append(pltpu.make_async_copy(whole.at[i], there, sems.at[i]))
            copies[-1].start()
        for copy in copies:
            copy.wait()

    return pl.pallas_call(
        kernel,
        out_shape=pltpu.HBM((tokens, count * chunk), BF16),
        in_specs=[IN_SMEM] + [IN_VMEM] * (len(streams) + 1 + len(rests)),
        out_specs=IN_HBM,
        scratch_shapes=[
            pltpu.VMEM((count, tokens, chunk), BF16),
            pltpu.SemaphoreType.DMA((count,)),
        ],
        compiler_params=params(SMALL),
        name="finish",
    )(index, *[in_vmem(array) for array in (*arrived, pair, *rests)])


def stacked(arrays):
    rows = arrays[0].shape[0]

    def kernel(*refs):
        for i, ref in enumerate(refs[:-1]):
            refs[-1][i * rows : (i + 1) * rows, :] = ref[...]

    return pl.pallas_call(
        kernel,
        out_shape=pltpu.VMEM((len(arrays) * rows, arrays[0].shape[1]), F32),
        in_specs=[IN_VMEM] * len(arrays),
        out_specs=IN_VMEM,
        compiler_params=params(SMALL),
        name="stacked",
    )(*[in_vmem(array) for array in arrays])


def added(arrays):
    def kernel(*refs):
        total = refs[0][...]
        for ref in refs[1:-1]:
            total = total + ref[...]
        refs[-1][...] = total

    return pl.pallas_call(
        kernel,
        out_shape=pltpu.VMEM(arrays[0].shape, F32),
        in_specs=[IN_VMEM] * len(arrays),
        out_specs=IN_VMEM,
        compiler_params=params(SMALL),
        name="added",
    )(*[in_vmem(array) for array in arrays])


STREAMS = 2
CHUNKS = 4
PARTS = 1


def stream_columns(chunk):
    lanes = 128
    tiles = chunk // lanes
    ends = [-(-tiles * (i + 1) // STREAMS) * lanes for i in range(STREAMS)]
    return [slice(start, end) for start, end in zip([0] + ends, ends)]


def shifted(array, by):
    sections = lax.axis_size("section")
    return lax.ppermute(array, "section", [(i, (i + by) % sections) for i in range(sections)])


def raised(array, by):
    sections = lax.axis_size("section")
    return lax.ppermute(array, "section", [(i, i + by) for i in range(sections - by)])


def swapped(array, step):
    groups = lax.axis_size("group")
    devices = lax.axis_size("dp")
    bits = devices.bit_length() - 1
    pairs = []
    for p in range(devices):
        for g in range(groups):
            pairs.append((p * groups + g, (p ^ (1 << ((step + g) % bits))) * groups + g))
    return lax.ppermute(array, ("dp", "group"), pairs)


def handed(array, by):
    groups = lax.axis_size("group")
    return lax.ppermute(array, "group", [(i, (i + by) % groups) for i in range(groups)])


def plane_places():
    groups = lax.axis_size("group")
    bits = lax.axis_size("dp").bit_length() - 1
    masks = []
    for g in range(groups):
        order = [0]
        for step in range(bits):
            order = order + [m ^ (1 << ((step + g) % bits)) for m in order]
        masks.append(order)
    masks = jnp.asarray(masks, jnp.int32)
    dp, member = lax.axis_index("dp"), lax.axis_index("group")
    places = []
    for r in range(groups):
        giver = (member + groups - r) % groups
        places.append((dp ^ masks[giver]) * groups + giver)
    return jnp.concatenate(places).astype(jnp.int32)


def local(tokens_in, cotangent, gains, w_qkv, w_out, segments, plan):
    sections = lax.axis_size("section")
    groups = lax.axis_size("group")
    devices = lax.axis_size("dp")
    plane = devices * groups
    section = lax.axis_index("section")
    member = lax.axis_index("group")
    rows_dev = plan.shape[1]
    length = segments.shape[1]
    tokens, width = tokens_in.shape
    head = w_out.shape[1]
    share = rows_dev // groups
    w_layer, out_layer = w_qkv[0], w_out[0]
    place = member.astype(jnp.int32)[None]
    layer = section.astype(jnp.int32)[None]

    slice_rows = head // plane
    mine = lax.axis_index("dp") * groups + member
    own_rows, *parts = pick(
        tokens_in.reshape(rows_dev, length, width),
        plan,
        place,
        groups,
        out_layer,
        mine.astype(jnp.int32)[None],
        slice_rows,
    )
    slices = [raised(own_rows, r) for r in range(sections - 1, 0, -1)]
    slices = [own_rows] + slices[::-1]
    chosen = jnp.take(segments, plan[0], axis=0, mode="clip").astype(BF16)
    chosen = chosen.reshape(groups, share, length)
    moved, moved_seg = [], []
    for r in range(groups):
        outgoing = lax.dynamic_index_in_dim(chosen, (member + r) % groups, 0, keepdims=False)
        moved.append(handed(parts[r], r) if r else parts[r])
        moved_seg.append(handed(outgoing, r) if r else outgoing)
    moved = [part.reshape(share * length, width) for part in moved]
    order = (member - jnp.arange(groups)) % groups
    seg = jnp.take(jnp.stack(moved_seg), order, axis=0, mode="clip").reshape(tokens)
    at = jnp.arange(tokens)
    mask = (
        (at[:, None] >= at[None, :])
        & (at[:, None] // length == at[None, :] // length)
        & (seg[:, None] == seg[None, :])
    ).astype(F32)

    last = (section == sections - 1).astype(jnp.int32)[None]
    bits = devices.bit_length() - 1
    places = plane_places()
    x, xz, norms = project(
        moved, cotangent, gains, w_layer, out_layer, place, []
    )
    coupling, stack = couple(slices, gains, w_layer, out_layer, last, [mask, places, xz])
    others = [shifted(coupling, r) for r in range(1, sections)]

    streams = stream_columns(width // CHUNKS)

    def facing(array, by):
        return lax.ppermute(array, "section", [(i, i ^ by) for i in range(sections)])

    arrays, masks, by = [hold(xz, others)], [0], sections // 2
    while by > 0:
        arrays = arrays + [facing(array, by) for array in arrays]
        masks = masks + [mask_of ^ by for mask_of in masks]
        by = by // 2
    xz_all = [arrays[masks.index(r)] for r in range(sections)]
    early = [xz_all[r] for r in range(1, sections) if r & (r - 1) == 0]
    late = [xz_all[r] for r in range(1, sections) if r & (r - 1) != 0]
    pieces = [compact([coupling] + others, layer, 3 * head, head, [xz])]

    rows = [stack[None]]
    for step in range(bits):
        if step > 0:
            pieces = [merge(*pieces, early)]
        pieces = pieces + [swapped(pieces[0], step)]
        if step == bits - 1:
            pieces[-1] = hold(pieces[-1], late)
        if step > 0:
            rows = [gather_two(*rows, pieces[-1:])]
        rows = rows + [swapped(rows[0], step)]
    pieces = pieces + [handed(array, r) for r in range(1, groups) for array in pieces]
    sent, total, mixes, *leaving = serial(
        xz_all, pieces, places, norms, mask, layer, gains, w_layer, out_layer, streams
    )
    back, pair = widen(sent, gains, w_layer, out_layer, width // CHUNKS)

    down = [(i, i - 1) for i in range(1, sections)]
    behind = sections - 1 - section

    def index(tick):
        return jnp.clip(tick - behind, 0, CHUNKS - 1).astype(jnp.int32)[None]

    def lowered(arrays):
        return [lax.ppermute(array, "section", down) for array in arrays]

    ticks = CHUNKS + sections - 1
    after = {}
    for tick in range(1, ticks):
        arrived = lowered(leaving)
        waits = after.get(tick, [])
        if tick < ticks - 2:
            for i, cols in enumerate(streams):
                leaving[i], pair = join(index(tick), arrived[i], pair, cols, waits)
        elif tick < ticks - 1:
            last_out, pair = join_last(index(tick), arrived, pair, streams, waits)
            leaving = [last_out]
        if tick == 1:
            rows = [hold(array, leaving) for array in rows]
            rows = rows + [handed(array, r) for r in range(1, groups) for array in rows]
            rests, halves = [], []
            for part in range(PARTS):
                rest, half = settle(
                    total, mixes, rows, places, x, cotangent, back, width // CHUNKS, part, PARTS
                )
                rests.append(rest)
                halves.append(half)
            sums = [stacked(halves)]
            for step in range(bits):
                sums.append(added([sums[-1], swapped(sums[-1], step)]))
            sums.append(added(sums[-1:] + [handed(sums[-1], r) for r in range(1, groups)]))
            gain_whole = sums[-1].reshape(1, width)
            after = {2 + i: [array] for i, array in enumerate(sums)}
    whole = [slice(0, width // CHUNKS)]
    out = finish(index(ticks - 1), arrived, pair, rests, whole)
    return (out[None], gain_whole)


def attend(hidden, segment, gain_row, w_layer, out_layer):
    count, length, width = hidden.shape
    head = out_layer.shape[0]
    scaled = hidden * lax.rsqrt(jnp.mean(hidden * hidden, axis=-1, keepdims=True) + EPS) * gain_row
    normed = scaled.astype(BF16).reshape(count * length, width)
    projected = jnp.dot(normed, w_layer, preferred_element_type=F32).reshape(count, length, 3 * head)
    query = projected[:, :, :head]
    keyed = projected[:, :, head : 2 * head]
    valued = projected[:, :, 2 * head :]
    positions = jnp.arange(length)
    allowed = (positions[:, None] >= positions[None, :])[None] & (
        segment[:, :, None] == segment[:, None, :]
    )
    scores = jnp.einsum("rid,rjd->rij", query, keyed, precision=lax.Precision.HIGHEST)
    scores = jnp.where(allowed, scores / math.sqrt(head), -1e30)
    weights = jax.nn.softmax(scores, axis=-1)
    mixed = jnp.einsum("rij,rjd->rid", weights, valued, precision=lax.Precision.HIGHEST)
    mixed = mixed.astype(BF16).reshape(count * length, head)
    output = jnp.dot(mixed, out_layer, preferred_element_type=F32).reshape(count, length, width)
    return hidden + output


MB_ROWS = 2


def relay(tokens_in, cotangent, gains, w_qkv, w_out, segments, plan):
    sections = lax.axis_size("section")
    section = lax.axis_index("section")
    rows_dev = plan.shape[1]
    width = tokens_in.shape[1]
    length = segments.shape[1]
    micro = rows_dev // MB_ROWS
    blocks = tokens_in.reshape(rows_dev, length, width)
    chosen = jnp.take(blocks, plan[0], axis=0)
    chosen_seg = jnp.take(segments, plan[0], axis=0).astype(BF16)
    assigned = lax.all_to_all(chosen, "group", split_axis=0, concat_axis=0, tiled=True)
    moved_seg = lax.all_to_all(chosen_seg, "group", split_axis=0, concat_axis=0, tiled=True)
    assigned = assigned.reshape(micro, MB_ROWS, length, width)
    seg_groups = moved_seg.reshape(micro, MB_ROWS, length)
    gain_row, w_layer, out_layer = gains[0], w_qkv[0], w_out[0]
    grad_rows = cotangent.reshape(micro, MB_ROWS, length, width)
    ticks = micro + sections - 1

    def passed_along(array, by):
        pairs = [(i, i + by) for i in range(sections) if 0 <= i + by < sections]
        return lax.ppermute(array, "section", pairs)

    def at(array, i):
        return lax.dynamic_index_in_dim(array, i, 0, keepdims=False)

    def forward_tick(tick, carry):
        saved, arrived = carry
        index = tick - section
        valid = (index >= 0) & (index < micro)
        clipped = jnp.clip(index, 0, micro - 1)
        entering = jnp.where(section == 0, at(assigned, clipped), arrived)
        kept = jnp.where(valid, entering, at(saved, clipped))
        saved = lax.dynamic_update_index_in_dim(saved, kept, clipped, 0)
        segment = at(seg_groups, clipped)

        def run_layer(value):
            return attend(value.astype(F32), segment, gain_row, w_layer, out_layer).astype(BF16)

        leaving = lax.cond(valid, run_layer, jnp.zeros_like, entering)
        return (saved, passed_along(leaving, 1))

    saved_init = jnp.zeros((micro, MB_ROWS, length, width), BF16)
    arrive_init = jnp.zeros((MB_ROWS, length, width), BF16)
    saved, _ = lax.fori_loop(0, ticks, forward_tick, (saved_init, arrive_init))

    def backward_tick(tick, carry):
        grads_x, gain_total, arrived = carry
        index = tick - (sections - 1 - section)
        valid = (index >= 0) & (index < micro)
        clipped = jnp.clip(index, 0, micro - 1)
        entering = jnp.where(section == sections - 1, at(grad_rows, clipped), arrived)
        segment = at(seg_groups, clipped)
        stored = at(saved, clipped).astype(F32)

        def local_layer(hidden, gains_here):
            return attend(hidden, segment, gains_here, w_layer, out_layer)

        def run_back(value):
            _, pullback = jax.vjp(local_layer, stored, gain_row)
            grad_hidden, grad_gain = pullback(value.astype(F32))
            return (grad_hidden.astype(BF16), grad_gain)

        def skip_back(value):
            return (jnp.zeros_like(value), jnp.zeros(gain_row.shape, F32))

        sending, grad_gain = lax.cond(valid, run_back, skip_back, entering)
        kept = jnp.where(valid, sending, at(grads_x, clipped))
        grads_x = lax.dynamic_update_index_in_dim(grads_x, kept, clipped, 0)
        return (grads_x, gain_total + grad_gain, passed_along(sending, -1))

    gain_init = jnp.zeros(gain_row.shape, F32)
    grads_x, gain_total, _ = lax.fori_loop(
        0, ticks, backward_tick, (saved_init, gain_init, arrive_init)
    )
    gain_whole = lax.psum(gain_total, ("dp", "group"))
    return (grads_x.reshape(1, rows_dev * length, width), gain_whole[None])


def solution(mesh):
    placed = (
        P(("dp", "group"), None),
        P(("dp", "group"), None),
        P("section", None),
        P("section", None, None),
        P("section", None, None),
        P(("dp", "group"), None),
        P(("dp", "group"), None),
    )

    def chosen(tokens_in, cotangent, gains, w_qkv, w_out, segments, plan):
        sections, head, width = w_out.shape
        devices = mesh.shape["dp"]
        small = sections * 4 * head < width and sections > 1
        halves = devices & (devices - 1) == 0 and sections & (sections - 1) == 0
        body = local if small and halves else relay
        return jax.shard_map(
            body,
            mesh=mesh,
            in_specs=placed,
            out_specs=(P("section", ("dp", "group"), None), P("section", None)),
            check_vma=False,
        )(tokens_in, cotangent, gains, w_qkv, w_out, segments, plan)

    return chosen
```

```python
import math

import jax
import jax.numpy as jnp
from jax import lax
from jax.experimental import pallas as pl
from jax.experimental.pallas import tpu as pltpu
from jax.sharding import PartitionSpec as P

EPS = 1e-05
VMEM_BYTES = 24 * 1024 * 1024
SMALL = 16 * 1024 * 1024
F32 = jnp.float32
BF16 = jnp.bfloat16


def dot_nn(a, b):
    return lax.dot_general(a, b, (((1,), (0,)), ((), ())), preferred_element_type=F32)


def dot_nt(a, b):
    return lax.dot_general(a, b, (((1,), (1,)), ((), ())), preferred_element_type=F32)


def dot_tn(a, b):
    return lax.dot_general(a, b, (((0,), (0,)), ((), ())), preferred_element_type=F32)


IN_HBM = pl.BlockSpec(memory_space=pltpu.HBM)
ANYWHERE = pl.BlockSpec(memory_space=pl.ANY)
IN_VMEM = pl.BlockSpec(memory_space=pltpu.VMEM)
IN_SMEM = pl.BlockSpec(memory_space=pltpu.SMEM)


def in_hbm(array):
    return pltpu.with_memory_space_constraint(array, pltpu.HBM)


def in_vmem(array):
    return pltpu.with_memory_space_constraint(array, pltpu.VMEM)


def mover(sems):
    used = []

    def start(source, target):
        copy = pltpu.make_async_copy(source, target, sems.at[len(used)])
        copy.start()
        used.append(copy)
        return copy

    return start


def steps(width):
    step = min(width, 1024)
    return [slice(at, at + step) for at in range(0, width, step)]


def params(limit=VMEM_BYTES):
    return pltpu.CompilerParams(vmem_limit_bytes=limit)


def pick(tokens, plan, place, groups, out_layer, mine, slice_rows):
    rows, length, width = tokens.shape
    share = rows // groups

    def kernel(plan_ref, place_ref, mine_ref, tokens_ref, o_ref, *rest):
        slice_ref, parts = rest[0], rest[1 : 1 + groups]
        slice_in, rows_in, sems = rest[1 + groups :]
        start = mover(sems)
        at = pl.ds(pl.multiple_of(mine_ref[0] * slice_rows, slice_rows), slice_rows)
        loads = [(start(o_ref.at[at], slice_in), slice_in, slice_ref)]
        for r in range(groups):
            target = lax.rem(place_ref[0] + r, groups)
            for c in range(share):
                here = rows_in.at[r * share + c]
                row = plan_ref[0, target * share + c]
                loads.append((start(tokens_ref.at[row], here), here, parts[r].at[c]))
        stores = []
        for load, here, there in loads:
            load.wait()
            stores.append(start(here, there))
        for store in stores:
            store.wait()

    return pl.pallas_call(
        kernel,
        out_shape=[pltpu.HBM((slice_rows, width), BF16)]
        + [pltpu.HBM((share, length, width), BF16)] * groups,
        in_specs=[IN_SMEM, IN_SMEM, IN_SMEM, IN_HBM, IN_HBM],
        out_specs=[IN_HBM] * (1 + groups),
        scratch_shapes=[
            pltpu.VMEM((slice_rows, width), BF16),
            pltpu.VMEM((rows, length, width), BF16),
            pltpu.SemaphoreType.DMA((2 * rows + 2,)),
        ],
        compiler_params=params(),
        name="pick",
    )(plan, place, mine, in_hbm(tokens), in_hbm(out_layer))


def project(parts, cotangent, gain, w_layer, out_layer, place, after):
    groups = len(parts)
    tokens, width = cotangent.shape
    head = out_layer.shape[0]
    wide = w_layer.shape[1]
    block = tokens // groups
    cuts = steps(width)
    copies = len(cuts) * (groups + 4)

    def kernel(place_ref, *refs):
        part_refs = refs[:groups]
        cot_ref, g_ref, w_ref, o_ref = refs[groups : groups + 4]
        x_ref, xz_ref, n_ref = refs[groups + 4 + len(after) : groups + 7 + len(after)]
        x_in, c_in, w_in, o_in, sems = refs[groups + 7 + len(after) :]
        start = mover(sems)
        loads = []
        for cut in cuts:
            mine = [start(w_ref.at[cut], w_in.at[cut])]
            mine.append(start(o_ref.at[:, cut], o_in.at[:, cut]))
            for r in range(groups):
                source = lax.rem(place_ref[0] + groups - r, groups)
                rows = pl.ds(pl.multiple_of(source * block, block), block)
                mine.append(start(part_refs[r].at[:, cut], x_in.at[rows, cut]))
            mine.append(start(cot_ref.at[:, cut], c_in.at[:, cut]))
            loads.append(mine)
        through = jnp.zeros((tokens, wide), F32)
        across = jnp.zeros((tokens, head), F32)
        back = jnp.zeros((tokens, head), F32)
        square = jnp.zeros((tokens, 1), F32)
        stores = []
        for cut, mine in zip(cuts, loads):
            for load in mine:
                load.wait()
            stores.append(start(x_in.at[:, cut], x_ref.at[:, cut]))
            x = x_in[:, cut]
            xf = x.astype(F32)
            through += dot_nn((xf * g_ref[:, cut]).astype(BF16), w_in[cut, :])
            across += dot_nt(x, o_in[:, cut])
            back += dot_nt(c_in[:, cut], o_in[:, cut])
            square += jnp.sum(xf * xf, axis=1, keepdims=True)
        xz_ref[:, :wide] = through.astype(BF16)
        xz_ref[:, wide : wide + head] = across.astype(BF16)
        xz_ref[:, wide + head :] = back.astype(BF16)
        n_ref[...] = square
        for store in stores:
            store.wait()

    return pl.pallas_call(
        kernel,
        out_shape=[
            pltpu.HBM((tokens, width), BF16),
            jax.ShapeDtypeStruct((tokens, wide + 2 * head), BF16),
            jax.ShapeDtypeStruct((tokens, 1), F32),
        ],
        in_specs=[IN_SMEM]
        + [ANYWHERE] * groups
        + [IN_HBM, IN_VMEM, IN_HBM, IN_HBM]
        + [ANYWHERE] * len(after),
        out_specs=[IN_HBM, IN_VMEM, IN_VMEM],
        scratch_shapes=[
            pltpu.VMEM((tokens, width), BF16),
            pltpu.VMEM((tokens, width), BF16),
            pltpu.VMEM((width, wide), BF16),
            pltpu.VMEM((head, width), BF16),
            pltpu.SemaphoreType.DMA((copies,)),
        ],
        compiler_params=params(),
        name="project",
    )(
        place,
        in_hbm(parts[0]),
        *[in_vmem(part) for part in parts[1:]],
        in_hbm(cotangent),
        gain,
        in_hbm(w_layer),
        in_hbm(out_layer),
        *after,
    )


def couple(slices, gain, w_layer, out_layer, last, after):
    sections = len(slices)
    count, width = slices[0].shape
    head = out_layer.shape[0]
    wide = w_layer.shape[1]
    below = (sections - 2) * wide
    packed = below + max(wide, (sections - 1) * head)
    cuts = steps(width)
    copies = len(cuts) * (sections + 2) + sections - 1

    def kernel(last_ref, *refs):
        s_refs = refs[:sections][::-1]
        g_ref, w_ref, o_ref = refs[sections : sections + 3]
        out_ref, stack_ref, r_in, w_in, o_in, sems = refs[sections + 3 + len(after) :]
        rows = [slice(r * count, (r + 1) * count) for r in range(sections)]
        start = mover(sems)
        loads = []
        for cut in cuts:
            mine = [start(w_ref.at[cut], w_in.at[cut])]
            mine.append(start(o_ref.at[:, cut], o_in.at[:, cut]))
            for r in range(sections):
                mine.append(start(s_refs[r].at[:, cut], r_in.at[rows[r], cut]))
            loads.append(mine)
        through = jnp.zeros((sections * count, wide), F32)
        across = jnp.zeros((sections * count, head), F32)
        for cut, mine in zip(cuts, loads):
            for load in mine:
                load.wait()
            r = r_in[:, cut]
            through += dot_nn((r.astype(F32) * g_ref[:, cut]).astype(BF16), w_in[cut, :])
            across += dot_nt(r, o_in[:, cut])
        stores = [start(r_in.at[rows[r]], stack_ref.at[r - 1]) for r in range(1, sections)]
        through = through.astype(BF16)
        across = across.astype(BF16)
        out_ref[...] = jnp.zeros_like(out_ref)
        for r in range(1, sections - 1):
            out_ref[:, (r - 1) * wide : r * wide] = through[rows[r]]

        @pl.when(last_ref[0] == 1)
        def _():
            out_ref[:, below : below + wide] = through[rows[-1]]

        @pl.when(last_ref[0] == 0)
        def _():
            for r in range(sections - 1):
                out_ref[:, below + r * head : below + (r + 1) * head] = across[rows[r]]

        for store in stores:
            store.wait()

    return pl.pallas_call(
        kernel,
        out_shape=[
            jax.ShapeDtypeStruct((count, packed), BF16),
            pltpu.HBM((sections - 1, count, width), BF16),
        ],
        in_specs=[IN_SMEM]
        + [ANYWHERE] * sections
        + [IN_VMEM, IN_HBM, IN_HBM]
        + [ANYWHERE] * len(after),
        out_specs=[IN_VMEM, IN_HBM],
        scratch_shapes=[
            pltpu.VMEM((sections * count, width), BF16),
            pltpu.VMEM((width, wide), BF16),
            pltpu.VMEM((head, width), BF16),
            pltpu.SemaphoreType.DMA((copies,)),
        ],
        compiler_params=params(),
        name="couple",
    )(last, *slices[::-1], gain, in_hbm(w_layer), in_hbm(out_layer), *after)


def layout(sections, wide, head):
    through, across, at = {}, {}, 0
    for k in range(sections):
        for j in range(k):
            through[j, k] = slice(at, at + wide)
            at += wide
        for j in range(k + 1 if k < sections - 1 else 0):
            across[j, k] = slice(at, at + head)
            at += head
    return through, across, at


def compact(parts, section, wide, head, after):
    sections = len(parts)
    count = parts[0].shape[0]
    below = (sections - 2) * wide
    through, across, total = layout(sections, wide, head)

    def kernel(s_ref, *refs):
        part_refs, out_ref = refs[:sections], refs[-1]
        mine = s_ref[0]

        def fill(k, r):
            for j in range(k):
                at = (k - j - 1) * wide
                out_ref[0, :, through[j, k]] = part_refs[r][:, at : at + wide]
            for j in range(k + 1 if k < sections - 1 else 0):
                at = below + (k - j) * head
                out_ref[0, :, across[j, k]] = part_refs[r][:, at : at + head]

        for s in range(sections):

            @pl.when(mine == s)
            def _(s=s):
                for r in range(sections):
                    fill((s - r) % sections, r)

    vmem = pl.BlockSpec(memory_space=pltpu.VMEM)
    return pl.pallas_call(
        kernel,
        out_shape=jax.ShapeDtypeStruct((1, count, total), BF16),
        in_specs=[IN_SMEM] + [vmem] * sections + [ANYWHERE] * len(after),
        out_specs=vmem,
        compiler_params=params(SMALL),
        name="compact",
    )(section, *parts, *after)


def merge(first, second, after):
    count = first.shape[0]

    def kernel(first_ref, second_ref, *refs):
        refs[-1][:count] = first_ref[...]
        refs[-1][count:] = second_ref[...]

    return pl.pallas_call(
        kernel,
        out_shape=jax.ShapeDtypeStruct((2 * count,) + first.shape[1:], first.dtype),
        in_specs=[IN_VMEM] * 2 + [ANYWHERE] * len(after),
        out_specs=IN_VMEM,
        compiler_params=params(SMALL),
        name="merge",
    )(first, second, *after)


def serial(xz, pieces, places, norms, mask, section, gain, w_layer, out_layer, streams):
    sections = len(xz)
    tokens = norms.shape[0]
    head, width = out_layer.shape
    wide = 3 * head
    scale = 1.0 / math.sqrt(head)
    lead = slice(0, streams[-1].stop)
    through_at, across_at, _ = layout(sections, wide, head)
    count, packed = pieces[0].shape[-2:]
    plane = head // count
    n_in = sections + len(pieces)
    copies = sections + plane + 4

    def kernel(s_ref, p_ref, *refs):
        xz_refs, piece_refs = refs[:sections], refs[sections:n_in]
        n_ref, mask_ref, g_ref, w_ref, o_ref = refs[n_in : n_in + 5]
        n_out = n_in + 5
        v_ref, t_out, a_out = refs[n_out : n_out + 3]
        first_refs = refs[n_out + 3 : n_out + 3 + len(streams)]
        scratch = refs[n_out + 3 + len(streams) :]
        xz_all, table, mixes, weights, projs, dmix, w_in, o_in, t_ref, a_ref, sems = scratch
        mine = s_ref[0]
        started = []

        def start(source, target):
            copy = pltpu.make_async_copy(source, target, sems.at[len(started)])
            copy.start()
            started.append(copy)

        for r in range(sections):
            start(xz_refs[r], xz_all.at[mine ^ r])
        at = 0
        for ref in piece_refs:
            for i in range(ref.shape[0]):
                start(ref.at[i], table.at[p_ref[at]])
                at += 1
        small = list(started)
        start(w_ref.at[lead], w_in)
        start(o_ref.at[:, lead], o_in)
        for copy in small:
            copy.wait()

        def through(j, k):
            return table[:, :, through_at[j, k]].reshape(head, wide)

        def across(j, k):
            return table[:, :, across_at[j, k]].reshape(head, head)

        allowed = mask_ref[...] > 0.5
        norm = n_ref[...]
        rstds, tails, mixed = [], [], []
        for s in range(sections):
            proj = xz_all[s, :, :wide].astype(F32)
            for j in range(s):
                proj = proj + dot_nn(mixed[j], through(j, s))
            rstd = lax.rsqrt(norm * (1.0 / width) + EPS)
            proj = proj * rstd
            projs[s] = proj.astype(BF16)
            q, k, v = (projs[s, :, i * head : (i + 1) * head] for i in range(3))
            scores = jnp.where(allowed, dot_nt(q, k) * scale, -1e30)
            scores = jnp.exp(scores - jnp.max(scores, axis=1, keepdims=True))
            soft = scores / jnp.sum(scores, axis=1, keepdims=True)
            weights[s] = soft
            mix = dot_nn(soft.astype(BF16), v).astype(BF16)
            mixed.append(mix)
            mixes[:, s * head : (s + 1) * head] = mix
            rstds.append(rstd)
            dmix[:, s * head : (s + 1) * head] = xz_all[s, :, wide + head :].astype(F32)
            if s == sections - 1:
                break
            y = xz_all[s, :, wide : wide + head].astype(F32)
            for j in range(s):
                y = y + dot_nn(mixed[j], across(j, s))
            tail = y + dot_nn(mix, across(s, s))
            norm = norm + jnp.sum(mix.astype(F32) * (y + tail), axis=1, keepdims=True)
            norm = jnp.maximum(norm, 0.0)
            tails.append(tail)
        total = jnp.zeros((tokens, 1), F32)
        a_ref[...] = jnp.zeros_like(a_ref)
        for s in reversed(range(sections)):
            cols = slice(s * head, (s + 1) * head)
            da = dmix[:, cols]
            if s < sections - 1:
                da = da - total * tails[s]
            da = da.astype(BF16)
            q, k, v = (projs[s, :, i * head : (i + 1) * head] for i in range(3))
            soft = weights[s]
            dv = dot_tn(soft.astype(BF16), da)
            dsoft = dot_nt(da, v)
            dscore = soft * (dsoft - jnp.sum(dsoft * soft, axis=1, keepdims=True))
            dscore = (dscore * scale).astype(BF16)
            dproj = jnp.concatenate([dot_nn(dscore, k), dot_tn(dscore, q), dv], axis=1)
            along = jnp.sum(dproj * projs[s].astype(F32), axis=1, keepdims=True)
            first = (dproj * rstds[s]).astype(BF16)
            second = (-total * mixes[:, cols].astype(F32)).astype(BF16)
            total = total + rstds[s] * rstds[s] * along * (1.0 / width)
            for j in reversed(range(s)):
                term = dot_nt(first, through(j, s))
                if s < sections - 1:
                    term = term + dot_nt(second, across(j, s))
                dmix[:, j * head : (j + 1) * head] += term

            @pl.when(mine == s)
            def _(first=first, second=second, total=total):
                v_ref[:, :wide] = first
                v_ref[:, wide:] = second
                t_ref[...] = total

            for r in range(1, sections - s):

                @pl.when(mine == s + r)
                def _(r=r, cols=cols):
                    a_ref[:, (r - 1) * head : r * head] = mixes[:, cols]

        weights_in = started[len(small) :]
        start(t_ref, t_out)
        start(a_ref, a_out)
        for copy in weights_in:
            copy.wait()
        own = dot_nt(v_ref[:, :wide], w_in[...]) * g_ref[:, lead]
        own = (own + dot_nn(v_ref[:, wide:], o_in[...])).astype(BF16)
        for ref, part in zip(first_refs, streams):
            ref[...] = own[:, part]
        for copy in started[-2:]:
            copy.wait()

    vmem = pl.BlockSpec(memory_space=pltpu.VMEM)
    smem = pl.BlockSpec(memory_space=pltpu.SMEM)
    return pl.pallas_call(
        kernel,
        out_shape=[
            pltpu.VMEM((tokens, wide + head), BF16),
            pltpu.HBM((tokens, 1), F32),
            pltpu.HBM((tokens, (sections - 1) * head), BF16),
        ]
        + [pltpu.VMEM((tokens, part.stop - part.start), BF16) for part in streams],
        in_specs=[smem, smem] + [ANYWHERE] * n_in + [vmem, vmem, vmem, IN_HBM, IN_HBM],
        out_specs=[vmem, IN_HBM, IN_HBM] + [vmem] * len(streams),
        scratch_shapes=[
            pltpu.VMEM((sections,) + xz[0].shape, BF16),
            pltpu.VMEM((plane, count, packed), BF16),
            pltpu.VMEM((tokens, sections * head), BF16),
            pltpu.VMEM((sections, tokens, tokens), F32),
            pltpu.VMEM((sections, tokens, wide), BF16),
            pltpu.VMEM((tokens, sections * head), F32),
            pltpu.VMEM((lead.stop, wide), BF16),
            pltpu.VMEM((head, lead.stop), BF16),
            pltpu.VMEM((tokens, 1), F32),
            pltpu.VMEM((tokens, (sections - 1) * head), BF16),
            pltpu.SemaphoreType.DMA((copies,)),
        ],
        compiler_params=params(),
        name="serial",
    )(
        section,
        places,
        *xz,
        *pieces,
        norms,
        mask,
        gain,
        in_hbm(w_layer),
        in_hbm(out_layer),
    )


def hold(array, after):
    def kernel(*refs):
        pass

    return pl.pallas_call(
        kernel,
        out_shape=jax.ShapeDtypeStruct(array.shape, array.dtype),
        in_specs=[ANYWHERE] * (1 + len(after)),
        out_specs=ANYWHERE,
        input_output_aliases={0: 0},
        compiler_params=params(SMALL),
        name="hold",
    )(array, *after)


def gather_two(first, second, after):
    count = first.shape[0]

    def kernel(first_ref, second_ref, *refs):
        out_ref, sems = refs[len(after) :]
        start = mover(sems)
        copies = [start(first_ref, out_ref.at[:count]), start(second_ref, out_ref.at[count:])]
        for copy in copies:
            copy.wait()

    return pl.pallas_call(
        kernel,
        out_shape=jax.ShapeDtypeStruct((2 * count,) + first.shape[1:], first.dtype),
        in_specs=[ANYWHERE] * (2 + len(after)),
        out_specs=IN_VMEM,
        scratch_shapes=[pltpu.SemaphoreType.DMA((2,))],
        compiler_params=params(SMALL),
        name="gather_two",
    )(first, second, *after)


def widen(sent, gain, w_layer, out_layer, chunk):
    tokens = sent.shape[0]
    head, width = out_layer.shape
    wide = w_layer.shape[1]
    cuts = [slice(at, at + chunk) for at in range(0, width, chunk)]

    def kernel(v_ref, g_ref, w_ref, o_ref, back_ref, pair_ref, back_in, w_in, o_in, sems):
        start = mover(sems)
        loads = [
            (start(w_ref.at[cut], w_in.at[cut]), start(o_ref.at[:, cut], o_in.at[:, cut]))
            for cut in cuts
        ]
        stores = []
        for i, (cut, mine) in enumerate(zip(cuts, loads)):
            for load in mine:
                load.wait()
            back = dot_nt(v_ref[:, :wide], w_in[cut, :])
            own = back * g_ref[:, cut] + dot_nn(v_ref[:, wide:], o_in[:, cut])
            back_in[:, cut] = back.astype(BF16)
            stores.append(start(back_in.at[:, cut], back_ref.at[:, cut]))
            pair_ref[0, i] = own.astype(BF16)
            pair_ref[1, i] = jnp.zeros_like(pair_ref[1, i])
        for store in stores:
            store.wait()

    return pl.pallas_call(
        kernel,
        out_shape=[
            pltpu.HBM((tokens, width), BF16),
            pltpu.VMEM((2, len(cuts), tokens, chunk), BF16),
        ],
        in_specs=[IN_VMEM, IN_VMEM, IN_HBM, IN_HBM],
        out_specs=[IN_HBM, IN_VMEM],
        scratch_shapes=[
            pltpu.VMEM((tokens, width), BF16),
            pltpu.VMEM((width, wide), BF16),
            pltpu.VMEM((head, width), BF16),
            pltpu.SemaphoreType.DMA((3 * len(cuts),)),
        ],
        compiler_params=params(),
        name="widen",
    )(in_vmem(sent), gain, in_hbm(w_layer), in_hbm(out_layer))


def settle(total, mixes, stacks, places, x, cotangent, back, chunk, part, parts):
    tokens, width = x.shape
    layers, rows = stacks[0].shape[1:3]
    entries = [(i, e) for i, stack in enumerate(stacks) for e in range(stack.shape[0])]
    plane = len(entries)
    head = plane * rows
    span = width // parts
    base = part * span
    cuts = [slice(at, at + chunk) for at in range(0, span, chunk)]
    copies = plane * layers + 3 * len(cuts) + 2

    def kernel(p_ref, t_far, a_far, x_ref, c_ref, back_ref, *refs):
        stack_refs = refs[: len(stacks)]
        rest_ref, dg_ref = refs[len(stacks) : len(stacks) + 2]
        lower, x_in, c_in, back_in, t_ref, a_ref, sems = refs[len(stacks) + 2 :]
        start = mover(sems)
        first = [start(t_far, t_ref), start(a_far, a_ref)]
        for at, (i, e) in enumerate(entries):
            for r in range(layers):
                here = pl.ds(base, span)
                first.append(start(stack_refs[i].at[e, r, :, here], lower.at[r, p_ref[at]]))
        loads = []
        for cut in cuts:
            there = pl.ds(base + cut.start, chunk)
            mine = [start(x_ref.at[:, there], x_in.at[:, cut])]
            mine.append(start(c_ref.at[:, there], c_in.at[:, cut]))
            mine.append(start(back_ref.at[:, there], back_in.at[:, cut]))
            loads.append(mine)
        for load in first:
            load.wait()
        for i, (cut, mine) in enumerate(zip(cuts, loads)):
            for load in mine:
                load.wait()
            below = lower[:, :, :, cut].reshape(layers * head, chunk)
            here = x_in[:, cut].astype(F32) + dot_nn(a_ref[...], below)
            rest_ref[i] = (c_in[:, cut].astype(F32) - t_ref[...] * here).astype(BF16)
            gain = jnp.sum(back_in[:, cut].astype(F32) * here, axis=0, keepdims=True)
            for at in range(0, chunk, head):
                row = (cut.start + at) // head
                dg_ref[row : row + 1, :] = gain[:, at : at + head]

    return pl.pallas_call(
        kernel,
        out_shape=[
            pltpu.VMEM((len(cuts), tokens, chunk), BF16),
            pltpu.VMEM((span // head, head), F32),
        ],
        in_specs=[IN_SMEM] + [IN_HBM] * (5 + len(stacks)),
        out_specs=[IN_VMEM] * 2,
        scratch_shapes=[
            pltpu.VMEM((layers, plane, rows, span), BF16),
            pltpu.VMEM((tokens, span), BF16),
            pltpu.VMEM((tokens, span), BF16),
            pltpu.VMEM((tokens, span), BF16),
            pltpu.VMEM((tokens, 1), F32),
            pltpu.VMEM((tokens, layers * head), BF16),
            pltpu.SemaphoreType.DMA((copies,)),
        ],
        compiler_params=params(),
        name="settle",
    )(
        places,
        *[in_hbm(array) for array in (total, mixes, x, cotangent, back, *stacks)],
    )


def join(index, arrived, pair, cols, after):
    tokens, part = arrived.shape

    def kernel(i_ref, r_ref, _, *refs):
        send_ref, pair_ref = refs[len(after) :]
        at = i_ref[0]
        r = r_ref[...]
        send_ref[...] = (pair_ref[0, at, :, cols].astype(F32) + r.astype(F32)).astype(BF16)
        pair_ref[1, at, :, cols] = r

    return pl.pallas_call(
        kernel,
        out_shape=[pltpu.VMEM((tokens, part), BF16), pltpu.VMEM(pair.shape, BF16)],
        in_specs=[IN_SMEM] + [IN_VMEM] * 2 + [ANYWHERE] * len(after),
        out_specs=[IN_VMEM] * 2,
        input_output_aliases={2: 1},
        compiler_params=params(SMALL),
        name="join",
    )(index, in_vmem(arrived), in_vmem(pair), *after)


def finish(index, arrived, pair, rests, streams):
    _, count, tokens, chunk = pair.shape

    def kernel(i_ref, *refs):
        r_refs = refs[: len(streams)]
        pair_ref, rest_refs = refs[len(streams)], refs[len(streams) + 1 :][: len(rests)]
        whole_ref, whole, sems = refs[len(streams) + 1 + len(rests) :]
        each = count // len(rests)
        at = i_ref[0]
        copies = []
        for i in range(count):
            full = rest_refs[i // each][i % each].astype(F32) + pair_ref[0, i].astype(F32)
            whole[i] = (full + pair_ref[1, i].astype(F32)).astype(BF16)

            @pl.when(at == i)
            def _(i=i, full=full):
                for ref, cols in zip(r_refs, streams):
                    whole[i, :, cols] = (full[:, cols] + ref[...].astype(F32)).astype(BF16)

            there = whole_ref.at[:, pl.ds(i * chunk, chunk)]
            copies.append(pltpu.make_async_copy(whole.at[i], there, sems.at[i]))
            copies[-1].start()
        for copy in copies:
            copy.wait()

    return pl.pallas_call(
        kernel,
        out_shape=pltpu.HBM((tokens, count * chunk), BF16),
        in_specs=[IN_SMEM] + [IN_VMEM] * (len(streams) + 1 + len(rests)),
        out_specs=IN_HBM,
        scratch_shapes=[
            pltpu.VMEM((count, tokens, chunk), BF16),
            pltpu.SemaphoreType.DMA((count,)),
        ],
        compiler_params=params(SMALL),
        name="finish",
    )(index, *[in_vmem(array) for array in (*arrived, pair, *rests)])


def stacked(arrays):
    rows = arrays[0].shape[0]

    def kernel(*refs):
        for i, ref in enumerate(refs[:-1]):
            refs[-1][i * rows : (i + 1) * rows, :] = ref[...]

    return pl.pallas_call(
        kernel,
        out_shape=pltpu.VMEM((len(arrays) * rows, arrays[0].shape[1]), F32),
        in_specs=[IN_VMEM] * len(arrays),
        out_specs=IN_VMEM,
        compiler_params=params(SMALL),
        name="stacked",
    )(*[in_vmem(array) for array in arrays])


def added(arrays):
    def kernel(*refs):
        total = refs[0][...]
        for ref in refs[1:-1]:
            total = total + ref[...]
        refs[-1][...] = total

    return pl.pallas_call(
        kernel,
        out_shape=pltpu.VMEM(arrays[0].shape, F32),
        in_specs=[IN_VMEM] * len(arrays),
        out_specs=IN_VMEM,
        compiler_params=params(SMALL),
        name="added",
    )(*[in_vmem(array) for array in arrays])


STREAMS = 2
CHUNKS = 4
PARTS = 1


def stream_columns(chunk):
    lanes = 128
    tiles = chunk // lanes
    ends = [-(-tiles * (i + 1) // STREAMS) * lanes for i in range(STREAMS)]
    return [slice(start, end) for start, end in zip([0] + ends, ends)]


def shifted(array, by):
    sections = lax.axis_size("section")
    return lax.ppermute(array, "section", [(i, (i + by) % sections) for i in range(sections)])


def raised(array, by):
    sections = lax.axis_size("section")
    return lax.ppermute(array, "section", [(i, i + by) for i in range(sections - by)])


def swapped(array, step):
    groups = lax.axis_size("group")
    devices = lax.axis_size("dp")
    bits = devices.bit_length() - 1
    pairs = []
    for p in range(devices):
        for g in range(groups):
            pairs.append((p * groups + g, (p ^ (1 << ((step + g) % bits))) * groups + g))
    return lax.ppermute(array, ("dp", "group"), pairs)


def handed(array, by):
    groups = lax.axis_size("group")
    return lax.ppermute(array, "group", [(i, (i + by) % groups) for i in range(groups)])


def plane_places():
    groups = lax.axis_size("group")
    bits = lax.axis_size("dp").bit_length() - 1
    masks = []
    for g in range(groups):
        order = [0]
        for step in range(bits):
            order = order + [m ^ (1 << ((step + g) % bits)) for m in order]
        masks.append(order)
    masks = jnp.asarray(masks, jnp.int32)
    dp, member = lax.axis_index("dp"), lax.axis_index("group")
    places = []
    for r in range(groups):
        giver = (member + groups - r) % groups
        places.append((dp ^ masks[giver]) * groups + giver)
    return jnp.concatenate(places).astype(jnp.int32)


def local(tokens_in, cotangent, gains, w_qkv, w_out, segments, plan):
    sections = lax.axis_size("section")
    groups = lax.axis_size("group")
    devices = lax.axis_size("dp")
    plane = devices * groups
    section = lax.axis_index("section")
    member = lax.axis_index("group")
    rows_dev = plan.shape[1]
    length = segments.shape[1]
    tokens, width = tokens_in.shape
    head = w_out.shape[1]
    share = rows_dev // groups
    w_layer, out_layer = w_qkv[0], w_out[0]
    place = member.astype(jnp.int32)[None]
    layer = section.astype(jnp.int32)[None]

    slice_rows = head // plane
    mine = lax.axis_index("dp") * groups + member
    own_rows, *parts = pick(
        tokens_in.reshape(rows_dev, length, width),
        plan,
        place,
        groups,
        out_layer,
        mine.astype(jnp.int32)[None],
        slice_rows,
    )
    slices = [raised(own_rows, r) for r in range(sections - 1, 0, -1)]
    slices = [own_rows] + slices[::-1]
    chosen = jnp.take(segments, plan[0], axis=0, mode="clip").astype(BF16)
    chosen = chosen.reshape(groups, share, length)
    moved, moved_seg = [], []
    for r in range(groups):
        outgoing = lax.dynamic_index_in_dim(chosen, (member + r) % groups, 0, keepdims=False)
        moved.append(handed(parts[r], r) if r else parts[r])
        moved_seg.append(handed(outgoing, r) if r else outgoing)
    moved = [part.reshape(share * length, width) for part in moved]
    order = (member - jnp.arange(groups)) % groups
    seg = jnp.take(jnp.stack(moved_seg), order, axis=0, mode="clip").reshape(tokens)
    at = jnp.arange(tokens)
    mask = (
        (at[:, None] >= at[None, :])
        & (at[:, None] // length == at[None, :] // length)
        & (seg[:, None] == seg[None, :])
    ).astype(F32)

    last = (section == sections - 1).astype(jnp.int32)[None]
    bits = devices.bit_length() - 1
    places = plane_places()
    x, xz, norms = project(
        moved, cotangent, gains, w_layer, out_layer, place, []
    )
    coupling, stack = couple(slices, gains, w_layer, out_layer, last, [mask, places, xz])
    others = [shifted(coupling, r) for r in range(1, sections)]

    streams = stream_columns(width // CHUNKS)

    def facing(array, by):
        return lax.ppermute(array, "section", [(i, i ^ by) for i in range(sections)])

    arrays, masks, by = [hold(xz, others)], [0], sections // 2
    while by > 0:
        arrays = arrays + [facing(array, by) for array in arrays]
        masks = masks + [mask_of ^ by for mask_of in masks]
        by = by // 2
    xz_all = [arrays[masks.index(r)] for r in range(sections)]
    early = [xz_all[r] for r in range(1, sections) if r & (r - 1) == 0]
    late = [xz_all[r] for r in range(1, sections) if r & (r - 1) != 0]
    pieces = [compact([coupling] + others, layer, 3 * head, head, [xz])]

    rows = [stack[None]]
    for step in range(bits):
        if step > 0:
            pieces = [merge(*pieces, early)]
        pieces = pieces + [swapped(pieces[0], step)]
        if step == bits - 1:
            pieces[-1] = hold(pieces[-1], late)
        if step > 0:
            rows = [gather_two(*rows, pieces[-1:])]
        rows = rows + [swapped(rows[0], step)]
    pieces = pieces + [handed(array, r) for r in range(1, groups) for array in pieces]
    sent, total, mixes, *leaving = serial(
        xz_all, pieces, places, norms, mask, layer, gains, w_layer, out_layer, streams
    )
    back, pair = widen(sent, gains, w_layer, out_layer, width // CHUNKS)

    down = [(i, i - 1) for i in range(1, sections)]
    behind = sections - 1 - section

    def index(tick):
        return jnp.clip(tick - behind, 0, CHUNKS - 1).astype(jnp.int32)[None]

    def lowered(arrays):
        return [lax.ppermute(array, "section", down) for array in arrays]

    ticks = CHUNKS + sections - 1
    after = {}
    for tick in range(1, ticks):
        arrived = lowered(leaving)
        if tick < ticks - 1:
            for i, cols in enumerate(streams):
                waits = after.get(tick, []) if tick < ticks - 2 or i == STREAMS - 1 else []
                leaving[i], pair = join(index(tick), arrived[i], pair, cols, waits)
        if tick == 1:
            rows = [hold(array, leaving) for array in rows]
            rows = rows + [handed(array, r) for r in range(1, groups) for array in rows]
            rests, halves = [], []
            for part in range(PARTS):
                rest, half = settle(
                    total, mixes, rows, places, x, cotangent, back, width // CHUNKS, part, PARTS
                )
                rests.append(rest)
                halves.append(half)
            sums = [stacked(halves)]
            for step in range(bits):
                sums.append(added([sums[-1], swapped(sums[-1], step)]))
            sums.append(added(sums[-1:] + [handed(sums[-1], r) for r in range(1, groups)]))
            gain_whole = sums[-1].reshape(1, width)
            after = {2 + i: [array] for i, array in enumerate(sums)}
    out = finish(index(ticks - 1), arrived, pair, rests, streams)
    return (out[None], gain_whole)


def attend(hidden, segment, gain_row, w_layer, out_layer):
    count, length, width = hidden.shape
    head = out_layer.shape[0]
    scaled = hidden * lax.rsqrt(jnp.mean(hidden * hidden, axis=-1, keepdims=True) + EPS) * gain_row
    normed = scaled.astype(BF16).reshape(count * length, width)
    projected = jnp.dot(normed, w_layer, preferred_element_type=F32).reshape(count, length, 3 * head)
    query = projected[:, :, :head]
    keyed = projected[:, :, head : 2 * head]
    valued = projected[:, :, 2 * head :]
    positions = jnp.arange(length)
    allowed = (positions[:, None] >= positions[None, :])[None] & (
        segment[:, :, None] == segment[:, None, :]
    )
    scores = jnp.einsum("rid,rjd->rij", query, keyed, precision=lax.Precision.HIGHEST)
    scores = jnp.where(allowed, scores / math.sqrt(head), -1e30)
    weights = jax.nn.softmax(scores, axis=-1)
    mixed = jnp.einsum("rij,rjd->rid", weights, valued, precision=lax.Precision.HIGHEST)
    mixed = mixed.astype(BF16).reshape(count * length, head)
    output = jnp.dot(mixed, out_layer, preferred_element_type=F32).reshape(count, length, width)
    return hidden + output


MB_ROWS = 2


def relay(tokens_in, cotangent, gains, w_qkv, w_out, segments, plan):
    sections = lax.axis_size("section")
    section = lax.axis_index("section")
    rows_dev = plan.shape[1]
    width = tokens_in.shape[1]
    length = segments.shape[1]
    micro = rows_dev // MB_ROWS
    blocks = tokens_in.reshape(rows_dev, length, width)
    chosen = jnp.take(blocks, plan[0], axis=0)
    chosen_seg = jnp.take(segments, plan[0], axis=0).astype(BF16)
    assigned = lax.all_to_all(chosen, "group", split_axis=0, concat_axis=0, tiled=True)
    moved_seg = lax.all_to_all(chosen_seg, "group", split_axis=0, concat_axis=0, tiled=True)
    assigned = assigned.reshape(micro, MB_ROWS, length, width)
    seg_groups = moved_seg.reshape(micro, MB_ROWS, length)
    gain_row, w_layer, out_layer = gains[0], w_qkv[0], w_out[0]
    grad_rows = cotangent.reshape(micro, MB_ROWS, length, width)
    ticks = micro + sections - 1

    def passed_along(array, by):
        pairs = [(i, i + by) for i in range(sections) if 0 <= i + by < sections]
        return lax.ppermute(array, "section", pairs)

    def at(array, i):
        return lax.dynamic_index_in_dim(array, i, 0, keepdims=False)

    def forward_tick(tick, carry):
        saved, arrived = carry
        index = tick - section
        valid = (index >= 0) & (index < micro)
        clipped = jnp.clip(index, 0, micro - 1)
        entering = jnp.where(section == 0, at(assigned, clipped), arrived)
        kept = jnp.where(valid, entering, at(saved, clipped))
        saved = lax.dynamic_update_index_in_dim(saved, kept, clipped, 0)
        segment = at(seg_groups, clipped)

        def run_layer(value):
            return attend(value.astype(F32), segment, gain_row, w_layer, out_layer).astype(BF16)

        leaving = lax.cond(valid, run_layer, jnp.zeros_like, entering)
        return (saved, passed_along(leaving, 1))

    saved_init = jnp.zeros((micro, MB_ROWS, length, width), BF16)
    arrive_init = jnp.zeros((MB_ROWS, length, width), BF16)
    saved, _ = lax.fori_loop(0, ticks, forward_tick, (saved_init, arrive_init))

    def backward_tick(tick, carry):
        grads_x, gain_total, arrived = carry
        index = tick - (sections - 1 - section)
        valid = (index >= 0) & (index < micro)
        clipped = jnp.clip(index, 0, micro - 1)
        entering = jnp.where(section == sections - 1, at(grad_rows, clipped), arrived)
        segment = at(seg_groups, clipped)
        stored = at(saved, clipped).astype(F32)

        def local_layer(hidden, gains_here):
            return attend(hidden, segment, gains_here, w_layer, out_layer)

        def run_back(value):
            _, pullback = jax.vjp(local_layer, stored, gain_row)
            grad_hidden, grad_gain = pullback(value.astype(F32))
            return (grad_hidden.astype(BF16), grad_gain)

        def skip_back(value):
            return (jnp.zeros_like(value), jnp.zeros(gain_row.shape, F32))

        sending, grad_gain = lax.cond(valid, run_back, skip_back, entering)
        kept = jnp.where(valid, sending, at(grads_x, clipped))
        grads_x = lax.dynamic_update_index_in_dim(grads_x, kept, clipped, 0)
        return (grads_x, gain_total + grad_gain, passed_along(sending, -1))

    gain_init = jnp.zeros(gain_row.shape, F32)
    grads_x, gain_total, _ = lax.fori_loop(
        0, ticks, backward_tick, (saved_init, gain_init, arrive_init)
    )
    gain_whole = lax.psum(gain_total, ("dp", "group"))
    return (grads_x.reshape(1, rows_dev * length, width), gain_whole[None])


def solution(mesh):
    placed = (
        P(("dp", "group"), None),
        P(("dp", "group"), None),
        P("section", None),
        P("section", None, None),
        P("section", None, None),
        P(("dp", "group"), None),
        P(("dp", "group"), None),
    )

    def chosen(tokens_in, cotangent, gains, w_qkv, w_out, segments, plan):
        sections, head, width = w_out.shape
        devices = mesh.shape["dp"]
        small = sections * 4 * head < width and sections > 1
        halves = devices & (devices - 1) == 0 and sections & (sections - 1) == 0
        body = local if small and halves else relay
        return jax.shard_map(
            body,
            mesh=mesh,
            in_specs=placed,
            out_specs=(P("section", ("dp", "group"), None), P("section", None)),
            check_vma=False,
        )(tokens_in, cotangent, gains, w_qkv, w_out, segments, plan)

    return chosen
```

```python
import math

import jax
import jax.numpy as jnp
from jax import lax
from jax.experimental import pallas as pl
from jax.experimental.pallas import tpu as pltpu
from jax.sharding import PartitionSpec as P

EPS = 1e-05
VMEM_BYTES = 24 * 1024 * 1024
SMALL = 16 * 1024 * 1024
F32 = jnp.float32
BF16 = jnp.bfloat16


def dot_nn(a, b):
    return lax.dot_general(a, b, (((1,), (0,)), ((), ())), preferred_element_type=F32)


def dot_nt(a, b):
    return lax.dot_general(a, b, (((1,), (1,)), ((), ())), preferred_element_type=F32)


def dot_tn(a, b):
    return lax.dot_general(a, b, (((0,), (0,)), ((), ())), preferred_element_type=F32)


IN_HBM = pl.BlockSpec(memory_space=pltpu.HBM)
ANYWHERE = pl.BlockSpec(memory_space=pl.ANY)
IN_VMEM = pl.BlockSpec(memory_space=pltpu.VMEM)
IN_SMEM = pl.BlockSpec(memory_space=pltpu.SMEM)


def in_hbm(array):
    return pltpu.with_memory_space_constraint(array, pltpu.HBM)


def in_vmem(array):
    return pltpu.with_memory_space_constraint(array, pltpu.VMEM)


def mover(sems):
    used = []

    def start(source, target):
        copy = pltpu.make_async_copy(source, target, sems.at[len(used)])
        copy.start()
        used.append(copy)
        return copy

    return start


def steps(width):
    step = min(width, 1024)
    return [slice(at, at + step) for at in range(0, width, step)]


def params(limit=VMEM_BYTES):
    return pltpu.CompilerParams(vmem_limit_bytes=limit)


def pick(tokens, plan, place, groups, out_layer, mine, slice_rows):
    rows, length, width = tokens.shape
    share = rows // groups

    def kernel(plan_ref, place_ref, mine_ref, tokens_ref, o_ref, *rest):
        slice_ref, parts = rest[0], rest[1 : 1 + groups]
        slice_in, rows_in, sems = rest[1 + groups :]
        start = mover(sems)
        at = pl.ds(pl.multiple_of(mine_ref[0] * slice_rows, slice_rows), slice_rows)
        loads = [(start(o_ref.at[at], slice_in), slice_in, slice_ref)]
        for r in range(groups):
            target = lax.rem(place_ref[0] + r, groups)
            for c in range(share):
                here = rows_in.at[r * share + c]
                row = plan_ref[0, target * share + c]
                loads.append((start(tokens_ref.at[row], here), here, parts[r].at[c]))
        stores = []
        for load, here, there in loads:
            load.wait()
            stores.append(start(here, there))
        for store in stores:
            store.wait()

    return pl.pallas_call(
        kernel,
        out_shape=[pltpu.HBM((slice_rows, width), BF16)]
        + [pltpu.HBM((share, length, width), BF16)] * groups,
        in_specs=[IN_SMEM, IN_SMEM, IN_SMEM, IN_HBM, IN_HBM],
        out_specs=[IN_HBM] * (1 + groups),
        scratch_shapes=[
            pltpu.VMEM((slice_rows, width), BF16),
            pltpu.VMEM((rows, length, width), BF16),
            pltpu.SemaphoreType.DMA((2 * rows + 2,)),
        ],
        compiler_params=params(),
        name="pick",
    )(plan, place, mine, in_hbm(tokens), in_hbm(out_layer))


def project(parts, cotangent, gain, w_layer, out_layer, place, after):
    groups = len(parts)
    tokens, width = cotangent.shape
    head = out_layer.shape[0]
    wide = w_layer.shape[1]
    block = tokens // groups
    cuts = steps(width)
    copies = len(cuts) * (groups + 4)

    def kernel(place_ref, *refs):
        part_refs = refs[:groups]
        cot_ref, g_ref, w_ref, o_ref = refs[groups : groups + 4]
        x_ref, xz_ref, n_ref = refs[groups + 4 + len(after) : groups + 7 + len(after)]
        x_in, c_in, w_in, o_in, sems = refs[groups + 7 + len(after) :]
        start = mover(sems)
        loads = []
        for cut in cuts:
            mine = [start(w_ref.at[cut], w_in.at[cut])]
            mine.append(start(o_ref.at[:, cut], o_in.at[:, cut]))
            for r in range(groups):
                source = lax.rem(place_ref[0] + groups - r, groups)
                rows = pl.ds(pl.multiple_of(source * block, block), block)
                mine.append(start(part_refs[r].at[:, cut], x_in.at[rows, cut]))
            mine.append(start(cot_ref.at[:, cut], c_in.at[:, cut]))
            loads.append(mine)
        through = jnp.zeros((tokens, wide), F32)
        across = jnp.zeros((tokens, head), F32)
        back = jnp.zeros((tokens, head), F32)
        square = jnp.zeros((tokens, 1), F32)
        stores = []
        for cut, mine in zip(cuts, loads):
            for load in mine:
                load.wait()
            stores.append(start(x_in.at[:, cut], x_ref.at[:, cut]))
            x = x_in[:, cut]
            xf = x.astype(F32)
            through += dot_nn((xf * g_ref[:, cut]).astype(BF16), w_in[cut, :])
            across += dot_nt(x, o_in[:, cut])
            back += dot_nt(c_in[:, cut], o_in[:, cut])
            square += jnp.sum(xf * xf, axis=1, keepdims=True)
        xz_ref[:, :wide] = through.astype(BF16)
        xz_ref[:, wide : wide + head] = across.astype(BF16)
        xz_ref[:, wide + head :] = back.astype(BF16)
        n_ref[...] = square
        for store in stores:
            store.wait()

    return pl.pallas_call(
        kernel,
        out_shape=[
            pltpu.HBM((tokens, width), BF16),
            jax.ShapeDtypeStruct((tokens, wide + 2 * head), BF16),
            jax.ShapeDtypeStruct((tokens, 1), F32),
        ],
        in_specs=[IN_SMEM]
        + [ANYWHERE] * groups
        + [IN_HBM, IN_VMEM, IN_HBM, IN_HBM]
        + [ANYWHERE] * len(after),
        out_specs=[IN_HBM, IN_VMEM, IN_VMEM],
        scratch_shapes=[
            pltpu.VMEM((tokens, width), BF16),
            pltpu.VMEM((tokens, width), BF16),
            pltpu.VMEM((width, wide), BF16),
            pltpu.VMEM((head, width), BF16),
            pltpu.SemaphoreType.DMA((copies,)),
        ],
        compiler_params=params(),
        name="project",
    )(
        place,
        in_hbm(parts[0]),
        *[in_vmem(part) for part in parts[1:]],
        in_hbm(cotangent),
        gain,
        in_hbm(w_layer),
        in_hbm(out_layer),
        *after,
    )


def couple(slices, gain, w_layer, out_layer, last, after):
    sections = len(slices)
    count, width = slices[0].shape
    head = out_layer.shape[0]
    wide = w_layer.shape[1]
    below = (sections - 2) * wide
    packed = below + max(wide, (sections - 1) * head)
    cuts = steps(width)
    copies = len(cuts) * (sections + 2) + sections - 1

    def kernel(last_ref, *refs):
        s_refs = refs[:sections][::-1]
        g_ref, w_ref, o_ref = refs[sections : sections + 3]
        out_ref, stack_ref, r_in, w_in, o_in, sems = refs[sections + 3 + len(after) :]
        rows = [slice(r * count, (r + 1) * count) for r in range(sections)]
        start = mover(sems)
        loads = []
        for cut in cuts:
            mine = [start(w_ref.at[cut], w_in.at[cut])]
            mine.append(start(o_ref.at[:, cut], o_in.at[:, cut]))
            for r in range(sections):
                mine.append(start(s_refs[r].at[:, cut], r_in.at[rows[r], cut]))
            loads.append(mine)
        through = jnp.zeros((sections * count, wide), F32)
        across = jnp.zeros((sections * count, head), F32)
        for cut, mine in zip(cuts, loads):
            for load in mine:
                load.wait()
            r = r_in[:, cut]
            through += dot_nn((r.astype(F32) * g_ref[:, cut]).astype(BF16), w_in[cut, :])
            across += dot_nt(r, o_in[:, cut])
        stores = [start(r_in.at[rows[r]], stack_ref.at[r - 1]) for r in range(1, sections)]
        through = through.astype(BF16)
        across = across.astype(BF16)
        out_ref[...] = jnp.zeros_like(out_ref)
        for r in range(1, sections - 1):
            out_ref[:, (r - 1) * wide : r * wide] = through[rows[r]]

        @pl.when(last_ref[0] == 1)
        def _():
            out_ref[:, below : below + wide] = through[rows[-1]]

        @pl.when(last_ref[0] == 0)
        def _():
            for r in range(sections - 1):
                out_ref[:, below + r * head : below + (r + 1) * head] = across[rows[r]]

        for store in stores:
            store.wait()

    return pl.pallas_call(
        kernel,
        out_shape=[
            jax.ShapeDtypeStruct((count, packed), BF16),
            pltpu.HBM((sections - 1, count, width), BF16),
        ],
        in_specs=[IN_SMEM]
        + [ANYWHERE] * sections
        + [IN_VMEM, IN_HBM, IN_HBM]
        + [ANYWHERE] * len(after),
        out_specs=[IN_VMEM, IN_HBM],
        scratch_shapes=[
            pltpu.VMEM((sections * count, width), BF16),
            pltpu.VMEM((width, wide), BF16),
            pltpu.VMEM((head, width), BF16),
            pltpu.SemaphoreType.DMA((copies,)),
        ],
        compiler_params=params(),
        name="couple",
    )(last, *slices[::-1], gain, in_hbm(w_layer), in_hbm(out_layer), *after)


def layout(sections, wide, head):
    through, across, at = {}, {}, 0
    for k in range(sections):
        for j in range(k):
            through[j, k] = slice(at, at + wide)
            at += wide
        for j in range(k + 1 if k < sections - 1 else 0):
            across[j, k] = slice(at, at + head)
            at += head
    return through, across, at


def compact(parts, section, wide, head, after):
    sections = len(parts)
    count = parts[0].shape[0]
    below = (sections - 2) * wide
    through, across, total = layout(sections, wide, head)

    def kernel(s_ref, *refs):
        part_refs, out_ref = refs[:sections], refs[-1]
        mine = s_ref[0]

        def fill(k, r):
            for j in range(k):
                at = (k - j - 1) * wide
                out_ref[0, :, through[j, k]] = part_refs[r][:, at : at + wide]
            for j in range(k + 1 if k < sections - 1 else 0):
                at = below + (k - j) * head
                out_ref[0, :, across[j, k]] = part_refs[r][:, at : at + head]

        for s in range(sections):

            @pl.when(mine == s)
            def _(s=s):
                for r in range(sections):
                    fill((s - r) % sections, r)

    vmem = pl.BlockSpec(memory_space=pltpu.VMEM)
    return pl.pallas_call(
        kernel,
        out_shape=jax.ShapeDtypeStruct((1, count, total), BF16),
        in_specs=[IN_SMEM] + [vmem] * sections + [ANYWHERE] * len(after),
        out_specs=vmem,
        compiler_params=params(SMALL),
        name="compact",
    )(section, *parts, *after)


def merge(first, second, after):
    count = first.shape[0]

    def kernel(first_ref, second_ref, *refs):
        refs[-1][:count] = first_ref[...]
        refs[-1][count:] = second_ref[...]

    return pl.pallas_call(
        kernel,
        out_shape=jax.ShapeDtypeStruct((2 * count,) + first.shape[1:], first.dtype),
        in_specs=[IN_VMEM] * 2 + [ANYWHERE] * len(after),
        out_specs=IN_VMEM,
        compiler_params=params(SMALL),
        name="merge",
    )(first, second, *after)


def serial(xz, pieces, places, norms, mask, section, gain, w_layer, out_layer, streams):
    sections = len(xz)
    tokens = norms.shape[0]
    head, width = out_layer.shape
    wide = 3 * head
    scale = 1.0 / math.sqrt(head)
    lead = slice(0, streams[-1].stop)
    through_at, across_at, _ = layout(sections, wide, head)
    count, packed = pieces[0].shape[-2:]
    plane = head // count
    n_in = sections + len(pieces)
    copies = sections + plane + 4

    def kernel(s_ref, p_ref, *refs):
        xz_refs, piece_refs = refs[:sections], refs[sections:n_in]
        n_ref, mask_ref, g_ref, w_ref, o_ref = refs[n_in : n_in + 5]
        n_out = n_in + 5
        v_ref, t_out, a_out = refs[n_out : n_out + 3]
        first_refs = refs[n_out + 3 : n_out + 3 + len(streams)]
        scratch = refs[n_out + 3 + len(streams) :]
        xz_all, table, mixes, weights, projs, dmix, w_in, o_in, t_ref, a_ref, sems = scratch
        mine = s_ref[0]
        started = []

        def start(source, target):
            copy = pltpu.make_async_copy(source, target, sems.at[len(started)])
            copy.start()
            started.append(copy)

        for r in range(sections):
            start(xz_refs[r], xz_all.at[mine ^ r])
        at = 0
        for ref in piece_refs:
            for i in range(ref.shape[0]):
                start(ref.at[i], table.at[p_ref[at]])
                at += 1
        small = list(started)
        start(w_ref.at[lead], w_in)
        start(o_ref.at[:, lead], o_in)
        for copy in small:
            copy.wait()

        def through(j, k):
            return table[:, :, through_at[j, k]].reshape(head, wide)

        def across(j, k):
            return table[:, :, across_at[j, k]].reshape(head, head)

        allowed = mask_ref[...] > 0.5
        norm = n_ref[...]
        rstds, tails, mixed = [], [], []
        for s in range(sections):
            proj = xz_all[s, :, :wide].astype(F32)
            for j in range(s):
                proj = proj + dot_nn(mixed[j], through(j, s))
            rstd = lax.rsqrt(norm * (1.0 / width) + EPS)
            proj = proj * rstd
            projs[s] = proj.astype(BF16)
            q, k, v = (projs[s, :, i * head : (i + 1) * head] for i in range(3))
            scores = jnp.where(allowed, dot_nt(q, k) * scale, -1e30)
            scores = jnp.exp(scores - jnp.max(scores, axis=1, keepdims=True))
            soft = scores / jnp.sum(scores, axis=1, keepdims=True)
            weights[s] = soft
            mix = dot_nn(soft.astype(BF16), v).astype(BF16)
            mixed.append(mix)
            mixes[:, s * head : (s + 1) * head] = mix
            rstds.append(rstd)
            dmix[:, s * head : (s + 1) * head] = xz_all[s, :, wide + head :].astype(F32)
            if s == sections - 1:
                break
            y = xz_all[s, :, wide : wide + head].astype(F32)
            for j in range(s):
                y = y + dot_nn(mixed[j], across(j, s))
            tail = y + dot_nn(mix, across(s, s))
            norm = norm + jnp.sum(mix.astype(F32) * (y + tail), axis=1, keepdims=True)
            norm = jnp.maximum(norm, 0.0)
            tails.append(tail)
        total = jnp.zeros((tokens, 1), F32)
        a_ref[...] = jnp.zeros_like(a_ref)
        for s in reversed(range(sections)):
            cols = slice(s * head, (s + 1) * head)
            da = dmix[:, cols]
            if s < sections - 1:
                da = da - total * tails[s]
            da = da.astype(BF16)
            q, k, v = (projs[s, :, i * head : (i + 1) * head] for i in range(3))
            soft = weights[s]
            dv = dot_tn(soft.astype(BF16), da)
            dsoft = dot_nt(da, v)
            dscore = soft * (dsoft - jnp.sum(dsoft * soft, axis=1, keepdims=True))
            dscore = (dscore * scale).astype(BF16)
            dproj = jnp.concatenate([dot_nn(dscore, k), dot_tn(dscore, q), dv], axis=1)
            along = jnp.sum(dproj * projs[s].astype(F32), axis=1, keepdims=True)
            first = (dproj * rstds[s]).astype(BF16)
            second = (-total * mixes[:, cols].astype(F32)).astype(BF16)
            total = total + rstds[s] * rstds[s] * along * (1.0 / width)
            for j in reversed(range(s)):
                term = dot_nt(first, through(j, s))
                if s < sections - 1:
                    term = term + dot_nt(second, across(j, s))
                dmix[:, j * head : (j + 1) * head] += term

            @pl.when(mine == s)
            def _(first=first, second=second, total=total):
                v_ref[:, :wide] = first
                v_ref[:, wide:] = second
                t_ref[...] = total

            for r in range(1, sections - s):

                @pl.when(mine == s + r)
                def _(r=r, cols=cols):
                    a_ref[:, (r - 1) * head : r * head] = mixes[:, cols]

        weights_in = started[len(small) :]
        start(t_ref, t_out)
        start(a_ref, a_out)
        for copy in weights_in:
            copy.wait()
        own = dot_nt(v_ref[:, :wide], w_in[...]) * g_ref[:, lead]
        own = (own + dot_nn(v_ref[:, wide:], o_in[...])).astype(BF16)
        for ref, part in zip(first_refs, streams):
            ref[...] = own[:, part]
        for copy in started[-2:]:
            copy.wait()

    vmem = pl.BlockSpec(memory_space=pltpu.VMEM)
    smem = pl.BlockSpec(memory_space=pltpu.SMEM)
    return pl.pallas_call(
        kernel,
        out_shape=[
            pltpu.VMEM((tokens, wide + head), BF16),
            pltpu.HBM((tokens, 1), F32),
            pltpu.HBM((tokens, (sections - 1) * head), BF16),
        ]
        + [pltpu.VMEM((tokens, part.stop - part.start), BF16) for part in streams],
        in_specs=[smem, smem] + [ANYWHERE] * n_in + [vmem, vmem, vmem, IN_HBM, IN_HBM],
        out_specs=[vmem, IN_HBM, IN_HBM] + [vmem] * len(streams),
        scratch_shapes=[
            pltpu.VMEM((sections,) + xz[0].shape, BF16),
            pltpu.VMEM((plane, count, packed), BF16),
            pltpu.VMEM((tokens, sections * head), BF16),
            pltpu.VMEM((sections, tokens, tokens), F32),
            pltpu.VMEM((sections, tokens, wide), BF16),
            pltpu.VMEM((tokens, sections * head), F32),
            pltpu.VMEM((lead.stop, wide), BF16),
            pltpu.VMEM((head, lead.stop), BF16),
            pltpu.VMEM((tokens, 1), F32),
            pltpu.VMEM((tokens, (sections - 1) * head), BF16),
            pltpu.SemaphoreType.DMA((copies,)),
        ],
        compiler_params=params(),
        name="serial",
    )(
        section,
        places,
        *xz,
        *pieces,
        norms,
        mask,
        gain,
        in_hbm(w_layer),
        in_hbm(out_layer),
    )


def hold(array, after):
    def kernel(*refs):
        pass

    return pl.pallas_call(
        kernel,
        out_shape=jax.ShapeDtypeStruct(array.shape, array.dtype),
        in_specs=[ANYWHERE] * (1 + len(after)),
        out_specs=ANYWHERE,
        input_output_aliases={0: 0},
        compiler_params=params(SMALL),
        name="hold",
    )(array, *after)


def gather_two(first, second, after):
    count = first.shape[0]

    def kernel(first_ref, second_ref, *refs):
        out_ref, sems = refs[len(after) :]
        start = mover(sems)
        copies = [start(first_ref, out_ref.at[:count]), start(second_ref, out_ref.at[count:])]
        for copy in copies:
            copy.wait()

    return pl.pallas_call(
        kernel,
        out_shape=jax.ShapeDtypeStruct((2 * count,) + first.shape[1:], first.dtype),
        in_specs=[ANYWHERE] * (2 + len(after)),
        out_specs=IN_VMEM,
        scratch_shapes=[pltpu.SemaphoreType.DMA((2,))],
        compiler_params=params(SMALL),
        name="gather_two",
    )(first, second, *after)


def widen(sent, gain, w_layer, out_layer, chunk):
    tokens = sent.shape[0]
    head, width = out_layer.shape
    wide = w_layer.shape[1]
    cuts = [slice(at, at + chunk) for at in range(0, width, chunk)]

    def kernel(v_ref, g_ref, w_ref, o_ref, back_ref, pair_ref, back_in, w_in, o_in, sems):
        start = mover(sems)
        loads = [
            (start(w_ref.at[cut], w_in.at[cut]), start(o_ref.at[:, cut], o_in.at[:, cut]))
            for cut in cuts
        ]
        stores = []
        for i, (cut, mine) in enumerate(zip(cuts, loads)):
            for load in mine:
                load.wait()
            back = dot_nt(v_ref[:, :wide], w_in[cut, :])
            own = back * g_ref[:, cut] + dot_nn(v_ref[:, wide:], o_in[:, cut])
            back_in[:, cut] = back.astype(BF16)
            stores.append(start(back_in.at[:, cut], back_ref.at[:, cut]))
            pair_ref[0, i] = own.astype(BF16)
            pair_ref[1, i] = jnp.zeros_like(pair_ref[1, i])
        for store in stores:
            store.wait()

    return pl.pallas_call(
        kernel,
        out_shape=[
            pltpu.HBM((tokens, width), BF16),
            pltpu.VMEM((2, len(cuts), tokens, chunk), BF16),
        ],
        in_specs=[IN_VMEM, IN_VMEM, IN_HBM, IN_HBM],
        out_specs=[IN_HBM, IN_VMEM],
        scratch_shapes=[
            pltpu.VMEM((tokens, width), BF16),
            pltpu.VMEM((width, wide), BF16),
            pltpu.VMEM((head, width), BF16),
            pltpu.SemaphoreType.DMA((3 * len(cuts),)),
        ],
        compiler_params=params(),
        name="widen",
    )(in_vmem(sent), gain, in_hbm(w_layer), in_hbm(out_layer))


def settle(total, mixes, stacks, places, x, cotangent, back, chunk, part, parts):
    tokens, width = x.shape
    layers, rows = stacks[0].shape[1:3]
    entries = [(i, e) for i, stack in enumerate(stacks) for e in range(stack.shape[0])]
    plane = len(entries)
    head = plane * rows
    span = width // parts
    base = part * span
    cuts = [slice(at, at + chunk) for at in range(0, span, chunk)]
    copies = plane * layers + 3 * len(cuts) + 2

    def kernel(p_ref, t_far, a_far, x_ref, c_ref, back_ref, *refs):
        stack_refs = refs[: len(stacks)]
        rest_ref, dg_ref = refs[len(stacks) : len(stacks) + 2]
        lower, x_in, c_in, back_in, t_ref, a_ref, sems = refs[len(stacks) + 2 :]
        start = mover(sems)
        first = [start(t_far, t_ref), start(a_far, a_ref)]
        for at, (i, e) in enumerate(entries):
            for r in range(layers):
                here = pl.ds(base, span)
                first.append(start(stack_refs[i].at[e, r, :, here], lower.at[r, p_ref[at]]))
        loads = []
        for cut in cuts:
            there = pl.ds(base + cut.start, chunk)
            mine = [start(x_ref.at[:, there], x_in.at[:, cut])]
            mine.append(start(c_ref.at[:, there], c_in.at[:, cut]))
            mine.append(start(back_ref.at[:, there], back_in.at[:, cut]))
            loads.append(mine)
        for load in first:
            load.wait()
        for i, (cut, mine) in enumerate(zip(cuts, loads)):
            for load in mine:
                load.wait()
            below = lower[:, :, :, cut].reshape(layers * head, chunk)
            here = x_in[:, cut].astype(F32) + dot_nn(a_ref[...], below)
            rest_ref[i] = (c_in[:, cut].astype(F32) - t_ref[...] * here).astype(BF16)
            gain = jnp.sum(back_in[:, cut].astype(F32) * here, axis=0, keepdims=True)
            for at in range(0, chunk, head):
                row = (cut.start + at) // head
                dg_ref[row : row + 1, :] = gain[:, at : at + head]

    return pl.pallas_call(
        kernel,
        out_shape=[
            pltpu.VMEM((len(cuts), tokens, chunk), BF16),
            pltpu.VMEM((span // head, head), F32),
        ],
        in_specs=[IN_SMEM] + [IN_HBM] * (5 + len(stacks)),
        out_specs=[IN_VMEM] * 2,
        scratch_shapes=[
            pltpu.VMEM((layers, plane, rows, span), BF16),
            pltpu.VMEM((tokens, span), BF16),
            pltpu.VMEM((tokens, span), BF16),
            pltpu.VMEM((tokens, span), BF16),
            pltpu.VMEM((tokens, 1), F32),
            pltpu.VMEM((tokens, layers * head), BF16),
            pltpu.SemaphoreType.DMA((copies,)),
        ],
        compiler_params=params(),
        name="settle",
    )(
        places,
        *[in_hbm(array) for array in (total, mixes, x, cotangent, back, *stacks)],
    )


def join(index, arrived, pair, cols, after):
    tokens, part = arrived.shape

    def kernel(i_ref, r_ref, _, *refs):
        send_ref, pair_ref = refs[len(after) :]
        at = i_ref[0]
        r = r_ref[...]
        send_ref[...] = (pair_ref[0, at, :, cols].astype(F32) + r.astype(F32)).astype(BF16)
        pair_ref[1, at, :, cols] = r

    return pl.pallas_call(
        kernel,
        out_shape=[pltpu.VMEM((tokens, part), BF16), pltpu.VMEM(pair.shape, BF16)],
        in_specs=[IN_SMEM] + [IN_VMEM] * 2 + [ANYWHERE] * len(after),
        out_specs=[IN_VMEM] * 2,
        input_output_aliases={2: 1},
        compiler_params=params(SMALL),
        name="join",
    )(index, in_vmem(arrived), in_vmem(pair), *after)


def finish(index, arrived, pair, rests, streams):
    _, count, tokens, chunk = pair.shape

    def kernel(i_ref, *refs):
        r_refs = refs[: len(streams)]
        pair_ref, rest_refs = refs[len(streams)], refs[len(streams) + 1 :][: len(rests)]
        whole_ref, whole, sems = refs[len(streams) + 1 + len(rests) :]
        each = count // len(rests)
        at = i_ref[0]
        copies = []
        for i in range(count):
            full = rest_refs[i // each][i % each].astype(F32) + pair_ref[0, i].astype(F32)
            whole[i] = (full + pair_ref[1, i].astype(F32)).astype(BF16)

            @pl.when(at == i)
            def _(i=i, full=full):
                for ref, cols in zip(r_refs, streams):
                    whole[i, :, cols] = (full[:, cols] + ref[...].astype(F32)).astype(BF16)

            there = whole_ref.at[:, pl.ds(i * chunk, chunk)]
            copies.append(pltpu.make_async_copy(whole.at[i], there, sems.at[i]))
            copies[-1].start()
        for copy in copies:
            copy.wait()

    return pl.pallas_call(
        kernel,
        out_shape=pltpu.HBM((tokens, count * chunk), BF16),
        in_specs=[IN_SMEM] + [IN_VMEM] * (len(streams) + 1 + len(rests)),
        out_specs=IN_HBM,
        scratch_shapes=[
            pltpu.VMEM((count, tokens, chunk), BF16),
            pltpu.SemaphoreType.DMA((count,)),
        ],
        compiler_params=params(SMALL),
        name="finish",
    )(index, *[in_vmem(array) for array in (*arrived, pair, *rests)])


def stacked(arrays):
    rows = arrays[0].shape[0]

    def kernel(*refs):
        for i, ref in enumerate(refs[:-1]):
            refs[-1][i * rows : (i + 1) * rows, :] = ref[...]

    return pl.pallas_call(
        kernel,
        out_shape=pltpu.VMEM((len(arrays) * rows, arrays[0].shape[1]), F32),
        in_specs=[IN_VMEM] * len(arrays),
        out_specs=IN_VMEM,
        compiler_params=params(SMALL),
        name="stacked",
    )(*[in_vmem(array) for array in arrays])


def added(arrays):
    def kernel(*refs):
        total = refs[0][...]
        for ref in refs[1:-1]:
            total = total + ref[...]
        refs[-1][...] = total

    return pl.pallas_call(
        kernel,
        out_shape=pltpu.VMEM(arrays[0].shape, F32),
        in_specs=[IN_VMEM] * len(arrays),
        out_specs=IN_VMEM,
        compiler_params=params(SMALL),
        name="added",
    )(*[in_vmem(array) for array in arrays])


STREAMS = 2
CHUNKS = 4
PARTS = 1


def stream_columns(chunk):
    lanes = 128
    tiles = chunk // lanes
    ends = [-(-tiles * (i + 1) // STREAMS) * lanes for i in range(STREAMS)]
    return [slice(start, end) for start, end in zip([0] + ends, ends)]


def shifted(array, by):
    sections = lax.axis_size("section")
    return lax.ppermute(array, "section", [(i, (i + by) % sections) for i in range(sections)])


def raised(array, by):
    sections = lax.axis_size("section")
    return lax.ppermute(array, "section", [(i, i + by) for i in range(sections - by)])


def swapped(array, step):
    groups = lax.axis_size("group")
    devices = lax.axis_size("dp")
    bits = devices.bit_length() - 1
    pairs = []
    for p in range(devices):
        for g in range(groups):
            pairs.append((p * groups + g, (p ^ (1 << ((step + g) % bits))) * groups + g))
    return lax.ppermute(array, ("dp", "group"), pairs)


def handed(array, by):
    groups = lax.axis_size("group")
    return lax.ppermute(array, "group", [(i, (i + by) % groups) for i in range(groups)])


def plane_places():
    groups = lax.axis_size("group")
    bits = lax.axis_size("dp").bit_length() - 1
    masks = []
    for g in range(groups):
        order = [0]
        for step in range(bits):
            order = order + [m ^ (1 << ((step + g) % bits)) for m in order]
        masks.append(order)
    masks = jnp.asarray(masks, jnp.int32)
    dp, member = lax.axis_index("dp"), lax.axis_index("group")
    places = []
    for r in range(groups):
        giver = (member + groups - r) % groups
        places.append((dp ^ masks[giver]) * groups + giver)
    return jnp.concatenate(places).astype(jnp.int32)


def local(tokens_in, cotangent, gains, w_qkv, w_out, segments, plan):
    sections = lax.axis_size("section")
    groups = lax.axis_size("group")
    devices = lax.axis_size("dp")
    plane = devices * groups
    section = lax.axis_index("section")
    member = lax.axis_index("group")
    rows_dev = plan.shape[1]
    length = segments.shape[1]
    tokens, width = tokens_in.shape
    head = w_out.shape[1]
    share = rows_dev // groups
    w_layer, out_layer = w_qkv[0], w_out[0]
    place = member.astype(jnp.int32)[None]
    layer = section.astype(jnp.int32)[None]

    slice_rows = head // plane
    mine = lax.axis_index("dp") * groups + member
    own_rows, *parts = pick(
        tokens_in.reshape(rows_dev, length, width),
        plan,
        place,
        groups,
        out_layer,
        mine.astype(jnp.int32)[None],
        slice_rows,
    )
    slices = [raised(own_rows, r) for r in range(sections - 1, 0, -1)]
    slices = [own_rows] + slices[::-1]
    chosen = jnp.take(segments, plan[0], axis=0, mode="clip").astype(BF16)
    chosen = chosen.reshape(groups, share, length)
    moved, moved_seg = [], []
    for r in range(groups):
        outgoing = lax.dynamic_index_in_dim(chosen, (member + r) % groups, 0, keepdims=False)
        moved.append(handed(parts[r], r) if r else parts[r])
        moved_seg.append(handed(outgoing, r) if r else outgoing)
    moved = [part.reshape(share * length, width) for part in moved]
    order = (member - jnp.arange(groups)) % groups
    seg = jnp.take(jnp.stack(moved_seg), order, axis=0, mode="clip").reshape(tokens)
    at = jnp.arange(tokens)
    mask = (
        (at[:, None] >= at[None, :])
        & (at[:, None] // length == at[None, :] // length)
        & (seg[:, None] == seg[None, :])
    ).astype(F32)

    last = (section == sections - 1).astype(jnp.int32)[None]
    bits = devices.bit_length() - 1
    places = plane_places()
    x, xz, norms = project(
        moved, cotangent, gains, w_layer, out_layer, place, []
    )
    coupling, stack = couple(slices, gains, w_layer, out_layer, last, [mask, places, xz])
    others = [shifted(coupling, r) for r in range(1, sections)]

    streams = stream_columns(width // CHUNKS)

    def facing(array, by):
        return lax.ppermute(array, "section", [(i, i ^ by) for i in range(sections)])

    arrays, masks, by = [hold(xz, others)], [0], sections // 2
    while by > 0:
        arrays = arrays + [facing(array, by) for array in arrays]
        masks = masks + [mask_of ^ by for mask_of in masks]
        by = by // 2
    xz_all = [arrays[masks.index(r)] for r in range(sections)]
    early = [xz_all[r] for r in range(1, sections) if r & (r - 1) == 0]
    late = [xz_all[r] for r in range(1, sections) if r & (r - 1) != 0]
    pieces = [compact([coupling] + others, layer, 3 * head, head, [xz])]

    rows = [stack[None]]
    for step in range(bits):
        if step > 0:
            pieces = [merge(*pieces, early)]
        pieces = pieces + [swapped(pieces[0], step)]
        if step == bits - 1:
            pieces[-1] = hold(pieces[-1], late)
        if step > 0:
            rows = [gather_two(*rows, pieces[-1:])]
        rows = rows + [swapped(rows[0], step)]
    pieces = pieces + [handed(array, r) for r in range(1, groups) for array in pieces]
    sent, total, mixes, *leaving = serial(
        xz_all, pieces, places, norms, mask, layer, gains, w_layer, out_layer, streams
    )
    back, pair = widen(sent, gains, w_layer, out_layer, width // CHUNKS)

    down = [(i, i - 1) for i in range(1, sections)]
    behind = sections - 1 - section

    def index(tick):
        return jnp.clip(tick - behind, 0, CHUNKS - 1).astype(jnp.int32)[None]

    def lowered(arrays):
        return [lax.ppermute(array, "section", down) for array in arrays]

    ticks = CHUNKS + sections - 1
    after = {}
    for tick in range(1, ticks):
        arrived = lowered(leaving)
        if tick < ticks - 1:
            for i, cols in enumerate(streams):
                waits = after.get(tick, []) if tick < ticks - 2 or i == STREAMS - 1 else []
                leaving[i], pair = join(index(tick), arrived[i], pair, cols, waits)
        if tick == 1:
            rows = [hold(array, leaving) for array in rows]
            rows = rows + [handed(array, r) for r in range(1, groups) for array in rows]
            rests, halves = [], []
            for part in range(PARTS):
                rest, half = settle(
                    total, mixes, rows, places, x, cotangent, back, width // CHUNKS, part, PARTS
                )
                rests.append(rest)
                halves.append(half)
            sums = [stacked(halves)]
            for step in range(bits):
                sums.append(added([sums[-1], swapped(sums[-1], step)]))
            sums.append(added(sums[-1:] + [handed(sums[-1], r) for r in range(1, groups)]))
            gain_whole = sums[-1].reshape(1, width)
            after = {2 + i + (i > 0): [array] for i, array in enumerate(sums)}
    out = finish(index(ticks - 1), arrived, pair, rests, streams)
    return (out[None], gain_whole)


def attend(hidden, segment, gain_row, w_layer, out_layer):
    count, length, width = hidden.shape
    head = out_layer.shape[0]
    scaled = hidden * lax.rsqrt(jnp.mean(hidden * hidden, axis=-1, keepdims=True) + EPS) * gain_row
    normed = scaled.astype(BF16).reshape(count * length, width)
    projected = jnp.dot(normed, w_layer, preferred_element_type=F32).reshape(count, length, 3 * head)
    query = projected[:, :, :head]
    keyed = projected[:, :, head : 2 * head]
    valued = projected[:, :, 2 * head :]
    positions = jnp.arange(length)
    allowed = (positions[:, None] >= positions[None, :])[None] & (
        segment[:, :, None] == segment[:, None, :]
    )
    scores = jnp.einsum("rid,rjd->rij", query, keyed, precision=lax.Precision.HIGHEST)
    scores = jnp.where(allowed, scores / math.sqrt(head), -1e30)
    weights = jax.nn.softmax(scores, axis=-1)
    mixed = jnp.einsum("rij,rjd->rid", weights, valued, precision=lax.Precision.HIGHEST)
    mixed = mixed.astype(BF16).reshape(count * length, head)
    output = jnp.dot(mixed, out_layer, preferred_element_type=F32).reshape(count, length, width)
    return hidden + output


MB_ROWS = 2


def relay(tokens_in, cotangent, gains, w_qkv, w_out, segments, plan):
    sections = lax.axis_size("section")
    section = lax.axis_index("section")
    rows_dev = plan.shape[1]
    width = tokens_in.shape[1]
    length = segments.shape[1]
    micro = rows_dev // MB_ROWS
    blocks = tokens_in.reshape(rows_dev, length, width)
    chosen = jnp.take(blocks, plan[0], axis=0)
    chosen_seg = jnp.take(segments, plan[0], axis=0).astype(BF16)
    assigned = lax.all_to_all(chosen, "group", split_axis=0, concat_axis=0, tiled=True)
    moved_seg = lax.all_to_all(chosen_seg, "group", split_axis=0, concat_axis=0, tiled=True)
    assigned = assigned.reshape(micro, MB_ROWS, length, width)
    seg_groups = moved_seg.reshape(micro, MB_ROWS, length)
    gain_row, w_layer, out_layer = gains[0], w_qkv[0], w_out[0]
    grad_rows = cotangent.reshape(micro, MB_ROWS, length, width)
    ticks = micro + sections - 1

    def passed_along(array, by):
        pairs = [(i, i + by) for i in range(sections) if 0 <= i + by < sections]
        return lax.ppermute(array, "section", pairs)

    def at(array, i):
        return lax.dynamic_index_in_dim(array, i, 0, keepdims=False)

    def forward_tick(tick, carry):
        saved, arrived = carry
        index = tick - section
        valid = (index >= 0) & (index < micro)
        clipped = jnp.clip(index, 0, micro - 1)
        entering = jnp.where(section == 0, at(assigned, clipped), arrived)
        kept = jnp.where(valid, entering, at(saved, clipped))
        saved = lax.dynamic_update_index_in_dim(saved, kept, clipped, 0)
        segment = at(seg_groups, clipped)

        def run_layer(value):
            return attend(value.astype(F32), segment, gain_row, w_layer, out_layer).astype(BF16)

        leaving = lax.cond(valid, run_layer, jnp.zeros_like, entering)
        return (saved, passed_along(leaving, 1))

    saved_init = jnp.zeros((micro, MB_ROWS, length, width), BF16)
    arrive_init = jnp.zeros((MB_ROWS, length, width), BF16)
    saved, _ = lax.fori_loop(0, ticks, forward_tick, (saved_init, arrive_init))

    def backward_tick(tick, carry):
        grads_x, gain_total, arrived = carry
        index = tick - (sections - 1 - section)
        valid = (index >= 0) & (index < micro)
        clipped = jnp.clip(index, 0, micro - 1)
        entering = jnp.where(section == sections - 1, at(grad_rows, clipped), arrived)
        segment = at(seg_groups, clipped)
        stored = at(saved, clipped).astype(F32)

        def local_layer(hidden, gains_here):
            return attend(hidden, segment, gains_here, w_layer, out_layer)

        def run_back(value):
            _, pullback = jax.vjp(local_layer, stored, gain_row)
            grad_hidden, grad_gain = pullback(value.astype(F32))
            return (grad_hidden.astype(BF16), grad_gain)

        def skip_back(value):
            return (jnp.zeros_like(value), jnp.zeros(gain_row.shape, F32))

        sending, grad_gain = lax.cond(valid, run_back, skip_back, entering)
        kept = jnp.where(valid, sending, at(grads_x, clipped))
        grads_x = lax.dynamic_update_index_in_dim(grads_x, kept, clipped, 0)
        return (grads_x, gain_total + grad_gain, passed_along(sending, -1))

    gain_init = jnp.zeros(gain_row.shape, F32)
    grads_x, gain_total, _ = lax.fori_loop(
        0, ticks, backward_tick, (saved_init, gain_init, arrive_init)
    )
    gain_whole = lax.psum(gain_total, ("dp", "group"))
    return (grads_x.reshape(1, rows_dev * length, width), gain_whole[None])


def solution(mesh):
    placed = (
        P(("dp", "group"), None),
        P(("dp", "group"), None),
        P("section", None),
        P("section", None, None),
        P("section", None, None),
        P(("dp", "group"), None),
        P(("dp", "group"), None),
    )

    def chosen(tokens_in, cotangent, gains, w_qkv, w_out, segments, plan):
        sections, head, width = w_out.shape
        devices = mesh.shape["dp"]
        small = sections * 4 * head < width and sections > 1
        halves = devices & (devices - 1) == 0 and sections & (sections - 1) == 0
        body = local if small and halves else relay
        return jax.shard_map(
            body,
            mesh=mesh,
            in_specs=placed,
            out_specs=(P("section", ("dp", "group"), None), P("section", None)),
            check_vma=False,
        )(tokens_in, cotangent, gains, w_qkv, w_out, segments, plan)

    return chosen
```
